32 devices in a mesh: fsdp: 16 (over z, y, core), tp: 2 (over x).
Axes of the slice: x: 2, y: 2, z: 4, core: 2. Of those that a mesh axis runs over, the one named last changes fastest.
Arguments:
- tokens: bfloat16 [2, 16, 288, 2048], P(None, 'fsdp', 'tp'), may hold values from -6 to 6
- cotangent: bfloat16 [2, 16, 288, 2048], P(None, 'fsdp', 'tp'), may hold values from -6 to 6
- norm1_gain: bfloat16 [2048], replicated, may hold values from 0.5 to 1.5
- w_query: bfloat16 [2048, 4096], P('fsdp', 'tp'), may hold values from -0.125 to 0.125
- key_projection_weight: bfloat16 [2048, 512], P('fsdp', 'tp'), may hold values from -0.125 to 0.125
- value_projection_weight: bfloat16 [2048, 512], P('fsdp', 'tp'), may hold values from -0.125 to 0.125
- query_gain: bfloat16 [128], replicated, may hold values from 0.25 to 1.75
- key_gain: bfloat16 [128], replicated, may hold values from 0.25 to 1.75
- w_out: bfloat16 [4096, 2048], P('tp', 'fsdp'), may hold values from -0.375 to 0.375
- norm2_gain: bfloat16 [2048], replicated, may hold values from 0.5 to 1.5
- w_gate: bfloat16 [32, 2048, 768], P('fsdp', None, 'tp'), may hold values from -0.125 to 0.125
- w_up: bfloat16 [32, 2048, 768], P('fsdp', None, 'tp'), may hold values from -0.125 to 0.125
- w_down: bfloat16 [32, 768, 2048], P('fsdp', 'tp'), may hold values from -0.875 to 0.875
- routes: int32 [2, 16, 288, 8], P(None, 'fsdp'), may hold values from 0 to 31, all different within a row; in each aligned block of 288 rows (0 to 287, 288 to 575, ..., all dimensions but the last counted through in order) at most 84 rows name the same one
- gates: float32 [2, 16, 288, 8], P(None, 'fsdp'), may hold values from 0.06 to 0.2
Outputs:
- block_out: bfloat16 [2, 16, 288, 2048], P(None, 'fsdp', 'tp')
- input_grad: bfloat16 [2, 16, 288, 2048], P(None, 'fsdp', 'tp')
- norm1_grad: float32 [2048], replicated
- query_grad: float32 [2048, 4096], P('fsdp', 'tp')
- key_grad: float32 [2048, 512], P('fsdp', 'tp')
- value_grad: float32 [2048, 512], P('fsdp', 'tp')
- qnorm_grad: float32 [128], replicated
- knorm_grad: float32 [128], replicated
- out_proj_grad: float32 [4096, 2048], P('tp', 'fsdp')
- norm2_grad: float32 [2048], replicated
- gate_grad: float32 [32, 2048, 768], P('fsdp', None, 'tp')
- up_grad: float32 [32, 2048, 768], P('fsdp', None, 'tp')
- down_grad: float32 [32, 768, 2048], P('fsdp', 'tp')
The draws below stay inside these ranges and needn't reach their ends.
Inputs may be any that keep to these rules, and one draw needn't show every extreme that they name: `routes`: A token names 8 different experts. The 288 tokens of one sequence in one micro-batch name each expert at most 84 times in all; in some sequences one expert is named exactly 84 times, and every expert is named somewhere.
All inputs are finite; a program needn't handle non-finite values.
Results may differ from the reference program's by a relative error of at most 0.02.
Values may be sent and summed in bfloat16 or wider, within the bound.
A program may use at most 512 MiB of HBM per device.

```python
import math
import jax
import jax.numpy as jnp
import numpy as np
from jax import lax

MODEL_DIMENSION = 2048
QUERY_HEADS = 32
KEY_VALUE_HEADS = 4
HEAD_FEATURES = 128
FF = 768
TOPK = 8
MICRO = 2
BLOCK = 256
SEQ = 288
SEQS = 16
EXPERTS = 32
CAP = 84


def level_of(key, dims, split, smallest, top_value):
    loudness = 1.0
    for position, blocks in split:
        heights = jax.random.uniform(jax.random.fold_in(jax.random.fold_in(key, 6), position), (blocks,), jnp.float32, smallest / len(split), top_value / len(split))
        loudness = loudness * jnp.repeat(jnp.exp(heights), dims[position] // blocks).reshape((-1,) + (1,) * (len(dims) - 1 - position))
    return loudness


def deal_out(rng, own, number, rows, amount, top, most, slope):
    ranking = jax.random.permutation(rng, amount)
    crowded, ordinary = shares(amount, rows * top, most, slope, True), shares(amount, rows * top, most, slope, False)
    places = jnp.arange(amount)

    def named(sizes, turn):
        used = int((sizes > 0).sum())
        fixed = max(1, used // 4)
        shifted = fixed + (places - fixed + turn * (used - fixed)) % max(1, amount - fixed)
        return jnp.zeros((amount,), jnp.int32).at[ranking[jnp.where(places < fixed, places, shifted)]].set(jnp.asarray(sizes, jnp.int32))

    sizes = jnp.where(number % 4 == 0, named(crowded, number // 4), named(ordinary, number - number // 4 - 1))
    mixed = jax.random.permutation(jax.random.fold_in(own, 3), amount)
    donor, sink = mixed[0:amount // 2 * 2:2], mixed[1:amount // 2 * 2:2]
    margin = jnp.minimum(sizes[donor] - 1, most - sizes[sink]) // 2
    margin = jnp.where((donor == ranking[0]) | (sink == ranking[0]) | (sizes[sink] == 0), 0, jnp.maximum(margin, 0))
    shifted = jax.random.randint(jax.random.fold_in(own, 4), (amount // 2,), 0, 1 << 20) % (margin + 1)
    sizes = sizes.at[donor].add(-shifted).at[sink].add(shifted)
    labels = jnp.searchsorted(jnp.cumsum(sizes), jnp.arange(rows * top), side="right").astype(jnp.int32)
    listing = labels.reshape(top, rows).T
    listing = listing[jax.random.permutation(jax.random.fold_in(own, 1), rows)]
    turn = jax.random.randint(jax.random.fold_in(own, 2), (rows, 1), 0, top)
    return jnp.take_along_axis(listing, (jnp.arange(top)[None, :] + turn) % top, axis=1)


def shares(amount, total, reach, slope, full):
    loads = [(1 << 20) // math.isqrt(grade ** slope) + 1 for grade in range(1, amount + 1)]
    largest = reach if full else min(reach, max(-(-total // amount), total * loads[0] // sum(loads)))
    least = 1 if total - largest >= amount - 1 else 0
    given, surplus = [largest] + [least] * (amount - 1), total - largest - least * (amount - 1)
    while surplus > 0:
        movable = [i for i in range(1, amount) if given[i] < largest] or [i for i in range(1, amount) if given[i] < reach]
        pool, left = sum([loads[i] for i in movable]), surplus
        for i in movable:
            extra = min(reach - given[i], max(1, left * loads[i] // pool), surplus)
            given[i] = given[i] + extra
            surplus = surplus - extra
    return np.array(given)


def noise(key, dims, deviation, most, pieces=(), kind=jnp.bfloat16):
    array = jax.random.normal(key, dims, jnp.float32) * deviation
    if len(pieces) > 0:
        array = level_of(key, dims, pieces, -0.22, 0.18) * array
    return jnp.clip(array, min=-most, max=most).astype(kind)


def setup_inputs(seed: int = 0) -> dict:
    arg_keys = jax.random.split(jax.random.key(seed), 16)
    tokens = noise(arg_keys[0], (MICRO, SEQS, SEQ, MODEL_DIMENSION), 1.0, 6.0, ((1, 16), (2, 2)))
    cotangent = noise(arg_keys[1], (MICRO, SEQS, SEQ, MODEL_DIMENSION), 1.0, 6.0, ((1, 16), (2, 2)))
    norm1_gain = jnp.clip(1.0 + 0.1 * jax.random.normal(arg_keys[2], (MODEL_DIMENSION,), jnp.float32), 0.5, 1.5).astype(jnp.bfloat16)
    w_query = noise(arg_keys[3], (MODEL_DIMENSION, QUERY_HEADS * HEAD_FEATURES), MODEL_DIMENSION ** -0.5, 0.125, ((0, 16), (1, 2)))
    key_projection_weight = noise(arg_keys[4], (MODEL_DIMENSION, KEY_VALUE_HEADS * HEAD_FEATURES), MODEL_DIMENSION ** -0.5, 0.125, ((0, 16), (1, 2)))
    value_projection_weight = noise(arg_keys[5], (MODEL_DIMENSION, KEY_VALUE_HEADS * HEAD_FEATURES), MODEL_DIMENSION ** -0.5, 0.125, ((0, 16), (1, 2)))
    query_gain = jnp.clip(1.0 + 0.15 * jax.random.normal(arg_keys[6], (HEAD_FEATURES,), jnp.float32), 0.25, 1.75).astype(jnp.bfloat16)
    key_gain = jnp.clip(1.0 + 0.15 * jax.random.normal(arg_keys[7], (HEAD_FEATURES,), jnp.float32), 0.25, 1.75).astype(jnp.bfloat16)
    w_out = noise(arg_keys[8], (QUERY_HEADS * HEAD_FEATURES, MODEL_DIMENSION), (QUERY_HEADS * HEAD_FEATURES // 16) ** -0.5, 0.375, ((0, 2), (1, 16)))
    norm2_gain = jnp.clip(1.0 + 0.1 * jax.random.normal(arg_keys[9], (MODEL_DIMENSION,), jnp.float32), 0.5, 1.5).astype(jnp.bfloat16)
    w_gate = noise(arg_keys[10], (EXPERTS, MODEL_DIMENSION, FF), MODEL_DIMENSION ** -0.5, 0.125, ((0, 16), (2, 2)))
    w_up = noise(arg_keys[11], (EXPERTS, MODEL_DIMENSION, FF), MODEL_DIMENSION ** -0.5, 0.125, ((0, 16), (2, 2)))
    w_down = noise(arg_keys[12], (EXPERTS, FF, MODEL_DIMENSION), (FF // 16) ** -0.5, 0.875, ((0, 16), (1, 2)))
    routes_keys = jax.random.split(jax.random.fold_in(arg_keys[13], 1), MICRO * SEQS * SEQ // SEQ)
    routes_turns = jax.random.permutation(jax.random.fold_in(arg_keys[13], 3), MICRO * SEQS * SEQ // SEQ)
    routes = jax.vmap(lambda own, number: deal_out(jax.random.fold_in(arg_keys[13], 2), own, number, SEQ, EXPERTS, TOPK, CAP, 1))(routes_keys, routes_turns).reshape((MICRO, SEQS, SEQ, TOPK))
    gates = jnp.clip(jnp.exp(math.log(0.2) - 1.2039728 * jax.random.uniform(arg_keys[14], (MICRO, SEQS, SEQ, TOPK), jnp.float32) ** level_of(arg_keys[14], (MICRO, SEQS, SEQ, TOPK), ((1, 16),), -0.2, 0.2)), 0.06, 0.2)
    return {"tokens": tokens, "cotangent": cotangent, "norm1_gain": norm1_gain, "w_query": w_query, "key_projection_weight": key_projection_weight, "value_projection_weight": value_projection_weight, "query_gain": query_gain, "key_gain": key_gain, "w_out": w_out, "norm2_gain": norm2_gain, "w_gate": w_gate, "w_up": w_up, "w_down": w_down, "routes": routes, "gates": gates}


EPSILON = 1e-06
ROPE_BASE = 1000000.0
MASKED = -1e+30
EXACT_PRECISION = lax.Precision.HIGHEST

@jax.custom_vjp
def reduced_value(v):
    return lax.optimization_barrier(v.astype(jnp.bfloat16)).astype(jnp.float32)

@jax.custom_vjp
def reduced_backward(v):
    return v

def low_keep(v):
    return (reduced_value(v), None)

def low_pass(kept, grad):
    return (grad,)

def back_keep(v):
    return (v, None)

def back_low(kept, grad):
    return (reduced_value(grad),)
reduced_value.defvjp(low_keep, low_pass)
reduced_backward.defvjp(back_keep, back_low)

def rms_scale(row_block, gain_row):
    return row_block * lax.rsqrt(lax.optimization_barrier(jnp.mean(row_block * row_block, axis=-1, keepdims=True)) + EPSILON) * gain_row

def rotary_tables(sequence_length, head_width):
    half_width = head_width // 2
    inverse = ROPE_BASE ** (-2.0 * jnp.arange(half_width, dtype=jnp.float32) / head_width)
    angles = jnp.arange(sequence_length, dtype=jnp.float32)[:, None] * inverse[None, :]
    cosine_table = jnp.concatenate([jnp.cos(angles), jnp.cos(angles)], axis=-1)[:, None, :]
    sine_values = jnp.concatenate([jnp.sin(angles), jnp.sin(angles)], axis=-1)[:, None, :]
    return (cosine_table, sine_values)

def rotate(head_rows, cosine_table, sine_values):
    half_width = head_rows.shape[-1] // 2
    turned = jnp.concatenate([-head_rows[..., half_width:], head_rows[..., :half_width]], axis=-1)
    return head_rows * cosine_table + turned * sine_values

def prepare_heads(projected, gain_row, cosine_table, sine_values):
    return rotate(rms_scale(projected, gain_row), cosine_table, sine_values)

def slot_tables(route_rows, expert_count, capacity):
    sequence_length = route_rows.shape[0]
    top_count = route_rows.shape[1]
    flat_routes = route_rows.reshape(-1)
    onehot = (flat_routes[:, None] == jnp.arange(expert_count, dtype=jnp.int32)[None, :]).astype(jnp.int32)
    before = jnp.cumsum(onehot, axis=0) - onehot
    slot_rank = lax.optimization_barrier(jnp.sum(before * onehot, axis=1)).astype(jnp.int32)
    slot_index = (flat_routes * capacity + slot_rank).astype(jnp.int32)
    pick_ids = jnp.arange(sequence_length * top_count, dtype=jnp.int32) // top_count
    slot_owner = jnp.full((expert_count * capacity,), sequence_length, jnp.int32).at[slot_index].set(pick_ids)
    return (slot_index, slot_owner)

def layer_sequence(row_block, params, slot_index, slot_owner, gate_rows):
    first_gain, query_weight, key_matrix, value_matrix, query_factor_scale, key_scale, out_weight, second_gain, gate_weight, up_weight, down_weight = params
    sequence_length = row_block.shape[0]
    model_width = row_block.shape[1]
    head_features = query_factor_scale.shape[0]
    cosine_table, sine_values = rotary_tables(sequence_length, head_features)
    normalized_rows = reduced_value(rms_scale(row_block, first_gain))
    query_projected = reduced_backward(jnp.dot(normalized_rows, query_weight, precision=EXACT_PRECISION, preferred_element_type=jnp.float32)).reshape(sequence_length, QUERY_HEADS, head_features)
    key_projected = reduced_backward(jnp.dot(normalized_rows, key_matrix, precision=EXACT_PRECISION, preferred_element_type=jnp.float32)).reshape(sequence_length, KEY_VALUE_HEADS, head_features)
    value_row_list = reduced_value(reduced_backward(jnp.dot(normalized_rows, value_matrix, precision=EXACT_PRECISION, preferred_element_type=jnp.float32))).reshape(sequence_length, KEY_VALUE_HEADS, head_features)
    query_fourfold = reduced_value(prepare_heads(query_projected, query_factor_scale, cosine_table, sine_values)).reshape(sequence_length, KEY_VALUE_HEADS, QUERY_HEADS // KEY_VALUE_HEADS, head_features)
    key_rot = reduced_value(prepare_heads(key_projected, key_scale, cosine_table, sine_values))
    raw_scores = reduced_backward(jnp.einsum('qcgd,kcd->cgqk', query_fourfold, key_rot, precision=EXACT_PRECISION, preferred_element_type=jnp.float32) * head_features ** (-0.5))
    block_ids = jnp.arange(sequence_length, dtype=jnp.int32) // BLOCK
    visible = (block_ids[None, :] <= block_ids[:, None])[None, None]
    scores = jnp.where(visible, raw_scores, MASKED)
    row_max = lax.optimization_barrier(jnp.max(scores, axis=-1, keepdims=True))
    exp_scores = jnp.exp(scores - row_max)
    prob_rows = reduced_value(exp_scores / lax.optimization_barrier(jnp.sum(exp_scores, axis=-1, keepdims=True)))
    context = reduced_value(reduced_backward(jnp.einsum('cgqk,kcd->qcgd', prob_rows, value_row_list, precision=EXACT_PRECISION, preferred_element_type=jnp.float32))).reshape(sequence_length, QUERY_HEADS * head_features)
    hidden = row_block + reduced_backward(jnp.dot(context, out_weight, precision=EXACT_PRECISION, preferred_element_type=jnp.float32))
    normed_two = reduced_value(rms_scale(hidden, second_gain))
    padded_rows = jnp.concatenate([normed_two, jnp.zeros((1, model_width), jnp.float32)], axis=0)
    expert_in = padded_rows[slot_owner].reshape(EXPERTS, CAP, model_width)
    gate_act = reduced_backward(jnp.einsum('ecd,edf->ecf', expert_in, gate_weight, precision=EXACT_PRECISION, preferred_element_type=jnp.float32))
    up_act = reduced_backward(jnp.einsum('ecd,edf->ecf', expert_in, up_weight, precision=EXACT_PRECISION, preferred_element_type=jnp.float32))
    act_rows = reduced_value(jax.nn.silu(gate_act) * up_act)
    expert_out = reduced_backward(jnp.einsum('ecf,efd->ecd', act_rows, down_weight, precision=EXACT_PRECISION, preferred_element_type=jnp.float32))
    picked = expert_out.reshape(EXPERTS * CAP, model_width)[slot_index].reshape(sequence_length, TOPK, model_width)
    return hidden + lax.optimization_barrier(jnp.sum(picked * gate_rows[:, :, None], axis=1))

def reference(tokens, cotangent, norm1_gain, w_query, key_projection_weight, value_projection_weight, query_gain, key_gain, w_out, norm2_gain, w_gate, w_up, w_down, routes, gates):
    model_width = tokens.shape[-1]
    row_blocks = tokens.reshape(-1, SEQ, model_width).astype(jnp.float32)
    cot_blocks = cotangent.reshape(-1, SEQ, model_width).astype(jnp.float32)
    route_blocks = routes.reshape(-1, SEQ, TOPK)
    gate_blocks = gates.reshape(-1, SEQ, TOPK).astype(jnp.float32)

    def tables_of(route_rows):
        return slot_tables(route_rows, EXPERTS, CAP)
    slot_index, slot_owner = lax.map(tables_of, route_blocks)
    params = tuple((weight_part.astype(jnp.float32) for weight_part in (norm1_gain, w_query, key_projection_weight, value_projection_weight, query_gain, key_gain, w_out, norm2_gain, w_gate, w_up, w_down)))

    def forward(rows_in, weights_in):

        def one_sequence(sequence_items):
            return layer_sequence(sequence_items[0], weights_in, sequence_items[1], sequence_items[2], sequence_items[3])
        return lax.map(jax.checkpoint(one_sequence), (rows_in, slot_index, slot_owner, gate_blocks))
    result, pullback = jax.vjp(forward, row_blocks, params)
    row_grads, weight_grads = pullback(cot_blocks)
    first_grad, query_grad, key_grad, value_grad, qnorm_grad, knorm_grad, out_grad, second_grad, gate_grad, up_grad, down_grad = weight_grads
    return (result.reshape(tokens.shape).astype(jnp.bfloat16), row_grads.reshape(tokens.shape).astype(jnp.bfloat16), first_grad, query_grad, key_grad, value_grad, qnorm_grad, knorm_grad, out_grad, second_grad, gate_grad, up_grad, down_grad)
```

```python
import functools

import jax
import jax.numpy as jnp
from jax import lax
from jax.experimental import pallas as pl
from jax.experimental.pallas import tpu as pltpu
from jax.sharding import PartitionSpec as P

BLOCK = 256


EPSILON = 1e-06
ROPE_BASE = 1000000.0
MASKED = -1e30
TILE_PICKS = 128


def rms_scale(row_block, gain_row):
    return (
        row_block
        * lax.rsqrt(jnp.mean(row_block * row_block, axis=-1, keepdims=True) + EPSILON)
        * gain_row
    )


def rotary_tables(sequence_length, head_width):
    half_width = head_width // 2
    inverse = ROPE_BASE ** (-2.0 * jnp.arange(half_width, dtype=jnp.float32) / head_width)
    angles = jnp.arange(sequence_length, dtype=jnp.float32)[:, None] * inverse[None, :]
    cosine_table = jnp.concatenate([jnp.cos(angles), jnp.cos(angles)], axis=-1)[:, None, :]
    sine_values = jnp.concatenate([jnp.sin(angles), jnp.sin(angles)], axis=-1)[:, None, :]
    return (cosine_table, sine_values)


def rotate(head_rows, cosine_table, sine_values):
    half_width = head_rows.shape[-1] // 2
    turned = jnp.concatenate([-head_rows[..., half_width:], head_rows[..., :half_width]], axis=-1)
    return head_rows * cosine_table + turned * sine_values


def prepare_heads(projected, gain_row, cosine_table, sine_values):
    return rotate(rms_scale(projected, gain_row), cosine_table, sine_values)


def swiglu(gate_act, up_act):
    return jax.nn.silu(gate_act) * up_act


def slot_tables(route_rows, gate_rows, expert_count, capacity):
    sequence_length = route_rows.shape[0]
    top_count = route_rows.shape[1]
    pick_count = sequence_length * top_count
    tile_count = pick_count // TILE_PICKS
    flat_routes = route_rows.reshape(-1)
    onehot = (flat_routes[:, None] == jnp.arange(expert_count, dtype=jnp.int32)[None, :]).astype(
        jnp.bfloat16
    )
    tiles = onehot.reshape(tile_count, TILE_PICKS, expert_count)
    positions = jnp.arange(TILE_PICKS, dtype=jnp.int32)
    lower = (positions[None, :] < positions[:, None]).astype(jnp.bfloat16)
    within = jnp.einsum("ij,bje->bie", lower, tiles, preferred_element_type=jnp.float32)
    tile_totals = jnp.sum(tiles.astype(jnp.float32), axis=1)
    offsets = jnp.cumsum(tile_totals, axis=0) - tile_totals
    before = within + offsets[:, None, :]
    slot_rank = jnp.sum(before * tiles.astype(jnp.float32), axis=-1).reshape(-1).astype(jnp.int32)
    slot_index = flat_routes * capacity + slot_rank
    pick_ids = jnp.arange(pick_count, dtype=jnp.int32) // top_count
    slot_owner = (
        jnp.full((expert_count * capacity,), sequence_length, jnp.int32)
        .at[slot_index]
        .set(pick_ids)
    )
    slot_weight = (
        jnp.zeros((expert_count * capacity,), jnp.float32).at[slot_index].set(gate_rows.reshape(-1))
    )
    return (slot_index, slot_owner, slot_weight)


def exchanged_layer(
    tokens,
    cotangent,
    norm1_gain,
    w_query,
    key_projection_weight,
    value_projection_weight,
    query_gain,
    key_gain,
    w_out,
    norm2_gain,
    w_gate,
    w_up,
    w_down,
    routes,
    gates,
):
    batch_count = tokens.shape[0]
    model_width = tokens.shape[3]
    sequence_length = routes.shape[2]
    top_count = routes.shape[3]
    head_features = query_gain.shape[0]
    local_experts = w_gate.shape[0]
    fsdp_count = lax.axis_size("fsdp")
    all_experts = local_experts * fsdp_count
    capacity = 7 * top_count * sequence_length // (6 * all_experts)
    query_heads = w_query.shape[1] // head_features
    kv_heads = key_projection_weight.shape[1] // head_features
    group_size = query_heads // kv_heads
    score_scale = head_features ** (-0.5)
    cosine_table, sine_values = rotary_tables(sequence_length, head_features)
    block_ids = jnp.arange(sequence_length, dtype=jnp.int32) // BLOCK
    visible = (block_ids[None, :] <= block_ids[:, None])[None, None]
    first_gain = norm1_gain.astype(jnp.float32)
    second_gain = norm2_gain.astype(jnp.float32)
    query_factor_scale = query_gain.astype(jnp.float32)
    key_scale = key_gain.astype(jnp.float32)
    zero_row = jnp.zeros((1, model_width), jnp.bfloat16)
    buffer_shape = (fsdp_count, local_experts, capacity, model_width)

    def masked_scores(query_fourfold, key_rows):
        raw_scores = (
            jnp.einsum(
                "qcgd,kcd->cgqk", query_fourfold, key_rows, preferred_element_type=jnp.float32
            )
            * score_scale
        )
        return jnp.where(visible, raw_scores, MASKED)

    def prep_heads(projected, gain_row):
        return prepare_heads(projected, gain_row, cosine_table, sine_values)

    gain_sums = (
        jnp.zeros((model_width,), jnp.float32),
        jnp.zeros((model_width,), jnp.float32),
        jnp.zeros((head_features,), jnp.float32),
        jnp.zeros((head_features,), jnp.float32),
    )
    expert_grads = (
        jnp.zeros(w_gate.shape, jnp.float32),
        jnp.zeros(w_up.shape, jnp.float32),
        jnp.zeros(w_down.shape, jnp.float32),
    )
    attn_grads = tuple(
        (
            jnp.zeros(weight_part.shape, jnp.float32)
            for weight_part in (w_query, key_projection_weight, value_projection_weight, w_out)
        )
    )
    outputs = []
    input_grads = []
    for batch_index in range(batch_count):
        query_full, key_full, value_full, out_full = (
            lax.all_gather(w_query, "fsdp", axis=0, tiled=True),
            lax.all_gather(key_projection_weight, "fsdp", axis=0, tiled=True),
            lax.all_gather(value_projection_weight, "fsdp", axis=0, tiled=True),
            lax.all_gather(w_out, "fsdp", axis=1, tiled=True),
        )
        own_rows = tokens[batch_index, 0].astype(jnp.float32)
        own_cot = cotangent[batch_index, 0]
        route_rows = routes[batch_index, 0]
        gate_rows = gates[batch_index, 0]
        first_normed = rms_scale(own_rows, first_gain).astype(jnp.bfloat16)
        normed_all = lax.all_gather(first_normed, "tp", axis=0, tiled=True)
        query_projected = jnp.dot(
            normed_all, query_full, preferred_element_type=jnp.float32
        ).reshape(sequence_length, query_heads, head_features)
        key_projected = jnp.dot(normed_all, key_full, preferred_element_type=jnp.float32).reshape(
            sequence_length, kv_heads, head_features
        )
        value_row_list = (
            jnp.dot(normed_all, value_full, preferred_element_type=jnp.float32)
            .astype(jnp.bfloat16)
            .reshape(sequence_length, kv_heads, head_features)
        )
        query_rot = prep_heads(query_projected, query_factor_scale).astype(jnp.bfloat16)
        key_rot = prep_heads(key_projected, key_scale).astype(jnp.bfloat16)
        query_fourfold = query_rot.reshape(sequence_length, kv_heads, group_size, head_features)
        scores = masked_scores(query_fourfold, key_rot)
        row_max = jnp.max(scores, axis=-1, keepdims=True)
        exp_scores = jnp.exp(scores - row_max)
        totals = jnp.sum(exp_scores, axis=-1, keepdims=True)
        log_total = row_max + jnp.log(totals)
        prob_rows = (exp_scores / totals).astype(jnp.bfloat16)
        context = (
            jnp.einsum(
                "cgqk,kcd->qcgd", prob_rows, value_row_list, preferred_element_type=jnp.float32
            )
            .astype(jnp.bfloat16)
            .reshape(sequence_length, query_heads * head_features)
        )
        attn_own = lax.psum_scatter(
            jnp.dot(context, out_full, preferred_element_type=jnp.float32).astype(jnp.bfloat16),
            "tp",
            scatter_dimension=0,
            tiled=True,
        ).astype(jnp.float32)
        hidden_own = own_rows + attn_own
        second_normed = rms_scale(hidden_own, second_gain).astype(jnp.bfloat16)
        normed_two, cot_all = (
            lax.all_gather(second_normed, "tp", axis=0, tiled=True),
            lax.all_gather(own_cot, "tp", axis=0, tiled=True),
        )
        slot_index, slot_owner, slot_weight = slot_tables(
            route_rows, gate_rows, all_experts, capacity
        )
        padded_rows = jnp.concatenate([normed_two, zero_row], axis=0)
        send_rows = padded_rows[slot_owner].reshape(buffer_shape)
        expert_in = lax.all_to_all(send_rows, "fsdp", split_axis=0, concat_axis=0, tiled=True)
        gate_act = jnp.einsum(
            "sekd,edf->sekf", expert_in, w_gate, preferred_element_type=jnp.float32
        )
        up_act = jnp.einsum("sekd,edf->sekf", expert_in, w_up, preferred_element_type=jnp.float32)
        act_rows = swiglu(gate_act, up_act).astype(jnp.bfloat16)
        expert_out = jnp.einsum(
            "sekf,efd->sekd", act_rows, w_down, preferred_element_type=jnp.float32
        )
        returned = lax.all_to_all(
            expert_out.astype(jnp.bfloat16), "fsdp", split_axis=0, concat_axis=0, tiled=True
        ).astype(expert_out.dtype)
        picked = returned.reshape(all_experts * capacity, model_width)[slot_index].reshape(
            sequence_length, top_count, model_width
        )
        moe_part = jnp.sum(picked * gate_rows[:, :, None], axis=1)
        moe_own = lax.psum_scatter(
            moe_part.astype(jnp.bfloat16), "tp", scatter_dimension=0, tiled=True
        ).astype(jnp.float32)
        outputs.append((hidden_own + moe_own).astype(jnp.bfloat16))
        cot_padded = jnp.concatenate([cot_all, zero_row], axis=0)
        send_grads = (
            (slot_weight[:, None] * cot_padded[slot_owner])
            .astype(jnp.bfloat16)
            .reshape(buffer_shape)
        )
        out_grads = lax.all_to_all(send_grads, "fsdp", split_axis=0, concat_axis=0, tiled=True)
        act_grads = jnp.einsum(
            "sekd,efd->sekf", out_grads, w_down, preferred_element_type=jnp.float32
        )
        _, swiglu_back = jax.vjp(swiglu, gate_act, up_act)
        gate_grads, up_grads = swiglu_back(act_grads)
        gate_grads = gate_grads.astype(jnp.bfloat16)
        up_grads = up_grads.astype(jnp.bfloat16)
        expert_grads = (
            expert_grads[0]
            + jnp.einsum(
                "sekd,sekf->edf", expert_in, gate_grads, preferred_element_type=jnp.float32
            ),
            expert_grads[1]
            + jnp.einsum("sekd,sekf->edf", expert_in, up_grads, preferred_element_type=jnp.float32),
            expert_grads[2]
            + jnp.einsum("sekf,sekd->efd", act_rows, out_grads, preferred_element_type=jnp.float32),
        )
        input_part = jnp.einsum(
            "sekf,edf->sekd", gate_grads, w_gate, preferred_element_type=jnp.float32
        ) + jnp.einsum("sekf,edf->sekd", up_grads, w_up, preferred_element_type=jnp.float32)
        input_back = lax.all_to_all(
            input_part.astype(jnp.bfloat16), "fsdp", split_axis=0, concat_axis=0, tiled=True
        ).astype(input_part.dtype)
        normed_grads = jnp.sum(
            input_back.reshape(all_experts * capacity, model_width)[slot_index].reshape(
                sequence_length, top_count, model_width
            ),
            axis=1,
        )
        normed_own = lax.psum_scatter(
            normed_grads.astype(jnp.bfloat16), "tp", scatter_dimension=0, tiled=True
        ).astype(jnp.float32)
        _, second_back = jax.vjp(rms_scale, hidden_own, second_gain)
        hidden_part, second_gain_grad = second_back(normed_own)
        hidden_grad = own_cot.astype(jnp.float32) + hidden_part
        attn_grad_all = lax.all_gather(hidden_grad.astype(jnp.bfloat16), "tp", axis=0, tiled=True)
        out_weight_grad = jnp.einsum(
            "th,td->hd", context, attn_grad_all, preferred_element_type=jnp.float32
        )
        context_grad = (
            jnp.einsum("td,hd->th", attn_grad_all, out_full, preferred_element_type=jnp.float32)
            .astype(jnp.bfloat16)
            .reshape(sequence_length, kv_heads, group_size, head_features)
        )
        exp_again = jnp.exp(masked_scores(query_fourfold, key_rot) - log_total)
        probs_again = exp_again.astype(jnp.bfloat16)
        prob_grads = jnp.einsum(
            "qcgd,kcd->cgqk", context_grad, value_row_list, preferred_element_type=jnp.float32
        )
        value_grads = (
            jnp.einsum(
                "cgqk,qcgd->kcd", probs_again, context_grad, preferred_element_type=jnp.float32
            )
            .astype(jnp.bfloat16)
            .reshape(sequence_length, kv_heads * head_features)
        )
        score_grads = (
            exp_again * (prob_grads - jnp.sum(exp_again * prob_grads, axis=-1, keepdims=True))
        ).astype(jnp.bfloat16)
        query_rot_grads = (
            jnp.einsum("cgqk,kcd->qcgd", score_grads, key_rot, preferred_element_type=jnp.float32)
            * score_scale
        ).reshape(sequence_length, query_heads, head_features)
        key_rot_grads = (
            jnp.einsum(
                "cgqk,qcgd->kcd", score_grads, query_fourfold, preferred_element_type=jnp.float32
            )
            * score_scale
        )
        _, query_back = jax.vjp(prep_heads, query_projected, query_factor_scale)
        query_proj_grads, query_gain_grad = query_back(query_rot_grads)
        _, key_back = jax.vjp(prep_heads, key_projected, key_scale)
        key_proj_grads, key_gain_grad = key_back(key_rot_grads)
        query_proj_grads = query_proj_grads.astype(jnp.bfloat16).reshape(
            sequence_length, query_heads * head_features
        )
        key_proj_grads = key_proj_grads.astype(jnp.bfloat16).reshape(
            sequence_length, kv_heads * head_features
        )
        first_normed_grads = (
            jnp.einsum(
                "tq,dq->td", query_proj_grads, query_full, preferred_element_type=jnp.float32
            )
            + jnp.einsum("tq,dq->td", key_proj_grads, key_full, preferred_element_type=jnp.float32)
            + jnp.einsum("tq,dq->td", value_grads, value_full, preferred_element_type=jnp.float32)
        )
        weight_parts = (
            jnp.einsum(
                "td,tq->dq", normed_all, query_proj_grads, preferred_element_type=jnp.float32
            ),
            jnp.einsum("td,tq->dq", normed_all, key_proj_grads, preferred_element_type=jnp.float32),
            jnp.einsum("td,tq->dq", normed_all, value_grads, preferred_element_type=jnp.float32),
            out_weight_grad,
        )
        first_own = lax.psum_scatter(
            first_normed_grads.astype(jnp.bfloat16), "tp", scatter_dimension=0, tiled=True
        ).astype(jnp.float32)
        _, first_back = jax.vjp(rms_scale, own_rows, first_gain)
        row_part, first_gain_grad = first_back(first_own)
        input_grads.append((hidden_grad + row_part).astype(jnp.bfloat16))
        gain_sums = (
            gain_sums[0] + first_gain_grad,
            gain_sums[1] + second_gain_grad,
            gain_sums[2] + query_gain_grad,
            gain_sums[3] + key_gain_grad,
        )
        attn_grads = jax.tree.map(
            jnp.add,
            attn_grads,
            (
                lax.psum_scatter(weight_parts[0], "fsdp", scatter_dimension=0, tiled=True),
                lax.psum_scatter(weight_parts[1], "fsdp", scatter_dimension=0, tiled=True),
                lax.psum_scatter(weight_parts[2], "fsdp", scatter_dimension=0, tiled=True),
                lax.psum_scatter(weight_parts[3], "fsdp", scatter_dimension=1, tiled=True),
            ),
        )
    summed = lax.psum((gain_sums[0], gain_sums[1], gain_sums[2], gain_sums[3]), ("fsdp", "tp"))
    block_out = jnp.stack(outputs)[:, None]
    input_grad = jnp.stack(input_grads)[:, None]
    return (
        block_out,
        input_grad,
        summed[0],
        attn_grads[0],
        attn_grads[1],
        attn_grads[2],
        summed[2],
        summed[3],
        attn_grads[3],
        summed[1],
        expert_grads[0],
        expert_grads[1],
        expert_grads[2],
    )


MESH = pl.DeviceIdType.MESH
PLANE = 4
LANES = 128
MIB = 1 << 20


class Spot:
    def __init__(self, line, wide):
        self.line = line
        self.wide = wide
        self.planes = 4 if wide else 2
        index = lax.axis_index("fsdp")
        self.x = lax.axis_index("tp")
        self.z = lax.div(index, PLANE)
        self.y = lax.rem(lax.div(index, 2), 2)
        self.core = lax.rem(index, 2)

    def flips(self, core, first, second):
        if not self.wide:
            return first, 0
        return (1 - core) * first + core * second, core * first + (1 - core) * second

    def block(self, core, first, second, z):
        flip_y, flip_x = self.flips(core, first, second)
        y = self.y + flip_y * (1 - 2 * self.y)
        x = self.x + flip_x * (1 - 2 * self.x)
        return z * PLANE + y * 2 + core, x

    def device(self, kind):
        if kind == "right":
            return self.block(self.core, 0, 0, self.z + 1)
        if kind == "left":
            return self.block(self.core, 0, 0, self.z - 1)
        if kind == "core":
            return self.block(1 - self.core, 0, 0, self.z)
        return self.block(self.core, int(kind == "first"), int(kind == "second"), self.z)

    def kinds(self):
        return ("first", "second", "core") if self.wide else ("first", "core")

    def number(self, first, second, z):
        return (second * 2 + first) * self.line + z

    def order(self, step):
        if step == 0:
            return [(self.z, None, None)]
        return [
            (self.z - step, self.z - step >= 0, "right"),
            (self.z + step, self.z + step < self.line, "left"),
        ]

    def greet(self):
        barrier = pltpu.get_barrier_semaphore()

        def signal(kind):
            pl.semaphore_signal(barrier, inc=1, device_id=self.device(kind), device_id_type=MESH)

        for kind in self.kinds():
            signal(kind)
        when(self.z + 1 < self.line, lambda: signal("right"))
        when(self.z > 0, lambda: signal("left"))
        around = (self.z + 1 < self.line).astype(jnp.int32) + (self.z > 0).astype(jnp.int32)
        pl.semaphore_wait(barrier, len(self.kinds()) + around)


def when(condition, action):
    def run():
        action()

    if condition is None:
        run()
    else:
        pl.when(condition)(run)


def spread(spot, items, send, receive, local):
    line, z, core = spot.line, spot.z, spot.core
    seconds = (0, 1) if spot.wide else (0,)
    sends = {"right": 0, "left": 1, "first": 2, "second": 3, "core": 5}

    def copy(item, first, second, zz, kind, own=False):
        source, slot = items[item]
        place = slot(*spot.block(core, first, second, zz))
        number = spot.number(first, second, zz)
        arrival = {
            "right": number,
            "left": number,
            "first": spot.number(1, 0, zz),
            "second": spot.number(first, 1, zz),
            "core": spot.planes * line + number,
        }[kind]
        return pltpu.make_async_remote_copy(
            src_ref=source if own else place,
            dst_ref=place,
            send_sem=send.at[item, sends[kind] * line + number],
            recv_sem=receive.at[item, arrival],
            device_id=spot.device(kind),
            device_id_type=MESH,
        )

    def arrived(item, first, second, zz, other=False):
        source, slot = items[item]
        place = slot(*spot.block(1 - core if other else core, first, second, zz))
        number = spot.number(first, second, zz) + (spot.planes * line if other else 0)
        pltpu.make_async_remote_copy(
            src_ref=place,
            dst_ref=place,
            send_sem=send.at[item, 0],
            recv_sem=receive.at[item, number],
            device_id=spot.device("core"),
            device_id_type=MESH,
        ).wait_recv()

    every = range(len(items))
    mine = [
        pltpu.make_async_copy(source, slot(*spot.block(core, 0, 0, z)), local.at[item])
        for item, (source, slot) in enumerate(items)
    ]

    def along(step, zz, way):
        for item in every:
            if step:
                arrived(item, 0, 0, zz)
            own = step == 0
            if way != "left":
                when(z + 1 < line, lambda: copy(item, 0, 0, zz, "right", own).start())
            if way != "right":
                when(z > 0, lambda: copy(item, 0, 0, zz, "left", own).start())
            copy(item, 0, 0, zz, "first", own).start()
            if spot.wide:
                copy(item, 0, 0, zz, "second", own).start()
            copy(item, 0, 0, zz, "core", own).start()

    def firsts(zz):
        for item in every:
            arrived(item, 1, 0, zz)
            if spot.wide:
                copy(item, 1, 0, zz, "second").start()
            copy(item, 1, 0, zz, "core").start()

    def lasts(first, zz):
        for item in every:
            arrived(item, first, 1, zz)
            copy(item, first, 1, zz, "core").start()

    for step in range(line):
        for zz, valid, way in spot.order(step):
            when(valid, lambda: along(step, zz, way))
        if step == 0:
            for one in mine:
                one.start()
        if step >= 1:
            for zz, valid, _ in spot.order(step - 1):
                when(valid, lambda: firsts(zz))
        if step >= 2 and spot.wide:
            for zz, valid, _ in spot.order(step - 2):
                when(valid, lambda: lasts(0, zz))
    for zz, valid, _ in spot.order(line - 1):
        when(valid, lambda: firsts(zz))
    if spot.wide:
        for step in range(max(line - 2, 0), line):
            for zz, valid, _ in spot.order(step):
                when(valid, lambda: lasts(0, zz))
        for step in range(line):
            for zz, valid, _ in spot.order(step):
                when(valid, lambda: lasts(1, zz))

    for one in mine:
        one.wait()
    for item in every:
        for zz in range(line):
            when(
                jnp.logical_and(z + 1 < line, zz <= z),
                lambda: copy(item, 0, 0, zz, "right").wait_send(),
            )
            when(
                jnp.logical_and(z > 0, zz >= z),
                lambda: copy(item, 0, 0, zz, "left").wait_send(),
            )
            copy(item, 0, 0, zz, "first").wait_send()
            for second in seconds:
                for first in (0, 1):
                    if spot.wide and not second:
                        copy(item, first, 0, zz, "second").wait_send()
                    copy(item, first, second, zz, "core").wait_send()
                    arrived(item, first, second, zz, other=True)


def spread_count(line, wide):
    return (9 if wide else 7) * line, (8 if wide else 4) * line


def spread_rows_kernel(line, rows_ref, all_ref, send, receive, local):
    spot = Spot(line, True)
    spot.greet()
    items = [
        (rows_ref.at[batch], lambda block, half, batch=batch: all_ref.at[batch, block, half])
        for batch in range(rows_ref.shape[0])
    ]
    spread(spot, items, send, receive, local)


def spread_rows(rows, fsdp_count):
    line = fsdp_count // PLANE
    batch, count, width = rows.shape
    sends, receives = spread_count(line, True)
    return pl.pallas_call(
        functools.partial(spread_rows_kernel, line),
        out_shape=jax.ShapeDtypeStruct((batch, fsdp_count, 2, count, width), rows.dtype),
        in_specs=[pl.BlockSpec(memory_space=pl.ANY)],
        out_specs=pl.BlockSpec(memory_space=pl.ANY),
        scratch_shapes=[
            pltpu.SemaphoreType.DMA((batch, sends)),
            pltpu.SemaphoreType.DMA((batch, receives)),
            pltpu.SemaphoreType.DMA((batch,)),
        ],
        compiler_params=pltpu.CompilerParams(collective_id=0, has_side_effects=True),
    )(rows)


def spread_weights_kernel(line, in_ref, out_ref, in_all, out_all, send, receive, local):
    spot = Spot(line, False)
    spot.greet()
    depth, width = in_ref.shape[0], out_ref.shape[1]
    items = [
        (in_ref, lambda block, half: in_all.at[pl.ds(pl.multiple_of(block * depth, depth), depth)]),
        (
            out_ref,
            lambda block, half: out_all.at[:, pl.ds(pl.multiple_of(block * width, width), width)],
        ),
    ]
    spread(spot, items, send, receive, local)


def spread_weights(weight_in, weight_out, fsdp_count):
    line = fsdp_count // PLANE
    sends, receives = spread_count(line, False)
    return pl.pallas_call(
        functools.partial(spread_weights_kernel, line),
        out_shape=(
            jax.ShapeDtypeStruct((weight_in.shape[0] * fsdp_count, weight_in.shape[1]), jnp.bfloat16),
            jax.ShapeDtypeStruct((weight_out.shape[0], weight_out.shape[1] * fsdp_count), jnp.bfloat16),
        ),
        in_specs=[pl.BlockSpec(memory_space=pl.ANY)] * 2,
        out_specs=(pl.BlockSpec(memory_space=pl.ANY),) * 2,
        scratch_shapes=[
            pltpu.SemaphoreType.DMA((2, sends)),
            pltpu.SemaphoreType.DMA((2, receives)),
            pltpu.SemaphoreType.DMA((2,)),
        ],
        compiler_params=pltpu.CompilerParams(collective_id=1, has_side_effects=True),
    )(weight_in, weight_out)


def add_rows(target, sources):
    count = target.shape[0]

    def body(step, _):
        rows = pl.ds(pl.multiple_of(step * 16, 16), 16)
        total = sources[0][rows, :].astype(jnp.float32)
        for source in sources[1:]:
            total = total + source[rows, :].astype(jnp.float32)
        target[rows, :] = total.astype(target.dtype)
        return 0

    lax.fori_loop(0, count // 16, body, 0)


def collect(spot, items, send, receive, local):
    line, z, core = spot.line, spot.z, spot.core
    sides = (1, 0) if spot.wide else (0,)
    every = range(len(items))
    blocks = spot.planes * line
    base = {"core": 0, "second": blocks, "first": blocks + 2 * line}
    base["right"] = base["first"] + line
    base["left"] = base["right"] + line

    def copy(item, kind, first, second, zz):
        part, _, own, cores, seconds, firsts, rights, lefts = items[item]
        number = spot.number(first, second, zz)
        source = own.at[number]
        if kind == "core":
            source, place, index = part(*spot.block(1 - core, first, second, zz)), cores.at[number], number
        elif kind == "second":
            index = first * line + zz
            place = seconds.at[index]
        else:
            index = zz
            place = {"first": firsts, "right": rights, "left": lefts}[kind].at[zz]
        return pltpu.make_async_remote_copy(
            src_ref=source,
            dst_ref=place,
            send_sem=send.at[item, base[kind] + index],
            recv_sem=receive.at[item, base[kind] + index],
            device_id=spot.device(kind),
            device_id_type=MESH,
        )

    def load(item, first, second, zz):
        part, own = items[item][0], items[item][2]
        number = spot.number(first, second, zz)
        return pltpu.make_async_copy(
            part(*spot.block(core, first, second, zz)), own.at[number], local.at[item, number]
        )

    def ordered(action):
        for step in reversed(range(line)):
            for zz, valid, _ in spot.order(step):
                when(valid, lambda: each(action, zz))

    def each(action, zz):
        for item in every:
            action(item, zz)

    def fetch(first, second):
        def action(item, zz):
            copy(item, "core", first, second, zz).start()
            load(item, first, second, zz).start()

        ordered(action)

    for second in sides:
        for first in (1, 0):
            fetch(first, second)

    def summed(item, first, second, zz, target=None, extra=()):
        _, _, own, cores, seconds, firsts, _, _ = items[item]
        number = spot.number(first, second, zz)
        load(item, first, second, zz).wait()
        copy(item, "core", first, second, zz).wait_recv()
        sources = [own.at[number], cores.at[number]]
        if spot.wide and not second:
            copy(item, "second", first, 0, zz).wait_recv()
            sources.append(seconds.at[first * line + zz])
        if not second and not first:
            copy(item, "first", 0, 0, zz).wait_recv()
            sources.append(firsts.at[zz])
        add_rows(own.at[number] if target is None else target, sources + list(extra))

    if spot.wide:
        for first in (1, 0):

            def to_second(item, zz):
                summed(item, first, 1, zz)
                pltpu.make_async_remote_copy(
                    src_ref=items[item][2].at[spot.number(first, 1, zz)],
                    dst_ref=items[item][4].at[first * line + zz],
                    send_sem=send.at[item, base["second"] + first * line + zz],
                    recv_sem=receive.at[item, base["second"] + first * line + zz],
                    device_id=spot.device("second"),
                    device_id_type=MESH,
                ).start()

            ordered(to_second)

    def first_copy(item, zz):
        return pltpu.make_async_remote_copy(
            src_ref=items[item][2].at[spot.number(1, 0, zz)],
            dst_ref=items[item][5].at[zz],
            send_sem=send.at[item, base["first"] + zz],
            recv_sem=receive.at[item, base["first"] + zz],
            device_id=spot.device("first"),
            device_id_type=MESH,
        )

    def to_first(item, zz):
        summed(item, 1, 0, zz)
        first_copy(item, zz).start()

    ordered(to_first)

    for step in reversed(range(1, line)):
        for zz, valid, way in spot.order(step):
            kind = "left" if way == "right" else "right"

            def onward(kind=kind, zz=zz):
                behind = z > 0 if kind == "right" else z + 1 < line
                for item in every:
                    incoming = items[item][6 if kind == "right" else 7].at[zz]

                    def with_incoming():
                        copy(item, kind, 0, 0, zz).wait_recv()
                        summed(item, 0, 0, zz, extra=[incoming])

                    when(behind, with_incoming)
                    when(jnp.logical_not(behind), lambda: summed(item, 0, 0, zz))
                    copy(item, kind, 0, 0, zz).start()

            when(valid, onward)

    def finish(extra):
        for item in every:
            for kind in extra:
                copy(item, kind, 0, 0, z).wait_recv()
            summed(
                item, 0, 0, z, target=items[item][1],
                extra=[items[item][6 if kind == "right" else 7].at[z] for kind in extra],
            )

    when(z == 0, lambda: finish(["left"]))
    when(z == line - 1, lambda: finish(["right"]))
    when(jnp.logical_and(z > 0, z < line - 1), lambda: finish(["right", "left"]))

    for item in every:
        for zz in range(line):
            when(zz > z, lambda: copy(item, "right", 0, 0, zz).wait_send())
            when(zz < z, lambda: copy(item, "left", 0, 0, zz).wait_send())
            first_copy(item, zz).wait_send()
            for first in (0, 1):
                if spot.wide:
                    copy(item, "second", first, 0, zz).wait_send()
                for second in sides:
                    copy(item, "core", first, second, zz).wait_send()


def collect_scratch(line, wide, shape):
    planes = 4 if wide else 2
    counts = (planes * line, planes * line, 2 * line if wide else 1, line, line, line)
    return [pltpu.VMEM((count, *shape), jnp.bfloat16) for count in counts]


def collect_count(line, wide):
    return (4 if wide else 2) * line + 5 * line


def collect_rows_kernel(line, part_ref, total_ref, *scratch):
    *buffers, send, receive, local = scratch
    spot = Spot(line, True)
    spot.greet()
    items = [(lambda block, half: part_ref.at[block, half], total_ref, *buffers)]
    collect(spot, items, send, receive, local)


def collect_rows(part, fsdp_count):
    line = fsdp_count // PLANE
    shape = part.shape[2:]
    count = collect_count(line, True)
    return pl.pallas_call(
        functools.partial(collect_rows_kernel, line),
        out_shape=jax.ShapeDtypeStruct(shape, jnp.float32),
        in_specs=[pl.BlockSpec(memory_space=pl.ANY)],
        out_specs=pl.BlockSpec(memory_space=pltpu.VMEM),
        scratch_shapes=collect_scratch(line, True, shape)
        + [
            pltpu.SemaphoreType.DMA((1, count)),
            pltpu.SemaphoreType.DMA((1, count)),
            pltpu.SemaphoreType.DMA((1, 4 * line)),
        ],
        compiler_params=pltpu.CompilerParams(
            collective_id=2, has_side_effects=True, vmem_limit_bytes=48 * MIB
        ),
    )(part)


def collect_weights_kernel(line, in_part, out_part, in_total, out_total, *scratch):
    buffers, (send, receive, local) = scratch[:-3], scratch[-3:]
    spot = Spot(line, False)
    spot.greet()
    depth, width = in_total.shape[0], out_total.shape[1]
    items = [
        (
            lambda block, half: in_part.at[pl.ds(pl.multiple_of(block * depth, depth), depth)],
            in_total,
            *buffers[:6],
        ),
        (
            lambda block, half: out_part.at[:, pl.ds(pl.multiple_of(block * width, width), width)],
            out_total,
            *buffers[6:],
        ),
    ]
    collect(spot, items, send, receive, local)


def collect_weights(in_part, out_part, fsdp_count):
    line = fsdp_count // PLANE
    in_shape = (in_part.shape[0] // fsdp_count, in_part.shape[1])
    out_shape = (out_part.shape[0], out_part.shape[1] // fsdp_count)
    count = collect_count(line, False)
    return pl.pallas_call(
        functools.partial(collect_weights_kernel, line),
        out_shape=(
            jax.ShapeDtypeStruct(in_shape, jnp.float32),
            jax.ShapeDtypeStruct(out_shape, jnp.float32),
        ),
        in_specs=[pl.BlockSpec(memory_space=pl.ANY)] * 2,
        out_specs=(pl.BlockSpec(memory_space=pltpu.VMEM),) * 2,
        scratch_shapes=collect_scratch(line, False, in_shape)
        + collect_scratch(line, False, out_shape)
        + [
            pltpu.SemaphoreType.DMA((2, count)),
            pltpu.SemaphoreType.DMA((2, count)),
            pltpu.SemaphoreType.DMA((2, 2 * line)),
        ],
        compiler_params=pltpu.CompilerParams(
            collective_id=3, has_side_effects=True, vmem_limit_bytes=56 * MIB
        ),
    )(in_part, out_part)


TRANSPOSED_LEFT = (((0,), (0,)), ((), ()))
TRANSPOSED_RIGHT = (((1,), (1,)), ((), ()))


def experts_kernel(
    group,
    slots,
    x_ref,
    c_ref,
    info_ref,
    hidden_ref,
    down_ref,
    out_ref,
    back_ref,
    xe_ref,
    ce_ref,
    act_ref,
    dgate_ref,
    dup_ref,
    picks,
    weigh,
    rows,
    hidden_grads,
):
    member = pl.program_id(1)
    length, width = x_ref.shape[1:]
    units = down_ref.shape[1]

    @pl.when(jnp.logical_and(pl.program_id(0) == 0, member == 0))
    def _():
        rows[...] = jnp.zeros_like(rows)

    info = info_ref[0]
    lanes = lax.broadcasted_iota(jnp.int32, (length, 2 * LANES), 1)
    ranks = info.astype(jnp.int32)
    lower = lanes < LANES
    hot = jnp.where(lower, ranks[:, 0:1], ranks[:, 1:2] + LANES) == lanes
    hot = jnp.logical_and(hot, jnp.where(lower, ranks[:, 0:1], ranks[:, 1:2]) >= 0)
    pick = hot.astype(jnp.float32).astype(jnp.bfloat16)
    picks[member] = pick
    shares = jnp.where(hot, jnp.where(lower, info[:, 2:3], info[:, 3:4]), 0.0)
    column = jnp.sum(shares, axis=0, keepdims=True)
    column = jnp.transpose(jnp.broadcast_to(column, (LANES, 2 * LANES)))
    here = pl.ds(pl.multiple_of(member * slots, 16), slots)
    for expert in range(2):
        weigh[expert, here, :] = column[expert * LANES : expert * LANES + slots]
    for source, target in ((x_ref, xe_ref), (c_ref, ce_ref)):
        for start in range(0, width, 512):
            chosen = lax.dot_general(
                pick,
                source[0, :, start : start + 512],
                TRANSPOSED_LEFT,
                preferred_element_type=jnp.float32,
            ).astype(jnp.bfloat16)
            for expert in range(2):
                target[expert, here, start : start + 512] = chosen[
                    expert * LANES : expert * LANES + slots
                ]

    @pl.when(member == group - 1)
    def _():
        def keep(expert, product, start):
            for one in range(group):
                rows[one, expert * LANES : expert * LANES + slots, start : start + 512] = product[
                    one * slots : (one + 1) * slots
                ].astype(jnp.bfloat16)

        def combine(target):
            for one in range(group):
                for start in range(0, width, 512):
                    target[one, :, start : start + 512] = jnp.dot(
                        picks[one],
                        rows[one, :, start : start + 512],
                        preferred_element_type=jnp.float32,
                    ).astype(jnp.bfloat16)

        for expert in range(2):
            hidden = jnp.dot(xe_ref[expert], hidden_ref[expert], preferred_element_type=jnp.float32)
            gate, up = hidden[:, :units], hidden[:, units:]
            sigmoid = jax.nn.sigmoid(gate)
            silu = gate * sigmoid
            scale = weigh[expert, :, 0:1]
            act = (silu * up * scale).astype(jnp.bfloat16)
            act_ref[expert] = act
            act_grads = scale * lax.dot_general(
                ce_ref[expert],
                down_ref[expert],
                TRANSPOSED_RIGHT,
                preferred_element_type=jnp.float32,
            )
            gate_grads = act_grads * up * (sigmoid * (1.0 + gate * (1.0 - sigmoid)))
            up_grads = act_grads * silu
            dgate_ref[expert] = gate_grads.astype(jnp.bfloat16)
            dup_ref[expert] = up_grads.astype(jnp.bfloat16)
            hidden_grads[expert, :, :units] = gate_grads.astype(jnp.bfloat16)
            hidden_grads[expert, :, units:] = up_grads.astype(jnp.bfloat16)
            for start in range(0, width, 512):
                keep(
                    expert,
                    jnp.dot(
                        act,
                        down_ref[expert, :, start : start + 512],
                        preferred_element_type=jnp.float32,
                    ),
                    start,
                )
        combine(out_ref)
        for expert in range(2):
            for start in range(0, width, 512):
                keep(
                    expert,
                    lax.dot_general(
                        hidden_grads[expert],
                        hidden_ref[expert, start : start + 512, :],
                        TRANSPOSED_RIGHT,
                        preferred_element_type=jnp.float32,
                    ),
                    start,
                )
        combine(back_ref)


def run_experts(rows_all, cot_all, info, hidden_weight, down_weight, capacity):
    sequences, length, width = rows_all.shape
    units = down_weight.shape[1]
    group = 4
    slots = -(-capacity // 16) * 16
    count = sequences * slots
    whole = lambda shape: pl.BlockSpec(
        shape, lambda i, j: (0,) * len(shape), pipeline_mode=pl.Buffered(1)
    )
    one = lambda last: pl.BlockSpec((1, length, last), lambda i, j: (i * group + j, 0, 0))
    grouped = pl.BlockSpec((group, length, width), lambda i, j: (i, 0, 0))
    slotted = lambda last: pl.BlockSpec((2, group * slots, last), lambda i, j: (0, i, 0))
    shape = lambda *dims: jax.ShapeDtypeStruct(dims, jnp.bfloat16)
    return pl.pallas_call(
        functools.partial(experts_kernel, group, slots),
        grid=(sequences // group, group),
        out_shape=(
            shape(sequences, length, width),
            shape(sequences, length, width),
            shape(2, count, width),
            shape(2, count, width),
            shape(2, count, units),
            shape(2, count, units),
            shape(2, count, units),
        ),
        in_specs=[
            one(width),
            one(width),
            one(info.shape[-1]),
            whole(hidden_weight.shape),
            whole(down_weight.shape),
        ],
        out_specs=(
            grouped,
            grouped,
            slotted(width),
            slotted(width),
            slotted(units),
            slotted(units),
            slotted(units),
        ),
        scratch_shapes=[
            pltpu.VMEM((group, length, 2 * LANES), jnp.bfloat16),
            pltpu.VMEM((2, group * slots, LANES), jnp.float32),
            pltpu.VMEM((group, 2 * LANES, width), jnp.bfloat16),
            pltpu.VMEM((2, group * slots, 2 * units), jnp.bfloat16),
        ],
        compiler_params=pltpu.CompilerParams(vmem_limit_bytes=62 * MIB),
    )(rows_all, cot_all, info, hidden_weight, down_weight)


def slot_info(routes, gates, local_experts):
    batch, _, length, top = routes.shape
    fsdp_count = lax.axis_size("fsdp")
    packed = jnp.concatenate([routes[:, 0].astype(jnp.float32), gates[:, 0]], axis=-1)
    packed = lax.all_gather(packed, "fsdp", axis=1)
    names = packed[..., :top, None].astype(jnp.int32)
    experts = lax.axis_index("fsdp") * local_experts + jnp.arange(local_experts, dtype=jnp.int32)
    same = names == experts
    hot = jnp.any(same, axis=3)
    shares = jnp.sum(jnp.where(same, packed[..., top:, None], 0.0), axis=3)
    position = jnp.arange(length)
    lower = (position[None, :] < position[:, None]).astype(jnp.bfloat16)
    rank = jnp.einsum(
        "pq,bsqe->bspe", lower, hot.astype(jnp.bfloat16), preferred_element_type=jnp.float32
    )
    rank = jnp.where(hot, rank, -1.0)
    return jnp.concatenate([rank, shares], axis=-1).reshape(
        batch * fsdp_count, length, 2 * local_experts
    )


def gathered_layer(
    tokens,
    cotangent,
    norm1_gain,
    w_query,
    key_projection_weight,
    value_projection_weight,
    query_gain,
    key_gain,
    w_out,
    norm2_gain,
    w_gate,
    w_up,
    w_down,
    routes,
    gates,
):
    batch_count = tokens.shape[0]
    model_width = tokens.shape[3]
    sequence_length = routes.shape[2]
    half_length = tokens.shape[2]
    top_count = routes.shape[3]
    head_features = query_gain.shape[0]
    local_experts = w_gate.shape[0]
    fsdp_count = lax.axis_size("fsdp")
    all_experts = local_experts * fsdp_count
    capacity = 7 * top_count * sequence_length // (6 * all_experts)
    query_width = w_query.shape[1]
    kv_width = key_projection_weight.shape[1]
    query_heads = query_width // head_features
    kv_heads = kv_width // head_features
    group_size = query_heads // kv_heads
    score_scale = head_features ** (-0.5)
    cosine_table, sine_values = rotary_tables(sequence_length, head_features)
    block_ids = jnp.arange(sequence_length, dtype=jnp.int32) // BLOCK
    visible = (block_ids[None, :] <= block_ids[:, None])[None, None]
    first_gain = norm1_gain.astype(jnp.float32)
    second_gain = norm2_gain.astype(jnp.float32)
    query_factor_scale = query_gain.astype(jnp.float32)
    key_scale = key_gain.astype(jnp.float32)

    def masked_scores(query_fourfold, key_rows):
        raw_scores = (
            jnp.einsum(
                "qcgd,kcd->cgqk", query_fourfold, key_rows, preferred_element_type=jnp.float32
            )
            * score_scale
        )
        return jnp.where(visible, raw_scores, MASKED)

    def prep_heads(projected, gain_row):
        return prepare_heads(projected, gain_row, cosine_table, sine_values)

    info = slot_info(routes, gates, local_experts)
    weight_in = jnp.concatenate([w_query, key_projection_weight, value_projection_weight], axis=1)
    in_full, out_full = spread_weights(weight_in, w_out, fsdp_count)
    cot_all = spread_rows(cotangent[:, 0], fsdp_count)

    kept = []
    for batch_index in range(batch_count):
        own_rows = tokens[batch_index, 0].astype(jnp.float32)
        first_normed = rms_scale(own_rows, first_gain).astype(jnp.bfloat16)
        normed_all = lax.all_gather(first_normed, "tp", axis=0, tiled=True)
        projected = jnp.dot(normed_all, in_full, preferred_element_type=jnp.float32)
        query_projected = projected[:, :query_width].reshape(
            sequence_length, query_heads, head_features
        )
        key_projected = projected[:, query_width : query_width + kv_width].reshape(
            sequence_length, kv_heads, head_features
        )
        value_row_list = (
            projected[:, query_width + kv_width :]
            .astype(jnp.bfloat16)
            .reshape(sequence_length, kv_heads, head_features)
        )
        query_rot = prep_heads(query_projected, query_factor_scale).astype(jnp.bfloat16)
        key_rot = prep_heads(key_projected, key_scale).astype(jnp.bfloat16)
        query_fourfold = query_rot.reshape(sequence_length, kv_heads, group_size, head_features)
        scores = masked_scores(query_fourfold, key_rot)
        row_max = jnp.max(scores, axis=-1, keepdims=True)
        exp_scores = jnp.exp(scores - row_max)
        totals = jnp.sum(exp_scores, axis=-1, keepdims=True)
        log_total = row_max + jnp.log(totals)
        prob_rows = (exp_scores / totals).astype(jnp.bfloat16)
        context = (
            jnp.einsum(
                "cgqk,kcd->qcgd", prob_rows, value_row_list, preferred_element_type=jnp.float32
            )
            .astype(jnp.bfloat16)
            .reshape(sequence_length, query_heads * head_features)
        )
        attn_own = lax.psum_scatter(
            jnp.dot(context, out_full, preferred_element_type=jnp.float32).astype(jnp.bfloat16),
            "tp",
            scatter_dimension=0,
            tiled=True,
        ).astype(jnp.float32)
        hidden_own = own_rows + attn_own
        second_normed = rms_scale(hidden_own, second_gain).astype(jnp.bfloat16)
        kept.append(
            (
                own_rows,
                normed_all,
                query_projected,
                key_projected,
                value_row_list,
                query_fourfold,
                key_rot,
                log_total,
                context,
                hidden_own,
                second_normed,
            )
        )

    normed_two = spread_rows(jnp.stack([items[-1] for items in kept]), fsdp_count)
    flat = (batch_count * fsdp_count, sequence_length, model_width)
    out_part, back_part, expert_rows, cot_rows, act_rows, gate_rows, up_rows = run_experts(
        normed_two.reshape(flat),
        cot_all.reshape(flat),
        info,
        jnp.concatenate([w_gate, w_up], axis=2),
        w_down,
        capacity,
    )
    blocks = (batch_count, fsdp_count, 2, half_length, model_width)
    out_part, back_part = out_part.reshape(blocks), back_part.reshape(blocks)
    moe_own = [collect_rows(out_part[i], fsdp_count) for i in range(batch_count)]
    normed_own = [collect_rows(back_part[i], fsdp_count) for i in range(batch_count)]
    expert_grads = (
        jnp.einsum("erd,erf->edf", expert_rows, gate_rows, preferred_element_type=jnp.float32),
        jnp.einsum("erd,erf->edf", expert_rows, up_rows, preferred_element_type=jnp.float32),
        jnp.einsum("erf,erd->efd", act_rows, cot_rows, preferred_element_type=jnp.float32),
    )

    outputs = []
    input_grads = []
    gain_sums = None
    in_grad, out_grad = 0.0, 0.0
    for batch_index in range(batch_count):
        (
            own_rows,
            normed_all,
            query_projected,
            key_projected,
            value_row_list,
            query_fourfold,
            key_rot,
            log_total,
            context,
            hidden_own,
            _,
        ) = kept[batch_index]
        own_cot = cotangent[batch_index, 0]
        outputs.append((hidden_own + moe_own[batch_index]).astype(jnp.bfloat16))
        _, second_back = jax.vjp(rms_scale, hidden_own, second_gain)
        hidden_part, second_gain_grad = second_back(normed_own[batch_index])
        hidden_grad = own_cot.astype(jnp.float32) + hidden_part
        attn_grad_all = lax.all_gather(hidden_grad.astype(jnp.bfloat16), "tp", axis=0, tiled=True)
        out_grad = out_grad + jnp.einsum(
            "th,td->hd", context, attn_grad_all, preferred_element_type=jnp.float32
        )
        context_grad = (
            jnp.einsum("td,hd->th", attn_grad_all, out_full, preferred_element_type=jnp.float32)
            .astype(jnp.bfloat16)
            .reshape(sequence_length, kv_heads, group_size, head_features)
        )
        exp_again = jnp.exp(masked_scores(query_fourfold, key_rot) - log_total)
        probs_again = exp_again.astype(jnp.bfloat16)
        prob_grads = jnp.einsum(
            "qcgd,kcd->cgqk", context_grad, value_row_list, preferred_element_type=jnp.float32
        )
        value_grads = (
            jnp.einsum(
                "cgqk,qcgd->kcd", probs_again, context_grad, preferred_element_type=jnp.float32
            )
            .astype(jnp.bfloat16)
            .reshape(sequence_length, kv_width)
        )
        score_grads = (
            exp_again * (prob_grads - jnp.sum(exp_again * prob_grads, axis=-1, keepdims=True))
        ).astype(jnp.bfloat16)
        query_rot_grads = (
            jnp.einsum("cgqk,kcd->qcgd", score_grads, key_rot, preferred_element_type=jnp.float32)
            * score_scale
        ).reshape(sequence_length, query_heads, head_features)
        key_rot_grads = (
            jnp.einsum(
                "cgqk,qcgd->kcd", score_grads, query_fourfold, preferred_element_type=jnp.float32
            )
            * score_scale
        )
        _, query_back = jax.vjp(prep_heads, query_projected, query_factor_scale)
        query_proj_grads, query_gain_grad = query_back(query_rot_grads)
        _, key_back = jax.vjp(prep_heads, key_projected, key_scale)
        key_proj_grads, key_gain_grad = key_back(key_rot_grads)
        projected_grads = jnp.concatenate(
            [
                query_proj_grads.astype(jnp.bfloat16).reshape(sequence_length, query_width),
                key_proj_grads.astype(jnp.bfloat16).reshape(sequence_length, kv_width),
                value_grads,
            ],
            axis=1,
        )
        first_normed_grads = jnp.einsum(
            "tq,dq->td", projected_grads, in_full, preferred_element_type=jnp.float32
        )
        in_grad = in_grad + jnp.einsum(
            "td,tq->dq", normed_all, projected_grads, preferred_element_type=jnp.float32
        )
        first_own = lax.psum_scatter(
            first_normed_grads.astype(jnp.bfloat16), "tp", scatter_dimension=0, tiled=True
        ).astype(jnp.float32)
        _, first_back = jax.vjp(rms_scale, own_rows, first_gain)
        row_part, first_gain_grad = first_back(first_own)
        input_grads.append((hidden_grad + row_part).astype(jnp.bfloat16))
        new_sums = (first_gain_grad, second_gain_grad, query_gain_grad, key_gain_grad)
        gain_sums = new_sums if gain_sums is None else jax.tree.map(jnp.add, gain_sums, new_sums)
    in_sum, out_sum = collect_weights(
        in_grad.astype(jnp.bfloat16), out_grad.astype(jnp.bfloat16), fsdp_count
    )
    summed = lax.psum(gain_sums, ("fsdp", "tp"))
    return (
        jnp.stack(outputs)[:, None],
        jnp.stack(input_grads)[:, None],
        summed[0],
        in_sum[:, :query_width],
        in_sum[:, query_width : query_width + kv_width],
        in_sum[:, query_width + kv_width :],
        summed[2],
        summed[3],
        out_sum,
        summed[1],
        expert_grads[0],
        expert_grads[1],
        expert_grads[2],
    )


def shards(*arrays):
    tokens, routes, w_gate = arrays[0], arrays[13], arrays[10]
    fsdp_count = lax.axis_size("fsdp")
    gathered = fsdp_count * routes.shape[2] * tokens.shape[3] * 2
    fits = gathered <= 24 * MIB and fsdp_count % PLANE == 0 and lax.axis_size("tp") == 2
    if fits and w_gate.shape[0] == 2:
        return gathered_layer(*arrays)
    return exchanged_layer(*arrays)


def solution(mesh):
    in_specs = (
        P(None, "fsdp", "tp", None),
        P(None, "fsdp", "tp", None),
        P(),
        P("fsdp", "tp"),
        P("fsdp", "tp"),
        P("fsdp", "tp"),
        P(),
        P(),
        P("tp", "fsdp"),
        P(),
        P("fsdp", None, "tp"),
        P("fsdp", None, "tp"),
        P("fsdp", "tp", None),
        P(None, "fsdp", None, None),
        P(None, "fsdp", None, None),
    )
    out_specs = (
        P(None, "fsdp", "tp", None),
        P(None, "fsdp", "tp", None),
        P(),
        P("fsdp", "tp"),
        P("fsdp", "tp"),
        P("fsdp", "tp"),
        P(),
        P(),
        P("tp", "fsdp"),
        P(),
        P("fsdp", None, "tp"),
        P("fsdp", None, "tp"),
        P("fsdp", "tp", None),
    )
    return jax.shard_map(shards, mesh=mesh, in_specs=in_specs, out_specs=out_specs, check_vma=False)
```

```python
import functools

import jax
import jax.numpy as jnp
from jax import lax
from jax.experimental import pallas as pl
from jax.experimental.pallas import tpu as pltpu
from jax.sharding import PartitionSpec as P

BLOCK = 256


EPSILON = 1e-06
ROPE_BASE = 1000000.0
MASKED = -1e30
TILE_PICKS = 128


def rms_scale(row_block, gain_row):
    return (
        row_block
        * lax.rsqrt(jnp.mean(row_block * row_block, axis=-1, keepdims=True) + EPSILON)
        * gain_row
    )


def rotary_tables(sequence_length, head_width):
    half_width = head_width // 2
    inverse = ROPE_BASE ** (-2.0 * jnp.arange(half_width, dtype=jnp.float32) / head_width)
    angles = jnp.arange(sequence_length, dtype=jnp.float32)[:, None] * inverse[None, :]
    cosine_table = jnp.concatenate([jnp.cos(angles), jnp.cos(angles)], axis=-1)[:, None, :]
    sine_values = jnp.concatenate([jnp.sin(angles), jnp.sin(angles)], axis=-1)[:, None, :]
    return (cosine_table, sine_values)


def rotate(head_rows, cosine_table, sine_values):
    half_width = head_rows.shape[-1] // 2
    turned = jnp.concatenate([-head_rows[..., half_width:], head_rows[..., :half_width]], axis=-1)
    return head_rows * cosine_table + turned * sine_values


def prepare_heads(projected, gain_row, cosine_table, sine_values):
    return rotate(rms_scale(projected, gain_row), cosine_table, sine_values)


def swiglu(gate_act, up_act):
    return jax.nn.silu(gate_act) * up_act


def slot_tables(route_rows, gate_rows, expert_count, capacity):
    sequence_length = route_rows.shape[0]
    top_count = route_rows.shape[1]
    pick_count = sequence_length * top_count
    tile_count = pick_count // TILE_PICKS
    flat_routes = route_rows.reshape(-1)
    onehot = (flat_routes[:, None] == jnp.arange(expert_count, dtype=jnp.int32)[None, :]).astype(
        jnp.bfloat16
    )
    tiles = onehot.reshape(tile_count, TILE_PICKS, expert_count)
    positions = jnp.arange(TILE_PICKS, dtype=jnp.int32)
    lower = (positions[None, :] < positions[:, None]).astype(jnp.bfloat16)
    within = jnp.einsum("ij,bje->bie", lower, tiles, preferred_element_type=jnp.float32)
    tile_totals = jnp.sum(tiles.astype(jnp.float32), axis=1)
    offsets = jnp.cumsum(tile_totals, axis=0) - tile_totals
    before = within + offsets[:, None, :]
    slot_rank = jnp.sum(before * tiles.astype(jnp.float32), axis=-1).reshape(-1).astype(jnp.int32)
    slot_index = flat_routes * capacity + slot_rank
    pick_ids = jnp.arange(pick_count, dtype=jnp.int32) // top_count
    slot_owner = (
        jnp.full((expert_count * capacity,), sequence_length, jnp.int32)
        .at[slot_index]
        .set(pick_ids)
    )
    slot_weight = (
        jnp.zeros((expert_count * capacity,), jnp.float32).at[slot_index].set(gate_rows.reshape(-1))
    )
    return (slot_index, slot_owner, slot_weight)


def exchanged_layer(
    tokens,
    cotangent,
    norm1_gain,
    w_query,
    key_projection_weight,
    value_projection_weight,
    query_gain,
    key_gain,
    w_out,
    norm2_gain,
    w_gate,
    w_up,
    w_down,
    routes,
    gates,
):
    batch_count = tokens.shape[0]
    model_width = tokens.shape[3]
    sequence_length = routes.shape[2]
    top_count = routes.shape[3]
    head_features = query_gain.shape[0]
    local_experts = w_gate.shape[0]
    fsdp_count = lax.axis_size("fsdp")
    all_experts = local_experts * fsdp_count
    capacity = 7 * top_count * sequence_length // (6 * all_experts)
    query_heads = w_query.shape[1] // head_features
    kv_heads = key_projection_weight.shape[1] // head_features
    group_size = query_heads // kv_heads
    score_scale = head_features ** (-0.5)
    cosine_table, sine_values = rotary_tables(sequence_length, head_features)
    block_ids = jnp.arange(sequence_length, dtype=jnp.int32) // BLOCK
    visible = (block_ids[None, :] <= block_ids[:, None])[None, None]
    first_gain = norm1_gain.astype(jnp.float32)
    second_gain = norm2_gain.astype(jnp.float32)
    query_factor_scale = query_gain.astype(jnp.float32)
    key_scale = key_gain.astype(jnp.float32)
    zero_row = jnp.zeros((1, model_width), jnp.bfloat16)
    buffer_shape = (fsdp_count, local_experts, capacity, model_width)

    def masked_scores(query_fourfold, key_rows):
        raw_scores = (
            jnp.einsum(
                "qcgd,kcd->cgqk", query_fourfold, key_rows, preferred_element_type=jnp.float32
            )
            * score_scale
        )
        return jnp.where(visible, raw_scores, MASKED)

    def prep_heads(projected, gain_row):
        return prepare_heads(projected, gain_row, cosine_table, sine_values)

    gain_sums = (
        jnp.zeros((model_width,), jnp.float32),
        jnp.zeros((model_width,), jnp.float32),
        jnp.zeros((head_features,), jnp.float32),
        jnp.zeros((head_features,), jnp.float32),
    )
    expert_grads = (
        jnp.zeros(w_gate.shape, jnp.float32),
        jnp.zeros(w_up.shape, jnp.float32),
        jnp.zeros(w_down.shape, jnp.float32),
    )
    attn_grads = tuple(
        (
            jnp.zeros(weight_part.shape, jnp.float32)
            for weight_part in (w_query, key_projection_weight, value_projection_weight, w_out)
        )
    )
    outputs = []
    input_grads = []
    for batch_index in range(batch_count):
        query_full, key_full, value_full, out_full = (
            lax.all_gather(w_query, "fsdp", axis=0, tiled=True),
            lax.all_gather(key_projection_weight, "fsdp", axis=0, tiled=True),
            lax.all_gather(value_projection_weight, "fsdp", axis=0, tiled=True),
            lax.all_gather(w_out, "fsdp", axis=1, tiled=True),
        )
        own_rows = tokens[batch_index, 0].astype(jnp.float32)
        own_cot = cotangent[batch_index, 0]
        route_rows = routes[batch_index, 0]
        gate_rows = gates[batch_index, 0]
        first_normed = rms_scale(own_rows, first_gain).astype(jnp.bfloat16)
        normed_all = lax.all_gather(first_normed, "tp", axis=0, tiled=True)
        query_projected = jnp.dot(
            normed_all, query_full, preferred_element_type=jnp.float32
        ).reshape(sequence_length, query_heads, head_features)
        key_projected = jnp.dot(normed_all, key_full, preferred_element_type=jnp.float32).reshape(
            sequence_length, kv_heads, head_features
        )
        value_row_list = (
            jnp.dot(normed_all, value_full, preferred_element_type=jnp.float32)
            .astype(jnp.bfloat16)
            .reshape(sequence_length, kv_heads, head_features)
        )
        query_rot = prep_heads(query_projected, query_factor_scale).astype(jnp.bfloat16)
        key_rot = prep_heads(key_projected, key_scale).astype(jnp.bfloat16)
        query_fourfold = query_rot.reshape(sequence_length, kv_heads, group_size, head_features)
        scores = masked_scores(query_fourfold, key_rot)
        row_max = jnp.max(scores, axis=-1, keepdims=True)
        exp_scores = jnp.exp(scores - row_max)
        totals = jnp.sum(exp_scores, axis=-1, keepdims=True)
        log_total = row_max + jnp.log(totals)
        prob_rows = (exp_scores / totals).astype(jnp.bfloat16)
        context = (
            jnp.einsum(
                "cgqk,kcd->qcgd", prob_rows, value_row_list, preferred_element_type=jnp.float32
            )
            .astype(jnp.bfloat16)
            .reshape(sequence_length, query_heads * head_features)
        )
        attn_own = lax.psum_scatter(
            jnp.dot(context, out_full, preferred_element_type=jnp.float32).astype(jnp.bfloat16),
            "tp",
            scatter_dimension=0,
            tiled=True,
        ).astype(jnp.float32)
        hidden_own = own_rows + attn_own
        second_normed = rms_scale(hidden_own, second_gain).astype(jnp.bfloat16)
        normed_two, cot_all = (
            lax.all_gather(second_normed, "tp", axis=0, tiled=True),
            lax.all_gather(own_cot, "tp", axis=0, tiled=True),
        )
        slot_index, slot_owner, slot_weight = slot_tables(
            route_rows, gate_rows, all_experts, capacity
        )
        padded_rows = jnp.concatenate([normed_two, zero_row], axis=0)
        send_rows = padded_rows[slot_owner].reshape(buffer_shape)
        expert_in = lax.all_to_all(send_rows, "fsdp", split_axis=0, concat_axis=0, tiled=True)
        gate_act = jnp.einsum(
            "sekd,edf->sekf", expert_in, w_gate, preferred_element_type=jnp.float32
        )
        up_act = jnp.einsum("sekd,edf->sekf", expert_in, w_up, preferred_element_type=jnp.float32)
        act_rows = swiglu(gate_act, up_act).astype(jnp.bfloat16)
        expert_out = jnp.einsum(
            "sekf,efd->sekd", act_rows, w_down, preferred_element_type=jnp.float32
        )
        returned = lax.all_to_all(
            expert_out.astype(jnp.bfloat16), "fsdp", split_axis=0, concat_axis=0, tiled=True
        ).astype(expert_out.dtype)
        picked = returned.reshape(all_experts * capacity, model_width)[slot_index].reshape(
            sequence_length, top_count, model_width
        )
        moe_part = jnp.sum(picked * gate_rows[:, :, None], axis=1)
        moe_own = lax.psum_scatter(
            moe_part.astype(jnp.bfloat16), "tp", scatter_dimension=0, tiled=True
        ).astype(jnp.float32)
        outputs.append((hidden_own + moe_own).astype(jnp.bfloat16))
        cot_padded = jnp.concatenate([cot_all, zero_row], axis=0)
        send_grads = (
            (slot_weight[:, None] * cot_padded[slot_owner])
            .astype(jnp.bfloat16)
            .reshape(buffer_shape)
        )
        out_grads = lax.all_to_all(send_grads, "fsdp", split_axis=0, concat_axis=0, tiled=True)
        act_grads = jnp.einsum(
            "sekd,efd->sekf", out_grads, w_down, preferred_element_type=jnp.float32
        )
        _, swiglu_back = jax.vjp(swiglu, gate_act, up_act)
        gate_grads, up_grads = swiglu_back(act_grads)
        gate_grads = gate_grads.astype(jnp.bfloat16)
        up_grads = up_grads.astype(jnp.bfloat16)
        expert_grads = (
            expert_grads[0]
            + jnp.einsum(
                "sekd,sekf->edf", expert_in, gate_grads, preferred_element_type=jnp.float32
            ),
            expert_grads[1]
            + jnp.einsum("sekd,sekf->edf", expert_in, up_grads, preferred_element_type=jnp.float32),
            expert_grads[2]
            + jnp.einsum("sekf,sekd->efd", act_rows, out_grads, preferred_element_type=jnp.float32),
        )
        input_part = jnp.einsum(
            "sekf,edf->sekd", gate_grads, w_gate, preferred_element_type=jnp.float32
        ) + jnp.einsum("sekf,edf->sekd", up_grads, w_up, preferred_element_type=jnp.float32)
        input_back = lax.all_to_all(
            input_part.astype(jnp.bfloat16), "fsdp", split_axis=0, concat_axis=0, tiled=True
        ).astype(input_part.dtype)
        normed_grads = jnp.sum(
            input_back.reshape(all_experts * capacity, model_width)[slot_index].reshape(
                sequence_length, top_count, model_width
            ),
            axis=1,
        )
        normed_own = lax.psum_scatter(
            normed_grads.astype(jnp.bfloat16), "tp", scatter_dimension=0, tiled=True
        ).astype(jnp.float32)
        _, second_back = jax.vjp(rms_scale, hidden_own, second_gain)
        hidden_part, second_gain_grad = second_back(normed_own)
        hidden_grad = own_cot.astype(jnp.float32) + hidden_part
        attn_grad_all = lax.all_gather(hidden_grad.astype(jnp.bfloat16), "tp", axis=0, tiled=True)
        out_weight_grad = jnp.einsum(
            "th,td->hd", context, attn_grad_all, preferred_element_type=jnp.float32
        )
        context_grad = (
            jnp.einsum("td,hd->th", attn_grad_all, out_full, preferred_element_type=jnp.float32)
            .astype(jnp.bfloat16)
            .reshape(sequence_length, kv_heads, group_size, head_features)
        )
        exp_again = jnp.exp(masked_scores(query_fourfold, key_rot) - log_total)
        probs_again = exp_again.astype(jnp.bfloat16)
        prob_grads = jnp.einsum(
            "qcgd,kcd->cgqk", context_grad, value_row_list, preferred_element_type=jnp.float32
        )
        value_grads = (
            jnp.einsum(
                "cgqk,qcgd->kcd", probs_again, context_grad, preferred_element_type=jnp.float32
            )
            .astype(jnp.bfloat16)
            .reshape(sequence_length, kv_heads * head_features)
        )
        score_grads = (
            exp_again * (prob_grads - jnp.sum(exp_again * prob_grads, axis=-1, keepdims=True))
        ).astype(jnp.bfloat16)
        query_rot_grads = (
            jnp.einsum("cgqk,kcd->qcgd", score_grads, key_rot, preferred_element_type=jnp.float32)
            * score_scale
        ).reshape(sequence_length, query_heads, head_features)
        key_rot_grads = (
            jnp.einsum(
                "cgqk,qcgd->kcd", score_grads, query_fourfold, preferred_element_type=jnp.float32
            )
            * score_scale
        )
        _, query_back = jax.vjp(prep_heads, query_projected, query_factor_scale)
        query_proj_grads, query_gain_grad = query_back(query_rot_grads)
        _, key_back = jax.vjp(prep_heads, key_projected, key_scale)
        key_proj_grads, key_gain_grad = key_back(key_rot_grads)
        query_proj_grads = query_proj_grads.astype(jnp.bfloat16).reshape(
            sequence_length, query_heads * head_features
        )
        key_proj_grads = key_proj_grads.astype(jnp.bfloat16).reshape(
            sequence_length, kv_heads * head_features
        )
        first_normed_grads = (
            jnp.einsum(
                "tq,dq->td", query_proj_grads, query_full, preferred_element_type=jnp.float32
            )
            + jnp.einsum("tq,dq->td", key_proj_grads, key_full, preferred_element_type=jnp.float32)
            + jnp.einsum("tq,dq->td", value_grads, value_full, preferred_element_type=jnp.float32)
        )
        weight_parts = (
            jnp.einsum(
                "td,tq->dq", normed_all, query_proj_grads, preferred_element_type=jnp.float32
            ),
            jnp.einsum("td,tq->dq", normed_all, key_proj_grads, preferred_element_type=jnp.float32),
            jnp.einsum("td,tq->dq", normed_all, value_grads, preferred_element_type=jnp.float32),
            out_weight_grad,
        )
        first_own = lax.psum_scatter(
            first_normed_grads.astype(jnp.bfloat16), "tp", scatter_dimension=0, tiled=True
        ).astype(jnp.float32)
        _, first_back = jax.vjp(rms_scale, own_rows, first_gain)
        row_part, first_gain_grad = first_back(first_own)
        input_grads.append((hidden_grad + row_part).astype(jnp.bfloat16))
        gain_sums = (
            gain_sums[0] + first_gain_grad,
            gain_sums[1] + second_gain_grad,
            gain_sums[2] + query_gain_grad,
            gain_sums[3] + key_gain_grad,
        )
        attn_grads = jax.tree.map(
            jnp.add,
            attn_grads,
            (
                lax.psum_scatter(weight_parts[0], "fsdp", scatter_dimension=0, tiled=True),
                lax.psum_scatter(weight_parts[1], "fsdp", scatter_dimension=0, tiled=True),
                lax.psum_scatter(weight_parts[2], "fsdp", scatter_dimension=0, tiled=True),
                lax.psum_scatter(weight_parts[3], "fsdp", scatter_dimension=1, tiled=True),
            ),
        )
    summed = lax.psum((gain_sums[0], gain_sums[1], gain_sums[2], gain_sums[3]), ("fsdp", "tp"))
    block_out = jnp.stack(outputs)[:, None]
    input_grad = jnp.stack(input_grads)[:, None]
    return (
        block_out,
        input_grad,
        summed[0],
        attn_grads[0],
        attn_grads[1],
        attn_grads[2],
        summed[2],
        summed[3],
        attn_grads[3],
        summed[1],
        expert_grads[0],
        expert_grads[1],
        expert_grads[2],
    )


MESH = pl.DeviceIdType.MESH
FSDP, TP = "fsdp", "tp"
PLANE = 4
LANES = 128
MIB = 1 << 20
RIGHT, LEFT, FIRST, SECOND, CORE = range(5)


class Spot:
    def __init__(self, line, wide):
        self.line = line
        self.wide = wide
        self.planes = 4 if wide else 2
        index = lax.axis_index(FSDP)
        self.x = lax.axis_index(TP)
        self.z = lax.div(index, PLANE)
        self.y = lax.rem(lax.div(index, 2), 2)
        self.core = lax.rem(index, 2)

    def side(self, core, first, second):
        flip_y, flip_x = first, 0
        if self.wide:
            flip_y = (1 - core) * first + core * second
            flip_x = core * first + (1 - core) * second
        return self.y + flip_y * (1 - 2 * self.y), self.x + flip_x * (1 - 2 * self.x)

    def block(self, core, first, second, z):
        y, x = self.side(core, first, second)
        return z * PLANE + y * 2 + core, x

    def device(self, kind):
        if kind == RIGHT:
            return self.block(self.core, 0, 0, self.z + 1)
        if kind == LEFT:
            return self.block(self.core, 0, 0, self.z - 1)
        if kind == CORE:
            return self.block(1 - self.core, 0, 0, self.z)
        return self.block(self.core, int(kind == FIRST), int(kind == SECOND), self.z)

    def kinds(self):
        return (FIRST, SECOND, CORE) if self.wide else (FIRST, CORE)

    def number(self, first, second, z):
        return (second * 2 + first) * self.line + z

    def order(self, step):
        if isinstance(step, int) and step == 0:
            return [(self.z, None)]
        return [(self.z - step, self.z - step >= 0), (self.z + step, self.z + step < self.line)]

    def greet(self):
        barrier = pltpu.get_barrier_semaphore()

        def signal(kind):
            pl.semaphore_signal(barrier, inc=1, device_id=self.device(kind), device_id_type=MESH)

        for kind in self.kinds():
            signal(kind)
        when(self.z + 1 < self.line, lambda: signal(RIGHT))
        when(self.z > 0, lambda: signal(LEFT))
        around = (self.z + 1 < self.line).astype(jnp.int32) + (self.z > 0).astype(jnp.int32)
        pl.semaphore_wait(barrier, len(self.kinds()) + around)

    def send(self, source, target, send_sem, receive_sem, kind):
        return pltpu.make_async_remote_copy(
            src_ref=source,
            dst_ref=target,
            send_sem=send_sem,
            recv_sem=receive_sem,
            device_id=self.device(kind),
            device_id_type=MESH,
        )


def when(condition, action):
    def run():
        action()

    if condition is None:
        run()
    else:
        pl.when(condition)(run)


class Spread:
    def __init__(self, spot, slot, send, receive):
        self.spot = spot
        self.slot = slot
        self.sends = send
        self.receives = receive

    def copy(self, first, second, z, kind):
        spot = self.spot
        place = self.slot(*spot.block(spot.core, first, second, z))
        number = spot.number(first, second, z)
        arrival = {
            RIGHT: number,
            LEFT: number,
            FIRST: spot.number(1, 0, z),
            SECOND: spot.number(first, 1, z),
            CORE: spot.planes * spot.line + number,
        }[kind]
        departure = {RIGHT: 0, LEFT: 1, FIRST: 2, SECOND: 3, CORE: 5}[kind] * spot.line + number
        return spot.send(place, place, self.sends.at[departure], self.receives.at[arrival], kind)

    def arrived(self, first, second, z, other=False):
        spot = self.spot
        core = 1 - spot.core if other else spot.core
        place = self.slot(*spot.block(core, first, second, z))
        number = spot.number(first, second, z) + (spot.planes * spot.line if other else 0)
        spot.send(place, place, self.sends.at[0], self.receives.at[number], CORE).wait_recv()

    def steps(self):
        return self.spot.line + (3 if self.spot.wide else 1)

    def step(self, step):
        spot = self.spot
        line, z = spot.line, spot.z

        def reached(away, action):
            inside = jnp.logical_and(away >= 0, away < line)
            when(jnp.logical_and(inside, z - away >= 0), lambda: action(z - away, True))
            when(
                jnp.logical_and(inside, jnp.logical_and(away > 0, z + away < line)),
                lambda: action(z + away, False),
            )

        def along(zz, from_left):
            own = step == 0
            when(jnp.logical_not(own), lambda: self.arrived(0, 0, zz))
            if from_left:
                when(z + 1 < line, lambda: self.copy(0, 0, zz, RIGHT).start())
                when(jnp.logical_and(own, z > 0), lambda: self.copy(0, 0, zz, LEFT).start())
            else:
                when(z > 0, lambda: self.copy(0, 0, zz, LEFT).start())
            self.copy(0, 0, zz, FIRST).start()
            if spot.wide:
                self.copy(0, 0, zz, SECOND).start()
            self.copy(0, 0, zz, CORE).start()

        def firsts(zz, _):
            self.arrived(1, 0, zz)
            if spot.wide:
                self.copy(1, 0, zz, SECOND).start()
            self.copy(1, 0, zz, CORE).start()

        def lasts(first):
            def action(zz, _):
                self.arrived(first, 1, zz)
                self.copy(first, 1, zz, CORE).start()

            return action

        step = jnp.asarray(step, jnp.int32)
        reached(step, along)
        reached(step - 1, firsts)
        if spot.wide:
            reached(step - 2, lasts(0))
            reached(step - 3, lasts(1))

    def run(self):
        lax.fori_loop(0, self.steps(), lambda step, _: (self.step(step), 0)[1], 0)

    def finish(self):
        spot = self.spot
        z = spot.z

        def body(zz, _):
            when(
                jnp.logical_and(z + 1 < spot.line, zz <= z),
                lambda: self.copy(0, 0, zz, RIGHT).wait_send(),
            )
            when(jnp.logical_and(z > 0, zz >= z), lambda: self.copy(0, 0, zz, LEFT).wait_send())
            self.copy(0, 0, zz, FIRST).wait_send()
            for second in range(2 if spot.wide else 1):
                for first in (0, 1):
                    if spot.wide and not second:
                        self.copy(first, 0, zz, SECOND).wait_send()
                    self.copy(first, second, zz, CORE).wait_send()
                    self.arrived(first, second, zz, other=True)
            return 0

        lax.fori_loop(0, spot.line, body, 0)


def spread_count(line, wide):
    return (9 if wide else 7) * line, (8 if wide else 4) * line


def local_copies(pairs, semaphores):
    copies = [
        pltpu.make_async_copy(source, target, semaphores.at[i])
        for i, (source, target) in enumerate(pairs)
    ]
    for copy in copies:
        copy.start()
    for copy in copies:
        copy.wait()


def rows_at(ref, index, size):
    return ref.at[pl.ds(pl.multiple_of(index * size, 16), size)]


def columns_at(ref, index, size):
    return ref.at[:, pl.ds(pl.multiple_of(index * size, LANES), size)]


def interleaved(trees):
    steps = trees[0].steps()

    def body(step, _):
        for tree in trees:
            tree.step(step)
        return 0

    lax.fori_loop(0, steps, body, 0)
    for tree in trees:
        tree.finish()


def spread_rows_kernel(line, rows_ref, all_ref, send, receive, local):
    spot = Spot(line, True)
    spot.greet()
    own = spot.block(spot.core, 0, 0, spot.z)
    length = rows_ref.shape[1]
    slots = [
        lambda block, half, i=i: rows_at(all_ref.at[i, block], half, length)
        for i in range(rows_ref.shape[0])
    ]
    local_copies([(rows_ref.at[i], slot(*own)) for i, slot in enumerate(slots)], local)
    interleaved([Spread(spot, slot, send.at[i], receive.at[i]) for i, slot in enumerate(slots)])


def spread_rows(rows, fsdp_count):
    line = fsdp_count // PLANE
    batch, count, width = rows.shape
    sends, receives = spread_count(line, True)
    return pl.pallas_call(
        functools.partial(spread_rows_kernel, line),
        out_shape=jax.ShapeDtypeStruct((batch, fsdp_count, 2 * count, width), rows.dtype),
        in_specs=[pl.BlockSpec(memory_space=pl.ANY)],
        out_specs=pl.BlockSpec(memory_space=pl.ANY),
        scratch_shapes=[
            pltpu.SemaphoreType.DMA((batch, sends)),
            pltpu.SemaphoreType.DMA((batch, receives)),
            pltpu.SemaphoreType.DMA((batch,)),
        ],
        compiler_params=pltpu.CompilerParams(collective_id=0, has_side_effects=True),
    )(rows)


def spread_weights_kernel(
    line, in_ref, out_ref, picks_ref, in_all, out_all, picks_all, send, receive, local
):
    spot = Spot(line, False)
    spot.greet()
    depth, width = in_ref.shape[0], out_ref.shape[1]
    slots = [
        lambda block, half: picks_all.at[block],
        lambda block, half: rows_at(in_all, block, depth),
        lambda block, half: columns_at(out_all, block, width),
    ]
    own = spot.block(spot.core, 0, 0, spot.z)
    sources = (picks_ref, in_ref, out_ref)
    local_copies([(source, slot(*own)) for source, slot in zip(sources, slots)], local)
    interleaved([Spread(spot, slot, send.at[i], receive.at[i]) for i, slot in enumerate(slots)])


def spread_weights(weight_in, weight_out, picks, fsdp_count):
    line = fsdp_count // PLANE
    sends, receives = spread_count(line, False)
    return pl.pallas_call(
        functools.partial(spread_weights_kernel, line),
        out_shape=(
            jax.ShapeDtypeStruct((weight_in.shape[0] * fsdp_count, weight_in.shape[1]), jnp.bfloat16),
            jax.ShapeDtypeStruct((weight_out.shape[0], weight_out.shape[1] * fsdp_count), jnp.bfloat16),
            jax.ShapeDtypeStruct((fsdp_count, *picks.shape), picks.dtype),
        ),
        in_specs=[pl.BlockSpec(memory_space=pl.ANY)] * 3,
        out_specs=(pl.BlockSpec(memory_space=pl.ANY),) * 3,
        scratch_shapes=[
            pltpu.SemaphoreType.DMA((3, sends)),
            pltpu.SemaphoreType.DMA((3, receives)),
            pltpu.SemaphoreType.DMA((3,)),
        ],
        compiler_params=pltpu.CompilerParams(collective_id=1, has_side_effects=True),
    )(weight_in, weight_out, picks)


def add_rows(target, sources):
    def body(step, _):
        rows = pl.ds(pl.multiple_of(step * 16, 16), 16)
        total = sources[0][rows, :].astype(jnp.float32)
        for source in sources[1:]:
            total = total + source[rows, :].astype(jnp.float32)
        target[rows, :] = total.astype(target.dtype)
        return 0

    lax.fori_loop(0, target.shape[0] // 16, body, 0)


def collect(spot, items, send, receive, local):
    line, z, core = spot.line, spot.z, spot.core
    every = range(len(items))
    base = {CORE: 0, FIRST: 2 * line, RIGHT: 3 * line, LEFT: 4 * line}

    def copy(item, kind, first, zz):
        part, _, own, cores, firsts, rights, lefts = items[item]
        number = first * line + zz
        index = number if kind == CORE else zz
        source = part(*spot.block(1 - core, first, 0, zz)) if kind == CORE else own.at[number]
        place = {CORE: cores, FIRST: firsts, RIGHT: rights, LEFT: lefts}[kind].at[index]
        return spot.send(
            source,
            place,
            send.at[item, base[kind] + index],
            receive.at[item, base[kind] + index],
            kind,
        )

    def load(item, first, zz):
        part, own = items[item][0], items[item][2]
        number = first * line + zz
        return pltpu.make_async_copy(
            part(*spot.block(core, first, 0, zz)), own.at[number], local.at[item, number]
        )

    def ordered(action):
        for step in reversed(range(line)):
            for zz, valid in spot.order(step):
                when(valid, lambda: [action(item, zz) for item in every])

    for first in (1, 0):

        def fetch(item, zz):
            copy(item, CORE, first, zz).start()
            load(item, first, zz).start()

        ordered(fetch)

    def summed(item, first, zz, target=None, extra=()):
        _, _, own, cores, firsts, _, _ = items[item]
        number = first * line + zz
        load(item, first, zz).wait()
        copy(item, CORE, first, zz).wait_recv()
        sources = [own.at[number], cores.at[number]]
        if not first:
            copy(item, FIRST, 1, zz).wait_recv()
            sources.append(firsts.at[zz])
        add_rows(own.at[number] if target is None else target, sources + list(extra))

    def to_first(item, zz):
        summed(item, 1, zz)
        copy(item, FIRST, 1, zz).start()

    ordered(to_first)

    for step in reversed(range(1, line)):
        for kind, zz, valid in zip((LEFT, RIGHT), *zip(*spot.order(step))):

            def onward():
                behind = z > 0 if kind == RIGHT else z + 1 < line
                for item in every:
                    incoming = items[item][5 if kind == RIGHT else 6].at[zz]

                    def with_incoming():
                        copy(item, kind, 0, zz).wait_recv()
                        summed(item, 0, zz, extra=[incoming])

                    when(behind, with_incoming)
                    when(jnp.logical_not(behind), lambda: summed(item, 0, zz))
                    copy(item, kind, 0, zz).start()

            when(valid, onward)

    def finish(kinds):
        for item in every:
            for kind in kinds:
                copy(item, kind, 0, z).wait_recv()
            incoming = [items[item][5 if kind == RIGHT else 6].at[z] for kind in kinds]
            summed(item, 0, z, target=items[item][1], extra=incoming)

    when(z == 0, lambda: finish([LEFT]))
    when(z == line - 1, lambda: finish([RIGHT]))
    when(jnp.logical_and(z > 0, z < line - 1), lambda: finish([RIGHT, LEFT]))

    for item in every:
        for zz in range(line):
            when(zz > z, lambda: copy(item, RIGHT, 0, zz).wait_send())
            when(zz < z, lambda: copy(item, LEFT, 0, zz).wait_send())
            copy(item, FIRST, 1, zz).wait_send()
            for first in (0, 1):
                copy(item, CORE, first, zz).wait_send()


def collect_scratch(line, shape):
    counts = (2 * line, 2 * line, line, line, line)
    return [pltpu.VMEM((count, *shape), jnp.bfloat16) for count in counts]


def collect_weights_kernel(
    line, in_part, out_part, gains_ref, in_total, out_total, gains_all, *scratch
):
    buffers, (send, receive, local, gain_send, gain_receive, gain_local) = (
        scratch[:-6],
        scratch[-6:],
    )
    narrow, spot = Spot(line, False), Spot(line, True)
    spot.greet()
    own = spot.block(spot.core, 0, 0, spot.z)
    slot = lambda block, half: gains_all.at[block, half]
    local_copies([(gains_ref, slot(*own))], gain_local)
    interleaved([Spread(spot, slot, gain_send, gain_receive)])
    depth, width = in_total.shape[0], out_total.shape[1]
    items = [
        (lambda block, half: rows_at(in_part, block, depth), in_total, *buffers[:5]),
        (lambda block, half: columns_at(out_part, block, width), out_total, *buffers[5:]),
    ]
    collect(narrow, items, send, receive, local)


def collect_weights(in_part, out_part, gains, fsdp_count):
    line = fsdp_count // PLANE
    in_shape = (in_part.shape[0] // fsdp_count, in_part.shape[1])
    out_shape = (out_part.shape[0], out_part.shape[1] // fsdp_count)
    sends, receives = spread_count(line, True)
    return pl.pallas_call(
        functools.partial(collect_weights_kernel, line),
        out_shape=(
            jax.ShapeDtypeStruct(in_shape, jnp.float32),
            jax.ShapeDtypeStruct(out_shape, jnp.float32),
            jax.ShapeDtypeStruct((fsdp_count, 2, *gains.shape), jnp.float32),
        ),
        in_specs=[pl.BlockSpec(memory_space=pl.ANY)] * 3,
        out_specs=(
            pl.BlockSpec(memory_space=pltpu.VMEM),
            pl.BlockSpec(memory_space=pltpu.VMEM),
            pl.BlockSpec(memory_space=pl.ANY),
        ),
        scratch_shapes=collect_scratch(line, in_shape)
        + collect_scratch(line, out_shape)
        + [
            pltpu.SemaphoreType.DMA((2, 5 * line)),
            pltpu.SemaphoreType.DMA((2, 5 * line)),
            pltpu.SemaphoreType.DMA((2, 2 * line)),
            pltpu.SemaphoreType.DMA((sends,)),
            pltpu.SemaphoreType.DMA((receives,)),
            pltpu.SemaphoreType.DMA((1,)),
        ],
        compiler_params=pltpu.CompilerParams(
            collective_id=3, has_side_effects=True, vmem_limit_bytes=56 * MIB
        ),
    )(in_part, out_part, gains)


TRANSPOSED_LEFT = (((0,), (0,)), ((), ()))
TRANSPOSED_RIGHT = (((1,), (1,)), ((), ()))
OUTPUT, BACK = range(2)
CHUNK = 512


def experts_kernel(
    line,
    slots,
    own_ref,
    cot_ref,
    info_ref,
    gate_ref,
    up_ref,
    down_ref,
    all_ref,
    total_ref,
    xe_all,
    ce_all,
    act_all,
    dgate_all,
    dup_all,
    part,
    cores,
    seconds,
    firsts,
    ends,
    hidden_w,
    down_w,
    x_rows,
    c_rows,
    xe,
    ce,
    acts,
    dgates,
    dups,
    hidden_grads,
    picks,
    weigh,
    rows,
    stage,
    inbox,
    outbox,
    summed,
    tree_send,
    tree_receive,
    load_sem,
    save_sem,
    stage_sem,
    inbox_sem,
    outbox_sem,
    weight_sem,
    core_receive,
    second_receive,
    first_receive,
    end_receive,
):
    spot = Spot(line, True)
    z, core = spot.z, spot.core
    batch, half, width = own_ref.shape
    length = 2 * half
    units = down_ref.shape[1]
    groups = batch * line
    weights = [
        pltpu.make_async_copy(source, target, weight_sem.at[i])
        for i, (source, target) in enumerate(
            [(down_ref, down_w)]
            + [(gate_ref.at[e], hidden_w.at[e, :, pl.ds(0, units)]) for e in range(2)]
            + [(up_ref.at[e], hidden_w.at[e, :, pl.ds(units, units)]) for e in range(2)]
        )
    ]
    for copy in weights:
        copy.start()
    rows[...] = jnp.zeros_like(rows)
    spot.greet()

    def half_of(ref, index):
        return rows_at(ref, index, half)

    own = spot.block(core, 0, 0, z)
    trees = []
    for i in range(batch):
        slot = lambda block, side, i=i: half_of(all_ref.at[i, block], side)
        trees.append(Spread(spot, slot, tree_send.at[i], tree_receive.at[i]))
    local_copies([(own_ref.at[i], tree.slot(*own)) for i, tree in enumerate(trees)], save_sem)
    trees[0].run()
    trees[0].finish()
    for copy in weights:
        copy.wait()

    def plane_of(group):
        turn = lax.rem(group, line)
        step = lax.div(turn, 2)
        return jnp.where(lax.rem(turn, 2) == 0, step, line - 1 - step)

    def load_group(group, member):
        at = lax.div(group, line)
        sequence = plane_of(group) * PLANE + member
        slot = lax.rem(member, 2)
        return [
            pltpu.make_async_copy(all_ref.at[at, sequence], x_rows.at[slot], load_sem.at[0, slot]),
            pltpu.make_async_copy(cot_ref.at[at, sequence], c_rows.at[slot], load_sem.at[1, slot]),
        ]

    def saves(group):
        to = lambda ref, expert: rows_at(ref.at[expert], group, PLANE * slots)
        pairs = ((xe, xe_all), (ce, ce_all), (acts, act_all), (dgates, dgate_all), (dups, dup_all))
        return [
            pltpu.make_async_copy(source.at[expert], to(target, expert), save_sem.at[2 * i + expert])
            for i, (source, target) in enumerate(pairs)
            for expert in range(2)
        ]

    def staged(group, tensor, y, mine):
        unit = group * 2 + tensor
        slot = y * 2 + mine
        if mine:
            return pltpu.make_async_copy(stage.at[slot], part.at[unit, y], stage_sem.at[slot])
        return spot.send(
            stage.at[slot], cores.at[unit, y], stage_sem.at[slot], core_receive.at[unit, y], CORE
        )

    def combine(group, tensor):
        for y in range(2):
            for mine in range(2):
                member = y * 2 + (core if mine else 1 - core)
                for start in range(0, width, CHUNK):
                    stage[y * 2 + mine, :, start : start + CHUNK] = lax.dot_general(
                        picks[member],
                        rows[member, :, start : start + CHUNK],
                        TRANSPOSED_LEFT,
                        preferred_element_type=jnp.float32,
                    ).astype(jnp.bfloat16)
                staged(group, tensor, y, mine).start()

    def stages_done(group, tensor):
        for y in range(2):
            staged(group, tensor, y, 1).wait()
            staged(group, tensor, y, 0).wait_send()

    def compute(group):
        when(group > 0, lambda: [copy.wait() for copy in saves(group - 1)] and None)

        def pick(member, _):
            slot = lax.rem(member, 2)
            for copy in load_group(group, member):
                copy.wait()

            @pl.when(member + 1 < PLANE)
            def _():
                for copy in load_group(group, member + 1):
                    copy.start()

            sequence = plane_of(group) * PLANE + member
            info = info_ref[lax.div(group, line) * line * PLANE + sequence]
            places = lax.broadcasted_iota(jnp.int32, (2 * LANES, length), 0)
            lower = places < LANES
            ranks = jnp.where(lower, info[0:1], info[1:2] + float(LANES)).astype(jnp.int32)
            some = jnp.where(lower, info[0:1], info[1:2]) >= 0.0
            hot = jnp.logical_and(ranks == places, some)
            chosen = hot.astype(jnp.float32).astype(jnp.bfloat16)
            picks[member] = chosen
            shares = jnp.where(hot, jnp.where(lower, info[2:3], info[3:4]), 0.0)
            column = jnp.sum(shares, axis=1, keepdims=True)
            here = pl.ds(pl.multiple_of(member * slots, 16), slots)
            for expert in range(2):
                weigh[expert, here, :] = jnp.broadcast_to(
                    column[expert * LANES : expert * LANES + slots], (slots, LANES)
                )
            for source, target in ((x_rows, xe), (c_rows, ce)):
                for start in range(0, width, CHUNK):
                    selected = jnp.dot(
                        chosen,
                        source[slot, :, start : start + CHUNK],
                        preferred_element_type=jnp.float32,
                    ).astype(jnp.bfloat16)
                    for expert in range(2):
                        target[expert, here, start : start + CHUNK] = selected[
                            expert * LANES : expert * LANES + slots
                        ]
            return 0

        lax.fori_loop(0, PLANE, pick, 0)

        def keep(expert, product, start):
            at = pl.ds(pl.multiple_of(expert * LANES, LANES), slots)
            for one in range(PLANE):
                rows[one, at, start : start + CHUNK] = product[
                    one * slots : (one + 1) * slots
                ].astype(jnp.bfloat16)

        def forward(expert, _):
            hidden = jnp.dot(xe[expert], hidden_w[expert], preferred_element_type=jnp.float32)
            gate, up = hidden[:, :units], hidden[:, units:]
            sigmoid = jax.nn.sigmoid(gate)
            silu = gate * sigmoid
            scale = weigh[expert, :, 0:1]
            acts[expert] = (silu * up * scale).astype(jnp.bfloat16)
            act_grads = scale * lax.dot_general(
                ce[expert], down_w[expert], TRANSPOSED_RIGHT, preferred_element_type=jnp.float32
            )
            gate_grads = (act_grads * up * (sigmoid * (1.0 + gate * (1.0 - sigmoid)))).astype(
                jnp.bfloat16
            )
            up_grads = (act_grads * silu).astype(jnp.bfloat16)
            dgates[expert] = gate_grads
            dups[expert] = up_grads
            hidden_grads[expert, :, :units] = gate_grads
            hidden_grads[expert, :, units:] = up_grads
            for start in range(0, width, CHUNK):
                keep(
                    expert,
                    jnp.dot(
                        acts[expert],
                        down_w[expert, :, start : start + CHUNK],
                        preferred_element_type=jnp.float32,
                    ),
                    start,
                )
            return 0

        lax.fori_loop(0, 2, forward, 0)
        for copy in saves(group):
            copy.start()
        combine(group, OUTPUT)

        def backward(expert, _):
            for start in range(0, width, CHUNK):
                keep(
                    expert,
                    lax.dot_general(
                        hidden_grads[expert],
                        hidden_w[expert, start : start + CHUNK, :],
                        TRANSPOSED_RIGHT,
                        preferred_element_type=jnp.float32,
                    ),
                    start,
                )
            return 0

        lax.fori_loop(0, 2, backward, 0)
        stages_done(group, OUTPUT)
        combine(group, BACK)

    def inside(group):
        return jnp.logical_and(group >= 0, group < groups)

    def second_send(group, tensor, first):
        unit, slot = group * 2 + tensor, tensor * 2 + first
        return spot.send(
            outbox.at[slot],
            seconds.at[unit, first],
            outbox_sem.at[slot],
            second_receive.at[unit, first],
            SECOND,
        )

    def first_send(group, tensor):
        unit, slot = group * 2 + tensor, 4 + tensor
        return spot.send(
            outbox.at[slot], firsts.at[unit], outbox_sem.at[slot], first_receive.at[unit], FIRST
        )

    def end_send(group, tensor, kind):
        unit, slot = group * 2 + tensor, 6 + tensor * 2 + kind
        return spot.send(
            outbox.at[slot],
            ends.at[unit, kind],
            outbox_sem.at[slot],
            end_receive.at[unit, kind],
            kind,
        )

    def sources(unit, first, second):
        y, x = spot.side(core, first, second)
        return [half_of(part.at[unit, y], x), half_of(cores.at[unit, y], x)]

    def load(source, slot):
        return pltpu.make_async_copy(source, inbox.at[slot], inbox_sem.at[slot])

    def end_roles(step, delay):
        group = step - 3 - delay
        plane = plane_of(jnp.maximum(group, 0))
        valid = inside(group)
        right = jnp.logical_and(valid, jnp.logical_and(z < plane, delay == z))
        left = jnp.logical_and(valid, jnp.logical_and(z > plane, delay == line - 1 - z))
        last = jnp.logical_and(
            valid,
            jnp.logical_and(z == plane, delay == jnp.maximum(plane, line - 1 - plane)),
        )
        return group, right, left, last

    def end_task(step, index):
        delay, tensor = lax.div(index, 2), lax.rem(index, 2)
        group, right, left, last = end_roles(step, delay)
        unit = group * 2 + tensor
        from_left = jnp.logical_and(jnp.logical_or(right, last), z > 0)
        from_right = jnp.logical_and(jnp.logical_or(left, last), z + 1 < line)

        @pl.when(jnp.logical_or(right, jnp.logical_or(left, last)))
        def _():
            seconds_in = spot.send(
                seconds.at[unit, 0],
                seconds.at[unit, 0],
                outbox_sem.at[0],
                second_receive.at[unit, 0],
                SECOND,
            )
            firsts_in = spot.send(
                firsts.at[unit], firsts.at[unit], outbox_sem.at[0], first_receive.at[unit], FIRST
            )
            seconds_in.wait_recv()
            firsts_in.wait_recv()
            loads = [
                load(source, i)
                for i, source in enumerate(
                    sources(unit, 0, 0) + [seconds.at[unit, 0], firsts.at[unit]]
                )
            ]
            for one in loads:
                one.start()
            for kind, present in ((RIGHT, from_left), (LEFT, from_right)):

                def fetch(kind=kind):
                    spot.send(
                        ends.at[unit, kind],
                        ends.at[unit, kind],
                        outbox_sem.at[0],
                        end_receive.at[unit, kind],
                        CORE,
                    ).wait_recv()
                    load(ends.at[unit, kind], 4 + kind).start()

                when(present, fetch)
            for one in loads:
                one.wait()
            add_rows(summed, [inbox.at[i] for i in range(4)])
            for kind, present in ((RIGHT, from_left), (LEFT, from_right)):

                def add(kind=kind):
                    load(ends.at[unit, kind], 4 + kind).wait()
                    add_rows(summed, [summed, inbox.at[4 + kind]])

                when(present, add)
            for kind, chosen in ((RIGHT, right), (LEFT, left)):

                def onward(kind=kind):
                    slot = 6 + tensor * 2 + kind
                    add_rows(outbox.at[slot], [summed])
                    end_send(group, tensor, kind).start()

                when(chosen, onward)

            @pl.when(last)
            def _():
                copy = pltpu.make_async_copy(
                    summed, total_ref.at[lax.div(group, line), tensor], inbox_sem.at[0]
                )
                copy.start()
                copy.wait()

    def retire(step):
        before = step - 1

        @pl.when(inside(before))
        def _():
            stages_done(before, BACK)

        for tensor in range(2):
            when(
                inside(before - 1),
                lambda: [second_send(before - 1, tensor, first).wait_send() for first in range(2)]
                and None,
            )
            when(inside(before - 2), lambda: first_send(before - 2, tensor).wait_send())

        def ends_done(index, _):
            group, right, left, _ = end_roles(before, lax.div(index, 2))
            tensor = lax.rem(index, 2)
            when(right, lambda: end_send(group, tensor, RIGHT).wait_send())
            when(left, lambda: end_send(group, tensor, LEFT).wait_send())
            return 0

        lax.fori_loop(0, 2 * line, ends_done, 0)

    def serve(step):
        def end_tasks(index, _):
            end_task(step, index)
            return 0

        lax.fori_loop(0, 2 * line, end_tasks, 0)
        tasks = []
        for tensor in range(2):
            unit = (step - 2) * 2 + tensor

            def second_in(unit=unit):
                spot.send(
                    seconds.at[unit, 1],
                    seconds.at[unit, 1],
                    outbox_sem.at[0],
                    second_receive.at[unit, 1],
                    SECOND,
                ).wait_recv()

            tasks.append(
                (
                    inside(step - 2),
                    second_in,
                    lambda unit=unit: sources(unit, 1, 0) + [seconds.at[unit, 1]],
                    4 + tensor,
                    lambda tensor=tensor: first_send(step - 2, tensor),
                )
            )
        for first in (1, 0):
            for tensor in range(2):
                unit = (step - 1) * 2 + tensor

                def cores_in(unit=unit):
                    for y in range(2):
                        spot.send(
                            cores.at[unit, y],
                            cores.at[unit, y],
                            outbox_sem.at[0],
                            core_receive.at[unit, y],
                            CORE,
                        ).wait_recv()

                tasks.append(
                    (
                        inside(step - 1),
                        cores_in if first else lambda: None,
                        lambda unit=unit, first=first: sources(unit, first, 1),
                        tensor * 2 + first,
                        lambda tensor=tensor, first=first: second_send(step - 1, tensor, first),
                    )
                )

        def begin(index):
            valid, ready, inputs, _, _ = tasks[index]

            def action():
                ready()
                for i, source in enumerate(inputs()):
                    load(source, (index % 2) * 3 + i).start()

            when(valid, action)

        begin(0)
        for index, (valid, _, inputs, slot, send) in enumerate(tasks):
            if index + 1 < len(tasks):
                begin(index + 1)

            def action():
                refs = inputs()
                base = (index % 2) * 3
                for i, source in enumerate(refs):
                    load(source, base + i).wait()
                add_rows(outbox.at[slot], [inbox.at[base + i] for i in range(len(refs))])
                send().start()

            when(valid, action)

    def step_body(step, _):
        for i in range(1, batch):
            when(step == i * line, trees[i].finish)

        @pl.when(step < groups)
        def _():
            for copy in load_group(step, 0):
                copy.start()

        for i in range(1, batch):
            turn = step - (i - 1) * line
            when(jnp.logical_and(turn >= 0, turn < line), lambda: trees[i].step(2 * turn))
        retire(step)
        serve(step)
        for i in range(1, batch):
            turn = step - (i - 1) * line
            when(jnp.logical_and(turn >= 0, turn < line), lambda: trees[i].step(2 * turn + 1))
        when(step < groups, lambda: compute(step))
        return 0

    steps = groups + line + 2
    lax.fori_loop(0, steps, step_body, 0)
    retire(jnp.int32(steps))
    for copy in saves(groups - 1):
        copy.wait()


def run_experts(rows, cot_all, info, w_gate, w_up, w_down, capacity, fsdp_count):
    line = fsdp_count // PLANE
    batch, half, width = rows.shape
    length = 2 * half
    units = w_down.shape[1]
    slots = -(-capacity // 16) * 16
    groups = batch * line
    count = groups * PLANE * slots
    taken = PLANE * slots
    sends, receives = spread_count(line, True)
    shape = lambda *dims: jax.ShapeDtypeStruct(dims, jnp.bfloat16)
    block = (half, width)
    anywhere = pl.BlockSpec(memory_space=pl.ANY)
    vmem = lambda *dims: pltpu.VMEM(dims, jnp.bfloat16)
    sem = lambda *dims: pltpu.SemaphoreType.DMA(dims)
    return pl.pallas_call(
        functools.partial(experts_kernel, line, slots),
        out_shape=(
            shape(batch, fsdp_count, length, width),
            jax.ShapeDtypeStruct((batch, 2, *block), jnp.float32),
            shape(2, count, width),
            shape(2, count, width),
            shape(2, count, units),
            shape(2, count, units),
            shape(2, count, units),
            shape(2 * groups, 2, length, width),
            shape(2 * groups, 2, length, width),
            shape(2 * groups, 2, *block),
            shape(2 * groups, *block),
            shape(2 * groups, 2, *block),
        ),
        in_specs=[
            anywhere,
            anywhere,
            pl.BlockSpec(memory_space=pltpu.VMEM),
            anywhere,
            anywhere,
            anywhere,
        ],
        out_specs=(anywhere,) * 12,
        scratch_shapes=[
            vmem(2, width, 2 * units),
            vmem(2, units, width),
            vmem(2, length, width),
            vmem(2, length, width),
            vmem(2, taken, width),
            vmem(2, taken, width),
            vmem(2, taken, units),
            vmem(2, taken, units),
            vmem(2, taken, units),
            vmem(2, taken, 2 * units),
            vmem(PLANE, 2 * LANES, length),
            pltpu.VMEM((2, taken, LANES), jnp.float32),
            vmem(PLANE, 2 * LANES, width),
            vmem(PLANE, length, width),
            vmem(6, *block),
            vmem(10, *block),
            pltpu.VMEM(block, jnp.float32),
            sem(batch, sends),
            sem(batch, receives),
            sem(2, 2),
            sem(10),
            sem(PLANE),
            sem(6),
            sem(10),
            sem(5),
            sem(2 * groups, 2),
            sem(2 * groups, 2),
            sem(2 * groups),
            sem(2 * groups, 2),
        ],
        compiler_params=pltpu.CompilerParams(
            collective_id=2, has_side_effects=True, vmem_limit_bytes=60 * MIB
        ),
    )(rows, cot_all, info, w_gate, w_up, w_down)[1:7]


def packed_picks(routes, gates):
    length = routes.shape[2]
    packed = jnp.concatenate([routes[:, 0].astype(jnp.float32), gates[:, 0]], axis=-1)
    packed = jnp.swapaxes(packed, 1, 2).reshape(-1, length)
    return jnp.pad(packed, ((0, 0), (0, -length % LANES)))


def slot_info(packed, batch, top, length, local_experts):
    fsdp_count = packed.shape[0]
    packed = packed[..., :length].reshape(fsdp_count, batch, 1, 2 * top, length)
    packed = jnp.swapaxes(packed, 0, 1)
    experts = lax.axis_index(FSDP) * local_experts + jnp.arange(local_experts, dtype=jnp.int32)
    same = packed[..., :top, :].astype(jnp.int32) == experts[:, None, None]
    hot = jnp.any(same, axis=3)
    shares = jnp.sum(jnp.where(same, packed[..., top:, :], 0.0), axis=3)
    position = jnp.arange(length)
    upper = (position[:, None] < position[None, :]).astype(jnp.bfloat16)
    rank = jnp.dot(
        hot.astype(jnp.bfloat16).reshape(-1, length), upper, preferred_element_type=jnp.float32
    )
    rank = jnp.where(hot, rank.reshape(hot.shape), -1.0)
    return jnp.concatenate([rank, shares], axis=2).reshape(-1, 2 * local_experts, length)


def gathered_layer(
    tokens,
    cotangent,
    norm1_gain,
    w_query,
    key_projection_weight,
    value_projection_weight,
    query_gain,
    key_gain,
    w_out,
    norm2_gain,
    w_gate,
    w_up,
    w_down,
    routes,
    gates,
):
    batch_count = tokens.shape[0]
    model_width = tokens.shape[3]
    sequence_length = routes.shape[2]
    half_length = tokens.shape[2]
    top_count = routes.shape[3]
    head_features = query_gain.shape[0]
    local_experts = w_gate.shape[0]
    fsdp_count = lax.axis_size(FSDP)
    all_experts = local_experts * fsdp_count
    capacity = 7 * top_count * sequence_length // (6 * all_experts)
    query_width = w_query.shape[1]
    kv_width = key_projection_weight.shape[1]
    query_heads = query_width // head_features
    kv_heads = kv_width // head_features
    group_size = query_heads // kv_heads
    score_scale = head_features ** (-0.5)
    cosine_table, sine_values = rotary_tables(sequence_length, head_features)
    block_ids = jnp.arange(sequence_length, dtype=jnp.int32) // BLOCK
    visible = (block_ids[None, :] <= block_ids[:, None])[None, None]
    first_gain = norm1_gain.astype(jnp.float32)
    second_gain = norm2_gain.astype(jnp.float32)
    query_factor_scale = query_gain.astype(jnp.float32)
    key_scale = key_gain.astype(jnp.float32)

    def masked_scores(query_fourfold, key_rows):
        raw_scores = (
            jnp.einsum(
                "qcgd,kcd->cgqk", query_fourfold, key_rows, preferred_element_type=jnp.float32
            )
            * score_scale
        )
        return jnp.where(visible, raw_scores, MASKED)

    def prep_heads(projected, gain_row):
        return prepare_heads(projected, gain_row, cosine_table, sine_values)

    weight_in = jnp.concatenate([w_query, key_projection_weight, value_projection_weight], axis=1)
    in_full, out_full, picks = spread_weights(
        weight_in, w_out, packed_picks(routes, gates), fsdp_count
    )
    info = slot_info(picks, batch_count, top_count, sequence_length, local_experts)
    cot_all = spread_rows(cotangent[:, 0], fsdp_count)

    kept = []
    for batch_index in range(batch_count):
        own_rows = tokens[batch_index, 0].astype(jnp.float32)
        first_normed = rms_scale(own_rows, first_gain).astype(jnp.bfloat16)
        normed_all = lax.all_gather(first_normed, TP, axis=0, tiled=True)
        projected = jnp.dot(normed_all, in_full, preferred_element_type=jnp.float32)
        query_projected = projected[:, :query_width].reshape(
            sequence_length, query_heads, head_features
        )
        key_projected = projected[:, query_width : query_width + kv_width].reshape(
            sequence_length, kv_heads, head_features
        )
        value_row_list = (
            projected[:, query_width + kv_width :]
            .astype(jnp.bfloat16)
            .reshape(sequence_length, kv_heads, head_features)
        )
        query_rot = prep_heads(query_projected, query_factor_scale).astype(jnp.bfloat16)
        key_rot = prep_heads(key_projected, key_scale).astype(jnp.bfloat16)
        query_fourfold = query_rot.reshape(sequence_length, kv_heads, group_size, head_features)
        scores = masked_scores(query_fourfold, key_rot)
        row_max = jnp.max(scores, axis=-1, keepdims=True)
        exp_scores = jnp.exp(scores - row_max)
        totals = jnp.sum(exp_scores, axis=-1, keepdims=True)
        log_total = row_max + jnp.log(totals)
        prob_rows = (exp_scores / totals).astype(jnp.bfloat16)
        context = (
            jnp.einsum(
                "cgqk,kcd->qcgd", prob_rows, value_row_list, preferred_element_type=jnp.float32
            )
            .astype(jnp.bfloat16)
            .reshape(sequence_length, query_heads * head_features)
        )
        attn_own = lax.psum_scatter(
            jnp.dot(context, out_full, preferred_element_type=jnp.float32).astype(jnp.bfloat16),
            TP,
            scatter_dimension=0,
            tiled=True,
        ).astype(jnp.float32)
        hidden_own = own_rows + attn_own
        second_normed = rms_scale(hidden_own, second_gain).astype(jnp.bfloat16)
        kept.append(
            (
                own_rows,
                normed_all,
                query_projected,
                key_projected,
                value_row_list,
                query_fourfold,
                key_rot,
                log_total,
                context,
                hidden_own,
                second_normed,
            )
        )

    totals, expert_rows, cot_rows, act_rows, gate_rows, up_rows = run_experts(
        jnp.stack([items[-1] for items in kept]),
        cot_all,
        info,
        w_gate,
        w_up,
        w_down,
        capacity,
        fsdp_count,
    )
    expert_grads = (
        jnp.einsum("erd,erf->edf", expert_rows, gate_rows, preferred_element_type=jnp.float32),
        jnp.einsum("erd,erf->edf", expert_rows, up_rows, preferred_element_type=jnp.float32),
        jnp.einsum("erf,erd->efd", act_rows, cot_rows, preferred_element_type=jnp.float32),
    )

    outputs = []
    input_grads = []
    gain_sums = None
    in_grad, out_grad = 0.0, 0.0
    for batch_index in range(batch_count):
        (
            own_rows,
            normed_all,
            query_projected,
            key_projected,
            value_row_list,
            query_fourfold,
            key_rot,
            log_total,
            context,
            hidden_own,
            _,
        ) = kept[batch_index]
        own_cot = cotangent[batch_index, 0]
        outputs.append((hidden_own + totals[batch_index, 0]).astype(jnp.bfloat16))
        _, second_back = jax.vjp(rms_scale, hidden_own, second_gain)
        hidden_part, second_gain_grad = second_back(totals[batch_index, 1])
        hidden_grad = own_cot.astype(jnp.float32) + hidden_part
        attn_grad_all = lax.all_gather(hidden_grad.astype(jnp.bfloat16), TP, axis=0, tiled=True)
        out_grad = out_grad + jnp.einsum(
            "th,td->hd", context, attn_grad_all, preferred_element_type=jnp.float32
        )
        context_grad = (
            jnp.einsum("td,hd->th", attn_grad_all, out_full, preferred_element_type=jnp.float32)
            .astype(jnp.bfloat16)
            .reshape(sequence_length, kv_heads, group_size, head_features)
        )
        exp_again = jnp.exp(masked_scores(query_fourfold, key_rot) - log_total)
        probs_again = exp_again.astype(jnp.bfloat16)
        prob_grads = jnp.einsum(
            "qcgd,kcd->cgqk", context_grad, value_row_list, preferred_element_type=jnp.float32
        )
        value_grads = (
            jnp.einsum(
                "cgqk,qcgd->kcd", probs_again, context_grad, preferred_element_type=jnp.float32
            )
            .astype(jnp.bfloat16)
            .reshape(sequence_length, kv_width)
        )
        score_grads = (
            exp_again * (prob_grads - jnp.sum(exp_again * prob_grads, axis=-1, keepdims=True))
        ).astype(jnp.bfloat16)
        query_rot_grads = (
            jnp.einsum("cgqk,kcd->qcgd", score_grads, key_rot, preferred_element_type=jnp.float32)
            * score_scale
        ).reshape(sequence_length, query_heads, head_features)
        key_rot_grads = (
            jnp.einsum(
                "cgqk,qcgd->kcd", score_grads, query_fourfold, preferred_element_type=jnp.float32
            )
            * score_scale
        )
        _, query_back = jax.vjp(prep_heads, query_projected, query_factor_scale)
        query_proj_grads, query_gain_grad = query_back(query_rot_grads)
        _, key_back = jax.vjp(prep_heads, key_projected, key_scale)
        key_proj_grads, key_gain_grad = key_back(key_rot_grads)
        projected_grads = jnp.concatenate(
            [
                query_proj_grads.astype(jnp.bfloat16).reshape(sequence_length, query_width),
                key_proj_grads.astype(jnp.bfloat16).reshape(sequence_length, kv_width),
                value_grads,
            ],
            axis=1,
        )
        first_normed_grads = jnp.einsum(
            "tq,dq->td", projected_grads, in_full, preferred_element_type=jnp.float32
        )
        in_grad = in_grad + jnp.einsum(
            "td,tq->dq", normed_all, projected_grads, preferred_element_type=jnp.float32
        )
        first_own = lax.psum_scatter(
            first_normed_grads.astype(jnp.bfloat16), TP, scatter_dimension=0, tiled=True
        ).astype(jnp.float32)
        _, first_back = jax.vjp(rms_scale, own_rows, first_gain)
        row_part, first_gain_grad = first_back(first_own)
        input_grads.append((hidden_grad + row_part).astype(jnp.bfloat16))
        new_sums = (first_gain_grad, second_gain_grad, query_gain_grad, key_gain_grad)
        gain_sums = new_sums if gain_sums is None else jax.tree.map(jnp.add, gain_sums, new_sums)
    ends = [0]
    for gains in gain_sums:
        ends.append(ends[-1] + gains.shape[0])
    packed_gains = jnp.concatenate(gain_sums)
    packed_gains = jnp.pad(packed_gains, (0, -ends[-1] % (8 * LANES))).reshape(8, -1)
    in_sum, out_sum, gains_all = collect_weights(
        in_grad.astype(jnp.bfloat16), out_grad.astype(jnp.bfloat16), packed_gains, fsdp_count
    )
    gains_sum = jnp.sum(gains_all, axis=(0, 1)).reshape(-1)
    summed = [gains_sum[ends[i] : ends[i + 1]] for i in range(4)]
    return (
        jnp.stack(outputs)[:, None],
        jnp.stack(input_grads)[:, None],
        summed[0],
        in_sum[:, :query_width],
        in_sum[:, query_width : query_width + kv_width],
        in_sum[:, query_width + kv_width :],
        summed[2],
        summed[3],
        out_sum,
        summed[1],
        expert_grads[0],
        expert_grads[1],
        expert_grads[2],
    )


def shards(*arrays):
    tokens, routes, w_gate = arrays[0], arrays[13], arrays[10]
    fsdp_count = lax.axis_size(FSDP)
    gathered = fsdp_count * routes.shape[2] * tokens.shape[3] * 2
    fits = gathered <= 24 * MIB and fsdp_count % PLANE == 0 and lax.axis_size(TP) == 2
    if fits and w_gate.shape[0] == 2:
        return gathered_layer(*arrays)
    return exchanged_layer(*arrays)


def solution(mesh):
    in_specs = (
        P(None, "fsdp", "tp", None),
        P(None, "fsdp", "tp", None),
        P(),
        P("fsdp", "tp"),
        P("fsdp", "tp"),
        P("fsdp", "tp"),
        P(),
        P(),
        P("tp", "fsdp"),
        P(),
        P("fsdp", None, "tp"),
        P("fsdp", None, "tp"),
        P("fsdp", "tp", None),
        P(None, "fsdp", None, None),
        P(None, "fsdp", None, None),
    )
    out_specs = (
        P(None, "fsdp", "tp", None),
        P(None, "fsdp", "tp", None),
        P(),
        P("fsdp", "tp"),
        P("fsdp", "tp"),
        P("fsdp", "tp"),
        P(),
        P(),
        P("tp", "fsdp"),
        P(),
        P("fsdp", None, "tp"),
        P("fsdp", None, "tp"),
        P("fsdp", "tp", None),
    )
    return jax.shard_map(shards, mesh=mesh, in_specs=in_specs, out_specs=out_specs, check_vma=False)
```

```python
import functools

import jax
import jax.numpy as jnp
from jax import lax
from jax.experimental import pallas as pl
from jax.experimental.pallas import tpu as pltpu
from jax.sharding import PartitionSpec as P

BLOCK = 256


EPSILON = 1e-06
ROPE_BASE = 1000000.0
MASKED = -1e30
TILE_PICKS = 128


def rms_scale(row_block, gain_row):
    return (
        row_block
        * lax.rsqrt(jnp.mean(row_block * row_block, axis=-1, keepdims=True) + EPSILON)
        * gain_row
    )


def rotary_tables(sequence_length, head_width):
    half_width = head_width // 2
    inverse = ROPE_BASE ** (-2.0 * jnp.arange(half_width, dtype=jnp.float32) / head_width)
    angles = jnp.arange(sequence_length, dtype=jnp.float32)[:, None] * inverse[None, :]
    cosine_table = jnp.concatenate([jnp.cos(angles), jnp.cos(angles)], axis=-1)[:, None, :]
    sine_values = jnp.concatenate([jnp.sin(angles), jnp.sin(angles)], axis=-1)[:, None, :]
    return (cosine_table, sine_values)


def rotate(head_rows, cosine_table, sine_values):
    half_width = head_rows.shape[-1] // 2
    turned = jnp.concatenate([-head_rows[..., half_width:], head_rows[..., :half_width]], axis=-1)
    return head_rows * cosine_table + turned * sine_values


def prepare_heads(projected, gain_row, cosine_table, sine_values):
    return rotate(rms_scale(projected, gain_row), cosine_table, sine_values)


def swiglu(gate_act, up_act):
    return jax.nn.silu(gate_act) * up_act


def slot_tables(route_rows, gate_rows, expert_count, capacity):
    sequence_length = route_rows.shape[0]
    top_count = route_rows.shape[1]
    pick_count = sequence_length * top_count
    tile_count = pick_count // TILE_PICKS
    flat_routes = route_rows.reshape(-1)
    onehot = (flat_routes[:, None] == jnp.arange(expert_count, dtype=jnp.int32)[None, :]).astype(
        jnp.bfloat16
    )
    tiles = onehot.reshape(tile_count, TILE_PICKS, expert_count)
    positions = jnp.arange(TILE_PICKS, dtype=jnp.int32)
    lower = (positions[None, :] < positions[:, None]).astype(jnp.bfloat16)
    within = jnp.einsum("ij,bje->bie", lower, tiles, preferred_element_type=jnp.float32)
    tile_totals = jnp.sum(tiles.astype(jnp.float32), axis=1)
    offsets = jnp.cumsum(tile_totals, axis=0) - tile_totals
    before = within + offsets[:, None, :]
    slot_rank = jnp.sum(before * tiles.astype(jnp.float32), axis=-1).reshape(-1).astype(jnp.int32)
    slot_index = flat_routes * capacity + slot_rank
    pick_ids = jnp.arange(pick_count, dtype=jnp.int32) // top_count
    slot_owner = (
        jnp.full((expert_count * capacity,), sequence_length, jnp.int32)
        .at[slot_index]
        .set(pick_ids)
    )
    slot_weight = (
        jnp.zeros((expert_count * capacity,), jnp.float32).at[slot_index].set(gate_rows.reshape(-1))
    )
    return (slot_index, slot_owner, slot_weight)


def exchanged_layer(
    tokens,
    cotangent,
    norm1_gain,
    w_query,
    key_projection_weight,
    value_projection_weight,
    query_gain,
    key_gain,
    w_out,
    norm2_gain,
    w_gate,
    w_up,
    w_down,
    routes,
    gates,
):
    batch_count = tokens.shape[0]
    model_width = tokens.shape[3]
    sequence_length = routes.shape[2]
    top_count = routes.shape[3]
    head_features = query_gain.shape[0]
    local_experts = w_gate.shape[0]
    fsdp_count = lax.axis_size("fsdp")
    all_experts = local_experts * fsdp_count
    capacity = 7 * top_count * sequence_length // (6 * all_experts)
    query_heads = w_query.shape[1] // head_features
    kv_heads = key_projection_weight.shape[1] // head_features
    group_size = query_heads // kv_heads
    score_scale = head_features ** (-0.5)
    cosine_table, sine_values = rotary_tables(sequence_length, head_features)
    block_ids = jnp.arange(sequence_length, dtype=jnp.int32) // BLOCK
    visible = (block_ids[None, :] <= block_ids[:, None])[None, None]
    first_gain = norm1_gain.astype(jnp.float32)
    second_gain = norm2_gain.astype(jnp.float32)
    query_factor_scale = query_gain.astype(jnp.float32)
    key_scale = key_gain.astype(jnp.float32)
    zero_row = jnp.zeros((1, model_width), jnp.bfloat16)
    buffer_shape = (fsdp_count, local_experts, capacity, model_width)

    def masked_scores(query_fourfold, key_rows):
        raw_scores = (
            jnp.einsum(
                "qcgd,kcd->cgqk", query_fourfold, key_rows, preferred_element_type=jnp.float32
            )
            * score_scale
        )
        return jnp.where(visible, raw_scores, MASKED)

    def prep_heads(projected, gain_row):
        return prepare_heads(projected, gain_row, cosine_table, sine_values)

    gain_sums = (
        jnp.zeros((model_width,), jnp.float32),
        jnp.zeros((model_width,), jnp.float32),
        jnp.zeros((head_features,), jnp.float32),
        jnp.zeros((head_features,), jnp.float32),
    )
    expert_grads = (
        jnp.zeros(w_gate.shape, jnp.float32),
        jnp.zeros(w_up.shape, jnp.float32),
        jnp.zeros(w_down.shape, jnp.float32),
    )
    attn_grads = tuple(
        (
            jnp.zeros(weight_part.shape, jnp.float32)
            for weight_part in (w_query, key_projection_weight, value_projection_weight, w_out)
        )
    )
    outputs = []
    input_grads = []
    for batch_index in range(batch_count):
        query_full, key_full, value_full, out_full = (
            lax.all_gather(w_query, "fsdp", axis=0, tiled=True),
            lax.all_gather(key_projection_weight, "fsdp", axis=0, tiled=True),
            lax.all_gather(value_projection_weight, "fsdp", axis=0, tiled=True),
            lax.all_gather(w_out, "fsdp", axis=1, tiled=True),
        )
        own_rows = tokens[batch_index, 0].astype(jnp.float32)
        own_cot = cotangent[batch_index, 0]
        route_rows = routes[batch_index, 0]
        gate_rows = gates[batch_index, 0]
        first_normed = rms_scale(own_rows, first_gain).astype(jnp.bfloat16)
        normed_all = lax.all_gather(first_normed, "tp", axis=0, tiled=True)
        query_projected = jnp.dot(
            normed_all, query_full, preferred_element_type=jnp.float32
        ).reshape(sequence_length, query_heads, head_features)
        key_projected = jnp.dot(normed_all, key_full, preferred_element_type=jnp.float32).reshape(
            sequence_length, kv_heads, head_features
        )
        value_row_list = (
            jnp.dot(normed_all, value_full, preferred_element_type=jnp.float32)
            .astype(jnp.bfloat16)
            .reshape(sequence_length, kv_heads, head_features)
        )
        query_rot = prep_heads(query_projected, query_factor_scale).astype(jnp.bfloat16)
        key_rot = prep_heads(key_projected, key_scale).astype(jnp.bfloat16)
        query_fourfold = query_rot.reshape(sequence_length, kv_heads, group_size, head_features)
        scores = masked_scores(query_fourfold, key_rot)
        row_max = jnp.max(scores, axis=-1, keepdims=True)
        exp_scores = jnp.exp(scores - row_max)
        totals = jnp.sum(exp_scores, axis=-1, keepdims=True)
        log_total = row_max + jnp.log(totals)
        prob_rows = (exp_scores / totals).astype(jnp.bfloat16)
        context = (
            jnp.einsum(
                "cgqk,kcd->qcgd", prob_rows, value_row_list, preferred_element_type=jnp.float32
            )
            .astype(jnp.bfloat16)
            .reshape(sequence_length, query_heads * head_features)
        )
        attn_own = lax.psum_scatter(
            jnp.dot(context, out_full, preferred_element_type=jnp.float32).astype(jnp.bfloat16),
            "tp",
            scatter_dimension=0,
            tiled=True,
        ).astype(jnp.float32)
        hidden_own = own_rows + attn_own
        second_normed = rms_scale(hidden_own, second_gain).astype(jnp.bfloat16)
        normed_two, cot_all = (
            lax.all_gather(second_normed, "tp", axis=0, tiled=True),
            lax.all_gather(own_cot, "tp", axis=0, tiled=True),
        )
        slot_index, slot_owner, slot_weight = slot_tables(
            route_rows, gate_rows, all_experts, capacity
        )
        padded_rows = jnp.concatenate([normed_two, zero_row], axis=0)
        send_rows = padded_rows[slot_owner].reshape(buffer_shape)
        expert_in = lax.all_to_all(send_rows, "fsdp", split_axis=0, concat_axis=0, tiled=True)
        gate_act = jnp.einsum(
            "sekd,edf->sekf", expert_in, w_gate, preferred_element_type=jnp.float32
        )
        up_act = jnp.einsum("sekd,edf->sekf", expert_in, w_up, preferred_element_type=jnp.float32)
        act_rows = swiglu(gate_act, up_act).astype(jnp.bfloat16)
        expert_out = jnp.einsum(
            "sekf,efd->sekd", act_rows, w_down, preferred_element_type=jnp.float32
        )
        returned = lax.all_to_all(
            expert_out.astype(jnp.bfloat16), "fsdp", split_axis=0, concat_axis=0, tiled=True
        ).astype(expert_out.dtype)
        picked = returned.reshape(all_experts * capacity, model_width)[slot_index].reshape(
            sequence_length, top_count, model_width
        )
        moe_part = jnp.sum(picked * gate_rows[:, :, None], axis=1)
        moe_own = lax.psum_scatter(
            moe_part.astype(jnp.bfloat16), "tp", scatter_dimension=0, tiled=True
        ).astype(jnp.float32)
        outputs.append((hidden_own + moe_own).astype(jnp.bfloat16))
        cot_padded = jnp.concatenate([cot_all, zero_row], axis=0)
        send_grads = (
            (slot_weight[:, None] * cot_padded[slot_owner])
            .astype(jnp.bfloat16)
            .reshape(buffer_shape)
        )
        out_grads = lax.all_to_all(send_grads, "fsdp", split_axis=0, concat_axis=0, tiled=True)
        act_grads = jnp.einsum(
            "sekd,efd->sekf", out_grads, w_down, preferred_element_type=jnp.float32
        )
        _, swiglu_back = jax.vjp(swiglu, gate_act, up_act)
        gate_grads, up_grads = swiglu_back(act_grads)
        gate_grads = gate_grads.astype(jnp.bfloat16)
        up_grads = up_grads.astype(jnp.bfloat16)
        expert_grads = (
            expert_grads[0]
            + jnp.einsum(
                "sekd,sekf->edf", expert_in, gate_grads, preferred_element_type=jnp.float32
            ),
            expert_grads[1]
            + jnp.einsum("sekd,sekf->edf", expert_in, up_grads, preferred_element_type=jnp.float32),
            expert_grads[2]
            + jnp.einsum("sekf,sekd->efd", act_rows, out_grads, preferred_element_type=jnp.float32),
        )
        input_part = jnp.einsum(
            "sekf,edf->sekd", gate_grads, w_gate, preferred_element_type=jnp.float32
        ) + jnp.einsum("sekf,edf->sekd", up_grads, w_up, preferred_element_type=jnp.float32)
        input_back = lax.all_to_all(
            input_part.astype(jnp.bfloat16), "fsdp", split_axis=0, concat_axis=0, tiled=True
        ).astype(input_part.dtype)
        normed_grads = jnp.sum(
            input_back.reshape(all_experts * capacity, model_width)[slot_index].reshape(
                sequence_length, top_count, model_width
            ),
            axis=1,
        )
        normed_own = lax.psum_scatter(
            normed_grads.astype(jnp.bfloat16), "tp", scatter_dimension=0, tiled=True
        ).astype(jnp.float32)
        _, second_back = jax.vjp(rms_scale, hidden_own, second_gain)
        hidden_part, second_gain_grad = second_back(normed_own)
        hidden_grad = own_cot.astype(jnp.float32) + hidden_part
        attn_grad_all = lax.all_gather(hidden_grad.astype(jnp.bfloat16), "tp", axis=0, tiled=True)
        out_weight_grad = jnp.einsum(
            "th,td->hd", context, attn_grad_all, preferred_element_type=jnp.float32
        )
        context_grad = (
            jnp.einsum("td,hd->th", attn_grad_all, out_full, preferred_element_type=jnp.float32)
            .astype(jnp.bfloat16)
            .reshape(sequence_length, kv_heads, group_size, head_features)
        )
        exp_again = jnp.exp(masked_scores(query_fourfold, key_rot) - log_total)
        probs_again = exp_again.astype(jnp.bfloat16)
        prob_grads = jnp.einsum(
            "qcgd,kcd->cgqk", context_grad, value_row_list, preferred_element_type=jnp.float32
        )
        value_grads = (
            jnp.einsum(
                "cgqk,qcgd->kcd", probs_again, context_grad, preferred_element_type=jnp.float32
            )
            .astype(jnp.bfloat16)
            .reshape(sequence_length, kv_heads * head_features)
        )
        score_grads = (
            exp_again * (prob_grads - jnp.sum(exp_again * prob_grads, axis=-1, keepdims=True))
        ).astype(jnp.bfloat16)
        query_rot_grads = (
            jnp.einsum("cgqk,kcd->qcgd", score_grads, key_rot, preferred_element_type=jnp.float32)
            * score_scale
        ).reshape(sequence_length, query_heads, head_features)
        key_rot_grads = (
            jnp.einsum(
                "cgqk,qcgd->kcd", score_grads, query_fourfold, preferred_element_type=jnp.float32
            )
            * score_scale
        )
        _, query_back = jax.vjp(prep_heads, query_projected, query_factor_scale)
        query_proj_grads, query_gain_grad = query_back(query_rot_grads)
        _, key_back = jax.vjp(prep_heads, key_projected, key_scale)
        key_proj_grads, key_gain_grad = key_back(key_rot_grads)
        query_proj_grads = query_proj_grads.astype(jnp.bfloat16).reshape(
            sequence_length, query_heads * head_features
        )
        key_proj_grads = key_proj_grads.astype(jnp.bfloat16).reshape(
            sequence_length, kv_heads * head_features
        )
        first_normed_grads = (
            jnp.einsum(
                "tq,dq->td", query_proj_grads, query_full, preferred_element_type=jnp.float32
            )
            + jnp.einsum("tq,dq->td", key_proj_grads, key_full, preferred_element_type=jnp.float32)
            + jnp.einsum("tq,dq->td", value_grads, value_full, preferred_element_type=jnp.float32)
        )
        weight_parts = (
            jnp.einsum(
                "td,tq->dq", normed_all, query_proj_grads, preferred_element_type=jnp.float32
            ),
            jnp.einsum("td,tq->dq", normed_all, key_proj_grads, preferred_element_type=jnp.float32),
            jnp.einsum("td,tq->dq", normed_all, value_grads, preferred_element_type=jnp.float32),
            out_weight_grad,
        )
        first_own = lax.psum_scatter(
            first_normed_grads.astype(jnp.bfloat16), "tp", scatter_dimension=0, tiled=True
        ).astype(jnp.float32)
        _, first_back = jax.vjp(rms_scale, own_rows, first_gain)
        row_part, first_gain_grad = first_back(first_own)
        input_grads.append((hidden_grad + row_part).astype(jnp.bfloat16))
        gain_sums = (
            gain_sums[0] + first_gain_grad,
            gain_sums[1] + second_gain_grad,
            gain_sums[2] + query_gain_grad,
            gain_sums[3] + key_gain_grad,
        )
        attn_grads = jax.tree.map(
            jnp.add,
            attn_grads,
            (
                lax.psum_scatter(weight_parts[0], "fsdp", scatter_dimension=0, tiled=True),
                lax.psum_scatter(weight_parts[1], "fsdp", scatter_dimension=0, tiled=True),
                lax.psum_scatter(weight_parts[2], "fsdp", scatter_dimension=0, tiled=True),
                lax.psum_scatter(weight_parts[3], "fsdp", scatter_dimension=1, tiled=True),
            ),
        )
    summed = lax.psum((gain_sums[0], gain_sums[1], gain_sums[2], gain_sums[3]), ("fsdp", "tp"))
    block_out = jnp.stack(outputs)[:, None]
    input_grad = jnp.stack(input_grads)[:, None]
    return (
        block_out,
        input_grad,
        summed[0],
        attn_grads[0],
        attn_grads[1],
        attn_grads[2],
        summed[2],
        summed[3],
        attn_grads[3],
        summed[1],
        expert_grads[0],
        expert_grads[1],
        expert_grads[2],
    )


MESH = pl.DeviceIdType.MESH
FSDP, TP = "fsdp", "tp"
PLANE = 4
LANES = 128
MIB = 1 << 20
RIGHT, LEFT, FIRST, SECOND, CORE, CROSS = range(6)
TRANSPOSED_LEFT = (((0,), (0,)), ((), ()))
TRANSPOSED_RIGHT = (((1,), (1,)), ((), ()))
OUTPUT, BACK = range(2)
CHUNK = 512


class Spot:
    def __init__(self, line, wide, turned=True):
        self.line = line
        self.wide = wide
        self.turned = turned
        self.planes = 4 if wide else 2
        index = lax.axis_index(FSDP)
        self.x = lax.axis_index(TP)
        self.z = lax.div(index, PLANE)
        self.y = lax.rem(lax.div(index, 2), 2)
        self.core = lax.rem(index, 2)

    def side(self, core, first, second):
        flip_y, flip_x = first, second
        if self.wide and self.turned:
            flip_y = (1 - core) * first + core * second
            flip_x = core * first + (1 - core) * second
        return self.y + flip_y * (1 - 2 * self.y), self.x + flip_x * (1 - 2 * self.x)

    def block(self, core, first, second, z):
        y, x = self.side(core, first, second)
        return z * PLANE + y * 2 + core, x

    def device(self, kind):
        if kind == RIGHT:
            return self.block(self.core, 0, 0, self.z + 1)
        if kind == LEFT:
            return self.block(self.core, 0, 0, self.z - 1)
        if kind == CORE:
            return self.block(1 - self.core, 0, 0, self.z)
        if kind == CROSS:
            return self.block(self.core, 0, 0, self.z)[0], 1 - self.x
        return self.block(self.core, int(kind == FIRST), int(kind == SECOND), self.z)

    def kinds(self):
        return (FIRST, SECOND, CORE) if self.wide else (FIRST, CORE)

    def number(self, first, second, z):
        return (second * 2 + first) * self.line + z

    def order(self, step):
        if isinstance(step, int) and step == 0:
            return [(self.z, None)]
        return [(self.z - step, self.z - step >= 0), (self.z + step, self.z + step < self.line)]

    def greet(self):
        barrier = pltpu.get_barrier_semaphore()

        def signal(kind):
            pl.semaphore_signal(barrier, inc=1, device_id=self.device(kind), device_id_type=MESH)

        for kind in self.kinds():
            signal(kind)
        when(self.z + 1 < self.line, lambda: signal(RIGHT))
        when(self.z > 0, lambda: signal(LEFT))
        around = (self.z + 1 < self.line).astype(jnp.int32) + (self.z > 0).astype(jnp.int32)
        pl.semaphore_wait(barrier, len(self.kinds()) + around)

    def send(self, source, target, send_sem, receive_sem, kind):
        return pltpu.make_async_remote_copy(
            src_ref=source,
            dst_ref=target,
            send_sem=send_sem,
            recv_sem=receive_sem,
            device_id=self.device(kind),
            device_id_type=MESH,
        )


def when(condition, action):
    def run():
        action()

    if condition is None:
        run()
    else:
        pl.when(condition)(run)


class Spread:
    def __init__(self, spot, source, slot, send, receive, local):
        self.spot = spot
        self.slot = slot
        self.source = source
        self.sends = send
        self.receives = receive
        self.mine = pltpu.make_async_copy(source, slot(*spot.block(spot.core, 0, 0, spot.z)), local)

    def copy(self, first, second, z, kind, own=False):
        spot = self.spot
        place = self.slot(*spot.block(spot.core, first, second, z))
        number = spot.number(first, second, z)
        arrival = {
            RIGHT: number,
            LEFT: number,
            FIRST: spot.number(1, 0, z),
            SECOND: spot.number(first, 1, z),
            CORE: spot.planes * spot.line + number,
        }[kind]
        departure = {RIGHT: 0, LEFT: 1, FIRST: 2, SECOND: 3, CORE: 5}[kind] * spot.line + number
        source = self.source if own else place
        return spot.send(source, place, self.sends.at[departure], self.receives.at[arrival], kind)

    def arrived(self, first, second, z, other=False):
        spot = self.spot
        core = 1 - spot.core if other else spot.core
        place = self.slot(*spot.block(core, first, second, z))
        number = spot.number(first, second, z) + (spot.planes * spot.line if other else 0)
        spot.send(place, place, self.sends.at[0], self.receives.at[number], CORE).wait_recv()

    def steps(self):
        return self.spot.line + (3 if self.spot.wide else 1)

    def begin(self):
        spot = self.spot
        z = spot.z
        when(z + 1 < spot.line, lambda: self.copy(0, 0, z, RIGHT, True).start())
        when(z > 0, lambda: self.copy(0, 0, z, LEFT, True).start())
        for kind in spot.kinds():
            self.copy(0, 0, z, kind, True).start()
        self.mine.start()

    def step(self, step):
        spot = self.spot
        line, z = spot.line, spot.z

        def reached(away, action):
            inside = jnp.logical_and(away >= 0, away < line)
            when(jnp.logical_and(inside, z - away >= 0), lambda: action(z - away, True))
            when(
                jnp.logical_and(inside, jnp.logical_and(away > 0, z + away < line)),
                lambda: action(z + away, False),
            )

        def along(zz, from_left):
            self.arrived(0, 0, zz)
            if from_left:
                when(z + 1 < line, lambda: self.copy(0, 0, zz, RIGHT).start())
            else:
                when(z > 0, lambda: self.copy(0, 0, zz, LEFT).start())
            for kind in spot.kinds():
                self.copy(0, 0, zz, kind).start()

        def firsts(zz, _):
            self.arrived(1, 0, zz)
            if spot.wide:
                self.copy(1, 0, zz, SECOND).start()
            self.copy(1, 0, zz, CORE).start()

        def lasts(first):
            def action(zz, _):
                self.arrived(first, 1, zz)
                self.copy(first, 1, zz, CORE).start()

            return action

        step = jnp.asarray(step, jnp.int32)
        reached(step, along)
        reached(step - 1, firsts)
        if spot.wide:
            reached(step - 2, lasts(0))
            reached(step - 3, lasts(1))

    def finish(self):
        spot = self.spot
        z = spot.z

        def body(zz, _):
            when(
                jnp.logical_and(z + 1 < spot.line, zz <= z),
                lambda: self.copy(0, 0, zz, RIGHT).wait_send(),
            )
            when(jnp.logical_and(z > 0, zz >= z), lambda: self.copy(0, 0, zz, LEFT).wait_send())
            self.copy(0, 0, zz, FIRST).wait_send()
            for second in range(2 if spot.wide else 1):
                for first in (0, 1):
                    if spot.wide and not second:
                        self.copy(first, 0, zz, SECOND).wait_send()
                    self.copy(first, second, zz, CORE).wait_send()
                    self.arrived(first, second, zz, other=True)
            return 0

        lax.fori_loop(0, spot.line, body, 0)
        self.mine.wait()


def run_trees(trees):
    for tree in trees:
        tree.begin()

    def body(step, _):
        for tree in trees:
            tree.step(step)
        return 0

    lax.fori_loop(1, max(tree.steps() for tree in trees), body, 0)
    for tree in trees:
        tree.finish()


def spread_count(line, wide):
    return (9 if wide else 7) * line, (8 if wide else 4) * line


def rows_at(ref, index, size):
    return ref.at[pl.ds(pl.multiple_of(index * size, 16), size)]


def columns_at(ref, index, size):
    return ref.at[:, pl.ds(pl.multiple_of(index * size, LANES), size)]


def norm_rows(target, source, gain):
    def body(step, _):
        rows = pl.ds(pl.multiple_of(step * 16, 16), 16)
        value = source[rows, :].astype(jnp.float32)
        target[rows, :] = rms_scale(value, gain[...]).astype(target.dtype)
        return 0

    lax.fori_loop(0, target.shape[0] // 16, body, 0)


def turned_heads(value, gain, cosine, sine):
    normed = rms_scale(value, gain)
    return normed * cosine + pltpu.roll(normed, normed.shape[-1] // 2, 1) * sine


def visible_blocks(length):
    return [
        (start, min(start + BLOCK, length), min(start + BLOCK, length))
        for start in range(0, length, BLOCK)
    ]


def forward_kernel(
    line,
    heads,
    kv_heads,
    tokens_ref,
    cot_ref,
    in_ref,
    out_ref,
    picks_ref,
    gain1_ref,
    gain2_ref,
    query_gain_ref,
    key_gain_ref,
    cosine_ref,
    sine_ref,
    cot_all,
    in_all,
    out_all,
    picks_all,
    normed_all,
    projected_all,
    context_all,
    hidden_all,
    second_all,
    in_w,
    out_w,
    tokens,
    normed,
    projected,
    context,
    keys,
    values,
    mixed,
    mixed_other,
    hidden,
    second,
    narrow_send,
    narrow_receive,
    wide_send,
    wide_receive,
    local,
    token_send,
    token_receive,
    mixed_send,
    mixed_receive,
    save_sem,
):
    batch, half, width = tokens_ref.shape
    length = 2 * half
    depth, out_width = in_ref.shape[0], out_ref.shape[1]
    features = query_gain_ref.shape[1]
    narrow = Spot(line, False)
    spots = [Spot(line, True, turned=i > 0) for i in range(batch)]
    spot = spots[0]
    x = spot.x
    spot.greet()
    slots = [
        (picks_ref, lambda block, side: picks_all.at[block]),
        (in_ref, lambda block, side: rows_at(in_w, block, depth)),
        (out_ref, lambda block, side: columns_at(out_w, block, out_width)),
    ]
    weights = [
        Spread(narrow, source, slot, narrow_send.at[i], narrow_receive.at[i], local.at[i])
        for i, (source, slot) in enumerate(slots)
    ]
    cots = [
        Spread(
            spots[i],
            cot_ref.at[i],
            lambda block, side, i=i: rows_at(cot_all.at[i, block], side, half),
            wide_send.at[i],
            wide_receive.at[i],
            local.at[3 + i],
        )
        for i in range(batch)
    ]
    for tree in weights:
        tree.begin()

    def token_copies(i):
        place = rows_at(tokens.at[i], x, half)
        return (
            pltpu.make_async_copy(tokens_ref.at[i], place, local.at[3 + batch + i]),
            spot.send(tokens_ref.at[i], place, token_send.at[i], token_receive.at[i], CROSS),
        )

    for i in range(batch):
        for copy in token_copies(i):
            copy.start()
    cots[0].begin()

    def steps(step, _):
        for tree in weights + cots[:1]:
            tree.step(step)
        return 0

    lax.fori_loop(1, weights[0].steps(), steps, 0)
    for i in range(batch):
        mine, other = token_copies(i)
        mine.wait()
        other.wait_send()
        place = rows_at(tokens.at[i], 1 - x, half)
        spot.send(place, place, token_send.at[i], token_receive.at[i], CROSS).wait_recv()
    for i in range(batch):
        norm_rows(normed.at[i], tokens.at[i], gain1_ref)
    for tree in weights:
        tree.finish()
    for tree in cots[1:]:
        tree.begin()

    def save(source, target, index):
        return pltpu.make_async_copy(source, target, save_sem.at[index])

    saves = [save(in_w, in_all, 0), save(out_w, out_all, 1)]
    for copy in saves:
        copy.start()

    def project(i):
        for start in range(0, in_w.shape[1], CHUNK):
            projected[i, :, start : start + CHUNK] = jnp.dot(
                normed[i], in_w[:, start : start + CHUNK], preferred_element_type=jnp.float32
            )

    scale = features ** (-0.5)

    def attend(i):
        base = heads * features
        for head in range(kv_heads):
            at = base + head * features
            keys[head] = turned_heads(
                projected[i, :, at : at + features],
                key_gain_ref[...],
                cosine_ref[...],
                sine_ref[...],
            ).astype(jnp.bfloat16)
            at = base + (kv_heads + head) * features
            values[head] = projected[i, :, at : at + features].astype(jnp.bfloat16)

        def one(head, _):
            columns = pl.ds(pl.multiple_of(head * features, LANES), features)
            query = turned_heads(
                projected[i, :, columns], query_gain_ref[...], cosine_ref[...], sine_ref[...]
            ).astype(jnp.bfloat16)
            shared = lax.div(head, heads // kv_heads)
            for start, stop, seen in visible_blocks(length):
                scores = (
                    lax.dot_general(
                        query[start:stop],
                        keys[shared, :seen, :],
                        TRANSPOSED_RIGHT,
                        preferred_element_type=jnp.float32,
                    )
                    * scale
                )
                raised = jnp.exp(scores - jnp.max(scores, axis=-1, keepdims=True))
                shares = raised / jnp.sum(raised, axis=-1, keepdims=True)
                context[i, start:stop, columns] = jnp.dot(
                    shares.astype(jnp.bfloat16),
                    values[shared, :seen, :],
                    preferred_element_type=jnp.float32,
                ).astype(jnp.bfloat16)
            return 0

        lax.fori_loop(0, heads, one, 0)

    def mixed_copy(i):
        return spot.send(
            rows_at(mixed.at[i], 1 - x, half),
            mixed_other.at[i],
            mixed_send.at[i],
            mixed_receive.at[i],
            CROSS,
        )

    def mix(i):
        for start in range(0, width, CHUNK):
            mixed[i, :, start : start + CHUNK] = jnp.dot(
                context[i], out_w[:, start : start + CHUNK], preferred_element_type=jnp.float32
            ).astype(jnp.bfloat16)
        mixed_copy(i).start()

    def close(i):
        mixed_copy(i).wait()
        add_rows(
            hidden.at[i],
            [rows_at(tokens.at[i], x, half), rows_at(mixed.at[i], x, half), mixed_other.at[i]],
        )
        norm_rows(second.at[i], hidden.at[i], gain2_ref)

    pending = []
    for i in range(batch):
        pending += [functools.partial(work, i) for work in (project, attend, mix)]
    pending += [functools.partial(close, i) for i in range(batch)]
    later = [(cots[0], step) for step in range(weights[0].steps(), cots[0].steps())]
    for tree in cots[1:]:
        later += [(tree, step) for step in range(1, tree.steps())]
    while pending or later:
        if pending:
            pending.pop(0)()
        for _ in range(2):
            if later:
                tree, step = later.pop(0)
                tree.step(step)

    saves += [
        save(source, target, 2 + i)
        for i, (source, target) in enumerate(
            [
                (normed, normed_all),
                (projected, projected_all),
                (context, context_all),
                (hidden, hidden_all),
                (second, second_all),
            ]
        )
    ]
    for copy in saves[2:]:
        copy.start()
    for tree in cots:
        tree.finish()
    for copy in saves:
        copy.wait()


def run_forward(tokens, cot, weight_in, weight_out, picks, gains, tables, fsdp_count, kv_heads):
    line = fsdp_count // PLANE
    batch, half, width = tokens.shape
    length = 2 * half
    features = gains[2].shape[1]
    heads = weight_out.shape[0] // features
    in_shape = (weight_in.shape[0] * fsdp_count, weight_in.shape[1])
    out_shape = (weight_out.shape[0], weight_out.shape[1] * fsdp_count)
    wide, narrow = spread_count(line, True), spread_count(line, False)
    anywhere = pl.BlockSpec(memory_space=pl.ANY)
    inside = pl.BlockSpec(memory_space=pltpu.VMEM)
    shape = lambda dims, kind=jnp.bfloat16: jax.ShapeDtypeStruct(dims, kind)
    vmem = lambda *dims: pltpu.VMEM(dims, jnp.bfloat16)
    sem = lambda *dims: pltpu.SemaphoreType.DMA(dims)
    kept = (
        ((batch, length, width), jnp.bfloat16),
        ((batch, length, weight_in.shape[1]), jnp.float32),
        ((batch, length, heads * features), jnp.bfloat16),
        ((batch, half, width), jnp.float32),
        ((batch, half, width), jnp.bfloat16),
    )
    return pl.pallas_call(
        functools.partial(forward_kernel, line, heads, kv_heads),
        out_shape=(
            shape((batch, fsdp_count, length, width)),
            shape(in_shape),
            shape(out_shape),
            shape((fsdp_count, *picks.shape), picks.dtype),
            *(shape(*one) for one in kept),
        ),
        in_specs=[anywhere] * 5 + [inside] * 6,
        out_specs=(anywhere,) * 9,
        scratch_shapes=[
            vmem(*in_shape),
            vmem(*out_shape),
            vmem(batch, length, width),
            *(pltpu.VMEM(*one) for one in kept[:3]),
            vmem(kv_heads, length, features),
            vmem(kv_heads, length, features),
            vmem(batch, length, width),
            vmem(batch, half, width),
            *(pltpu.VMEM(*one) for one in kept[3:]),
            sem(3, narrow[0]),
            sem(3, narrow[1]),
            sem(batch, wide[0]),
            sem(batch, wide[1]),
            sem(3 + 2 * batch),
            sem(batch),
            sem(batch),
            sem(batch),
            sem(batch),
            sem(7),
        ],
        compiler_params=pltpu.CompilerParams(
            collective_id=1, has_side_effects=True, vmem_limit_bytes=60 * MIB
        ),
    )(tokens, cot, weight_in, weight_out, picks, *gains, *tables)


def add_rows(target, sources):
    def body(step, _):
        rows = pl.ds(pl.multiple_of(step * 16, 16), 16)
        total = sources[0][rows, :].astype(jnp.float32)
        for source in sources[1:]:
            total = total + source[rows, :].astype(jnp.float32)
        target[rows, :] = total.astype(target.dtype)
        return 0

    lax.fori_loop(0, target.shape[0] // 16, body, 0)


def collect(spot, items, send, receive, local):
    line, z, core = spot.line, spot.z, spot.core
    every = range(len(items))
    base = {CORE: 0, FIRST: 2 * line, RIGHT: 3 * line, LEFT: 4 * line}

    def copy(item, kind, first, zz):
        part, _, own, cores, firsts, rights, lefts = items[item]
        number = first * line + zz
        index = number if kind == CORE else zz
        source = part(*spot.block(1 - core, first, 0, zz)) if kind == CORE else own.at[number]
        place = {CORE: cores, FIRST: firsts, RIGHT: rights, LEFT: lefts}[kind].at[index]
        return spot.send(
            source,
            place,
            send.at[item, base[kind] + index],
            receive.at[item, base[kind] + index],
            kind,
        )

    def load(item, first, zz):
        part, own = items[item][0], items[item][2]
        number = first * line + zz
        return pltpu.make_async_copy(
            part(*spot.block(core, first, 0, zz)), own.at[number], local.at[item, number]
        )

    def ordered(action):
        for step in reversed(range(line)):
            for zz, valid in spot.order(step):
                when(valid, lambda: [action(item, zz) for item in every])

    for first in (1, 0):

        def fetch(item, zz):
            copy(item, CORE, first, zz).start()
            load(item, first, zz).start()

        ordered(fetch)

    def summed(item, first, zz, target=None, extra=()):
        _, _, own, cores, firsts, _, _ = items[item]
        number = first * line + zz
        load(item, first, zz).wait()
        copy(item, CORE, first, zz).wait_recv()
        sources = [own.at[number], cores.at[number]]
        if not first:
            copy(item, FIRST, 1, zz).wait_recv()
            sources.append(firsts.at[zz])
        add_rows(own.at[number] if target is None else target, sources + list(extra))

    def to_first(item, zz):
        summed(item, 1, zz)
        copy(item, FIRST, 1, zz).start()

    ordered(to_first)

    for step in reversed(range(1, line)):
        for kind, zz, valid in zip((LEFT, RIGHT), *zip(*spot.order(step))):

            def onward():
                behind = z > 0 if kind == RIGHT else z + 1 < line
                for item in every:
                    incoming = items[item][5 if kind == RIGHT else 6].at[zz]

                    def with_incoming():
                        copy(item, kind, 0, zz).wait_recv()
                        summed(item, 0, zz, extra=[incoming])

                    when(behind, with_incoming)
                    when(jnp.logical_not(behind), lambda: summed(item, 0, zz))
                    copy(item, kind, 0, zz).start()

            when(valid, onward)

    def finish(kinds):
        for item in every:
            for kind in kinds:
                copy(item, kind, 0, z).wait_recv()
            incoming = [items[item][5 if kind == RIGHT else 6].at[z] for kind in kinds]
            summed(item, 0, z, target=items[item][1], extra=incoming)

    when(z == 0, lambda: finish([LEFT]))
    when(z == line - 1, lambda: finish([RIGHT]))
    when(jnp.logical_and(z > 0, z < line - 1), lambda: finish([RIGHT, LEFT]))

    for item in every:
        for zz in range(line):
            when(zz > z, lambda: copy(item, RIGHT, 0, zz).wait_send())
            when(zz < z, lambda: copy(item, LEFT, 0, zz).wait_send())
            copy(item, FIRST, 1, zz).wait_send()
            for first in (0, 1):
                copy(item, CORE, first, zz).wait_send()


def collect_scratch(line, shape):
    counts = (2 * line, 2 * line, line, line, line)
    return [pltpu.VMEM((count, *shape), jnp.bfloat16) for count in counts]


def collect_weights_kernel(
    line, in_part, out_part, gains_ref, in_total, out_total, gains_all, *scratch
):
    buffers, (send, receive, local, gain_send, gain_receive, gain_local) = (
        scratch[:-6],
        scratch[-6:],
    )
    narrow, spot = Spot(line, False), Spot(line, True)
    spot.greet()
    slot = lambda block, half: gains_all.at[block, half]
    run_trees([Spread(spot, gains_ref, slot, gain_send, gain_receive, gain_local.at[0])])
    depth, width = in_total.shape[0], out_total.shape[1]
    items = [
        (lambda block, half: rows_at(in_part, block, depth), in_total, *buffers[:5]),
        (lambda block, half: columns_at(out_part, block, width), out_total, *buffers[5:]),
    ]
    collect(narrow, items, send, receive, local)


def collect_weights(in_part, out_part, gains, fsdp_count):
    line = fsdp_count // PLANE
    in_shape = (in_part.shape[0] // fsdp_count, in_part.shape[1])
    out_shape = (out_part.shape[0], out_part.shape[1] // fsdp_count)
    sends, receives = spread_count(line, True)
    return pl.pallas_call(
        functools.partial(collect_weights_kernel, line),
        out_shape=(
            jax.ShapeDtypeStruct(in_shape, jnp.float32),
            jax.ShapeDtypeStruct(out_shape, jnp.float32),
            jax.ShapeDtypeStruct((fsdp_count, 2, *gains.shape), jnp.float32),
        ),
        in_specs=[pl.BlockSpec(memory_space=pl.ANY)] * 3,
        out_specs=(
            pl.BlockSpec(memory_space=pltpu.VMEM),
            pl.BlockSpec(memory_space=pltpu.VMEM),
            pl.BlockSpec(memory_space=pl.ANY),
        ),
        scratch_shapes=collect_scratch(line, in_shape)
        + collect_scratch(line, out_shape)
        + [
            pltpu.SemaphoreType.DMA((2, 5 * line)),
            pltpu.SemaphoreType.DMA((2, 5 * line)),
            pltpu.SemaphoreType.DMA((2, 2 * line)),
            pltpu.SemaphoreType.DMA((sends,)),
            pltpu.SemaphoreType.DMA((receives,)),
            pltpu.SemaphoreType.DMA((1,)),
        ],
        compiler_params=pltpu.CompilerParams(
            collective_id=3, has_side_effects=True, vmem_limit_bytes=56 * MIB
        ),
    )(in_part, out_part, gains)


def experts_kernel(
    line,
    slots,
    own_ref,
    cot_ref,
    info_ref,
    gate_ref,
    up_ref,
    down_ref,
    all_ref,
    total_ref,
    xe_all,
    ce_all,
    act_all,
    dgate_all,
    dup_all,
    part,
    cores,
    seconds,
    firsts,
    ends,
    hidden_w,
    down_w,
    x_rows,
    c_rows,
    xe,
    ce,
    acts,
    dgates,
    dups,
    hidden_grads,
    picks,
    weigh,
    rows,
    stage,
    inbox,
    outbox,
    summed,
    tree_send,
    tree_receive,
    tree_local,
    load_sem,
    save_sem,
    stage_sem,
    inbox_sem,
    outbox_sem,
    weight_sem,
    core_receive,
    second_receive,
    first_receive,
    end_receive,
):
    spot = Spot(line, True)
    z, core = spot.z, spot.core
    batch, half, width = own_ref.shape
    length = 2 * half
    units = down_ref.shape[1]
    groups = batch * line
    weights = [
        pltpu.make_async_copy(source, target, weight_sem.at[i])
        for i, (source, target) in enumerate(
            [(down_ref, down_w)]
            + [(gate_ref.at[e], hidden_w.at[e, :, pl.ds(0, units)]) for e in range(2)]
            + [(up_ref.at[e], hidden_w.at[e, :, pl.ds(units, units)]) for e in range(2)]
        )
    ]
    for copy in weights:
        copy.start()
    rows[...] = jnp.zeros_like(rows)
    spot.greet()

    def half_of(ref, index):
        return rows_at(ref, index, half)

    trees = [
        Spread(
            spot,
            own_ref.at[i],
            lambda block, side, i=i: half_of(all_ref.at[i, block], side),
            tree_send.at[i],
            tree_receive.at[i],
            tree_local.at[i],
        )
        for i in range(batch)
    ]
    run_trees(trees[:1])
    for tree in trees[1:]:
        tree.begin()
    for copy in weights:
        copy.wait()

    def plane_of(group):
        turn = lax.rem(group, line)
        step = lax.div(turn, 2)
        return jnp.where(lax.rem(turn, 2) == 0, step, line - 1 - step)

    def load_group(group, member):
        at = lax.div(group, line)
        sequence = plane_of(group) * PLANE + member
        slot = lax.rem(member, 2)
        return [
            pltpu.make_async_copy(all_ref.at[at, sequence], x_rows.at[slot], load_sem.at[0, slot]),
            pltpu.make_async_copy(cot_ref.at[at, sequence], c_rows.at[slot], load_sem.at[1, slot]),
        ]

    def saves(group):
        to = lambda ref, expert: rows_at(ref.at[expert], group, PLANE * slots)
        pairs = ((xe, xe_all), (ce, ce_all), (acts, act_all), (dgates, dgate_all), (dups, dup_all))
        return [
            pltpu.make_async_copy(source.at[expert], to(target, expert), save_sem.at[2 * i + expert])
            for i, (source, target) in enumerate(pairs)
            for expert in range(2)
        ]

    def staged(group, tensor, y, mine):
        unit = group * 2 + tensor
        slot = y * 2 + mine
        if mine:
            return pltpu.make_async_copy(stage.at[slot], part.at[unit, y], stage_sem.at[slot])
        return spot.send(
            stage.at[slot], cores.at[unit, y], stage_sem.at[slot], core_receive.at[unit, y], CORE
        )

    def combine(group, tensor):
        for y in range(2):
            for mine in range(2):
                member = y * 2 + (core if mine else 1 - core)
                for start in range(0, width, CHUNK):
                    stage[y * 2 + mine, :, start : start + CHUNK] = lax.dot_general(
                        picks[member],
                        rows[member, :, start : start + CHUNK],
                        TRANSPOSED_LEFT,
                        preferred_element_type=jnp.float32,
                    ).astype(jnp.bfloat16)
                staged(group, tensor, y, mine).start()

    def stages_done(group, tensor):
        for y in range(2):
            staged(group, tensor, y, 1).wait()
            staged(group, tensor, y, 0).wait_send()

    def compute(group):
        when(group > 0, lambda: [copy.wait() for copy in saves(group - 1)] and None)

        def pick(member, _):
            slot = lax.rem(member, 2)
            for copy in load_group(group, member):
                copy.wait()

            @pl.when(member + 1 < PLANE)
            def _():
                for copy in load_group(group, member + 1):
                    copy.start()

            sequence = plane_of(group) * PLANE + member
            info = info_ref[lax.div(group, line) * line * PLANE + sequence]
            places = lax.broadcasted_iota(jnp.int32, (2 * LANES, length), 0)
            lower = places < LANES
            ranks = jnp.where(lower, info[0:1], info[1:2] + float(LANES)).astype(jnp.int32)
            some = jnp.where(lower, info[0:1], info[1:2]) >= 0.0
            hot = jnp.logical_and(ranks == places, some)
            chosen = hot.astype(jnp.float32).astype(jnp.bfloat16)
            picks[member] = chosen
            shares = jnp.where(hot, jnp.where(lower, info[2:3], info[3:4]), 0.0)
            column = jnp.sum(shares, axis=1, keepdims=True)
            here = pl.ds(pl.multiple_of(member * slots, 16), slots)
            for expert in range(2):
                weigh[expert, here, :] = jnp.broadcast_to(
                    column[expert * LANES : expert * LANES + slots], (slots, LANES)
                )
            for source, target in ((x_rows, xe), (c_rows, ce)):
                for start in range(0, width, CHUNK):
                    selected = jnp.dot(
                        chosen,
                        source[slot, :, start : start + CHUNK],
                        preferred_element_type=jnp.float32,
                    ).astype(jnp.bfloat16)
                    for expert in range(2):
                        target[expert, here, start : start + CHUNK] = selected[
                            expert * LANES : expert * LANES + slots
                        ]
            return 0

        lax.fori_loop(0, PLANE, pick, 0)

        def keep(expert, product, start):
            at = pl.ds(pl.multiple_of(expert * LANES, LANES), slots)
            for one in range(PLANE):
                rows[one, at, start : start + CHUNK] = product[
                    one * slots : (one + 1) * slots
                ].astype(jnp.bfloat16)

        def forward(expert, _):
            hidden = jnp.dot(xe[expert], hidden_w[expert], preferred_element_type=jnp.float32)
            gate, up = hidden[:, :units], hidden[:, units:]
            sigmoid = jax.nn.sigmoid(gate)
            silu = gate * sigmoid
            scale = weigh[expert, :, 0:1]
            acts[expert] = (silu * up * scale).astype(jnp.bfloat16)
            act_grads = scale * lax.dot_general(
                ce[expert], down_w[expert], TRANSPOSED_RIGHT, preferred_element_type=jnp.float32
            )
            gate_grads = (act_grads * up * (sigmoid * (1.0 + gate * (1.0 - sigmoid)))).astype(
                jnp.bfloat16
            )
            up_grads = (act_grads * silu).astype(jnp.bfloat16)
            dgates[expert] = gate_grads
            dups[expert] = up_grads
            hidden_grads[expert, :, :units] = gate_grads
            hidden_grads[expert, :, units:] = up_grads
            for start in range(0, width, CHUNK):
                keep(
                    expert,
                    jnp.dot(
                        acts[expert],
                        down_w[expert, :, start : start + CHUNK],
                        preferred_element_type=jnp.float32,
                    ),
                    start,
                )
            return 0

        lax.fori_loop(0, 2, forward, 0)
        for copy in saves(group):
            copy.start()
        combine(group, OUTPUT)

        def backward(expert, _):
            for start in range(0, width, CHUNK):
                keep(
                    expert,
                    lax.dot_general(
                        hidden_grads[expert],
                        hidden_w[expert, start : start + CHUNK, :],
                        TRANSPOSED_RIGHT,
                        preferred_element_type=jnp.float32,
                    ),
                    start,
                )
            return 0

        lax.fori_loop(0, 2, backward, 0)
        stages_done(group, OUTPUT)
        combine(group, BACK)

    def inside(group):
        return jnp.logical_and(group >= 0, group < groups)

    def second_send(group, tensor, first):
        unit, slot = group * 2 + tensor, tensor * 2 + first
        return spot.send(
            outbox.at[slot],
            seconds.at[unit, first],
            outbox_sem.at[slot],
            second_receive.at[unit, first],
            SECOND,
        )

    def first_send(group, tensor):
        unit, slot = group * 2 + tensor, 4 + tensor
        return spot.send(
            outbox.at[slot], firsts.at[unit], outbox_sem.at[slot], first_receive.at[unit], FIRST
        )

    def end_send(group, tensor, kind):
        unit, slot = group * 2 + tensor, 6 + tensor * 2 + kind
        return spot.send(
            outbox.at[slot],
            ends.at[unit, kind],
            outbox_sem.at[slot],
            end_receive.at[unit, kind],
            kind,
        )

    def sources(unit, first, second):
        y, x = spot.side(core, first, second)
        return [half_of(part.at[unit, y], x), half_of(cores.at[unit, y], x)]

    def load(source, slot):
        return pltpu.make_async_copy(source, inbox.at[slot], inbox_sem.at[slot])

    def end_roles(step, delay):
        group = step - 3 - delay
        plane = plane_of(jnp.maximum(group, 0))
        valid = inside(group)
        right = jnp.logical_and(valid, jnp.logical_and(z < plane, delay == z))
        left = jnp.logical_and(valid, jnp.logical_and(z > plane, delay == line - 1 - z))
        last = jnp.logical_and(
            valid,
            jnp.logical_and(z == plane, delay == jnp.maximum(plane, line - 1 - plane)),
        )
        return group, right, left, last

    def end_task(step, index):
        delay, tensor = lax.div(index, 2), lax.rem(index, 2)
        group, right, left, last = end_roles(step, delay)
        unit = group * 2 + tensor
        from_left = jnp.logical_and(jnp.logical_or(right, last), z > 0)
        from_right = jnp.logical_and(jnp.logical_or(left, last), z + 1 < line)

        @pl.when(jnp.logical_or(right, jnp.logical_or(left, last)))
        def _():
            seconds_in = spot.send(
                seconds.at[unit, 0],
                seconds.at[unit, 0],
                outbox_sem.at[0],
                second_receive.at[unit, 0],
                SECOND,
            )
            firsts_in = spot.send(
                firsts.at[unit], firsts.at[unit], outbox_sem.at[0], first_receive.at[unit], FIRST
            )
            seconds_in.wait_recv()
            firsts_in.wait_recv()
            loads = [
                load(source, i)
                for i, source in enumerate(
                    sources(unit, 0, 0) + [seconds.at[unit, 0], firsts.at[unit]]
                )
            ]
            for one in loads:
                one.start()
            for kind, present in ((RIGHT, from_left), (LEFT, from_right)):

                def fetch(kind=kind):
                    spot.send(
                        ends.at[unit, kind],
                        ends.at[unit, kind],
                        outbox_sem.at[0],
                        end_receive.at[unit, kind],
                        CORE,
                    ).wait_recv()
                    load(ends.at[unit, kind], 4 + kind).start()

                when(present, fetch)
            for one in loads:
                one.wait()
            base = [inbox.at[i] for i in range(4)]
            for kind, present in ((RIGHT, from_left), (LEFT, from_right)):
                when(present, lambda: load(ends.at[unit, kind], 4 + kind).wait())
            for kind, chosen, behind in ((RIGHT, right, z > 0), (LEFT, left, z + 1 < line)):

                def onward():
                    target = outbox.at[6 + tensor * 2 + kind]
                    when(behind, lambda: add_rows(target, base + [inbox.at[4 + kind]]))
                    when(jnp.logical_not(behind), lambda: add_rows(target, base))
                    end_send(group, tensor, kind).start()

                when(chosen, onward)
            both = jnp.logical_and(from_left, from_right)
            when(
                jnp.logical_and(last, both),
                lambda: add_rows(summed, base + [inbox.at[4], inbox.at[5]]),
            )
            for kind, present in ((RIGHT, from_left), (LEFT, from_right)):
                when(
                    jnp.logical_and(last, jnp.logical_and(present, jnp.logical_not(both))),
                    lambda: add_rows(summed, base + [inbox.at[4 + kind]]),
                )

            @pl.when(last)
            def _():
                copy = pltpu.make_async_copy(
                    summed, total_ref.at[lax.div(group, line), tensor], inbox_sem.at[0]
                )
                copy.start()
                copy.wait()

    def retire(step):
        before = step - 1

        @pl.when(inside(before))
        def _():
            stages_done(before, BACK)

        for tensor in range(2):
            when(
                inside(before - 1),
                lambda: [second_send(before - 1, tensor, first).wait_send() for first in range(2)]
                and None,
            )
            when(inside(before - 2), lambda: first_send(before - 2, tensor).wait_send())

        def ends_done(index, _):
            group, right, left, _ = end_roles(before, lax.div(index, 2))
            tensor = lax.rem(index, 2)
            when(right, lambda: end_send(group, tensor, RIGHT).wait_send())
            when(left, lambda: end_send(group, tensor, LEFT).wait_send())
            return 0

        lax.fori_loop(0, 2 * line, ends_done, 0)

    def serve(step):
        def end_tasks(index, _):
            end_task(step, index)
            return 0

        lax.fori_loop(0, 2 * line, end_tasks, 0)
        tasks = []
        for tensor in range(2):
            unit = (step - 2) * 2 + tensor

            def second_in(unit=unit):
                spot.send(
                    seconds.at[unit, 1],
                    seconds.at[unit, 1],
                    outbox_sem.at[0],
                    second_receive.at[unit, 1],
                    SECOND,
                ).wait_recv()

            tasks.append(
                (
                    inside(step - 2),
                    second_in,
                    lambda unit=unit: sources(unit, 1, 0) + [seconds.at[unit, 1]],
                    4 + tensor,
                    lambda tensor=tensor: first_send(step - 2, tensor),
                )
            )
        for first in (1, 0):
            for tensor in range(2):
                unit = (step - 1) * 2 + tensor

                def cores_in(unit=unit):
                    for y in range(2):
                        spot.send(
                            cores.at[unit, y],
                            cores.at[unit, y],
                            outbox_sem.at[0],
                            core_receive.at[unit, y],
                            CORE,
                        ).wait_recv()

                tasks.append(
                    (
                        inside(step - 1),
                        cores_in if first else lambda: None,
                        lambda unit=unit, first=first: sources(unit, first, 1),
                        tensor * 2 + first,
                        lambda tensor=tensor, first=first: second_send(step - 1, tensor, first),
                    )
                )

        def begin(index):
            valid, ready, inputs, _, _ = tasks[index]

            def action():
                ready()
                for i, source in enumerate(inputs()):
                    load(source, (index % 2) * 3 + i).start()

            when(valid, action)

        begin(0)
        for index, (valid, _, inputs, slot, send) in enumerate(tasks):
            if index + 1 < len(tasks):
                begin(index + 1)

            def action():
                refs = inputs()
                base = (index % 2) * 3
                for i, source in enumerate(refs):
                    load(source, base + i).wait()
                add_rows(outbox.at[slot], [inbox.at[base + i] for i in range(len(refs))])
                send().start()

            when(valid, action)

    def step_body(step, _):
        for i in range(1, batch):
            when(step == i * line, trees[i].finish)

        @pl.when(step < groups)
        def _():
            for copy in load_group(step, 0):
                copy.start()

        for i in range(1, batch):
            turn = step - (i - 1) * line
            when(jnp.logical_and(turn >= 0, turn < line), lambda: trees[i].step(2 * turn + 1))
        retire(step)
        serve(step)
        for i in range(1, batch):
            turn = step - (i - 1) * line
            when(jnp.logical_and(turn >= 0, turn < line), lambda: trees[i].step(2 * turn + 2))
        when(step < groups, lambda: compute(step))
        return 0

    steps = groups + line + 2
    lax.fori_loop(0, steps, step_body, 0)
    retire(jnp.int32(steps))
    for copy in saves(groups - 1):
        copy.wait()


def run_experts(rows, cot_all, info, w_gate, w_up, w_down, capacity, fsdp_count):
    line = fsdp_count // PLANE
    batch, half, width = rows.shape
    length = 2 * half
    units = w_down.shape[1]
    slots = -(-capacity // 16) * 16
    groups = batch * line
    count = groups * PLANE * slots
    taken = PLANE * slots
    sends, receives = spread_count(line, True)
    shape = lambda *dims: jax.ShapeDtypeStruct(dims, jnp.bfloat16)
    block = (half, width)
    anywhere = pl.BlockSpec(memory_space=pl.ANY)
    vmem = lambda *dims: pltpu.VMEM(dims, jnp.bfloat16)
    sem = lambda *dims: pltpu.SemaphoreType.DMA(dims)
    return pl.pallas_call(
        functools.partial(experts_kernel, line, slots),
        out_shape=(
            shape(batch, fsdp_count, length, width),
            jax.ShapeDtypeStruct((batch, 2, *block), jnp.float32),
            shape(2, count, width),
            shape(2, count, width),
            shape(2, count, units),
            shape(2, count, units),
            shape(2, count, units),
            shape(2 * groups, 2, length, width),
            shape(2 * groups, 2, length, width),
            shape(2 * groups, 2, *block),
            shape(2 * groups, *block),
            shape(2 * groups, 2, *block),
        ),
        in_specs=[
            anywhere,
            anywhere,
            pl.BlockSpec(memory_space=pltpu.VMEM),
            anywhere,
            anywhere,
            anywhere,
        ],
        out_specs=(anywhere,) * 12,
        scratch_shapes=[
            vmem(2, width, 2 * units),
            vmem(2, units, width),
            vmem(2, length, width),
            vmem(2, length, width),
            vmem(2, taken, width),
            vmem(2, taken, width),
            vmem(2, taken, units),
            vmem(2, taken, units),
            vmem(2, taken, units),
            vmem(2, taken, 2 * units),
            vmem(PLANE, 2 * LANES, length),
            pltpu.VMEM((2, taken, LANES), jnp.float32),
            vmem(PLANE, 2 * LANES, width),
            vmem(PLANE, length, width),
            vmem(6, *block),
            vmem(10, *block),
            pltpu.VMEM(block, jnp.float32),
            sem(batch, sends),
            sem(batch, receives),
            sem(batch),
            sem(2, 2),
            sem(10),
            sem(PLANE),
            sem(6),
            sem(10),
            sem(5),
            sem(2 * groups, 2),
            sem(2 * groups, 2),
            sem(2 * groups),
            sem(2 * groups, 2),
        ],
        compiler_params=pltpu.CompilerParams(
            collective_id=2, has_side_effects=True, vmem_limit_bytes=60 * MIB
        ),
    )(rows, cot_all, info, w_gate, w_up, w_down)[1:7]


def packed_picks(routes, gates):
    length = routes.shape[2]
    packed = jnp.concatenate([routes[:, 0].astype(jnp.float32), gates[:, 0]], axis=-1)
    packed = jnp.swapaxes(packed, 1, 2).reshape(-1, length)
    return jnp.pad(packed, ((0, 0), (0, -length % LANES)))


def slot_info(packed, batch, top, length, local_experts):
    fsdp_count = packed.shape[0]
    packed = packed[..., :length].reshape(fsdp_count, batch, 1, 2 * top, length)
    packed = jnp.swapaxes(packed, 0, 1)
    experts = lax.axis_index(FSDP) * local_experts + jnp.arange(local_experts, dtype=jnp.int32)
    same = packed[..., :top, :].astype(jnp.int32) == experts[:, None, None]
    hot = jnp.any(same, axis=3)
    shares = jnp.sum(jnp.where(same, packed[..., top:, :], 0.0), axis=3)
    position = jnp.arange(length)
    upper = (position[:, None] < position[None, :]).astype(jnp.bfloat16)
    rank = jnp.dot(
        hot.astype(jnp.bfloat16).reshape(-1, length), upper, preferred_element_type=jnp.float32
    )
    rank = jnp.where(hot, rank.reshape(hot.shape), -1.0)
    return jnp.concatenate([rank, shares], axis=2).reshape(-1, 2 * local_experts, length)


def gathered_layer(
    tokens,
    cotangent,
    norm1_gain,
    w_query,
    key_projection_weight,
    value_projection_weight,
    query_gain,
    key_gain,
    w_out,
    norm2_gain,
    w_gate,
    w_up,
    w_down,
    routes,
    gates,
):
    batch_count = tokens.shape[0]
    model_width = tokens.shape[3]
    sequence_length = routes.shape[2]
    half_length = tokens.shape[2]
    top_count = routes.shape[3]
    head_features = query_gain.shape[0]
    local_experts = w_gate.shape[0]
    fsdp_count = lax.axis_size(FSDP)
    all_experts = local_experts * fsdp_count
    capacity = 7 * top_count * sequence_length // (6 * all_experts)
    query_width = w_query.shape[1]
    kv_width = key_projection_weight.shape[1]
    query_heads = query_width // head_features
    kv_heads = kv_width // head_features
    group_size = query_heads // kv_heads
    score_scale = head_features ** (-0.5)
    cosine_table, sine_values = rotary_tables(sequence_length, head_features)
    block_ids = jnp.arange(sequence_length, dtype=jnp.int32) // BLOCK
    visible = (block_ids[None, :] <= block_ids[:, None])[None, None]
    first_gain = norm1_gain.astype(jnp.float32)
    second_gain = norm2_gain.astype(jnp.float32)
    query_factor_scale = query_gain.astype(jnp.float32)
    key_scale = key_gain.astype(jnp.float32)

    def masked_scores(query_fourfold, key_rows):
        raw_scores = (
            jnp.einsum(
                "qcgd,kcd->cgqk", query_fourfold, key_rows, preferred_element_type=jnp.float32
            )
            * score_scale
        )
        return jnp.where(visible, raw_scores, MASKED)

    def prep_heads(projected, gain_row):
        return prepare_heads(projected, gain_row, cosine_table, sine_values)

    weight_in = jnp.concatenate([w_query, key_projection_weight, value_projection_weight], axis=1)
    half_signs = jnp.where(jnp.arange(head_features) < head_features // 2, -1.0, 1.0)
    tables = (cosine_table[:, 0], sine_values[:, 0] * half_signs)
    gains = [
        gain[None, :] for gain in (first_gain, second_gain, query_factor_scale, key_scale)
    ]
    cot_all, in_full, out_full, picks, normed, projected, contexts, hidden, second = run_forward(
        tokens[:, 0],
        cotangent[:, 0],
        weight_in,
        w_out,
        packed_picks(routes, gates),
        gains,
        tables,
        fsdp_count,
        kv_heads,
    )
    info = slot_info(picks, batch_count, top_count, sequence_length, local_experts)
    totals, expert_rows, cot_rows, act_rows, gate_rows, up_rows = run_experts(
        second,
        cot_all,
        info,
        w_gate,
        w_up,
        w_down,
        capacity,
        fsdp_count,
    )
    expert_grads = (
        jnp.einsum("erd,erf->edf", expert_rows, gate_rows, preferred_element_type=jnp.float32),
        jnp.einsum("erd,erf->edf", expert_rows, up_rows, preferred_element_type=jnp.float32),
        jnp.einsum("erf,erd->efd", act_rows, cot_rows, preferred_element_type=jnp.float32),
    )

    outputs = []
    input_grads = []
    gain_sums = None
    in_grad, out_grad = 0.0, 0.0
    for batch_index in range(batch_count):
        own_rows = tokens[batch_index, 0].astype(jnp.float32)
        normed_all = normed[batch_index]
        context = contexts[batch_index]
        hidden_own = hidden[batch_index]
        query_projected = projected[batch_index, :, :query_width].reshape(
            sequence_length, query_heads, head_features
        )
        key_projected = projected[batch_index, :, query_width : query_width + kv_width].reshape(
            sequence_length, kv_heads, head_features
        )
        value_row_list = (
            projected[batch_index, :, query_width + kv_width :]
            .astype(jnp.bfloat16)
            .reshape(sequence_length, kv_heads, head_features)
        )
        query_rot = prep_heads(query_projected, query_factor_scale).astype(jnp.bfloat16)
        key_rot = prep_heads(key_projected, key_scale).astype(jnp.bfloat16)
        query_fourfold = query_rot.reshape(sequence_length, kv_heads, group_size, head_features)
        own_cot = cotangent[batch_index, 0]
        outputs.append((hidden_own + totals[batch_index, 0]).astype(jnp.bfloat16))
        _, second_back = jax.vjp(rms_scale, hidden_own, second_gain)
        hidden_part, second_gain_grad = second_back(totals[batch_index, 1])
        hidden_grad = own_cot.astype(jnp.float32) + hidden_part
        attn_grad_all = lax.all_gather(hidden_grad.astype(jnp.bfloat16), TP, axis=0, tiled=True)
        out_grad = out_grad + jnp.einsum(
            "th,td->hd", context, attn_grad_all, preferred_element_type=jnp.float32
        )
        context_grad = (
            jnp.einsum("td,hd->th", attn_grad_all, out_full, preferred_element_type=jnp.float32)
            .astype(jnp.bfloat16)
            .reshape(sequence_length, kv_heads, group_size, head_features)
        )
        exp_again = jax.nn.softmax(masked_scores(query_fourfold, key_rot), axis=-1)
        probs_again = exp_again.astype(jnp.bfloat16)
        prob_grads = jnp.einsum(
            "qcgd,kcd->cgqk", context_grad, value_row_list, preferred_element_type=jnp.float32
        )
        value_grads = (
            jnp.einsum(
                "cgqk,qcgd->kcd", probs_again, context_grad, preferred_element_type=jnp.float32
            )
            .astype(jnp.bfloat16)
            .reshape(sequence_length, kv_width)
        )
        score_grads = (
            exp_again * (prob_grads - jnp.sum(exp_again * prob_grads, axis=-1, keepdims=True))
        ).astype(jnp.bfloat16)
        query_rot_grads = (
            jnp.einsum("cgqk,kcd->qcgd", score_grads, key_rot, preferred_element_type=jnp.float32)
            * score_scale
        ).reshape(sequence_length, query_heads, head_features)
        key_rot_grads = (
            jnp.einsum(
                "cgqk,qcgd->kcd", score_grads, query_fourfold, preferred_element_type=jnp.float32
            )
            * score_scale
        )
        _, query_back = jax.vjp(prep_heads, query_projected, query_factor_scale)
        query_proj_grads, query_gain_grad = query_back(query_rot_grads)
        _, key_back = jax.vjp(prep_heads, key_projected, key_scale)
        key_proj_grads, key_gain_grad = key_back(key_rot_grads)
        projected_grads = jnp.concatenate(
            [
                query_proj_grads.astype(jnp.bfloat16).reshape(sequence_length, query_width),
                key_proj_grads.astype(jnp.bfloat16).reshape(sequence_length, kv_width),
                value_grads,
            ],
            axis=1,
        )
        first_normed_grads = jnp.einsum(
            "tq,dq->td", projected_grads, in_full, preferred_element_type=jnp.float32
        )
        in_grad = in_grad + jnp.einsum(
            "td,tq->dq", normed_all, projected_grads, preferred_element_type=jnp.float32
        )
        first_own = lax.psum_scatter(
            first_normed_grads.astype(jnp.bfloat16), TP, scatter_dimension=0, tiled=True
        ).astype(jnp.float32)
        _, first_back = jax.vjp(rms_scale, own_rows, first_gain)
        row_part, first_gain_grad = first_back(first_own)
        input_grads.append((hidden_grad + row_part).astype(jnp.bfloat16))
        new_sums = (first_gain_grad, second_gain_grad, query_gain_grad, key_gain_grad)
        gain_sums = new_sums if gain_sums is None else jax.tree.map(jnp.add, gain_sums, new_sums)
    ends = [0]
    for gains in gain_sums:
        ends.append(ends[-1] + gains.shape[0])
    packed_gains = jnp.concatenate(gain_sums)
    packed_gains = jnp.pad(packed_gains, (0, -ends[-1] % (8 * LANES))).reshape(8, -1)
    in_sum, out_sum, gains_all = collect_weights(
        in_grad.astype(jnp.bfloat16), out_grad.astype(jnp.bfloat16), packed_gains, fsdp_count
    )
    gains_sum = jnp.sum(gains_all, axis=(0, 1)).reshape(-1)
    summed = [gains_sum[ends[i] : ends[i + 1]] for i in range(4)]
    return (
        jnp.stack(outputs)[:, None],
        jnp.stack(input_grads)[:, None],
        summed[0],
        in_sum[:, :query_width],
        in_sum[:, query_width : query_width + kv_width],
        in_sum[:, query_width + kv_width :],
        summed[2],
        summed[3],
        out_sum,
        summed[1],
        expert_grads[0],
        expert_grads[1],
        expert_grads[2],
    )


def shards(*arrays):
    tokens, routes, w_gate = arrays[0], arrays[13], arrays[10]
    fsdp_count = lax.axis_size(FSDP)
    gathered = fsdp_count * routes.shape[2] * tokens.shape[3] * 2
    fits = gathered <= 24 * MIB and fsdp_count % PLANE == 0 and lax.axis_size(TP) == 2
    if fits and w_gate.shape[0] == 2:
        return gathered_layer(*arrays)
    return exchanged_layer(*arrays)


def solution(mesh):
    in_specs = (
        P(None, "fsdp", "tp", None),
        P(None, "fsdp", "tp", None),
        P(),
        P("fsdp", "tp"),
        P("fsdp", "tp"),
        P("fsdp", "tp"),
        P(),
        P(),
        P("tp", "fsdp"),
        P(),
        P("fsdp", None, "tp"),
        P("fsdp", None, "tp"),
        P("fsdp", "tp", None),
        P(None, "fsdp", None, None),
        P(None, "fsdp", None, None),
    )
    out_specs = (
        P(None, "fsdp", "tp", None),
        P(None, "fsdp", "tp", None),
        P(),
        P("fsdp", "tp"),
        P("fsdp", "tp"),
        P("fsdp", "tp"),
        P(),
        P(),
        P("tp", "fsdp"),
        P(),
        P("fsdp", None, "tp"),
        P("fsdp", None, "tp"),
        P("fsdp", "tp", None),
    )
    return jax.shard_map(shards, mesh=mesh, in_specs=in_specs, out_specs=out_specs, check_vma=False)
```

```python
import functools

import jax
import jax.numpy as jnp
from jax import lax
from jax.experimental import pallas as pl
from jax.experimental.pallas import tpu as pltpu
from jax.sharding import PartitionSpec as P

BLOCK = 256


EPSILON = 1e-06
ROPE_BASE = 1000000.0
MASKED = -1e30
TILE_PICKS = 128


def rms_scale(row_block, gain_row):
    return (
        row_block
        * lax.rsqrt(jnp.mean(row_block * row_block, axis=-1, keepdims=True) + EPSILON)
        * gain_row
    )


def rotary_tables(sequence_length, head_width):
    half_width = head_width // 2
    inverse = ROPE_BASE ** (-2.0 * jnp.arange(half_width, dtype=jnp.float32) / head_width)
    angles = jnp.arange(sequence_length, dtype=jnp.float32)[:, None] * inverse[None, :]
    cosine_table = jnp.concatenate([jnp.cos(angles), jnp.cos(angles)], axis=-1)[:, None, :]
    sine_values = jnp.concatenate([jnp.sin(angles), jnp.sin(angles)], axis=-1)[:, None, :]
    return (cosine_table, sine_values)


def rotate(head_rows, cosine_table, sine_values):
    half_width = head_rows.shape[-1] // 2
    turned = jnp.concatenate([-head_rows[..., half_width:], head_rows[..., :half_width]], axis=-1)
    return head_rows * cosine_table + turned * sine_values


def prepare_heads(projected, gain_row, cosine_table, sine_values):
    return rotate(rms_scale(projected, gain_row), cosine_table, sine_values)


def swiglu(gate_act, up_act):
    return jax.nn.silu(gate_act) * up_act


def slot_tables(route_rows, gate_rows, expert_count, capacity):
    sequence_length = route_rows.shape[0]
    top_count = route_rows.shape[1]
    pick_count = sequence_length * top_count
    tile_count = pick_count // TILE_PICKS
    flat_routes = route_rows.reshape(-1)
    onehot = (flat_routes[:, None] == jnp.arange(expert_count, dtype=jnp.int32)[None, :]).astype(
        jnp.bfloat16
    )
    tiles = onehot.reshape(tile_count, TILE_PICKS, expert_count)
    positions = jnp.arange(TILE_PICKS, dtype=jnp.int32)
    lower = (positions[None, :] < positions[:, None]).astype(jnp.bfloat16)
    within = jnp.einsum("ij,bje->bie", lower, tiles, preferred_element_type=jnp.float32)
    tile_totals = jnp.sum(tiles.astype(jnp.float32), axis=1)
    offsets = jnp.cumsum(tile_totals, axis=0) - tile_totals
    before = within + offsets[:, None, :]
    slot_rank = jnp.sum(before * tiles.astype(jnp.float32), axis=-1).reshape(-1).astype(jnp.int32)
    slot_index = flat_routes * capacity + slot_rank
    pick_ids = jnp.arange(pick_count, dtype=jnp.int32) // top_count
    slot_owner = (
        jnp.full((expert_count * capacity,), sequence_length, jnp.int32)
        .at[slot_index]
        .set(pick_ids)
    )
    slot_weight = (
        jnp.zeros((expert_count * capacity,), jnp.float32).at[slot_index].set(gate_rows.reshape(-1))
    )
    return (slot_index, slot_owner, slot_weight)


def exchanged_layer(
    tokens,
    cotangent,
    norm1_gain,
    w_query,
    key_projection_weight,
    value_projection_weight,
    query_gain,
    key_gain,
    w_out,
    norm2_gain,
    w_gate,
    w_up,
    w_down,
    routes,
    gates,
):
    batch_count = tokens.shape[0]
    model_width = tokens.shape[3]
    sequence_length = routes.shape[2]
    top_count = routes.shape[3]
    head_features = query_gain.shape[0]
    local_experts = w_gate.shape[0]
    fsdp_count = lax.axis_size("fsdp")
    all_experts = local_experts * fsdp_count
    capacity = 7 * top_count * sequence_length // (6 * all_experts)
    query_heads = w_query.shape[1] // head_features
    kv_heads = key_projection_weight.shape[1] // head_features
    group_size = query_heads // kv_heads
    score_scale = head_features ** (-0.5)
    cosine_table, sine_values = rotary_tables(sequence_length, head_features)
    block_ids = jnp.arange(sequence_length, dtype=jnp.int32) // BLOCK
    visible = (block_ids[None, :] <= block_ids[:, None])[None, None]
    first_gain = norm1_gain.astype(jnp.float32)
    second_gain = norm2_gain.astype(jnp.float32)
    query_factor_scale = query_gain.astype(jnp.float32)
    key_scale = key_gain.astype(jnp.float32)
    zero_row = jnp.zeros((1, model_width), jnp.bfloat16)
    buffer_shape = (fsdp_count, local_experts, capacity, model_width)

    def masked_scores(query_fourfold, key_rows):
        raw_scores = (
            jnp.einsum(
                "qcgd,kcd->cgqk", query_fourfold, key_rows, preferred_element_type=jnp.float32
            )
            * score_scale
        )
        return jnp.where(visible, raw_scores, MASKED)

    def prep_heads(projected, gain_row):
        return prepare_heads(projected, gain_row, cosine_table, sine_values)

    gain_sums = (
        jnp.zeros((model_width,), jnp.float32),
        jnp.zeros((model_width,), jnp.float32),
        jnp.zeros((head_features,), jnp.float32),
        jnp.zeros((head_features,), jnp.float32),
    )
    expert_grads = (
        jnp.zeros(w_gate.shape, jnp.float32),
        jnp.zeros(w_up.shape, jnp.float32),
        jnp.zeros(w_down.shape, jnp.float32),
    )
    attn_grads = tuple(
        (
            jnp.zeros(weight_part.shape, jnp.float32)
            for weight_part in (w_query, key_projection_weight, value_projection_weight, w_out)
        )
    )
    outputs = []
    input_grads = []
    for batch_index in range(batch_count):
        query_full, key_full, value_full, out_full = (
            lax.all_gather(w_query, "fsdp", axis=0, tiled=True),
            lax.all_gather(key_projection_weight, "fsdp", axis=0, tiled=True),
            lax.all_gather(value_projection_weight, "fsdp", axis=0, tiled=True),
            lax.all_gather(w_out, "fsdp", axis=1, tiled=True),
        )
        own_rows = tokens[batch_index, 0].astype(jnp.float32)
        own_cot = cotangent[batch_index, 0]
        route_rows = routes[batch_index, 0]
        gate_rows = gates[batch_index, 0]
        first_normed = rms_scale(own_rows, first_gain).astype(jnp.bfloat16)
        normed_all = lax.all_gather(first_normed, "tp", axis=0, tiled=True)
        query_projected = jnp.dot(
            normed_all, query_full, preferred_element_type=jnp.float32
        ).reshape(sequence_length, query_heads, head_features)
        key_projected = jnp.dot(normed_all, key_full, preferred_element_type=jnp.float32).reshape(
            sequence_length, kv_heads, head_features
        )
        value_row_list = (
            jnp.dot(normed_all, value_full, preferred_element_type=jnp.float32)
            .astype(jnp.bfloat16)
            .reshape(sequence_length, kv_heads, head_features)
        )
        query_rot = prep_heads(query_projected, query_factor_scale).astype(jnp.bfloat16)
        key_rot = prep_heads(key_projected, key_scale).astype(jnp.bfloat16)
        query_fourfold = query_rot.reshape(sequence_length, kv_heads, group_size, head_features)
        scores = masked_scores(query_fourfold, key_rot)
        row_max = jnp.max(scores, axis=-1, keepdims=True)
        exp_scores = jnp.exp(scores - row_max)
        totals = jnp.sum(exp_scores, axis=-1, keepdims=True)
        log_total = row_max + jnp.log(totals)
        prob_rows = (exp_scores / totals).astype(jnp.bfloat16)
        context = (
            jnp.einsum(
                "cgqk,kcd->qcgd", prob_rows, value_row_list, preferred_element_type=jnp.float32
            )
            .astype(jnp.bfloat16)
            .reshape(sequence_length, query_heads * head_features)
        )
        attn_own = lax.psum_scatter(
            jnp.dot(context, out_full, preferred_element_type=jnp.float32).astype(jnp.bfloat16),
            "tp",
            scatter_dimension=0,
            tiled=True,
        ).astype(jnp.float32)
        hidden_own = own_rows + attn_own
        second_normed = rms_scale(hidden_own, second_gain).astype(jnp.bfloat16)
        normed_two, cot_all = (
            lax.all_gather(second_normed, "tp", axis=0, tiled=True),
            lax.all_gather(own_cot, "tp", axis=0, tiled=True),
        )
        slot_index, slot_owner, slot_weight = slot_tables(
            route_rows, gate_rows, all_experts, capacity
        )
        padded_rows = jnp.concatenate([normed_two, zero_row], axis=0)
        send_rows = padded_rows[slot_owner].reshape(buffer_shape)
        expert_in = lax.all_to_all(send_rows, "fsdp", split_axis=0, concat_axis=0, tiled=True)
        gate_act = jnp.einsum(
            "sekd,edf->sekf", expert_in, w_gate, preferred_element_type=jnp.float32
        )
        up_act = jnp.einsum("sekd,edf->sekf", expert_in, w_up, preferred_element_type=jnp.float32)
        act_rows = swiglu(gate_act, up_act).astype(jnp.bfloat16)
        expert_out = jnp.einsum(
            "sekf,efd->sekd", act_rows, w_down, preferred_element_type=jnp.float32
        )
        returned = lax.all_to_all(
            expert_out.astype(jnp.bfloat16), "fsdp", split_axis=0, concat_axis=0, tiled=True
        ).astype(expert_out.dtype)
        picked = returned.reshape(all_experts * capacity, model_width)[slot_index].reshape(
            sequence_length, top_count, model_width
        )
        moe_part = jnp.sum(picked * gate_rows[:, :, None], axis=1)
        moe_own = lax.psum_scatter(
            moe_part.astype(jnp.bfloat16), "tp", scatter_dimension=0, tiled=True
        ).astype(jnp.float32)
        outputs.append((hidden_own + moe_own).astype(jnp.bfloat16))
        cot_padded = jnp.concatenate([cot_all, zero_row], axis=0)
        send_grads = (
            (slot_weight[:, None] * cot_padded[slot_owner])
            .astype(jnp.bfloat16)
            .reshape(buffer_shape)
        )
        out_grads = lax.all_to_all(send_grads, "fsdp", split_axis=0, concat_axis=0, tiled=True)
        act_grads = jnp.einsum(
            "sekd,efd->sekf", out_grads, w_down, preferred_element_type=jnp.float32
        )
        _, swiglu_back = jax.vjp(swiglu, gate_act, up_act)
        gate_grads, up_grads = swiglu_back(act_grads)
        gate_grads = gate_grads.astype(jnp.bfloat16)
        up_grads = up_grads.astype(jnp.bfloat16)
        expert_grads = (
            expert_grads[0]
            + jnp.einsum(
                "sekd,sekf->edf", expert_in, gate_grads, preferred_element_type=jnp.float32
            ),
            expert_grads[1]
            + jnp.einsum("sekd,sekf->edf", expert_in, up_grads, preferred_element_type=jnp.float32),
            expert_grads[2]
            + jnp.einsum("sekf,sekd->efd", act_rows, out_grads, preferred_element_type=jnp.float32),
        )
        input_part = jnp.einsum(
            "sekf,edf->sekd", gate_grads, w_gate, preferred_element_type=jnp.float32
        ) + jnp.einsum("sekf,edf->sekd", up_grads, w_up, preferred_element_type=jnp.float32)
        input_back = lax.all_to_all(
            input_part.astype(jnp.bfloat16), "fsdp", split_axis=0, concat_axis=0, tiled=True
        ).astype(input_part.dtype)
        normed_grads = jnp.sum(
            input_back.reshape(all_experts * capacity, model_width)[slot_index].reshape(
                sequence_length, top_count, model_width
            ),
            axis=1,
        )
        normed_own = lax.psum_scatter(
            normed_grads.astype(jnp.bfloat16), "tp", scatter_dimension=0, tiled=True
        ).astype(jnp.float32)
        _, second_back = jax.vjp(rms_scale, hidden_own, second_gain)
        hidden_part, second_gain_grad = second_back(normed_own)
        hidden_grad = own_cot.astype(jnp.float32) + hidden_part
        attn_grad_all = lax.all_gather(hidden_grad.astype(jnp.bfloat16), "tp", axis=0, tiled=True)
        out_weight_grad = jnp.einsum(
            "th,td->hd", context, attn_grad_all, preferred_element_type=jnp.float32
        )
        context_grad = (
            jnp.einsum("td,hd->th", attn_grad_all, out_full, preferred_element_type=jnp.float32)
            .astype(jnp.bfloat16)
            .reshape(sequence_length, kv_heads, group_size, head_features)
        )
        exp_again = jnp.exp(masked_scores(query_fourfold, key_rot) - log_total)
        probs_again = exp_again.astype(jnp.bfloat16)
        prob_grads = jnp.einsum(
            "qcgd,kcd->cgqk", context_grad, value_row_list, preferred_element_type=jnp.float32
        )
        value_grads = (
            jnp.einsum(
                "cgqk,qcgd->kcd", probs_again, context_grad, preferred_element_type=jnp.float32
            )
            .astype(jnp.bfloat16)
            .reshape(sequence_length, kv_heads * head_features)
        )
        score_grads = (
            exp_again * (prob_grads - jnp.sum(exp_again * prob_grads, axis=-1, keepdims=True))
        ).astype(jnp.bfloat16)
        query_rot_grads = (
            jnp.einsum("cgqk,kcd->qcgd", score_grads, key_rot, preferred_element_type=jnp.float32)
            * score_scale
        ).reshape(sequence_length, query_heads, head_features)
        key_rot_grads = (
            jnp.einsum(
                "cgqk,qcgd->kcd", score_grads, query_fourfold, preferred_element_type=jnp.float32
            )
            * score_scale
        )
        _, query_back = jax.vjp(prep_heads, query_projected, query_factor_scale)
        query_proj_grads, query_gain_grad = query_back(query_rot_grads)
        _, key_back = jax.vjp(prep_heads, key_projected, key_scale)
        key_proj_grads, key_gain_grad = key_back(key_rot_grads)
        query_proj_grads = query_proj_grads.astype(jnp.bfloat16).reshape(
            sequence_length, query_heads * head_features
        )
        key_proj_grads = key_proj_grads.astype(jnp.bfloat16).reshape(
            sequence_length, kv_heads * head_features
        )
        first_normed_grads = (
            jnp.einsum(
                "tq,dq->td", query_proj_grads, query_full, preferred_element_type=jnp.float32
            )
            + jnp.einsum("tq,dq->td", key_proj_grads, key_full, preferred_element_type=jnp.float32)
            + jnp.einsum("tq,dq->td", value_grads, value_full, preferred_element_type=jnp.float32)
        )
        weight_parts = (
            jnp.einsum(
                "td,tq->dq", normed_all, query_proj_grads, preferred_element_type=jnp.float32
            ),
            jnp.einsum("td,tq->dq", normed_all, key_proj_grads, preferred_element_type=jnp.float32),
            jnp.einsum("td,tq->dq", normed_all, value_grads, preferred_element_type=jnp.float32),
            out_weight_grad,
        )
        first_own = lax.psum_scatter(
            first_normed_grads.astype(jnp.bfloat16), "tp", scatter_dimension=0, tiled=True
        ).astype(jnp.float32)
        _, first_back = jax.vjp(rms_scale, own_rows, first_gain)
        row_part, first_gain_grad = first_back(first_own)
        input_grads.append((hidden_grad + row_part).astype(jnp.bfloat16))
        gain_sums = (
            gain_sums[0] + first_gain_grad,
            gain_sums[1] + second_gain_grad,
            gain_sums[2] + query_gain_grad,
            gain_sums[3] + key_gain_grad,
        )
        attn_grads = jax.tree.map(
            jnp.add,
            attn_grads,
            (
                lax.psum_scatter(weight_parts[0], "fsdp", scatter_dimension=0, tiled=True),
                lax.psum_scatter(weight_parts[1], "fsdp", scatter_dimension=0, tiled=True),
                lax.psum_scatter(weight_parts[2], "fsdp", scatter_dimension=0, tiled=True),
                lax.psum_scatter(weight_parts[3], "fsdp", scatter_dimension=1, tiled=True),
            ),
        )
    summed = lax.psum((gain_sums[0], gain_sums[1], gain_sums[2], gain_sums[3]), ("fsdp", "tp"))
    block_out = jnp.stack(outputs)[:, None]
    input_grad = jnp.stack(input_grads)[:, None]
    return (
        block_out,
        input_grad,
        summed[0],
        attn_grads[0],
        attn_grads[1],
        attn_grads[2],
        summed[2],
        summed[3],
        attn_grads[3],
        summed[1],
        expert_grads[0],
        expert_grads[1],
        expert_grads[2],
    )


MESH = pl.DeviceIdType.MESH
FSDP, TP = "fsdp", "tp"
PLANE = 4
LANES = 128
MIB = 1 << 20
FIRST, SECOND, CORE, CROSS, LINE = range(5)
TRANSPOSED_LEFT = (((0,), (0,)), ((), ()))
TRANSPOSED_RIGHT = (((1,), (1,)), ((), ()))
OUTPUT, BACK = range(2)
CHUNK = 512


class Spot:
    def __init__(self, line, wide, turned=True):
        self.line = line
        self.wide = wide
        self.turned = turned
        self.planes = 4 if wide else 2
        index = lax.axis_index(FSDP)
        self.x = lax.axis_index(TP)
        self.z = lax.div(index, PLANE)
        self.y = lax.rem(lax.div(index, 2), 2)
        self.core = lax.rem(index, 2)

    def side(self, core, first, second):
        flip_y, flip_x = first, second
        if self.wide and self.turned:
            flip_y = (1 - core) * first + core * second
            flip_x = core * first + (1 - core) * second
        return self.y + flip_y * (1 - 2 * self.y), self.x + flip_x * (1 - 2 * self.x)

    def block(self, core, first, second, z):
        y, x = self.side(core, first, second)
        return z * PLANE + y * 2 + core, x

    def device(self, kind, z=None):
        if kind == LINE:
            return self.block(self.core, 0, 0, z)
        if kind == CORE:
            return self.block(1 - self.core, 0, 0, self.z)
        if kind == CROSS:
            return self.block(self.core, 0, 0, self.z)[0], 1 - self.x
        return self.block(self.core, int(kind == FIRST), int(kind == SECOND), self.z)

    def kinds(self):
        return (FIRST, SECOND, CORE) if self.wide else (FIRST, CORE)

    def number(self, first, second, z):
        return (second * 2 + first) * self.line + z

    def places(self, action):
        for z in range(self.line):
            when(z != self.z, functools.partial(action, z))

    def greet(self):
        barrier = pltpu.get_barrier_semaphore()

        def signal(kind, z=None):
            pl.semaphore_signal(
                barrier, inc=1, device_id=self.device(kind, z), device_id_type=MESH
            )

        for kind in self.kinds():
            signal(kind)
        self.places(lambda z: signal(LINE, z))
        pl.semaphore_wait(barrier, len(self.kinds()) + self.line - 1)

    def send(self, source, target, send_sem, receive_sem, kind, z=None):
        return pltpu.make_async_remote_copy(
            src_ref=source,
            dst_ref=target,
            send_sem=send_sem,
            recv_sem=receive_sem,
            device_id=self.device(kind, z),
            device_id_type=MESH,
        )


def when(condition, action):
    def run():
        action()

    if condition is None:
        run()
    else:
        pl.when(condition)(run)


class Spread:
    def __init__(self, spot, source, slot, send, receive, local):
        self.spot = spot
        self.slot = slot
        self.source = source
        self.sends = send
        self.receives = receive
        self.mine = pltpu.make_async_copy(source, slot(*spot.block(spot.core, 0, 0, spot.z)), local)

    def copy(self, first, second, z, kind, own=False, to=None):
        spot = self.spot
        place = self.slot(*spot.block(spot.core, first, second, z))
        number = spot.number(first, second, z)
        arrival = {
            LINE: number,
            FIRST: spot.number(1, 0, z),
            SECOND: spot.number(first, 1, z),
            CORE: spot.planes * spot.line + number,
        }[kind]
        if kind == LINE:
            number = to
        departure = {LINE: 0, FIRST: 1, SECOND: 2, CORE: 4}[kind] * spot.line + number
        source = self.source if own else place
        return spot.send(source, place, self.sends.at[departure], self.receives.at[arrival], kind, to)

    def arrived(self, first, second, z, other=False):
        spot = self.spot
        core = 1 - spot.core if other else spot.core
        place = self.slot(*spot.block(core, first, second, z))
        number = spot.number(first, second, z) + (spot.planes * spot.line if other else 0)
        spot.send(place, place, self.sends.at[0], self.receives.at[number], CORE).wait_recv()

    def steps(self):
        return self.spot.line + (3 if self.spot.wide else 1)

    def begin(self):
        spot = self.spot
        for kind in spot.kinds():
            if kind != CORE:
                self.copy(0, 0, spot.z, kind, True).start()
        spot.places(lambda z: self.copy(0, 0, spot.z, LINE, True, z).start())
        self.copy(0, 0, spot.z, CORE, True).start()
        self.mine.start()

    def step(self, step):
        spot = self.spot
        line, z = spot.line, spot.z

        def reached(away, action):
            inside = jnp.logical_and(away >= 0, away < line)
            when(jnp.logical_and(inside, z - away >= 0), lambda: action(z - away))
            when(
                jnp.logical_and(inside, jnp.logical_and(away > 0, z + away < line)),
                lambda: action(z + away),
            )

        def along(zz):
            self.arrived(0, 0, zz)
            for kind in spot.kinds():
                self.copy(0, 0, zz, kind).start()

        def firsts(zz):
            self.arrived(1, 0, zz)
            if spot.wide:
                self.copy(1, 0, zz, SECOND).start()
            self.copy(1, 0, zz, CORE).start()

        def lasts(first):
            def action(zz):
                self.arrived(first, 1, zz)
                self.copy(first, 1, zz, CORE).start()

            return action

        step = jnp.asarray(step, jnp.int32)
        reached(step, along)
        reached(step - 1, firsts)
        if spot.wide:
            reached(step - 2, lasts(0))
            reached(step - 3, lasts(1))

    def finish(self):
        spot = self.spot
        spot.places(lambda z: self.copy(0, 0, spot.z, LINE, True, z).wait_send())

        def body(zz, _):
            self.copy(0, 0, zz, FIRST).wait_send()
            for second in range(2 if spot.wide else 1):
                for first in (0, 1):
                    if spot.wide and not second:
                        self.copy(first, 0, zz, SECOND).wait_send()
                    self.copy(first, second, zz, CORE).wait_send()
                    self.arrived(first, second, zz, other=True)
            return 0

        lax.fori_loop(0, spot.line, body, 0)
        self.mine.wait()


def run_trees(trees):
    for tree in trees:
        tree.begin()

    def body(step, _):
        for tree in trees:
            tree.step(step)
        return 0

    lax.fori_loop(1, max(tree.steps() for tree in trees), body, 0)
    for tree in trees:
        tree.finish()


def spread_count(line, wide):
    return (8 if wide else 6) * line, (8 if wide else 4) * line


def rows_at(ref, index, size):
    return ref.at[pl.ds(pl.multiple_of(index * size, 16), size)]


def columns_at(ref, index, size):
    return ref.at[:, pl.ds(pl.multiple_of(index * size, LANES), size)]


def norm_rows(target, source, gain):
    def body(step, _):
        rows = pl.ds(pl.multiple_of(step * 16, 16), 16)
        value = source[rows, :].astype(jnp.float32)
        target[rows, :] = rms_scale(value, gain[...]).astype(target.dtype)
        return 0

    lax.fori_loop(0, target.shape[0] // 16, body, 0)


def turned_heads(value, gain, cosine, sine):
    normed = rms_scale(value, gain)
    return normed * cosine + pltpu.roll(normed, normed.shape[-1] // 2, 1) * sine


def visible_blocks(length, group):
    blocks = []
    for start in range(0, length, BLOCK):
        stop = min(start + BLOCK, length)
        heads = max(1, BLOCK // (stop - start))
        while group % heads:
            heads -= 1
        blocks.append((start, stop, stop, heads))
    return blocks


def softmax(scores):
    raised = jnp.exp(scores - jnp.max(scores, axis=-1, keepdims=True))
    return raised * (1.0 / jnp.sum(raised, axis=-1, keepdims=True))


def for_heads(group, heads, body):
    turns = 2 if heads == 1 and group % 2 == 0 else 1

    def turn(step, _):
        for i in range(turns):
            body((step * turns + i) * heads)
        return 0

    count = group // (heads * turns)
    if count == 1:
        turn(0, 0)
    else:
        lax.fori_loop(0, count, turn, 0)


def head_columns(head, features):
    return pl.ds(pl.multiple_of(head * features, LANES), features)


def forward_kernel(
    line,
    heads,
    kv_heads,
    tokens_ref,
    cot_ref,
    in_ref,
    out_ref,
    picks_ref,
    gain1_ref,
    gain2_ref,
    query_gain_ref,
    key_gain_ref,
    cosine_ref,
    sine_ref,
    cot_all,
    in_all,
    out_all,
    picks_all,
    normed_all,
    projected_all,
    context_all,
    hidden_all,
    second_all,
    in_w,
    out_w,
    tokens,
    normed,
    projected,
    context,
    queries,
    keys,
    values,
    mixed,
    mixed_other,
    hidden,
    second,
    narrow_send,
    narrow_receive,
    wide_send,
    wide_receive,
    local,
    token_send,
    token_receive,
    mixed_send,
    mixed_receive,
    save_sem,
):
    batch, half, width = tokens_ref.shape
    length = 2 * half
    depth, out_width = in_ref.shape[0], out_ref.shape[1]
    features = query_gain_ref.shape[1]
    narrow = Spot(line, False)
    spots = [Spot(line, True, turned=i > 0) for i in range(batch)]
    spot = spots[0]
    x = spot.x
    spot.greet()
    slots = [
        (picks_ref, lambda block, side: picks_all.at[block]),
        (in_ref, lambda block, side: rows_at(in_w, block, depth)),
        (out_ref, lambda block, side: columns_at(out_w, block, out_width)),
    ]
    weights = [
        Spread(narrow, source, slot, narrow_send.at[i], narrow_receive.at[i], local.at[i])
        for i, (source, slot) in enumerate(slots)
    ]
    cots = [
        Spread(
            spots[i],
            cot_ref.at[i],
            lambda block, side, i=i: rows_at(cot_all.at[i, block], side, half),
            wide_send.at[i],
            wide_receive.at[i],
            local.at[3 + i],
        )
        for i in range(batch)
    ]
    for tree in weights:
        tree.begin()

    def token_copies(i):
        place = rows_at(tokens.at[i], x, half)
        return (
            pltpu.make_async_copy(tokens_ref.at[i], place, local.at[3 + batch + i]),
            spot.send(tokens_ref.at[i], place, token_send.at[i], token_receive.at[i], CROSS),
        )

    for i in range(batch):
        for copy in token_copies(i):
            copy.start()
    cots[0].begin()

    def steps(step, _):
        for tree in weights + cots[:1]:
            tree.step(step)
        return 0

    lax.fori_loop(1, weights[0].steps(), steps, 0)
    for i in range(batch):
        mine, other = token_copies(i)
        mine.wait()
        other.wait_send()
        place = rows_at(tokens.at[i], 1 - x, half)
        spot.send(place, place, token_send.at[i], token_receive.at[i], CROSS).wait_recv()
    for i in range(batch):
        norm_rows(normed.at[i], tokens.at[i], gain1_ref)
    for tree in weights:
        tree.finish()
    for tree in cots[1:]:
        tree.begin()

    def save(source, target, index):
        return pltpu.make_async_copy(source, target, save_sem.at[index])

    saves = [save(in_w, in_all, 0), save(out_w, out_all, 1)]
    for copy in saves:
        copy.start()

    def project(i):
        for start in range(0, in_w.shape[1], CHUNK):
            projected[i, :, start : start + CHUNK] = jnp.dot(
                normed[i], in_w[:, start : start + CHUNK], preferred_element_type=jnp.float32
            )

    scale = features ** (-0.5)

    def attend(i):
        base = heads * features
        for head in range(kv_heads):
            at = base + head * features
            keys[head] = turned_heads(
                projected[i, :, at : at + features],
                key_gain_ref[...],
                cosine_ref[...],
                sine_ref[...],
            ).astype(jnp.bfloat16)
            at = base + (kv_heads + head) * features
            values[head] = projected[i, :, at : at + features].astype(jnp.bfloat16)

        group = heads // kv_heads

        def one(shared, _):
            def prepare(member):
                columns = head_columns(shared * group + member, features)
                queries[member] = turned_heads(
                    projected[i, :, columns], query_gain_ref[...], cosine_ref[...], sine_ref[...]
                ).astype(jnp.bfloat16)

            for_heads(group, 1, prepare)
            for start, stop, seen, at_once in visible_blocks(length, group):
                count = stop - start

                def block(member):
                    query = queries[pl.ds(member, at_once), start:stop, :].reshape(-1, features)
                    scores = lax.dot_general(
                        query,
                        keys[shared, :seen, :],
                        TRANSPOSED_RIGHT,
                        preferred_element_type=jnp.float32,
                    )
                    rows = jnp.dot(
                        softmax(scores * scale).astype(jnp.bfloat16),
                        values[shared, :seen, :],
                        preferred_element_type=jnp.float32,
                    ).astype(jnp.bfloat16)
                    for j in range(at_once):
                        columns = head_columns(shared * group + member + j, features)
                        context[i, start:stop, columns] = rows[j * count : (j + 1) * count]

                for_heads(group, at_once, block)
            return 0

        lax.fori_loop(0, kv_heads, one, 0)

    def mixed_copy(i):
        return spot.send(
            rows_at(mixed.at[i], 1 - x, half),
            mixed_other.at[i],
            mixed_send.at[i],
            mixed_receive.at[i],
            CROSS,
        )

    def mix(i):
        for start in range(0, width, CHUNK):
            mixed[i, :, start : start + CHUNK] = jnp.dot(
                context[i], out_w[:, start : start + CHUNK], preferred_element_type=jnp.float32
            ).astype(jnp.bfloat16)
        mixed_copy(i).start()

    def close(i):
        mixed_copy(i).wait()
        add_rows(
            hidden.at[i],
            [rows_at(tokens.at[i], x, half), rows_at(mixed.at[i], x, half), mixed_other.at[i]],
        )
        norm_rows(second.at[i], hidden.at[i], gain2_ref)

    pending = []
    for i in range(batch):
        pending += [functools.partial(work, i) for work in (project, attend, mix)]
    pending += [functools.partial(close, i) for i in range(batch)]
    later = [(cots[0], step) for step in range(weights[0].steps(), cots[0].steps())]
    for tree in cots[1:]:
        later += [(tree, step) for step in range(1, tree.steps())]
    while pending or later:
        if pending:
            pending.pop(0)()
        for _ in range(2):
            if later:
                tree, step = later.pop(0)
                tree.step(step)

    saves += [
        save(source, target, 2 + i)
        for i, (source, target) in enumerate(
            [
                (normed, normed_all),
                (projected, projected_all),
                (context, context_all),
                (hidden, hidden_all),
                (second, second_all),
            ]
        )
    ]
    for copy in saves[2:]:
        copy.start()
    for tree in cots:
        tree.finish()
    for copy in saves:
        copy.wait()


def run_forward(tokens, cot, weight_in, weight_out, picks, gains, tables, fsdp_count, kv_heads):
    line = fsdp_count // PLANE
    batch, half, width = tokens.shape
    length = 2 * half
    features = gains[2].shape[1]
    heads = weight_out.shape[0] // features
    in_shape = (weight_in.shape[0] * fsdp_count, weight_in.shape[1])
    out_shape = (weight_out.shape[0], weight_out.shape[1] * fsdp_count)
    wide, narrow = spread_count(line, True), spread_count(line, False)
    anywhere = pl.BlockSpec(memory_space=pl.ANY)
    inside = pl.BlockSpec(memory_space=pltpu.VMEM)
    shape = lambda dims, kind=jnp.bfloat16: jax.ShapeDtypeStruct(dims, kind)
    vmem = lambda *dims: pltpu.VMEM(dims, jnp.bfloat16)
    sem = lambda *dims: pltpu.SemaphoreType.DMA(dims)
    kept = (
        ((batch, length, width), jnp.bfloat16),
        ((batch, length, weight_in.shape[1]), jnp.float32),
        ((batch, length, heads * features), jnp.bfloat16),
        ((batch, half, width), jnp.float32),
        ((batch, half, width), jnp.bfloat16),
    )
    return pl.pallas_call(
        functools.partial(forward_kernel, line, heads, kv_heads),
        out_shape=(
            shape((batch, fsdp_count, length, width)),
            shape(in_shape),
            shape(out_shape),
            shape((fsdp_count, *picks.shape), picks.dtype),
            *(shape(*one) for one in kept),
        ),
        in_specs=[anywhere] * 5 + [inside] * 6,
        out_specs=(anywhere,) * 9,
        scratch_shapes=[
            vmem(*in_shape),
            vmem(*out_shape),
            vmem(batch, length, width),
            *(pltpu.VMEM(*one) for one in kept[:3]),
            vmem(heads // kv_heads, length, features),
            vmem(kv_heads, length, features),
            vmem(kv_heads, length, features),
            vmem(batch, length, width),
            vmem(batch, half, width),
            *(pltpu.VMEM(*one) for one in kept[3:]),
            sem(3, narrow[0]),
            sem(3, narrow[1]),
            sem(batch, wide[0]),
            sem(batch, wide[1]),
            sem(3 + 2 * batch),
            sem(batch),
            sem(batch),
            sem(batch),
            sem(batch),
            sem(7),
        ],
        compiler_params=pltpu.CompilerParams(
            collective_id=1, has_side_effects=True, vmem_limit_bytes=60 * MIB
        ),
    )(tokens, cot, weight_in, weight_out, picks, *gains, *tables)


def add_rows(target, sources):
    def body(step, _):
        rows = pl.ds(pl.multiple_of(step * 16, 16), 16)
        total = sources[0][rows, :].astype(jnp.float32)
        for source in sources[1:]:
            total = total + source[rows, :].astype(jnp.float32)
        target[rows, :] = total.astype(target.dtype)
        return 0

    lax.fori_loop(0, target.shape[0] // 16, body, 0)


class Collect:
    def __init__(self, spot, part, total, cores, firsts, ends, send, receive):
        self.spot = spot
        self.part = part
        self.total = total
        self.places = {CORE: cores, FIRST: firsts, LINE: ends}
        self.sends = send
        self.receives = receive

    def copy(self, kind, first, z):
        spot = self.spot
        line = spot.line
        base = {CORE: 0, FIRST: 2 * line, LINE: 3 * line}[kind]
        number = first * line + z if kind == CORE else z
        core = 1 - spot.core if kind == CORE else spot.core
        source = self.part(*spot.block(core, first, 0, z))
        target = spot.z if kind == LINE else number
        return spot.send(
            source,
            self.places[kind].at[target],
            self.sends.at[base + number],
            self.receives.at[base + target],
            kind,
            z if kind == LINE else None,
        )

    def arrived(self, kind, index):
        spot = self.spot
        base = {CORE: 0, FIRST: 2 * spot.line, LINE: 3 * spot.line}[kind]
        place = self.places[kind].at[index]
        spot.send(place, place, self.sends.at[0], self.receives.at[base + index], CORE).wait_recv()
        return place

    def begin(self, z):
        for first in (1, 0):
            self.copy(CORE, first, z).start()

    def to_first(self, z):
        own = self.part(*self.spot.block(self.spot.core, 1, 0, z))
        add_rows(own, [own, self.arrived(CORE, self.spot.line + z)])
        self.copy(FIRST, 1, z).start()

    def onward(self, z):
        own = self.part(*self.spot.block(self.spot.core, 0, 0, z))
        sources = [own, self.arrived(CORE, z), self.arrived(FIRST, z)]

        def to_end():
            add_rows(own, sources)
            self.copy(LINE, 0, z).start()

        when(z != self.spot.z, to_end)

    def last(self):
        spot = self.spot
        z = spot.z
        own = self.part(*spot.block(spot.core, 0, 0, z))
        sources = [own, self.places[CORE].at[z], self.places[FIRST].at[z]]
        for step in range(1, spot.line):
            other = lax.rem(z + step, spot.line)
            sources.append(self.arrived(LINE, other))
        add_rows(self.total, sources)

    def finish(self):
        spot = self.spot
        for z in range(spot.line):
            for first in (0, 1):
                self.copy(CORE, first, z).wait_send()
            self.copy(FIRST, 1, z).wait_send()
            when(z != spot.z, lambda: self.copy(LINE, 0, z).wait_send())

    def tasks(self):
        spot = self.spot
        line = spot.line
        others = [lax.rem(spot.z + step, line) for step in range(1, line)] + [spot.z]
        work = [functools.partial(self.to_first, z) for z in others]
        work += [functools.partial(self.onward, z) for z in others]
        return work + [self.last, self.finish]


def collect_scratch(line, shape):
    return [pltpu.VMEM((count, *shape), jnp.bfloat16) for count in (2 * line, line, line)] + [
        pltpu.SemaphoreType.DMA((4 * line,)),
        pltpu.SemaphoreType.DMA((4 * line,)),
    ]


def norm_back(value, grads, gain):
    scale = lax.rsqrt(jnp.mean(value * value, axis=-1, keepdims=True) + EPSILON)
    unit = value * scale
    scaled = grads * gain
    back = scale * (scaled - unit * jnp.mean(scaled * unit, axis=-1, keepdims=True))
    return back, grads * unit


def backward_kernel(
    line,
    heads,
    kv_heads,
    cot_ref,
    totals_ref,
    hidden_ref,
    projected_ref,
    context_ref,
    in_ref,
    out_ref,
    tokens_ref,
    gain1_ref,
    gain2_ref,
    query_gain_ref,
    key_gain_ref,
    cosine_ref,
    sine_ref,
    block_out,
    input_grad,
    grads_all,
    out_total,
    gain_grads,
    elements,
    cots,
    tokens,
    kept,
    result,
    context,
    hidden_grads,
    context_grads,
    grads,
    normed_grads,
    normed_other,
    out_rows,
    in_rows,
    queries_f,
    shared_f,
    queries,
    query_grads,
    sums,
    out_grads,
    cores,
    firsts,
    ends,
    tree_send,
    tree_receive,
    load_sem,
    row_sem,
    head_sem,
    save_sem,
    hidden_send,
    hidden_receive,
    normed_send,
    normed_receive,
):
    batch, half, width = cot_ref.shape
    length = 2 * half
    features = query_gain_ref.shape[1]
    group = heads // kv_heads
    base = heads * features
    out_width = out_total.shape[1]
    narrow, spot = Spot(line, False), Spot(line, True)
    x = spot.x
    scale = features ** (-0.5)

    def load(source, target, index):
        return pltpu.make_async_copy(source, target, load_sem.at[index])

    def element_loads(i):
        return [
            load(hidden_ref.at[i], elements.at[0], 0),
            load(totals_ref.at[i, OUTPUT], elements.at[1], 1),
            load(totals_ref.at[i, BACK], elements.at[2], 2),
        ]

    first_loads = [load(cot_ref, cots, 3), load(tokens_ref, tokens, 4)] + [
        load(context_ref.at[i], rows_at(context, i, length), 5 + i) for i in range(batch)
    ]
    for copy in element_loads(0) + first_loads:
        copy.start()

    def out_load(step):
        slot = lax.rem(step, 2)
        return pltpu.make_async_copy(
            rows_at(out_ref, step, CHUNK), out_rows.at[slot], row_sem.at[0, slot]
        )

    def in_load(step):
        slot = lax.rem(step, 2)
        return pltpu.make_async_copy(
            rows_at(in_ref, step, CHUNK), in_rows.at[slot], row_sem.at[1, slot]
        )

    out_steps, in_steps = out_ref.shape[0] // CHUNK, in_ref.shape[0] // CHUNK
    for step in range(2):
        out_load(step).start()
        in_load(step).start()
    gain_grads[...] = jnp.zeros_like(gain_grads)
    spot.greet()
    for copy in first_loads:
        copy.wait()

    def result_save(i, target):
        return pltpu.make_async_copy(result.at[i], target.at[i], save_sem.at[i])

    def half_copy(ref, i, side):
        return ref.at[pl.ds(pl.multiple_of(i * length + side * half, 16), half)]

    def hidden_copy(i):
        place = half_copy(hidden_grads, i, x)
        return spot.send(place, place, hidden_send.at[i], hidden_receive.at[i], CROSS)

    for i in range(batch):
        for copy in element_loads(i):
            copy.wait()

        def elementwise(step, _):
            rows = pl.ds(pl.multiple_of(step * 16, 16), 16)
            value = elements[0, rows, :]
            result[i, rows, :] = (value + elements[1, rows, :]).astype(jnp.bfloat16)
            back, gain_rows = norm_back(value, elements[2, rows, :], gain2_ref[...])
            gain_grads[1:2, :] += jnp.sum(gain_rows, axis=0, keepdims=True)
            total = cots[i, rows, :].astype(jnp.float32) + back
            kept[i, rows, :] = total
            place = pl.ds(pl.multiple_of(i * length + x * half + step * 16, 16), 16)
            hidden_grads[place, :] = total.astype(jnp.bfloat16)
            return 0

        lax.fori_loop(0, half // 16, elementwise, 0)
        hidden_copy(i).start()
        result_save(i, block_out).start()
        if i + 1 < batch:
            for copy in element_loads(i + 1):
                copy.start()
    for i in range(batch):
        hidden_copy(i).wait_send()
        place = half_copy(hidden_grads, i, 1 - x)
        spot.send(place, place, hidden_send.at[i], hidden_receive.at[i], CROSS).wait_recv()

    def context_step(step, _):
        out_load(step).wait()
        columns = pl.ds(pl.multiple_of(step * CHUNK, LANES), CHUNK)
        context_grads[:, columns] = lax.dot_general(
            hidden_grads[...],
            out_rows[lax.rem(step, 2)],
            TRANSPOSED_RIGHT,
            preferred_element_type=jnp.float32,
        ).astype(jnp.bfloat16)
        when(step + 2 < out_steps, lambda: out_load(step + 2).start())
        for start in range(0, width, CHUNK):
            out_grads[pl.ds(pl.multiple_of(step * CHUNK, 16), CHUNK), start : start + CHUNK] = (
                lax.dot_general(
                    context[:, columns],
                    hidden_grads[:, start : start + CHUNK],
                    TRANSPOSED_LEFT,
                    preferred_element_type=jnp.float32,
                ).astype(jnp.bfloat16)
            )
        return 0

    lax.fori_loop(0, out_steps, context_step, 0)
    tree = Collect(
        narrow,
        lambda block, side: columns_at(out_grads, block, out_width),
        out_total,
        cores,
        firsts,
        ends,
        tree_send,
        tree_receive,
    )
    for z in range(line):
        tree.begin(z)
    work = tree.tasks()

    def turns():
        return [(i, shared) for i in range(batch) for shared in range(kv_heads)]

    def head_loads(index):
        i, shared = turns()[index]
        slot = index % 2
        return [
            pltpu.make_async_copy(
                projected_ref.at[i, :, pl.ds(shared * group * features, group * features)],
                queries_f.at[slot],
                head_sem.at[slot, 0],
            )
        ] + [
            pltpu.make_async_copy(
                projected_ref.at[i, :, pl.ds(base + (shared + j * kv_heads) * features, features)],
                shared_f.at[slot, j],
                head_sem.at[slot, 1 + j],
            )
            for j in range(2)
        ]

    for copy in head_loads(0):
        copy.start()

    def turn_back(grads_in):
        return grads_in * cosine_ref[...] + pltpu.roll(
            grads_in * sine_ref[...], features // 2, 1
        )

    def attend(index):
        i, shared = turns()[index]
        slot = index % 2
        for copy in head_loads(index):
            copy.wait()
        if index + 1 < len(turns()):
            for copy in head_loads(index + 1):
                copy.start()
        top = i * length
        key = turned_heads(
            shared_f[slot, 0], key_gain_ref[...], cosine_ref[...], sine_ref[...]
        ).astype(jnp.bfloat16)
        queries[group] = key
        queries[group + 1] = shared_f[slot, 1].astype(jnp.bfloat16)
        sums[...] = jnp.zeros_like(sums)

        def columns_of(member):
            return pl.ds(pl.multiple_of(member * features, LANES), features)

        def prepare(member):
            queries[member] = turned_heads(
                queries_f[slot, :, columns_of(member)],
                query_gain_ref[...],
                cosine_ref[...],
                sine_ref[...],
            ).astype(jnp.bfloat16)

        for_heads(group, 1, prepare)
        for start, stop, seen, at_once in visible_blocks(length, group):
            count = stop - start

            def block(member):
                query = queries[pl.ds(member, at_once), start:stop, :].reshape(-1, features)
                keys, values = queries[group, :seen, :], queries[group + 1, :seen, :]
                out_grad = jnp.concatenate(
                    [
                        context_grads[
                            top + start : top + stop,
                            head_columns(shared * group + member + j, features),
                        ]
                        for j in range(at_once)
                    ],
                    axis=0,
                )
                scores = lax.dot_general(
                    query, keys, TRANSPOSED_RIGHT, preferred_element_type=jnp.float32
                )
                shares = softmax(scores * scale)
                share_grads = lax.dot_general(
                    out_grad, values, TRANSPOSED_RIGHT, preferred_element_type=jnp.float32
                )
                sums[1, :seen, :] += lax.dot_general(
                    shares.astype(jnp.bfloat16),
                    out_grad,
                    TRANSPOSED_LEFT,
                    preferred_element_type=jnp.float32,
                )
                inner = jnp.sum(shares * share_grads, axis=-1, keepdims=True)
                score_grads = (shares * (share_grads - inner)).astype(jnp.bfloat16)
                rows = scale * jnp.dot(score_grads, keys, preferred_element_type=jnp.float32)
                query_grads[pl.ds(member, at_once), start:stop, :] = rows.reshape(
                    at_once, count, features
                )
                sums[0, :seen, :] += lax.dot_general(
                    score_grads, query, TRANSPOSED_LEFT, preferred_element_type=jnp.float32
                )

            for_heads(group, at_once, block)

        def finish(member):
            back, gain_rows = norm_back(
                queries_f[slot, :, columns_of(member)],
                turn_back(query_grads[member]),
                query_gain_ref[...],
            )
            gain_grads[2:3, :features] += jnp.sum(gain_rows, axis=0, keepdims=True)
            grads[top : top + length, head_columns(shared * group + member, features)] = (
                back.astype(jnp.bfloat16)
            )

        for_heads(group, 1, finish)
        back, gain_rows = norm_back(
            shared_f[slot, 0], turn_back(sums[0] * scale), key_gain_ref[...]
        )
        gain_grads[3:4, :features] += jnp.sum(gain_rows, axis=0, keepdims=True)
        at = base + shared * features
        grads[top : top + length, at : at + features] = back.astype(jnp.bfloat16)
        at += kv_heads * features
        grads[top : top + length, at : at + features] = sums[1].astype(jnp.bfloat16)

    for index in range(len(turns())):
        attend(index)
        for _ in range(2):
            if work:
                work.pop(0)()

    saves = [
        pltpu.make_async_copy(rows_at(grads, i, length), grads_all.at[i], save_sem.at[batch + i])
        for i in range(batch)
    ]
    for copy in saves:
        copy.start()

    def normed_step(step, _):
        in_load(step).wait()
        columns = pl.ds(pl.multiple_of(step * CHUNK, LANES), CHUNK)
        normed_grads[:, columns] = lax.dot_general(
            grads[...],
            in_rows[lax.rem(step, 2)],
            TRANSPOSED_RIGHT,
            preferred_element_type=jnp.float32,
        ).astype(jnp.bfloat16)
        when(step + 2 < in_steps, lambda: in_load(step + 2).start())
        return 0

    lax.fori_loop(0, in_steps, normed_step, 0)

    def normed_copy(i):
        return spot.send(
            half_copy(normed_grads, i, 1 - x),
            normed_other.at[i],
            normed_send.at[i],
            normed_receive.at[i],
            CROSS,
        )

    for i in range(batch):
        normed_copy(i).start()
    while work:
        work.pop(0)()
    for i in range(batch):
        normed_copy(i).wait()
        result_save(i, block_out).wait()

        def input_rows(step, _):
            rows = pl.ds(pl.multiple_of(step * 16, 16), 16)
            place = pl.ds(pl.multiple_of(i * length + x * half + step * 16, 16), 16)
            total = normed_grads[place, :].astype(jnp.float32) + normed_other[i, rows, :].astype(
                jnp.float32
            )
            back, gain_rows = norm_back(
                tokens[i, rows, :].astype(jnp.float32), total, gain1_ref[...]
            )
            gain_grads[0:1, :] += jnp.sum(gain_rows, axis=0, keepdims=True)
            result[i, rows, :] = (kept[i, rows, :] + back).astype(jnp.bfloat16)
            return 0

        lax.fori_loop(0, half // 16, input_rows, 0)
        result_save(i, input_grad).start()
    for i in range(batch):
        result_save(i, input_grad).wait()
    for copy in saves:
        copy.wait()


def run_backward(
    cot, totals, hidden, projected, context, in_full, out_full, tokens, gains, tables, fsdp_count, kv_heads
):
    line = fsdp_count // PLANE
    batch, half, width = tokens.shape
    length = 2 * half
    features = gains[2].shape[1]
    heads = out_full.shape[0] // features
    group = heads // kv_heads
    in_width, out_depth = in_full.shape[1], out_full.shape[0]
    out_shape = (out_depth, width // fsdp_count)
    anywhere = pl.BlockSpec(memory_space=pl.ANY)
    inside = pl.BlockSpec(memory_space=pltpu.VMEM)
    vmem = lambda *dims: pltpu.VMEM(dims, jnp.bfloat16)
    wide = lambda *dims: pltpu.VMEM(dims, jnp.float32)
    sem = lambda *dims: pltpu.SemaphoreType.DMA(dims)
    rows = batch * length
    return pl.pallas_call(
        functools.partial(backward_kernel, line, heads, kv_heads),
        out_shape=(
            jax.ShapeDtypeStruct((batch, half, width), jnp.bfloat16),
            jax.ShapeDtypeStruct((batch, half, width), jnp.bfloat16),
            jax.ShapeDtypeStruct((batch, length, in_width), jnp.bfloat16),
            jax.ShapeDtypeStruct(out_shape, jnp.float32),
            jax.ShapeDtypeStruct((8, width), jnp.float32),
        ),
        in_specs=[anywhere] * 8 + [inside] * 6,
        out_specs=(anywhere, anywhere, anywhere, inside, inside),
        scratch_shapes=[
            wide(3, half, width),
            vmem(batch, half, width),
            vmem(batch, half, width),
            wide(batch, half, width),
            vmem(batch, half, width),
            vmem(rows, out_depth),
            vmem(rows, width),
            vmem(rows, out_depth),
            vmem(rows, in_width),
            vmem(rows, width),
            vmem(batch, half, width),
            vmem(2, CHUNK, width),
            vmem(2, CHUNK, in_width),
            wide(2, length, group * features),
            wide(2, 2, length, features),
            vmem(group + 2, length, features),
            wide(group, length, features),
            wide(2, length, features),
            vmem(out_depth, width),
            *collect_scratch(line, out_shape),
            sem(5 + batch),
            sem(2, 2),
            sem(2, 3),
            sem(2 * batch),
            sem(batch),
            sem(batch),
            sem(batch),
            sem(batch),
        ],
        compiler_params=pltpu.CompilerParams(
            collective_id=3, has_side_effects=True, vmem_limit_bytes=62 * MIB
        ),
    )(cot, totals, hidden, projected, context, in_full, out_full, tokens, *gains, *tables)


def gradients_kernel(
    line,
    normed,
    grads,
    gains_ref,
    in_total,
    gains_all,
    parts,
    cores,
    firsts,
    ends,
    tree_send,
    tree_receive,
    gain_send,
    gain_receive,
    gain_local,
):
    narrow, spot = Spot(line, False), Spot(line, True)
    spot.greet()
    gains = Spread(
        spot,
        gains_ref,
        lambda block, half: gains_all.at[block, half],
        gain_send,
        gain_receive,
        gain_local.at[0],
    )
    gains.begin()
    depth, width = in_total.shape
    tree = Collect(
        narrow,
        lambda block, half: rows_at(parts, block, depth),
        in_total,
        cores,
        firsts,
        ends,
        tree_send,
        tree_receive,
    )
    chunk = PLANE * depth

    def plane(step, _):
        z = lax.rem(narrow.z + 1 + step, line)
        columns = pl.ds(pl.multiple_of(z * chunk, LANES), chunk)
        for start in range(0, width, CHUNK):
            parts[pl.ds(pl.multiple_of(z * chunk, 16), chunk), start : start + CHUNK] = (
                lax.dot_general(
                    normed[:, columns],
                    grads[:, start : start + CHUNK],
                    TRANSPOSED_LEFT,
                    preferred_element_type=jnp.float32,
                ).astype(jnp.bfloat16)
            )
        tree.begin(z)
        return 0

    lax.fori_loop(0, line, plane, 0)
    work = tree.tasks()
    steps = list(range(1, gains.steps()))
    while work:
        work.pop(0)()
        if steps:
            gains.step(steps.pop(0))
    gains.finish()


def run_gradients(normed, grads, gains, fsdp_count):
    line = fsdp_count // PLANE
    width = grads.shape[1]
    shape = (normed.shape[1] // fsdp_count, width)
    sends, receives = spread_count(line, True)
    inside = pl.BlockSpec(memory_space=pltpu.VMEM)
    anywhere = pl.BlockSpec(memory_space=pl.ANY)
    return pl.pallas_call(
        functools.partial(gradients_kernel, line),
        out_shape=(
            jax.ShapeDtypeStruct(shape, jnp.float32),
            jax.ShapeDtypeStruct((fsdp_count, 2, *gains.shape), jnp.float32),
        ),
        in_specs=[inside, inside, anywhere],
        out_specs=(inside, anywhere),
        scratch_shapes=[
            pltpu.VMEM((normed.shape[1], width), jnp.bfloat16),
            *collect_scratch(line, shape),
            pltpu.SemaphoreType.DMA((sends,)),
            pltpu.SemaphoreType.DMA((receives,)),
            pltpu.SemaphoreType.DMA((1,)),
        ],
        compiler_params=pltpu.CompilerParams(
            collective_id=4, has_side_effects=True, vmem_limit_bytes=56 * MIB
        ),
    )(normed, grads, gains)


def experts_kernel(
    line,
    slots,
    own_ref,
    cot_ref,
    info_ref,
    gate_ref,
    up_ref,
    down_ref,
    all_ref,
    total_ref,
    xe_all,
    ce_all,
    act_all,
    dgate_all,
    dup_all,
    part,
    cores,
    seconds,
    firsts,
    ends,
    hidden_w,
    down_w,
    x_rows,
    c_rows,
    xe,
    ce,
    acts,
    dgates,
    dups,
    hidden_grads,
    picks,
    weigh,
    rows,
    stage,
    inbox,
    outbox,
    summed,
    tree_send,
    tree_receive,
    tree_local,
    load_sem,
    save_sem,
    stage_sem,
    inbox_sem,
    outbox_sem,
    total_sem,
    weight_sem,
    core_receive,
    second_receive,
    first_receive,
    end_receive,
):
    spot = Spot(line, True)
    z, core = spot.z, spot.core
    batch, half, width = own_ref.shape
    length = 2 * half
    units = down_ref.shape[1]
    groups = batch * line
    weights = [
        pltpu.make_async_copy(source, target, weight_sem.at[i])
        for i, (source, target) in enumerate(
            [(down_ref, down_w)]
            + [(gate_ref.at[e], hidden_w.at[e, :, pl.ds(0, units)]) for e in range(2)]
            + [(up_ref.at[e], hidden_w.at[e, :, pl.ds(units, units)]) for e in range(2)]
        )
    ]
    for copy in weights:
        copy.start()
    rows[...] = jnp.zeros_like(rows)
    spot.greet()

    def half_of(ref, index):
        return rows_at(ref, index, half)

    trees = [
        Spread(
            spot,
            own_ref.at[i],
            lambda block, side, i=i: half_of(all_ref.at[i, block], side),
            tree_send.at[i],
            tree_receive.at[i],
            tree_local.at[i],
        )
        for i in range(batch)
    ]
    run_trees(trees[:1])
    for tree in trees[1:]:
        tree.begin()
    for copy in weights:
        copy.wait()

    def plane_of(group):
        turn = lax.rem(group, line)
        step = lax.div(turn, 2)
        return jnp.where(lax.rem(turn, 2) == 0, step, line - 1 - step)

    def load_group(group, member):
        at = lax.div(group, line)
        sequence = plane_of(group) * PLANE + member
        slot = lax.rem(member, 2)
        return [
            pltpu.make_async_copy(all_ref.at[at, sequence], x_rows.at[slot], load_sem.at[0, slot]),
            pltpu.make_async_copy(cot_ref.at[at, sequence], c_rows.at[slot], load_sem.at[1, slot]),
        ]

    def saves(group):
        to = lambda ref, expert: rows_at(ref.at[expert], group, PLANE * slots)
        pairs = ((xe, xe_all), (ce, ce_all), (acts, act_all), (dgates, dgate_all), (dups, dup_all))
        return [
            pltpu.make_async_copy(source.at[expert], to(target, expert), save_sem.at[2 * i + expert])
            for i, (source, target) in enumerate(pairs)
            for expert in range(2)
        ]

    def staged(group, tensor, y, mine):
        unit = group * 2 + tensor
        slot = y * 2 + mine
        if mine:
            return pltpu.make_async_copy(stage.at[slot], part.at[unit, y], stage_sem.at[slot])
        return spot.send(
            stage.at[slot], cores.at[unit, y], stage_sem.at[slot], core_receive.at[unit, y], CORE
        )

    def combine(group, tensor):
        for y in range(2):
            for mine in range(2):
                member = y * 2 + (core if mine else 1 - core)
                for start in range(0, width, CHUNK):
                    stage[y * 2 + mine, :, start : start + CHUNK] = lax.dot_general(
                        picks[member],
                        rows[member, :, start : start + CHUNK],
                        TRANSPOSED_LEFT,
                        preferred_element_type=jnp.float32,
                    ).astype(jnp.bfloat16)
                staged(group, tensor, y, mine).start()

    def stages_done(group, tensor):
        for y in range(2):
            staged(group, tensor, y, 1).wait()
            staged(group, tensor, y, 0).wait_send()

    def compute(group):
        when(group > 0, lambda: [copy.wait() for copy in saves(group - 1)] and None)

        def pick(member, _):
            slot = lax.rem(member, 2)
            for copy in load_group(group, member):
                copy.wait()

            @pl.when(member + 1 < PLANE)
            def _():
                for copy in load_group(group, member + 1):
                    copy.start()

            sequence = plane_of(group) * PLANE + member
            info = info_ref[lax.div(group, line) * line * PLANE + sequence]
            places = lax.broadcasted_iota(jnp.int32, (2 * LANES, length), 0)
            lower = places < LANES
            ranks = jnp.where(lower, info[0:1], info[1:2] + float(LANES)).astype(jnp.int32)
            some = jnp.where(lower, info[0:1], info[1:2]) >= 0.0
            hot = jnp.logical_and(ranks == places, some)
            chosen = hot.astype(jnp.float32).astype(jnp.bfloat16)
            picks[member] = chosen
            shares = jnp.where(hot, jnp.where(lower, info[2:3], info[3:4]), 0.0)
            column = jnp.sum(shares, axis=1, keepdims=True)
            here = pl.ds(pl.multiple_of(member * slots, 16), slots)
            for expert in range(2):
                weigh[expert, here, :] = jnp.broadcast_to(
                    column[expert * LANES : expert * LANES + slots], (slots, LANES)
                )
            for source, target in ((x_rows, xe), (c_rows, ce)):
                for start in range(0, width, CHUNK):
                    selected = jnp.dot(
                        chosen,
                        source[slot, :, start : start + CHUNK],
                        preferred_element_type=jnp.float32,
                    ).astype(jnp.bfloat16)
                    for expert in range(2):
                        target[expert, here, start : start + CHUNK] = selected[
                            expert * LANES : expert * LANES + slots
                        ]
            return 0

        lax.fori_loop(0, PLANE, pick, 0)

        def keep(expert, product, start):
            at = pl.ds(pl.multiple_of(expert * LANES, LANES), slots)
            for one in range(PLANE):
                rows[one, at, start : start + CHUNK] = product[
                    one * slots : (one + 1) * slots
                ].astype(jnp.bfloat16)

        def forward(expert, _):
            hidden = jnp.dot(xe[expert], hidden_w[expert], preferred_element_type=jnp.float32)
            gate, up = hidden[:, :units], hidden[:, units:]
            sigmoid = jax.nn.sigmoid(gate)
            silu = gate * sigmoid
            scale = weigh[expert, :, 0:1]
            acts[expert] = (silu * up * scale).astype(jnp.bfloat16)
            act_grads = scale * lax.dot_general(
                ce[expert], down_w[expert], TRANSPOSED_RIGHT, preferred_element_type=jnp.float32
            )
            gate_grads = (act_grads * up * (sigmoid * (1.0 + gate * (1.0 - sigmoid)))).astype(
                jnp.bfloat16
            )
            up_grads = (act_grads * silu).astype(jnp.bfloat16)
            dgates[expert] = gate_grads
            dups[expert] = up_grads
            hidden_grads[expert, :, :units] = gate_grads
            hidden_grads[expert, :, units:] = up_grads
            for start in range(0, width, CHUNK):
                keep(
                    expert,
                    jnp.dot(
                        acts[expert],
                        down_w[expert, :, start : start + CHUNK],
                        preferred_element_type=jnp.float32,
                    ),
                    start,
                )
            return 0

        lax.fori_loop(0, 2, forward, 0)
        for copy in saves(group):
            copy.start()
        combine(group, OUTPUT)

        def backward(expert, _):
            for start in range(0, width, CHUNK):
                keep(
                    expert,
                    lax.dot_general(
                        hidden_grads[expert],
                        hidden_w[expert, start : start + CHUNK, :],
                        TRANSPOSED_RIGHT,
                        preferred_element_type=jnp.float32,
                    ),
                    start,
                )
            return 0

        lax.fori_loop(0, 2, backward, 0)
        stages_done(group, OUTPUT)
        combine(group, BACK)

    def inside(group):
        return jnp.logical_and(group >= 0, group < groups)

    def second_send(group, tensor, first):
        unit, slot = group * 2 + tensor, tensor * 2 + first
        return spot.send(
            outbox.at[slot],
            seconds.at[unit, first],
            outbox_sem.at[slot],
            second_receive.at[unit, first],
            SECOND,
        )

    def first_send(group, tensor):
        unit, slot = group * 2 + tensor, 4 + tensor
        return spot.send(
            outbox.at[slot], firsts.at[unit], outbox_sem.at[slot], first_receive.at[unit], FIRST
        )

    def end_send(group, tensor):
        unit, slot = group * 2 + tensor, 6 + tensor
        return spot.send(
            outbox.at[slot],
            ends.at[unit, z],
            outbox_sem.at[slot],
            end_receive.at[unit, z],
            LINE,
            plane_of(group),
        )

    def sources(unit, first, second):
        y, x = spot.side(core, first, second)
        return [half_of(part.at[unit, y], x), half_of(cores.at[unit, y], x)]

    def load(source, slot):
        return pltpu.make_async_copy(source, inbox.at[slot], inbox_sem.at[slot])

    def away(group):
        return jnp.logical_and(inside(group), plane_of(jnp.maximum(group, 0)) != z)

    def here(group):
        return jnp.logical_and(inside(group), plane_of(jnp.maximum(group, 0)) == z)

    def received(place, semaphore):
        spot.send(place, place, outbox_sem.at[0], semaphore, CORE).wait_recv()

    def retire(step):
        before = step - 1

        @pl.when(inside(before))
        def _():
            stages_done(before, BACK)

        for tensor in range(2):
            when(
                inside(before - 1),
                lambda: [second_send(before - 1, tensor, first).wait_send() for first in range(2)]
                and None,
            )
            when(inside(before - 2), lambda: first_send(before - 2, tensor).wait_send())

            when(away(before - 3), lambda: end_send(before - 3, tensor).wait_send())

    def serve(step):
        tasks = []
        for tensor in range(2):
            group = step - 4
            unit = group * 2 + tensor

            def ends_in(unit=unit):
                for i in range(1, line):
                    other = lax.rem(z + i, line)
                    received(ends.at[unit, other], end_receive.at[unit, other])

            tasks.append(
                (
                    here(group),
                    ends_in,
                    lambda unit=unit: sources(unit, 0, 0)
                    + [seconds.at[unit, 0], firsts.at[unit]]
                    + [ends.at[unit, lax.rem(z + i, line)] for i in range(1, line)],
                    None,
                    lambda group=group, tensor=tensor: pltpu.make_async_copy(
                        summed, total_ref.at[lax.div(group, line), tensor], total_sem.at[0]
                    ),
                )
            )
        for tensor in range(2):
            group = step - 3
            unit = group * 2 + tensor

            def both_in(unit=unit):
                received(seconds.at[unit, 0], second_receive.at[unit, 0])
                received(firsts.at[unit], first_receive.at[unit])

            when(inside(group), both_in)
            tasks.append(
                (
                    away(group),
                    lambda: None,
                    lambda unit=unit: sources(unit, 0, 0) + [seconds.at[unit, 0], firsts.at[unit]],
                    6 + tensor,
                    lambda group=group, tensor=tensor: end_send(group, tensor),
                )
            )
        for tensor in range(2):
            unit = (step - 2) * 2 + tensor
            tasks.append(
                (
                    inside(step - 2),
                    lambda unit=unit: received(seconds.at[unit, 1], second_receive.at[unit, 1]),
                    lambda unit=unit: sources(unit, 1, 0) + [seconds.at[unit, 1]],
                    4 + tensor,
                    lambda tensor=tensor: first_send(step - 2, tensor),
                )
            )
        for first in (1, 0):
            for tensor in range(2):
                unit = (step - 1) * 2 + tensor

                def cores_in(unit=unit):
                    for y in range(2):
                        received(cores.at[unit, y], core_receive.at[unit, y])

                tasks.append(
                    (
                        inside(step - 1),
                        cores_in if first else lambda: None,
                        lambda unit=unit, first=first: sources(unit, first, 1),
                        tensor * 2 + first,
                        lambda tensor=tensor, first=first: second_send(step - 1, tensor, first),
                    )
                )
        boxes = inbox.shape[0] // 2

        def begin(index):
            valid, ready, inputs, _, _ = tasks[index]

            def action():
                ready()
                for i, source in enumerate(inputs()):
                    load(source, (index % 2) * boxes + i).start()

            when(valid, action)

        begin(0)
        for index, (valid, _, inputs, slot, send) in enumerate(tasks):
            if index + 1 < len(tasks):
                begin(index + 1)

            def action():
                refs = inputs()
                base = (index % 2) * boxes
                for i, source in enumerate(refs):
                    load(source, base + i).wait()
                target = summed if slot is None else outbox.at[slot]
                add_rows(target, [inbox.at[base + i] for i in range(len(refs))])
                send().start()
                if slot is None:
                    send().wait()

            when(valid, action)

    def step_body(step, _):
        for i in range(1, batch):
            when(step == i * line, trees[i].finish)

        @pl.when(step < groups)
        def _():
            for copy in load_group(step, 0):
                copy.start()

        for i in range(1, batch):
            turn = step - (i - 1) * line
            when(jnp.logical_and(turn >= 0, turn < line), lambda: trees[i].step(2 * turn + 1))
        retire(step)
        serve(step)
        for i in range(1, batch):
            turn = step - (i - 1) * line
            when(jnp.logical_and(turn >= 0, turn < line), lambda: trees[i].step(2 * turn + 2))
        when(step < groups, lambda: compute(step))
        return 0

    steps = groups + 4
    lax.fori_loop(0, steps, step_body, 0)
    retire(jnp.int32(steps))
    for copy in saves(groups - 1):
        copy.wait()


def run_experts(rows, cot_all, info, w_gate, w_up, w_down, capacity, fsdp_count):
    line = fsdp_count // PLANE
    batch, half, width = rows.shape
    length = 2 * half
    units = w_down.shape[1]
    slots = -(-capacity // 16) * 16
    groups = batch * line
    count = groups * PLANE * slots
    taken = PLANE * slots
    sends, receives = spread_count(line, True)
    shape = lambda *dims: jax.ShapeDtypeStruct(dims, jnp.bfloat16)
    block = (half, width)
    anywhere = pl.BlockSpec(memory_space=pl.ANY)
    vmem = lambda *dims: pltpu.VMEM(dims, jnp.bfloat16)
    sem = lambda *dims: pltpu.SemaphoreType.DMA(dims)
    return pl.pallas_call(
        functools.partial(experts_kernel, line, slots),
        out_shape=(
            shape(batch, fsdp_count, length, width),
            jax.ShapeDtypeStruct((batch, 2, *block), jnp.float32),
            shape(2, count, width),
            shape(2, count, width),
            shape(2, count, units),
            shape(2, count, units),
            shape(2, count, units),
            shape(2 * groups, 2, length, width),
            shape(2 * groups, 2, length, width),
            shape(2 * groups, 2, *block),
            shape(2 * groups, *block),
            shape(2 * groups, line, *block),
        ),
        in_specs=[
            anywhere,
            anywhere,
            pl.BlockSpec(memory_space=pltpu.VMEM),
            anywhere,
            anywhere,
            anywhere,
        ],
        out_specs=(anywhere,) * 12,
        scratch_shapes=[
            vmem(2, width, 2 * units),
            vmem(2, units, width),
            vmem(2, length, width),
            vmem(2, length, width),
            vmem(2, taken, width),
            vmem(2, taken, width),
            vmem(2, taken, units),
            vmem(2, taken, units),
            vmem(2, taken, units),
            vmem(2, taken, 2 * units),
            vmem(PLANE, 2 * LANES, length),
            pltpu.VMEM((2, taken, LANES), jnp.float32),
            vmem(PLANE, 2 * LANES, width),
            vmem(PLANE, length, width),
            vmem(2 * (3 + line), *block),
            vmem(8, *block),
            pltpu.VMEM(block, jnp.float32),
            sem(batch, sends),
            sem(batch, receives),
            sem(batch),
            sem(2, 2),
            sem(10),
            sem(PLANE),
            sem(2 * (3 + line)),
            sem(8),
            sem(1),
            sem(5),
            sem(2 * groups, 2),
            sem(2 * groups, 2),
            sem(2 * groups),
            sem(2 * groups, line),
        ],
        compiler_params=pltpu.CompilerParams(
            collective_id=2, has_side_effects=True, vmem_limit_bytes=60 * MIB
        ),
    )(rows, cot_all, info, w_gate, w_up, w_down)[1:7]


def packed_picks(routes, gates):
    length = routes.shape[2]
    packed = jnp.concatenate([routes[:, 0].astype(jnp.float32), gates[:, 0]], axis=-1)
    packed = jnp.swapaxes(packed, 1, 2).reshape(-1, length)
    return jnp.pad(packed, ((0, 0), (0, -length % LANES)))


def slot_info(packed, batch, top, length, local_experts):
    fsdp_count = packed.shape[0]
    packed = packed[..., :length].reshape(fsdp_count, batch, 1, 2 * top, length)
    packed = jnp.swapaxes(packed, 0, 1)
    experts = lax.axis_index(FSDP) * local_experts + jnp.arange(local_experts, dtype=jnp.int32)
    same = packed[..., :top, :].astype(jnp.int32) == experts[:, None, None]
    hot = jnp.any(same, axis=3)
    shares = jnp.sum(jnp.where(same, packed[..., top:, :], 0.0), axis=3)
    position = jnp.arange(length)
    upper = (position[:, None] < position[None, :]).astype(jnp.bfloat16)
    rank = jnp.dot(
        hot.astype(jnp.bfloat16).reshape(-1, length), upper, preferred_element_type=jnp.float32
    )
    rank = jnp.where(hot, rank.reshape(hot.shape), -1.0)
    return jnp.concatenate([rank, shares], axis=2).reshape(-1, 2 * local_experts, length)


def gathered_layer(
    tokens,
    cotangent,
    norm1_gain,
    w_query,
    key_projection_weight,
    value_projection_weight,
    query_gain,
    key_gain,
    w_out,
    norm2_gain,
    w_gate,
    w_up,
    w_down,
    routes,
    gates,
):
    batch_count = tokens.shape[0]
    model_width = tokens.shape[3]
    sequence_length = routes.shape[2]
    half_length = tokens.shape[2]
    top_count = routes.shape[3]
    head_features = query_gain.shape[0]
    local_experts = w_gate.shape[0]
    fsdp_count = lax.axis_size(FSDP)
    all_experts = local_experts * fsdp_count
    capacity = 7 * top_count * sequence_length // (6 * all_experts)
    query_width = w_query.shape[1]
    kv_width = key_projection_weight.shape[1]
    kv_heads = kv_width // head_features
    cosine_table, sine_values = rotary_tables(sequence_length, head_features)
    first_gain = norm1_gain.astype(jnp.float32)
    second_gain = norm2_gain.astype(jnp.float32)
    query_factor_scale = query_gain.astype(jnp.float32)
    key_scale = key_gain.astype(jnp.float32)

    weight_in = jnp.concatenate([w_query, key_projection_weight, value_projection_weight], axis=1)
    half_signs = jnp.where(jnp.arange(head_features) < head_features // 2, -1.0, 1.0)
    tables = (cosine_table[:, 0], sine_values[:, 0] * half_signs)
    gains = [
        gain[None, :] for gain in (first_gain, second_gain, query_factor_scale, key_scale)
    ]
    cot_all, in_full, out_full, picks, normed, projected, contexts, hidden, second = run_forward(
        tokens[:, 0],
        cotangent[:, 0],
        weight_in,
        w_out,
        packed_picks(routes, gates),
        gains,
        tables,
        fsdp_count,
        kv_heads,
    )
    info = slot_info(picks, batch_count, top_count, sequence_length, local_experts)
    totals, expert_rows, cot_rows, act_rows, gate_rows, up_rows = run_experts(
        second,
        cot_all,
        info,
        w_gate,
        w_up,
        w_down,
        capacity,
        fsdp_count,
    )
    expert_grads = (
        jnp.einsum("erd,erf->edf", expert_rows, gate_rows, preferred_element_type=jnp.float32),
        jnp.einsum("erd,erf->edf", expert_rows, up_rows, preferred_element_type=jnp.float32),
        jnp.einsum("erf,erd->efd", act_rows, cot_rows, preferred_element_type=jnp.float32),
    )

    block_out, input_grad, projected_grads, out_sum, gain_grads = run_backward(
        cotangent[:, 0],
        totals,
        hidden,
        projected,
        contexts,
        in_full,
        out_full,
        tokens[:, 0],
        gains,
        tables,
        fsdp_count,
        kv_heads,
    )
    rows = batch_count * sequence_length
    in_sum, gains_all = run_gradients(
        normed.reshape(rows, -1), projected_grads.reshape(rows, -1), gain_grads, fsdp_count
    )
    gains_sum = jnp.sum(gains_all, axis=(0, 1))
    return (
        block_out[:, None],
        input_grad[:, None],
        gains_sum[0],
        in_sum[:, :query_width],
        in_sum[:, query_width : query_width + kv_width],
        in_sum[:, query_width + kv_width :],
        gains_sum[2, :head_features],
        gains_sum[3, :head_features],
        out_sum,
        gains_sum[1],
        expert_grads[0],
        expert_grads[1],
        expert_grads[2],
    )


def shards(*arrays):
    tokens, routes, w_gate = arrays[0], arrays[13], arrays[10]
    fsdp_count = lax.axis_size(FSDP)
    gathered = fsdp_count * routes.shape[2] * tokens.shape[3] * 2
    fits = gathered <= 24 * MIB and fsdp_count % PLANE == 0 and lax.axis_size(TP) == 2
    if fits and w_gate.shape[0] == 2:
        return gathered_layer(*arrays)
    return exchanged_layer(*arrays)


def solution(mesh):
    in_specs = (
        P(None, "fsdp", "tp", None),
        P(None, "fsdp", "tp", None),
        P(),
        P("fsdp", "tp"),
        P("fsdp", "tp"),
        P("fsdp", "tp"),
        P(),
        P(),
        P("tp", "fsdp"),
        P(),
        P("fsdp", None, "tp"),
        P("fsdp", None, "tp"),
        P("fsdp", "tp", None),
        P(None, "fsdp", None, None),
        P(None, "fsdp", None, None),
    )
    out_specs = (
        P(None, "fsdp", "tp", None),
        P(None, "fsdp", "tp", None),
        P(),
        P("fsdp", "tp"),
        P("fsdp", "tp"),
        P("fsdp", "tp"),
        P(),
        P(),
        P("tp", "fsdp"),
        P(),
        P("fsdp", None, "tp"),
        P("fsdp", None, "tp"),
        P("fsdp", "tp", None),
    )
    return jax.shard_map(shards, mesh=mesh, in_specs=in_specs, out_specs=out_specs, check_vma=False)
```

```python
import functools

import jax
import jax.numpy as jnp
from jax import lax
from jax.experimental import pallas as pl
from jax.experimental.pallas import tpu as pltpu
from jax.sharding import PartitionSpec as P

BLOCK = 256


EPSILON = 1e-06
ROPE_BASE = 1000000.0
MASKED = -1e30
TILE_PICKS = 128


def rms_scale(row_block, gain_row):
    return (
        row_block
        * lax.rsqrt(jnp.mean(row_block * row_block, axis=-1, keepdims=True) + EPSILON)
        * gain_row
    )


def rotary_tables(sequence_length, head_width):
    half_width = head_width // 2
    inverse = ROPE_BASE ** (-2.0 * jnp.arange(half_width, dtype=jnp.float32) / head_width)
    angles = jnp.arange(sequence_length, dtype=jnp.float32)[:, None] * inverse[None, :]
    cosine_table = jnp.concatenate([jnp.cos(angles), jnp.cos(angles)], axis=-1)[:, None, :]
    sine_values = jnp.concatenate([jnp.sin(angles), jnp.sin(angles)], axis=-1)[:, None, :]
    return (cosine_table, sine_values)


def rotate(head_rows, cosine_table, sine_values):
    half_width = head_rows.shape[-1] // 2
    turned = jnp.concatenate([-head_rows[..., half_width:], head_rows[..., :half_width]], axis=-1)
    return head_rows * cosine_table + turned * sine_values


def prepare_heads(projected, gain_row, cosine_table, sine_values):
    return rotate(rms_scale(projected, gain_row), cosine_table, sine_values)


def swiglu(gate_act, up_act):
    return jax.nn.silu(gate_act) * up_act


def slot_tables(route_rows, gate_rows, expert_count, capacity):
    sequence_length = route_rows.shape[0]
    top_count = route_rows.shape[1]
    pick_count = sequence_length * top_count
    tile_count = pick_count // TILE_PICKS
    flat_routes = route_rows.reshape(-1)
    onehot = (flat_routes[:, None] == jnp.arange(expert_count, dtype=jnp.int32)[None, :]).astype(
        jnp.bfloat16
    )
    tiles = onehot.reshape(tile_count, TILE_PICKS, expert_count)
    positions = jnp.arange(TILE_PICKS, dtype=jnp.int32)
    lower = (positions[None, :] < positions[:, None]).astype(jnp.bfloat16)
    within = jnp.einsum("ij,bje->bie", lower, tiles, preferred_element_type=jnp.float32)
    tile_totals = jnp.sum(tiles.astype(jnp.float32), axis=1)
    offsets = jnp.cumsum(tile_totals, axis=0) - tile_totals
    before = within + offsets[:, None, :]
    slot_rank = jnp.sum(before * tiles.astype(jnp.float32), axis=-1).reshape(-1).astype(jnp.int32)
    slot_index = flat_routes * capacity + slot_rank
    pick_ids = jnp.arange(pick_count, dtype=jnp.int32) // top_count
    slot_owner = (
        jnp.full((expert_count * capacity,), sequence_length, jnp.int32)
        .at[slot_index]
        .set(pick_ids)
    )
    slot_weight = (
        jnp.zeros((expert_count * capacity,), jnp.float32).at[slot_index].set(gate_rows.reshape(-1))
    )
    return (slot_index, slot_owner, slot_weight)


def exchanged_layer(
    tokens,
    cotangent,
    norm1_gain,
    w_query,
    key_projection_weight,
    value_projection_weight,
    query_gain,
    key_gain,
    w_out,
    norm2_gain,
    w_gate,
    w_up,
    w_down,
    routes,
    gates,
):
    batch_count = tokens.shape[0]
    model_width = tokens.shape[3]
    sequence_length = routes.shape[2]
    top_count = routes.shape[3]
    head_features = query_gain.shape[0]
    local_experts = w_gate.shape[0]
    fsdp_count = lax.axis_size("fsdp")
    all_experts = local_experts * fsdp_count
    capacity = 7 * top_count * sequence_length // (6 * all_experts)
    query_heads = w_query.shape[1] // head_features
    kv_heads = key_projection_weight.shape[1] // head_features
    group_size = query_heads // kv_heads
    score_scale = head_features ** (-0.5)
    cosine_table, sine_values = rotary_tables(sequence_length, head_features)
    block_ids = jnp.arange(sequence_length, dtype=jnp.int32) // BLOCK
    visible = (block_ids[None, :] <= block_ids[:, None])[None, None]
    first_gain = norm1_gain.astype(jnp.float32)
    second_gain = norm2_gain.astype(jnp.float32)
    query_factor_scale = query_gain.astype(jnp.float32)
    key_scale = key_gain.astype(jnp.float32)
    zero_row = jnp.zeros((1, model_width), jnp.bfloat16)
    buffer_shape = (fsdp_count, local_experts, capacity, model_width)

    def masked_scores(query_fourfold, key_rows):
        raw_scores = (
            jnp.einsum(
                "qcgd,kcd->cgqk", query_fourfold, key_rows, preferred_element_type=jnp.float32
            )
            * score_scale
        )
        return jnp.where(visible, raw_scores, MASKED)

    def prep_heads(projected, gain_row):
        return prepare_heads(projected, gain_row, cosine_table, sine_values)

    gain_sums = (
        jnp.zeros((model_width,), jnp.float32),
        jnp.zeros((model_width,), jnp.float32),
        jnp.zeros((head_features,), jnp.float32),
        jnp.zeros((head_features,), jnp.float32),
    )
    expert_grads = (
        jnp.zeros(w_gate.shape, jnp.float32),
        jnp.zeros(w_up.shape, jnp.float32),
        jnp.zeros(w_down.shape, jnp.float32),
    )
    attn_grads = tuple(
        (
            jnp.zeros(weight_part.shape, jnp.float32)
            for weight_part in (w_query, key_projection_weight, value_projection_weight, w_out)
        )
    )
    outputs = []
    input_grads = []
    for batch_index in range(batch_count):
        query_full, key_full, value_full, out_full = (
            lax.all_gather(w_query, "fsdp", axis=0, tiled=True),
            lax.all_gather(key_projection_weight, "fsdp", axis=0, tiled=True),
            lax.all_gather(value_projection_weight, "fsdp", axis=0, tiled=True),
            lax.all_gather(w_out, "fsdp", axis=1, tiled=True),
        )
        own_rows = tokens[batch_index, 0].astype(jnp.float32)
        own_cot = cotangent[batch_index, 0]
        route_rows = routes[batch_index, 0]
        gate_rows = gates[batch_index, 0]
        first_normed = rms_scale(own_rows, first_gain).astype(jnp.bfloat16)
        normed_all = lax.all_gather(first_normed, "tp", axis=0, tiled=True)
        query_projected = jnp.dot(
            normed_all, query_full, preferred_element_type=jnp.float32
        ).reshape(sequence_length, query_heads, head_features)
        key_projected = jnp.dot(normed_all, key_full, preferred_element_type=jnp.float32).reshape(
            sequence_length, kv_heads, head_features
        )
        value_row_list = (
            jnp.dot(normed_all, value_full, preferred_element_type=jnp.float32)
            .astype(jnp.bfloat16)
            .reshape(sequence_length, kv_heads, head_features)
        )
        query_rot = prep_heads(query_projected, query_factor_scale).astype(jnp.bfloat16)
        key_rot = prep_heads(key_projected, key_scale).astype(jnp.bfloat16)
        query_fourfold = query_rot.reshape(sequence_length, kv_heads, group_size, head_features)
        scores = masked_scores(query_fourfold, key_rot)
        row_max = jnp.max(scores, axis=-1, keepdims=True)
        exp_scores = jnp.exp(scores - row_max)
        totals = jnp.sum(exp_scores, axis=-1, keepdims=True)
        log_total = row_max + jnp.log(totals)
        prob_rows = (exp_scores / totals).astype(jnp.bfloat16)
        context = (
            jnp.einsum(
                "cgqk,kcd->qcgd", prob_rows, value_row_list, preferred_element_type=jnp.float32
            )
            .astype(jnp.bfloat16)
            .reshape(sequence_length, query_heads * head_features)
        )
        attn_own = lax.psum_scatter(
            jnp.dot(context, out_full, preferred_element_type=jnp.float32).astype(jnp.bfloat16),
            "tp",
            scatter_dimension=0,
            tiled=True,
        ).astype(jnp.float32)
        hidden_own = own_rows + attn_own
        second_normed = rms_scale(hidden_own, second_gain).astype(jnp.bfloat16)
        normed_two, cot_all = (
            lax.all_gather(second_normed, "tp", axis=0, tiled=True),
            lax.all_gather(own_cot, "tp", axis=0, tiled=True),
        )
        slot_index, slot_owner, slot_weight = slot_tables(
            route_rows, gate_rows, all_experts, capacity
        )
        padded_rows = jnp.concatenate([normed_two, zero_row], axis=0)
        send_rows = padded_rows[slot_owner].reshape(buffer_shape)
        expert_in = lax.all_to_all(send_rows, "fsdp", split_axis=0, concat_axis=0, tiled=True)
        gate_act = jnp.einsum(
            "sekd,edf->sekf", expert_in, w_gate, preferred_element_type=jnp.float32
        )
        up_act = jnp.einsum("sekd,edf->sekf", expert_in, w_up, preferred_element_type=jnp.float32)
        act_rows = swiglu(gate_act, up_act).astype(jnp.bfloat16)
        expert_out = jnp.einsum(
            "sekf,efd->sekd", act_rows, w_down, preferred_element_type=jnp.float32
        )
        returned = lax.all_to_all(
            expert_out.astype(jnp.bfloat16), "fsdp", split_axis=0, concat_axis=0, tiled=True
        ).astype(expert_out.dtype)
        picked = returned.reshape(all_experts * capacity, model_width)[slot_index].reshape(
            sequence_length, top_count, model_width
        )
        moe_part = jnp.sum(picked * gate_rows[:, :, None], axis=1)
        moe_own = lax.psum_scatter(
            moe_part.astype(jnp.bfloat16), "tp", scatter_dimension=0, tiled=True
        ).astype(jnp.float32)
        outputs.append((hidden_own + moe_own).astype(jnp.bfloat16))
        cot_padded = jnp.concatenate([cot_all, zero_row], axis=0)
        send_grads = (
            (slot_weight[:, None] * cot_padded[slot_owner])
            .astype(jnp.bfloat16)
            .reshape(buffer_shape)
        )
        out_grads = lax.all_to_all(send_grads, "fsdp", split_axis=0, concat_axis=0, tiled=True)
        act_grads = jnp.einsum(
            "sekd,efd->sekf", out_grads, w_down, preferred_element_type=jnp.float32
        )
        _, swiglu_back = jax.vjp(swiglu, gate_act, up_act)
        gate_grads, up_grads = swiglu_back(act_grads)
        gate_grads = gate_grads.astype(jnp.bfloat16)
        up_grads = up_grads.astype(jnp.bfloat16)
        expert_grads = (
            expert_grads[0]
            + jnp.einsum(
                "sekd,sekf->edf", expert_in, gate_grads, preferred_element_type=jnp.float32
            ),
            expert_grads[1]
            + jnp.einsum("sekd,sekf->edf", expert_in, up_grads, preferred_element_type=jnp.float32),
            expert_grads[2]
            + jnp.einsum("sekf,sekd->efd", act_rows, out_grads, preferred_element_type=jnp.float32),
        )
        input_part = jnp.einsum(
            "sekf,edf->sekd", gate_grads, w_gate, preferred_element_type=jnp.float32
        ) + jnp.einsum("sekf,edf->sekd", up_grads, w_up, preferred_element_type=jnp.float32)
        input_back = lax.all_to_all(
            input_part.astype(jnp.bfloat16), "fsdp", split_axis=0, concat_axis=0, tiled=True
        ).astype(input_part.dtype)
        normed_grads = jnp.sum(
            input_back.reshape(all_experts * capacity, model_width)[slot_index].reshape(
                sequence_length, top_count, model_width
            ),
            axis=1,
        )
        normed_own = lax.psum_scatter(
            normed_grads.astype(jnp.bfloat16), "tp", scatter_dimension=0, tiled=True
        ).astype(jnp.float32)
        _, second_back = jax.vjp(rms_scale, hidden_own, second_gain)
        hidden_part, second_gain_grad = second_back(normed_own)
        hidden_grad = own_cot.astype(jnp.float32) + hidden_part
        attn_grad_all = lax.all_gather(hidden_grad.astype(jnp.bfloat16), "tp", axis=0, tiled=True)
        out_weight_grad = jnp.einsum(
            "th,td->hd", context, attn_grad_all, preferred_element_type=jnp.float32
        )
        context_grad = (
            jnp.einsum("td,hd->th", attn_grad_all, out_full, preferred_element_type=jnp.float32)
            .astype(jnp.bfloat16)
            .reshape(sequence_length, kv_heads, group_size, head_features)
        )
        exp_again = jnp.exp(masked_scores(query_fourfold, key_rot) - log_total)
        probs_again = exp_again.astype(jnp.bfloat16)
        prob_grads = jnp.einsum(
            "qcgd,kcd->cgqk", context_grad, value_row_list, preferred_element_type=jnp.float32
        )
        value_grads = (
            jnp.einsum(
                "cgqk,qcgd->kcd", probs_again, context_grad, preferred_element_type=jnp.float32
            )
            .astype(jnp.bfloat16)
            .reshape(sequence_length, kv_heads * head_features)
        )
        score_grads = (
            exp_again * (prob_grads - jnp.sum(exp_again * prob_grads, axis=-1, keepdims=True))
        ).astype(jnp.bfloat16)
        query_rot_grads = (
            jnp.einsum("cgqk,kcd->qcgd", score_grads, key_rot, preferred_element_type=jnp.float32)
            * score_scale
        ).reshape(sequence_length, query_heads, head_features)
        key_rot_grads = (
            jnp.einsum(
                "cgqk,qcgd->kcd", score_grads, query_fourfold, preferred_element_type=jnp.float32
            )
            * score_scale
        )
        _, query_back = jax.vjp(prep_heads, query_projected, query_factor_scale)
        query_proj_grads, query_gain_grad = query_back(query_rot_grads)
        _, key_back = jax.vjp(prep_heads, key_projected, key_scale)
        key_proj_grads, key_gain_grad = key_back(key_rot_grads)
        query_proj_grads = query_proj_grads.astype(jnp.bfloat16).reshape(
            sequence_length, query_heads * head_features
        )
        key_proj_grads = key_proj_grads.astype(jnp.bfloat16).reshape(
            sequence_length, kv_heads * head_features
        )
        first_normed_grads = (
            jnp.einsum(
                "tq,dq->td", query_proj_grads, query_full, preferred_element_type=jnp.float32
            )
            + jnp.einsum("tq,dq->td", key_proj_grads, key_full, preferred_element_type=jnp.float32)
            + jnp.einsum("tq,dq->td", value_grads, value_full, preferred_element_type=jnp.float32)
        )
        weight_parts = (
            jnp.einsum(
                "td,tq->dq", normed_all, query_proj_grads, preferred_element_type=jnp.float32
            ),
            jnp.einsum("td,tq->dq", normed_all, key_proj_grads, preferred_element_type=jnp.float32),
            jnp.einsum("td,tq->dq", normed_all, value_grads, preferred_element_type=jnp.float32),
            out_weight_grad,
        )
        first_own = lax.psum_scatter(
            first_normed_grads.astype(jnp.bfloat16), "tp", scatter_dimension=0, tiled=True
        ).astype(jnp.float32)
        _, first_back = jax.vjp(rms_scale, own_rows, first_gain)
        row_part, first_gain_grad = first_back(first_own)
        input_grads.append((hidden_grad + row_part).astype(jnp.bfloat16))
        gain_sums = (
            gain_sums[0] + first_gain_grad,
            gain_sums[1] + second_gain_grad,
            gain_sums[2] + query_gain_grad,
            gain_sums[3] + key_gain_grad,
        )
        attn_grads = jax.tree.map(
            jnp.add,
            attn_grads,
            (
                lax.psum_scatter(weight_parts[0], "fsdp", scatter_dimension=0, tiled=True),
                lax.psum_scatter(weight_parts[1], "fsdp", scatter_dimension=0, tiled=True),
                lax.psum_scatter(weight_parts[2], "fsdp", scatter_dimension=0, tiled=True),
                lax.psum_scatter(weight_parts[3], "fsdp", scatter_dimension=1, tiled=True),
            ),
        )
    summed = lax.psum((gain_sums[0], gain_sums[1], gain_sums[2], gain_sums[3]), ("fsdp", "tp"))
    block_out = jnp.stack(outputs)[:, None]
    input_grad = jnp.stack(input_grads)[:, None]
    return (
        block_out,
        input_grad,
        summed[0],
        attn_grads[0],
        attn_grads[1],
        attn_grads[2],
        summed[2],
        summed[3],
        attn_grads[3],
        summed[1],
        expert_grads[0],
        expert_grads[1],
        expert_grads[2],
    )


MESH = pl.DeviceIdType.MESH
FSDP, TP = "fsdp", "tp"
PLANE = 4
LANES = 128
MIB = 1 << 20
RIGHT, LEFT, FIRST, SECOND, CORE, CROSS = range(6)
TRANSPOSED_LEFT = (((0,), (0,)), ((), ()))
TRANSPOSED_RIGHT = (((1,), (1,)), ((), ()))
OUTPUT, BACK = range(2)
CHUNK = 512


class Spot:
    def __init__(self, line, wide):
        self.line = line
        self.wide = wide
        self.planes = 4 if wide else 2
        index = lax.axis_index(FSDP)
        self.x = lax.axis_index(TP)
        self.z = lax.div(index, PLANE)
        self.y = lax.rem(lax.div(index, 2), 2)
        self.core = lax.rem(index, 2)

    def side(self, core, first, second):
        flip_y, flip_x = first, second
        if self.wide:
            flip_y = (1 - core) * first + core * second
            flip_x = core * first + (1 - core) * second
        return self.y + flip_y * (1 - 2 * self.y), self.x + flip_x * (1 - 2 * self.x)

    def block(self, core, first, second, z):
        y, x = self.side(core, first, second)
        return z * PLANE + y * 2 + core, x

    def device(self, kind):
        if kind == RIGHT:
            return self.block(self.core, 0, 0, self.z + 1)
        if kind == LEFT:
            return self.block(self.core, 0, 0, self.z - 1)
        if kind == CORE:
            return self.block(1 - self.core, 0, 0, self.z)
        if kind == CROSS:
            return self.block(self.core, 0, 0, self.z)[0], 1 - self.x
        return self.block(self.core, int(kind == FIRST), int(kind == SECOND), self.z)

    def kinds(self):
        return (FIRST, SECOND, CORE) if self.wide else (FIRST, CORE)

    def number(self, first, second, z):
        return (second * 2 + first) * self.line + z

    def order(self, step):
        if isinstance(step, int) and step == 0:
            return [(self.z, None)]
        return [(self.z - step, self.z - step >= 0), (self.z + step, self.z + step < self.line)]

    def greet(self):
        barrier = pltpu.get_barrier_semaphore()

        def signal(kind):
            pl.semaphore_signal(barrier, inc=1, device_id=self.device(kind), device_id_type=MESH)

        for kind in self.kinds():
            signal(kind)
        when(self.z + 1 < self.line, lambda: signal(RIGHT))
        when(self.z > 0, lambda: signal(LEFT))
        around = (self.z + 1 < self.line).astype(jnp.int32) + (self.z > 0).astype(jnp.int32)
        pl.semaphore_wait(barrier, len(self.kinds()) + around)

    def send(self, source, target, send_sem, receive_sem, kind):
        return pltpu.make_async_remote_copy(
            src_ref=source,
            dst_ref=target,
            send_sem=send_sem,
            recv_sem=receive_sem,
            device_id=self.device(kind),
            device_id_type=MESH,
        )


def when(condition, action):
    def run():
        action()

    if condition is None:
        run()
    else:
        pl.when(condition)(run)


class Spread:
    def __init__(self, spot, source, slot, send, receive, local):
        self.spot = spot
        self.slot = slot
        self.source = source
        self.sends = send
        self.receives = receive
        self.mine = pltpu.make_async_copy(source, slot(*spot.block(spot.core, 0, 0, spot.z)), local)

    def copy(self, first, second, z, kind, own=False):
        spot = self.spot
        place = self.slot(*spot.block(spot.core, first, second, z))
        number = spot.number(first, second, z)
        arrival = {
            RIGHT: number,
            LEFT: number,
            FIRST: spot.number(1, 0, z),
            SECOND: spot.number(first, 1, z),
            CORE: spot.planes * spot.line + number,
        }[kind]
        departure = {RIGHT: 0, LEFT: 1, FIRST: 2, SECOND: 3, CORE: 5}[kind] * spot.line + number
        source = self.source if own else place
        return spot.send(source, place, self.sends.at[departure], self.receives.at[arrival], kind)

    def arrived(self, first, second, z, other=False):
        spot = self.spot
        core = 1 - spot.core if other else spot.core
        place = self.slot(*spot.block(core, first, second, z))
        number = spot.number(first, second, z) + (spot.planes * spot.line if other else 0)
        spot.send(place, place, self.sends.at[0], self.receives.at[number], CORE).wait_recv()

    def steps(self):
        return self.spot.line + (3 if self.spot.wide else 1)

    def begin(self):
        spot = self.spot
        z = spot.z
        when(z + 1 < spot.line, lambda: self.copy(0, 0, z, RIGHT, True).start())
        when(z > 0, lambda: self.copy(0, 0, z, LEFT, True).start())
        for kind in spot.kinds():
            self.copy(0, 0, z, kind, True).start()
        self.mine.start()

    def step(self, step):
        spot = self.spot
        line, z = spot.line, spot.z

        def reached(away, action):
            inside = jnp.logical_and(away >= 0, away < line)
            when(jnp.logical_and(inside, z - away >= 0), lambda: action(z - away, True))
            when(
                jnp.logical_and(inside, jnp.logical_and(away > 0, z + away < line)),
                lambda: action(z + away, False),
            )

        def along(zz, from_left):
            self.arrived(0, 0, zz)
            if from_left:
                when(z + 1 < line, lambda: self.copy(0, 0, zz, RIGHT).start())
            else:
                when(z > 0, lambda: self.copy(0, 0, zz, LEFT).start())
            for kind in spot.kinds():
                self.copy(0, 0, zz, kind).start()

        def firsts(zz, _):
            self.arrived(1, 0, zz)
            if spot.wide:
                self.copy(1, 0, zz, SECOND).start()
            self.copy(1, 0, zz, CORE).start()

        def lasts(first):
            def action(zz, _):
                self.arrived(first, 1, zz)
                self.copy(first, 1, zz, CORE).start()

            return action

        step = jnp.asarray(step, jnp.int32)
        reached(step, along)
        reached(step - 1, firsts)
        if spot.wide:
            reached(step - 2, lasts(0))
            reached(step - 3, lasts(1))

    def finish(self):
        spot = self.spot
        z = spot.z

        def body(zz, _):
            when(
                jnp.logical_and(z + 1 < spot.line, zz <= z),
                lambda: self.copy(0, 0, zz, RIGHT).wait_send(),
            )
            when(jnp.logical_and(z > 0, zz >= z), lambda: self.copy(0, 0, zz, LEFT).wait_send())
            self.copy(0, 0, zz, FIRST).wait_send()
            for second in range(2 if spot.wide else 1):
                for first in (0, 1):
                    if spot.wide and not second:
                        self.copy(first, 0, zz, SECOND).wait_send()
                    self.copy(first, second, zz, CORE).wait_send()
                    self.arrived(first, second, zz, other=True)
            return 0

        lax.fori_loop(0, spot.line, body, 0)
        self.mine.wait()


def run_trees(trees):
    for tree in trees:
        tree.begin()

    def body(step, _):
        for tree in trees:
            tree.step(step)
        return 0

    lax.fori_loop(1, max(tree.steps() for tree in trees), body, 0)
    for tree in trees:
        tree.finish()


def spread_count(line, wide):
    return (9 if wide else 7) * line, (8 if wide else 4) * line


def rows_at(ref, index, size):
    return ref.at[pl.ds(pl.multiple_of(index * size, 16), size)]


def columns_at(ref, index, size):
    return ref.at[:, pl.ds(pl.multiple_of(index * size, LANES), size)]


def norm_rows(target, source, gain):
    def body(step, _):
        rows = pl.ds(pl.multiple_of(step * 16, 16), 16)
        value = source[rows, :].astype(jnp.float32)
        target[rows, :] = rms_scale(value, gain[...]).astype(target.dtype)
        return 0

    lax.fori_loop(0, target.shape[0] // 16, body, 0)


def turned_heads(value, gain, cosine, sine):
    normed = rms_scale(value, gain)
    return normed * cosine + pltpu.roll(normed, normed.shape[-1] // 2, 1) * sine


def visible_blocks(length, group):
    blocks = []
    for start in range(0, length, BLOCK):
        stop = min(start + BLOCK, length)
        heads = max(1, BLOCK // (stop - start))
        while group % heads:
            heads -= 1
        blocks.append((start, stop, stop, heads))
    return blocks


def softmax(scores):
    raised = jnp.exp(scores - jnp.max(scores, axis=-1, keepdims=True))
    return raised * (1.0 / jnp.sum(raised, axis=-1, keepdims=True))


def for_heads(low, high, heads, body):
    turns = 2 if heads == 1 and (high - low) % 2 == 0 else 1

    def turn(step, _):
        for i in range(turns):
            body(low + (step * turns + i) * heads)
        return 0

    count = (high - low) // (heads * turns)
    if count == 1:
        turn(0, 0)
    else:
        lax.fori_loop(0, count, turn, 0)


def head_columns(head, features):
    return pl.ds(pl.multiple_of(head * features, LANES), features)


def forward_kernel(
    line,
    heads,
    kv_heads,
    tokens_ref,
    cot_ref,
    in_ref,
    out_ref,
    picks_ref,
    gain1_ref,
    gain2_ref,
    query_gain_ref,
    key_gain_ref,
    cosine_ref,
    sine_ref,
    cot_all,
    in_all,
    out_all,
    picks_all,
    normed_all,
    projected_all,
    context_all,
    hidden_all,
    second_all,
    in_w,
    out_w,
    tokens,
    normed,
    projected,
    context,
    queries,
    keys,
    values,
    mixed,
    mixed_other,
    hidden,
    second,
    narrow_send,
    narrow_receive,
    wide_send,
    wide_receive,
    local,
    token_send,
    token_receive,
    mixed_send,
    mixed_receive,
    save_sem,
):
    batch, half, width = tokens_ref.shape
    length = 2 * half
    depth, out_width = in_ref.shape[0], out_ref.shape[1]
    features = query_gain_ref.shape[1]
    narrow = Spot(line, False)
    spot = Spot(line, True)
    x = spot.x
    spot.greet()
    slots = [
        (picks_ref, lambda block, side: picks_all.at[block]),
        (in_ref, lambda block, side: rows_at(in_w, block, depth)),
        (out_ref, lambda block, side: columns_at(out_w, block, out_width)),
    ]
    weights = [
        Spread(narrow, source, slot, narrow_send.at[i], narrow_receive.at[i], local.at[i])
        for i, (source, slot) in enumerate(slots)
    ]
    cots = [
        Spread(
            spot,
            cot_ref.at[i],
            lambda block, side, i=i: rows_at(cot_all.at[i, block], side, half),
            wide_send.at[i],
            wide_receive.at[i],
            local.at[3 + i],
        )
        for i in range(batch)
    ]
    for tree in weights:
        tree.begin()

    def token_copies(i):
        place = rows_at(tokens.at[i], x, half)
        return (
            pltpu.make_async_copy(tokens_ref.at[i], place, local.at[3 + batch + i]),
            spot.send(tokens_ref.at[i], place, token_send.at[i], token_receive.at[i], CROSS),
        )

    for i in range(batch):
        for copy in token_copies(i):
            copy.start()
    def steps(step, _):
        for tree in weights:
            tree.step(step)
        return 0

    lax.fori_loop(1, weights[0].steps(), steps, 0)
    for i in range(batch):
        mine, other = token_copies(i)
        mine.wait()
        other.wait_send()
        place = rows_at(tokens.at[i], 1 - x, half)
        spot.send(place, place, token_send.at[i], token_receive.at[i], CROSS).wait_recv()
    for i in range(batch):
        norm_rows(normed.at[i], tokens.at[i], gain1_ref)
    for tree in cots:
        tree.begin()
    for tree in weights:
        tree.finish()

    def save(source, target, index):
        return pltpu.make_async_copy(source, target, save_sem.at[index])

    saves = [save(in_w, in_all, 0), save(out_w, out_all, 1)]
    for copy in saves:
        copy.start()

    def project(i, start, stop):
        for at in range(start, stop, CHUNK):
            projected[i, :, at : at + CHUNK] = jnp.dot(
                normed[i], in_w[:, at : at + CHUNK], preferred_element_type=jnp.float32
            )

    scale = features ** (-0.5)

    group = heads // kv_heads

    def prepare_keys(i):
        base = heads * features
        for head in range(kv_heads):
            at = base + head * features
            keys[head] = turned_heads(
                projected[i, :, at : at + features],
                key_gain_ref[...],
                cosine_ref[...],
                sine_ref[...],
            ).astype(jnp.bfloat16)
            at = base + (kv_heads + head) * features
            values[head] = projected[i, :, at : at + features].astype(jnp.bfloat16)

    def prepare_queries(i, shared):
        def prepare(member):
            columns = head_columns(shared * group + member, features)
            queries[member] = turned_heads(
                projected[i, :, columns], query_gain_ref[...], cosine_ref[...], sine_ref[...]
            ).astype(jnp.bfloat16)

        for_heads(0, group, 1, prepare)

    def attend(i, shared, start, stop, seen, at_once, low, high):
        count = stop - start

        def block(member):
            query = queries[pl.ds(member, at_once), start:stop, :].reshape(-1, features)
            scores = lax.dot_general(
                query,
                keys[shared, :seen, :],
                TRANSPOSED_RIGHT,
                preferred_element_type=jnp.float32,
            )
            rows = jnp.dot(
                softmax(scores * scale).astype(jnp.bfloat16),
                values[shared, :seen, :],
                preferred_element_type=jnp.float32,
            ).astype(jnp.bfloat16)
            for j in range(at_once):
                columns = head_columns(shared * group + member + j, features)
                context[i, start:stop, columns] = rows[j * count : (j + 1) * count]

        for_heads(low, high, at_once, block)

    def mixed_copy(i):
        return spot.send(
            rows_at(mixed.at[i], 1 - x, half),
            mixed_other.at[i],
            mixed_send.at[i],
            mixed_receive.at[i],
            CROSS,
        )

    def mix(i, start, stop):
        for at in range(start, stop, CHUNK):
            mixed[i, :, at : at + CHUNK] = jnp.dot(
                context[i], out_w[:, at : at + CHUNK], preferred_element_type=jnp.float32
            ).astype(jnp.bfloat16)
        if stop == width:
            mixed_copy(i).start()

    def close(i):
        mixed_copy(i).wait()
        add_rows(
            hidden.at[i],
            [rows_at(tokens.at[i], x, half), rows_at(mixed.at[i], x, half), mixed_other.at[i]],
        )
        norm_rows(second.at[i], hidden.at[i], gain2_ref)

    pending = []
    in_width = in_w.shape[1]
    parts = lambda size: [(at, min(at + 2 * CHUNK, size)) for at in range(0, size, 2 * CHUNK)]
    for i in range(batch):
        pending += [functools.partial(project, i, *part) for part in parts(in_width)]
        pending.append(functools.partial(prepare_keys, i))
        for shared in range(kv_heads):
            pending.append(functools.partial(prepare_queries, i, shared))
            for start, stop, seen, at_once in visible_blocks(length, group):
                share = max(at_once, group // 2)
                for low in range(0, group, share):
                    pending.append(
                        functools.partial(
                            attend, i, shared, start, stop, seen, at_once, low, low + share
                        )
                    )
        pending += [functools.partial(mix, i, *part) for part in parts(width)]
    pending += [functools.partial(close, i) for i in range(batch)]
    later = [
        functools.partial(tree.step, step) for step in range(1, cots[0].steps()) for tree in cots
    ]
    while pending or later:
        for _ in range(2):
            if pending:
                pending.pop(0)()
        if later:
            later.pop(0)()

    saves += [
        save(source, target, 2 + i)
        for i, (source, target) in enumerate(
            [
                (normed, normed_all),
                (projected, projected_all),
                (context, context_all),
                (hidden, hidden_all),
                (second, second_all),
            ]
        )
    ]
    for copy in saves[2:]:
        copy.start()
    for tree in cots:
        tree.finish()
    for copy in saves:
        copy.wait()


def run_forward(tokens, cot, weight_in, weight_out, picks, gains, tables, fsdp_count, kv_heads):
    line = fsdp_count // PLANE
    batch, half, width = tokens.shape
    length = 2 * half
    features = gains[2].shape[1]
    heads = weight_out.shape[0] // features
    in_shape = (weight_in.shape[0] * fsdp_count, weight_in.shape[1])
    out_shape = (weight_out.shape[0], weight_out.shape[1] * fsdp_count)
    wide, narrow = spread_count(line, True), spread_count(line, False)
    anywhere = pl.BlockSpec(memory_space=pl.ANY)
    inside = pl.BlockSpec(memory_space=pltpu.VMEM)
    shape = lambda dims, kind=jnp.bfloat16: jax.ShapeDtypeStruct(dims, kind)
    vmem = lambda *dims: pltpu.VMEM(dims, jnp.bfloat16)
    sem = lambda *dims: pltpu.SemaphoreType.DMA(dims)
    kept = (
        ((batch, length, width), jnp.bfloat16),
        ((batch, length, weight_in.shape[1]), jnp.float32),
        ((batch, length, heads * features), jnp.bfloat16),
        ((batch, half, width), jnp.float32),
        ((batch, half, width), jnp.bfloat16),
    )
    return pl.pallas_call(
        functools.partial(forward_kernel, line, heads, kv_heads),
        out_shape=(
            shape((batch, fsdp_count, length, width)),
            shape(in_shape),
            shape(out_shape),
            shape((fsdp_count, *picks.shape), picks.dtype),
            *(shape(*one) for one in kept),
        ),
        in_specs=[anywhere] * 5 + [inside] * 6,
        out_specs=(anywhere,) * 9,
        scratch_shapes=[
            vmem(*in_shape),
            vmem(*out_shape),
            vmem(batch, length, width),
            *(pltpu.VMEM(*one) for one in kept[:3]),
            vmem(heads // kv_heads, length, features),
            vmem(kv_heads, length, features),
            vmem(kv_heads, length, features),
            vmem(batch, length, width),
            vmem(batch, half, width),
            *(pltpu.VMEM(*one) for one in kept[3:]),
            sem(3, narrow[0]),
            sem(3, narrow[1]),
            sem(batch, wide[0]),
            sem(batch, wide[1]),
            sem(3 + 2 * batch),
            sem(batch),
            sem(batch),
            sem(batch),
            sem(batch),
            sem(7),
        ],
        compiler_params=pltpu.CompilerParams(
            collective_id=1, has_side_effects=True, vmem_limit_bytes=60 * MIB
        ),
    )(tokens, cot, weight_in, weight_out, picks, *gains, *tables)


def add_rows(target, sources):
    def body(step, _):
        rows = pl.ds(pl.multiple_of(step * 16, 16), 16)
        total = sources[0][rows, :].astype(jnp.float32)
        for source in sources[1:]:
            total = total + source[rows, :].astype(jnp.float32)
        target[rows, :] = total.astype(target.dtype)
        return 0

    lax.fori_loop(0, target.shape[0] // 16, body, 0)


class Collect:
    def __init__(self, spot, part, total, cores, firsts, rights, lefts, send, receive):
        self.spot = spot
        self.part = part
        self.total = total
        self.places = {CORE: cores, FIRST: firsts, RIGHT: rights, LEFT: lefts}
        line = spot.line
        self.base = {CORE: 0, FIRST: 2 * line, RIGHT: 3 * line, LEFT: 4 * line}
        self.sends = send
        self.receives = receive

    def own(self, first, z):
        return self.part(*self.spot.block(self.spot.core, first, 0, z))

    def copy(self, kind, first, z):
        spot = self.spot
        number = first * spot.line + z if kind == CORE else z
        source = self.part(*spot.block(1 - spot.core, first, 0, z)) if kind == CORE else self.own(first, z)
        at = self.base[kind] + number
        return spot.send(
            source, self.places[kind].at[number], self.sends.at[at], self.receives.at[at], kind
        )

    def arrived(self, kind, number):
        place = self.places[kind].at[number]
        at = self.base[kind] + number
        self.spot.send(place, place, self.sends.at[0], self.receives.at[at], CORE).wait_recv()
        return place

    def begin(self, z):
        for first in (1, 0):
            self.copy(CORE, first, z).start()

    def to_first(self, z):
        add_rows(self.own(1, z), [self.own(1, z), self.arrived(CORE, self.spot.line + z)])
        self.copy(FIRST, 1, z).start()

    def summands(self, z):
        return [self.own(0, z), self.arrived(CORE, z), self.arrived(FIRST, z)]

    def onward(self, kind, zz):
        spot = self.spot
        sources = self.summands(zz)
        target = self.own(0, zz)
        behind = spot.z > 0 if kind == RIGHT else spot.z + 1 < spot.line
        when(behind, lambda: add_rows(target, sources + [self.arrived(kind, zz)]))
        when(jnp.logical_not(behind), lambda: add_rows(target, sources))
        self.copy(kind, 0, zz).start()

    def last(self):
        z, line = self.spot.z, self.spot.line
        sources = self.summands(z)

        def end(kinds):
            add_rows(self.total, sources + [self.arrived(kind, z) for kind in kinds])

        when(z == 0, lambda: end([LEFT]))
        when(z == line - 1, lambda: end([RIGHT]))
        when(jnp.logical_and(z > 0, z < line - 1), lambda: end([RIGHT, LEFT]))

    def finish(self):
        spot = self.spot
        for zz in range(spot.line):
            for first in (0, 1):
                self.copy(CORE, first, zz).wait_send()
            self.copy(FIRST, 1, zz).wait_send()
            when(zz > spot.z, lambda: self.copy(RIGHT, 0, zz).wait_send())
            when(zz < spot.z, lambda: self.copy(LEFT, 0, zz).wait_send())

    def tasks(self):
        spot = self.spot
        work = []
        for step in reversed(range(spot.line)):
            for zz, valid in spot.order(step):
                work.append(functools.partial(when, valid, functools.partial(self.to_first, zz)))
        for step in reversed(range(1, spot.line)):
            for kind, (zz, valid) in zip((LEFT, RIGHT), spot.order(step)):
                action = functools.partial(self.onward, kind, zz)
                work.append(functools.partial(when, valid, action))
        return work + [self.last, self.finish]


def collect_scratch(line, shape):
    counts = (2 * line, line, line, line)
    return [pltpu.VMEM((count, *shape), jnp.bfloat16) for count in counts] + [
        pltpu.SemaphoreType.DMA((5 * line,)),
        pltpu.SemaphoreType.DMA((5 * line,)),
    ]


def norm_back(value, grads, gain):
    scale = lax.rsqrt(jnp.mean(value * value, axis=-1, keepdims=True) + EPSILON)
    unit = value * scale
    scaled = grads * gain
    back = scale * (scaled - unit * jnp.mean(scaled * unit, axis=-1, keepdims=True))
    return back, grads * unit


def backward_kernel(
    line,
    heads,
    kv_heads,
    cot_ref,
    totals_ref,
    hidden_ref,
    projected_ref,
    context_ref,
    in_ref,
    out_ref,
    tokens_ref,
    gain1_ref,
    gain2_ref,
    query_gain_ref,
    key_gain_ref,
    cosine_ref,
    sine_ref,
    block_out,
    input_grad,
    grads_all,
    out_total,
    gain_grads,
    elements,
    cots,
    tokens,
    kept,
    result,
    context,
    hidden_grads,
    context_grads,
    grads,
    normed_grads,
    normed_other,
    out_rows,
    in_rows,
    queries_f,
    shared_f,
    queries,
    query_grads,
    sums,
    out_grads,
    cores,
    firsts,
    rights,
    lefts,
    tree_send,
    tree_receive,
    load_sem,
    row_sem,
    head_sem,
    save_sem,
    hidden_send,
    hidden_receive,
    normed_send,
    normed_receive,
):
    batch, half, width = cot_ref.shape
    length = 2 * half
    features = query_gain_ref.shape[1]
    group = heads // kv_heads
    base = heads * features
    out_width = out_total.shape[1]
    narrow, spot = Spot(line, False), Spot(line, True)
    x = spot.x
    scale = features ** (-0.5)

    def load(source, target, index):
        return pltpu.make_async_copy(source, target, load_sem.at[index])

    def element_loads(i):
        return [
            load(hidden_ref.at[i], elements.at[0], 0),
            load(totals_ref.at[i, OUTPUT], elements.at[1], 1),
            load(totals_ref.at[i, BACK], elements.at[2], 2),
        ]

    first_loads = [load(cot_ref, cots, 3), load(tokens_ref, tokens, 4)] + [
        load(context_ref.at[i], rows_at(context, i, length), 5 + i) for i in range(batch)
    ]
    for copy in element_loads(0) + first_loads:
        copy.start()

    def out_load(step):
        slot = lax.rem(step, 2)
        return pltpu.make_async_copy(
            rows_at(out_ref, step, CHUNK), out_rows.at[slot], row_sem.at[0, slot]
        )

    def in_load(step):
        slot = lax.rem(step, 2)
        return pltpu.make_async_copy(
            rows_at(in_ref, step, CHUNK), in_rows.at[slot], row_sem.at[1, slot]
        )

    out_steps, in_steps = out_ref.shape[0] // CHUNK, in_ref.shape[0] // CHUNK
    for step in range(2):
        out_load(step).start()
        in_load(step).start()
    gain_grads[...] = jnp.zeros_like(gain_grads)
    spot.greet()
    for copy in first_loads:
        copy.wait()

    def result_save(i, target):
        return pltpu.make_async_copy(result.at[i], target.at[i], save_sem.at[i])

    def half_copy(ref, i, side):
        return ref.at[pl.ds(pl.multiple_of(i * length + side * half, 16), half)]

    def hidden_copy(i):
        place = half_copy(hidden_grads, i, x)
        return spot.send(place, place, hidden_send.at[i], hidden_receive.at[i], CROSS)

    for i in range(batch):
        for copy in element_loads(i):
            copy.wait()

        def elementwise(step, _):
            rows = pl.ds(pl.multiple_of(step * 16, 16), 16)
            value = elements[0, rows, :]
            result[i, rows, :] = (value + elements[1, rows, :]).astype(jnp.bfloat16)
            back, gain_rows = norm_back(value, elements[2, rows, :], gain2_ref[...])
            gain_grads[1:2, :] += jnp.sum(gain_rows, axis=0, keepdims=True)
            total = cots[i, rows, :].astype(jnp.float32) + back
            kept[i, rows, :] = total
            place = pl.ds(pl.multiple_of(i * length + x * half + step * 16, 16), 16)
            hidden_grads[place, :] = total.astype(jnp.bfloat16)
            return 0

        lax.fori_loop(0, half // 16, elementwise, 0)
        hidden_copy(i).start()
        result_save(i, block_out).start()
        if i + 1 < batch:
            for copy in element_loads(i + 1):
                copy.start()
    for i in range(batch):
        hidden_copy(i).wait_send()
        place = half_copy(hidden_grads, i, 1 - x)
        spot.send(place, place, hidden_send.at[i], hidden_receive.at[i], CROSS).wait_recv()

    def context_step(step, _):
        out_load(step).wait()
        columns = pl.ds(pl.multiple_of(step * CHUNK, LANES), CHUNK)
        context_grads[:, columns] = lax.dot_general(
            hidden_grads[...],
            out_rows[lax.rem(step, 2)],
            TRANSPOSED_RIGHT,
            preferred_element_type=jnp.float32,
        ).astype(jnp.bfloat16)
        when(step + 2 < out_steps, lambda: out_load(step + 2).start())
        for start in range(0, width, CHUNK):
            out_grads[pl.ds(pl.multiple_of(step * CHUNK, 16), CHUNK), start : start + CHUNK] = (
                lax.dot_general(
                    context[:, columns],
                    hidden_grads[:, start : start + CHUNK],
                    TRANSPOSED_LEFT,
                    preferred_element_type=jnp.float32,
                ).astype(jnp.bfloat16)
            )
        return 0

    lax.fori_loop(0, out_steps, context_step, 0)
    tree = Collect(
        narrow,
        lambda block, side: columns_at(out_grads, block, out_width),
        out_total,
        cores,
        firsts,
        rights,
        lefts,
        tree_send,
        tree_receive,
    )
    for z in range(line):
        tree.begin(z)
    work = tree.tasks()

    def turns():
        return [(i, shared) for i in range(batch) for shared in range(kv_heads)]

    def head_loads(index):
        i, shared = turns()[index]
        slot = index % 2
        return [
            pltpu.make_async_copy(
                projected_ref.at[i, :, pl.ds(shared * group * features, group * features)],
                queries_f.at[slot],
                head_sem.at[slot, 0],
            )
        ] + [
            pltpu.make_async_copy(
                projected_ref.at[i, :, pl.ds(base + (shared + j * kv_heads) * features, features)],
                shared_f.at[slot, j],
                head_sem.at[slot, 1 + j],
            )
            for j in range(2)
        ]

    for copy in head_loads(0):
        copy.start()

    def turn_back(grads_in):
        return grads_in * cosine_ref[...] + pltpu.roll(
            grads_in * sine_ref[...], features // 2, 1
        )

    def attend(index):
        i, shared = turns()[index]
        slot = index % 2
        for copy in head_loads(index):
            copy.wait()
        if index + 1 < len(turns()):
            for copy in head_loads(index + 1):
                copy.start()
        top = i * length
        key = turned_heads(
            shared_f[slot, 0], key_gain_ref[...], cosine_ref[...], sine_ref[...]
        ).astype(jnp.bfloat16)
        queries[group] = key
        queries[group + 1] = shared_f[slot, 1].astype(jnp.bfloat16)
        sums[...] = jnp.zeros_like(sums)

        def columns_of(member):
            return pl.ds(pl.multiple_of(member * features, LANES), features)

        def prepare(member):
            queries[member] = turned_heads(
                queries_f[slot, :, columns_of(member)],
                query_gain_ref[...],
                cosine_ref[...],
                sine_ref[...],
            ).astype(jnp.bfloat16)

        for_heads(0, group, 1, prepare)
        for start, stop, seen, at_once in visible_blocks(length, group):
            count = stop - start

            def block(member):
                query = queries[pl.ds(member, at_once), start:stop, :].reshape(-1, features)
                keys, values = queries[group, :seen, :], queries[group + 1, :seen, :]
                out_grad = jnp.concatenate(
                    [
                        context_grads[
                            top + start : top + stop,
                            head_columns(shared * group + member + j, features),
                        ]
                        for j in range(at_once)
                    ],
                    axis=0,
                )
                scores = lax.dot_general(
                    query, keys, TRANSPOSED_RIGHT, preferred_element_type=jnp.float32
                )
                shares = softmax(scores * scale)
                share_grads = lax.dot_general(
                    out_grad, values, TRANSPOSED_RIGHT, preferred_element_type=jnp.float32
                )
                sums[1, :seen, :] += lax.dot_general(
                    shares.astype(jnp.bfloat16),
                    out_grad,
                    TRANSPOSED_LEFT,
                    preferred_element_type=jnp.float32,
                )
                inner = jnp.sum(shares * share_grads, axis=-1, keepdims=True)
                score_grads = (shares * (share_grads - inner)).astype(jnp.bfloat16)
                rows = scale * jnp.dot(score_grads, keys, preferred_element_type=jnp.float32)
                query_grads[pl.ds(member, at_once), start:stop, :] = rows.reshape(
                    at_once, count, features
                )
                sums[0, :seen, :] += lax.dot_general(
                    score_grads, query, TRANSPOSED_LEFT, preferred_element_type=jnp.float32
                )

            for_heads(0, group, at_once, block)

        def finish(member):
            back, gain_rows = norm_back(
                queries_f[slot, :, columns_of(member)],
                turn_back(query_grads[member]),
                query_gain_ref[...],
            )
            gain_grads[2:3, :features] += jnp.sum(gain_rows, axis=0, keepdims=True)
            grads[top : top + length, head_columns(shared * group + member, features)] = (
                back.astype(jnp.bfloat16)
            )

        for_heads(0, group, 1, finish)
        back, gain_rows = norm_back(
            shared_f[slot, 0], turn_back(sums[0] * scale), key_gain_ref[...]
        )
        gain_grads[3:4, :features] += jnp.sum(gain_rows, axis=0, keepdims=True)
        at = base + shared * features
        grads[top : top + length, at : at + features] = back.astype(jnp.bfloat16)
        at += kv_heads * features
        grads[top : top + length, at : at + features] = sums[1].astype(jnp.bfloat16)

    for index in range(len(turns())):
        attend(index)
        for _ in range(4):
            if work:
                work.pop(0)()

    saves = [
        pltpu.make_async_copy(rows_at(grads, i, length), grads_all.at[i], save_sem.at[batch + i])
        for i in range(batch)
    ]
    for copy in saves:
        copy.start()

    def normed_step(step, _):
        in_load(step).wait()
        columns = pl.ds(pl.multiple_of(step * CHUNK, LANES), CHUNK)
        normed_grads[:, columns] = lax.dot_general(
            grads[...],
            in_rows[lax.rem(step, 2)],
            TRANSPOSED_RIGHT,
            preferred_element_type=jnp.float32,
        ).astype(jnp.bfloat16)
        when(step + 2 < in_steps, lambda: in_load(step + 2).start())
        return 0

    lax.fori_loop(0, in_steps, normed_step, 0)

    def normed_copy(i):
        return spot.send(
            half_copy(normed_grads, i, 1 - x),
            normed_other.at[i],
            normed_send.at[i],
            normed_receive.at[i],
            CROSS,
        )

    for i in range(batch):
        normed_copy(i).start()
    while work:
        work.pop(0)()
    for i in range(batch):
        normed_copy(i).wait()
        result_save(i, block_out).wait()

        def input_rows(step, _):
            rows = pl.ds(pl.multiple_of(step * 16, 16), 16)
            place = pl.ds(pl.multiple_of(i * length + x * half + step * 16, 16), 16)
            total = normed_grads[place, :].astype(jnp.float32) + normed_other[i, rows, :].astype(
                jnp.float32
            )
            back, gain_rows = norm_back(
                tokens[i, rows, :].astype(jnp.float32), total, gain1_ref[...]
            )
            gain_grads[0:1, :] += jnp.sum(gain_rows, axis=0, keepdims=True)
            result[i, rows, :] = (kept[i, rows, :] + back).astype(jnp.bfloat16)
            return 0

        lax.fori_loop(0, half // 16, input_rows, 0)
        result_save(i, input_grad).start()
    for i in range(batch):
        result_save(i, input_grad).wait()
    for copy in saves:
        copy.wait()


def run_backward(
    cot, totals, hidden, projected, context, in_full, out_full, tokens, gains, tables, fsdp_count, kv_heads
):
    line = fsdp_count // PLANE
    batch, half, width = tokens.shape
    length = 2 * half
    features = gains[2].shape[1]
    heads = out_full.shape[0] // features
    group = heads // kv_heads
    in_width, out_depth = in_full.shape[1], out_full.shape[0]
    out_shape = (out_depth, width // fsdp_count)
    anywhere = pl.BlockSpec(memory_space=pl.ANY)
    inside = pl.BlockSpec(memory_space=pltpu.VMEM)
    vmem = lambda *dims: pltpu.VMEM(dims, jnp.bfloat16)
    wide = lambda *dims: pltpu.VMEM(dims, jnp.float32)
    sem = lambda *dims: pltpu.SemaphoreType.DMA(dims)
    rows = batch * length
    return pl.pallas_call(
        functools.partial(backward_kernel, line, heads, kv_heads),
        out_shape=(
            jax.ShapeDtypeStruct((batch, half, width), jnp.bfloat16),
            jax.ShapeDtypeStruct((batch, half, width), jnp.bfloat16),
            jax.ShapeDtypeStruct((batch, length, in_width), jnp.bfloat16),
            jax.ShapeDtypeStruct(out_shape, jnp.float32),
            jax.ShapeDtypeStruct((8, width), jnp.float32),
        ),
        in_specs=[anywhere] * 8 + [inside] * 6,
        out_specs=(anywhere, anywhere, anywhere, inside, inside),
        scratch_shapes=[
            wide(3, half, width),
            vmem(batch, half, width),
            vmem(batch, half, width),
            wide(batch, half, width),
            vmem(batch, half, width),
            vmem(rows, out_depth),
            vmem(rows, width),
            vmem(rows, out_depth),
            vmem(rows, in_width),
            vmem(rows, width),
            vmem(batch, half, width),
            vmem(2, CHUNK, width),
            vmem(2, CHUNK, in_width),
            wide(2, length, group * features),
            wide(2, 2, length, features),
            vmem(group + 2, length, features),
            wide(group, length, features),
            wide(2, length, features),
            vmem(out_depth, width),
            *collect_scratch(line, out_shape),
            sem(5 + batch),
            sem(2, 2),
            sem(2, 3),
            sem(2 * batch),
            sem(batch),
            sem(batch),
            sem(batch),
            sem(batch),
        ],
        compiler_params=pltpu.CompilerParams(
            collective_id=3, has_side_effects=True, vmem_limit_bytes=62 * MIB
        ),
    )(cot, totals, hidden, projected, context, in_full, out_full, tokens, *gains, *tables)


def gradients_kernel(
    line,
    normed,
    grads,
    gains_ref,
    xe_ref,
    ce_ref,
    act_ref,
    dgate_ref,
    dup_ref,
    in_total,
    gains_all,
    gate_total,
    up_total,
    down_total,
    parts,
    cores,
    firsts,
    rights,
    lefts,
    tree_send,
    tree_receive,
    gain_send,
    gain_receive,
    gain_local,
    wide_rows,
    slim_rows,
    gate_sum,
    up_sum,
    down_sum,
    load_sem,
    save_sem,
):
    narrow, spot = Spot(line, False), Spot(line, True)
    experts, count, _ = xe_ref.shape
    share = wide_rows.shape[1]
    turns = count // share
    pieces = [
        (expert, kind, turn)
        for expert in range(experts)
        for kind in range(2)
        for turn in range(turns)
    ]

    def loads(index):
        expert, kind, turn = pieces[index]
        slot = index % 2
        rows = pl.ds(turn * share, share)
        slim = (dgate_ref, dup_ref) if kind == 0 else (act_ref,)
        return [
            pltpu.make_async_copy(
                (xe_ref, ce_ref)[kind].at[expert, rows], wide_rows.at[slot], load_sem.at[slot, 0]
            )
        ] + [
            pltpu.make_async_copy(
                ref.at[expert, rows], slim_rows.at[slot, i], load_sem.at[slot, 1 + i]
            )
            for i, ref in enumerate(slim)
        ]

    def saves(expert, kind):
        pairs = ((gate_sum, gate_total), (up_sum, up_total))
        if kind:
            return [pltpu.make_async_copy(down_sum, down_total.at[expert], save_sem.at[2])]
        return [
            pltpu.make_async_copy(source, target.at[expert], save_sem.at[i])
            for i, (source, target) in enumerate(pairs)
        ]

    for copy in loads(0):
        copy.start()
    spot.greet()
    gains = Spread(
        spot,
        gains_ref,
        lambda block, half: gains_all.at[block, half],
        gain_send,
        gain_receive,
        gain_local.at[0],
    )
    gains.begin()
    depth, width = in_total.shape
    tree = Collect(
        narrow,
        lambda block, half: rows_at(parts, block, depth),
        in_total,
        cores,
        firsts,
        rights,
        lefts,
        tree_send,
        tree_receive,
    )
    chunk = PLANE * depth

    def plane(step, _):
        z = lax.rem(narrow.z + 1 + step, line)
        columns = pl.ds(pl.multiple_of(z * chunk, LANES), chunk)
        for start in range(0, width, CHUNK):
            parts[pl.ds(pl.multiple_of(z * chunk, 16), chunk), start : start + CHUNK] = (
                lax.dot_general(
                    normed[:, columns],
                    grads[:, start : start + CHUNK],
                    TRANSPOSED_LEFT,
                    preferred_element_type=jnp.float32,
                ).astype(jnp.bfloat16)
            )
        tree.begin(z)
        return 0

    lax.fori_loop(0, line, plane, 0)

    def piece(index):
        expert, kind, turn = pieces[index]
        slot = index % 2
        for copy in loads(index):
            copy.wait()
        if index + 1 < len(pieces):
            for copy in loads(index + 1):
                copy.start()
        if turn == 0 and expert:
            for copy in saves(expert - 1, kind):
                copy.wait()
        size = wide_rows.shape[2] // 4

        def add(target, place, left, right):
            product = lax.dot_general(
                left, right, TRANSPOSED_LEFT, preferred_element_type=jnp.float32
            )
            if turn:
                product = target[place] + product
            target[place] = product

        def part(step, _):
            at = pl.ds(pl.multiple_of(step * size, LANES), size)
            if kind:
                add(down_sum, (slice(None), at), slim_rows[slot, 0], wide_rows[slot, :, at])
            else:
                for i, target in enumerate((gate_sum, up_sum)):
                    add(target, (at, slice(None)), wide_rows[slot, :, at], slim_rows[slot, i])
            return 0

        lax.fori_loop(0, 4, part, 0)
        if turn == turns - 1:
            for copy in saves(expert, kind):
                copy.start()

    work = tree.tasks()
    steps = list(range(1, gains.steps()))
    filler = list(range(len(pieces)))
    while work or filler:
        if filler:
            piece(filler.pop(0))
        if work:
            work.pop(0)()
        if steps:
            gains.step(steps.pop(0))
    gains.finish()
    for copy in saves(experts - 1, 0) + saves(experts - 1, 1):
        copy.wait()


def run_gradients(normed, grads, gains, expert_rows, fsdp_count):
    line = fsdp_count // PLANE
    width = grads.shape[1]
    experts, count, depth = expert_rows[0].shape
    units = expert_rows[2].shape[2]
    share = 2 * CHUNK if count % (2 * CHUNK) == 0 else count // (2 * line)
    shape = (normed.shape[1] // fsdp_count, width)
    sends, receives = spread_count(line, True)
    inside = pl.BlockSpec(memory_space=pltpu.VMEM)
    anywhere = pl.BlockSpec(memory_space=pl.ANY)
    return pl.pallas_call(
        functools.partial(gradients_kernel, line),
        out_shape=(
            jax.ShapeDtypeStruct(shape, jnp.float32),
            jax.ShapeDtypeStruct((fsdp_count, 2, *gains.shape), jnp.float32),
            jax.ShapeDtypeStruct((experts, depth, units), jnp.float32),
            jax.ShapeDtypeStruct((experts, depth, units), jnp.float32),
            jax.ShapeDtypeStruct((experts, units, depth), jnp.float32),
        ),
        in_specs=[inside, inside] + [anywhere] * 6,
        out_specs=(inside,) + (anywhere,) * 4,
        scratch_shapes=[
            pltpu.VMEM((normed.shape[1], width), jnp.bfloat16),
            *collect_scratch(line, shape),
            pltpu.SemaphoreType.DMA((sends,)),
            pltpu.SemaphoreType.DMA((receives,)),
            pltpu.SemaphoreType.DMA((1,)),
            pltpu.VMEM((2, share, depth), jnp.bfloat16),
            pltpu.VMEM((2, 2, share, units), jnp.bfloat16),
            pltpu.VMEM((depth, units), jnp.float32),
            pltpu.VMEM((depth, units), jnp.float32),
            pltpu.VMEM((units, depth), jnp.float32),
            pltpu.SemaphoreType.DMA((2, 3)),
            pltpu.SemaphoreType.DMA((3,)),
        ],
        compiler_params=pltpu.CompilerParams(
            collective_id=4, has_side_effects=True, vmem_limit_bytes=60 * MIB
        ),
    )(normed, grads, gains, *expert_rows)


def experts_kernel(
    line,
    slots,
    own_ref,
    cot_ref,
    info_ref,
    gate_ref,
    up_ref,
    down_ref,
    all_ref,
    total_ref,
    xe_all,
    ce_all,
    act_all,
    dgate_all,
    dup_all,
    part,
    cores,
    seconds,
    firsts,
    ends,
    hidden_w,
    down_w,
    x_rows,
    c_rows,
    xe,
    ce,
    acts,
    dgates,
    dups,
    hidden_grads,
    picks,
    weigh,
    rows,
    stage,
    inbox,
    outbox,
    summed,
    tree_send,
    tree_receive,
    tree_local,
    load_sem,
    save_sem,
    stage_sem,
    inbox_sem,
    outbox_sem,
    total_sem,
    weight_sem,
    core_receive,
    second_receive,
    first_receive,
    end_receive,
):
    spot = Spot(line, True)
    z, core = spot.z, spot.core
    batch, half, width = own_ref.shape
    length = 2 * half
    units = down_ref.shape[1]
    groups = batch * line
    weights = [
        pltpu.make_async_copy(source, target, weight_sem.at[i])
        for i, (source, target) in enumerate(
            [(down_ref, down_w)]
            + [(gate_ref.at[e], hidden_w.at[e, :, pl.ds(0, units)]) for e in range(2)]
            + [(up_ref.at[e], hidden_w.at[e, :, pl.ds(units, units)]) for e in range(2)]
        )
    ]
    for copy in weights:
        copy.start()
    rows[...] = jnp.zeros_like(rows)
    spot.greet()

    def half_of(ref, index):
        return rows_at(ref, index, half)

    trees = [
        Spread(
            spot,
            own_ref.at[i],
            lambda block, side, i=i: half_of(all_ref.at[i, block], side),
            tree_send.at[i],
            tree_receive.at[i],
            tree_local.at[i],
        )
        for i in range(batch)
    ]
    run_trees(trees[:1])
    for tree in trees[1:]:
        tree.begin()
    for copy in weights:
        copy.wait()

    def plane_of(group):
        turn = lax.rem(group, line)
        step = lax.div(turn, 2)
        return jnp.where(lax.rem(turn, 2) == 0, step, line - 1 - step)

    def load_group(group, member):
        at = lax.div(group, line)
        sequence = plane_of(group) * PLANE + member
        slot = member % 2
        return [
            pltpu.make_async_copy(all_ref.at[at, sequence], x_rows.at[slot], load_sem.at[0, slot]),
            pltpu.make_async_copy(cot_ref.at[at, sequence], c_rows.at[slot], load_sem.at[1, slot]),
        ]

    def saves(group):
        to = lambda ref, expert: rows_at(ref.at[expert], group, PLANE * slots)
        pairs = ((xe, xe_all), (ce, ce_all), (acts, act_all), (dgates, dgate_all), (dups, dup_all))
        return [
            pltpu.make_async_copy(source.at[expert], to(target, expert), save_sem.at[2 * i + expert])
            for i, (source, target) in enumerate(pairs)
            for expert in range(2)
        ]

    def staged(unit, y, mine):
        slot = y * 2 + mine
        if mine:
            return pltpu.make_async_copy(stage.at[slot], part.at[unit, y], stage_sem.at[slot])
        return spot.send(
            stage.at[slot], cores.at[unit, y], stage_sem.at[slot], core_receive.at[unit, y], CORE
        )

    def combine(unit, y):
        for mine in range(2):
            member = y * 2 + (core if mine else 1 - core)
            for start in range(0, width, CHUNK):
                stage[y * 2 + mine, :, start : start + CHUNK] = lax.dot_general(
                    picks[member],
                    rows[member, :, start : start + CHUNK],
                    TRANSPOSED_LEFT,
                    preferred_element_type=jnp.float32,
                ).astype(jnp.bfloat16)
            staged(unit, y, mine).start()

    def pick(group, member):
        slot = member % 2
        for copy in load_group(group, member):
            copy.wait()
        if member + 1 < PLANE:
            for copy in load_group(group, member + 1):
                copy.start()
        sequence = plane_of(group) * PLANE + member
        info = info_ref[lax.div(group, line) * line * PLANE + sequence]
        places = lax.broadcasted_iota(jnp.int32, (2 * LANES, length), 0)
        lower = places < LANES
        ranks = jnp.where(lower, info[0:1], info[1:2] + float(LANES)).astype(jnp.int32)
        some = jnp.where(lower, info[0:1], info[1:2]) >= 0.0
        hot = jnp.logical_and(ranks == places, some)
        chosen = hot.astype(jnp.float32).astype(jnp.bfloat16)
        picks[member] = chosen
        shares = jnp.where(hot, jnp.where(lower, info[2:3], info[3:4]), 0.0)
        column = jnp.sum(shares, axis=1, keepdims=True)
        here = pl.ds(member * slots, slots)
        for expert in range(2):
            weigh[expert, here, :] = jnp.broadcast_to(
                column[expert * LANES : expert * LANES + slots], (slots, LANES)
            )
        for source, target in ((x_rows, xe), (c_rows, ce)):
            for start in range(0, width, CHUNK):
                selected = jnp.dot(
                    chosen,
                    source[slot, :, start : start + CHUNK],
                    preferred_element_type=jnp.float32,
                ).astype(jnp.bfloat16)
                for expert in range(2):
                    target[expert, here, start : start + CHUNK] = selected[
                        expert * LANES : expert * LANES + slots
                    ]

    def keep(expert, product, start):
        at = pl.ds(expert * LANES, slots)
        for one in range(PLANE):
            rows[one, at, start : start + CHUNK] = product[one * slots : (one + 1) * slots].astype(
                jnp.bfloat16
            )

    def forward(expert):
        hidden = jnp.dot(xe[expert], hidden_w[expert], preferred_element_type=jnp.float32)
        gate, up = hidden[:, :units], hidden[:, units:]
        sigmoid = jax.nn.sigmoid(gate)
        silu = gate * sigmoid
        scale = weigh[expert, :, 0:1]
        acts[expert] = (silu * up * scale).astype(jnp.bfloat16)
        act_grads = scale * lax.dot_general(
            ce[expert], down_w[expert], TRANSPOSED_RIGHT, preferred_element_type=jnp.float32
        )
        gate_grads = (act_grads * up * (sigmoid * (1.0 + gate * (1.0 - sigmoid)))).astype(
            jnp.bfloat16
        )
        up_grads = (act_grads * silu).astype(jnp.bfloat16)
        dgates[expert] = gate_grads
        dups[expert] = up_grads
        hidden_grads[expert, :, :units] = gate_grads
        hidden_grads[expert, :, units:] = up_grads
        for start in range(0, width, CHUNK):
            keep(
                expert,
                jnp.dot(
                    acts[expert],
                    down_w[expert, :, start : start + CHUNK],
                    preferred_element_type=jnp.float32,
                ),
                start,
            )

    def backward(expert):
        for start in range(0, width, CHUNK):
            keep(
                expert,
                lax.dot_general(
                    hidden_grads[expert],
                    hidden_w[expert, start : start + CHUNK, :],
                    TRANSPOSED_RIGHT,
                    preferred_element_type=jnp.float32,
                ),
                start,
            )

    units_all = 2 * groups

    def inside(unit):
        return jnp.logical_and(unit >= 0, unit < units_all)

    def second_send(unit, tensor, first):
        slot = tensor * 2 + first
        return spot.send(
            outbox.at[slot],
            seconds.at[unit, first],
            outbox_sem.at[slot],
            second_receive.at[unit, first],
            SECOND,
        )

    def first_send(unit, tensor):
        slot = 4 + tensor
        return spot.send(
            outbox.at[slot], firsts.at[unit], outbox_sem.at[slot], first_receive.at[unit], FIRST
        )

    def end_send(unit, tensor, kind):
        slot = 6 + tensor * 2 + kind
        return spot.send(
            outbox.at[slot],
            ends.at[unit, kind],
            outbox_sem.at[slot],
            end_receive.at[unit, kind],
            kind,
        )

    def received(place, semaphore):
        spot.send(place, place, outbox_sem.at[0], semaphore, CORE).wait_recv()

    def sources(unit, first, second):
        y, x = spot.side(core, first, second)
        return [half_of(part.at[unit, y], x), half_of(cores.at[unit, y], x)]

    def load(source, slot):
        return pltpu.make_async_copy(source, inbox.at[slot], inbox_sem.at[slot])

    def add_inbox(target, base, numbers):
        add_rows(target, [inbox.at[base + i] for i in numbers])

    def end_roles(half_step, delay):
        unit = half_step - 3 - delay
        plane = plane_of(lax.div(jnp.maximum(unit, 0), 2))
        valid = inside(unit)
        right = jnp.logical_and(valid, jnp.logical_and(z < plane, delay == z))
        left = jnp.logical_and(valid, jnp.logical_and(z > plane, delay == line - 1 - z))
        last = jnp.logical_and(
            valid,
            jnp.logical_and(z == plane, delay == jnp.maximum(plane, line - 1 - plane)),
        )
        return unit, right, left, last

    def end_task(half_step, delay, parity):
        tensor = (parity - 3 - delay) % 2
        unit, right, left, last = end_roles(half_step, delay)
        some = jnp.logical_or(right, jnp.logical_or(left, last))
        from_left = jnp.logical_and(jnp.logical_or(right, last), z > 0)
        from_right = jnp.logical_and(jnp.logical_or(left, last), z + 1 < line)
        present = ((RIGHT, from_left), (LEFT, from_right))

        def fetch(base):
            def action():
                received(seconds.at[unit, 0], second_receive.at[unit, 0])
                received(firsts.at[unit], first_receive.at[unit])
                inputs = sources(unit, 0, 0) + [seconds.at[unit, 0], firsts.at[unit]]
                for i, source in enumerate(inputs):
                    load(source, base + i).start()
                for kind, there in present:

                    def arrive():
                        received(ends.at[unit, kind], end_receive.at[unit, kind])
                        load(ends.at[unit, kind], base + 4 + kind).start()

                    when(there, arrive)

            when(some, action)

        def add(base):
            def action():
                inputs = sources(unit, 0, 0) + [seconds.at[unit, 0], firsts.at[unit]]
                for i, source in enumerate(inputs):
                    load(source, base + i).wait()
                for kind, there in present:
                    when(there, lambda: load(ends.at[unit, kind], base + 4 + kind).wait())
                summands = list(range(4))
                for kind, chosen, behind in ((RIGHT, right, z > 0), (LEFT, left, z + 1 < line)):

                    def onward():
                        target = outbox.at[6 + tensor * 2 + kind]
                        when(behind, lambda: add_inbox(target, base, summands + [4 + kind]))
                        when(jnp.logical_not(behind), lambda: add_inbox(target, base, summands))
                        end_send(unit, tensor, kind).start()

                    when(chosen, onward)

                @pl.when(last)
                def _():
                    both = jnp.logical_and(from_left, from_right)
                    when(both, lambda: add_inbox(summed, base, summands + [4, 5]))
                    for kind, there in present:
                        when(
                            jnp.logical_and(there, jnp.logical_not(both)),
                            lambda: add_inbox(summed, base, summands + [4 + kind]),
                        )
                    copy = pltpu.make_async_copy(
                        summed, total_ref.at[lax.div(unit, 2 * line), tensor], total_sem.at[0]
                    )
                    copy.start()
                    copy.wait()

            when(some, action)

        return fetch, add

    def retire(half_step, parity):
        before = half_step - 2
        now, then = (parity - 1) % 2, parity
        when(
            inside(before - 1),
            lambda: [second_send(before - 1, now, first).wait_send() for first in range(2)],
        )
        when(inside(before - 2), lambda: first_send(before - 2, then).wait_send())
        for delay in range(line):
            unit, right, left, _ = end_roles(before, delay)
            tensor = (parity - 3 - delay) % 2
            when(right, lambda: end_send(unit, tensor, RIGHT).wait_send())
            when(left, lambda: end_send(unit, tensor, LEFT).wait_send())

    def simple_task(valid, ready, inputs, slot, send):
        def fetch(base):
            def action():
                ready()
                for i, source in enumerate(inputs()):
                    load(source, base + i).start()

            when(valid, action)

        def add(base):
            def action():
                refs = inputs()
                for i, source in enumerate(refs):
                    load(source, base + i).wait()
                add_inbox(outbox.at[slot], base, range(len(refs)))
                send().start()

            when(valid, action)

        return fetch, add

    def half_tasks(half_step, parity):
        one, two = half_step - 1, half_step - 2
        now, then = (parity - 1) % 2, parity

        def cores_in():
            for y in range(2):
                staged(one, y, 1).wait()
                staged(one, y, 0).wait_send()
                received(cores.at[one, y], core_receive.at[one, y])

        tasks = [
            simple_task(
                inside(one),
                cores_in if first else lambda: None,
                lambda first=first: sources(one, first, 1),
                now * 2 + first,
                lambda first=first: second_send(one, now, first),
            )
            for first in (1, 0)
        ]
        tasks.append(
            simple_task(
                inside(two),
                lambda: received(seconds.at[two, 1], second_receive.at[two, 1]),
                lambda: sources(two, 1, 0) + [seconds.at[two, 1]],
                4 + then,
                lambda: first_send(two, then),
            )
        )
        return tasks + [end_task(half_step, delay, parity) for delay in range(line)]

    def woven(tasks, pieces):
        boxes = inbox.shape[0] // 2
        tasks[0][0](0)
        for index, (_, add) in enumerate(tasks):
            if index + 1 < len(tasks):
                tasks[index + 1][0]((index + 1) % 2 * boxes)
            share = -(-len(pieces) // (len(tasks) - index))
            for piece in pieces[:share]:
                piece()
            pieces = pieces[share:]
            add(index % 2 * boxes)

    def tree_turn(half_step, last):
        for i in range(1, batch):
            turn = half_step - (i - 1) * 2 * line
            if last:
                when(turn == 2 * line - 1, trees[i].finish)
            else:
                inner = jnp.logical_and(turn >= 0, turn < 2 * line - 1)
                when(inner, lambda: trees[i].step(turn + 1))

    def begin_pick(group):
        for copy in load_group(group, 0):
            copy.start()

    begin_pick(0)
    for member in range(PLANE):
        pick(0, member)

    def step_body(step, _):
        busy = step < groups
        more = step + 1 < groups
        for parity in range(2):
            half_step = step * 2 + parity
            tree_turn(half_step, False)
            retire(half_step, parity)
            tasks = half_tasks(half_step, parity)
            pieces = []
            for expert in range(2):
                pieces.append(functools.partial((forward, backward)[parity], expert))
            if parity == 0:
                pieces.append(lambda: [copy.start() for copy in saves(step)])
            for y in range(2):
                pieces.append(functools.partial(combine, half_step, y))
            pieces = [functools.partial(when, busy, piece) for piece in pieces]
            if parity == 1:

                def prepare():
                    for copy in saves(step):
                        copy.wait()
                    begin_pick(step + 1)

                tree_end = functools.partial(tree_turn, half_step, True)
                pieces += [tree_end, functools.partial(when, more, prepare)]
                for member in range(PLANE):
                    pieces.append(
                        functools.partial(when, more, functools.partial(pick, step + 1, member))
                    )
            woven(tasks, pieces)
        return 0

    half_steps = units_all + line + 2
    lax.fori_loop(0, -(-half_steps // 2), step_body, 0)
    end = -(-half_steps // 2) * 2
    for parity in range(2):
        retire(jnp.int32(end + parity), parity)
    for copy in saves(groups - 1):
        copy.wait()


def run_experts(rows, cot_all, info, w_gate, w_up, w_down, capacity, fsdp_count):
    line = fsdp_count // PLANE
    batch, half, width = rows.shape
    length = 2 * half
    units = w_down.shape[1]
    slots = -(-capacity // 16) * 16
    groups = batch * line
    count = groups * PLANE * slots
    taken = PLANE * slots
    sends, receives = spread_count(line, True)
    shape = lambda *dims: jax.ShapeDtypeStruct(dims, jnp.bfloat16)
    block = (half, width)
    anywhere = pl.BlockSpec(memory_space=pl.ANY)
    vmem = lambda *dims: pltpu.VMEM(dims, jnp.bfloat16)
    sem = lambda *dims: pltpu.SemaphoreType.DMA(dims)
    return pl.pallas_call(
        functools.partial(experts_kernel, line, slots),
        out_shape=(
            shape(batch, fsdp_count, length, width),
            jax.ShapeDtypeStruct((batch, 2, *block), jnp.float32),
            shape(2, count, width),
            shape(2, count, width),
            shape(2, count, units),
            shape(2, count, units),
            shape(2, count, units),
            shape(2 * groups, 2, length, width),
            shape(2 * groups, 2, length, width),
            shape(2 * groups, 2, *block),
            shape(2 * groups, *block),
            shape(2 * groups, 2, *block),
        ),
        in_specs=[
            anywhere,
            anywhere,
            pl.BlockSpec(memory_space=pltpu.VMEM),
            anywhere,
            anywhere,
            anywhere,
        ],
        out_specs=(anywhere,) * 12,
        scratch_shapes=[
            vmem(2, width, 2 * units),
            vmem(2, units, width),
            vmem(2, length, width),
            vmem(2, length, width),
            vmem(2, taken, width),
            vmem(2, taken, width),
            vmem(2, taken, units),
            vmem(2, taken, units),
            vmem(2, taken, units),
            vmem(2, taken, 2 * units),
            vmem(PLANE, 2 * LANES, length),
            pltpu.VMEM((2, taken, LANES), jnp.float32),
            vmem(PLANE, 2 * LANES, width),
            vmem(PLANE, length, width),
            vmem(12, *block),
            vmem(10, *block),
            pltpu.VMEM(block, jnp.float32),
            sem(batch, sends),
            sem(batch, receives),
            sem(batch),
            sem(2, 2),
            sem(10),
            sem(PLANE),
            sem(12),
            sem(10),
            sem(1),
            sem(5),
            sem(2 * groups, 2),
            sem(2 * groups, 2),
            sem(2 * groups),
            sem(2 * groups, 2),
        ],
        compiler_params=pltpu.CompilerParams(
            collective_id=2, has_side_effects=True, vmem_limit_bytes=60 * MIB
        ),
    )(rows, cot_all, info, w_gate, w_up, w_down)[1:7]


def packed_picks(routes, gates):
    length = routes.shape[2]
    packed = jnp.concatenate([routes[:, 0].astype(jnp.float32), gates[:, 0]], axis=-1)
    packed = jnp.swapaxes(packed, 1, 2).reshape(-1, length)
    return jnp.pad(packed, ((0, 0), (0, -length % LANES)))


def slot_info(packed, batch, top, length, local_experts):
    fsdp_count = packed.shape[0]
    packed = packed[..., :length].reshape(fsdp_count, batch, 1, 2 * top, length)
    packed = jnp.swapaxes(packed, 0, 1)
    experts = lax.axis_index(FSDP) * local_experts + jnp.arange(local_experts, dtype=jnp.int32)
    same = packed[..., :top, :].astype(jnp.int32) == experts[:, None, None]
    hot = jnp.any(same, axis=3)
    shares = jnp.sum(jnp.where(same, packed[..., top:, :], 0.0), axis=3)
    position = jnp.arange(length)
    upper = (position[:, None] < position[None, :]).astype(jnp.bfloat16)
    rank = jnp.dot(
        hot.astype(jnp.bfloat16).reshape(-1, length), upper, preferred_element_type=jnp.float32
    )
    rank = jnp.where(hot, rank.reshape(hot.shape), -1.0)
    return jnp.concatenate([rank, shares], axis=2).reshape(-1, 2 * local_experts, length)


def gathered_layer(
    tokens,
    cotangent,
    norm1_gain,
    w_query,
    key_projection_weight,
    value_projection_weight,
    query_gain,
    key_gain,
    w_out,
    norm2_gain,
    w_gate,
    w_up,
    w_down,
    routes,
    gates,
):
    batch_count = tokens.shape[0]
    model_width = tokens.shape[3]
    sequence_length = routes.shape[2]
    half_length = tokens.shape[2]
    top_count = routes.shape[3]
    head_features = query_gain.shape[0]
    local_experts = w_gate.shape[0]
    fsdp_count = lax.axis_size(FSDP)
    all_experts = local_experts * fsdp_count
    capacity = 7 * top_count * sequence_length // (6 * all_experts)
    query_width = w_query.shape[1]
    kv_width = key_projection_weight.shape[1]
    kv_heads = kv_width // head_features
    cosine_table, sine_values = rotary_tables(sequence_length, head_features)
    first_gain = norm1_gain.astype(jnp.float32)
    second_gain = norm2_gain.astype(jnp.float32)
    query_factor_scale = query_gain.astype(jnp.float32)
    key_scale = key_gain.astype(jnp.float32)

    weight_in = jnp.concatenate([w_query, key_projection_weight, value_projection_weight], axis=1)
    half_signs = jnp.where(jnp.arange(head_features) < head_features // 2, -1.0, 1.0)
    tables = (cosine_table[:, 0], sine_values[:, 0] * half_signs)
    gains = [
        gain[None, :] for gain in (first_gain, second_gain, query_factor_scale, key_scale)
    ]
    cot_all, in_full, out_full, picks, normed, projected, contexts, hidden, second = run_forward(
        tokens[:, 0],
        cotangent[:, 0],
        weight_in,
        w_out,
        packed_picks(routes, gates),
        gains,
        tables,
        fsdp_count,
        kv_heads,
    )
    info = slot_info(picks, batch_count, top_count, sequence_length, local_experts)
    totals, *expert_rows = run_experts(
        second, cot_all, info, w_gate, w_up, w_down, capacity, fsdp_count
    )
    block_out, input_grad, projected_grads, out_sum, gain_grads = run_backward(
        cotangent[:, 0],
        totals,
        hidden,
        projected,
        contexts,
        in_full,
        out_full,
        tokens[:, 0],
        gains,
        tables,
        fsdp_count,
        kv_heads,
    )
    rows = batch_count * sequence_length
    in_sum, gains_all, *expert_grads = run_gradients(
        normed.reshape(rows, -1),
        projected_grads.reshape(rows, -1),
        gain_grads,
        expert_rows,
        fsdp_count,
    )
    gains_sum = jnp.sum(gains_all, axis=(0, 1))
    return (
        block_out[:, None],
        input_grad[:, None],
        gains_sum[0],
        in_sum[:, :query_width],
        in_sum[:, query_width : query_width + kv_width],
        in_sum[:, query_width + kv_width :],
        gains_sum[2, :head_features],
        gains_sum[3, :head_features],
        out_sum,
        gains_sum[1],
        *expert_grads,
    )


def shards(*arrays):
    tokens, routes, w_gate = arrays[0], arrays[13], arrays[10]
    fsdp_count = lax.axis_size(FSDP)
    gathered = fsdp_count * routes.shape[2] * tokens.shape[3] * 2
    fits = gathered <= 24 * MIB and fsdp_count % PLANE == 0 and lax.axis_size(TP) == 2
    if fits and w_gate.shape[0] == 2:
        return gathered_layer(*arrays)
    return exchanged_layer(*arrays)


def solution(mesh):
    in_specs = (
        P(None, "fsdp", "tp", None),
        P(None, "fsdp", "tp", None),
        P(),
        P("fsdp", "tp"),
        P("fsdp", "tp"),
        P("fsdp", "tp"),
        P(),
        P(),
        P("tp", "fsdp"),
        P(),
        P("fsdp", None, "tp"),
        P("fsdp", None, "tp"),
        P("fsdp", "tp", None),
        P(None, "fsdp", None, None),
        P(None, "fsdp", None, None),
    )
    out_specs = (
        P(None, "fsdp", "tp", None),
        P(None, "fsdp", "tp", None),
        P(),
        P("fsdp", "tp"),
        P("fsdp", "tp"),
        P("fsdp", "tp"),
        P(),
        P(),
        P("tp", "fsdp"),
        P(),
        P("fsdp", None, "tp"),
        P("fsdp", None, "tp"),
        P("fsdp", "tp", None),
    )
    return jax.shard_map(shards, mesh=mesh, in_specs=in_specs, out_specs=out_specs, check_vma=False)
```

```python
import functools

import jax
import jax.numpy as jnp
from jax import lax
from jax.experimental import pallas as pl
from jax.experimental.pallas import tpu as pltpu
from jax.sharding import PartitionSpec as P

BLOCK = 256


EPSILON = 1e-06
ROPE_BASE = 1000000.0
MASKED = -1e30
TILE_PICKS = 128


def rms_scale(row_block, gain_row):
    return (
        row_block
        * lax.rsqrt(jnp.mean(row_block * row_block, axis=-1, keepdims=True) + EPSILON)
        * gain_row
    )


def rotary_tables(sequence_length, head_width):
    half_width = head_width // 2
    inverse = ROPE_BASE ** (-2.0 * jnp.arange(half_width, dtype=jnp.float32) / head_width)
    angles = jnp.arange(sequence_length, dtype=jnp.float32)[:, None] * inverse[None, :]
    cosine_table = jnp.concatenate([jnp.cos(angles), jnp.cos(angles)], axis=-1)[:, None, :]
    sine_values = jnp.concatenate([jnp.sin(angles), jnp.sin(angles)], axis=-1)[:, None, :]
    return (cosine_table, sine_values)


def rotate(head_rows, cosine_table, sine_values):
    half_width = head_rows.shape[-1] // 2
    turned = jnp.concatenate([-head_rows[..., half_width:], head_rows[..., :half_width]], axis=-1)
    return head_rows * cosine_table + turned * sine_values


def prepare_heads(projected, gain_row, cosine_table, sine_values):
    return rotate(rms_scale(projected, gain_row), cosine_table, sine_values)


def swiglu(gate_act, up_act):
    return jax.nn.silu(gate_act) * up_act


def slot_tables(route_rows, gate_rows, expert_count, capacity):
    sequence_length = route_rows.shape[0]
    top_count = route_rows.shape[1]
    pick_count = sequence_length * top_count
    tile_count = pick_count // TILE_PICKS
    flat_routes = route_rows.reshape(-1)
    onehot = (flat_routes[:, None] == jnp.arange(expert_count, dtype=jnp.int32)[None, :]).astype(
        jnp.bfloat16
    )
    tiles = onehot.reshape(tile_count, TILE_PICKS, expert_count)
    positions = jnp.arange(TILE_PICKS, dtype=jnp.int32)
    lower = (positions[None, :] < positions[:, None]).astype(jnp.bfloat16)
    within = jnp.einsum("ij,bje->bie", lower, tiles, preferred_element_type=jnp.float32)
    tile_totals = jnp.sum(tiles.astype(jnp.float32), axis=1)
    offsets = jnp.cumsum(tile_totals, axis=0) - tile_totals
    before = within + offsets[:, None, :]
    slot_rank = jnp.sum(before * tiles.astype(jnp.float32), axis=-1).reshape(-1).astype(jnp.int32)
    slot_index = flat_routes * capacity + slot_rank
    pick_ids = jnp.arange(pick_count, dtype=jnp.int32) // top_count
    slot_owner = (
        jnp.full((expert_count * capacity,), sequence_length, jnp.int32)
        .at[slot_index]
        .set(pick_ids)
    )
    slot_weight = (
        jnp.zeros((expert_count * capacity,), jnp.float32).at[slot_index].set(gate_rows.reshape(-1))
    )
    return (slot_index, slot_owner, slot_weight)


def exchanged_layer(
    tokens,
    cotangent,
    norm1_gain,
    w_query,
    key_projection_weight,
    value_projection_weight,
    query_gain,
    key_gain,
    w_out,
    norm2_gain,
    w_gate,
    w_up,
    w_down,
    routes,
    gates,
):
    batch_count = tokens.shape[0]
    model_width = tokens.shape[3]
    sequence_length = routes.shape[2]
    top_count = routes.shape[3]
    head_features = query_gain.shape[0]
    local_experts = w_gate.shape[0]
    fsdp_count = lax.axis_size("fsdp")
    all_experts = local_experts * fsdp_count
    capacity = 7 * top_count * sequence_length // (6 * all_experts)
    query_heads = w_query.shape[1] // head_features
    kv_heads = key_projection_weight.shape[1] // head_features
    group_size = query_heads // kv_heads
    score_scale = head_features ** (-0.5)
    cosine_table, sine_values = rotary_tables(sequence_length, head_features)
    block_ids = jnp.arange(sequence_length, dtype=jnp.int32) // BLOCK
    visible = (block_ids[None, :] <= block_ids[:, None])[None, None]
    first_gain = norm1_gain.astype(jnp.float32)
    second_gain = norm2_gain.astype(jnp.float32)
    query_factor_scale = query_gain.astype(jnp.float32)
    key_scale = key_gain.astype(jnp.float32)
    zero_row = jnp.zeros((1, model_width), jnp.bfloat16)
    buffer_shape = (fsdp_count, local_experts, capacity, model_width)

    def masked_scores(query_fourfold, key_rows):
        raw_scores = (
            jnp.einsum(
                "qcgd,kcd->cgqk", query_fourfold, key_rows, preferred_element_type=jnp.float32
            )
            * score_scale
        )
        return jnp.where(visible, raw_scores, MASKED)

    def prep_heads(projected, gain_row):
        return prepare_heads(projected, gain_row, cosine_table, sine_values)

    gain_sums = (
        jnp.zeros((model_width,), jnp.float32),
        jnp.zeros((model_width,), jnp.float32),
        jnp.zeros((head_features,), jnp.float32),
        jnp.zeros((head_features,), jnp.float32),
    )
    expert_grads = (
        jnp.zeros(w_gate.shape, jnp.float32),
        jnp.zeros(w_up.shape, jnp.float32),
        jnp.zeros(w_down.shape, jnp.float32),
    )
    attn_grads = tuple(
        (
            jnp.zeros(weight_part.shape, jnp.float32)
            for weight_part in (w_query, key_projection_weight, value_projection_weight, w_out)
        )
    )
    outputs = []
    input_grads = []
    for batch_index in range(batch_count):
        query_full, key_full, value_full, out_full = (
            lax.all_gather(w_query, "fsdp", axis=0, tiled=True),
            lax.all_gather(key_projection_weight, "fsdp", axis=0, tiled=True),
            lax.all_gather(value_projection_weight, "fsdp", axis=0, tiled=True),
            lax.all_gather(w_out, "fsdp", axis=1, tiled=True),
        )
        own_rows = tokens[batch_index, 0].astype(jnp.float32)
        own_cot = cotangent[batch_index, 0]
        route_rows = routes[batch_index, 0]
        gate_rows = gates[batch_index, 0]
        first_normed = rms_scale(own_rows, first_gain).astype(jnp.bfloat16)
        normed_all = lax.all_gather(first_normed, "tp", axis=0, tiled=True)
        query_projected = jnp.dot(
            normed_all, query_full, preferred_element_type=jnp.float32
        ).reshape(sequence_length, query_heads, head_features)
        key_projected = jnp.dot(normed_all, key_full, preferred_element_type=jnp.float32).reshape(
            sequence_length, kv_heads, head_features
        )
        value_row_list = (
            jnp.dot(normed_all, value_full, preferred_element_type=jnp.float32)
            .astype(jnp.bfloat16)
            .reshape(sequence_length, kv_heads, head_features)
        )
        query_rot = prep_heads(query_projected, query_factor_scale).astype(jnp.bfloat16)
        key_rot = prep_heads(key_projected, key_scale).astype(jnp.bfloat16)
        query_fourfold = query_rot.reshape(sequence_length, kv_heads, group_size, head_features)
        scores = masked_scores(query_fourfold, key_rot)
        row_max = jnp.max(scores, axis=-1, keepdims=True)
        exp_scores = jnp.exp(scores - row_max)
        totals = jnp.sum(exp_scores, axis=-1, keepdims=True)
        log_total = row_max + jnp.log(totals)
        prob_rows = (exp_scores / totals).astype(jnp.bfloat16)
        context = (
            jnp.einsum(
                "cgqk,kcd->qcgd", prob_rows, value_row_list, preferred_element_type=jnp.float32
            )
            .astype(jnp.bfloat16)
            .reshape(sequence_length, query_heads * head_features)
        )
        attn_own = lax.psum_scatter(
            jnp.dot(context, out_full, preferred_element_type=jnp.float32).astype(jnp.bfloat16),
            "tp",
            scatter_dimension=0,
            tiled=True,
        ).astype(jnp.float32)
        hidden_own = own_rows + attn_own
        second_normed = rms_scale(hidden_own, second_gain).astype(jnp.bfloat16)
        normed_two, cot_all = (
            lax.all_gather(second_normed, "tp", axis=0, tiled=True),
            lax.all_gather(own_cot, "tp", axis=0, tiled=True),
        )
        slot_index, slot_owner, slot_weight = slot_tables(
            route_rows, gate_rows, all_experts, capacity
        )
        padded_rows = jnp.concatenate([normed_two, zero_row], axis=0)
        send_rows = padded_rows[slot_owner].reshape(buffer_shape)
        expert_in = lax.all_to_all(send_rows, "fsdp", split_axis=0, concat_axis=0, tiled=True)
        gate_act = jnp.einsum(
            "sekd,edf->sekf", expert_in, w_gate, preferred_element_type=jnp.float32
        )
        up_act = jnp.einsum("sekd,edf->sekf", expert_in, w_up, preferred_element_type=jnp.float32)
        act_rows = swiglu(gate_act, up_act).astype(jnp.bfloat16)
        expert_out = jnp.einsum(
            "sekf,efd->sekd", act_rows, w_down, preferred_element_type=jnp.float32
        )
        returned = lax.all_to_all(
            expert_out.astype(jnp.bfloat16), "fsdp", split_axis=0, concat_axis=0, tiled=True
        ).astype(expert_out.dtype)
        picked = returned.reshape(all_experts * capacity, model_width)[slot_index].reshape(
            sequence_length, top_count, model_width
        )
        moe_part = jnp.sum(picked * gate_rows[:, :, None], axis=1)
        moe_own = lax.psum_scatter(
            moe_part.astype(jnp.bfloat16), "tp", scatter_dimension=0, tiled=True
        ).astype(jnp.float32)
        outputs.append((hidden_own + moe_own).astype(jnp.bfloat16))
        cot_padded = jnp.concatenate([cot_all, zero_row], axis=0)
        send_grads = (
            (slot_weight[:, None] * cot_padded[slot_owner])
            .astype(jnp.bfloat16)
            .reshape(buffer_shape)
        )
        out_grads = lax.all_to_all(send_grads, "fsdp", split_axis=0, concat_axis=0, tiled=True)
        act_grads = jnp.einsum(
            "sekd,efd->sekf", out_grads, w_down, preferred_element_type=jnp.float32
        )
        _, swiglu_back = jax.vjp(swiglu, gate_act, up_act)
        gate_grads, up_grads = swiglu_back(act_grads)
        gate_grads = gate_grads.astype(jnp.bfloat16)
        up_grads = up_grads.astype(jnp.bfloat16)
        expert_grads = (
            expert_grads[0]
            + jnp.einsum(
                "sekd,sekf->edf", expert_in, gate_grads, preferred_element_type=jnp.float32
            ),
            expert_grads[1]
            + jnp.einsum("sekd,sekf->edf", expert_in, up_grads, preferred_element_type=jnp.float32),
            expert_grads[2]
            + jnp.einsum("sekf,sekd->efd", act_rows, out_grads, preferred_element_type=jnp.float32),
        )
        input_part = jnp.einsum(
            "sekf,edf->sekd", gate_grads, w_gate, preferred_element_type=jnp.float32
        ) + jnp.einsum("sekf,edf->sekd", up_grads, w_up, preferred_element_type=jnp.float32)
        input_back = lax.all_to_all(
            input_part.astype(jnp.bfloat16), "fsdp", split_axis=0, concat_axis=0, tiled=True
        ).astype(input_part.dtype)
        normed_grads = jnp.sum(
            input_back.reshape(all_experts * capacity, model_width)[slot_index].reshape(
                sequence_length, top_count, model_width
            ),
            axis=1,
        )
        normed_own = lax.psum_scatter(
            normed_grads.astype(jnp.bfloat16), "tp", scatter_dimension=0, tiled=True
        ).astype(jnp.float32)
        _, second_back = jax.vjp(rms_scale, hidden_own, second_gain)
        hidden_part, second_gain_grad = second_back(normed_own)
        hidden_grad = own_cot.astype(jnp.float32) + hidden_part
        attn_grad_all = lax.all_gather(hidden_grad.astype(jnp.bfloat16), "tp", axis=0, tiled=True)
        out_weight_grad = jnp.einsum(
            "th,td->hd", context, attn_grad_all, preferred_element_type=jnp.float32
        )
        context_grad = (
            jnp.einsum("td,hd->th", attn_grad_all, out_full, preferred_element_type=jnp.float32)
            .astype(jnp.bfloat16)
            .reshape(sequence_length, kv_heads, group_size, head_features)
        )
        exp_again = jnp.exp(masked_scores(query_fourfold, key_rot) - log_total)
        probs_again = exp_again.astype(jnp.bfloat16)
        prob_grads = jnp.einsum(
            "qcgd,kcd->cgqk", context_grad, value_row_list, preferred_element_type=jnp.float32
        )
        value_grads = (
            jnp.einsum(
                "cgqk,qcgd->kcd", probs_again, context_grad, preferred_element_type=jnp.float32
            )
            .astype(jnp.bfloat16)
            .reshape(sequence_length, kv_heads * head_features)
        )
        score_grads = (
            exp_again * (prob_grads - jnp.sum(exp_again * prob_grads, axis=-1, keepdims=True))
        ).astype(jnp.bfloat16)
        query_rot_grads = (
            jnp.einsum("cgqk,kcd->qcgd", score_grads, key_rot, preferred_element_type=jnp.float32)
            * score_scale
        ).reshape(sequence_length, query_heads, head_features)
        key_rot_grads = (
            jnp.einsum(
                "cgqk,qcgd->kcd", score_grads, query_fourfold, preferred_element_type=jnp.float32
            )
            * score_scale
        )
        _, query_back = jax.vjp(prep_heads, query_projected, query_factor_scale)
        query_proj_grads, query_gain_grad = query_back(query_rot_grads)
        _, key_back = jax.vjp(prep_heads, key_projected, key_scale)
        key_proj_grads, key_gain_grad = key_back(key_rot_grads)
        query_proj_grads = query_proj_grads.astype(jnp.bfloat16).reshape(
            sequence_length, query_heads * head_features
        )
        key_proj_grads = key_proj_grads.astype(jnp.bfloat16).reshape(
            sequence_length, kv_heads * head_features
        )
        first_normed_grads = (
            jnp.einsum(
                "tq,dq->td", query_proj_grads, query_full, preferred_element_type=jnp.float32
            )
            + jnp.einsum("tq,dq->td", key_proj_grads, key_full, preferred_element_type=jnp.float32)
            + jnp.einsum("tq,dq->td", value_grads, value_full, preferred_element_type=jnp.float32)
        )
        weight_parts = (
            jnp.einsum(
                "td,tq->dq", normed_all, query_proj_grads, preferred_element_type=jnp.float32
            ),
            jnp.einsum("td,tq->dq", normed_all, key_proj_grads, preferred_element_type=jnp.float32),
            jnp.einsum("td,tq->dq", normed_all, value_grads, preferred_element_type=jnp.float32),
            out_weight_grad,
        )
        first_own = lax.psum_scatter(
            first_normed_grads.astype(jnp.bfloat16), "tp", scatter_dimension=0, tiled=True
        ).astype(jnp.float32)
        _, first_back = jax.vjp(rms_scale, own_rows, first_gain)
        row_part, first_gain_grad = first_back(first_own)
        input_grads.append((hidden_grad + row_part).astype(jnp.bfloat16))
        gain_sums = (
            gain_sums[0] + first_gain_grad,
            gain_sums[1] + second_gain_grad,
            gain_sums[2] + query_gain_grad,
            gain_sums[3] + key_gain_grad,
        )
        attn_grads = jax.tree.map(
            jnp.add,
            attn_grads,
            (
                lax.psum_scatter(weight_parts[0], "fsdp", scatter_dimension=0, tiled=True),
                lax.psum_scatter(weight_parts[1], "fsdp", scatter_dimension=0, tiled=True),
                lax.psum_scatter(weight_parts[2], "fsdp", scatter_dimension=0, tiled=True),
                lax.psum_scatter(weight_parts[3], "fsdp", scatter_dimension=1, tiled=True),
            ),
        )
    summed = lax.psum((gain_sums[0], gain_sums[1], gain_sums[2], gain_sums[3]), ("fsdp", "tp"))
    block_out = jnp.stack(outputs)[:, None]
    input_grad = jnp.stack(input_grads)[:, None]
    return (
        block_out,
        input_grad,
        summed[0],
        attn_grads[0],
        attn_grads[1],
        attn_grads[2],
        summed[2],
        summed[3],
        attn_grads[3],
        summed[1],
        expert_grads[0],
        expert_grads[1],
        expert_grads[2],
    )


MESH = pl.DeviceIdType.MESH
FSDP, TP = "fsdp", "tp"
PLANE = 4
LANES = 128
MIB = 1 << 20
RIGHT, LEFT, FIRST, SECOND, CORE, CROSS = range(6)
TRANSPOSED_LEFT = (((0,), (0,)), ((), ()))
TRANSPOSED_RIGHT = (((1,), (1,)), ((), ()))
OUTPUT, BACK = range(2)
CHUNK = 512


class Spot:
    def __init__(self, line, wide, turned=True):
        self.line = line
        self.wide = wide
        self.turned = turned
        self.planes = 4 if wide else 2
        index = lax.axis_index(FSDP)
        self.x = lax.axis_index(TP)
        self.z = lax.div(index, PLANE)
        self.y = lax.rem(lax.div(index, 2), 2)
        self.core = lax.rem(index, 2)

    def side(self, core, first, second):
        flip_y, flip_x = first, second
        if self.wide and self.turned:
            flip_y = (1 - core) * first + core * second
            flip_x = core * first + (1 - core) * second
        return self.y + flip_y * (1 - 2 * self.y), self.x + flip_x * (1 - 2 * self.x)

    def block(self, core, first, second, z):
        y, x = self.side(core, first, second)
        return z * PLANE + y * 2 + core, x

    def device(self, kind):
        if kind == RIGHT:
            return self.block(self.core, 0, 0, self.z + 1)
        if kind == LEFT:
            return self.block(self.core, 0, 0, self.z - 1)
        if kind == CORE:
            return self.block(1 - self.core, 0, 0, self.z)
        if kind == CROSS:
            return self.block(self.core, 0, 0, self.z)[0], 1 - self.x
        return self.block(self.core, int(kind == FIRST), int(kind == SECOND), self.z)

    def kinds(self):
        return (FIRST, SECOND, CORE) if self.wide else (FIRST, CORE)

    def number(self, first, second, z):
        return (second * 2 + first) * self.line + z

    def order(self, step):
        if isinstance(step, int) and step == 0:
            return [(self.z, None)]
        return [(self.z - step, self.z - step >= 0), (self.z + step, self.z + step < self.line)]

    def greet(self):
        barrier = pltpu.get_barrier_semaphore()

        def signal(kind):
            pl.semaphore_signal(barrier, inc=1, device_id=self.device(kind), device_id_type=MESH)

        for kind in self.kinds():
            signal(kind)
        when(self.z + 1 < self.line, lambda: signal(RIGHT))
        when(self.z > 0, lambda: signal(LEFT))
        around = (self.z + 1 < self.line).astype(jnp.int32) + (self.z > 0).astype(jnp.int32)
        pl.semaphore_wait(barrier, len(self.kinds()) + around)

    def send(self, source, target, send_sem, receive_sem, kind):
        return pltpu.make_async_remote_copy(
            src_ref=source,
            dst_ref=target,
            send_sem=send_sem,
            recv_sem=receive_sem,
            device_id=self.device(kind),
            device_id_type=MESH,
        )


def when(condition, action):
    def run():
        action()

    if condition is None:
        run()
    else:
        pl.when(condition)(run)


class Spread:
    def __init__(self, spot, source, slot, send, receive, local):
        self.spot = spot
        self.slot = slot
        self.source = source
        self.sends = send
        self.receives = receive
        self.mine = pltpu.make_async_copy(source, slot(*spot.block(spot.core, 0, 0, spot.z)), local)

    def copy(self, first, second, z, kind, own=False):
        spot = self.spot
        place = self.slot(*spot.block(spot.core, first, second, z))
        number = spot.number(first, second, z)
        arrival = {
            RIGHT: number,
            LEFT: number,
            FIRST: spot.number(1, 0, z),
            SECOND: spot.number(first, 1, z),
            CORE: spot.planes * spot.line + number,
        }[kind]
        departure = {RIGHT: 0, LEFT: 1, FIRST: 2, SECOND: 3, CORE: 5}[kind] * spot.line + number
        source = self.source if own else place
        return spot.send(source, place, self.sends.at[departure], self.receives.at[arrival], kind)

    def arrived(self, first, second, z, other=False):
        spot = self.spot
        core = 1 - spot.core if other else spot.core
        place = self.slot(*spot.block(core, first, second, z))
        number = spot.number(first, second, z) + (spot.planes * spot.line if other else 0)
        spot.send(place, place, self.sends.at[0], self.receives.at[number], CORE).wait_recv()

    def steps(self):
        return self.spot.line + (3 if self.spot.wide else 1)

    def begin(self):
        spot = self.spot
        z = spot.z
        when(z + 1 < spot.line, lambda: self.copy(0, 0, z, RIGHT, True).start())
        when(z > 0, lambda: self.copy(0, 0, z, LEFT, True).start())
        for kind in spot.kinds():
            self.copy(0, 0, z, kind, True).start()
        self.mine.start()

    def step(self, step):
        spot = self.spot
        line, z = spot.line, spot.z

        def reached(away, action):
            inside = jnp.logical_and(away >= 0, away < line)
            when(jnp.logical_and(inside, z - away >= 0), lambda: action(z - away, True))
            when(
                jnp.logical_and(inside, jnp.logical_and(away > 0, z + away < line)),
                lambda: action(z + away, False),
            )

        def along(zz, from_left):
            self.arrived(0, 0, zz)
            if from_left:
                when(z + 1 < line, lambda: self.copy(0, 0, zz, RIGHT).start())
            else:
                when(z > 0, lambda: self.copy(0, 0, zz, LEFT).start())
            for kind in spot.kinds():
                self.copy(0, 0, zz, kind).start()

        def firsts(zz, _):
            self.arrived(1, 0, zz)
            if spot.wide:
                self.copy(1, 0, zz, SECOND).start()
            self.copy(1, 0, zz, CORE).start()

        def lasts(first):
            def action(zz, _):
                self.arrived(first, 1, zz)
                self.copy(first, 1, zz, CORE).start()

            return action

        step = jnp.asarray(step, jnp.int32)
        reached(step, along)
        reached(step - 1, firsts)
        if spot.wide:
            reached(step - 2, lasts(0))
            reached(step - 3, lasts(1))

    def finish(self):
        spot = self.spot
        z = spot.z

        def body(zz, _):
            when(
                jnp.logical_and(z + 1 < spot.line, zz <= z),
                lambda: self.copy(0, 0, zz, RIGHT).wait_send(),
            )
            when(jnp.logical_and(z > 0, zz >= z), lambda: self.copy(0, 0, zz, LEFT).wait_send())
            self.copy(0, 0, zz, FIRST).wait_send()
            for second in range(2 if spot.wide else 1):
                for first in (0, 1):
                    if spot.wide and not second:
                        self.copy(first, 0, zz, SECOND).wait_send()
                    self.copy(first, second, zz, CORE).wait_send()
                    self.arrived(first, second, zz, other=True)
            return 0

        lax.fori_loop(0, spot.line, body, 0)
        self.mine.wait()


def run_trees(trees):
    for tree in trees:
        tree.begin()

    def body(step, _):
        for tree in trees:
            tree.step(step)
        return 0

    lax.fori_loop(1, max(tree.steps() for tree in trees), body, 0)
    for tree in trees:
        tree.finish()


def spread_count(line, wide):
    return (9 if wide else 7) * line, (8 if wide else 4) * line


def rows_at(ref, index, size):
    return ref.at[pl.ds(pl.multiple_of(index * size, 16), size)]


def columns_at(ref, index, size):
    return ref.at[:, pl.ds(pl.multiple_of(index * size, LANES), size)]


def norm_rows(target, source, gain):
    def body(step, _):
        rows = pl.ds(pl.multiple_of(step * 16, 16), 16)
        value = source[rows, :].astype(jnp.float32)
        target[rows, :] = rms_scale(value, gain[...].astype(jnp.float32)).astype(target.dtype)
        return 0

    lax.fori_loop(0, target.shape[0] // 16, body, 0)


def turned_heads(value, gain, cosine, sine):
    normed = rms_scale(value, gain)
    return normed * cosine + pltpu.roll(normed, normed.shape[-1] // 2, 1) * sine


def visible_blocks(length, group):
    blocks = []
    for start in range(0, length, BLOCK):
        stop = min(start + BLOCK, length)
        heads = max(1, BLOCK // (stop - start))
        while group % heads:
            heads -= 1
        blocks.append((start, stop, stop, heads))
    return blocks


def softmax(scores):
    raised = jnp.exp(scores - jnp.max(scores, axis=0, keepdims=True))
    return raised * (1.0 / jnp.sum(raised, axis=0, keepdims=True))


def for_heads(low, high, heads, body):
    turns = 2 if heads == 1 and (high - low) % 2 == 0 else 1

    def turn(step, _):
        for i in range(turns):
            body(low + (step * turns + i) * heads)
        return 0

    count = (high - low) // (heads * turns)
    if count == 1:
        turn(0, 0)
    else:
        lax.fori_loop(0, count, turn, 0)


def head_columns(head, features):
    return pl.ds(pl.multiple_of(head * features, LANES), features)


def forward_kernel(
    line,
    heads,
    kv_heads,
    tokens_ref,
    cot_ref,
    in_ref,
    out_ref,
    picks_ref,
    gain1_ref,
    gain2_ref,
    query_gain_ref,
    key_gain_ref,
    cosine_ref,
    sine_ref,
    cot_all,
    in_all,
    out_all,
    picks_all,
    normed_all,
    projected_all,
    context_all,
    hidden_all,
    second_all,
    in_w,
    out_w,
    tokens,
    normed,
    projected,
    context,
    queries,
    keys,
    values,
    mixed,
    mixed_other,
    hidden,
    second,
    narrow_send,
    narrow_receive,
    wide_send,
    wide_receive,
    local,
    token_send,
    token_receive,
    mixed_send,
    mixed_receive,
    save_sem,
):
    batch, half, width = tokens_ref.shape
    length = 2 * half
    depth, out_width = in_ref.shape[0], out_ref.shape[1]
    features = query_gain_ref.shape[1]
    narrow = Spot(line, False)
    spots = [Spot(line, True, turned=i % 2 == 1) for i in range(batch)]
    spot = spots[0]
    x = spot.x
    spot.greet()
    slots = [
        (picks_ref, lambda block, side: picks_all.at[block]),
        (in_ref, lambda block, side: rows_at(in_w, block, depth)),
        (out_ref, lambda block, side: columns_at(out_w, block, out_width)),
    ]
    weights = [
        Spread(narrow, source, slot, narrow_send.at[i], narrow_receive.at[i], local.at[i])
        for i, (source, slot) in enumerate(slots)
    ]
    cots = [
        Spread(
            spots[i],
            cot_ref.at[i],
            lambda block, side, i=i: rows_at(cot_all.at[i, block], side, half),
            wide_send.at[i],
            wide_receive.at[i],
            local.at[3 + i],
        )
        for i in range(batch)
    ]
    early, late = weights[:2], weights[2]
    for tree in early:
        tree.begin()

    def token_copies(i):
        place = rows_at(tokens.at[i], x, half)
        return (
            pltpu.make_async_copy(tokens_ref.at[i], place, local.at[3 + batch + i]),
            spot.send(tokens_ref.at[i], place, token_send.at[i], token_receive.at[i], CROSS),
        )

    for i in range(batch):
        for copy in token_copies(i):
            copy.start()
    for tree in cots:
        tree.begin()

    def steps(step, _):
        for tree in early:
            tree.step(step)
        return 0

    lax.fori_loop(1, late.steps(), steps, 0)
    late.begin()
    for i in range(batch):
        mine, other = token_copies(i)
        mine.wait()
        other.wait_send()
        place = rows_at(tokens.at[i], 1 - x, half)
        spot.send(place, place, token_send.at[i], token_receive.at[i], CROSS).wait_recv()
    for i in range(batch):
        norm_rows(normed.at[i], tokens.at[i], gain1_ref)
    for tree in early:
        tree.finish()

    def save(source, target, index):
        return pltpu.make_async_copy(source, target, save_sem.at[index])

    saves = [save(in_w, in_all, 0), save(out_w, out_all, 1)]
    saves[0].start()

    def project(i, start, stop):
        for at in range(start, stop, CHUNK):
            projected[i, :, at : at + CHUNK] = jnp.dot(
                normed[i], in_w[:, at : at + CHUNK], preferred_element_type=jnp.float32
            )

    scale = features ** (-0.5)

    group = heads // kv_heads

    def prepare_keys(i):
        base = heads * features
        for head in range(kv_heads):
            at = base + head * features
            keys[head] = turned_heads(
                projected[i, :, at : at + features],
                key_gain_ref[...].astype(jnp.float32),
                cosine_ref[...],
                sine_ref[...],
            ).astype(jnp.bfloat16)
            at = base + (kv_heads + head) * features
            values[head] = projected[i, :, at : at + features].astype(jnp.bfloat16)

    def prepare_queries(i, shared):
        def prepare(member):
            columns = head_columns(shared * group + member, features)
            queries[member] = turned_heads(
                projected[i, :, columns], query_gain_ref[...].astype(jnp.float32), cosine_ref[...], sine_ref[...]
            ).astype(jnp.bfloat16)

        for_heads(0, group, 1, prepare)

    def attend(i, shared, start, stop, seen, at_once, low, high):
        count = stop - start

        def block(member):
            query = queries[pl.ds(member, at_once), start:stop, :].reshape(-1, features)
            scores = lax.dot_general(
                keys[shared, :seen, :],
                query,
                TRANSPOSED_RIGHT,
                preferred_element_type=jnp.float32,
            )
            rows = lax.dot_general(
                softmax(scores * scale).astype(jnp.bfloat16),
                values[shared, :seen, :],
                TRANSPOSED_LEFT,
                preferred_element_type=jnp.float32,
            ).astype(jnp.bfloat16)
            for j in range(at_once):
                columns = head_columns(shared * group + member + j, features)
                context[i, start:stop, columns] = rows[j * count : (j + 1) * count]

        for_heads(low, high, at_once, block)

    def mixed_copy(i):
        return spot.send(
            rows_at(mixed.at[i], 1 - x, half),
            mixed_other.at[i],
            mixed_send.at[i],
            mixed_receive.at[i],
            CROSS,
        )

    def mix(i, start, stop):
        for at in range(start, stop, CHUNK):
            mixed[i, :, at : at + CHUNK] = jnp.dot(
                context[i], out_w[:, at : at + CHUNK], preferred_element_type=jnp.float32
            ).astype(jnp.bfloat16)
        if stop == width:
            mixed_copy(i).start()

    def close(i):
        mixed_copy(i).wait()
        add_rows(
            hidden.at[i],
            [rows_at(tokens.at[i], x, half), rows_at(mixed.at[i], x, half), mixed_other.at[i]],
        )
        norm_rows(second.at[i], hidden.at[i], gain2_ref)

    later = [
        functools.partial(tree.step, step)
        for step in range(1, cots[0].steps())
        for tree in [late] + cots
        if step < tree.steps()
    ]
    final = late.steps() - 1

    def late_done():
        while later and len(later) > len(later_rest):
            later.pop(0)()
        late.finish()
        saves[1].start()

    later_rest = later[(final - 1) * (1 + batch) + 1 :]
    pending = []
    in_width = in_w.shape[1]
    parts = lambda size: [(at, min(at + 2 * CHUNK, size)) for at in range(0, size, 2 * CHUNK)]
    for i in range(batch):
        pending += [functools.partial(project, i, *part) for part in parts(in_width)]
        pending.append(functools.partial(prepare_keys, i))
        for shared in range(kv_heads):
            pending.append(functools.partial(prepare_queries, i, shared))
            for start, stop, seen, at_once in visible_blocks(length, group):
                share = max(at_once, group // 2)
                for low in range(0, group, share):
                    pending.append(
                        functools.partial(
                            attend, i, shared, start, stop, seen, at_once, low, low + share
                        )
                    )
        if i == 0:
            pending.append(late_done)
        pending += [functools.partial(mix, i, *part) for part in parts(width)]
    pending += [functools.partial(close, i) for i in range(batch)]
    while pending or later:
        for _ in range(-(-len(pending) // max(1, len(later)))):
            pending.pop(0)()
        if later:
            later.pop(0)()

    saves += [
        save(source, target, 2 + i)
        for i, (source, target) in enumerate(
            [
                (normed, normed_all),
                (projected, projected_all),
                (context, context_all),
                (hidden, hidden_all),
                (second, second_all),
            ]
        )
    ]
    for copy in saves[2:]:
        copy.start()
    for tree in cots:
        tree.finish()
    for copy in saves:
        copy.wait()


def run_forward(tokens, cot, weight_in, weight_out, picks, gains, tables, fsdp_count, kv_heads):
    line = fsdp_count // PLANE
    batch, half, width = tokens.shape
    length = 2 * half
    features = gains[2].shape[1]
    heads = weight_out.shape[0] // features
    in_shape = (weight_in.shape[0] * fsdp_count, weight_in.shape[1])
    out_shape = (weight_out.shape[0], weight_out.shape[1] * fsdp_count)
    wide, narrow = spread_count(line, True), spread_count(line, False)
    anywhere = pl.BlockSpec(memory_space=pl.ANY)
    inside = pl.BlockSpec(memory_space=pltpu.VMEM)
    shape = lambda dims, kind=jnp.bfloat16: jax.ShapeDtypeStruct(dims, kind)
    vmem = lambda *dims: pltpu.VMEM(dims, jnp.bfloat16)
    sem = lambda *dims: pltpu.SemaphoreType.DMA(dims)
    kept = (
        ((batch, length, width), jnp.bfloat16),
        ((batch, length, weight_in.shape[1]), jnp.float32),
        ((batch, length, heads * features), jnp.bfloat16),
        ((batch, half, width), jnp.float32),
        ((batch, half, width), jnp.bfloat16),
    )
    return pl.pallas_call(
        functools.partial(forward_kernel, line, heads, kv_heads),
        out_shape=(
            shape((batch, fsdp_count, length, width)),
            shape(in_shape),
            shape(out_shape),
            shape((fsdp_count, *picks.shape), picks.dtype),
            *(shape(*one) for one in kept),
        ),
        in_specs=[anywhere] * 5 + [inside] * 6,
        out_specs=(anywhere,) * 9,
        scratch_shapes=[
            vmem(*in_shape),
            vmem(*out_shape),
            vmem(batch, length, width),
            *(pltpu.VMEM(*one) for one in kept[:3]),
            vmem(heads // kv_heads, length, features),
            vmem(kv_heads, length, features),
            vmem(kv_heads, length, features),
            vmem(batch, length, width),
            vmem(batch, half, width),
            *(pltpu.VMEM(*one) for one in kept[3:]),
            sem(3, narrow[0]),
            sem(3, narrow[1]),
            sem(batch, wide[0]),
            sem(batch, wide[1]),
            sem(3 + 2 * batch),
            sem(batch),
            sem(batch),
            sem(batch),
            sem(batch),
            sem(7),
        ],
        compiler_params=pltpu.CompilerParams(
            collective_id=1, has_side_effects=True, vmem_limit_bytes=60 * MIB
        ),
    )(tokens, cot, weight_in, weight_out, picks, *gains, *tables)


def add_rows(target, sources):
    def body(step, _):
        rows = pl.ds(pl.multiple_of(step * 16, 16), 16)
        total = sources[0][rows, :].astype(jnp.float32)
        for source in sources[1:]:
            total = total + source[rows, :].astype(jnp.float32)
        target[rows, :] = total.astype(target.dtype)
        return 0

    lax.fori_loop(0, target.shape[0] // 16, body, 0)


class Collect:
    def __init__(self, spot, part, total, cores, firsts, rights, lefts, send, receive):
        self.spot = spot
        self.part = part
        self.total = total
        self.places = {CORE: cores, FIRST: firsts, RIGHT: rights, LEFT: lefts}
        line = spot.line
        self.base = {CORE: 0, FIRST: 2 * line, RIGHT: 3 * line, LEFT: 4 * line}
        self.sends = send
        self.receives = receive

    def own(self, first, z):
        return self.part(*self.spot.block(self.spot.core, first, 0, z))

    def copy(self, kind, first, z):
        spot = self.spot
        number = first * spot.line + z if kind == CORE else z
        source = self.part(*spot.block(1 - spot.core, first, 0, z)) if kind == CORE else self.own(first, z)
        at = self.base[kind] + number
        return spot.send(
            source, self.places[kind].at[number], self.sends.at[at], self.receives.at[at], kind
        )

    def arrived(self, kind, number):
        place = self.places[kind].at[number]
        at = self.base[kind] + number
        self.spot.send(place, place, self.sends.at[0], self.receives.at[at], CORE).wait_recv()
        return place

    def begin(self, z):
        for first in (1, 0):
            self.copy(CORE, first, z).start()

    def to_first(self, z):
        add_rows(self.own(1, z), [self.own(1, z), self.arrived(CORE, self.spot.line + z)])
        self.copy(FIRST, 1, z).start()

    def summands(self, z):
        return [self.own(0, z), self.arrived(CORE, z), self.arrived(FIRST, z)]

    def cross(self):
        for step in reversed(range(self.spot.line)):
            for zz, valid in self.spot.order(step):
                when(valid, functools.partial(self.to_first, zz))

    def onward(self, kind, zz):
        spot = self.spot
        sources = self.summands(zz)
        target = self.own(0, zz)
        behind = spot.z > 0 if kind == RIGHT else spot.z + 1 < spot.line
        when(behind, lambda: add_rows(target, sources + [self.arrived(kind, zz)]))
        when(jnp.logical_not(behind), lambda: add_rows(target, sources))
        self.copy(kind, 0, zz).start()

    def last(self):
        z, line = self.spot.z, self.spot.line
        sources = self.summands(z)

        def end(kinds):
            add_rows(self.total, sources + [self.arrived(kind, z) for kind in kinds])

        when(z == 0, lambda: end([LEFT]))
        when(z == line - 1, lambda: end([RIGHT]))
        when(jnp.logical_and(z > 0, z < line - 1), lambda: end([RIGHT, LEFT]))

    def finish(self):
        spot = self.spot
        for zz in range(spot.line):
            for first in (0, 1):
                self.copy(CORE, first, zz).wait_send()
            self.copy(FIRST, 1, zz).wait_send()
            when(zz > spot.z, lambda: self.copy(RIGHT, 0, zz).wait_send())
            when(zz < spot.z, lambda: self.copy(LEFT, 0, zz).wait_send())

    def tasks(self):
        spot = self.spot
        work = []
        for step in reversed(range(1, spot.line)):
            for kind, (zz, valid) in zip((LEFT, RIGHT), spot.order(step)):
                action = functools.partial(self.onward, kind, zz)
                work.append(functools.partial(when, valid, action))
        return work + [self.last, self.finish]


def collect_scratch(line, shape):
    counts = (2 * line, line, line, line)
    return [pltpu.VMEM((count, *shape), jnp.bfloat16) for count in counts] + [
        pltpu.SemaphoreType.DMA((5 * line,)),
        pltpu.SemaphoreType.DMA((5 * line,)),
    ]


def norm_back(value, grads, gain):
    scale = lax.rsqrt(jnp.mean(value * value, axis=-1, keepdims=True) + EPSILON)
    unit = value * scale
    scaled = grads * gain
    back = scale * (scaled - unit * jnp.mean(scaled * unit, axis=-1, keepdims=True))
    return back, grads * unit


def backward_kernel(
    line,
    heads,
    kv_heads,
    cot_ref,
    totals_ref,
    hidden_ref,
    projected_ref,
    context_ref,
    in_ref,
    out_ref,
    tokens_ref,
    gain1_ref,
    gain2_ref,
    query_gain_ref,
    key_gain_ref,
    cosine_ref,
    sine_ref,
    block_out,
    input_grad,
    grads_all,
    out_total,
    gain_grads,
    elements,
    cots,
    tokens,
    kept,
    result,
    context,
    hidden_grads,
    context_grads,
    grads,
    normed_grads,
    normed_other,
    out_rows,
    in_rows,
    queries_f,
    shared_f,
    queries,
    query_grads,
    sums,
    out_grads,
    cores,
    firsts,
    rights,
    lefts,
    tree_send,
    tree_receive,
    load_sem,
    row_sem,
    head_sem,
    save_sem,
    hidden_send,
    hidden_receive,
    normed_send,
    normed_receive,
):
    batch, half, width = cot_ref.shape
    length = 2 * half
    features = query_gain_ref.shape[1]
    group = heads // kv_heads
    base = heads * features
    out_width = out_total.shape[1]
    narrow, spot = Spot(line, False), Spot(line, True)
    x = spot.x
    scale = features ** (-0.5)

    def load(source, target, index):
        return pltpu.make_async_copy(source, target, load_sem.at[index])

    def element_loads(i):
        return [
            load(hidden_ref.at[i], elements.at[0], 0),
            load(totals_ref.at[i, OUTPUT], elements.at[1], 1),
            load(totals_ref.at[i, BACK], elements.at[2], 2),
        ]

    first_loads = [load(cot_ref, cots, 3), load(tokens_ref, tokens, 4)] + [
        load(context_ref.at[i], rows_at(context, i, length), 5 + i) for i in range(batch)
    ]
    for copy in element_loads(0) + first_loads:
        copy.start()

    def out_load(step):
        slot = lax.rem(step, 2)
        return pltpu.make_async_copy(
            rows_at(out_ref, step, CHUNK), out_rows.at[slot], row_sem.at[0, slot]
        )

    def in_load(step):
        slot = lax.rem(step, 2)
        return pltpu.make_async_copy(
            rows_at(in_ref, step, CHUNK), in_rows.at[slot], row_sem.at[1, slot]
        )

    out_steps, in_steps = out_ref.shape[0] // CHUNK, in_ref.shape[0] // CHUNK
    for step in range(2):
        out_load(step).start()
        in_load(step).start()
    gain_grads[...] = jnp.zeros_like(gain_grads)
    spot.greet()
    for copy in first_loads:
        copy.wait()

    def result_save(i, target):
        return pltpu.make_async_copy(result.at[i], target.at[i], save_sem.at[i])

    def half_copy(ref, i, side):
        return ref.at[pl.ds(pl.multiple_of(i * length + side * half, 16), half)]

    def hidden_copy(i):
        place = half_copy(hidden_grads, i, x)
        return spot.send(place, place, hidden_send.at[i], hidden_receive.at[i], CROSS)

    for i in range(batch):
        for copy in element_loads(i):
            copy.wait()

        def elementwise(step, _):
            rows = pl.ds(pl.multiple_of(step * 16, 16), 16)
            value = elements[0, rows, :]
            result[i, rows, :] = (value + elements[1, rows, :]).astype(jnp.bfloat16)
            back, gain_rows = norm_back(value, elements[2, rows, :], gain2_ref[...].astype(jnp.float32))
            gain_grads[1:2, :] += jnp.sum(gain_rows, axis=0, keepdims=True)
            total = cots[i, rows, :].astype(jnp.float32) + back
            kept[i, rows, :] = total
            place = pl.ds(pl.multiple_of(i * length + x * half + step * 16, 16), 16)
            hidden_grads[place, :] = total.astype(jnp.bfloat16)
            return 0

        lax.fori_loop(0, half // 16, elementwise, 0)
        hidden_copy(i).start()
        result_save(i, block_out).start()
        if i + 1 < batch:
            for copy in element_loads(i + 1):
                copy.start()
    for i in range(batch):
        hidden_copy(i).wait_send()
        place = half_copy(hidden_grads, i, 1 - x)
        spot.send(place, place, hidden_send.at[i], hidden_receive.at[i], CROSS).wait_recv()

    def context_step(step, _):
        out_load(step).wait()
        columns = pl.ds(pl.multiple_of(step * CHUNK, LANES), CHUNK)
        context_grads[:, columns] = lax.dot_general(
            hidden_grads[...],
            out_rows[lax.rem(step, 2)],
            TRANSPOSED_RIGHT,
            preferred_element_type=jnp.float32,
        ).astype(jnp.bfloat16)
        when(step + 2 < out_steps, lambda: out_load(step + 2).start())
        for start in range(0, width, CHUNK):
            out_grads[pl.ds(pl.multiple_of(step * CHUNK, 16), CHUNK), start : start + CHUNK] = (
                lax.dot_general(
                    context[:, columns],
                    hidden_grads[:, start : start + CHUNK],
                    TRANSPOSED_LEFT,
                    preferred_element_type=jnp.float32,
                ).astype(jnp.bfloat16)
            )
        return 0

    lax.fori_loop(0, out_steps, context_step, 0)
    tree = Collect(
        narrow,
        lambda block, side: columns_at(out_grads, block, out_width),
        out_total,
        cores,
        firsts,
        rights,
        lefts,
        tree_send,
        tree_receive,
    )
    for z in range(line):
        tree.begin(z)
    tree.cross()
    work = tree.tasks()

    def turns():
        return [(i, shared) for i in range(batch) for shared in range(kv_heads)]

    def head_loads(index):
        i, shared = turns()[index]
        slot = index % 2
        return [
            pltpu.make_async_copy(
                projected_ref.at[i, :, pl.ds(shared * group * features, group * features)],
                queries_f.at[slot],
                head_sem.at[slot, 0],
            )
        ] + [
            pltpu.make_async_copy(
                projected_ref.at[i, :, pl.ds(base + (shared + j * kv_heads) * features, features)],
                shared_f.at[slot, j],
                head_sem.at[slot, 1 + j],
            )
            for j in range(2)
        ]

    for copy in head_loads(0):
        copy.start()

    def turn_back(grads_in):
        return grads_in * cosine_ref[...] + pltpu.roll(
            grads_in * sine_ref[...], features // 2, 1
        )

    def attend(index):
        i, shared = turns()[index]
        slot = index % 2
        for copy in head_loads(index):
            copy.wait()
        if index + 1 < len(turns()):
            for copy in head_loads(index + 1):
                copy.start()
        top = i * length
        key = turned_heads(
            shared_f[slot, 0], key_gain_ref[...].astype(jnp.float32), cosine_ref[...], sine_ref[...]
        ).astype(jnp.bfloat16)
        queries[group] = key
        queries[group + 1] = shared_f[slot, 1].astype(jnp.bfloat16)
        sums[...] = jnp.zeros_like(sums)

        def columns_of(member):
            return pl.ds(pl.multiple_of(member * features, LANES), features)

        def prepare(member):
            queries[member] = turned_heads(
                queries_f[slot, :, columns_of(member)],
                query_gain_ref[...].astype(jnp.float32),
                cosine_ref[...],
                sine_ref[...],
            ).astype(jnp.bfloat16)

        for_heads(0, group, 1, prepare)
        for start, stop, seen, at_once in visible_blocks(length, group):
            count = stop - start

            def block(member):
                query = queries[pl.ds(member, at_once), start:stop, :].reshape(-1, features)
                keys, values = queries[group, :seen, :], queries[group + 1, :seen, :]
                out_grad = jnp.concatenate(
                    [
                        context_grads[
                            top + start : top + stop,
                            head_columns(shared * group + member + j, features),
                        ]
                        for j in range(at_once)
                    ],
                    axis=0,
                )
                scores = lax.dot_general(
                    keys, query, TRANSPOSED_RIGHT, preferred_element_type=jnp.float32
                )
                shares = softmax(scores * scale)
                share_grads = lax.dot_general(
                    values, out_grad, TRANSPOSED_RIGHT, preferred_element_type=jnp.float32
                )
                sums[1, :seen, :] += jnp.dot(
                    shares.astype(jnp.bfloat16), out_grad, preferred_element_type=jnp.float32
                )
                inner = jnp.sum(shares * share_grads, axis=0, keepdims=True)
                score_grads = (shares * (share_grads - inner)).astype(jnp.bfloat16)
                rows = scale * lax.dot_general(
                    score_grads, keys, TRANSPOSED_LEFT, preferred_element_type=jnp.float32
                )
                query_grads[pl.ds(member, at_once), start:stop, :] = rows.reshape(
                    at_once, count, features
                )
                sums[0, :seen, :] += jnp.dot(
                    score_grads, query, preferred_element_type=jnp.float32
                )

            for_heads(0, group, at_once, block)

        def finish(member):
            back, gain_rows = norm_back(
                queries_f[slot, :, columns_of(member)],
                turn_back(query_grads[member]),
                query_gain_ref[...].astype(jnp.float32),
            )
            gain_grads[2:3, :features] += jnp.sum(gain_rows, axis=0, keepdims=True)
            grads[top : top + length, head_columns(shared * group + member, features)] = (
                back.astype(jnp.bfloat16)
            )

        for_heads(0, group, 1, finish)
        back, gain_rows = norm_back(
            shared_f[slot, 0], turn_back(sums[0] * scale), key_gain_ref[...].astype(jnp.float32)
        )
        gain_grads[3:4, :features] += jnp.sum(gain_rows, axis=0, keepdims=True)
        at = base + shared * features
        grads[top : top + length, at : at + features] = back.astype(jnp.bfloat16)
        at += kv_heads * features
        grads[top : top + length, at : at + features] = sums[1].astype(jnp.bfloat16)

    for index in range(len(turns())):
        attend(index)
        for _ in range(2):
            if work:
                work.pop(0)()

    saves = [
        pltpu.make_async_copy(rows_at(grads, i, length), grads_all.at[i], save_sem.at[batch + i])
        for i in range(batch)
    ]
    for copy in saves:
        copy.start()

    def normed_step(step, _):
        in_load(step).wait()
        columns = pl.ds(pl.multiple_of(step * CHUNK, LANES), CHUNK)
        normed_grads[:, columns] = lax.dot_general(
            grads[...],
            in_rows[lax.rem(step, 2)],
            TRANSPOSED_RIGHT,
            preferred_element_type=jnp.float32,
        ).astype(jnp.bfloat16)
        when(step + 2 < in_steps, lambda: in_load(step + 2).start())
        return 0

    lax.fori_loop(0, in_steps, normed_step, 0)

    def normed_copy(i):
        return spot.send(
            half_copy(normed_grads, i, 1 - x),
            normed_other.at[i],
            normed_send.at[i],
            normed_receive.at[i],
            CROSS,
        )

    for i in range(batch):
        normed_copy(i).start()
    while work:
        work.pop(0)()
    for i in range(batch):
        normed_copy(i).wait()
        result_save(i, block_out).wait()

        def input_rows(step, _):
            rows = pl.ds(pl.multiple_of(step * 16, 16), 16)
            place = pl.ds(pl.multiple_of(i * length + x * half + step * 16, 16), 16)
            total = normed_grads[place, :].astype(jnp.float32) + normed_other[i, rows, :].astype(
                jnp.float32
            )
            back, gain_rows = norm_back(
                tokens[i, rows, :].astype(jnp.float32), total, gain1_ref[...].astype(jnp.float32)
            )
            gain_grads[0:1, :] += jnp.sum(gain_rows, axis=0, keepdims=True)
            result[i, rows, :] = (kept[i, rows, :] + back).astype(jnp.bfloat16)
            return 0

        lax.fori_loop(0, half // 16, input_rows, 0)
        result_save(i, input_grad).start()
    for i in range(batch):
        result_save(i, input_grad).wait()
    for copy in saves:
        copy.wait()


def run_backward(
    cot, totals, hidden, projected, context, in_full, out_full, tokens, gains, tables, fsdp_count, kv_heads
):
    line = fsdp_count // PLANE
    batch, half, width = tokens.shape
    length = 2 * half
    features = gains[2].shape[1]
    heads = out_full.shape[0] // features
    group = heads // kv_heads
    in_width, out_depth = in_full.shape[1], out_full.shape[0]
    out_shape = (out_depth, width // fsdp_count)
    anywhere = pl.BlockSpec(memory_space=pl.ANY)
    inside = pl.BlockSpec(memory_space=pltpu.VMEM)
    vmem = lambda *dims: pltpu.VMEM(dims, jnp.bfloat16)
    wide = lambda *dims: pltpu.VMEM(dims, jnp.float32)
    sem = lambda *dims: pltpu.SemaphoreType.DMA(dims)
    rows = batch * length
    return pl.pallas_call(
        functools.partial(backward_kernel, line, heads, kv_heads),
        out_shape=(
            jax.ShapeDtypeStruct((batch, half, width), jnp.bfloat16),
            jax.ShapeDtypeStruct((batch, half, width), jnp.bfloat16),
            jax.ShapeDtypeStruct((batch, length, in_width), jnp.bfloat16),
            jax.ShapeDtypeStruct(out_shape, jnp.float32),
            jax.ShapeDtypeStruct((8, width), jnp.float32),
        ),
        in_specs=[anywhere] * 8 + [inside] * 6,
        out_specs=(anywhere, anywhere, anywhere, inside, inside),
        scratch_shapes=[
            wide(3, half, width),
            vmem(batch, half, width),
            vmem(batch, half, width),
            wide(batch, half, width),
            vmem(batch, half, width),
            vmem(rows, out_depth),
            vmem(rows, width),
            vmem(rows, out_depth),
            vmem(rows, in_width),
            vmem(rows, width),
            vmem(batch, half, width),
            vmem(2, CHUNK, width),
            vmem(2, CHUNK, in_width),
            wide(2, length, group * features),
            wide(2, 2, length, features),
            vmem(group + 2, length, features),
            wide(group, length, features),
            wide(2, length, features),
            vmem(out_depth, width),
            *collect_scratch(line, out_shape),
            sem(5 + batch),
            sem(2, 2),
            sem(2, 3),
            sem(2 * batch),
            sem(batch),
            sem(batch),
            sem(batch),
            sem(batch),
        ],
        compiler_params=pltpu.CompilerParams(
            collective_id=3, has_side_effects=True, vmem_limit_bytes=62 * MIB
        ),
    )(cot, totals, hidden, projected, context, in_full, out_full, tokens, *gains, *tables)


def gradients_kernel(
    line,
    normed,
    grads,
    gains_ref,
    xe_ref,
    ce_ref,
    act_ref,
    dgate_ref,
    dup_ref,
    in_total,
    gains_all,
    gate_total,
    up_total,
    down_total,
    parts,
    cores,
    firsts,
    rights,
    lefts,
    tree_send,
    tree_receive,
    gain_send,
    gain_receive,
    gain_local,
    wide_rows,
    slim_rows,
    gate_sum,
    up_sum,
    down_sum,
    load_sem,
    save_sem,
):
    narrow, spot = Spot(line, False), Spot(line, True)
    experts, count, _ = xe_ref.shape
    share = wide_rows.shape[1]
    turns = count // share
    pieces = [
        (expert, kind, turn)
        for expert in range(experts)
        for kind in range(2)
        for turn in range(turns)
    ]

    def loads(index):
        expert, kind, turn = pieces[index]
        slot = index % 2
        rows = pl.ds(turn * share, share)
        slim = (dgate_ref, dup_ref) if kind == 0 else (act_ref,)
        return [
            pltpu.make_async_copy(
                (xe_ref, ce_ref)[kind].at[expert, rows], wide_rows.at[slot], load_sem.at[slot, 0]
            )
        ] + [
            pltpu.make_async_copy(
                ref.at[expert, rows], slim_rows.at[slot, i], load_sem.at[slot, 1 + i]
            )
            for i, ref in enumerate(slim)
        ]

    def saves(expert, kind):
        pairs = ((gate_sum, gate_total), (up_sum, up_total))
        if kind:
            return [pltpu.make_async_copy(down_sum, down_total.at[expert], save_sem.at[2])]
        return [
            pltpu.make_async_copy(source, target.at[expert], save_sem.at[i])
            for i, (source, target) in enumerate(pairs)
        ]

    for copy in loads(0):
        copy.start()
    spot.greet()
    gains = Spread(
        spot,
        gains_ref,
        lambda block, half: gains_all.at[block, half],
        gain_send,
        gain_receive,
        gain_local.at[0],
    )
    gains.begin()
    depth, width = in_total.shape
    tree = Collect(
        narrow,
        lambda block, half: rows_at(parts, block, depth),
        in_total,
        cores,
        firsts,
        rights,
        lefts,
        tree_send,
        tree_receive,
    )
    chunk = PLANE * depth

    def plane(step, _):
        z = lax.rem(narrow.z + 1 + step, line)
        columns = pl.ds(pl.multiple_of(z * chunk, LANES), chunk)
        for start in range(0, width, CHUNK):
            parts[pl.ds(pl.multiple_of(z * chunk, 16), chunk), start : start + CHUNK] = (
                lax.dot_general(
                    normed[:, columns],
                    grads[:, start : start + CHUNK],
                    TRANSPOSED_LEFT,
                    preferred_element_type=jnp.float32,
                ).astype(jnp.bfloat16)
            )
        tree.begin(z)
        return 0

    lax.fori_loop(0, line, plane, 0)

    def piece(index):
        expert, kind, turn = pieces[index]
        slot = index % 2
        for copy in loads(index):
            copy.wait()
        if index + 1 < len(pieces):
            for copy in loads(index + 1):
                copy.start()
        if turn == 0 and expert:
            for copy in saves(expert - 1, kind):
                copy.wait()
        size = wide_rows.shape[2] // 4

        def add(target, place, left, right):
            product = lax.dot_general(
                left, right, TRANSPOSED_LEFT, preferred_element_type=jnp.float32
            )
            if turn:
                product = target[place] + product
            target[place] = product

        def part(step, _):
            at = pl.ds(pl.multiple_of(step * size, LANES), size)
            if kind:
                add(down_sum, (slice(None), at), slim_rows[slot, 0], wide_rows[slot, :, at])
            else:
                for i, target in enumerate((gate_sum, up_sum)):
                    add(target, (at, slice(None)), wide_rows[slot, :, at], slim_rows[slot, i])
            return 0

        lax.fori_loop(0, 4, part, 0)
        if turn == turns - 1:
            for copy in saves(expert, kind):
                copy.start()

    tree.cross()
    work = tree.tasks()
    steps = list(range(1, gains.steps()))
    filler = list(range(len(pieces)))
    while work or filler:
        for _ in range(2 if len(filler) > len(work) else 1):
            if filler:
                piece(filler.pop(0))
        if work:
            work.pop(0)()
        if steps:
            gains.step(steps.pop(0))
    gains.finish()
    for copy in saves(experts - 1, 0) + saves(experts - 1, 1):
        copy.wait()


def run_gradients(normed, grads, gains, expert_rows, fsdp_count):
    line = fsdp_count // PLANE
    width = grads.shape[1]
    experts, count, depth = expert_rows[0].shape
    units = expert_rows[2].shape[2]
    share = 2 * CHUNK if count % (2 * CHUNK) == 0 else count // (2 * line)
    shape = (normed.shape[1] // fsdp_count, width)
    sends, receives = spread_count(line, True)
    inside = pl.BlockSpec(memory_space=pltpu.VMEM)
    anywhere = pl.BlockSpec(memory_space=pl.ANY)
    return pl.pallas_call(
        functools.partial(gradients_kernel, line),
        out_shape=(
            jax.ShapeDtypeStruct(shape, jnp.float32),
            jax.ShapeDtypeStruct((fsdp_count, 2, *gains.shape), jnp.float32),
            jax.ShapeDtypeStruct((experts, depth, units), jnp.float32),
            jax.ShapeDtypeStruct((experts, depth, units), jnp.float32),
            jax.ShapeDtypeStruct((experts, units, depth), jnp.float32),
        ),
        in_specs=[inside, inside] + [anywhere] * 6,
        out_specs=(inside,) + (anywhere,) * 4,
        scratch_shapes=[
            pltpu.VMEM((normed.shape[1], width), jnp.bfloat16),
            *collect_scratch(line, shape),
            pltpu.SemaphoreType.DMA((sends,)),
            pltpu.SemaphoreType.DMA((receives,)),
            pltpu.SemaphoreType.DMA((1,)),
            pltpu.VMEM((2, share, depth), jnp.bfloat16),
            pltpu.VMEM((2, 2, share, units), jnp.bfloat16),
            pltpu.VMEM((depth, units), jnp.float32),
            pltpu.VMEM((depth, units), jnp.float32),
            pltpu.VMEM((units, depth), jnp.float32),
            pltpu.SemaphoreType.DMA((2, 3)),
            pltpu.SemaphoreType.DMA((3,)),
        ],
        compiler_params=pltpu.CompilerParams(
            collective_id=4, has_side_effects=True, vmem_limit_bytes=60 * MIB
        ),
    )(normed, grads, gains, *expert_rows)


def experts_kernel(
    line,
    slots,
    own_ref,
    cot_ref,
    info_ref,
    gate_ref,
    up_ref,
    down_ref,
    all_ref,
    total_ref,
    xe_all,
    ce_all,
    act_all,
    dgate_all,
    dup_all,
    part,
    cores,
    seconds,
    firsts,
    ends,
    hidden_w,
    down_w,
    x_rows,
    c_rows,
    xe,
    ce,
    acts,
    dgates,
    dups,
    hidden_grads,
    picks,
    weigh,
    rows,
    stage,
    inbox,
    outbox,
    summed,
    tree_send,
    tree_receive,
    tree_local,
    load_sem,
    save_sem,
    stage_sem,
    inbox_sem,
    outbox_sem,
    total_sem,
    weight_sem,
    core_receive,
    second_receive,
    first_receive,
    end_receive,
):
    spot = Spot(line, True)
    z, core = spot.z, spot.core
    batch, half, width = own_ref.shape
    length = 2 * half
    units = down_ref.shape[1]
    groups = batch * line
    weights = [
        pltpu.make_async_copy(source, target, weight_sem.at[i])
        for i, (source, target) in enumerate(
            [(down_ref, down_w)]
            + [(gate_ref.at[e], hidden_w.at[e, :, pl.ds(0, units)]) for e in range(2)]
            + [(up_ref.at[e], hidden_w.at[e, :, pl.ds(units, units)]) for e in range(2)]
        )
    ]
    for copy in weights:
        copy.start()
    rows[...] = jnp.zeros_like(rows)
    spot.greet()

    def half_of(ref, index):
        return rows_at(ref, index, half)

    trees = [
        Spread(
            spot,
            own_ref.at[i],
            lambda block, side, i=i: half_of(all_ref.at[i, block], side),
            tree_send.at[i],
            tree_receive.at[i],
            tree_local.at[i],
        )
        for i in range(batch)
    ]
    run_trees(trees[:1])
    for tree in trees[1:]:
        tree.begin()
    for copy in weights:
        copy.wait()

    def plane_of(group):
        turn = lax.rem(group, line)
        step = lax.div(turn, 2)
        return jnp.where(lax.rem(turn, 2) == 0, step, line - 1 - step)

    def load_group(group, member):
        at = lax.div(group, line)
        sequence = plane_of(group) * PLANE + member
        slot = member % 2
        return [
            pltpu.make_async_copy(all_ref.at[at, sequence], x_rows.at[slot], load_sem.at[0, slot]),
            pltpu.make_async_copy(cot_ref.at[at, sequence], c_rows.at[slot], load_sem.at[1, slot]),
        ]

    def saves(group):
        to = lambda ref, expert: rows_at(ref.at[expert], group, PLANE * slots)
        pairs = ((xe, xe_all), (ce, ce_all), (acts, act_all), (dgates, dgate_all), (dups, dup_all))
        return [
            pltpu.make_async_copy(source.at[expert], to(target, expert), save_sem.at[2 * i + expert])
            for i, (source, target) in enumerate(pairs)
            for expert in range(2)
        ]

    def staged(unit, y, mine):
        slot = y * 2 + mine
        if mine:
            return pltpu.make_async_copy(stage.at[slot], part.at[unit, y], stage_sem.at[slot])
        return spot.send(
            stage.at[slot], cores.at[unit, y], stage_sem.at[slot], core_receive.at[unit, y], CORE
        )

    def combine(unit, y):
        for mine in range(2):
            member = y * 2 + (core if mine else 1 - core)
            for start in range(0, width, CHUNK):
                stage[y * 2 + mine, :, start : start + CHUNK] = lax.dot_general(
                    picks[member],
                    rows[member, :, start : start + CHUNK],
                    TRANSPOSED_LEFT,
                    preferred_element_type=jnp.float32,
                ).astype(jnp.bfloat16)
            staged(unit, y, mine).start()

    def pick(group, member):
        slot = member % 2
        for copy in load_group(group, member):
            copy.wait()
        if member + 1 < PLANE:
            for copy in load_group(group, member + 1):
                copy.start()
        sequence = plane_of(group) * PLANE + member
        info = info_ref[lax.div(group, line) * line * PLANE + sequence]
        places = lax.broadcasted_iota(jnp.int32, (2 * LANES, length), 0)
        lower = places < LANES
        ranks = jnp.where(lower, info[0:1], info[1:2] + float(LANES)).astype(jnp.int32)
        some = jnp.where(lower, info[0:1], info[1:2]) >= 0.0
        hot = jnp.logical_and(ranks == places, some)
        chosen = hot.astype(jnp.float32).astype(jnp.bfloat16)
        picks[member] = chosen
        shares = jnp.where(hot, jnp.where(lower, info[2:3], info[3:4]), 0.0)
        column = jnp.sum(shares, axis=1, keepdims=True)
        here = pl.ds(member * slots, slots)
        for expert in range(2):
            weigh[expert, here, :] = jnp.broadcast_to(
                column[expert * LANES : expert * LANES + slots], (slots, LANES)
            )
        for source, target in ((x_rows, xe), (c_rows, ce)):
            for start in range(0, width, CHUNK):
                selected = jnp.dot(
                    chosen,
                    source[slot, :, start : start + CHUNK],
                    preferred_element_type=jnp.float32,
                ).astype(jnp.bfloat16)
                for expert in range(2):
                    target[expert, here, start : start + CHUNK] = selected[
                        expert * LANES : expert * LANES + slots
                    ]

    def keep(expert, product, start):
        at = pl.ds(expert * LANES, slots)
        for one in range(PLANE):
            rows[one, at, start : start + CHUNK] = product[one * slots : (one + 1) * slots].astype(
                jnp.bfloat16
            )

    def forward(expert):
        hidden = jnp.dot(xe[expert], hidden_w[expert], preferred_element_type=jnp.float32)
        gate, up = hidden[:, :units], hidden[:, units:]
        sigmoid = jax.nn.sigmoid(gate)
        silu = gate * sigmoid
        scale = weigh[expert, :, 0:1]
        acts[expert] = (silu * up * scale).astype(jnp.bfloat16)
        act_grads = scale * lax.dot_general(
            ce[expert], down_w[expert], TRANSPOSED_RIGHT, preferred_element_type=jnp.float32
        )
        gate_grads = (act_grads * up * (sigmoid * (1.0 + gate * (1.0 - sigmoid)))).astype(
            jnp.bfloat16
        )
        up_grads = (act_grads * silu).astype(jnp.bfloat16)
        dgates[expert] = gate_grads
        dups[expert] = up_grads
        hidden_grads[expert, :, :units] = gate_grads
        hidden_grads[expert, :, units:] = up_grads
        for start in range(0, width, CHUNK):
            keep(
                expert,
                jnp.dot(
                    acts[expert],
                    down_w[expert, :, start : start + CHUNK],
                    preferred_element_type=jnp.float32,
                ),
                start,
            )

    def backward(expert):
        for start in range(0, width, CHUNK):
            keep(
                expert,
                lax.dot_general(
                    hidden_grads[expert],
                    hidden_w[expert, start : start + CHUNK, :],
                    TRANSPOSED_RIGHT,
                    preferred_element_type=jnp.float32,
                ),
                start,
            )

    units_all = 2 * groups

    def inside(unit):
        return jnp.logical_and(unit >= 0, unit < units_all)

    def second_send(unit, tensor, first):
        slot = tensor * 2 + first
        return spot.send(
            outbox.at[slot],
            seconds.at[unit, first],
            outbox_sem.at[slot],
            second_receive.at[unit, first],
            SECOND,
        )

    def first_send(unit, tensor):
        slot = 4 + tensor
        return spot.send(
            outbox.at[slot], firsts.at[unit], outbox_sem.at[slot], first_receive.at[unit], FIRST
        )

    def end_send(unit, tensor, kind):
        slot = 6 + tensor * 2 + kind
        return spot.send(
            outbox.at[slot],
            ends.at[unit, kind],
            outbox_sem.at[slot],
            end_receive.at[unit, kind],
            kind,
        )

    def received(place, semaphore):
        spot.send(place, place, outbox_sem.at[0], semaphore, CORE).wait_recv()

    def sources(unit, first, second):
        y, x = spot.side(core, first, second)
        return [half_of(part.at[unit, y], x), half_of(cores.at[unit, y], x)]

    def load(source, slot):
        return pltpu.make_async_copy(source, inbox.at[slot], inbox_sem.at[slot])

    def add_inbox(target, base, numbers):
        add_rows(target, [inbox.at[base + i] for i in numbers])

    def end_roles(half_step, delay):
        unit = half_step - 3 - delay
        plane = plane_of(lax.div(jnp.maximum(unit, 0), 2))
        valid = inside(unit)
        right = jnp.logical_and(valid, jnp.logical_and(z < plane, delay == z))
        left = jnp.logical_and(valid, jnp.logical_and(z > plane, delay == line - 1 - z))
        last = jnp.logical_and(
            valid,
            jnp.logical_and(z == plane, delay == jnp.maximum(plane, line - 1 - plane)),
        )
        return unit, right, left, last

    def end_task(half_step, delay, parity):
        tensor = (parity - 3 - delay) % 2
        unit, right, left, last = end_roles(half_step, delay)
        some = jnp.logical_or(right, jnp.logical_or(left, last))
        from_left = jnp.logical_and(jnp.logical_or(right, last), z > 0)
        from_right = jnp.logical_and(jnp.logical_or(left, last), z + 1 < line)
        present = ((RIGHT, from_left), (LEFT, from_right))

        def fetch(base):
            def action():
                received(seconds.at[unit, 0], second_receive.at[unit, 0])
                received(firsts.at[unit], first_receive.at[unit])
                inputs = sources(unit, 0, 0) + [seconds.at[unit, 0], firsts.at[unit]]
                for i, source in enumerate(inputs):
                    load(source, base + i).start()
                for kind, there in present:

                    def arrive():
                        received(ends.at[unit, kind], end_receive.at[unit, kind])
                        load(ends.at[unit, kind], base + 4 + kind).start()

                    when(there, arrive)

            when(some, action)

        def add(base):
            def action():
                inputs = sources(unit, 0, 0) + [seconds.at[unit, 0], firsts.at[unit]]
                for i, source in enumerate(inputs):
                    load(source, base + i).wait()
                for kind, there in present:
                    when(there, lambda: load(ends.at[unit, kind], base + 4 + kind).wait())
                summands = list(range(4))
                for kind, chosen, behind in ((RIGHT, right, z > 0), (LEFT, left, z + 1 < line)):

                    def onward():
                        target = outbox.at[6 + tensor * 2 + kind]
                        when(behind, lambda: add_inbox(target, base, summands + [4 + kind]))
                        when(jnp.logical_not(behind), lambda: add_inbox(target, base, summands))
                        end_send(unit, tensor, kind).start()

                    when(chosen, onward)

                @pl.when(last)
                def _():
                    both = jnp.logical_and(from_left, from_right)
                    when(both, lambda: add_inbox(summed, base, summands + [4, 5]))
                    for kind, there in present:
                        when(
                            jnp.logical_and(there, jnp.logical_not(both)),
                            lambda: add_inbox(summed, base, summands + [4 + kind]),
                        )
                    copy = pltpu.make_async_copy(
                        summed, total_ref.at[lax.div(unit, 2 * line), tensor], total_sem.at[0]
                    )
                    copy.start()
                    copy.wait()

            when(some, action)

        return fetch, add

    def retire(half_step, parity):
        before = half_step - 2
        now, then = (parity - 1) % 2, parity
        when(
            inside(before - 1),
            lambda: [second_send(before - 1, now, first).wait_send() for first in range(2)],
        )
        when(inside(before - 2), lambda: first_send(before - 2, then).wait_send())
        for delay in range(line):
            unit, right, left, _ = end_roles(before, delay)
            tensor = (parity - 3 - delay) % 2
            when(right, lambda: end_send(unit, tensor, RIGHT).wait_send())
            when(left, lambda: end_send(unit, tensor, LEFT).wait_send())

    def simple_task(valid, ready, inputs, slot, send):
        def fetch(base):
            def action():
                ready()
                for i, source in enumerate(inputs()):
                    load(source, base + i).start()

            when(valid, action)

        def add(base):
            def action():
                refs = inputs()
                for i, source in enumerate(refs):
                    load(source, base + i).wait()
                add_inbox(outbox.at[slot], base, range(len(refs)))
                send().start()

            when(valid, action)

        return fetch, add

    def half_tasks(half_step, parity):
        one, two = half_step - 1, half_step - 2
        now, then = (parity - 1) % 2, parity

        def cores_in():
            for y in range(2):
                staged(one, y, 1).wait()
                staged(one, y, 0).wait_send()
                received(cores.at[one, y], core_receive.at[one, y])

        tasks = [
            simple_task(
                inside(one),
                cores_in if first else lambda: None,
                lambda first=first: sources(one, first, 1),
                now * 2 + first,
                lambda first=first: second_send(one, now, first),
            )
            for first in (1, 0)
        ]
        tasks.append(
            simple_task(
                inside(two),
                lambda: received(seconds.at[two, 1], second_receive.at[two, 1]),
                lambda: sources(two, 1, 0) + [seconds.at[two, 1]],
                4 + then,
                lambda: first_send(two, then),
            )
        )
        return tasks + [end_task(half_step, delay, parity) for delay in range(line)]

    def woven(tasks, pieces):
        boxes = inbox.shape[0] // 2
        tasks[0][0](0)
        for index, (_, add) in enumerate(tasks):
            if index + 1 < len(tasks):
                tasks[index + 1][0]((index + 1) % 2 * boxes)
            share = -(-len(pieces) // (len(tasks) - index))
            for piece in pieces[:share]:
                piece()
            pieces = pieces[share:]
            add(index % 2 * boxes)

    def tree_turn(half_step, last):
        for i in range(1, batch):
            turn = half_step - (i - 1) * 2 * line
            if last:
                when(turn == 2 * line - 1, trees[i].finish)
            else:
                inner = jnp.logical_and(turn >= 0, turn < 2 * line - 1)
                when(inner, lambda: trees[i].step(turn + 1))

    def begin_pick(group):
        for copy in load_group(group, 0):
            copy.start()

    begin_pick(0)
    for member in range(PLANE):
        pick(0, member)

    def step_body(step, _):
        busy = step < groups
        more = step + 1 < groups
        for parity in range(2):
            half_step = step * 2 + parity
            tree_turn(half_step, False)
            retire(half_step, parity)
            tasks = half_tasks(half_step, parity)
            pieces = []
            for expert in range(2):
                pieces.append(functools.partial((forward, backward)[parity], expert))
            if parity == 0:
                pieces.append(lambda: [copy.start() for copy in saves(step)])
            for y in range(2):
                pieces.append(functools.partial(combine, half_step, y))
            pieces = [functools.partial(when, busy, piece) for piece in pieces]
            if parity == 1:

                def prepare():
                    for copy in saves(step):
                        copy.wait()
                    begin_pick(step + 1)

                tree_end = functools.partial(tree_turn, half_step, True)
                pieces += [tree_end, functools.partial(when, more, prepare)]
                for member in range(PLANE):
                    pieces.append(
                        functools.partial(when, more, functools.partial(pick, step + 1, member))
                    )
            woven(tasks, pieces)
        return 0

    half_steps = units_all + line + 2
    lax.fori_loop(0, -(-half_steps // 2), step_body, 0)
    end = -(-half_steps // 2) * 2
    for parity in range(2):
        retire(jnp.int32(end + parity), parity)
    for copy in saves(groups - 1):
        copy.wait()


def run_experts(rows, cot_all, info, w_gate, w_up, w_down, capacity, fsdp_count):
    line = fsdp_count // PLANE
    batch, half, width = rows.shape
    length = 2 * half
    units = w_down.shape[1]
    slots = -(-capacity // 16) * 16
    groups = batch * line
    count = groups * PLANE * slots
    taken = PLANE * slots
    sends, receives = spread_count(line, True)
    shape = lambda *dims: jax.ShapeDtypeStruct(dims, jnp.bfloat16)
    block = (half, width)
    anywhere = pl.BlockSpec(memory_space=pl.ANY)
    vmem = lambda *dims: pltpu.VMEM(dims, jnp.bfloat16)
    sem = lambda *dims: pltpu.SemaphoreType.DMA(dims)
    return pl.pallas_call(
        functools.partial(experts_kernel, line, slots),
        out_shape=(
            shape(batch, fsdp_count, length, width),
            jax.ShapeDtypeStruct((batch, 2, *block), jnp.float32),
            shape(2, count, width),
            shape(2, count, width),
            shape(2, count, units),
            shape(2, count, units),
            shape(2, count, units),
            shape(2 * groups, 2, length, width),
            shape(2 * groups, 2, length, width),
            shape(2 * groups, 2, *block),
            shape(2 * groups, *block),
            shape(2 * groups, 2, *block),
        ),
        in_specs=[
            anywhere,
            anywhere,
            pl.BlockSpec(memory_space=pltpu.VMEM),
            anywhere,
            anywhere,
            anywhere,
        ],
        out_specs=(anywhere,) * 12,
        scratch_shapes=[
            vmem(2, width, 2 * units),
            vmem(2, units, width),
            vmem(2, length, width),
            vmem(2, length, width),
            vmem(2, taken, width),
            vmem(2, taken, width),
            vmem(2, taken, units),
            vmem(2, taken, units),
            vmem(2, taken, units),
            vmem(2, taken, 2 * units),
            vmem(PLANE, 2 * LANES, length),
            pltpu.VMEM((2, taken, LANES), jnp.float32),
            vmem(PLANE, 2 * LANES, width),
            vmem(PLANE, length, width),
            vmem(12, *block),
            vmem(10, *block),
            pltpu.VMEM(block, jnp.float32),
            sem(batch, sends),
            sem(batch, receives),
            sem(batch),
            sem(2, 2),
            sem(10),
            sem(PLANE),
            sem(12),
            sem(10),
            sem(1),
            sem(5),
            sem(2 * groups, 2),
            sem(2 * groups, 2),
            sem(2 * groups),
            sem(2 * groups, 2),
        ],
        compiler_params=pltpu.CompilerParams(
            collective_id=2, has_side_effects=True, vmem_limit_bytes=60 * MIB
        ),
    )(rows, cot_all, info, w_gate, w_up, w_down)[1:7]


def packed_picks(routes, gates):
    length = routes.shape[2]
    packed = jnp.concatenate([routes[:, 0].astype(jnp.float32), gates[:, 0]], axis=-1)
    packed = jnp.swapaxes(packed, 1, 2).reshape(-1, length)
    return jnp.pad(packed, ((0, 0), (0, -length % LANES)))


def slot_info(packed, batch, top, length, local_experts):
    fsdp_count = packed.shape[0]
    packed = packed[..., :length].reshape(fsdp_count, batch, 1, 2 * top, length)
    packed = jnp.swapaxes(packed, 0, 1)
    experts = lax.axis_index(FSDP) * local_experts + jnp.arange(local_experts, dtype=jnp.int32)
    same = packed[..., :top, :].astype(jnp.int32) == experts[:, None, None]
    hot = jnp.any(same, axis=3)
    shares = jnp.sum(jnp.where(same, packed[..., top:, :], 0.0), axis=3)
    position = jnp.arange(length)
    upper = (position[:, None] < position[None, :]).astype(jnp.bfloat16)
    rank = jnp.dot(
        hot.astype(jnp.bfloat16).reshape(-1, length), upper, preferred_element_type=jnp.float32
    )
    rank = jnp.where(hot, rank.reshape(hot.shape), -1.0)
    return jnp.concatenate([rank, shares], axis=2).reshape(-1, 2 * local_experts, length)


def gathered_layer(
    tokens,
    cotangent,
    norm1_gain,
    w_query,
    key_projection_weight,
    value_projection_weight,
    query_gain,
    key_gain,
    w_out,
    norm2_gain,
    w_gate,
    w_up,
    w_down,
    routes,
    gates,
):
    batch_count = tokens.shape[0]
    model_width = tokens.shape[3]
    sequence_length = routes.shape[2]
    half_length = tokens.shape[2]
    top_count = routes.shape[3]
    head_features = query_gain.shape[0]
    local_experts = w_gate.shape[0]
    fsdp_count = lax.axis_size(FSDP)
    all_experts = local_experts * fsdp_count
    capacity = 7 * top_count * sequence_length // (6 * all_experts)
    query_width = w_query.shape[1]
    kv_width = key_projection_weight.shape[1]
    kv_heads = kv_width // head_features
    cosine_table, sine_values = rotary_tables(sequence_length, head_features)
    weight_in = jnp.concatenate([w_query, key_projection_weight, value_projection_weight], axis=1)
    half_signs = jnp.where(jnp.arange(head_features) < head_features // 2, -1.0, 1.0)
    tables = (cosine_table[:, 0], sine_values[:, 0] * half_signs)
    gains = [gain[None, :] for gain in (norm1_gain, norm2_gain, query_gain, key_gain)]
    cot_all, in_full, out_full, picks, normed, projected, contexts, hidden, second = run_forward(
        tokens[:, 0],
        cotangent[:, 0],
        weight_in,
        w_out,
        packed_picks(routes, gates),
        gains,
        tables,
        fsdp_count,
        kv_heads,
    )
    info = slot_info(picks, batch_count, top_count, sequence_length, local_experts)
    totals, *expert_rows = run_experts(
        second, cot_all, info, w_gate, w_up, w_down, capacity, fsdp_count
    )
    block_out, input_grad, projected_grads, out_sum, gain_grads = run_backward(
        cotangent[:, 0],
        totals,
        hidden,
        projected,
        contexts,
        in_full,
        out_full,
        tokens[:, 0],
        gains,
        tables,
        fsdp_count,
        kv_heads,
    )
    rows = batch_count * sequence_length
    in_sum, gains_all, *expert_grads = run_gradients(
        normed.reshape(rows, -1),
        projected_grads.reshape(rows, -1),
        gain_grads,
        expert_rows,
        fsdp_count,
    )
    gains_sum = jnp.sum(gains_all, axis=(0, 1))
    return (
        block_out[:, None],
        input_grad[:, None],
        gains_sum[0],
        in_sum[:, :query_width],
        in_sum[:, query_width : query_width + kv_width],
        in_sum[:, query_width + kv_width :],
        gains_sum[2, :head_features],
        gains_sum[3, :head_features],
        out_sum,
        gains_sum[1],
        *expert_grads,
    )


def shards(*arrays):
    tokens, routes, w_gate = arrays[0], arrays[13], arrays[10]
    fsdp_count = lax.axis_size(FSDP)
    gathered = fsdp_count * routes.shape[2] * tokens.shape[3] * 2
    fits = gathered <= 24 * MIB and fsdp_count % PLANE == 0 and lax.axis_size(TP) == 2
    if fits and w_gate.shape[0] == 2:
        return gathered_layer(*arrays)
    return exchanged_layer(*arrays)


def solution(mesh):
    in_specs = (
        P(None, "fsdp", "tp", None),
        P(None, "fsdp", "tp", None),
        P(),
        P("fsdp", "tp"),
        P("fsdp", "tp"),
        P("fsdp", "tp"),
        P(),
        P(),
        P("tp", "fsdp"),
        P(),
        P("fsdp", None, "tp"),
        P("fsdp", None, "tp"),
        P("fsdp", "tp", None),
        P(None, "fsdp", None, None),
        P(None, "fsdp", None, None),
    )
    out_specs = (
        P(None, "fsdp", "tp", None),
        P(None, "fsdp", "tp", None),
        P(),
        P("fsdp", "tp"),
        P("fsdp", "tp"),
        P("fsdp", "tp"),
        P(),
        P(),
        P("tp", "fsdp"),
        P(),
        P("fsdp", None, "tp"),
        P("fsdp", None, "tp"),
        P("fsdp", "tp", None),
    )
    return jax.shard_map(shards, mesh=mesh, in_specs=in_specs, out_specs=out_specs, check_vma=False)
```

```python
import functools

import jax
import jax.numpy as jnp
from jax import lax
from jax.experimental import pallas as pl
from jax.experimental.pallas import tpu as pltpu
from jax.sharding import PartitionSpec as P

BLOCK = 256


EPSILON = 1e-06
ROPE_BASE = 1000000.0
MASKED = -1e30
TILE_PICKS = 128


def rms_scale(row_block, gain_row):
    return (
        row_block
        * lax.rsqrt(jnp.mean(row_block * row_block, axis=-1, keepdims=True) + EPSILON)
        * gain_row
    )


def rotary_tables(sequence_length, head_width):
    half_width = head_width // 2
    inverse = ROPE_BASE ** (-2.0 * jnp.arange(half_width, dtype=jnp.float32) / head_width)
    angles = jnp.arange(sequence_length, dtype=jnp.float32)[:, None] * inverse[None, :]
    cosine_table = jnp.concatenate([jnp.cos(angles), jnp.cos(angles)], axis=-1)[:, None, :]
    sine_values = jnp.concatenate([jnp.sin(angles), jnp.sin(angles)], axis=-1)[:, None, :]
    return (cosine_table, sine_values)


def rotate(head_rows, cosine_table, sine_values):
    half_width = head_rows.shape[-1] // 2
    turned = jnp.concatenate([-head_rows[..., half_width:], head_rows[..., :half_width]], axis=-1)
    return head_rows * cosine_table + turned * sine_values


def prepare_heads(projected, gain_row, cosine_table, sine_values):
    return rotate(rms_scale(projected, gain_row), cosine_table, sine_values)


def swiglu(gate_act, up_act):
    return jax.nn.silu(gate_act) * up_act


def slot_tables(route_rows, gate_rows, expert_count, capacity):
    sequence_length = route_rows.shape[0]
    top_count = route_rows.shape[1]
    pick_count = sequence_length * top_count
    tile_count = pick_count // TILE_PICKS
    flat_routes = route_rows.reshape(-1)
    onehot = (flat_routes[:, None] == jnp.arange(expert_count, dtype=jnp.int32)[None, :]).astype(
        jnp.bfloat16
    )
    tiles = onehot.reshape(tile_count, TILE_PICKS, expert_count)
    positions = jnp.arange(TILE_PICKS, dtype=jnp.int32)
    lower = (positions[None, :] < positions[:, None]).astype(jnp.bfloat16)
    within = jnp.einsum("ij,bje->bie", lower, tiles, preferred_element_type=jnp.float32)
    tile_totals = jnp.sum(tiles.astype(jnp.float32), axis=1)
    offsets = jnp.cumsum(tile_totals, axis=0) - tile_totals
    before = within + offsets[:, None, :]
    slot_rank = jnp.sum(before * tiles.astype(jnp.float32), axis=-1).reshape(-1).astype(jnp.int32)
    slot_index = flat_routes * capacity + slot_rank
    pick_ids = jnp.arange(pick_count, dtype=jnp.int32) // top_count
    slot_owner = (
        jnp.full((expert_count * capacity,), sequence_length, jnp.int32)
        .at[slot_index]
        .set(pick_ids)
    )
    slot_weight = (
        jnp.zeros((expert_count * capacity,), jnp.float32).at[slot_index].set(gate_rows.reshape(-1))
    )
    return (slot_index, slot_owner, slot_weight)


def exchanged_layer(
    tokens,
    cotangent,
    norm1_gain,
    w_query,
    key_projection_weight,
    value_projection_weight,
    query_gain,
    key_gain,
    w_out,
    norm2_gain,
    w_gate,
    w_up,
    w_down,
    routes,
    gates,
):
    batch_count = tokens.shape[0]
    model_width = tokens.shape[3]
    sequence_length = routes.shape[2]
    top_count = routes.shape[3]
    head_features = query_gain.shape[0]
    local_experts = w_gate.shape[0]
    fsdp_count = lax.axis_size("fsdp")
    all_experts = local_experts * fsdp_count
    capacity = 7 * top_count * sequence_length // (6 * all_experts)
    query_heads = w_query.shape[1] // head_features
    kv_heads = key_projection_weight.shape[1] // head_features
    group_size = query_heads // kv_heads
    score_scale = head_features ** (-0.5)
    cosine_table, sine_values = rotary_tables(sequence_length, head_features)
    block_ids = jnp.arange(sequence_length, dtype=jnp.int32) // BLOCK
    visible = (block_ids[None, :] <= block_ids[:, None])[None, None]
    first_gain = norm1_gain.astype(jnp.float32)
    second_gain = norm2_gain.astype(jnp.float32)
    query_factor_scale = query_gain.astype(jnp.float32)
    key_scale = key_gain.astype(jnp.float32)
    zero_row = jnp.zeros((1, model_width), jnp.bfloat16)
    buffer_shape = (fsdp_count, local_experts, capacity, model_width)

    def masked_scores(query_fourfold, key_rows):
        raw_scores = (
            jnp.einsum(
                "qcgd,kcd->cgqk", query_fourfold, key_rows, preferred_element_type=jnp.float32
            )
            * score_scale
        )
        return jnp.where(visible, raw_scores, MASKED)

    def prep_heads(projected, gain_row):
        return prepare_heads(projected, gain_row, cosine_table, sine_values)

    gain_sums = (
        jnp.zeros((model_width,), jnp.float32),
        jnp.zeros((model_width,), jnp.float32),
        jnp.zeros((head_features,), jnp.float32),
        jnp.zeros((head_features,), jnp.float32),
    )
    expert_grads = (
        jnp.zeros(w_gate.shape, jnp.float32),
        jnp.zeros(w_up.shape, jnp.float32),
        jnp.zeros(w_down.shape, jnp.float32),
    )
    attn_grads = tuple(
        (
            jnp.zeros(weight_part.shape, jnp.float32)
            for weight_part in (w_query, key_projection_weight, value_projection_weight, w_out)
        )
    )
    outputs = []
    input_grads = []
    for batch_index in range(batch_count):
        query_full, key_full, value_full, out_full = (
            lax.all_gather(w_query, "fsdp", axis=0, tiled=True),
            lax.all_gather(key_projection_weight, "fsdp", axis=0, tiled=True),
            lax.all_gather(value_projection_weight, "fsdp", axis=0, tiled=True),
            lax.all_gather(w_out, "fsdp", axis=1, tiled=True),
        )
        own_rows = tokens[batch_index, 0].astype(jnp.float32)
        own_cot = cotangent[batch_index, 0]
        route_rows = routes[batch_index, 0]
        gate_rows = gates[batch_index, 0]
        first_normed = rms_scale(own_rows, first_gain).astype(jnp.bfloat16)
        normed_all = lax.all_gather(first_normed, "tp", axis=0, tiled=True)
        query_projected = jnp.dot(
            normed_all, query_full, preferred_element_type=jnp.float32
        ).reshape(sequence_length, query_heads, head_features)
        key_projected = jnp.dot(normed_all, key_full, preferred_element_type=jnp.float32).reshape(
            sequence_length, kv_heads, head_features
        )
        value_row_list = (
            jnp.dot(normed_all, value_full, preferred_element_type=jnp.float32)
            .astype(jnp.bfloat16)
            .reshape(sequence_length, kv_heads, head_features)
        )
        query_rot = prep_heads(query_projected, query_factor_scale).astype(jnp.bfloat16)
        key_rot = prep_heads(key_projected, key_scale).astype(jnp.bfloat16)
        query_fourfold = query_rot.reshape(sequence_length, kv_heads, group_size, head_features)
        scores = masked_scores(query_fourfold, key_rot)
        row_max = jnp.max(scores, axis=-1, keepdims=True)
        exp_scores = jnp.exp(scores - row_max)
        totals = jnp.sum(exp_scores, axis=-1, keepdims=True)
        log_total = row_max + jnp.log(totals)
        prob_rows = (exp_scores / totals).astype(jnp.bfloat16)
        context = (
            jnp.einsum(
                "cgqk,kcd->qcgd", prob_rows, value_row_list, preferred_element_type=jnp.float32
            )
            .astype(jnp.bfloat16)
            .reshape(sequence_length, query_heads * head_features)
        )
        attn_own = lax.psum_scatter(
            jnp.dot(context, out_full, preferred_element_type=jnp.float32).astype(jnp.bfloat16),
            "tp",
            scatter_dimension=0,
            tiled=True,
        ).astype(jnp.float32)
        hidden_own = own_rows + attn_own
        second_normed = rms_scale(hidden_own, second_gain).astype(jnp.bfloat16)
        normed_two, cot_all = (
            lax.all_gather(second_normed, "tp", axis=0, tiled=True),
            lax.all_gather(own_cot, "tp", axis=0, tiled=True),
        )
        slot_index, slot_owner, slot_weight = slot_tables(
            route_rows, gate_rows, all_experts, capacity
        )
        padded_rows = jnp.concatenate([normed_two, zero_row], axis=0)
        send_rows = padded_rows[slot_owner].reshape(buffer_shape)
        expert_in = lax.all_to_all(send_rows, "fsdp", split_axis=0, concat_axis=0, tiled=True)
        gate_act = jnp.einsum(
            "sekd,edf->sekf", expert_in, w_gate, preferred_element_type=jnp.float32
        )
        up_act = jnp.einsum("sekd,edf->sekf", expert_in, w_up, preferred_element_type=jnp.float32)
        act_rows = swiglu(gate_act, up_act).astype(jnp.bfloat16)
        expert_out = jnp.einsum(
            "sekf,efd->sekd", act_rows, w_down, preferred_element_type=jnp.float32
        )
        returned = lax.all_to_all(
            expert_out.astype(jnp.bfloat16), "fsdp", split_axis=0, concat_axis=0, tiled=True
        ).astype(expert_out.dtype)
        picked = returned.reshape(all_experts * capacity, model_width)[slot_index].reshape(
            sequence_length, top_count, model_width
        )
        moe_part = jnp.sum(picked * gate_rows[:, :, None], axis=1)
        moe_own = lax.psum_scatter(
            moe_part.astype(jnp.bfloat16), "tp", scatter_dimension=0, tiled=True
        ).astype(jnp.float32)
        outputs.append((hidden_own + moe_own).astype(jnp.bfloat16))
        cot_padded = jnp.concatenate([cot_all, zero_row], axis=0)
        send_grads = (
            (slot_weight[:, None] * cot_padded[slot_owner])
            .astype(jnp.bfloat16)
            .reshape(buffer_shape)
        )
        out_grads = lax.all_to_all(send_grads, "fsdp", split_axis=0, concat_axis=0, tiled=True)
        act_grads = jnp.einsum(
            "sekd,efd->sekf", out_grads, w_down, preferred_element_type=jnp.float32
        )
        _, swiglu_back = jax.vjp(swiglu, gate_act, up_act)
        gate_grads, up_grads = swiglu_back(act_grads)
        gate_grads = gate_grads.astype(jnp.bfloat16)
        up_grads = up_grads.astype(jnp.bfloat16)
        expert_grads = (
            expert_grads[0]
            + jnp.einsum(
                "sekd,sekf->edf", expert_in, gate_grads, preferred_element_type=jnp.float32
            ),
            expert_grads[1]
            + jnp.einsum("sekd,sekf->edf", expert_in, up_grads, preferred_element_type=jnp.float32),
            expert_grads[2]
            + jnp.einsum("sekf,sekd->efd", act_rows, out_grads, preferred_element_type=jnp.float32),
        )
        input_part = jnp.einsum(
            "sekf,edf->sekd", gate_grads, w_gate, preferred_element_type=jnp.float32
        ) + jnp.einsum("sekf,edf->sekd", up_grads, w_up, preferred_element_type=jnp.float32)
        input_back = lax.all_to_all(
            input_part.astype(jnp.bfloat16), "fsdp", split_axis=0, concat_axis=0, tiled=True
        ).astype(input_part.dtype)
        normed_grads = jnp.sum(
            input_back.reshape(all_experts * capacity, model_width)[slot_index].reshape(
                sequence_length, top_count, model_width
            ),
            axis=1,
        )
        normed_own = lax.psum_scatter(
            normed_grads.astype(jnp.bfloat16), "tp", scatter_dimension=0, tiled=True
        ).astype(jnp.float32)
        _, second_back = jax.vjp(rms_scale, hidden_own, second_gain)
        hidden_part, second_gain_grad = second_back(normed_own)
        hidden_grad = own_cot.astype(jnp.float32) + hidden_part
        attn_grad_all = lax.all_gather(hidden_grad.astype(jnp.bfloat16), "tp", axis=0, tiled=True)
        out_weight_grad = jnp.einsum(
            "th,td->hd", context, attn_grad_all, preferred_element_type=jnp.float32
        )
        context_grad = (
            jnp.einsum("td,hd->th", attn_grad_all, out_full, preferred_element_type=jnp.float32)
            .astype(jnp.bfloat16)
            .reshape(sequence_length, kv_heads, group_size, head_features)
        )
        exp_again = jnp.exp(masked_scores(query_fourfold, key_rot) - log_total)
        probs_again = exp_again.astype(jnp.bfloat16)
        prob_grads = jnp.einsum(
            "qcgd,kcd->cgqk", context_grad, value_row_list, preferred_element_type=jnp.float32
        )
        value_grads = (
            jnp.einsum(
                "cgqk,qcgd->kcd", probs_again, context_grad, preferred_element_type=jnp.float32
            )
            .astype(jnp.bfloat16)
            .reshape(sequence_length, kv_heads * head_features)
        )
        score_grads = (
            exp_again * (prob_grads - jnp.sum(exp_again * prob_grads, axis=-1, keepdims=True))
        ).astype(jnp.bfloat16)
        query_rot_grads = (
            jnp.einsum("cgqk,kcd->qcgd", score_grads, key_rot, preferred_element_type=jnp.float32)
            * score_scale
        ).reshape(sequence_length, query_heads, head_features)
        key_rot_grads = (
            jnp.einsum(
                "cgqk,qcgd->kcd", score_grads, query_fourfold, preferred_element_type=jnp.float32
            )
            * score_scale
        )
        _, query_back = jax.vjp(prep_heads, query_projected, query_factor_scale)
        query_proj_grads, query_gain_grad = query_back(query_rot_grads)
        _, key_back = jax.vjp(prep_heads, key_projected, key_scale)
        key_proj_grads, key_gain_grad = key_back(key_rot_grads)
        query_proj_grads = query_proj_grads.astype(jnp.bfloat16).reshape(
            sequence_length, query_heads * head_features
        )
        key_proj_grads = key_proj_grads.astype(jnp.bfloat16).reshape(
            sequence_length, kv_heads * head_features
        )
        first_normed_grads = (
            jnp.einsum(
                "tq,dq->td", query_proj_grads, query_full, preferred_element_type=jnp.float32
            )
            + jnp.einsum("tq,dq->td", key_proj_grads, key_full, preferred_element_type=jnp.float32)
            + jnp.einsum("tq,dq->td", value_grads, value_full, preferred_element_type=jnp.float32)
        )
        weight_parts = (
            jnp.einsum(
                "td,tq->dq", normed_all, query_proj_grads, preferred_element_type=jnp.float32
            ),
            jnp.einsum("td,tq->dq", normed_all, key_proj_grads, preferred_element_type=jnp.float32),
            jnp.einsum("td,tq->dq", normed_all, value_grads, preferred_element_type=jnp.float32),
            out_weight_grad,
        )
        first_own = lax.psum_scatter(
            first_normed_grads.astype(jnp.bfloat16), "tp", scatter_dimension=0, tiled=True
        ).astype(jnp.float32)
        _, first_back = jax.vjp(rms_scale, own_rows, first_gain)
        row_part, first_gain_grad = first_back(first_own)
        input_grads.append((hidden_grad + row_part).astype(jnp.bfloat16))
        gain_sums = (
            gain_sums[0] + first_gain_grad,
            gain_sums[1] + second_gain_grad,
            gain_sums[2] + query_gain_grad,
            gain_sums[3] + key_gain_grad,
        )
        attn_grads = jax.tree.map(
            jnp.add,
            attn_grads,
            (
                lax.psum_scatter(weight_parts[0], "fsdp", scatter_dimension=0, tiled=True),
                lax.psum_scatter(weight_parts[1], "fsdp", scatter_dimension=0, tiled=True),
                lax.psum_scatter(weight_parts[2], "fsdp", scatter_dimension=0, tiled=True),
                lax.psum_scatter(weight_parts[3], "fsdp", scatter_dimension=1, tiled=True),
            ),
        )
    summed = lax.psum((gain_sums[0], gain_sums[1], gain_sums[2], gain_sums[3]), ("fsdp", "tp"))
    block_out = jnp.stack(outputs)[:, None]
    input_grad = jnp.stack(input_grads)[:, None]
    return (
        block_out,
        input_grad,
        summed[0],
        attn_grads[0],
        attn_grads[1],
        attn_grads[2],
        summed[2],
        summed[3],
        attn_grads[3],
        summed[1],
        expert_grads[0],
        expert_grads[1],
        expert_grads[2],
    )


MESH = pl.DeviceIdType.MESH
FSDP, TP = "fsdp", "tp"
PLANE = 4
LANES = 128
MIB = 1 << 20
RIGHT, LEFT, FIRST, SECOND, CORE, CROSS = range(6)
TRANSPOSED_LEFT = (((0,), (0,)), ((), ()))
TRANSPOSED_RIGHT = (((1,), (1,)), ((), ()))
OUTPUT, BACK = range(2)
CHUNK = 512


class Spot:
    def __init__(self, line, wide, turned=True):
        self.line = line
        self.wide = wide
        self.turned = turned
        self.planes = 4 if wide else 2
        index = lax.axis_index(FSDP)
        self.x = lax.axis_index(TP)
        self.z = lax.div(index, PLANE)
        self.y = lax.rem(lax.div(index, 2), 2)
        self.core = lax.rem(index, 2)

    def side(self, core, first, second):
        flip_y, flip_x = first, second
        if self.wide and self.turned:
            flip_y = (1 - core) * first + core * second
            flip_x = core * first + (1 - core) * second
        return self.y + flip_y * (1 - 2 * self.y), self.x + flip_x * (1 - 2 * self.x)

    def block(self, core, first, second, z):
        y, x = self.side(core, first, second)
        return z * PLANE + y * 2 + core, x

    def device(self, kind):
        if kind == RIGHT:
            return self.block(self.core, 0, 0, self.z + 1)
        if kind == LEFT:
            return self.block(self.core, 0, 0, self.z - 1)
        if kind == CORE:
            return self.block(1 - self.core, 0, 0, self.z)
        if kind == CROSS:
            return self.block(self.core, 0, 0, self.z)[0], 1 - self.x
        return self.block(self.core, int(kind == FIRST), int(kind == SECOND), self.z)

    def kinds(self):
        return (FIRST, SECOND, CORE) if self.wide else (FIRST, CORE)

    def number(self, first, second, z):
        return (second * 2 + first) * self.line + z

    def order(self, step):
        if isinstance(step, int) and step == 0:
            return [(self.z, None)]
        return [(self.z - step, self.z - step >= 0), (self.z + step, self.z + step < self.line)]

    def greet(self):
        barrier = pltpu.get_barrier_semaphore()

        def signal(kind):
            pl.semaphore_signal(barrier, inc=1, device_id=self.device(kind), device_id_type=MESH)

        for kind in self.kinds():
            signal(kind)
        when(self.z + 1 < self.line, lambda: signal(RIGHT))
        when(self.z > 0, lambda: signal(LEFT))
        around = (self.z + 1 < self.line).astype(jnp.int32) + (self.z > 0).astype(jnp.int32)
        pl.semaphore_wait(barrier, len(self.kinds()) + around)

    def send(self, source, target, send_sem, receive_sem, kind):
        return pltpu.make_async_remote_copy(
            src_ref=source,
            dst_ref=target,
            send_sem=send_sem,
            recv_sem=receive_sem,
            device_id=self.device(kind),
            device_id_type=MESH,
        )


def when(condition, action):
    def run():
        action()

    if condition is None or condition is True:
        run()
    elif condition is not False:
        pl.when(condition)(run)


class Spread:
    def __init__(self, spot, source, slot, send, receive, local):
        self.spot = spot
        self.slot = slot
        self.source = source
        self.sends = send
        self.receives = receive
        self.mine = pltpu.make_async_copy(source, slot(*spot.block(spot.core, 0, 0, spot.z)), local)

    def copy(self, first, second, z, kind, own=False):
        spot = self.spot
        place = self.slot(*spot.block(spot.core, first, second, z))
        number = spot.number(first, second, z)
        arrival = {
            RIGHT: number,
            LEFT: number,
            FIRST: spot.number(1, 0, z),
            SECOND: spot.number(first, 1, z),
            CORE: spot.planes * spot.line + number,
        }[kind]
        departure = {RIGHT: 0, LEFT: 1, FIRST: 2, SECOND: 3, CORE: 5}[kind] * spot.line + number
        source = self.source if own else place
        return spot.send(source, place, self.sends.at[departure], self.receives.at[arrival], kind)

    def arrived(self, first, second, z, other=False):
        spot = self.spot
        core = 1 - spot.core if other else spot.core
        place = self.slot(*spot.block(core, first, second, z))
        number = spot.number(first, second, z) + (spot.planes * spot.line if other else 0)
        spot.send(place, place, self.sends.at[0], self.receives.at[number], CORE).wait_recv()

    def steps(self):
        return self.spot.line + (3 if self.spot.wide else 1)

    def begin(self):
        spot = self.spot
        z = spot.z
        when(z + 1 < spot.line, lambda: self.copy(0, 0, z, RIGHT, True).start())
        when(z > 0, lambda: self.copy(0, 0, z, LEFT, True).start())
        for kind in spot.kinds():
            self.copy(0, 0, z, kind, True).start()
        self.mine.start()

    def step(self, step):
        spot = self.spot
        line, z = spot.line, spot.z

        def reached(away, action):
            inside = jnp.logical_and(away >= 0, away < line)
            when(jnp.logical_and(inside, z - away >= 0), lambda: action(z - away, True))
            when(
                jnp.logical_and(inside, jnp.logical_and(away > 0, z + away < line)),
                lambda: action(z + away, False),
            )

        def along(zz, from_left):
            self.arrived(0, 0, zz)
            if from_left:
                when(z + 1 < line, lambda: self.copy(0, 0, zz, RIGHT).start())
            else:
                when(z > 0, lambda: self.copy(0, 0, zz, LEFT).start())
            for kind in spot.kinds():
                self.copy(0, 0, zz, kind).start()

        def firsts(zz, _):
            self.arrived(1, 0, zz)
            if spot.wide:
                self.copy(1, 0, zz, SECOND).start()
            self.copy(1, 0, zz, CORE).start()

        def lasts(first):
            def action(zz, _):
                self.arrived(first, 1, zz)
                self.copy(first, 1, zz, CORE).start()

            return action

        step = jnp.asarray(step, jnp.int32)
        reached(step, along)
        reached(step - 1, firsts)
        if spot.wide:
            reached(step - 2, lasts(0))
            reached(step - 3, lasts(1))

    def finish(self):
        spot = self.spot
        z = spot.z

        def body(zz, _):
            when(
                jnp.logical_and(z + 1 < spot.line, zz <= z),
                lambda: self.copy(0, 0, zz, RIGHT).wait_send(),
            )
            when(jnp.logical_and(z > 0, zz >= z), lambda: self.copy(0, 0, zz, LEFT).wait_send())
            self.copy(0, 0, zz, FIRST).wait_send()
            for second in range(2 if spot.wide else 1):
                for first in (0, 1):
                    if spot.wide and not second:
                        self.copy(first, 0, zz, SECOND).wait_send()
                    self.copy(first, second, zz, CORE).wait_send()
                    self.arrived(first, second, zz, other=True)
            return 0

        lax.fori_loop(0, spot.line, body, 0)
        self.mine.wait()


def run_trees(trees):
    for tree in trees:
        tree.begin()

    def body(step, _):
        for tree in trees:
            tree.step(step)
        return 0

    lax.fori_loop(1, max(tree.steps() for tree in trees), body, 0)
    for tree in trees:
        tree.finish()


def spread_count(line, wide):
    return (9 if wide else 7) * line, (8 if wide else 4) * line


def rows_at(ref, index, size):
    return ref.at[pl.ds(pl.multiple_of(index * size, 16), size)]


def columns_at(ref, index, size):
    return ref.at[:, pl.ds(pl.multiple_of(index * size, LANES), size)]


def norm_rows(target, source, gain):
    def body(step, _):
        rows = pl.ds(pl.multiple_of(step * 16, 16), 16)
        value = source[rows, :].astype(jnp.float32)
        target[rows, :] = rms_scale(value, gain[...].astype(jnp.float32)).astype(target.dtype)
        return 0

    lax.fori_loop(0, target.shape[0] // 16, body, 0)


def turned_heads(value, gain, cosine, sine):
    normed = rms_scale(value, gain)
    return normed * cosine + pltpu.roll(normed, normed.shape[-1] // 2, 1) * sine


def visible_blocks(length, group):
    blocks = []
    for start in range(0, length, BLOCK):
        stop = min(start + BLOCK, length)
        heads = max(1, BLOCK // (stop - start))
        while group % heads:
            heads -= 1
        blocks.append((start, stop, stop, heads))
    return blocks


def softmax(scores):
    raised = jnp.exp(scores - jnp.max(scores, axis=0, keepdims=True))
    return raised * (1.0 / jnp.sum(raised, axis=0, keepdims=True))


def for_heads(low, high, heads, body):
    turns = 2 if heads == 1 and (high - low) % 2 == 0 else 1

    def turn(step, _):
        for i in range(turns):
            body(low + (step * turns + i) * heads)
        return 0

    count = (high - low) // (heads * turns)
    if count == 1:
        turn(0, 0)
    else:
        lax.fori_loop(0, count, turn, 0)


def head_columns(head, features):
    return pl.ds(pl.multiple_of(head * features, LANES), features)


def forward_kernel(
    line,
    heads,
    kv_heads,
    tokens_ref,
    cot_ref,
    in_ref,
    out_ref,
    picks_ref,
    gain1_ref,
    gain2_ref,
    query_gain_ref,
    key_gain_ref,
    cosine_ref,
    sine_ref,
    cot_all,
    in_all,
    out_all,
    picks_all,
    normed_all,
    projected_all,
    context_all,
    hidden_all,
    second_all,
    in_w,
    out_w,
    tokens,
    normed,
    projected,
    context,
    queries,
    keys,
    values,
    mixed,
    mixed_other,
    hidden,
    second,
    narrow_send,
    narrow_receive,
    wide_send,
    wide_receive,
    local,
    token_send,
    token_receive,
    mixed_send,
    mixed_receive,
    save_sem,
):
    batch, half, width = tokens_ref.shape
    length = 2 * half
    depth, out_width = in_ref.shape[0], out_ref.shape[1]
    features = query_gain_ref.shape[1]
    narrow = Spot(line, False)
    spots = [Spot(line, True, turned=i % 2 == 1) for i in range(batch)]
    spot = spots[0]
    x = spot.x
    spot.greet()
    slots = [
        (picks_ref, lambda block, side: picks_all.at[block]),
        (in_ref, lambda block, side: rows_at(in_w, block, depth)),
        (out_ref, lambda block, side: columns_at(out_w, block, out_width)),
    ]
    weights = [
        Spread(narrow, source, slot, narrow_send.at[i], narrow_receive.at[i], local.at[i])
        for i, (source, slot) in enumerate(slots)
    ]
    cots = [
        Spread(
            spots[i],
            cot_ref.at[i],
            lambda block, side, i=i: rows_at(cot_all.at[i, block], side, half),
            wide_send.at[i],
            wide_receive.at[i],
            local.at[3 + i],
        )
        for i in range(batch)
    ]
    early, late = weights[:2], weights[2]
    for tree in early:
        tree.begin()

    def token_copies(i):
        place = rows_at(tokens.at[i], x, half)
        return (
            pltpu.make_async_copy(tokens_ref.at[i], place, local.at[3 + batch + i]),
            spot.send(tokens_ref.at[i], place, token_send.at[i], token_receive.at[i], CROSS),
        )

    for i in range(batch):
        for copy in token_copies(i):
            copy.start()
    for tree in cots:
        tree.begin()

    def steps(step, _):
        for tree in early:
            tree.step(step)
        return 0

    lax.fori_loop(1, late.steps(), steps, 0)
    late.begin()
    for i in range(batch):
        mine, other = token_copies(i)
        mine.wait()
        other.wait_send()
        place = rows_at(tokens.at[i], 1 - x, half)
        spot.send(place, place, token_send.at[i], token_receive.at[i], CROSS).wait_recv()
    for i in range(batch):
        norm_rows(normed.at[i], tokens.at[i], gain1_ref)
    for tree in early:
        tree.finish()

    def save(source, target, index):
        return pltpu.make_async_copy(source, target, save_sem.at[index])

    saves = [save(in_w, in_all, 0), save(out_w, out_all, 1)]
    saves[0].start()

    def project(i, start, stop):
        for at in range(start, stop, CHUNK):
            projected[i, :, at : at + CHUNK] = jnp.dot(
                normed[i], in_w[:, at : at + CHUNK], preferred_element_type=jnp.float32
            )

    scale = features ** (-0.5)

    group = heads // kv_heads

    def prepare_keys(i):
        base = heads * features
        for head in range(kv_heads):
            at = base + head * features
            keys[head] = turned_heads(
                projected[i, :, at : at + features],
                key_gain_ref[...].astype(jnp.float32),
                cosine_ref[...],
                sine_ref[...],
            ).astype(jnp.bfloat16)
            at = base + (kv_heads + head) * features
            values[head] = projected[i, :, at : at + features].astype(jnp.bfloat16)

    def prepare_queries(i, shared):
        def prepare(member):
            columns = head_columns(shared * group + member, features)
            queries[member] = turned_heads(
                projected[i, :, columns], query_gain_ref[...].astype(jnp.float32), cosine_ref[...], sine_ref[...]
            ).astype(jnp.bfloat16)

        for_heads(0, group, 1, prepare)

    def attend(i, shared, start, stop, seen, at_once, low, high):
        count = stop - start

        def block(member):
            query = queries[pl.ds(member, at_once), start:stop, :].reshape(-1, features)
            scores = lax.dot_general(
                keys[shared, :seen, :],
                query,
                TRANSPOSED_RIGHT,
                preferred_element_type=jnp.float32,
            )
            rows = lax.dot_general(
                softmax(scores * scale).astype(jnp.bfloat16),
                values[shared, :seen, :],
                TRANSPOSED_LEFT,
                preferred_element_type=jnp.float32,
            ).astype(jnp.bfloat16)
            for j in range(at_once):
                columns = head_columns(shared * group + member + j, features)
                context[i, start:stop, columns] = rows[j * count : (j + 1) * count]

        for_heads(low, high, at_once, block)

    def mixed_copy(i):
        return spot.send(
            rows_at(mixed.at[i], 1 - x, half),
            mixed_other.at[i],
            mixed_send.at[i],
            mixed_receive.at[i],
            CROSS,
        )

    def mix(i, start, stop):
        for at in range(start, stop, CHUNK):
            mixed[i, :, at : at + CHUNK] = jnp.dot(
                context[i], out_w[:, at : at + CHUNK], preferred_element_type=jnp.float32
            ).astype(jnp.bfloat16)
        if stop == width:
            mixed_copy(i).start()

    def close(i):
        mixed_copy(i).wait()
        add_rows(
            hidden.at[i],
            [rows_at(tokens.at[i], x, half), rows_at(mixed.at[i], x, half), mixed_other.at[i]],
        )
        norm_rows(second.at[i], hidden.at[i], gain2_ref)

    later = [
        functools.partial(tree.step, step)
        for step in range(1, cots[0].steps())
        for tree in [late] + cots
        if step < tree.steps()
    ]
    final = late.steps() - 1

    def late_done():
        while later and len(later) > len(later_rest):
            later.pop(0)()
        late.finish()
        saves[1].start()

    later_rest = later[(final - 1) * (1 + batch) + 1 :]
    pending = []
    in_width = in_w.shape[1]
    parts = lambda size: [(at, min(at + 2 * CHUNK, size)) for at in range(0, size, 2 * CHUNK)]
    for i in range(batch):
        pending += [functools.partial(project, i, *part) for part in parts(in_width)]
        pending.append(functools.partial(prepare_keys, i))
        for shared in range(kv_heads):
            pending.append(functools.partial(prepare_queries, i, shared))
            for start, stop, seen, at_once in visible_blocks(length, group):
                share = max(at_once, group // 2)
                for low in range(0, group, share):
                    pending.append(
                        functools.partial(
                            attend, i, shared, start, stop, seen, at_once, low, low + share
                        )
                    )
        if i == 0:
            pending.append(late_done)
        pending += [functools.partial(mix, i, *part) for part in parts(width)]
    pending += [functools.partial(close, i) for i in range(batch)]
    while pending or later:
        for _ in range(-(-len(pending) // max(1, len(later)))):
            pending.pop(0)()
        if later:
            later.pop(0)()

    saves += [
        save(source, target, 2 + i)
        for i, (source, target) in enumerate(
            [
                (normed, normed_all),
                (projected, projected_all),
                (context, context_all),
                (hidden, hidden_all),
                (second, second_all),
            ]
        )
    ]
    for copy in saves[2:]:
        copy.start()
    for tree in cots:
        tree.finish()
    for copy in saves:
        copy.wait()


def run_forward(tokens, cot, weight_in, weight_out, picks, gains, tables, fsdp_count, kv_heads):
    line = fsdp_count // PLANE
    batch, half, width = tokens.shape
    length = 2 * half
    features = gains[2].shape[1]
    heads = weight_out.shape[0] // features
    in_shape = (weight_in.shape[0] * fsdp_count, weight_in.shape[1])
    out_shape = (weight_out.shape[0], weight_out.shape[1] * fsdp_count)
    wide, narrow = spread_count(line, True), spread_count(line, False)
    anywhere = pl.BlockSpec(memory_space=pl.ANY)
    inside = pl.BlockSpec(memory_space=pltpu.VMEM)
    shape = lambda dims, kind=jnp.bfloat16: jax.ShapeDtypeStruct(dims, kind)
    vmem = lambda *dims: pltpu.VMEM(dims, jnp.bfloat16)
    sem = lambda *dims: pltpu.SemaphoreType.DMA(dims)
    kept = (
        ((batch, length, width), jnp.bfloat16),
        ((batch, length, weight_in.shape[1]), jnp.float32),
        ((batch, length, heads * features), jnp.bfloat16),
        ((batch, half, width), jnp.float32),
        ((batch, half, width), jnp.bfloat16),
    )
    return pl.pallas_call(
        functools.partial(forward_kernel, line, heads, kv_heads),
        out_shape=(
            shape((batch, fsdp_count, length, width)),
            shape(in_shape),
            shape(out_shape),
            shape((fsdp_count, *picks.shape), picks.dtype),
            *(shape(*one) for one in kept),
        ),
        in_specs=[anywhere] * 5 + [inside] * 6,
        out_specs=(anywhere,) * 9,
        scratch_shapes=[
            vmem(*in_shape),
            vmem(*out_shape),
            vmem(batch, length, width),
            *(pltpu.VMEM(*one) for one in kept[:3]),
            vmem(heads // kv_heads, length, features),
            vmem(kv_heads, length, features),
            vmem(kv_heads, length, features),
            vmem(batch, length, width),
            vmem(batch, half, width),
            *(pltpu.VMEM(*one) for one in kept[3:]),
            sem(3, narrow[0]),
            sem(3, narrow[1]),
            sem(batch, wide[0]),
            sem(batch, wide[1]),
            sem(3 + 2 * batch),
            sem(batch),
            sem(batch),
            sem(batch),
            sem(batch),
            sem(7),
        ],
        compiler_params=pltpu.CompilerParams(
            collective_id=1, has_side_effects=True, vmem_limit_bytes=60 * MIB
        ),
    )(tokens, cot, weight_in, weight_out, picks, *gains, *tables)


def add_rows(target, sources):
    def body(step, _):
        rows = pl.ds(pl.multiple_of(step * 16, 16), 16)
        total = sources[0][rows, :].astype(jnp.float32)
        for source in sources[1:]:
            total = total + source[rows, :].astype(jnp.float32)
        target[rows, :] = total.astype(target.dtype)
        return 0

    lax.fori_loop(0, target.shape[0] // 16, body, 0)


class Collect:
    def __init__(self, spot, part, total, cores, firsts, rights, lefts, send, receive):
        self.spot = spot
        self.part = part
        self.total = total
        self.places = {CORE: cores, FIRST: firsts, RIGHT: rights, LEFT: lefts}
        line = spot.line
        self.base = {CORE: 0, FIRST: 2 * line, RIGHT: 3 * line, LEFT: 4 * line}
        self.sends = send
        self.receives = receive

    def own(self, first, z):
        return self.part(*self.spot.block(self.spot.core, first, 0, z))

    def copy(self, kind, first, z):
        spot = self.spot
        number = first * spot.line + z if kind == CORE else z
        source = self.part(*spot.block(1 - spot.core, first, 0, z)) if kind == CORE else self.own(first, z)
        at = self.base[kind] + number
        return spot.send(
            source, self.places[kind].at[number], self.sends.at[at], self.receives.at[at], kind
        )

    def arrived(self, kind, number):
        place = self.places[kind].at[number]
        at = self.base[kind] + number
        self.spot.send(place, place, self.sends.at[0], self.receives.at[at], CORE).wait_recv()
        return place

    def begin(self, z):
        for first in (1, 0):
            self.copy(CORE, first, z).start()

    def to_first(self, z):
        add_rows(self.own(1, z), [self.own(1, z), self.arrived(CORE, self.spot.line + z)])
        self.copy(FIRST, 1, z).start()

    def summands(self, z):
        return [self.own(0, z), self.arrived(CORE, z), self.arrived(FIRST, z)]

    def cross(self):
        for step in reversed(range(self.spot.line)):
            for zz, valid in self.spot.order(step):
                when(valid, functools.partial(self.to_first, zz))

    def onward(self, kind, zz):
        spot = self.spot
        sources = self.summands(zz)
        target = self.own(0, zz)
        behind = spot.z > 0 if kind == RIGHT else spot.z + 1 < spot.line
        when(behind, lambda: add_rows(target, sources + [self.arrived(kind, zz)]))
        when(jnp.logical_not(behind), lambda: add_rows(target, sources))
        self.copy(kind, 0, zz).start()

    def last(self):
        z, line = self.spot.z, self.spot.line
        sources = self.summands(z)

        def end(kinds):
            add_rows(self.total, sources + [self.arrived(kind, z) for kind in kinds])

        when(z == 0, lambda: end([LEFT]))
        when(z == line - 1, lambda: end([RIGHT]))
        when(jnp.logical_and(z > 0, z < line - 1), lambda: end([RIGHT, LEFT]))

    def finish(self):
        spot = self.spot
        for zz in range(spot.line):
            for first in (0, 1):
                self.copy(CORE, first, zz).wait_send()
            self.copy(FIRST, 1, zz).wait_send()
            when(zz > spot.z, lambda: self.copy(RIGHT, 0, zz).wait_send())
            when(zz < spot.z, lambda: self.copy(LEFT, 0, zz).wait_send())

    def tasks(self):
        spot = self.spot
        work = []
        for step in reversed(range(1, spot.line)):
            for kind, (zz, valid) in zip((LEFT, RIGHT), spot.order(step)):
                action = functools.partial(self.onward, kind, zz)
                work.append(functools.partial(when, valid, action))
        return work + [self.last, self.finish]


def collect_scratch(line, shape):
    counts = (2 * line, line, line, line)
    return [pltpu.VMEM((count, *shape), jnp.bfloat16) for count in counts] + [
        pltpu.SemaphoreType.DMA((5 * line,)),
        pltpu.SemaphoreType.DMA((5 * line,)),
    ]


BOXES = 6


def plane_in_turn(line, group):
    turn = lax.rem(group, line)
    step = lax.div(turn, 2)
    return jnp.where(lax.rem(turn, 2) == 0, step, line - 1 - step)


class Sums:
    def __init__(self, spot, parts, cores, places, inbox, outbox, semaphores, plane, inside, ready, done, turns):
        self.spot = spot
        self.parts = parts
        self.cores = cores
        self.seconds, self.firsts, self.ends = places
        self.inbox = inbox
        self.outbox = outbox
        (
            self.inbox_sem,
            self.outbox_sem,
            self.second_receive,
            self.first_receive,
            self.end_receive,
        ) = semaphores
        self.plane = plane
        self.inside = inside
        self.ready = ready
        self.done = done
        self.turns = turns

    def second_send(self, unit, turn, first):
        slot = turn * 2 + first
        return self.spot.send(
            self.outbox.at[slot],
            self.seconds.at[unit, first],
            self.outbox_sem.at[slot],
            self.second_receive.at[unit, first],
            SECOND,
        )

    def first_send(self, unit, turn):
        slot = 2 * self.turns + turn
        return self.spot.send(
            self.outbox.at[slot],
            self.firsts.at[unit],
            self.outbox_sem.at[slot],
            self.first_receive.at[unit],
            FIRST,
        )

    def end_send(self, unit, turn, kind):
        slot = 3 * self.turns + turn * 2 + kind
        return self.spot.send(
            self.outbox.at[slot],
            self.ends.at[unit, kind],
            self.outbox_sem.at[slot],
            self.end_receive.at[unit, kind],
            kind,
        )

    def received(self, place, semaphore):
        self.spot.send(place, place, self.outbox_sem.at[0], semaphore, CORE).wait_recv()

    def sources(self, unit, first, second):
        y, x = self.spot.side(self.spot.core, first, second)
        half = self.inbox.shape[1]
        return [rows_at(self.parts(unit, y), x, half), rows_at(self.cores(unit, y), x, half)]

    def summands(self, unit):
        return self.sources(unit, 0, 0) + [self.seconds.at[unit, 0], self.firsts.at[unit]]

    def load(self, source, slot):
        return pltpu.make_async_copy(source, self.inbox.at[slot], self.inbox_sem.at[slot])

    def add(self, target, base, numbers):
        add_rows(target, [self.inbox.at[base + i] for i in numbers])

    def end_roles(self, half_step, delay):
        z, line = self.spot.z, self.spot.line
        unit = half_step - 3 - delay
        valid = self.inside(unit)
        plane = self.plane(unit)
        right = jnp.logical_and(valid, jnp.logical_and(z < plane, delay == z))
        left = jnp.logical_and(valid, jnp.logical_and(z > plane, delay == line - 1 - z))
        last = jnp.logical_and(
            valid,
            jnp.logical_and(z == plane, delay == jnp.maximum(plane, line - 1 - plane)),
        )
        return unit, right, left, last

    def end_task(self, half_step, delay, parity):
        z, line = self.spot.z, self.spot.line
        turn = (parity - 3 - delay) % self.turns
        unit, right, left, last = self.end_roles(half_step, delay)
        some = jnp.logical_or(right, jnp.logical_or(left, last))
        from_left = jnp.logical_and(jnp.logical_or(right, last), z > 0)
        from_right = jnp.logical_and(jnp.logical_or(left, last), z + 1 < line)
        present = ((RIGHT, from_left), (LEFT, from_right))

        def fetch(base):
            def action():
                self.received(self.seconds.at[unit, 0], self.second_receive.at[unit, 0])
                self.received(self.firsts.at[unit], self.first_receive.at[unit])
                for i, source in enumerate(self.summands(unit)):
                    self.load(source, base + i).start()
                for kind, there in present:

                    def arrive():
                        self.received(self.ends.at[unit, kind], self.end_receive.at[unit, kind])
                        self.load(self.ends.at[unit, kind], base + 4 + kind).start()

                    when(there, arrive)

            when(some, action)

        def add(base):
            def action():
                for i, source in enumerate(self.summands(unit)):
                    self.load(source, base + i).wait()
                for kind, there in present:
                    when(there, lambda: self.load(self.ends.at[unit, kind], base + 4 + kind).wait())
                numbers = list(range(4))
                for kind, chosen, behind in ((RIGHT, right, z > 0), (LEFT, left, z + 1 < line)):

                    def onward():
                        target = self.outbox.at[3 * self.turns + turn * 2 + kind]
                        when(behind, lambda: self.add(target, base, numbers + [4 + kind]))
                        when(jnp.logical_not(behind), lambda: self.add(target, base, numbers))
                        self.end_send(unit, turn, kind).start()

                    when(chosen, onward)

                def finish():
                    def into(target):
                        both = jnp.logical_and(from_left, from_right)
                        when(both, lambda: self.add(target, base, numbers + [4, 5]))
                        for kind, there in present:
                            when(
                                jnp.logical_and(there, jnp.logical_not(both)),
                                lambda: self.add(target, base, numbers + [4 + kind]),
                            )

                    self.done(unit, turn, into)

                when(last, finish)

            when(some, action)

        return fetch, add

    def retire(self, half_step, parity):
        before = half_step - self.turns
        now, then = (parity - 1) % self.turns, (parity - 2) % self.turns
        when(
            self.inside(before - 1),
            lambda: [self.second_send(before - 1, now, first).wait_send() for first in range(2)],
        )
        when(self.inside(before - 2), lambda: self.first_send(before - 2, then).wait_send())
        for delay in range(self.spot.line):
            if self.inside(before - 3 - delay) is False:
                continue
            unit, right, left, _ = self.end_roles(before, delay)
            turn = (parity - 3 - delay) % self.turns
            when(right, lambda: self.end_send(unit, turn, RIGHT).wait_send())
            when(left, lambda: self.end_send(unit, turn, LEFT).wait_send())

    def simple_task(self, valid, ready, inputs, slot, send):
        def fetch(base):
            ready()

            def action():
                for i, source in enumerate(inputs()):
                    self.load(source, base + i).start()

            when(valid, action)

        def add(base):
            def action():
                refs = inputs()
                for i, source in enumerate(refs):
                    self.load(source, base + i).wait()
                self.add(self.outbox.at[slot], base, range(len(refs)))
                send().start()

            when(valid, action)

        return fetch, add

    def tasks(self, half_step, parity):
        one, two = half_step - 1, half_step - 2
        now, then = (parity - 1) % self.turns, (parity - 2) % self.turns
        tasks = []
        for first in (1, 0):
            tasks.append(
                self.simple_task(
                    self.inside(one),
                    functools.partial(self.ready, one) if first else lambda: None,
                    lambda first=first: self.sources(one, first, 1),
                    now * 2 + first,
                    lambda first=first: self.second_send(one, now, first),
                )
            )
        arrive = lambda: self.received(self.seconds.at[two, 1], self.second_receive.at[two, 1])
        tasks.append(
            self.simple_task(
                self.inside(two),
                lambda: when(self.inside(two), arrive),
                lambda: self.sources(two, 1, 0) + [self.seconds.at[two, 1]],
                2 * self.turns + then,
                lambda: self.first_send(two, then),
            )
        )
        for delay in range(self.spot.line):
            if self.inside(half_step - 3 - delay) is not False:
                tasks.append(self.end_task(half_step, delay, parity))
        return tasks

    def weave(self, tasks, pieces):
        buffers = self.inbox.shape[0] // BOXES
        if buffers > 1:
            tasks[0][0](0)
        for index, (fetch, add) in enumerate(tasks):
            if buffers == 1:
                fetch(0)
            elif index + 1 < len(tasks):
                tasks[index + 1][0]((index + 1) % 2 * BOXES)
            share = -(-len(pieces) // (len(tasks) - index))
            for piece in pieces[:share]:
                piece()
            pieces = pieces[share:]
            add(index % buffers * BOXES)

    def half_steps(self, units):
        return units + self.spot.line + 2


def norm_back(value, grads, gain):
    scale = lax.rsqrt(jnp.mean(value * value, axis=-1, keepdims=True) + EPSILON)
    unit = value * scale
    scaled = grads * gain
    back = scale * (scaled - unit * jnp.mean(scaled * unit, axis=-1, keepdims=True))
    return back, grads * unit


def backward_kernel(
    line,
    heads,
    kv_heads,
    cot_ref,
    totals_ref,
    hidden_ref,
    projected_ref,
    context_ref,
    in_ref,
    out_ref,
    tokens_ref,
    part_ref,
    cores_ref,
    gain1_ref,
    gain2_ref,
    query_gain_ref,
    key_gain_ref,
    cosine_ref,
    sine_ref,
    block_out,
    input_grad,
    grads_all,
    out_total,
    gain_grads,
    seconds,
    middle,
    ends,
    elements,
    cots,
    tokens,
    kept,
    result,
    context,
    hidden_grads,
    context_grads,
    grads,
    normed_other,
    weight_rows,
    queries_f,
    shared_f,
    queries,
    query_grads,
    sums,
    out_grads,
    cores,
    firsts,
    rights,
    lefts,
    tree_send,
    tree_receive,
    load_sem,
    row_sem,
    head_sem,
    save_sem,
    hidden_send,
    hidden_receive,
    normed_send,
    normed_receive,
    inbox,
    outbox,
    summed,
    inbox_sem,
    outbox_sem,
    second_receive,
    first_receive,
    end_receive,
):
    batch, half, width = cot_ref.shape
    length = 2 * half
    features = query_gain_ref.shape[1]
    group = heads // kv_heads
    base = heads * features
    out_width = out_total.shape[1]
    narrow, spot = Spot(line, False), Spot(line, True)
    x = spot.x
    scale = features ** (-0.5)
    normed_grads = context_grads

    def load(source, target, index):
        return pltpu.make_async_copy(source, target, load_sem.at[index])

    def element_loads(i):
        copies = [
            load(hidden_ref.at[i], elements.at[0], 0),
            load(totals_ref.at[i, BACK], elements.at[1], 1),
        ]
        if i:
            copies.append(load(totals_ref.at[i, OUTPUT], elements.at[2], 2))
        return copies

    first_loads = [load(cot_ref, cots, 3), load(tokens_ref, tokens, 4)] + [
        load(context_ref.at[i], rows_at(context, i, length), 5 + i) for i in range(batch)
    ]
    for copy in element_loads(0) + first_loads:
        copy.start()

    def weight_load(ref, step):
        slot = step % 2
        return pltpu.make_async_copy(
            rows_at(ref, step, CHUNK),
            weight_rows.at[slot, :, pl.ds(0, ref.shape[1])],
            row_sem.at[slot],
        )

    out_steps, in_steps = out_ref.shape[0] // CHUNK, in_ref.shape[0] // CHUNK
    for step in range(2):
        weight_load(out_ref, step).start()
    gain_grads[...] = jnp.zeros_like(gain_grads)
    spot.greet()
    for copy in first_loads:
        copy.wait()

    def result_save(i, target):
        return pltpu.make_async_copy(result.at[i], target.at[i], save_sem.at[i])

    def half_copy(ref, i, side):
        return ref.at[pl.ds(pl.multiple_of(i * length + side * half, 16), half), pl.ds(0, width)]

    def hidden_copy(i):
        place = half_copy(hidden_grads, i, x)
        return spot.send(place, place, hidden_send.at[i], hidden_receive.at[i], CROSS)

    def element_rows(i):
        for copy in element_loads(i):
            copy.wait()

        def elementwise(step, _):
            rows = pl.ds(pl.multiple_of(step * 16, 16), 16)
            value = elements[0, rows, :]
            if i:
                result[i, rows, :] = (value + elements[2, rows, :]).astype(jnp.bfloat16)
            back, gain_rows = norm_back(
                value, elements[1, rows, :], gain2_ref[...].astype(jnp.float32)
            )
            gain_grads[1:2, :] += jnp.sum(gain_rows, axis=0, keepdims=True)
            total = cots[i, rows, :].astype(jnp.float32) + back
            kept[i, rows, :] = total
            place = pl.ds(pl.multiple_of(i * length + x * half + step * 16, 16), 16)
            hidden_grads[place, :] = total.astype(jnp.bfloat16)
            return 0

        lax.fori_loop(0, half // 16, elementwise, 0)
        hidden_copy(i).start()
        if i:
            result_save(i, block_out).start()
        if i + 1 < batch:
            for copy in element_loads(i + 1):
                copy.start()

    def hidden_done():
        load(hidden_ref.at[0], elements.at[0], 0).start()
        for i in range(batch):
            hidden_copy(i).wait_send()
            place = half_copy(hidden_grads, i, 1 - x)
            spot.send(place, place, hidden_send.at[i], hidden_receive.at[i], CROSS).wait_recv()

    def context_step(step):
        weight_load(out_ref, step).wait()
        columns = slice(step * CHUNK, (step + 1) * CHUNK)
        context_grads[:, columns] = lax.dot_general(
            hidden_grads[...],
            weight_rows[step % 2, :, :width],
            TRANSPOSED_RIGHT,
            preferred_element_type=jnp.float32,
        ).astype(jnp.bfloat16)
        if step + 2 < out_steps:
            weight_load(out_ref, step + 2).start()

    def out_step(step):
        columns = slice(step * CHUNK, (step + 1) * CHUNK)
        for start in range(0, width, CHUNK):
            out_grads[columns, start : start + CHUNK] = lax.dot_general(
                context[:, columns],
                hidden_grads[:, start : start + CHUNK],
                TRANSPOSED_LEFT,
                preferred_element_type=jnp.float32,
            ).astype(jnp.bfloat16)

    tree = Collect(
        narrow,
        lambda block, side: columns_at(out_grads, block, out_width),
        out_total,
        cores,
        firsts,
        rights,
        lefts,
        tree_send,
        tree_receive,
    )

    def in_start():
        for step in range(2):
            weight_load(in_ref, step).start()

    def tree_start():
        for z in range(line):
            tree.begin(z)
        for copy in head_loads(0):
            copy.start()

    def turns():
        return [(i, shared) for i in range(batch) for shared in range(kv_heads)]

    def head_loads(index):
        i, shared = turns()[index]
        slot = index % 2
        return [
            pltpu.make_async_copy(
                projected_ref.at[i, :, pl.ds(shared * group * features, group * features)],
                queries_f.at[slot],
                head_sem.at[slot, 0],
            )
        ] + [
            pltpu.make_async_copy(
                projected_ref.at[i, :, pl.ds(base + (shared + j * kv_heads) * features, features)],
                shared_f.at[slot, j],
                head_sem.at[slot, 1 + j],
            )
            for j in range(2)
        ]

    def turn_back(grads_in):
        return grads_in * cosine_ref[...] + pltpu.roll(
            grads_in * sine_ref[...], features // 2, 1
        )

    query_gain = lambda: query_gain_ref[...].astype(jnp.float32)
    key_gain = lambda: key_gain_ref[...].astype(jnp.float32)

    def attend_pieces(index):
        i, shared = turns()[index]
        slot = index % 2
        top = i * length

        def columns_of(member):
            return pl.ds(pl.multiple_of(member * features, LANES), features)

        def prepare():
            for copy in head_loads(index):
                copy.wait()
            if index + 1 < len(turns()):
                for copy in head_loads(index + 1):
                    copy.start()
            queries[group] = turned_heads(
                shared_f[slot, 0], key_gain(), cosine_ref[...], sine_ref[...]
            ).astype(jnp.bfloat16)
            queries[group + 1] = shared_f[slot, 1].astype(jnp.bfloat16)
            sums[...] = jnp.zeros_like(sums)

            def one(member):
                queries[member] = turned_heads(
                    queries_f[slot, :, columns_of(member)],
                    query_gain(),
                    cosine_ref[...],
                    sine_ref[...],
                ).astype(jnp.bfloat16)

            for_heads(0, group, 1, one)

        def rows_block(start, stop, seen, at_once, low, high):
            count = stop - start

            def block(member):
                query = queries[pl.ds(member, at_once), start:stop, :].reshape(-1, features)
                keys, values = queries[group, :seen, :], queries[group + 1, :seen, :]
                out_grad = jnp.concatenate(
                    [
                        context_grads[
                            top + start : top + stop,
                            head_columns(shared * group + member + j, features),
                        ]
                        for j in range(at_once)
                    ],
                    axis=0,
                )
                scores = lax.dot_general(
                    keys, query, TRANSPOSED_RIGHT, preferred_element_type=jnp.float32
                )
                shares = softmax(scores * scale)
                share_grads = lax.dot_general(
                    values, out_grad, TRANSPOSED_RIGHT, preferred_element_type=jnp.float32
                )
                sums[1, :seen, :] += jnp.dot(
                    shares.astype(jnp.bfloat16), out_grad, preferred_element_type=jnp.float32
                )
                inner = jnp.sum(shares * share_grads, axis=0, keepdims=True)
                score_grads = (shares * (share_grads - inner)).astype(jnp.bfloat16)
                rows = scale * lax.dot_general(
                    score_grads, keys, TRANSPOSED_LEFT, preferred_element_type=jnp.float32
                )
                query_grads[pl.ds(member, at_once), start:stop, :] = rows.reshape(
                    at_once, count, features
                )
                sums[0, :seen, :] += jnp.dot(
                    score_grads, query, preferred_element_type=jnp.float32
                )

            for_heads(low, high, at_once, block)

        def finish_queries():
            def finish(member):
                back, gain_rows = norm_back(
                    queries_f[slot, :, columns_of(member)],
                    turn_back(query_grads[member]),
                    query_gain(),
                )
                gain_grads[2:3, :features] += jnp.sum(gain_rows, axis=0, keepdims=True)
                grads[top : top + length, head_columns(shared * group + member, features)] = (
                    back.astype(jnp.bfloat16)
                )

            for_heads(0, group, 1, finish)

        def finish_keys():
            back, gain_rows = norm_back(shared_f[slot, 0], turn_back(sums[0] * scale), key_gain())
            gain_grads[3:4, :features] += jnp.sum(gain_rows, axis=0, keepdims=True)
            at = base + shared * features
            grads[top : top + length, at : at + features] = back.astype(jnp.bfloat16)
            at += kv_heads * features
            grads[top : top + length, at : at + features] = sums[1].astype(jnp.bfloat16)

        pieces = [prepare]
        for start, stop, seen, at_once in visible_blocks(length, group):
            share = max(at_once, group // 2)
            for low in range(0, group, share):
                pieces.append(
                    functools.partial(rows_block, start, stop, seen, at_once, low, low + share)
                )
        return pieces + [finish_queries, finish_keys]

    saves = [
        pltpu.make_async_copy(rows_at(grads, i, length), grads_all.at[i], save_sem.at[batch + i])
        for i in range(batch)
    ]

    def normed_step(step):
        weight_load(in_ref, step).wait()
        normed_grads[:, step * CHUNK : (step + 1) * CHUNK] = lax.dot_general(
            grads[...],
            weight_rows[step % 2],
            TRANSPOSED_RIGHT,
            preferred_element_type=jnp.float32,
        ).astype(jnp.bfloat16)
        if step + 2 < in_steps:
            weight_load(in_ref, step + 2).start()

    def normed_copy(i):
        return spot.send(
            half_copy(normed_grads, i, 1 - x),
            normed_other.at[i],
            normed_send.at[i],
            normed_receive.at[i],
            CROSS,
        )

    def input_rows(i):
        normed_copy(i).wait()
        if i:
            result_save(i, block_out).wait()

        def body(step, _):
            rows = pl.ds(pl.multiple_of(step * 16, 16), 16)
            place = pl.ds(pl.multiple_of(i * length + x * half + step * 16, 16), 16)
            total = normed_grads[place, :width].astype(jnp.float32) + normed_other[
                i, rows, :
            ].astype(jnp.float32)
            back, gain_rows = norm_back(
                tokens[i, rows, :].astype(jnp.float32), total, gain1_ref[...].astype(jnp.float32)
            )
            gain_grads[0:1, :] += jnp.sum(gain_rows, axis=0, keepdims=True)
            kept[i, rows, :] = kept[i, rows, :] + back
            return 0

        lax.fori_loop(0, half // 16, body, 0)
        add_rows(result.at[i], [kept.at[i]])
        result_save(i, input_grad).start()

    moved = Sums(
        spot,
        lambda unit, y: part_ref.at[2 * unit + OUTPUT, y],
        lambda unit, y: cores_ref.at[2 * unit + OUTPUT, y],
        (seconds, middle, ends),
        inbox,
        outbox,
        (inbox_sem, outbox_sem, second_receive, first_receive, end_receive),
        lambda unit: plane_in_turn(line, unit),
        lambda unit: 0 <= unit < line,
        lambda unit: None,
        lambda unit, turn, into: into(summed),
        1,
    )
    pieces = [functools.partial(element_rows, i) for i in range(batch)] + [hidden_done]
    pieces += [functools.partial(out_step, step) for step in range(out_steps)]
    pieces += [tree_start, functools.partial(context_step, 0), tree.cross]
    pieces += [functools.partial(context_step, step) for step in range(1, out_steps)]
    pieces.append(in_start)
    attending = [piece for index in range(len(turns())) for piece in attend_pieces(index)]
    work = tree.tasks()
    share = -(-len(attending) // len(work))
    while attending or work:
        pieces += attending[:share]
        attending = attending[share:]
        pieces += work[:1]
        work = work[1:]
    pieces += [copy.start for copy in saves]
    pieces += [functools.partial(normed_step, step) for step in range(in_steps)]
    pieces += [normed_copy(i).start for i in range(batch)]
    pieces += [functools.partial(input_rows, i) for i in range(batch)]

    count = moved.half_steps(line)
    for half_step in range(1, count):
        moved.retire(half_step, 0)
        take = -(-len(pieces) // (count - half_step))
        moved.weave(moved.tasks(half_step, 0), pieces[:take])
        pieces = pieces[take:]
    moved.retire(count, 0)
    load(hidden_ref.at[0], elements.at[0], 0).wait()
    result_save(0, input_grad).wait()
    add_rows(result.at[0], [elements.at[0], summed])
    result_save(0, block_out).start()
    result_save(0, block_out).wait()
    for i in range(1, batch):
        result_save(i, input_grad).wait()
    for copy in saves:
        copy.wait()


def run_backward(
    cot,
    totals,
    hidden,
    projected,
    context,
    in_full,
    out_full,
    tokens,
    part,
    cores,
    gains,
    tables,
    fsdp_count,
    kv_heads,
):
    line = fsdp_count // PLANE
    batch, half, width = tokens.shape
    length = 2 * half
    features = gains[2].shape[1]
    heads = out_full.shape[0] // features
    group = heads // kv_heads
    in_width, out_depth = in_full.shape[1], out_full.shape[0]
    out_shape = (out_depth, width // fsdp_count)
    anywhere = pl.BlockSpec(memory_space=pl.ANY)
    inside = pl.BlockSpec(memory_space=pltpu.VMEM)
    shape = lambda *dims: jax.ShapeDtypeStruct(dims, jnp.bfloat16)
    vmem = lambda *dims: pltpu.VMEM(dims, jnp.bfloat16)
    wide = lambda *dims: pltpu.VMEM(dims, jnp.float32)
    sem = lambda *dims: pltpu.SemaphoreType.DMA(dims)
    rows = batch * length
    return pl.pallas_call(
        functools.partial(backward_kernel, line, heads, kv_heads),
        out_shape=(
            shape(batch, half, width),
            shape(batch, half, width),
            shape(batch, length, in_width),
            jax.ShapeDtypeStruct(out_shape, jnp.float32),
            jax.ShapeDtypeStruct((8, width), jnp.float32),
            shape(line, 2, half, width),
            shape(line, half, width),
            shape(line, 2, half, width),
        ),
        in_specs=[anywhere] * 10 + [inside] * 6,
        out_specs=(anywhere, anywhere, anywhere, inside, inside, anywhere, anywhere, anywhere),
        scratch_shapes=[
            wide(3, half, width),
            vmem(batch, half, width),
            vmem(batch, half, width),
            wide(batch, half, width),
            vmem(batch, half, width),
            vmem(rows, out_depth),
            vmem(rows, width),
            vmem(rows, max(out_depth, width)),
            vmem(rows, in_width),
            vmem(batch, half, width),
            vmem(2, CHUNK, max(width, in_width)),
            wide(2, length, group * features),
            wide(2, 2, length, features),
            vmem(group + 2, length, features),
            wide(group, length, features),
            wide(2, length, features),
            vmem(out_depth, width),
            *collect_scratch(line, out_shape),
            sem(5 + batch),
            sem(2),
            sem(2, 3),
            sem(2 * batch),
            sem(batch),
            sem(batch),
            sem(batch),
            sem(batch),
            vmem(BOXES, half, width),
            vmem(5, half, width),
            wide(half, width),
            sem(BOXES),
            sem(5),
            sem(line, 2),
            sem(line),
            sem(line, 2),
        ],
        compiler_params=pltpu.CompilerParams(
            collective_id=3, has_side_effects=True, vmem_limit_bytes=62 * MIB
        ),
    )(
        cot,
        totals,
        hidden,
        projected,
        context,
        in_full,
        out_full,
        tokens,
        part,
        cores,
        *gains,
        *tables,
    )[:5]


def gradients_kernel(
    line,
    normed,
    grads,
    gains_ref,
    xe_ref,
    ce_ref,
    act_ref,
    dgate_ref,
    dup_ref,
    in_total,
    gains_all,
    gate_total,
    up_total,
    down_total,
    parts,
    cores,
    firsts,
    rights,
    lefts,
    tree_send,
    tree_receive,
    gain_send,
    gain_receive,
    gain_local,
    wide_rows,
    slim_rows,
    gate_sum,
    up_sum,
    down_sum,
    load_sem,
    save_sem,
):
    narrow, spot = Spot(line, False), Spot(line, True)
    experts, count, _ = xe_ref.shape
    share = wide_rows.shape[1]
    turns = count // share
    pieces = [
        (expert, kind, turn)
        for expert in range(experts)
        for kind in range(2)
        for turn in range(turns)
    ]

    def loads(index):
        expert, kind, turn = pieces[index]
        slot = index % 2
        rows = pl.ds(turn * share, share)
        slim = (dgate_ref, dup_ref) if kind == 0 else (act_ref,)
        return [
            pltpu.make_async_copy(
                (xe_ref, ce_ref)[kind].at[expert, rows], wide_rows.at[slot], load_sem.at[slot, 0]
            )
        ] + [
            pltpu.make_async_copy(
                ref.at[expert, rows], slim_rows.at[slot, i], load_sem.at[slot, 1 + i]
            )
            for i, ref in enumerate(slim)
        ]

    def saves(expert, kind):
        pairs = ((gate_sum, gate_total), (up_sum, up_total))
        if kind:
            return [pltpu.make_async_copy(down_sum, down_total.at[expert], save_sem.at[2])]
        return [
            pltpu.make_async_copy(source, target.at[expert], save_sem.at[i])
            for i, (source, target) in enumerate(pairs)
        ]

    for copy in loads(0):
        copy.start()
    spot.greet()
    gains = Spread(
        spot,
        gains_ref,
        lambda block, half: gains_all.at[block, half],
        gain_send,
        gain_receive,
        gain_local.at[0],
    )
    gains.begin()
    depth, width = in_total.shape
    tree = Collect(
        narrow,
        lambda block, half: rows_at(parts, block, depth),
        in_total,
        cores,
        firsts,
        rights,
        lefts,
        tree_send,
        tree_receive,
    )
    chunk = PLANE * depth

    def plane(step, _):
        z = lax.rem(narrow.z + 1 + step, line)
        columns = pl.ds(pl.multiple_of(z * chunk, LANES), chunk)
        for start in range(0, width, CHUNK):
            parts[pl.ds(pl.multiple_of(z * chunk, 16), chunk), start : start + CHUNK] = (
                lax.dot_general(
                    normed[:, columns],
                    grads[:, start : start + CHUNK],
                    TRANSPOSED_LEFT,
                    preferred_element_type=jnp.float32,
                ).astype(jnp.bfloat16)
            )
        tree.begin(z)
        return 0

    lax.fori_loop(0, line, plane, 0)

    def piece(index):
        expert, kind, turn = pieces[index]
        slot = index % 2
        for copy in loads(index):
            copy.wait()
        if index + 1 < len(pieces):
            for copy in loads(index + 1):
                copy.start()
        if turn == 0 and expert:
            for copy in saves(expert - 1, kind):
                copy.wait()
        size = wide_rows.shape[2] // 4

        def add(target, place, left, right):
            product = lax.dot_general(
                left, right, TRANSPOSED_LEFT, preferred_element_type=jnp.float32
            )
            if turn:
                product = target[place] + product
            target[place] = product

        def part(step, _):
            at = pl.ds(pl.multiple_of(step * size, LANES), size)
            if kind:
                add(down_sum, (slice(None), at), slim_rows[slot, 0], wide_rows[slot, :, at])
            else:
                for i, target in enumerate((gate_sum, up_sum)):
                    add(target, (at, slice(None)), wide_rows[slot, :, at], slim_rows[slot, i])
            return 0

        lax.fori_loop(0, 4, part, 0)
        if turn == turns - 1:
            for copy in saves(expert, kind):
                copy.start()

    tree.cross()
    work = tree.tasks()
    steps = list(range(1, gains.steps()))
    filler = list(range(len(pieces)))
    while work or filler:
        for _ in range(2 if len(filler) > len(work) else 1):
            if filler:
                piece(filler.pop(0))
        if work:
            work.pop(0)()
        if steps:
            gains.step(steps.pop(0))
    gains.finish()
    for copy in saves(experts - 1, 0) + saves(experts - 1, 1):
        copy.wait()


def run_gradients(normed, grads, gains, expert_rows, fsdp_count):
    line = fsdp_count // PLANE
    width = grads.shape[1]
    experts, count, depth = expert_rows[0].shape
    units = expert_rows[2].shape[2]
    share = 2 * CHUNK if count % (2 * CHUNK) == 0 else count // (2 * line)
    shape = (normed.shape[1] // fsdp_count, width)
    sends, receives = spread_count(line, True)
    inside = pl.BlockSpec(memory_space=pltpu.VMEM)
    anywhere = pl.BlockSpec(memory_space=pl.ANY)
    return pl.pallas_call(
        functools.partial(gradients_kernel, line),
        out_shape=(
            jax.ShapeDtypeStruct(shape, jnp.float32),
            jax.ShapeDtypeStruct((fsdp_count, 2, *gains.shape), jnp.float32),
            jax.ShapeDtypeStruct((experts, depth, units), jnp.float32),
            jax.ShapeDtypeStruct((experts, depth, units), jnp.float32),
            jax.ShapeDtypeStruct((experts, units, depth), jnp.float32),
        ),
        in_specs=[inside, inside] + [anywhere] * 6,
        out_specs=(inside,) + (anywhere,) * 4,
        scratch_shapes=[
            pltpu.VMEM((normed.shape[1], width), jnp.bfloat16),
            *collect_scratch(line, shape),
            pltpu.SemaphoreType.DMA((sends,)),
            pltpu.SemaphoreType.DMA((receives,)),
            pltpu.SemaphoreType.DMA((1,)),
            pltpu.VMEM((2, share, depth), jnp.bfloat16),
            pltpu.VMEM((2, 2, share, units), jnp.bfloat16),
            pltpu.VMEM((depth, units), jnp.float32),
            pltpu.VMEM((depth, units), jnp.float32),
            pltpu.VMEM((units, depth), jnp.float32),
            pltpu.SemaphoreType.DMA((2, 3)),
            pltpu.SemaphoreType.DMA((3,)),
        ],
        compiler_params=pltpu.CompilerParams(
            collective_id=4, has_side_effects=True, vmem_limit_bytes=60 * MIB
        ),
    )(normed, grads, gains, *expert_rows)


def experts_kernel(
    line,
    slots,
    own_ref,
    cot_ref,
    info_ref,
    gate_ref,
    up_ref,
    down_ref,
    all_ref,
    total_ref,
    xe_all,
    ce_all,
    act_all,
    dgate_all,
    dup_all,
    part,
    cores,
    seconds,
    firsts,
    ends,
    hidden_w,
    down_w,
    x_rows,
    c_rows,
    xe,
    ce,
    acts,
    dgates,
    dups,
    hidden_grads,
    picks,
    weigh,
    rows,
    stage,
    inbox,
    outbox,
    summed,
    tree_send,
    tree_receive,
    tree_local,
    load_sem,
    save_sem,
    stage_sem,
    inbox_sem,
    outbox_sem,
    total_sem,
    weight_sem,
    core_receive,
    second_receive,
    first_receive,
    end_receive,
):
    spot = Spot(line, True)
    z, core = spot.z, spot.core
    batch, half, width = own_ref.shape
    length = 2 * half
    units = down_ref.shape[1]
    groups = batch * line
    weights = [
        pltpu.make_async_copy(source, target, weight_sem.at[i])
        for i, (source, target) in enumerate(
            [(down_ref, down_w)]
            + [(gate_ref.at[e], hidden_w.at[e, :, pl.ds(0, units)]) for e in range(2)]
            + [(up_ref.at[e], hidden_w.at[e, :, pl.ds(units, units)]) for e in range(2)]
        )
    ]
    for copy in weights:
        copy.start()
    rows[...] = jnp.zeros_like(rows)
    spot.greet()

    def half_of(ref, index):
        return rows_at(ref, index, half)

    trees = [
        Spread(
            spot,
            own_ref.at[i],
            lambda block, side, i=i: half_of(all_ref.at[i, block], side),
            tree_send.at[i],
            tree_receive.at[i],
            tree_local.at[i],
        )
        for i in range(batch)
    ]
    run_trees(trees[:1])
    for tree in trees[1:]:
        tree.begin()
    for copy in weights:
        copy.wait()

    plane_of = functools.partial(plane_in_turn, line)

    def load_group(group, member):
        at = lax.div(group, line)
        sequence = plane_of(group) * PLANE + member
        slot = member % 2
        return [
            pltpu.make_async_copy(all_ref.at[at, sequence], x_rows.at[slot], load_sem.at[0, slot]),
            pltpu.make_async_copy(cot_ref.at[at, sequence], c_rows.at[slot], load_sem.at[1, slot]),
        ]

    def saves(group):
        to = lambda ref, expert: rows_at(ref.at[expert], group, PLANE * slots)
        pairs = ((xe, xe_all), (ce, ce_all), (acts, act_all), (dgates, dgate_all), (dups, dup_all))
        return [
            pltpu.make_async_copy(source.at[expert], to(target, expert), save_sem.at[2 * i + expert])
            for i, (source, target) in enumerate(pairs)
            for expert in range(2)
        ]

    def staged(unit, y, mine):
        slot = y * 2 + mine
        if mine:
            return pltpu.make_async_copy(stage.at[slot], part.at[unit, y], stage_sem.at[slot])
        return spot.send(
            stage.at[slot], cores.at[unit, y], stage_sem.at[slot], core_receive.at[unit, y], CORE
        )

    def combine(unit, y):
        for mine in range(2):
            member = y * 2 + (core if mine else 1 - core)
            for start in range(0, width, CHUNK):
                stage[y * 2 + mine, :, start : start + CHUNK] = lax.dot_general(
                    picks[member],
                    rows[member, :, start : start + CHUNK],
                    TRANSPOSED_LEFT,
                    preferred_element_type=jnp.float32,
                ).astype(jnp.bfloat16)
            staged(unit, y, mine).start()

    def pick(group, member):
        slot = member % 2
        for copy in load_group(group, member):
            copy.wait()
        if member + 1 < PLANE:
            for copy in load_group(group, member + 1):
                copy.start()
        sequence = plane_of(group) * PLANE + member
        info = info_ref[lax.div(group, line) * line * PLANE + sequence]
        places = lax.broadcasted_iota(jnp.int32, (2 * LANES, length), 0)
        lower = places < LANES
        ranks = jnp.where(lower, info[0:1], info[1:2] + float(LANES)).astype(jnp.int32)
        some = jnp.where(lower, info[0:1], info[1:2]) >= 0.0
        hot = jnp.logical_and(ranks == places, some)
        chosen = hot.astype(jnp.float32).astype(jnp.bfloat16)
        picks[member] = chosen
        shares = jnp.where(hot, jnp.where(lower, info[2:3], info[3:4]), 0.0)
        column = jnp.sum(shares, axis=1, keepdims=True)
        here = pl.ds(member * slots, slots)
        for expert in range(2):
            weigh[expert, here, :] = jnp.broadcast_to(
                column[expert * LANES : expert * LANES + slots], (slots, LANES)
            )
        for source, target in ((x_rows, xe), (c_rows, ce)):
            for start in range(0, width, CHUNK):
                selected = jnp.dot(
                    chosen,
                    source[slot, :, start : start + CHUNK],
                    preferred_element_type=jnp.float32,
                ).astype(jnp.bfloat16)
                for expert in range(2):
                    target[expert, here, start : start + CHUNK] = selected[
                        expert * LANES : expert * LANES + slots
                    ]

    def keep(expert, product, start):
        at = pl.ds(expert * LANES, slots)
        for one in range(PLANE):
            rows[one, at, start : start + CHUNK] = product[one * slots : (one + 1) * slots].astype(
                jnp.bfloat16
            )

    def forward(expert):
        hidden = jnp.dot(xe[expert], hidden_w[expert], preferred_element_type=jnp.float32)
        gate, up = hidden[:, :units], hidden[:, units:]
        sigmoid = jax.nn.sigmoid(gate)
        silu = gate * sigmoid
        scale = weigh[expert, :, 0:1]
        acts[expert] = (silu * up * scale).astype(jnp.bfloat16)
        act_grads = scale * lax.dot_general(
            ce[expert], down_w[expert], TRANSPOSED_RIGHT, preferred_element_type=jnp.float32
        )
        gate_grads = (act_grads * up * (sigmoid * (1.0 + gate * (1.0 - sigmoid)))).astype(
            jnp.bfloat16
        )
        up_grads = (act_grads * silu).astype(jnp.bfloat16)
        dgates[expert] = gate_grads
        dups[expert] = up_grads
        hidden_grads[expert, :, :units] = gate_grads
        hidden_grads[expert, :, units:] = up_grads
        for start in range(0, width, CHUNK):
            keep(
                expert,
                jnp.dot(
                    acts[expert],
                    down_w[expert, :, start : start + CHUNK],
                    preferred_element_type=jnp.float32,
                ),
                start,
            )

    def backward(expert):
        for start in range(0, width, CHUNK):
            keep(
                expert,
                lax.dot_general(
                    hidden_grads[expert],
                    hidden_w[expert, start : start + CHUNK, :],
                    TRANSPOSED_RIGHT,
                    preferred_element_type=jnp.float32,
                ),
                start,
            )

    units_all = 2 * groups

    def inside(unit):
        valid = jnp.logical_and(unit >= 0, unit < units_all)
        return jnp.logical_and(valid, jnp.logical_or(unit >= 2 * line, unit % 2 == BACK))

    def ready(unit):
        @pl.when(jnp.logical_and(unit >= 0, unit < units_all))
        def _():
            for y in range(2):
                staged(unit, y, 1).wait()
                staged(unit, y, 0).wait_send()
                place, semaphore = cores.at[unit, y], core_receive.at[unit, y]
                spot.send(place, place, outbox_sem.at[0], semaphore, CORE).wait_recv()

    def done(unit, tensor, into):
        into(summed)
        copy = pltpu.make_async_copy(
            summed, total_ref.at[lax.div(unit, 2 * line), tensor], total_sem.at[0]
        )
        copy.start()
        copy.wait()

    sums = Sums(
        spot,
        lambda unit, y: part.at[unit, y],
        lambda unit, y: cores.at[unit, y],
        (seconds, firsts, ends),
        inbox,
        outbox,
        (inbox_sem, outbox_sem, second_receive, first_receive, end_receive),
        lambda unit: plane_of(lax.div(jnp.maximum(unit, 0), 2)),
        inside,
        ready,
        done,
        2,
    )

    def tree_turn(half_step, last):
        for i in range(1, batch):
            turn = half_step - (i - 1) * 2 * line
            if last:
                when(turn == 2 * line - 1, trees[i].finish)
            else:
                inner = jnp.logical_and(turn >= 0, turn < 2 * line - 1)
                when(inner, lambda: trees[i].step(turn + 1))

    def begin_pick(group):
        for copy in load_group(group, 0):
            copy.start()

    begin_pick(0)
    for member in range(PLANE):
        pick(0, member)

    def step_body(step, _):
        busy = step < groups
        more = step + 1 < groups
        for parity in range(2):
            half_step = step * 2 + parity
            tree_turn(half_step, False)
            sums.retire(half_step, parity)
            tasks = sums.tasks(half_step, parity)
            pieces = []
            for expert in range(2):
                pieces.append(functools.partial((forward, backward)[parity], expert))
            if parity == 0:
                pieces.append(lambda: [copy.start() for copy in saves(step)])
            for y in range(2):
                pieces.append(functools.partial(combine, half_step, y))
            pieces = [functools.partial(when, busy, piece) for piece in pieces]
            if parity == 1:

                def prepare():
                    for copy in saves(step):
                        copy.wait()
                    begin_pick(step + 1)

                tree_end = functools.partial(tree_turn, half_step, True)
                pieces += [tree_end, functools.partial(when, more, prepare)]
                for member in range(PLANE):
                    pieces.append(
                        functools.partial(when, more, functools.partial(pick, step + 1, member))
                    )
            sums.weave(tasks, pieces)
        return 0

    half_steps = sums.half_steps(units_all)
    lax.fori_loop(0, -(-half_steps // 2), step_body, 0)
    end = -(-half_steps // 2) * 2
    for parity in range(2):
        sums.retire(jnp.int32(end + parity), parity)
    for copy in saves(groups - 1):
        copy.wait()


def run_experts(rows, cot_all, info, w_gate, w_up, w_down, capacity, fsdp_count):
    line = fsdp_count // PLANE
    batch, half, width = rows.shape
    length = 2 * half
    units = w_down.shape[1]
    slots = -(-capacity // 16) * 16
    groups = batch * line
    count = groups * PLANE * slots
    taken = PLANE * slots
    sends, receives = spread_count(line, True)
    shape = lambda *dims: jax.ShapeDtypeStruct(dims, jnp.bfloat16)
    block = (half, width)
    anywhere = pl.BlockSpec(memory_space=pl.ANY)
    vmem = lambda *dims: pltpu.VMEM(dims, jnp.bfloat16)
    sem = lambda *dims: pltpu.SemaphoreType.DMA(dims)
    return pl.pallas_call(
        functools.partial(experts_kernel, line, slots),
        out_shape=(
            shape(batch, fsdp_count, length, width),
            jax.ShapeDtypeStruct((batch, 2, *block), jnp.float32),
            shape(2, count, width),
            shape(2, count, width),
            shape(2, count, units),
            shape(2, count, units),
            shape(2, count, units),
            shape(2 * groups, 2, length, width),
            shape(2 * groups, 2, length, width),
            shape(2 * groups, 2, *block),
            shape(2 * groups, *block),
            shape(2 * groups, 2, *block),
        ),
        in_specs=[
            anywhere,
            anywhere,
            pl.BlockSpec(memory_space=pltpu.VMEM),
            anywhere,
            anywhere,
            anywhere,
        ],
        out_specs=(anywhere,) * 12,
        scratch_shapes=[
            vmem(2, width, 2 * units),
            vmem(2, units, width),
            vmem(2, length, width),
            vmem(2, length, width),
            vmem(2, taken, width),
            vmem(2, taken, width),
            vmem(2, taken, units),
            vmem(2, taken, units),
            vmem(2, taken, units),
            vmem(2, taken, 2 * units),
            vmem(PLANE, 2 * LANES, length),
            pltpu.VMEM((2, taken, LANES), jnp.float32),
            vmem(PLANE, 2 * LANES, width),
            vmem(PLANE, length, width),
            vmem(12, *block),
            vmem(10, *block),
            pltpu.VMEM(block, jnp.float32),
            sem(batch, sends),
            sem(batch, receives),
            sem(batch),
            sem(2, 2),
            sem(10),
            sem(PLANE),
            sem(12),
            sem(10),
            sem(1),
            sem(5),
            sem(2 * groups, 2),
            sem(2 * groups, 2),
            sem(2 * groups),
            sem(2 * groups, 2),
        ],
        compiler_params=pltpu.CompilerParams(
            collective_id=2, has_side_effects=True, vmem_limit_bytes=60 * MIB
        ),
    )(rows, cot_all, info, w_gate, w_up, w_down)[1:9]


def packed_picks(routes, gates):
    length = routes.shape[2]
    packed = jnp.concatenate([routes[:, 0].astype(jnp.float32), gates[:, 0]], axis=-1)
    packed = jnp.swapaxes(packed, 1, 2).reshape(-1, length)
    return jnp.pad(packed, ((0, 0), (0, -length % LANES)))


def slot_info(packed, batch, top, length, local_experts):
    fsdp_count = packed.shape[0]
    packed = packed[..., :length].reshape(fsdp_count, batch, 1, 2 * top, length)
    packed = jnp.swapaxes(packed, 0, 1)
    experts = lax.axis_index(FSDP) * local_experts + jnp.arange(local_experts, dtype=jnp.int32)
    same = packed[..., :top, :].astype(jnp.int32) == experts[:, None, None]
    hot = jnp.any(same, axis=3)
    shares = jnp.sum(jnp.where(same, packed[..., top:, :], 0.0), axis=3)
    position = jnp.arange(length)
    upper = (position[:, None] < position[None, :]).astype(jnp.bfloat16)
    rank = jnp.dot(
        hot.astype(jnp.bfloat16).reshape(-1, length), upper, preferred_element_type=jnp.float32
    )
    rank = jnp.where(hot, rank.reshape(hot.shape), -1.0)
    return jnp.concatenate([rank, shares], axis=2).reshape(-1, 2 * local_experts, length)


def gathered_layer(
    tokens,
    cotangent,
    norm1_gain,
    w_query,
    key_projection_weight,
    value_projection_weight,
    query_gain,
    key_gain,
    w_out,
    norm2_gain,
    w_gate,
    w_up,
    w_down,
    routes,
    gates,
):
    batch_count = tokens.shape[0]
    model_width = tokens.shape[3]
    sequence_length = routes.shape[2]
    half_length = tokens.shape[2]
    top_count = routes.shape[3]
    head_features = query_gain.shape[0]
    local_experts = w_gate.shape[0]
    fsdp_count = lax.axis_size(FSDP)
    all_experts = local_experts * fsdp_count
    capacity = 7 * top_count * sequence_length // (6 * all_experts)
    query_width = w_query.shape[1]
    kv_width = key_projection_weight.shape[1]
    kv_heads = kv_width // head_features
    cosine_table, sine_values = rotary_tables(sequence_length, head_features)
    weight_in = jnp.concatenate([w_query, key_projection_weight, value_projection_weight], axis=1)
    half_signs = jnp.where(jnp.arange(head_features) < head_features // 2, -1.0, 1.0)
    tables = (cosine_table[:, 0], sine_values[:, 0] * half_signs)
    gains = [gain[None, :] for gain in (norm1_gain, norm2_gain, query_gain, key_gain)]
    cot_all, in_full, out_full, picks, normed, projected, contexts, hidden, second = run_forward(
        tokens[:, 0],
        cotangent[:, 0],
        weight_in,
        w_out,
        packed_picks(routes, gates),
        gains,
        tables,
        fsdp_count,
        kv_heads,
    )
    info = slot_info(picks, batch_count, top_count, sequence_length, local_experts)
    totals, *expert_rows, part, cores = run_experts(
        second, cot_all, info, w_gate, w_up, w_down, capacity, fsdp_count
    )
    block_out, input_grad, projected_grads, out_sum, gain_grads = run_backward(
        cotangent[:, 0],
        totals,
        hidden,
        projected,
        contexts,
        in_full,
        out_full,
        tokens[:, 0],
        part,
        cores,
        gains,
        tables,
        fsdp_count,
        kv_heads,
    )
    rows = batch_count * sequence_length
    in_sum, gains_all, *expert_grads = run_gradients(
        normed.reshape(rows, -1),
        projected_grads.reshape(rows, -1),
        gain_grads,
        expert_rows,
        fsdp_count,
    )
    gains_sum = jnp.sum(gains_all, axis=(0, 1))
    return (
        block_out[:, None],
        input_grad[:, None],
        gains_sum[0],
        in_sum[:, :query_width],
        in_sum[:, query_width : query_width + kv_width],
        in_sum[:, query_width + kv_width :],
        gains_sum[2, :head_features],
        gains_sum[3, :head_features],
        out_sum,
        gains_sum[1],
        *expert_grads,
    )


def shards(*arrays):
    tokens, routes, w_gate = arrays[0], arrays[13], arrays[10]
    fsdp_count = lax.axis_size(FSDP)
    gathered = fsdp_count * routes.shape[2] * tokens.shape[3] * 2
    fits = gathered <= 24 * MIB and fsdp_count % PLANE == 0 and lax.axis_size(TP) == 2
    if fits and w_gate.shape[0] == 2:
        return gathered_layer(*arrays)
    return exchanged_layer(*arrays)


def solution(mesh):
    in_specs = (
        P(None, "fsdp", "tp", None),
        P(None, "fsdp", "tp", None),
        P(),
        P("fsdp", "tp"),
        P("fsdp", "tp"),
        P("fsdp", "tp"),
        P(),
        P(),
        P("tp", "fsdp"),
        P(),
        P("fsdp", None, "tp"),
        P("fsdp", None, "tp"),
        P("fsdp", "tp", None),
        P(None, "fsdp", None, None),
        P(None, "fsdp", None, None),
    )
    out_specs = (
        P(None, "fsdp", "tp", None),
        P(None, "fsdp", "tp", None),
        P(),
        P("fsdp", "tp"),
        P("fsdp", "tp"),
        P("fsdp", "tp"),
        P(),
        P(),
        P("tp", "fsdp"),
        P(),
        P("fsdp", None, "tp"),
        P("fsdp", None, "tp"),
        P("fsdp", "tp", None),
    )
    return jax.shard_map(shards, mesh=mesh, in_specs=in_specs, out_specs=out_specs, check_vma=False)
```

```python
import functools

import jax
import jax.numpy as jnp
from jax import lax
from jax.experimental import pallas as pl
from jax.experimental.pallas import tpu as pltpu
from jax.sharding import PartitionSpec as P

BLOCK = 256


EPSILON = 1e-06
ROPE_BASE = 1000000.0
MASKED = -1e30
TILE_PICKS = 128


def rms_scale(row_block, gain_row):
    return (
        row_block
        * lax.rsqrt(jnp.mean(row_block * row_block, axis=-1, keepdims=True) + EPSILON)
        * gain_row
    )


def rotary_tables(sequence_length, head_width):
    half_width = head_width // 2
    inverse = ROPE_BASE ** (-2.0 * jnp.arange(half_width, dtype=jnp.float32) / head_width)
    angles = jnp.arange(sequence_length, dtype=jnp.float32)[:, None] * inverse[None, :]
    cosine_table = jnp.concatenate([jnp.cos(angles), jnp.cos(angles)], axis=-1)[:, None, :]
    sine_values = jnp.concatenate([jnp.sin(angles), jnp.sin(angles)], axis=-1)[:, None, :]
    return (cosine_table, sine_values)


def rotate(head_rows, cosine_table, sine_values):
    half_width = head_rows.shape[-1] // 2
    turned = jnp.concatenate([-head_rows[..., half_width:], head_rows[..., :half_width]], axis=-1)
    return head_rows * cosine_table + turned * sine_values


def prepare_heads(projected, gain_row, cosine_table, sine_values):
    return rotate(rms_scale(projected, gain_row), cosine_table, sine_values)


def swiglu(gate_act, up_act):
    return jax.nn.silu(gate_act) * up_act


def slot_tables(route_rows, gate_rows, expert_count, capacity):
    sequence_length = route_rows.shape[0]
    top_count = route_rows.shape[1]
    pick_count = sequence_length * top_count
    tile_count = pick_count // TILE_PICKS
    flat_routes = route_rows.reshape(-1)
    onehot = (flat_routes[:, None] == jnp.arange(expert_count, dtype=jnp.int32)[None, :]).astype(
        jnp.bfloat16
    )
    tiles = onehot.reshape(tile_count, TILE_PICKS, expert_count)
    positions = jnp.arange(TILE_PICKS, dtype=jnp.int32)
    lower = (positions[None, :] < positions[:, None]).astype(jnp.bfloat16)
    within = jnp.einsum("ij,bje->bie", lower, tiles, preferred_element_type=jnp.float32)
    tile_totals = jnp.sum(tiles.astype(jnp.float32), axis=1)
    offsets = jnp.cumsum(tile_totals, axis=0) - tile_totals
    before = within + offsets[:, None, :]
    slot_rank = jnp.sum(before * tiles.astype(jnp.float32), axis=-1).reshape(-1).astype(jnp.int32)
    slot_index = flat_routes * capacity + slot_rank
    pick_ids = jnp.arange(pick_count, dtype=jnp.int32) // top_count
    slot_owner = (
        jnp.full((expert_count * capacity,), sequence_length, jnp.int32)
        .at[slot_index]
        .set(pick_ids)
    )
    slot_weight = (
        jnp.zeros((expert_count * capacity,), jnp.float32).at[slot_index].set(gate_rows.reshape(-1))
    )
    return (slot_index, slot_owner, slot_weight)


def exchanged_layer(
    tokens,
    cotangent,
    norm1_gain,
    w_query,
    key_projection_weight,
    value_projection_weight,
    query_gain,
    key_gain,
    w_out,
    norm2_gain,
    w_gate,
    w_up,
    w_down,
    routes,
    gates,
):
    batch_count = tokens.shape[0]
    model_width = tokens.shape[3]
    sequence_length = routes.shape[2]
    top_count = routes.shape[3]
    head_features = query_gain.shape[0]
    local_experts = w_gate.shape[0]
    fsdp_count = lax.axis_size("fsdp")
    all_experts = local_experts * fsdp_count
    capacity = 7 * top_count * sequence_length // (6 * all_experts)
    query_heads = w_query.shape[1] // head_features
    kv_heads = key_projection_weight.shape[1] // head_features
    group_size = query_heads // kv_heads
    score_scale = head_features ** (-0.5)
    cosine_table, sine_values = rotary_tables(sequence_length, head_features)
    block_ids = jnp.arange(sequence_length, dtype=jnp.int32) // BLOCK
    visible = (block_ids[None, :] <= block_ids[:, None])[None, None]
    first_gain = norm1_gain.astype(jnp.float32)
    second_gain = norm2_gain.astype(jnp.float32)
    query_factor_scale = query_gain.astype(jnp.float32)
    key_scale = key_gain.astype(jnp.float32)
    zero_row = jnp.zeros((1, model_width), jnp.bfloat16)
    buffer_shape = (fsdp_count, local_experts, capacity, model_width)

    def masked_scores(query_fourfold, key_rows):
        raw_scores = (
            jnp.einsum(
                "qcgd,kcd->cgqk", query_fourfold, key_rows, preferred_element_type=jnp.float32
            )
            * score_scale
        )
        return jnp.where(visible, raw_scores, MASKED)

    def prep_heads(projected, gain_row):
        return prepare_heads(projected, gain_row, cosine_table, sine_values)

    gain_sums = (
        jnp.zeros((model_width,), jnp.float32),
        jnp.zeros((model_width,), jnp.float32),
        jnp.zeros((head_features,), jnp.float32),
        jnp.zeros((head_features,), jnp.float32),
    )
    expert_grads = (
        jnp.zeros(w_gate.shape, jnp.float32),
        jnp.zeros(w_up.shape, jnp.float32),
        jnp.zeros(w_down.shape, jnp.float32),
    )
    attn_grads = tuple(
        (
            jnp.zeros(weight_part.shape, jnp.float32)
            for weight_part in (w_query, key_projection_weight, value_projection_weight, w_out)
        )
    )
    outputs = []
    input_grads = []
    for batch_index in range(batch_count):
        query_full, key_full, value_full, out_full = (
            lax.all_gather(w_query, "fsdp", axis=0, tiled=True),
            lax.all_gather(key_projection_weight, "fsdp", axis=0, tiled=True),
            lax.all_gather(value_projection_weight, "fsdp", axis=0, tiled=True),
            lax.all_gather(w_out, "fsdp", axis=1, tiled=True),
        )
        own_rows = tokens[batch_index, 0].astype(jnp.float32)
        own_cot = cotangent[batch_index, 0]
        route_rows = routes[batch_index, 0]
        gate_rows = gates[batch_index, 0]
        first_normed = rms_scale(own_rows, first_gain).astype(jnp.bfloat16)
        normed_all = lax.all_gather(first_normed, "tp", axis=0, tiled=True)
        query_projected = jnp.dot(
            normed_all, query_full, preferred_element_type=jnp.float32
        ).reshape(sequence_length, query_heads, head_features)
        key_projected = jnp.dot(normed_all, key_full, preferred_element_type=jnp.float32).reshape(
            sequence_length, kv_heads, head_features
        )
        value_row_list = (
            jnp.dot(normed_all, value_full, preferred_element_type=jnp.float32)
            .astype(jnp.bfloat16)
            .reshape(sequence_length, kv_heads, head_features)
        )
        query_rot = prep_heads(query_projected, query_factor_scale).astype(jnp.bfloat16)
        key_rot = prep_heads(key_projected, key_scale).astype(jnp.bfloat16)
        query_fourfold = query_rot.reshape(sequence_length, kv_heads, group_size, head_features)
        scores = masked_scores(query_fourfold, key_rot)
        row_max = jnp.max(scores, axis=-1, keepdims=True)
        exp_scores = jnp.exp(scores - row_max)
        totals = jnp.sum(exp_scores, axis=-1, keepdims=True)
        log_total = row_max + jnp.log(totals)
        prob_rows = (exp_scores / totals).astype(jnp.bfloat16)
        context = (
            jnp.einsum(
                "cgqk,kcd->qcgd", prob_rows, value_row_list, preferred_element_type=jnp.float32
            )
            .astype(jnp.bfloat16)
            .reshape(sequence_length, query_heads * head_features)
        )
        attn_own = lax.psum_scatter(
            jnp.dot(context, out_full, preferred_element_type=jnp.float32).astype(jnp.bfloat16),
            "tp",
            scatter_dimension=0,
            tiled=True,
        ).astype(jnp.float32)
        hidden_own = own_rows + attn_own
        second_normed = rms_scale(hidden_own, second_gain).astype(jnp.bfloat16)
        normed_two, cot_all = (
            lax.all_gather(second_normed, "tp", axis=0, tiled=True),
            lax.all_gather(own_cot, "tp", axis=0, tiled=True),
        )
        slot_index, slot_owner, slot_weight = slot_tables(
            route_rows, gate_rows, all_experts, capacity
        )
        padded_rows = jnp.concatenate([normed_two, zero_row], axis=0)
        send_rows = padded_rows[slot_owner].reshape(buffer_shape)
        expert_in = lax.all_to_all(send_rows, "fsdp", split_axis=0, concat_axis=0, tiled=True)
        gate_act = jnp.einsum(
            "sekd,edf->sekf", expert_in, w_gate, preferred_element_type=jnp.float32
        )
        up_act = jnp.einsum("sekd,edf->sekf", expert_in, w_up, preferred_element_type=jnp.float32)
        act_rows = swiglu(gate_act, up_act).astype(jnp.bfloat16)
        expert_out = jnp.einsum(
            "sekf,efd->sekd", act_rows, w_down, preferred_element_type=jnp.float32
        )
        returned = lax.all_to_all(
            expert_out.astype(jnp.bfloat16), "fsdp", split_axis=0, concat_axis=0, tiled=True
        ).astype(expert_out.dtype)
        picked = returned.reshape(all_experts * capacity, model_width)[slot_index].reshape(
            sequence_length, top_count, model_width
        )
        moe_part = jnp.sum(picked * gate_rows[:, :, None], axis=1)
        moe_own = lax.psum_scatter(
            moe_part.astype(jnp.bfloat16), "tp", scatter_dimension=0, tiled=True
        ).astype(jnp.float32)
        outputs.append((hidden_own + moe_own).astype(jnp.bfloat16))
        cot_padded = jnp.concatenate([cot_all, zero_row], axis=0)
        send_grads = (
            (slot_weight[:, None] * cot_padded[slot_owner])
            .astype(jnp.bfloat16)
            .reshape(buffer_shape)
        )
        out_grads = lax.all_to_all(send_grads, "fsdp", split_axis=0, concat_axis=0, tiled=True)
        act_grads = jnp.einsum(
            "sekd,efd->sekf", out_grads, w_down, preferred_element_type=jnp.float32
        )
        _, swiglu_back = jax.vjp(swiglu, gate_act, up_act)
        gate_grads, up_grads = swiglu_back(act_grads)
        gate_grads = gate_grads.astype(jnp.bfloat16)
        up_grads = up_grads.astype(jnp.bfloat16)
        expert_grads = (
            expert_grads[0]
            + jnp.einsum(
                "sekd,sekf->edf", expert_in, gate_grads, preferred_element_type=jnp.float32
            ),
            expert_grads[1]
            + jnp.einsum("sekd,sekf->edf", expert_in, up_grads, preferred_element_type=jnp.float32),
            expert_grads[2]
            + jnp.einsum("sekf,sekd->efd", act_rows, out_grads, preferred_element_type=jnp.float32),
        )
        input_part = jnp.einsum(
            "sekf,edf->sekd", gate_grads, w_gate, preferred_element_type=jnp.float32
        ) + jnp.einsum("sekf,edf->sekd", up_grads, w_up, preferred_element_type=jnp.float32)
        input_back = lax.all_to_all(
            input_part.astype(jnp.bfloat16), "fsdp", split_axis=0, concat_axis=0, tiled=True
        ).astype(input_part.dtype)
        normed_grads = jnp.sum(
            input_back.reshape(all_experts * capacity, model_width)[slot_index].reshape(
                sequence_length, top_count, model_width
            ),
            axis=1,
        )
        normed_own = lax.psum_scatter(
            normed_grads.astype(jnp.bfloat16), "tp", scatter_dimension=0, tiled=True
        ).astype(jnp.float32)
        _, second_back = jax.vjp(rms_scale, hidden_own, second_gain)
        hidden_part, second_gain_grad = second_back(normed_own)
        hidden_grad = own_cot.astype(jnp.float32) + hidden_part
        attn_grad_all = lax.all_gather(hidden_grad.astype(jnp.bfloat16), "tp", axis=0, tiled=True)
        out_weight_grad = jnp.einsum(
            "th,td->hd", context, attn_grad_all, preferred_element_type=jnp.float32
        )
        context_grad = (
            jnp.einsum("td,hd->th", attn_grad_all, out_full, preferred_element_type=jnp.float32)
            .astype(jnp.bfloat16)
            .reshape(sequence_length, kv_heads, group_size, head_features)
        )
        exp_again = jnp.exp(masked_scores(query_fourfold, key_rot) - log_total)
        probs_again = exp_again.astype(jnp.bfloat16)
        prob_grads = jnp.einsum(
            "qcgd,kcd->cgqk", context_grad, value_row_list, preferred_element_type=jnp.float32
        )
        value_grads = (
            jnp.einsum(
                "cgqk,qcgd->kcd", probs_again, context_grad, preferred_element_type=jnp.float32
            )
            .astype(jnp.bfloat16)
            .reshape(sequence_length, kv_heads * head_features)
        )
        score_grads = (
            exp_again * (prob_grads - jnp.sum(exp_again * prob_grads, axis=-1, keepdims=True))
        ).astype(jnp.bfloat16)
        query_rot_grads = (
            jnp.einsum("cgqk,kcd->qcgd", score_grads, key_rot, preferred_element_type=jnp.float32)
            * score_scale
        ).reshape(sequence_length, query_heads, head_features)
        key_rot_grads = (
            jnp.einsum(
                "cgqk,qcgd->kcd", score_grads, query_fourfold, preferred_element_type=jnp.float32
            )
            * score_scale
        )
        _, query_back = jax.vjp(prep_heads, query_projected, query_factor_scale)
        query_proj_grads, query_gain_grad = query_back(query_rot_grads)
        _, key_back = jax.vjp(prep_heads, key_projected, key_scale)
        key_proj_grads, key_gain_grad = key_back(key_rot_grads)
        query_proj_grads = query_proj_grads.astype(jnp.bfloat16).reshape(
            sequence_length, query_heads * head_features
        )
        key_proj_grads = key_proj_grads.astype(jnp.bfloat16).reshape(
            sequence_length, kv_heads * head_features
        )
        first_normed_grads = (
            jnp.einsum(
                "tq,dq->td", query_proj_grads, query_full, preferred_element_type=jnp.float32
            )
            + jnp.einsum("tq,dq->td", key_proj_grads, key_full, preferred_element_type=jnp.float32)
            + jnp.einsum("tq,dq->td", value_grads, value_full, preferred_element_type=jnp.float32)
        )
        weight_parts = (
            jnp.einsum(
                "td,tq->dq", normed_all, query_proj_grads, preferred_element_type=jnp.float32
            ),
            jnp.einsum("td,tq->dq", normed_all, key_proj_grads, preferred_element_type=jnp.float32),
            jnp.einsum("td,tq->dq", normed_all, value_grads, preferred_element_type=jnp.float32),
            out_weight_grad,
        )
        first_own = lax.psum_scatter(
            first_normed_grads.astype(jnp.bfloat16), "tp", scatter_dimension=0, tiled=True
        ).astype(jnp.float32)
        _, first_back = jax.vjp(rms_scale, own_rows, first_gain)
        row_part, first_gain_grad = first_back(first_own)
        input_grads.append((hidden_grad + row_part).astype(jnp.bfloat16))
        gain_sums = (
            gain_sums[0] + first_gain_grad,
            gain_sums[1] + second_gain_grad,
            gain_sums[2] + query_gain_grad,
            gain_sums[3] + key_gain_grad,
        )
        attn_grads = jax.tree.map(
            jnp.add,
            attn_grads,
            (
                lax.psum_scatter(weight_parts[0], "fsdp", scatter_dimension=0, tiled=True),
                lax.psum_scatter(weight_parts[1], "fsdp", scatter_dimension=0, tiled=True),
                lax.psum_scatter(weight_parts[2], "fsdp", scatter_dimension=0, tiled=True),
                lax.psum_scatter(weight_parts[3], "fsdp", scatter_dimension=1, tiled=True),
            ),
        )
    summed = lax.psum((gain_sums[0], gain_sums[1], gain_sums[2], gain_sums[3]), ("fsdp", "tp"))
    block_out = jnp.stack(outputs)[:, None]
    input_grad = jnp.stack(input_grads)[:, None]
    return (
        block_out,
        input_grad,
        summed[0],
        attn_grads[0],
        attn_grads[1],
        attn_grads[2],
        summed[2],
        summed[3],
        attn_grads[3],
        summed[1],
        expert_grads[0],
        expert_grads[1],
        expert_grads[2],
    )


MESH = pl.DeviceIdType.MESH
FSDP, TP = "fsdp", "tp"
PLANE = 4
LANES = 128
MIB = 1 << 20
RIGHT, LEFT, FIRST, SECOND, CORE, CROSS = range(6)
TRANSPOSED_LEFT = (((0,), (0,)), ((), ()))
TRANSPOSED_RIGHT = (((1,), (1,)), ((), ()))
OUTPUT, BACK = range(2)
CHUNK = 512


class Spot:
    def __init__(self, line, wide, turned=True):
        self.line = line
        self.wide = wide
        self.turned = turned
        self.planes = 4 if wide else 2
        index = lax.axis_index(FSDP)
        self.x = lax.axis_index(TP)
        self.z = lax.div(index, PLANE)
        self.y = lax.rem(lax.div(index, 2), 2)
        self.core = lax.rem(index, 2)

    def side(self, core, first, second):
        flip_y, flip_x = first, second
        if self.wide and self.turned:
            flip_y = (1 - core) * first + core * second
            flip_x = core * first + (1 - core) * second
        return self.y + flip_y * (1 - 2 * self.y), self.x + flip_x * (1 - 2 * self.x)

    def block(self, core, first, second, z):
        y, x = self.side(core, first, second)
        return z * PLANE + y * 2 + core, x

    def device(self, kind):
        if kind == RIGHT:
            return self.block(self.core, 0, 0, self.z + 1)
        if kind == LEFT:
            return self.block(self.core, 0, 0, self.z - 1)
        if kind == CORE:
            return self.block(1 - self.core, 0, 0, self.z)
        if kind == CROSS:
            return self.block(self.core, 0, 0, self.z)[0], 1 - self.x
        return self.block(self.core, int(kind == FIRST), int(kind == SECOND), self.z)

    def kinds(self):
        return (FIRST, SECOND, CORE) if self.wide else (FIRST, CORE)

    def number(self, first, second, z):
        return (second * 2 + first) * self.line + z

    def order(self, step):
        if isinstance(step, int) and step == 0:
            return [(self.z, None)]
        return [(self.z - step, self.z - step >= 0), (self.z + step, self.z + step < self.line)]

    def greet(self):
        barrier = pltpu.get_barrier_semaphore()

        def signal(kind):
            pl.semaphore_signal(barrier, inc=1, device_id=self.device(kind), device_id_type=MESH)

        for kind in self.kinds():
            signal(kind)
        when(self.z + 1 < self.line, lambda: signal(RIGHT))
        when(self.z > 0, lambda: signal(LEFT))
        around = (self.z + 1 < self.line).astype(jnp.int32) + (self.z > 0).astype(jnp.int32)
        pl.semaphore_wait(barrier, len(self.kinds()) + around)

    def send(self, source, target, send_sem, receive_sem, kind):
        return pltpu.make_async_remote_copy(
            src_ref=source,
            dst_ref=target,
            send_sem=send_sem,
            recv_sem=receive_sem,
            device_id=self.device(kind),
            device_id_type=MESH,
        )


def when(condition, action):
    def run():
        action()

    if condition is None or condition is True:
        run()
    elif condition is not False:
        pl.when(condition)(run)


class Spread:
    def __init__(self, spot, source, slot, send, receive, local):
        self.spot = spot
        self.slot = slot
        self.source = source
        self.sends = send
        self.receives = receive
        self.mine = pltpu.make_async_copy(source, slot(*spot.block(spot.core, 0, 0, spot.z)), local)

    def copy(self, first, second, z, kind, own=False):
        spot = self.spot
        place = self.slot(*spot.block(spot.core, first, second, z))
        number = spot.number(first, second, z)
        arrival = {
            RIGHT: number,
            LEFT: number,
            FIRST: spot.number(1, 0, z),
            SECOND: spot.number(first, 1, z),
            CORE: spot.planes * spot.line + number,
        }[kind]
        departure = {RIGHT: 0, LEFT: 1, FIRST: 2, SECOND: 3, CORE: 5}[kind] * spot.line + number
        source = self.source if own else place
        return spot.send(source, place, self.sends.at[departure], self.receives.at[arrival], kind)

    def arrived(self, first, second, z, other=False):
        spot = self.spot
        core = 1 - spot.core if other else spot.core
        place = self.slot(*spot.block(core, first, second, z))
        number = spot.number(first, second, z) + (spot.planes * spot.line if other else 0)
        spot.send(place, place, self.sends.at[0], self.receives.at[number], CORE).wait_recv()

    def steps(self):
        return self.spot.line + (3 if self.spot.wide else 1)

    def begin(self):
        spot = self.spot
        z = spot.z
        when(z + 1 < spot.line, lambda: self.copy(0, 0, z, RIGHT, True).start())
        when(z > 0, lambda: self.copy(0, 0, z, LEFT, True).start())
        for kind in spot.kinds():
            self.copy(0, 0, z, kind, True).start()
        self.mine.start()

    def step(self, step):
        spot = self.spot
        line, z = spot.line, spot.z

        def reached(away, action):
            inside = jnp.logical_and(away >= 0, away < line)
            when(jnp.logical_and(inside, z - away >= 0), lambda: action(z - away, True))
            when(
                jnp.logical_and(inside, jnp.logical_and(away > 0, z + away < line)),
                lambda: action(z + away, False),
            )

        def along(zz, from_left):
            self.arrived(0, 0, zz)
            if from_left:
                when(z + 1 < line, lambda: self.copy(0, 0, zz, RIGHT).start())
            else:
                when(z > 0, lambda: self.copy(0, 0, zz, LEFT).start())
            for kind in spot.kinds():
                self.copy(0, 0, zz, kind).start()

        def firsts(zz, _):
            self.arrived(1, 0, zz)
            if spot.wide:
                self.copy(1, 0, zz, SECOND).start()
            self.copy(1, 0, zz, CORE).start()

        def lasts(first):
            def action(zz, _):
                self.arrived(first, 1, zz)
                self.copy(first, 1, zz, CORE).start()

            return action

        step = jnp.asarray(step, jnp.int32)
        reached(step, along)
        reached(step - 1, firsts)
        if spot.wide:
            reached(step - 2, lasts(0))
            reached(step - 3, lasts(1))

    def finish(self):
        spot = self.spot
        z = spot.z

        def body(zz, _):
            when(
                jnp.logical_and(z + 1 < spot.line, zz <= z),
                lambda: self.copy(0, 0, zz, RIGHT).wait_send(),
            )
            when(jnp.logical_and(z > 0, zz >= z), lambda: self.copy(0, 0, zz, LEFT).wait_send())
            self.copy(0, 0, zz, FIRST).wait_send()
            for second in range(2 if spot.wide else 1):
                for first in (0, 1):
                    if spot.wide and not second:
                        self.copy(first, 0, zz, SECOND).wait_send()
                    self.copy(first, second, zz, CORE).wait_send()
                    self.arrived(first, second, zz, other=True)
            return 0

        lax.fori_loop(0, spot.line, body, 0)
        self.mine.wait()


class LateSpread(Spread):
    def steps(self):
        return self.spot.line + 2

    def copy(self, first, second, z, kind, own=False):
        spot = self.spot
        place = self.slot(*spot.block(spot.core, first, second, z))
        number = spot.number(first, second, z)
        arrival = {
            RIGHT: number,
            LEFT: number,
            FIRST: spot.number(1, 0, z),
            SECOND: spot.number(first, 1, z),
            CORE: spot.planes * spot.line + number,
        }[kind]
        departure = {RIGHT: 0, LEFT: 4, CORE: 8, FIRST: 12, SECOND: 13}[kind] * spot.line + number
        source = self.source if own else place
        return spot.send(source, place, self.sends.at[departure], self.receives.at[arrival], kind)

    def along_both(self, first, second, own=False):
        spot = self.spot
        z = spot.z
        when(z + 1 < spot.line, lambda: self.copy(first, second, z, RIGHT, own).start())
        when(z > 0, lambda: self.copy(first, second, z, LEFT, own).start())
        self.copy(first, second, z, CORE, own).start()

    def begin(self):
        self.copy(0, 0, self.spot.z, FIRST, True).start()
        self.copy(0, 0, self.spot.z, SECOND, True).start()
        self.along_both(0, 0, True)
        self.mine.start()

    def step(self, step):
        spot = self.spot
        line, z = spot.line, spot.z
        step = jnp.asarray(step, jnp.int32)

        def passed(first, second, zz, kind, more):
            self.arrived(first, second, zz)
            when(more, lambda: self.copy(first, second, zz, kind).start())
            self.copy(first, second, zz, CORE).start()

        for first, second in ((0, 0), (1, 0), (0, 1), (1, 1)):
            away = step - (first + second)

            def here():
                self.arrived(first, second, z)
                if first and not second:
                    self.copy(1, 0, z, SECOND).start()
                self.along_both(first, second)

            if first or second:
                when(away == 0, here)
            far = jnp.logical_and(away > 0, away < line)
            when(
                jnp.logical_and(far, z - away >= 0),
                lambda: passed(first, second, z - away, RIGHT, z + 1 < line),
            )
            when(
                jnp.logical_and(far, z + away < line),
                lambda: passed(first, second, z + away, LEFT, z > 0),
            )

    def finish(self):
        spot = self.spot
        z = spot.z

        def body(zz, _):
            for second in (0, 1):
                for first in (0, 1):
                    when(
                        jnp.logical_and(z + 1 < spot.line, zz <= z),
                        lambda: self.copy(first, second, zz, RIGHT).wait_send(),
                    )
                    when(
                        jnp.logical_and(z > 0, zz >= z),
                        lambda: self.copy(first, second, zz, LEFT).wait_send(),
                    )
                    self.copy(first, second, zz, CORE).wait_send()
                    self.arrived(first, second, zz, other=True)
            return 0

        lax.fori_loop(0, spot.line, body, 0)
        self.copy(0, 0, z, FIRST).wait_send()
        for first in (0, 1):
            self.copy(first, 0, z, SECOND).wait_send()
        self.mine.wait()


def rows_spread(spot, source, place, rows, semaphores, at):
    late = late_rows(rows)
    early = rows - late
    send, receive, late_send, late_receive, local = semaphores

    def slot(start, size):
        return lambda block, side: place(block, side * rows + start, size)

    return [
        Spread(
            spot,
            source.at[pl.ds(0, early)],
            slot(0, early),
            send.at[at],
            receive.at[at],
            local.at[at, 0],
        ),
        LateSpread(
            spot,
            source.at[pl.ds(early, late)],
            slot(early, late),
            late_send.at[at],
            late_receive.at[at],
            local.at[at, 1],
        ),
    ]


def late_rows(rows):
    return max(16, round(rows * 2 / 9 / 16) * 16)


def rows_semaphores(batch, line):
    counts = (*spread_count(line, True), 15 * line, 8 * line, 2)
    return [pltpu.SemaphoreType.DMA((batch, count)) for count in counts]


def run_trees(trees):
    for tree in trees:
        tree.begin()

    def body(step, _):
        for tree in trees:
            tree.step(step)
        return 0

    lax.fori_loop(1, max(tree.steps() for tree in trees), body, 0)
    for tree in trees:
        tree.finish()


def spread_count(line, wide):
    return (9 if wide else 7) * line, (8 if wide else 4) * line


def rows_at(ref, index, size):
    return ref.at[pl.ds(pl.multiple_of(index * size, 16), size)]


def columns_at(ref, index, size):
    return ref.at[:, pl.ds(pl.multiple_of(index * size, LANES), size)]


def norm_rows(target, source, gain):
    def body(step, _):
        rows = pl.ds(pl.multiple_of(step * 16, 16), 16)
        value = source[rows, :].astype(jnp.float32)
        target[rows, :] = rms_scale(value, gain[...].astype(jnp.float32)).astype(target.dtype)
        return 0

    lax.fori_loop(0, target.shape[0] // 16, body, 0)


def turned_heads(value, gain, cosine, sine):
    normed = rms_scale(value, gain)
    return normed * cosine + pltpu.roll(normed, normed.shape[-1] // 2, 1) * sine


def visible_blocks(length, group):
    blocks = []
    for start in range(0, length, BLOCK):
        stop = min(start + BLOCK, length)
        heads = max(1, BLOCK // (stop - start))
        while group % heads:
            heads -= 1
        blocks.append((start, stop, stop, heads))
    return blocks


def softmax(scores):
    raised = jnp.exp(scores - jnp.max(scores, axis=0, keepdims=True))
    return raised * (1.0 / jnp.sum(raised, axis=0, keepdims=True))


def for_heads(low, high, heads, body):
    turns = 2 if heads == 1 and (high - low) % 2 == 0 else 1

    def turn(step, _):
        for i in range(turns):
            body(low + (step * turns + i) * heads)
        return 0

    count = (high - low) // (heads * turns)
    if count == 1:
        turn(0, 0)
    else:
        lax.fori_loop(0, count, turn, 0)


def head_columns(head, features):
    return pl.ds(pl.multiple_of(head * features, LANES), features)


def forward_kernel(
    line,
    heads,
    kv_heads,
    tokens_ref,
    cot_ref,
    in_ref,
    out_ref,
    picks_ref,
    gain1_ref,
    gain2_ref,
    query_gain_ref,
    key_gain_ref,
    cosine_ref,
    sine_ref,
    cot_all,
    in_all,
    out_all,
    picks_all,
    normed_all,
    projected_all,
    context_all,
    hidden_all,
    second_all,
    in_w,
    out_w,
    tokens,
    normed,
    projected,
    context,
    queries,
    keys,
    values,
    mixed,
    mixed_other,
    hidden,
    second,
    narrow_send,
    narrow_receive,
    cot_send,
    cot_receive,
    cot_late_send,
    cot_late_receive,
    cot_local,
    local,
    token_send,
    token_receive,
    mixed_send,
    mixed_receive,
    save_sem,
):
    cot_semaphores = (cot_send, cot_receive, cot_late_send, cot_late_receive, cot_local)
    batch, half, width = tokens_ref.shape
    length = 2 * half
    depth, out_width = in_ref.shape[0], out_ref.shape[1]
    features = query_gain_ref.shape[1]
    narrow = Spot(line, False)
    spot = Spot(line, True, turned=False)
    x = spot.x
    spot.greet()
    slots = [
        (picks_ref, lambda block, side: picks_all.at[block]),
        (in_ref, lambda block, side: rows_at(in_w, block, depth)),
        (out_ref, lambda block, side: columns_at(out_w, block, out_width)),
    ]
    weights = [
        Spread(narrow, source, slot, narrow_send.at[i], narrow_receive.at[i], local.at[i])
        for i, (source, slot) in enumerate(slots)
    ]
    cots = []
    for i in range(batch):
        place = lambda block, start, size, i=i: cot_all.at[
            i, block, pl.ds(pl.multiple_of(start, 16), size)
        ]
        cots += rows_spread(spot, cot_ref.at[i], place, half, cot_semaphores, i)
    early, late = weights[:2], weights[2]
    for tree in early:
        tree.begin()

    def token_copies(i):
        place = rows_at(tokens.at[i], x, half)
        return (
            pltpu.make_async_copy(tokens_ref.at[i], place, local.at[3 + i]),
            spot.send(tokens_ref.at[i], place, token_send.at[i], token_receive.at[i], CROSS),
        )

    for i in range(batch):
        for copy in token_copies(i):
            copy.start()
    for tree in cots:
        tree.begin()

    def steps(step, _):
        for tree in early:
            tree.step(step)
        return 0

    lax.fori_loop(1, late.steps(), steps, 0)
    late.begin()
    for i in range(batch):
        mine, other = token_copies(i)
        mine.wait()
        other.wait_send()
        place = rows_at(tokens.at[i], 1 - x, half)
        spot.send(place, place, token_send.at[i], token_receive.at[i], CROSS).wait_recv()
    for i in range(batch):
        norm_rows(normed.at[i], tokens.at[i], gain1_ref)
    for tree in early:
        tree.finish()

    def save(source, target, index):
        return pltpu.make_async_copy(source, target, save_sem.at[index])

    saves = [save(in_w, in_all, 0), save(out_w, out_all, 1)]
    saves[0].start()

    def project(i, start, stop):
        for at in range(start, stop, CHUNK):
            projected[i, :, at : at + CHUNK] = jnp.dot(
                normed[i], in_w[:, at : at + CHUNK], preferred_element_type=jnp.float32
            )

    scale = features ** (-0.5)

    group = heads // kv_heads

    def prepare_keys(i):
        base = heads * features
        for head in range(kv_heads):
            at = base + head * features
            keys[head] = turned_heads(
                projected[i, :, at : at + features],
                key_gain_ref[...].astype(jnp.float32),
                cosine_ref[...],
                sine_ref[...],
            ).astype(jnp.bfloat16)
            at = base + (kv_heads + head) * features
            values[head] = projected[i, :, at : at + features].astype(jnp.bfloat16)

    def prepare_queries(i, shared):
        def prepare(member):
            columns = head_columns(shared * group + member, features)
            queries[member] = turned_heads(
                projected[i, :, columns], query_gain_ref[...].astype(jnp.float32), cosine_ref[...], sine_ref[...]
            ).astype(jnp.bfloat16)

        for_heads(0, group, 1, prepare)

    def attend(i, shared, start, stop, seen, at_once, low, high):
        count = stop - start

        def block(member):
            query = queries[pl.ds(member, at_once), start:stop, :].reshape(-1, features)
            scores = lax.dot_general(
                keys[shared, :seen, :],
                query,
                TRANSPOSED_RIGHT,
                preferred_element_type=jnp.float32,
            )
            rows = lax.dot_general(
                softmax(scores * scale).astype(jnp.bfloat16),
                values[shared, :seen, :],
                TRANSPOSED_LEFT,
                preferred_element_type=jnp.float32,
            ).astype(jnp.bfloat16)
            for j in range(at_once):
                columns = head_columns(shared * group + member + j, features)
                context[i, start:stop, columns] = rows[j * count : (j + 1) * count]

        for_heads(low, high, at_once, block)

    def mixed_copy(i):
        return spot.send(
            rows_at(mixed.at[i], 1 - x, half),
            mixed_other.at[i],
            mixed_send.at[i],
            mixed_receive.at[i],
            CROSS,
        )

    def mix(i, start, stop):
        for at in range(start, stop, CHUNK):
            mixed[i, :, at : at + CHUNK] = jnp.dot(
                context[i], out_w[:, at : at + CHUNK], preferred_element_type=jnp.float32
            ).astype(jnp.bfloat16)
        if stop == width:
            mixed_copy(i).start()

    def close(i):
        mixed_copy(i).wait()
        add_rows(
            hidden.at[i],
            [rows_at(tokens.at[i], x, half), rows_at(mixed.at[i], x, half), mixed_other.at[i]],
        )
        norm_rows(second.at[i], hidden.at[i], gain2_ref)

    later = [
        functools.partial(tree.step, step)
        for step in range(1, cots[0].steps())
        for tree in [late] + cots
        if step < tree.steps()
    ]
    final = late.steps() - 1

    def late_done():
        while later and len(later) > len(later_rest):
            later.pop(0)()
        late.finish()
        saves[1].start()

    later_rest = later[(final - 1) * (1 + len(cots)) + 1 :]
    pending = []
    in_width = in_w.shape[1]
    parts = lambda size: [(at, min(at + 2 * CHUNK, size)) for at in range(0, size, 2 * CHUNK)]
    for i in range(batch):
        pending += [functools.partial(project, i, *part) for part in parts(in_width)]
        pending.append(functools.partial(prepare_keys, i))
        for shared in range(kv_heads):
            pending.append(functools.partial(prepare_queries, i, shared))
            for start, stop, seen, at_once in visible_blocks(length, group):
                share = max(at_once, group // 2)
                for low in range(0, group, share):
                    pending.append(
                        functools.partial(
                            attend, i, shared, start, stop, seen, at_once, low, low + share
                        )
                    )
        if i == 0:
            pending.append(late_done)
        pending += [functools.partial(mix, i, *part) for part in parts(width)]
    pending += [functools.partial(close, i) for i in range(batch)]
    while pending or later:
        for _ in range(-(-len(pending) // max(1, len(later)))):
            pending.pop(0)()
        if later:
            later.pop(0)()

    saves += [
        save(source, target, 2 + i)
        for i, (source, target) in enumerate(
            [
                (normed, normed_all),
                (projected, projected_all),
                (context, context_all),
                (hidden, hidden_all),
                (second, second_all),
            ]
        )
    ]
    for copy in saves[2:]:
        copy.start()
    for tree in cots:
        tree.finish()
    for copy in saves:
        copy.wait()


def run_forward(tokens, cot, weight_in, weight_out, picks, gains, tables, fsdp_count, kv_heads):
    line = fsdp_count // PLANE
    batch, half, width = tokens.shape
    length = 2 * half
    features = gains[2].shape[1]
    heads = weight_out.shape[0] // features
    in_shape = (weight_in.shape[0] * fsdp_count, weight_in.shape[1])
    out_shape = (weight_out.shape[0], weight_out.shape[1] * fsdp_count)
    narrow = spread_count(line, False)
    anywhere = pl.BlockSpec(memory_space=pl.ANY)
    inside = pl.BlockSpec(memory_space=pltpu.VMEM)
    shape = lambda dims, kind=jnp.bfloat16: jax.ShapeDtypeStruct(dims, kind)
    vmem = lambda *dims: pltpu.VMEM(dims, jnp.bfloat16)
    sem = lambda *dims: pltpu.SemaphoreType.DMA(dims)
    kept = (
        ((batch, length, width), jnp.bfloat16),
        ((batch, length, weight_in.shape[1]), jnp.float32),
        ((batch, length, heads * features), jnp.bfloat16),
        ((batch, half, width), jnp.float32),
        ((batch, half, width), jnp.bfloat16),
    )
    return pl.pallas_call(
        functools.partial(forward_kernel, line, heads, kv_heads),
        out_shape=(
            shape((batch, fsdp_count, length, width)),
            shape(in_shape),
            shape(out_shape),
            shape((fsdp_count, *picks.shape), picks.dtype),
            *(shape(*one) for one in kept),
        ),
        in_specs=[anywhere] * 5 + [inside] * 6,
        out_specs=(anywhere,) * 9,
        scratch_shapes=[
            vmem(*in_shape),
            vmem(*out_shape),
            vmem(batch, length, width),
            *(pltpu.VMEM(*one) for one in kept[:3]),
            vmem(heads // kv_heads, length, features),
            vmem(kv_heads, length, features),
            vmem(kv_heads, length, features),
            vmem(batch, length, width),
            vmem(batch, half, width),
            *(pltpu.VMEM(*one) for one in kept[3:]),
            sem(3, narrow[0]),
            sem(3, narrow[1]),
            *rows_semaphores(batch, line),
            sem(3 + batch),
            sem(batch),
            sem(batch),
            sem(batch),
            sem(batch),
            sem(7),
        ],
        compiler_params=pltpu.CompilerParams(
            collective_id=1, has_side_effects=True, vmem_limit_bytes=60 * MIB
        ),
    )(tokens, cot, weight_in, weight_out, picks, *gains, *tables)


def add_rows(target, sources):
    def body(step, _):
        rows = pl.ds(pl.multiple_of(step * 16, 16), 16)
        total = sources[0][rows, :].astype(jnp.float32)
        for source in sources[1:]:
            total = total + source[rows, :].astype(jnp.float32)
        target[rows, :] = total.astype(target.dtype)
        return 0

    lax.fori_loop(0, target.shape[0] // 16, body, 0)


class Collect:
    def __init__(self, spot, part, total, cores, firsts, rights, lefts, send, receive):
        self.spot = spot
        self.part = part
        self.total = total
        self.places = {CORE: cores, FIRST: firsts, RIGHT: rights, LEFT: lefts}
        line = spot.line
        self.base = {CORE: 0, FIRST: 2 * line, RIGHT: 3 * line, LEFT: 4 * line}
        self.sends = send
        self.receives = receive

    def own(self, first, z):
        return self.part(*self.spot.block(self.spot.core, first, 0, z))

    def copy(self, kind, first, z):
        spot = self.spot
        number = first * spot.line + z if kind == CORE else z
        source = self.part(*spot.block(1 - spot.core, first, 0, z)) if kind == CORE else self.own(first, z)
        at = self.base[kind] + number
        return spot.send(
            source, self.places[kind].at[number], self.sends.at[at], self.receives.at[at], kind
        )

    def arrived(self, kind, number):
        place = self.places[kind].at[number]
        at = self.base[kind] + number
        self.spot.send(place, place, self.sends.at[0], self.receives.at[at], CORE).wait_recv()
        return place

    def begin(self, z):
        for first in (1, 0):
            self.copy(CORE, first, z).start()

    def to_first(self, z):
        add_rows(self.own(1, z), [self.own(1, z), self.arrived(CORE, self.spot.line + z)])
        self.copy(FIRST, 1, z).start()

    def summands(self, z):
        return [self.own(0, z), self.arrived(CORE, z), self.arrived(FIRST, z)]

    def cross(self):
        for step in reversed(range(self.spot.line)):
            for zz, valid in self.spot.order(step):
                when(valid, functools.partial(self.to_first, zz))

    def onward(self, kind, zz):
        spot = self.spot
        sources = self.summands(zz)
        target = self.own(0, zz)
        behind = spot.z > 0 if kind == RIGHT else spot.z + 1 < spot.line
        when(behind, lambda: add_rows(target, sources + [self.arrived(kind, zz)]))
        when(jnp.logical_not(behind), lambda: add_rows(target, sources))
        self.copy(kind, 0, zz).start()

    def last(self):
        z, line = self.spot.z, self.spot.line
        sources = self.summands(z)

        def end(kinds):
            add_rows(self.total, sources + [self.arrived(kind, z) for kind in kinds])

        when(z == 0, lambda: end([LEFT]))
        when(z == line - 1, lambda: end([RIGHT]))
        when(jnp.logical_and(z > 0, z < line - 1), lambda: end([RIGHT, LEFT]))

    def finish(self):
        spot = self.spot
        for zz in range(spot.line):
            for first in (0, 1):
                self.copy(CORE, first, zz).wait_send()
            self.copy(FIRST, 1, zz).wait_send()
            when(zz > spot.z, lambda: self.copy(RIGHT, 0, zz).wait_send())
            when(zz < spot.z, lambda: self.copy(LEFT, 0, zz).wait_send())

    def tasks(self):
        spot = self.spot
        work = []
        for step in reversed(range(1, spot.line)):
            for kind, (zz, valid) in zip((LEFT, RIGHT), spot.order(step)):
                action = functools.partial(self.onward, kind, zz)
                work.append(functools.partial(when, valid, action))
        return work + [self.last, self.finish]


def collect_scratch(line, shape):
    counts = (2 * line, line, line, line)
    return [pltpu.VMEM((count, *shape), jnp.bfloat16) for count in counts] + [
        pltpu.SemaphoreType.DMA((5 * line,)),
        pltpu.SemaphoreType.DMA((5 * line,)),
    ]


BOXES = 6


def plane_in_turn(line, group):
    turn = lax.rem(group, line)
    step = lax.div(turn, 2)
    return jnp.where(lax.rem(turn, 2) == 0, step, line - 1 - step)


class Sums:
    def __init__(self, spot, parts, cores, places, inbox, outbox, semaphores, plane, inside, ready, done, turns):
        self.spot = spot
        self.parts = parts
        self.cores = cores
        self.seconds, self.firsts, self.ends = places
        self.inbox = inbox
        self.outbox = outbox
        (
            self.inbox_sem,
            self.outbox_sem,
            self.second_receive,
            self.first_receive,
            self.end_receive,
        ) = semaphores
        self.plane = plane
        self.inside = inside
        self.ready = ready
        self.done = done
        self.turns = turns

    def second_slot(self, turn, first):
        return turn * 2 + first

    def first_slot(self, turn):
        return 2 * self.turns + turn

    def end_slot(self, turn, kind):
        return 3 * self.turns + turn * 2 + kind

    def free(self, unit, turn, first):
        pass

    def second_send(self, unit, turn, first):
        slot = self.second_slot(turn, first)
        return self.spot.send(
            self.outbox.at[slot],
            self.seconds.at[unit, first],
            self.outbox_sem.at[slot],
            self.second_receive.at[unit, first],
            SECOND,
        )

    def first_send(self, unit, turn):
        slot = self.first_slot(turn)
        return self.spot.send(
            self.outbox.at[slot],
            self.firsts.at[unit],
            self.outbox_sem.at[slot],
            self.first_receive.at[unit],
            FIRST,
        )

    def end_send(self, unit, turn, kind):
        slot = self.end_slot(turn, kind)
        return self.spot.send(
            self.outbox.at[slot],
            self.ends.at[unit, kind],
            self.outbox_sem.at[slot],
            self.end_receive.at[unit, kind],
            kind,
        )

    def received(self, place, semaphore):
        self.spot.send(place, place, self.outbox_sem.at[0], semaphore, CORE).wait_recv()

    def sources(self, unit, first, second):
        y, x = self.spot.side(self.spot.core, first, second)
        half = self.inbox.shape[1]
        return [rows_at(self.parts(unit, y), x, half), rows_at(self.cores(unit, y), x, half)]

    def summands(self, unit):
        return self.sources(unit, 0, 0) + [self.seconds.at[unit, 0], self.firsts.at[unit]]

    def load(self, source, slot):
        return pltpu.make_async_copy(source, self.inbox.at[slot], self.inbox_sem.at[slot])

    def add(self, target, base, numbers):
        add_rows(target, [self.inbox.at[base + i] for i in numbers])

    def end_roles(self, half_step, delay):
        z, line = self.spot.z, self.spot.line
        unit = half_step - 3 - delay
        valid = self.inside(unit)
        plane = self.plane(unit)
        right = jnp.logical_and(valid, jnp.logical_and(z < plane, delay == z))
        left = jnp.logical_and(valid, jnp.logical_and(z > plane, delay == line - 1 - z))
        last = jnp.logical_and(
            valid,
            jnp.logical_and(z == plane, delay == jnp.maximum(plane, line - 1 - plane)),
        )
        return unit, right, left, last

    def end_task(self, half_step, delay, parity):
        z, line = self.spot.z, self.spot.line
        turn = (parity - 3 - delay) % self.turns
        unit, right, left, last = self.end_roles(half_step, delay)
        some = jnp.logical_or(right, jnp.logical_or(left, last))
        from_left = jnp.logical_and(jnp.logical_or(right, last), z > 0)
        from_right = jnp.logical_and(jnp.logical_or(left, last), z + 1 < line)
        present = ((RIGHT, from_left), (LEFT, from_right))

        def fetch(base):
            def action():
                self.received(self.seconds.at[unit, 0], self.second_receive.at[unit, 0])
                self.received(self.firsts.at[unit], self.first_receive.at[unit])
                for i, source in enumerate(self.summands(unit)):
                    self.load(source, base + i).start()
                for kind, there in present:

                    def arrive():
                        self.received(self.ends.at[unit, kind], self.end_receive.at[unit, kind])
                        self.load(self.ends.at[unit, kind], base + 4 + kind).start()

                    when(there, arrive)

            when(some, action)

        def add(base):
            def action():
                for i, source in enumerate(self.summands(unit)):
                    self.load(source, base + i).wait()
                for kind, there in present:
                    when(there, lambda: self.load(self.ends.at[unit, kind], base + 4 + kind).wait())
                numbers = list(range(4))
                for kind, chosen, behind in ((RIGHT, right, z > 0), (LEFT, left, z + 1 < line)):

                    def onward():
                        target = self.outbox.at[self.end_slot(turn, kind)]
                        self.free(unit, turn, 0)
                        when(behind, lambda: self.add(target, base, numbers + [4 + kind]))
                        when(jnp.logical_not(behind), lambda: self.add(target, base, numbers))
                        self.end_send(unit, turn, kind).start()

                    when(chosen, onward)

                def finish():
                    def into(target):
                        both = jnp.logical_and(from_left, from_right)
                        when(both, lambda: self.add(target, base, numbers + [4, 5]))
                        for kind, there in present:
                            when(
                                jnp.logical_and(there, jnp.logical_not(both)),
                                lambda: self.add(target, base, numbers + [4 + kind]),
                            )

                    self.done(unit, turn, into)

                when(last, finish)

            when(some, action)

        return fetch, add

    def retire(self, half_step, parity):
        before = half_step - self.turns
        now, then = (parity - 1) % self.turns, (parity - 2) % self.turns
        when(
            self.inside(before - 1),
            lambda: [self.second_send(before - 1, now, first).wait_send() for first in range(2)],
        )
        when(self.inside(before - 2), lambda: self.first_send(before - 2, then).wait_send())
        for delay in range(self.spot.line):
            if self.inside(before - 3 - delay) is False:
                continue
            unit, right, left, _ = self.end_roles(before, delay)
            turn = (parity - 3 - delay) % self.turns
            when(right, lambda: self.end_send(unit, turn, RIGHT).wait_send())
            when(left, lambda: self.end_send(unit, turn, LEFT).wait_send())

    def simple_task(self, valid, ready, inputs, slot, send, free=lambda: None):
        def fetch(base):
            ready()

            def action():
                for i, source in enumerate(inputs()):
                    self.load(source, base + i).start()

            when(valid, action)

        def add(base):
            def action():
                refs = inputs()
                for i, source in enumerate(refs):
                    self.load(source, base + i).wait()
                free()
                self.add(self.outbox.at[slot], base, range(len(refs)))
                send().start()

            when(valid, action)

        return fetch, add

    def tasks(self, half_step, parity):
        one, two = half_step - 1, half_step - 2
        now, then = (parity - 1) % self.turns, (parity - 2) % self.turns
        tasks = [
            self.second_task(one, now, 1, functools.partial(self.ready, one)),
            self.second_task(one, now, 0, lambda: None),
            self.first_task(two, then),
        ]
        for delay in range(self.spot.line):
            if self.inside(half_step - 3 - delay) is not False:
                tasks.append(self.end_task(half_step, delay, parity))
        return tasks

    def second_task(self, unit, turn, first, ready):
        return self.simple_task(
            self.inside(unit),
            ready,
            lambda: self.sources(unit, first, 1),
            self.second_slot(turn, first),
            lambda: self.second_send(unit, turn, first),
        )

    def first_task(self, unit, turn):
        arrive = lambda: self.received(self.seconds.at[unit, 1], self.second_receive.at[unit, 1])

        def send():
            return self.first_send(unit, turn)

        return self.simple_task(
            self.inside(unit),
            lambda: when(self.inside(unit), arrive),
            lambda: self.sources(unit, 1, 0) + [self.seconds.at[unit, 1]],
            self.first_slot(turn),
            send,
            lambda: self.free(unit, turn, 1),
        )

    def weave(self, tasks, pieces):
        buffers = self.inbox.shape[0] // BOXES
        if buffers > 1:
            tasks[0][0](0)
        for index, (fetch, add) in enumerate(tasks):
            if buffers == 1:
                fetch(0)
            elif index + 1 < len(tasks):
                tasks[index + 1][0]((index + 1) % 2 * BOXES)
            share = -(-len(pieces) // (len(tasks) - index))
            for piece in pieces[:share]:
                piece()
            pieces = pieces[share:]
            add(index % buffers * BOXES)

    def half_steps(self, units):
        return units + self.spot.line + 2


class ReadySums(Sums):
    def first_slot(self, turn):
        return turn * 2 + 1

    def end_slot(self, turn, kind):
        return turn * 2

    def free(self, unit, turn, first):
        self.second_send(unit, turn, first).wait_send()

    def all_tasks(self, units):
        tasks = [
            self.second_task(unit, unit, first, lambda: None)
            for first in (1, 0)
            for unit in range(units)
        ]
        tasks += [self.first_task(unit, unit) for unit in range(units)]
        for delay in range(self.spot.line):
            for unit in range(units):
                half_step = unit + 3 + delay
                tasks.append(self.end_task(half_step, delay, half_step))
        return tasks

    def finish(self, units):
        for unit in range(units):
            self.first_send(unit, unit).wait_send()
            plane, z = self.plane(unit), self.spot.z
            when(plane > z, lambda: self.end_send(unit, unit, RIGHT).wait_send())
            when(plane < z, lambda: self.end_send(unit, unit, LEFT).wait_send())
            when(plane == z, lambda: self.free(unit, unit, 0))


def norm_back(value, grads, gain):
    scale = lax.rsqrt(jnp.mean(value * value, axis=-1, keepdims=True) + EPSILON)
    unit = value * scale
    scaled = grads * gain
    back = scale * (scaled - unit * jnp.mean(scaled * unit, axis=-1, keepdims=True))
    return back, grads * unit


def backward_kernel(
    line,
    heads,
    kv_heads,
    cot_ref,
    totals_ref,
    hidden_ref,
    projected_ref,
    context_ref,
    in_ref,
    out_ref,
    tokens_ref,
    part_ref,
    cores_ref,
    gain1_ref,
    gain2_ref,
    query_gain_ref,
    key_gain_ref,
    cosine_ref,
    sine_ref,
    block_out,
    input_grad,
    grads_all,
    out_total,
    gain_grads,
    seconds,
    middle,
    ends,
    elements,
    cots,
    tokens,
    kept,
    result,
    context,
    hidden_grads,
    context_grads,
    grads,
    normed_other,
    weight_rows,
    queries_f,
    shared_f,
    queries,
    query_grads,
    sums,
    out_grads,
    cores,
    firsts,
    rights,
    lefts,
    tree_send,
    tree_receive,
    load_sem,
    row_sem,
    head_sem,
    save_sem,
    hidden_send,
    hidden_receive,
    normed_send,
    normed_receive,
    inbox,
    outbox,
    summed,
    inbox_sem,
    outbox_sem,
    second_receive,
    first_receive,
    end_receive,
):
    batch, half, width = cot_ref.shape
    length = 2 * half
    features = query_gain_ref.shape[1]
    group = heads // kv_heads
    base = heads * features
    out_width = out_total.shape[1]
    narrow, spot = Spot(line, False), Spot(line, True)
    x = spot.x
    scale = features ** (-0.5)
    normed_grads = context_grads

    def load(source, target, index):
        return pltpu.make_async_copy(source, target, load_sem.at[index])

    def element_loads(i):
        copies = [
            load(hidden_ref.at[i], elements.at[0], 0),
            load(totals_ref.at[i, BACK], elements.at[1], 1),
        ]
        if i:
            copies.append(load(totals_ref.at[i, OUTPUT], elements.at[2], 2))
        return copies

    first_loads = [load(cot_ref, cots, 3), load(tokens_ref, tokens, 4)] + [
        load(context_ref.at[i], rows_at(context, i, length), 5 + i) for i in range(batch)
    ]
    for copy in element_loads(0) + first_loads:
        copy.start()

    def weight_load(ref, step):
        slot = step % 2
        return pltpu.make_async_copy(
            rows_at(ref, step, CHUNK),
            weight_rows.at[slot, :, pl.ds(0, ref.shape[1])],
            row_sem.at[slot],
        )

    out_steps, in_steps = out_ref.shape[0] // CHUNK, in_ref.shape[0] // CHUNK
    for step in range(2):
        weight_load(out_ref, step).start()
    gain_grads[...] = jnp.zeros_like(gain_grads)
    spot.greet()
    for copy in first_loads:
        copy.wait()

    def result_save(i, target):
        return pltpu.make_async_copy(result.at[i], target.at[i], save_sem.at[i])

    def half_copy(ref, i, side):
        return ref.at[pl.ds(pl.multiple_of(i * length + side * half, 16), half), pl.ds(0, width)]

    def hidden_copy(i):
        place = half_copy(hidden_grads, i, x)
        return spot.send(place, place, hidden_send.at[i], hidden_receive.at[i], CROSS)

    def element_rows(i):
        for copy in element_loads(i):
            copy.wait()

        def elementwise(step, _):
            rows = pl.ds(pl.multiple_of(step * 16, 16), 16)
            value = elements[0, rows, :]
            if i:
                result[i, rows, :] = (value + elements[2, rows, :]).astype(jnp.bfloat16)
            back, gain_rows = norm_back(
                value, elements[1, rows, :], gain2_ref[...].astype(jnp.float32)
            )
            gain_grads[1:2, :] += jnp.sum(gain_rows, axis=0, keepdims=True)
            total = cots[i, rows, :].astype(jnp.float32) + back
            kept[i, rows, :] = total
            place = pl.ds(pl.multiple_of(i * length + x * half + step * 16, 16), 16)
            hidden_grads[place, :] = total.astype(jnp.bfloat16)
            return 0

        lax.fori_loop(0, half // 16, elementwise, 0)
        hidden_copy(i).start()
        if i:
            result_save(i, block_out).start()
        if i + 1 < batch:
            for copy in element_loads(i + 1):
                copy.start()

    def hidden_done():
        load(hidden_ref.at[0], elements.at[0], 0).start()
        for i in range(batch):
            hidden_copy(i).wait_send()
            place = half_copy(hidden_grads, i, 1 - x)
            spot.send(place, place, hidden_send.at[i], hidden_receive.at[i], CROSS).wait_recv()

    def context_step(step):
        weight_load(out_ref, step).wait()
        columns = slice(step * CHUNK, (step + 1) * CHUNK)
        context_grads[:, columns] = lax.dot_general(
            hidden_grads[...],
            weight_rows[step % 2, :, :width],
            TRANSPOSED_RIGHT,
            preferred_element_type=jnp.float32,
        ).astype(jnp.bfloat16)
        if step + 2 < out_steps:
            weight_load(out_ref, step + 2).start()

    def out_step(step):
        columns = slice(step * CHUNK, (step + 1) * CHUNK)
        for start in range(0, width, CHUNK):
            out_grads[columns, start : start + CHUNK] = lax.dot_general(
                context[:, columns],
                hidden_grads[:, start : start + CHUNK],
                TRANSPOSED_LEFT,
                preferred_element_type=jnp.float32,
            ).astype(jnp.bfloat16)

    tree = Collect(
        narrow,
        lambda block, side: columns_at(out_grads, block, out_width),
        out_total,
        cores,
        firsts,
        rights,
        lefts,
        tree_send,
        tree_receive,
    )

    def in_start():
        for step in range(2):
            weight_load(in_ref, step).start()

    def tree_start():
        for z in range(line):
            tree.begin(z)
        for copy in head_loads(0):
            copy.start()

    def turns():
        return [(i, shared) for i in range(batch) for shared in range(kv_heads)]

    def head_loads(index):
        i, shared = turns()[index]
        slot = index % 2
        return [
            pltpu.make_async_copy(
                projected_ref.at[i, :, pl.ds(shared * group * features, group * features)],
                queries_f.at[slot],
                head_sem.at[slot, 0],
            )
        ] + [
            pltpu.make_async_copy(
                projected_ref.at[i, :, pl.ds(base + (shared + j * kv_heads) * features, features)],
                shared_f.at[slot, j],
                head_sem.at[slot, 1 + j],
            )
            for j in range(2)
        ]

    def turn_back(grads_in):
        return grads_in * cosine_ref[...] + pltpu.roll(
            grads_in * sine_ref[...], features // 2, 1
        )

    query_gain = lambda: query_gain_ref[...].astype(jnp.float32)
    key_gain = lambda: key_gain_ref[...].astype(jnp.float32)

    def attend_pieces(index):
        i, shared = turns()[index]
        slot = index % 2
        top = i * length

        def columns_of(member):
            return pl.ds(pl.multiple_of(member * features, LANES), features)

        def prepare():
            for copy in head_loads(index):
                copy.wait()
            if index + 1 < len(turns()):
                for copy in head_loads(index + 1):
                    copy.start()
            queries[group] = turned_heads(
                shared_f[slot, 0], key_gain(), cosine_ref[...], sine_ref[...]
            ).astype(jnp.bfloat16)
            queries[group + 1] = shared_f[slot, 1].astype(jnp.bfloat16)
            sums[...] = jnp.zeros_like(sums)

            def one(member):
                queries[member] = turned_heads(
                    queries_f[slot, :, columns_of(member)],
                    query_gain(),
                    cosine_ref[...],
                    sine_ref[...],
                ).astype(jnp.bfloat16)

            for_heads(0, group, 1, one)

        def rows_block(start, stop, seen, at_once, low, high):
            count = stop - start

            def block(member):
                query = queries[pl.ds(member, at_once), start:stop, :].reshape(-1, features)
                keys, values = queries[group, :seen, :], queries[group + 1, :seen, :]
                out_grad = jnp.concatenate(
                    [
                        context_grads[
                            top + start : top + stop,
                            head_columns(shared * group + member + j, features),
                        ]
                        for j in range(at_once)
                    ],
                    axis=0,
                )
                scores = lax.dot_general(
                    keys, query, TRANSPOSED_RIGHT, preferred_element_type=jnp.float32
                )
                shares = softmax(scores * scale)
                share_grads = lax.dot_general(
                    values, out_grad, TRANSPOSED_RIGHT, preferred_element_type=jnp.float32
                )
                sums[1, :seen, :] += jnp.dot(
                    shares.astype(jnp.bfloat16), out_grad, preferred_element_type=jnp.float32
                )
                inner = jnp.sum(shares * share_grads, axis=0, keepdims=True)
                score_grads = (shares * (share_grads - inner)).astype(jnp.bfloat16)
                rows = scale * lax.dot_general(
                    score_grads, keys, TRANSPOSED_LEFT, preferred_element_type=jnp.float32
                )
                query_grads[pl.ds(member, at_once), start:stop, :] = rows.reshape(
                    at_once, count, features
                )
                sums[0, :seen, :] += jnp.dot(
                    score_grads, query, preferred_element_type=jnp.float32
                )

            for_heads(low, high, at_once, block)

        def finish_queries():
            def finish(member):
                back, gain_rows = norm_back(
                    queries_f[slot, :, columns_of(member)],
                    turn_back(query_grads[member]),
                    query_gain(),
                )
                gain_grads[2:3, :features] += jnp.sum(gain_rows, axis=0, keepdims=True)
                grads[top : top + length, head_columns(shared * group + member, features)] = (
                    back.astype(jnp.bfloat16)
                )

            for_heads(0, group, 1, finish)

        def finish_keys():
            back, gain_rows = norm_back(shared_f[slot, 0], turn_back(sums[0] * scale), key_gain())
            gain_grads[3:4, :features] += jnp.sum(gain_rows, axis=0, keepdims=True)
            at = base + shared * features
            grads[top : top + length, at : at + features] = back.astype(jnp.bfloat16)
            at += kv_heads * features
            grads[top : top + length, at : at + features] = sums[1].astype(jnp.bfloat16)

        pieces = [prepare]
        for start, stop, seen, at_once in visible_blocks(length, group):
            share = max(at_once, group // 2)
            for low in range(0, group, share):
                pieces.append(
                    functools.partial(rows_block, start, stop, seen, at_once, low, low + share)
                )
        return pieces + [finish_queries, finish_keys]

    saves = [
        pltpu.make_async_copy(rows_at(grads, i, length), grads_all.at[i], save_sem.at[batch + i])
        for i in range(batch)
    ]

    def normed_step(step):
        weight_load(in_ref, step).wait()
        normed_grads[:, step * CHUNK : (step + 1) * CHUNK] = lax.dot_general(
            grads[...],
            weight_rows[step % 2],
            TRANSPOSED_RIGHT,
            preferred_element_type=jnp.float32,
        ).astype(jnp.bfloat16)
        if step + 2 < in_steps:
            weight_load(in_ref, step + 2).start()

    def normed_copy(i):
        return spot.send(
            half_copy(normed_grads, i, 1 - x),
            normed_other.at[i],
            normed_send.at[i],
            normed_receive.at[i],
            CROSS,
        )

    def input_rows(i):
        normed_copy(i).wait()
        if i:
            result_save(i, block_out).wait()

        def body(step, _):
            rows = pl.ds(pl.multiple_of(step * 16, 16), 16)
            place = pl.ds(pl.multiple_of(i * length + x * half + step * 16, 16), 16)
            total = normed_grads[place, :width].astype(jnp.float32) + normed_other[
                i, rows, :
            ].astype(jnp.float32)
            back, gain_rows = norm_back(
                tokens[i, rows, :].astype(jnp.float32), total, gain1_ref[...].astype(jnp.float32)
            )
            gain_grads[0:1, :] += jnp.sum(gain_rows, axis=0, keepdims=True)
            kept[i, rows, :] = kept[i, rows, :] + back
            return 0

        lax.fori_loop(0, half // 16, body, 0)
        add_rows(result.at[i], [kept.at[i]])
        result_save(i, input_grad).start()

    moved = ReadySums(
        spot,
        lambda unit, y: part_ref.at[2 * unit + OUTPUT, y],
        lambda unit, y: cores_ref.at[2 * unit + OUTPUT, y],
        (seconds, middle, ends),
        inbox,
        outbox,
        (inbox_sem, outbox_sem, second_receive, first_receive, end_receive),
        lambda unit: plane_in_turn(line, unit),
        lambda unit: 0 <= unit < line,
        lambda unit: None,
        lambda unit, turn, into: into(summed),
        line,
    )
    pieces = [functools.partial(element_rows, i) for i in range(batch)] + [hidden_done]
    pieces += [functools.partial(out_step, step) for step in range(out_steps)]
    pieces += [tree_start, functools.partial(context_step, 0), tree.cross]
    pieces += [functools.partial(context_step, step) for step in range(1, out_steps)]
    pieces.append(in_start)
    attending = [piece for index in range(len(turns())) for piece in attend_pieces(index)]
    work = tree.tasks()
    share = -(-len(attending) // len(work))
    while attending or work:
        pieces += attending[:share]
        attending = attending[share:]
        pieces += work[:1]
        work = work[1:]
    pieces += [copy.start for copy in saves]
    pieces += [functools.partial(normed_step, step) for step in range(in_steps)]
    pieces += [normed_copy(i).start for i in range(batch)]
    pieces += [functools.partial(input_rows, i) for i in range(batch)]

    moved.weave(moved.all_tasks(line), pieces)
    moved.finish(line)
    load(hidden_ref.at[0], elements.at[0], 0).wait()
    result_save(0, input_grad).wait()
    add_rows(result.at[0], [elements.at[0], summed])
    result_save(0, block_out).start()
    result_save(0, block_out).wait()
    for i in range(1, batch):
        result_save(i, input_grad).wait()
    for copy in saves:
        copy.wait()


def run_backward(
    cot,
    totals,
    hidden,
    projected,
    context,
    in_full,
    out_full,
    tokens,
    part,
    cores,
    gains,
    tables,
    fsdp_count,
    kv_heads,
):
    line = fsdp_count // PLANE
    batch, half, width = tokens.shape
    length = 2 * half
    features = gains[2].shape[1]
    heads = out_full.shape[0] // features
    group = heads // kv_heads
    in_width, out_depth = in_full.shape[1], out_full.shape[0]
    out_shape = (out_depth, width // fsdp_count)
    anywhere = pl.BlockSpec(memory_space=pl.ANY)
    inside = pl.BlockSpec(memory_space=pltpu.VMEM)
    shape = lambda *dims: jax.ShapeDtypeStruct(dims, jnp.bfloat16)
    vmem = lambda *dims: pltpu.VMEM(dims, jnp.bfloat16)
    wide = lambda *dims: pltpu.VMEM(dims, jnp.float32)
    sem = lambda *dims: pltpu.SemaphoreType.DMA(dims)
    rows = batch * length
    return pl.pallas_call(
        functools.partial(backward_kernel, line, heads, kv_heads),
        out_shape=(
            shape(batch, half, width),
            shape(batch, half, width),
            shape(batch, length, in_width),
            jax.ShapeDtypeStruct(out_shape, jnp.float32),
            jax.ShapeDtypeStruct((8, width), jnp.float32),
            shape(line, 2, half, width),
            shape(line, half, width),
            shape(line, 2, half, width),
        ),
        in_specs=[anywhere] * 10 + [inside] * 6,
        out_specs=(anywhere, anywhere, anywhere, inside, inside, anywhere, anywhere, anywhere),
        scratch_shapes=[
            wide(3, half, width),
            vmem(batch, half, width),
            vmem(batch, half, width),
            wide(batch, half, width),
            vmem(batch, half, width),
            vmem(rows, out_depth),
            vmem(rows, width),
            vmem(rows, max(out_depth, width)),
            vmem(rows, in_width),
            vmem(batch, half, width),
            vmem(2, CHUNK, max(width, in_width)),
            wide(2, length, group * features),
            wide(2, 2, length, features),
            vmem(group + 2, length, features),
            wide(group, length, features),
            wide(2, length, features),
            vmem(out_depth, width),
            *collect_scratch(line, out_shape),
            sem(5 + batch),
            sem(2),
            sem(2, 3),
            sem(2 * batch),
            sem(batch),
            sem(batch),
            sem(batch),
            sem(batch),
            vmem(BOXES, half, width),
            vmem(2 * line, half, width),
            wide(half, width),
            sem(BOXES),
            sem(2 * line),
            sem(line, 2),
            sem(line),
            sem(line, 2),
        ],
        compiler_params=pltpu.CompilerParams(
            collective_id=3, has_side_effects=True, vmem_limit_bytes=62 * MIB
        ),
    )(
        cot,
        totals,
        hidden,
        projected,
        context,
        in_full,
        out_full,
        tokens,
        part,
        cores,
        *gains,
        *tables,
    )[:5]


def gradients_kernel(
    line,
    normed,
    grads,
    gains_ref,
    xe_ref,
    ce_ref,
    act_ref,
    dgate_ref,
    dup_ref,
    in_total,
    gains_all,
    gate_total,
    up_total,
    down_total,
    parts,
    cores,
    firsts,
    rights,
    lefts,
    tree_send,
    tree_receive,
    gain_send,
    gain_receive,
    gain_local,
    wide_rows,
    slim_rows,
    gate_sum,
    up_sum,
    down_sum,
    load_sem,
    save_sem,
):
    narrow, spot = Spot(line, False), Spot(line, True)
    experts, count, _ = xe_ref.shape
    share = wide_rows.shape[1]
    turns = count // share
    pieces = [
        (expert, kind, turn)
        for expert in range(experts)
        for kind in range(2)
        for turn in range(turns)
    ]

    def loads(index):
        expert, kind, turn = pieces[index]
        slot = index % 2
        rows = pl.ds(turn * share, share)
        slim = (dgate_ref, dup_ref) if kind == 0 else (act_ref,)
        return [
            pltpu.make_async_copy(
                (xe_ref, ce_ref)[kind].at[expert, rows], wide_rows.at[slot], load_sem.at[slot, 0]
            )
        ] + [
            pltpu.make_async_copy(
                ref.at[expert, rows], slim_rows.at[slot, i], load_sem.at[slot, 1 + i]
            )
            for i, ref in enumerate(slim)
        ]

    def saves(expert, kind):
        pairs = ((gate_sum, gate_total), (up_sum, up_total))
        if kind:
            return [pltpu.make_async_copy(down_sum, down_total.at[expert], save_sem.at[2])]
        return [
            pltpu.make_async_copy(source, target.at[expert], save_sem.at[i])
            for i, (source, target) in enumerate(pairs)
        ]

    for copy in loads(0):
        copy.start()
    spot.greet()
    gains = Spread(
        spot,
        gains_ref,
        lambda block, half: gains_all.at[block, half],
        gain_send,
        gain_receive,
        gain_local.at[0],
    )
    gains.begin()
    depth, width = in_total.shape
    tree = Collect(
        narrow,
        lambda block, half: rows_at(parts, block, depth),
        in_total,
        cores,
        firsts,
        rights,
        lefts,
        tree_send,
        tree_receive,
    )
    chunk = PLANE * depth

    def plane(step, _):
        z = lax.rem(narrow.z + 1 + step, line)
        columns = pl.ds(pl.multiple_of(z * chunk, LANES), chunk)
        for start in range(0, width, CHUNK):
            parts[pl.ds(pl.multiple_of(z * chunk, 16), chunk), start : start + CHUNK] = (
                lax.dot_general(
                    normed[:, columns],
                    grads[:, start : start + CHUNK],
                    TRANSPOSED_LEFT,
                    preferred_element_type=jnp.float32,
                ).astype(jnp.bfloat16)
            )
        tree.begin(z)
        return 0

    lax.fori_loop(0, line, plane, 0)

    def piece(index):
        expert, kind, turn = pieces[index]
        slot = index % 2
        for copy in loads(index):
            copy.wait()
        if index + 1 < len(pieces):
            for copy in loads(index + 1):
                copy.start()
        if turn == 0 and expert:
            for copy in saves(expert - 1, kind):
                copy.wait()
        size = wide_rows.shape[2] // 4

        def add(target, place, left, right):
            product = lax.dot_general(
                left, right, TRANSPOSED_LEFT, preferred_element_type=jnp.float32
            )
            if turn:
                product = target[place] + product
            target[place] = product

        def part(step, _):
            at = pl.ds(pl.multiple_of(step * size, LANES), size)
            if kind:
                add(down_sum, (slice(None), at), slim_rows[slot, 0], wide_rows[slot, :, at])
            else:
                for i, target in enumerate((gate_sum, up_sum)):
                    add(target, (at, slice(None)), wide_rows[slot, :, at], slim_rows[slot, i])
            return 0

        lax.fori_loop(0, 4, part, 0)
        if turn == turns - 1:
            for copy in saves(expert, kind):
                copy.start()

    tree.cross()
    work = tree.tasks()
    steps = list(range(1, gains.steps()))
    filler = list(range(len(pieces)))
    while work or filler:
        for _ in range(2 if len(filler) > len(work) else 1):
            if filler:
                piece(filler.pop(0))
        if work:
            work.pop(0)()
        if steps:
            gains.step(steps.pop(0))
    gains.finish()
    for copy in saves(experts - 1, 0) + saves(experts - 1, 1):
        copy.wait()


def run_gradients(normed, grads, gains, expert_rows, fsdp_count):
    line = fsdp_count // PLANE
    width = grads.shape[1]
    experts, count, depth = expert_rows[0].shape
    units = expert_rows[2].shape[2]
    share = 2 * CHUNK if count % (2 * CHUNK) == 0 else count // (2 * line)
    shape = (normed.shape[1] // fsdp_count, width)
    sends, receives = spread_count(line, True)
    inside = pl.BlockSpec(memory_space=pltpu.VMEM)
    anywhere = pl.BlockSpec(memory_space=pl.ANY)
    return pl.pallas_call(
        functools.partial(gradients_kernel, line),
        out_shape=(
            jax.ShapeDtypeStruct(shape, jnp.float32),
            jax.ShapeDtypeStruct((fsdp_count, 2, *gains.shape), jnp.float32),
            jax.ShapeDtypeStruct((experts, depth, units), jnp.float32),
            jax.ShapeDtypeStruct((experts, depth, units), jnp.float32),
            jax.ShapeDtypeStruct((experts, units, depth), jnp.float32),
        ),
        in_specs=[inside, inside] + [anywhere] * 6,
        out_specs=(inside,) + (anywhere,) * 4,
        scratch_shapes=[
            pltpu.VMEM((normed.shape[1], width), jnp.bfloat16),
            *collect_scratch(line, shape),
            pltpu.SemaphoreType.DMA((sends,)),
            pltpu.SemaphoreType.DMA((receives,)),
            pltpu.SemaphoreType.DMA((1,)),
            pltpu.VMEM((2, share, depth), jnp.bfloat16),
            pltpu.VMEM((2, 2, share, units), jnp.bfloat16),
            pltpu.VMEM((depth, units), jnp.float32),
            pltpu.VMEM((depth, units), jnp.float32),
            pltpu.VMEM((units, depth), jnp.float32),
            pltpu.SemaphoreType.DMA((2, 3)),
            pltpu.SemaphoreType.DMA((3,)),
        ],
        compiler_params=pltpu.CompilerParams(
            collective_id=4, has_side_effects=True, vmem_limit_bytes=60 * MIB
        ),
    )(normed, grads, gains, *expert_rows)


def experts_kernel(
    line,
    slots,
    own_ref,
    cot_ref,
    info_ref,
    gate_ref,
    up_ref,
    down_ref,
    all_ref,
    total_ref,
    xe_all,
    ce_all,
    act_all,
    dgate_all,
    dup_all,
    part,
    cores,
    seconds,
    firsts,
    ends,
    hidden_w,
    down_w,
    x_rows,
    c_rows,
    xe,
    ce,
    acts,
    dgates,
    dups,
    hidden_grads,
    picks,
    weigh,
    rows,
    stage,
    inbox,
    outbox,
    summed,
    rows_send,
    rows_receive,
    rows_late_send,
    rows_late_receive,
    rows_local,
    load_sem,
    save_sem,
    stage_sem,
    inbox_sem,
    outbox_sem,
    total_sem,
    weight_sem,
    core_receive,
    second_receive,
    first_receive,
    end_receive,
):
    spot = Spot(line, True)
    z, core = spot.z, spot.core
    tree_semaphores = (rows_send, rows_receive, rows_late_send, rows_late_receive, rows_local)
    batch, half, width = own_ref.shape
    length = 2 * half
    units = down_ref.shape[1]
    groups = batch * line
    weights = [
        pltpu.make_async_copy(source, target, weight_sem.at[i])
        for i, (source, target) in enumerate(
            [(down_ref, down_w)]
            + [(gate_ref.at[e], hidden_w.at[e, :, pl.ds(0, units)]) for e in range(2)]
            + [(up_ref.at[e], hidden_w.at[e, :, pl.ds(units, units)]) for e in range(2)]
        )
    ]
    for copy in weights:
        copy.start()
    rows[...] = jnp.zeros_like(rows)
    spot.greet()

    def half_of(ref, index):
        return rows_at(ref, index, half)

    trees = []
    for i in range(batch):
        place = lambda block, start, size, i=i: all_ref.at[
            i, block, pl.ds(pl.multiple_of(start, 16), size)
        ]
        trees.append(rows_spread(spot, own_ref.at[i], place, half, tree_semaphores, i))
    run_trees(trees[0])
    for tree in sum(trees[1:], []):
        tree.begin()
    for copy in weights:
        copy.wait()

    plane_of = functools.partial(plane_in_turn, line)

    def load_group(group, member):
        at = lax.div(group, line)
        sequence = plane_of(group) * PLANE + member
        slot = member % 2
        return [
            pltpu.make_async_copy(all_ref.at[at, sequence], x_rows.at[slot], load_sem.at[0, slot]),
            pltpu.make_async_copy(cot_ref.at[at, sequence], c_rows.at[slot], load_sem.at[1, slot]),
        ]

    def saves(group):
        to = lambda ref, expert: rows_at(ref.at[expert], group, PLANE * slots)
        pairs = ((xe, xe_all), (ce, ce_all), (acts, act_all), (dgates, dgate_all), (dups, dup_all))
        return [
            pltpu.make_async_copy(source.at[expert], to(target, expert), save_sem.at[2 * i + expert])
            for i, (source, target) in enumerate(pairs)
            for expert in range(2)
        ]

    def staged(unit, y, mine):
        slot = y * 2 + mine
        if mine:
            return pltpu.make_async_copy(stage.at[slot], part.at[unit, y], stage_sem.at[slot])
        return spot.send(
            stage.at[slot], cores.at[unit, y], stage_sem.at[slot], core_receive.at[unit, y], CORE
        )

    def combine(unit, y):
        for mine in range(2):
            member = y * 2 + (core if mine else 1 - core)
            for start in range(0, width, CHUNK):
                stage[y * 2 + mine, :, start : start + CHUNK] = lax.dot_general(
                    picks[member],
                    rows[member, :, start : start + CHUNK],
                    TRANSPOSED_LEFT,
                    preferred_element_type=jnp.float32,
                ).astype(jnp.bfloat16)
            staged(unit, y, mine).start()

    def pick(group, member):
        slot = member % 2
        for copy in load_group(group, member):
            copy.wait()
        if member + 1 < PLANE:
            for copy in load_group(group, member + 1):
                copy.start()
        sequence = plane_of(group) * PLANE + member
        info = info_ref[lax.div(group, line) * line * PLANE + sequence]
        places = lax.broadcasted_iota(jnp.int32, (2 * LANES, length), 0)
        lower = places < LANES
        ranks = jnp.where(lower, info[0:1], info[1:2] + float(LANES)).astype(jnp.int32)
        some = jnp.where(lower, info[0:1], info[1:2]) >= 0.0
        hot = jnp.logical_and(ranks == places, some)
        chosen = hot.astype(jnp.float32).astype(jnp.bfloat16)
        picks[member] = chosen
        shares = jnp.where(hot, jnp.where(lower, info[2:3], info[3:4]), 0.0)
        column = jnp.sum(shares, axis=1, keepdims=True)
        here = pl.ds(member * slots, slots)
        for expert in range(2):
            weigh[expert, here, :] = jnp.broadcast_to(
                column[expert * LANES : expert * LANES + slots], (slots, LANES)
            )
        for source, target in ((x_rows, xe), (c_rows, ce)):
            for start in range(0, width, CHUNK):
                selected = jnp.dot(
                    chosen,
                    source[slot, :, start : start + CHUNK],
                    preferred_element_type=jnp.float32,
                ).astype(jnp.bfloat16)
                for expert in range(2):
                    target[expert, here, start : start + CHUNK] = selected[
                        expert * LANES : expert * LANES + slots
                    ]

    def keep(expert, product, start):
        at = pl.ds(expert * LANES, slots)
        for one in range(PLANE):
            rows[one, at, start : start + CHUNK] = product[one * slots : (one + 1) * slots].astype(
                jnp.bfloat16
            )

    def forward(expert):
        hidden = jnp.dot(xe[expert], hidden_w[expert], preferred_element_type=jnp.float32)
        gate, up = hidden[:, :units], hidden[:, units:]
        sigmoid = jax.nn.sigmoid(gate)
        silu = gate * sigmoid
        scale = weigh[expert, :, 0:1]
        acts[expert] = (silu * up * scale).astype(jnp.bfloat16)
        act_grads = scale * lax.dot_general(
            ce[expert], down_w[expert], TRANSPOSED_RIGHT, preferred_element_type=jnp.float32
        )
        gate_grads = (act_grads * up * (sigmoid * (1.0 + gate * (1.0 - sigmoid)))).astype(
            jnp.bfloat16
        )
        up_grads = (act_grads * silu).astype(jnp.bfloat16)
        dgates[expert] = gate_grads
        dups[expert] = up_grads
        hidden_grads[expert, :, :units] = gate_grads
        hidden_grads[expert, :, units:] = up_grads
        for start in range(0, width, CHUNK):
            keep(
                expert,
                jnp.dot(
                    acts[expert],
                    down_w[expert, :, start : start + CHUNK],
                    preferred_element_type=jnp.float32,
                ),
                start,
            )

    def backward(expert):
        for start in range(0, width, CHUNK):
            keep(
                expert,
                lax.dot_general(
                    hidden_grads[expert],
                    hidden_w[expert, start : start + CHUNK, :],
                    TRANSPOSED_RIGHT,
                    preferred_element_type=jnp.float32,
                ),
                start,
            )

    units_all = 2 * groups

    def inside(unit):
        valid = jnp.logical_and(unit >= 0, unit < units_all)
        return jnp.logical_and(valid, jnp.logical_or(unit >= 2 * line, unit % 2 == BACK))

    def ready(unit):
        @pl.when(jnp.logical_and(unit >= 0, unit < units_all))
        def _():
            for y in range(2):
                staged(unit, y, 1).wait()
                staged(unit, y, 0).wait_send()
                place, semaphore = cores.at[unit, y], core_receive.at[unit, y]
                spot.send(place, place, outbox_sem.at[0], semaphore, CORE).wait_recv()

    def done(unit, tensor, into):
        into(summed)
        copy = pltpu.make_async_copy(
            summed, total_ref.at[lax.div(unit, 2 * line), tensor], total_sem.at[0]
        )
        copy.start()
        copy.wait()

    sums = Sums(
        spot,
        lambda unit, y: part.at[unit, y],
        lambda unit, y: cores.at[unit, y],
        (seconds, firsts, ends),
        inbox,
        outbox,
        (inbox_sem, outbox_sem, second_receive, first_receive, end_receive),
        lambda unit: plane_of(lax.div(jnp.maximum(unit, 0), 2)),
        inside,
        ready,
        done,
        2,
    )

    def tree_turn(half_step, last):
        for i in range(1, batch):
            turn = half_step - (i - 1) * 2 * line
            if last:
                when(turn == 2 * line - 1, lambda: [tree.finish() for tree in trees[i]])
            else:
                inner = jnp.logical_and(turn >= 0, turn < 2 * line - 1)
                when(inner, lambda: [tree.step(turn + 1) for tree in trees[i]])

    def begin_pick(group):
        for copy in load_group(group, 0):
            copy.start()

    begin_pick(0)
    for member in range(PLANE):
        pick(0, member)

    def step_body(step, _):
        busy = step < groups
        more = step + 1 < groups
        for parity in range(2):
            half_step = step * 2 + parity
            tree_turn(half_step, False)
            sums.retire(half_step, parity)
            tasks = sums.tasks(half_step, parity)
            pieces = []
            for expert in range(2):
                pieces.append(functools.partial((forward, backward)[parity], expert))
            if parity == 0:
                pieces.append(lambda: [copy.start() for copy in saves(step)])
            for y in range(2):
                pieces.append(functools.partial(combine, half_step, y))
            pieces = [functools.partial(when, busy, piece) for piece in pieces]
            if parity == 1:

                def prepare():
                    for copy in saves(step):
                        copy.wait()
                    begin_pick(step + 1)

                tree_end = functools.partial(tree_turn, half_step, True)
                pieces += [tree_end, functools.partial(when, more, prepare)]
                for member in range(PLANE):
                    pieces.append(
                        functools.partial(when, more, functools.partial(pick, step + 1, member))
                    )
            sums.weave(tasks, pieces)
        return 0

    half_steps = sums.half_steps(units_all)
    lax.fori_loop(0, -(-half_steps // 2), step_body, 0)
    end = -(-half_steps // 2) * 2
    for parity in range(2):
        sums.retire(jnp.int32(end + parity), parity)
    for copy in saves(groups - 1):
        copy.wait()


def run_experts(rows, cot_all, info, w_gate, w_up, w_down, capacity, fsdp_count):
    line = fsdp_count // PLANE
    batch, half, width = rows.shape
    length = 2 * half
    units = w_down.shape[1]
    slots = -(-capacity // 16) * 16
    groups = batch * line
    count = groups * PLANE * slots
    taken = PLANE * slots
    shape = lambda *dims: jax.ShapeDtypeStruct(dims, jnp.bfloat16)
    block = (half, width)
    anywhere = pl.BlockSpec(memory_space=pl.ANY)
    vmem = lambda *dims: pltpu.VMEM(dims, jnp.bfloat16)
    sem = lambda *dims: pltpu.SemaphoreType.DMA(dims)
    return pl.pallas_call(
        functools.partial(experts_kernel, line, slots),
        out_shape=(
            shape(batch, fsdp_count, length, width),
            jax.ShapeDtypeStruct((batch, 2, *block), jnp.float32),
            shape(2, count, width),
            shape(2, count, width),
            shape(2, count, units),
            shape(2, count, units),
            shape(2, count, units),
            shape(2 * groups, 2, length, width),
            shape(2 * groups, 2, length, width),
            shape(2 * groups, 2, *block),
            shape(2 * groups, *block),
            shape(2 * groups, 2, *block),
        ),
        in_specs=[
            anywhere,
            anywhere,
            pl.BlockSpec(memory_space=pltpu.VMEM),
            anywhere,
            anywhere,
            anywhere,
        ],
        out_specs=(anywhere,) * 12,
        scratch_shapes=[
            vmem(2, width, 2 * units),
            vmem(2, units, width),
            vmem(2, length, width),
            vmem(2, length, width),
            vmem(2, taken, width),
            vmem(2, taken, width),
            vmem(2, taken, units),
            vmem(2, taken, units),
            vmem(2, taken, units),
            vmem(2, taken, 2 * units),
            vmem(PLANE, 2 * LANES, length),
            pltpu.VMEM((2, taken, LANES), jnp.float32),
            vmem(PLANE, 2 * LANES, width),
            vmem(PLANE, length, width),
            vmem(12, *block),
            vmem(10, *block),
            pltpu.VMEM(block, jnp.float32),
            *rows_semaphores(batch, line),
            sem(2, 2),
            sem(10),
            sem(PLANE),
            sem(12),
            sem(10),
            sem(1),
            sem(5),
            sem(2 * groups, 2),
            sem(2 * groups, 2),
            sem(2 * groups),
            sem(2 * groups, 2),
        ],
        compiler_params=pltpu.CompilerParams(
            collective_id=2, has_side_effects=True, vmem_limit_bytes=60 * MIB
        ),
    )(rows, cot_all, info, w_gate, w_up, w_down)[1:9]


def packed_picks(routes, gates):
    length = routes.shape[2]
    packed = jnp.concatenate([routes[:, 0].astype(jnp.float32), gates[:, 0]], axis=-1)
    packed = jnp.swapaxes(packed, 1, 2).reshape(-1, length)
    return jnp.pad(packed, ((0, 0), (0, -length % LANES)))


def slot_info(packed, batch, top, length, local_experts):
    fsdp_count = packed.shape[0]
    packed = packed[..., :length].reshape(fsdp_count, batch, 1, 2 * top, length)
    packed = jnp.swapaxes(packed, 0, 1)
    experts = lax.axis_index(FSDP) * local_experts + jnp.arange(local_experts, dtype=jnp.int32)
    same = packed[..., :top, :].astype(jnp.int32) == experts[:, None, None]
    hot = jnp.any(same, axis=3)
    shares = jnp.sum(jnp.where(same, packed[..., top:, :], 0.0), axis=3)
    position = jnp.arange(length)
    upper = (position[:, None] < position[None, :]).astype(jnp.bfloat16)
    rank = jnp.dot(
        hot.astype(jnp.bfloat16).reshape(-1, length), upper, preferred_element_type=jnp.float32
    )
    rank = jnp.where(hot, rank.reshape(hot.shape), -1.0)
    return jnp.concatenate([rank, shares], axis=2).reshape(-1, 2 * local_experts, length)


def gathered_layer(
    tokens,
    cotangent,
    norm1_gain,
    w_query,
    key_projection_weight,
    value_projection_weight,
    query_gain,
    key_gain,
    w_out,
    norm2_gain,
    w_gate,
    w_up,
    w_down,
    routes,
    gates,
):
    batch_count = tokens.shape[0]
    model_width = tokens.shape[3]
    sequence_length = routes.shape[2]
    half_length = tokens.shape[2]
    top_count = routes.shape[3]
    head_features = query_gain.shape[0]
    local_experts = w_gate.shape[0]
    fsdp_count = lax.axis_size(FSDP)
    all_experts = local_experts * fsdp_count
    capacity = 7 * top_count * sequence_length // (6 * all_experts)
    query_width = w_query.shape[1]
    kv_width = key_projection_weight.shape[1]
    kv_heads = kv_width // head_features
    cosine_table, sine_values = rotary_tables(sequence_length, head_features)
    weight_in = jnp.concatenate([w_query, key_projection_weight, value_projection_weight], axis=1)
    half_signs = jnp.where(jnp.arange(head_features) < head_features // 2, -1.0, 1.0)
    tables = (cosine_table[:, 0], sine_values[:, 0] * half_signs)
    gains = [gain[None, :] for gain in (norm1_gain, norm2_gain, query_gain, key_gain)]
    cot_all, in_full, out_full, picks, normed, projected, contexts, hidden, second = run_forward(
        tokens[:, 0],
        cotangent[:, 0],
        weight_in,
        w_out,
        packed_picks(routes, gates),
        gains,
        tables,
        fsdp_count,
        kv_heads,
    )
    info = slot_info(picks, batch_count, top_count, sequence_length, local_experts)
    totals, *expert_rows, part, cores = run_experts(
        second, cot_all, info, w_gate, w_up, w_down, capacity, fsdp_count
    )
    block_out, input_grad, projected_grads, out_sum, gain_grads = run_backward(
        cotangent[:, 0],
        totals,
        hidden,
        projected,
        contexts,
        in_full,
        out_full,
        tokens[:, 0],
        part,
        cores,
        gains,
        tables,
        fsdp_count,
        kv_heads,
    )
    rows = batch_count * sequence_length
    in_sum, gains_all, *expert_grads = run_gradients(
        normed.reshape(rows, -1),
        projected_grads.reshape(rows, -1),
        gain_grads,
        expert_rows,
        fsdp_count,
    )
    gains_sum = jnp.sum(gains_all, axis=(0, 1))
    return (
        block_out[:, None],
        input_grad[:, None],
        gains_sum[0],
        in_sum[:, :query_width],
        in_sum[:, query_width : query_width + kv_width],
        in_sum[:, query_width + kv_width :],
        gains_sum[2, :head_features],
        gains_sum[3, :head_features],
        out_sum,
        gains_sum[1],
        *expert_grads,
    )


def shards(*arrays):
    tokens, routes, w_gate = arrays[0], arrays[13], arrays[10]
    fsdp_count = lax.axis_size(FSDP)
    gathered = fsdp_count * routes.shape[2] * tokens.shape[3] * 2
    fits = gathered <= 24 * MIB and fsdp_count % PLANE == 0 and lax.axis_size(TP) == 2
    if fits and w_gate.shape[0] == 2:
        return gathered_layer(*arrays)
    return exchanged_layer(*arrays)


def solution(mesh):
    in_specs = (
        P(None, "fsdp", "tp", None),
        P(None, "fsdp", "tp", None),
        P(),
        P("fsdp", "tp"),
        P("fsdp", "tp"),
        P("fsdp", "tp"),
        P(),
        P(),
        P("tp", "fsdp"),
        P(),
        P("fsdp", None, "tp"),
        P("fsdp", None, "tp"),
        P("fsdp", "tp", None),
        P(None, "fsdp", None, None),
        P(None, "fsdp", None, None),
    )
    out_specs = (
        P(None, "fsdp", "tp", None),
        P(None, "fsdp", "tp", None),
        P(),
        P("fsdp", "tp"),
        P("fsdp", "tp"),
        P("fsdp", "tp"),
        P(),
        P(),
        P("tp", "fsdp"),
        P(),
        P("fsdp", None, "tp"),
        P("fsdp", None, "tp"),
        P("fsdp", "tp", None),
    )
    return jax.shard_map(shards, mesh=mesh, in_specs=in_specs, out_specs=out_specs, check_vma=False)
```

```python
import functools

import jax
import jax.numpy as jnp
from jax import lax
from jax.experimental import pallas as pl
from jax.experimental.pallas import tpu as pltpu
from jax.sharding import PartitionSpec as P

BLOCK = 256


EPSILON = 1e-06
ROPE_BASE = 1000000.0
MASKED = -1e30
TILE_PICKS = 128


def rms_scale(row_block, gain_row):
    return (
        row_block
        * lax.rsqrt(jnp.mean(row_block * row_block, axis=-1, keepdims=True) + EPSILON)
        * gain_row
    )


def rotary_tables(sequence_length, head_width):
    half_width = head_width // 2
    inverse = ROPE_BASE ** (-2.0 * jnp.arange(half_width, dtype=jnp.float32) / head_width)
    angles = jnp.arange(sequence_length, dtype=jnp.float32)[:, None] * inverse[None, :]
    cosine_table = jnp.concatenate([jnp.cos(angles), jnp.cos(angles)], axis=-1)[:, None, :]
    sine_values = jnp.concatenate([jnp.sin(angles), jnp.sin(angles)], axis=-1)[:, None, :]
    return (cosine_table, sine_values)


def rotate(head_rows, cosine_table, sine_values):
    half_width = head_rows.shape[-1] // 2
    turned = jnp.concatenate([-head_rows[..., half_width:], head_rows[..., :half_width]], axis=-1)
    return head_rows * cosine_table + turned * sine_values


def prepare_heads(projected, gain_row, cosine_table, sine_values):
    return rotate(rms_scale(projected, gain_row), cosine_table, sine_values)


def swiglu(gate_act, up_act):
    return jax.nn.silu(gate_act) * up_act


def slot_tables(route_rows, gate_rows, expert_count, capacity):
    sequence_length = route_rows.shape[0]
    top_count = route_rows.shape[1]
    pick_count = sequence_length * top_count
    tile_count = pick_count // TILE_PICKS
    flat_routes = route_rows.reshape(-1)
    onehot = (flat_routes[:, None] == jnp.arange(expert_count, dtype=jnp.int32)[None, :]).astype(
        jnp.bfloat16
    )
    tiles = onehot.reshape(tile_count, TILE_PICKS, expert_count)
    positions = jnp.arange(TILE_PICKS, dtype=jnp.int32)
    lower = (positions[None, :] < positions[:, None]).astype(jnp.bfloat16)
    within = jnp.einsum("ij,bje->bie", lower, tiles, preferred_element_type=jnp.float32)
    tile_totals = jnp.sum(tiles.astype(jnp.float32), axis=1)
    offsets = jnp.cumsum(tile_totals, axis=0) - tile_totals
    before = within + offsets[:, None, :]
    slot_rank = jnp.sum(before * tiles.astype(jnp.float32), axis=-1).reshape(-1).astype(jnp.int32)
    slot_index = flat_routes * capacity + slot_rank
    pick_ids = jnp.arange(pick_count, dtype=jnp.int32) // top_count
    slot_owner = (
        jnp.full((expert_count * capacity,), sequence_length, jnp.int32)
        .at[slot_index]
        .set(pick_ids)
    )
    slot_weight = (
        jnp.zeros((expert_count * capacity,), jnp.float32).at[slot_index].set(gate_rows.reshape(-1))
    )
    return (slot_index, slot_owner, slot_weight)


def exchanged_layer(
    tokens,
    cotangent,
    norm1_gain,
    w_query,
    key_projection_weight,
    value_projection_weight,
    query_gain,
    key_gain,
    w_out,
    norm2_gain,
    w_gate,
    w_up,
    w_down,
    routes,
    gates,
):
    batch_count = tokens.shape[0]
    model_width = tokens.shape[3]
    sequence_length = routes.shape[2]
    top_count = routes.shape[3]
    head_features = query_gain.shape[0]
    local_experts = w_gate.shape[0]
    fsdp_count = lax.axis_size("fsdp")
    all_experts = local_experts * fsdp_count
    capacity = 7 * top_count * sequence_length // (6 * all_experts)
    query_heads = w_query.shape[1] // head_features
    kv_heads = key_projection_weight.shape[1] // head_features
    group_size = query_heads // kv_heads
    score_scale = head_features ** (-0.5)
    cosine_table, sine_values = rotary_tables(sequence_length, head_features)
    block_ids = jnp.arange(sequence_length, dtype=jnp.int32) // BLOCK
    visible = (block_ids[None, :] <= block_ids[:, None])[None, None]
    first_gain = norm1_gain.astype(jnp.float32)
    second_gain = norm2_gain.astype(jnp.float32)
    query_factor_scale = query_gain.astype(jnp.float32)
    key_scale = key_gain.astype(jnp.float32)
    zero_row = jnp.zeros((1, model_width), jnp.bfloat16)
    buffer_shape = (fsdp_count, local_experts, capacity, model_width)

    def masked_scores(query_fourfold, key_rows):
        raw_scores = (
            jnp.einsum(
                "qcgd,kcd->cgqk", query_fourfold, key_rows, preferred_element_type=jnp.float32
            )
            * score_scale
        )
        return jnp.where(visible, raw_scores, MASKED)

    def prep_heads(projected, gain_row):
        return prepare_heads(projected, gain_row, cosine_table, sine_values)

    gain_sums = (
        jnp.zeros((model_width,), jnp.float32),
        jnp.zeros((model_width,), jnp.float32),
        jnp.zeros((head_features,), jnp.float32),
        jnp.zeros((head_features,), jnp.float32),
    )
    expert_grads = (
        jnp.zeros(w_gate.shape, jnp.float32),
        jnp.zeros(w_up.shape, jnp.float32),
        jnp.zeros(w_down.shape, jnp.float32),
    )
    attn_grads = tuple(
        (
            jnp.zeros(weight_part.shape, jnp.float32)
            for weight_part in (w_query, key_projection_weight, value_projection_weight, w_out)
        )
    )
    outputs = []
    input_grads = []
    for batch_index in range(batch_count):
        query_full, key_full, value_full, out_full = (
            lax.all_gather(w_query, "fsdp", axis=0, tiled=True),
            lax.all_gather(key_projection_weight, "fsdp", axis=0, tiled=True),
            lax.all_gather(value_projection_weight, "fsdp", axis=0, tiled=True),
            lax.all_gather(w_out, "fsdp", axis=1, tiled=True),
        )
        own_rows = tokens[batch_index, 0].astype(jnp.float32)
        own_cot = cotangent[batch_index, 0]
        route_rows = routes[batch_index, 0]
        gate_rows = gates[batch_index, 0]
        first_normed = rms_scale(own_rows, first_gain).astype(jnp.bfloat16)
        normed_all = lax.all_gather(first_normed, "tp", axis=0, tiled=True)
        query_projected = jnp.dot(
            normed_all, query_full, preferred_element_type=jnp.float32
        ).reshape(sequence_length, query_heads, head_features)
        key_projected = jnp.dot(normed_all, key_full, preferred_element_type=jnp.float32).reshape(
            sequence_length, kv_heads, head_features
        )
        value_row_list = (
            jnp.dot(normed_all, value_full, preferred_element_type=jnp.float32)
            .astype(jnp.bfloat16)
            .reshape(sequence_length, kv_heads, head_features)
        )
        query_rot = prep_heads(query_projected, query_factor_scale).astype(jnp.bfloat16)
        key_rot = prep_heads(key_projected, key_scale).astype(jnp.bfloat16)
        query_fourfold = query_rot.reshape(sequence_length, kv_heads, group_size, head_features)
        scores = masked_scores(query_fourfold, key_rot)
        row_max = jnp.max(scores, axis=-1, keepdims=True)
        exp_scores = jnp.exp(scores - row_max)
        totals = jnp.sum(exp_scores, axis=-1, keepdims=True)
        log_total = row_max + jnp.log(totals)
        prob_rows = (exp_scores / totals).astype(jnp.bfloat16)
        context = (
            jnp.einsum(
                "cgqk,kcd->qcgd", prob_rows, value_row_list, preferred_element_type=jnp.float32
            )
            .astype(jnp.bfloat16)
            .reshape(sequence_length, query_heads * head_features)
        )
        attn_own = lax.psum_scatter(
            jnp.dot(context, out_full, preferred_element_type=jnp.float32).astype(jnp.bfloat16),
            "tp",
            scatter_dimension=0,
            tiled=True,
        ).astype(jnp.float32)
        hidden_own = own_rows + attn_own
        second_normed = rms_scale(hidden_own, second_gain).astype(jnp.bfloat16)
        normed_two, cot_all = (
            lax.all_gather(second_normed, "tp", axis=0, tiled=True),
            lax.all_gather(own_cot, "tp", axis=0, tiled=True),
        )
        slot_index, slot_owner, slot_weight = slot_tables(
            route_rows, gate_rows, all_experts, capacity
        )
        padded_rows = jnp.concatenate([normed_two, zero_row], axis=0)
        send_rows = padded_rows[slot_owner].reshape(buffer_shape)
        expert_in = lax.all_to_all(send_rows, "fsdp", split_axis=0, concat_axis=0, tiled=True)
        gate_act = jnp.einsum(
            "sekd,edf->sekf", expert_in, w_gate, preferred_element_type=jnp.float32
        )
        up_act = jnp.einsum("sekd,edf->sekf", expert_in, w_up, preferred_element_type=jnp.float32)
        act_rows = swiglu(gate_act, up_act).astype(jnp.bfloat16)
        expert_out = jnp.einsum(
            "sekf,efd->sekd", act_rows, w_down, preferred_element_type=jnp.float32
        )
        returned = lax.all_to_all(
            expert_out.astype(jnp.bfloat16), "fsdp", split_axis=0, concat_axis=0, tiled=True
        ).astype(expert_out.dtype)
        picked = returned.reshape(all_experts * capacity, model_width)[slot_index].reshape(
            sequence_length, top_count, model_width
        )
        moe_part = jnp.sum(picked * gate_rows[:, :, None], axis=1)
        moe_own = lax.psum_scatter(
            moe_part.astype(jnp.bfloat16), "tp", scatter_dimension=0, tiled=True
        ).astype(jnp.float32)
        outputs.append((hidden_own + moe_own).astype(jnp.bfloat16))
        cot_padded = jnp.concatenate([cot_all, zero_row], axis=0)
        send_grads = (
            (slot_weight[:, None] * cot_padded[slot_owner])
            .astype(jnp.bfloat16)
            .reshape(buffer_shape)
        )
        out_grads = lax.all_to_all(send_grads, "fsdp", split_axis=0, concat_axis=0, tiled=True)
        act_grads = jnp.einsum(
            "sekd,efd->sekf", out_grads, w_down, preferred_element_type=jnp.float32
        )
        _, swiglu_back = jax.vjp(swiglu, gate_act, up_act)
        gate_grads, up_grads = swiglu_back(act_grads)
        gate_grads = gate_grads.astype(jnp.bfloat16)
        up_grads = up_grads.astype(jnp.bfloat16)
        expert_grads = (
            expert_grads[0]
            + jnp.einsum(
                "sekd,sekf->edf", expert_in, gate_grads, preferred_element_type=jnp.float32
            ),
            expert_grads[1]
            + jnp.einsum("sekd,sekf->edf", expert_in, up_grads, preferred_element_type=jnp.float32),
            expert_grads[2]
            + jnp.einsum("sekf,sekd->efd", act_rows, out_grads, preferred_element_type=jnp.float32),
        )
        input_part = jnp.einsum(
            "sekf,edf->sekd", gate_grads, w_gate, preferred_element_type=jnp.float32
        ) + jnp.einsum("sekf,edf->sekd", up_grads, w_up, preferred_element_type=jnp.float32)
        input_back = lax.all_to_all(
            input_part.astype(jnp.bfloat16), "fsdp", split_axis=0, concat_axis=0, tiled=True
        ).astype(input_part.dtype)
        normed_grads = jnp.sum(
            input_back.reshape(all_experts * capacity, model_width)[slot_index].reshape(
                sequence_length, top_count, model_width
            ),
            axis=1,
        )
        normed_own = lax.psum_scatter(
            normed_grads.astype(jnp.bfloat16), "tp", scatter_dimension=0, tiled=True
        ).astype(jnp.float32)
        _, second_back = jax.vjp(rms_scale, hidden_own, second_gain)
        hidden_part, second_gain_grad = second_back(normed_own)
        hidden_grad = own_cot.astype(jnp.float32) + hidden_part
        attn_grad_all = lax.all_gather(hidden_grad.astype(jnp.bfloat16), "tp", axis=0, tiled=True)
        out_weight_grad = jnp.einsum(
            "th,td->hd", context, attn_grad_all, preferred_element_type=jnp.float32
        )
        context_grad = (
            jnp.einsum("td,hd->th", attn_grad_all, out_full, preferred_element_type=jnp.float32)
            .astype(jnp.bfloat16)
            .reshape(sequence_length, kv_heads, group_size, head_features)
        )
        exp_again = jnp.exp(masked_scores(query_fourfold, key_rot) - log_total)
        probs_again = exp_again.astype(jnp.bfloat16)
        prob_grads = jnp.einsum(
            "qcgd,kcd->cgqk", context_grad, value_row_list, preferred_element_type=jnp.float32
        )
        value_grads = (
            jnp.einsum(
                "cgqk,qcgd->kcd", probs_again, context_grad, preferred_element_type=jnp.float32
            )
            .astype(jnp.bfloat16)
            .reshape(sequence_length, kv_heads * head_features)
        )
        score_grads = (
            exp_again * (prob_grads - jnp.sum(exp_again * prob_grads, axis=-1, keepdims=True))
        ).astype(jnp.bfloat16)
        query_rot_grads = (
            jnp.einsum("cgqk,kcd->qcgd", score_grads, key_rot, preferred_element_type=jnp.float32)
            * score_scale
        ).reshape(sequence_length, query_heads, head_features)
        key_rot_grads = (
            jnp.einsum(
                "cgqk,qcgd->kcd", score_grads, query_fourfold, preferred_element_type=jnp.float32
            )
            * score_scale
        )
        _, query_back = jax.vjp(prep_heads, query_projected, query_factor_scale)
        query_proj_grads, query_gain_grad = query_back(query_rot_grads)
        _, key_back = jax.vjp(prep_heads, key_projected, key_scale)
        key_proj_grads, key_gain_grad = key_back(key_rot_grads)
        query_proj_grads = query_proj_grads.astype(jnp.bfloat16).reshape(
            sequence_length, query_heads * head_features
        )
        key_proj_grads = key_proj_grads.astype(jnp.bfloat16).reshape(
            sequence_length, kv_heads * head_features
        )
        first_normed_grads = (
            jnp.einsum(
                "tq,dq->td", query_proj_grads, query_full, preferred_element_type=jnp.float32
            )
            + jnp.einsum("tq,dq->td", key_proj_grads, key_full, preferred_element_type=jnp.float32)
            + jnp.einsum("tq,dq->td", value_grads, value_full, preferred_element_type=jnp.float32)
        )
        weight_parts = (
            jnp.einsum(
                "td,tq->dq", normed_all, query_proj_grads, preferred_element_type=jnp.float32
            ),
            jnp.einsum("td,tq->dq", normed_all, key_proj_grads, preferred_element_type=jnp.float32),
            jnp.einsum("td,tq->dq", normed_all, value_grads, preferred_element_type=jnp.float32),
            out_weight_grad,
        )
        first_own = lax.psum_scatter(
            first_normed_grads.astype(jnp.bfloat16), "tp", scatter_dimension=0, tiled=True
        ).astype(jnp.float32)
        _, first_back = jax.vjp(rms_scale, own_rows, first_gain)
        row_part, first_gain_grad = first_back(first_own)
        input_grads.append((hidden_grad + row_part).astype(jnp.bfloat16))
        gain_sums = (
            gain_sums[0] + first_gain_grad,
            gain_sums[1] + second_gain_grad,
            gain_sums[2] + query_gain_grad,
            gain_sums[3] + key_gain_grad,
        )
        attn_grads = jax.tree.map(
            jnp.add,
            attn_grads,
            (
                lax.psum_scatter(weight_parts[0], "fsdp", scatter_dimension=0, tiled=True),
                lax.psum_scatter(weight_parts[1], "fsdp", scatter_dimension=0, tiled=True),
                lax.psum_scatter(weight_parts[2], "fsdp", scatter_dimension=0, tiled=True),
                lax.psum_scatter(weight_parts[3], "fsdp", scatter_dimension=1, tiled=True),
            ),
        )
    summed = lax.psum((gain_sums[0], gain_sums[1], gain_sums[2], gain_sums[3]), ("fsdp", "tp"))
    block_out = jnp.stack(outputs)[:, None]
    input_grad = jnp.stack(input_grads)[:, None]
    return (
        block_out,
        input_grad,
        summed[0],
        attn_grads[0],
        attn_grads[1],
        attn_grads[2],
        summed[2],
        summed[3],
        attn_grads[3],
        summed[1],
        expert_grads[0],
        expert_grads[1],
        expert_grads[2],
    )


MESH = pl.DeviceIdType.MESH
FSDP, TP = "fsdp", "tp"
PLANE = 4
LANES = 128
MIB = 1 << 20
RIGHT, LEFT, FIRST, SECOND, CORE, CROSS = range(6)
TRANSPOSED_LEFT = (((0,), (0,)), ((), ()))
TRANSPOSED_RIGHT = (((1,), (1,)), ((), ()))
OUTPUT, BACK = range(2)
CHUNK = 512


class Spot:
    def __init__(self, line, wide, turned=True):
        self.line = line
        self.wide = wide
        self.turned = turned
        self.planes = 4 if wide else 2
        index = lax.axis_index(FSDP)
        self.x = lax.axis_index(TP)
        self.z = lax.div(index, PLANE)
        self.y = lax.rem(lax.div(index, 2), 2)
        self.core = lax.rem(index, 2)

    def side(self, core, first, second):
        flip_y, flip_x = first, second
        if self.wide and self.turned:
            flip_y = (1 - core) * first + core * second
            flip_x = core * first + (1 - core) * second
        return self.y + flip_y * (1 - 2 * self.y), self.x + flip_x * (1 - 2 * self.x)

    def block(self, core, first, second, z):
        y, x = self.side(core, first, second)
        return z * PLANE + y * 2 + core, x

    def device(self, kind):
        if kind == RIGHT:
            return self.block(self.core, 0, 0, self.z + 1)
        if kind == LEFT:
            return self.block(self.core, 0, 0, self.z - 1)
        if kind == CORE:
            return self.block(1 - self.core, 0, 0, self.z)
        if kind == CROSS:
            return self.block(self.core, 0, 0, self.z)[0], 1 - self.x
        return self.block(self.core, int(kind == FIRST), int(kind == SECOND), self.z)

    def kinds(self):
        return (FIRST, SECOND, CORE) if self.wide else (FIRST, CORE)

    def number(self, first, second, z):
        return (second * 2 + first) * self.line + z

    def order(self, step):
        if isinstance(step, int) and step == 0:
            return [(self.z, None)]
        return [(self.z - step, self.z - step >= 0), (self.z + step, self.z + step < self.line)]

    def greet(self):
        barrier = pltpu.get_barrier_semaphore()

        def signal(kind):
            pl.semaphore_signal(barrier, inc=1, device_id=self.device(kind), device_id_type=MESH)

        for kind in self.kinds():
            signal(kind)
        when(self.z + 1 < self.line, lambda: signal(RIGHT))
        when(self.z > 0, lambda: signal(LEFT))
        around = (self.z + 1 < self.line).astype(jnp.int32) + (self.z > 0).astype(jnp.int32)
        pl.semaphore_wait(barrier, len(self.kinds()) + around)

    def send(self, source, target, send_sem, receive_sem, kind):
        return pltpu.make_async_remote_copy(
            src_ref=source,
            dst_ref=target,
            send_sem=send_sem,
            recv_sem=receive_sem,
            device_id=self.device(kind),
            device_id_type=MESH,
        )


def when(condition, action):
    def run():
        action()

    if condition is None or condition is True:
        run()
    elif condition is not False:
        pl.when(condition)(run)


class Spread:
    def __init__(self, spot, source, slot, send, receive, local):
        self.spot = spot
        self.slot = slot
        self.source = source
        self.sends = send
        self.receives = receive
        self.mine = pltpu.make_async_copy(source, slot(*spot.block(spot.core, 0, 0, spot.z)), local)

    def copy(self, first, second, z, kind, own=False):
        spot = self.spot
        place = self.slot(*spot.block(spot.core, first, second, z))
        number = spot.number(first, second, z)
        arrival = {
            RIGHT: number,
            LEFT: number,
            FIRST: spot.number(1, 0, z),
            SECOND: spot.number(first, 1, z),
            CORE: spot.planes * spot.line + number,
        }[kind]
        departure = {RIGHT: 0, LEFT: 1, FIRST: 2, SECOND: 3, CORE: 5}[kind] * spot.line + number
        source = self.source if own else place
        return spot.send(source, place, self.sends.at[departure], self.receives.at[arrival], kind)

    def arrived(self, first, second, z, other=False):
        spot = self.spot
        core = 1 - spot.core if other else spot.core
        place = self.slot(*spot.block(core, first, second, z))
        number = spot.number(first, second, z) + (spot.planes * spot.line if other else 0)
        spot.send(place, place, self.sends.at[0], self.receives.at[number], CORE).wait_recv()

    def steps(self):
        return self.spot.line + (3 if self.spot.wide else 1)

    def begin(self):
        spot = self.spot
        z = spot.z
        when(z + 1 < spot.line, lambda: self.copy(0, 0, z, RIGHT, True).start())
        when(z > 0, lambda: self.copy(0, 0, z, LEFT, True).start())
        for kind in spot.kinds():
            self.copy(0, 0, z, kind, True).start()
        self.mine.start()

    def step(self, step):
        spot = self.spot
        line, z = spot.line, spot.z

        def reached(away, action):
            inside = jnp.logical_and(away >= 0, away < line)
            when(jnp.logical_and(inside, z - away >= 0), lambda: action(z - away, True))
            when(
                jnp.logical_and(inside, jnp.logical_and(away > 0, z + away < line)),
                lambda: action(z + away, False),
            )

        def along(zz, from_left):
            self.arrived(0, 0, zz)
            if from_left:
                when(z + 1 < line, lambda: self.copy(0, 0, zz, RIGHT).start())
            else:
                when(z > 0, lambda: self.copy(0, 0, zz, LEFT).start())
            for kind in spot.kinds():
                self.copy(0, 0, zz, kind).start()

        def firsts(zz, _):
            self.arrived(1, 0, zz)
            if spot.wide:
                self.copy(1, 0, zz, SECOND).start()
            self.copy(1, 0, zz, CORE).start()

        def lasts(first):
            def action(zz, _):
                self.arrived(first, 1, zz)
                self.copy(first, 1, zz, CORE).start()

            return action

        step = jnp.asarray(step, jnp.int32)
        reached(step, along)
        reached(step - 1, firsts)
        if spot.wide:
            reached(step - 2, lasts(0))
            reached(step - 3, lasts(1))

    def finish(self):
        spot = self.spot
        z = spot.z

        def body(zz, _):
            when(
                jnp.logical_and(z + 1 < spot.line, zz <= z),
                lambda: self.copy(0, 0, zz, RIGHT).wait_send(),
            )
            when(jnp.logical_and(z > 0, zz >= z), lambda: self.copy(0, 0, zz, LEFT).wait_send())
            self.copy(0, 0, zz, FIRST).wait_send()
            for second in range(2 if spot.wide else 1):
                for first in (0, 1):
                    if spot.wide and not second:
                        self.copy(first, 0, zz, SECOND).wait_send()
                    self.copy(first, second, zz, CORE).wait_send()
                    self.arrived(first, second, zz, other=True)
            return 0

        lax.fori_loop(0, spot.line, body, 0)
        self.mine.wait()


class LateSpread(Spread):
    def steps(self):
        return self.spot.line + 2

    def copy(self, first, second, z, kind, own=False):
        spot = self.spot
        place = self.slot(*spot.block(spot.core, first, second, z))
        number = spot.number(first, second, z)
        arrival = {
            RIGHT: number,
            LEFT: number,
            FIRST: spot.number(1, 0, z),
            SECOND: spot.number(first, 1, z),
            CORE: spot.planes * spot.line + number,
        }[kind]
        departure = {RIGHT: 0, LEFT: 4, CORE: 8, FIRST: 12, SECOND: 13}[kind] * spot.line + number
        source = self.source if own else place
        return spot.send(source, place, self.sends.at[departure], self.receives.at[arrival], kind)

    def along_both(self, first, second, own=False):
        spot = self.spot
        z = spot.z
        when(z + 1 < spot.line, lambda: self.copy(first, second, z, RIGHT, own).start())
        when(z > 0, lambda: self.copy(first, second, z, LEFT, own).start())
        self.copy(first, second, z, CORE, own).start()

    def begin(self):
        self.copy(0, 0, self.spot.z, FIRST, True).start()
        self.copy(0, 0, self.spot.z, SECOND, True).start()
        self.along_both(0, 0, True)
        self.mine.start()

    def step(self, step):
        spot = self.spot
        line, z = spot.line, spot.z
        step = jnp.asarray(step, jnp.int32)

        def passed(first, second, zz, kind, more):
            self.arrived(first, second, zz)
            when(more, lambda: self.copy(first, second, zz, kind).start())
            self.copy(first, second, zz, CORE).start()

        for first, second in ((0, 0), (1, 0), (0, 1), (1, 1)):
            away = step - (first + second)

            def here():
                self.arrived(first, second, z)
                if first and not second:
                    self.copy(1, 0, z, SECOND).start()
                self.along_both(first, second)

            if first or second:
                when(away == 0, here)
            far = jnp.logical_and(away > 0, away < line)
            when(
                jnp.logical_and(far, z - away >= 0),
                lambda: passed(first, second, z - away, RIGHT, z + 1 < line),
            )
            when(
                jnp.logical_and(far, z + away < line),
                lambda: passed(first, second, z + away, LEFT, z > 0),
            )

    def finish(self):
        spot = self.spot
        z = spot.z

        def body(zz, _):
            for second in (0, 1):
                for first in (0, 1):
                    when(
                        jnp.logical_and(z + 1 < spot.line, zz <= z),
                        lambda: self.copy(first, second, zz, RIGHT).wait_send(),
                    )
                    when(
                        jnp.logical_and(z > 0, zz >= z),
                        lambda: self.copy(first, second, zz, LEFT).wait_send(),
                    )
                    self.copy(first, second, zz, CORE).wait_send()
                    self.arrived(first, second, zz, other=True)
            return 0

        lax.fori_loop(0, spot.line, body, 0)
        self.copy(0, 0, z, FIRST).wait_send()
        for first in (0, 1):
            self.copy(first, 0, z, SECOND).wait_send()
        self.mine.wait()


def rows_spread(spot, source, place, rows, semaphores, at):
    late = late_rows(rows)
    early = rows - late
    send, receive, late_send, late_receive, local = semaphores

    def slot(start, size):
        return lambda block, side: place(block, side * rows + start, size)

    return [
        Spread(
            spot,
            source.at[pl.ds(0, early)],
            slot(0, early),
            send.at[at],
            receive.at[at],
            local.at[at, 0],
        ),
        LateSpread(
            spot,
            source.at[pl.ds(early, late)],
            slot(early, late),
            late_send.at[at],
            late_receive.at[at],
            local.at[at, 1],
        ),
    ]


def late_rows(rows):
    return max(16, round(rows * 2 / 9 / 16) * 16)


def rows_semaphores(batch, line):
    counts = (*spread_count(line, True), 15 * line, 8 * line, 2)
    return [pltpu.SemaphoreType.DMA((batch, count)) for count in counts]


def run_trees(trees):
    for tree in trees:
        tree.begin()

    def body(step, _):
        for tree in trees:
            tree.step(step)
        return 0

    lax.fori_loop(1, max(tree.steps() for tree in trees), body, 0)
    for tree in trees:
        tree.finish()


def spread_count(line, wide):
    return (9 if wide else 7) * line, (8 if wide else 4) * line


def rows_at(ref, index, size):
    return ref.at[pl.ds(pl.multiple_of(index * size, 16), size)]


def columns_at(ref, index, size):
    return ref.at[:, pl.ds(pl.multiple_of(index * size, LANES), size)]


def norm_rows(target, source, gain):
    def body(step, _):
        rows = pl.ds(pl.multiple_of(step * 16, 16), 16)
        value = source[rows, :].astype(jnp.float32)
        target[rows, :] = rms_scale(value, gain[...].astype(jnp.float32)).astype(target.dtype)
        return 0

    lax.fori_loop(0, target.shape[0] // 16, body, 0)


def turned_heads(value, gain, cosine, sine):
    normed = rms_scale(value, gain)
    return normed * cosine + pltpu.roll(normed, normed.shape[-1] // 2, 1) * sine


def visible_blocks(length, group):
    blocks = []
    for start in range(0, length, BLOCK):
        stop = min(start + BLOCK, length)
        heads = max(1, BLOCK // (stop - start))
        while group % heads:
            heads -= 1
        blocks.append((start, stop, stop, heads))
    return blocks


def softmax(scores):
    raised = jnp.exp(scores - jnp.max(scores, axis=0, keepdims=True))
    return raised * (1.0 / jnp.sum(raised, axis=0, keepdims=True))


def for_heads(low, high, heads, body):
    turns = 2 if heads == 1 and (high - low) % 2 == 0 else 1

    def turn(step, _):
        for i in range(turns):
            body(low + (step * turns + i) * heads)
        return 0

    count = (high - low) // (heads * turns)
    if count == 1:
        turn(0, 0)
    else:
        lax.fori_loop(0, count, turn, 0)


def head_columns(head, features):
    return pl.ds(pl.multiple_of(head * features, LANES), features)


def forward_kernel(
    line,
    heads,
    kv_heads,
    tokens_ref,
    cot_ref,
    in_ref,
    out_ref,
    picks_ref,
    gain1_ref,
    gain2_ref,
    query_gain_ref,
    key_gain_ref,
    cosine_ref,
    sine_ref,
    cot_all,
    in_all,
    out_all,
    picks_all,
    normed_all,
    projected_all,
    context_all,
    hidden_all,
    second_all,
    in_w,
    out_w,
    tokens,
    normed,
    projected,
    context,
    queries,
    keys,
    values,
    mixed,
    mixed_other,
    hidden,
    second,
    narrow_send,
    narrow_receive,
    cot_send,
    cot_receive,
    cot_late_send,
    cot_late_receive,
    cot_local,
    local,
    token_send,
    token_receive,
    mixed_send,
    mixed_receive,
    save_sem,
):
    cot_semaphores = (cot_send, cot_receive, cot_late_send, cot_late_receive, cot_local)
    batch, half, width = tokens_ref.shape
    length = 2 * half
    depth, out_width = in_ref.shape[0], out_ref.shape[1]
    features = query_gain_ref.shape[1]
    narrow = Spot(line, False)
    spot = Spot(line, True, turned=False)
    x = spot.x
    spot.greet()
    slots = [
        (picks_ref, lambda block, side: picks_all.at[block]),
        (in_ref, lambda block, side: rows_at(in_w, block, depth)),
        (out_ref, lambda block, side: columns_at(out_w, block, out_width)),
    ]
    weights = [
        Spread(narrow, source, slot, narrow_send.at[i], narrow_receive.at[i], local.at[i])
        for i, (source, slot) in enumerate(slots)
    ]
    cots = []
    for i in range(batch):
        place = lambda block, start, size, i=i: cot_all.at[
            i, block, pl.ds(pl.multiple_of(start, 16), size)
        ]
        cots += rows_spread(spot, cot_ref.at[i], place, half, cot_semaphores, i)
    early, late = weights[:2], weights[2]
    for tree in early:
        tree.begin()

    def token_copies(i):
        place = rows_at(tokens.at[i], x, half)
        return (
            pltpu.make_async_copy(tokens_ref.at[i], place, local.at[3 + i]),
            spot.send(tokens_ref.at[i], place, token_send.at[i], token_receive.at[i], CROSS),
        )

    for i in range(batch):
        for copy in token_copies(i):
            copy.start()
    for tree in cots:
        tree.begin()

    first_cots, other_cots = cots[:2], cots[2:]

    def steps(step, _):
        for tree in early + first_cots:
            tree.step(step)
        return 0

    lax.fori_loop(1, late.steps(), steps, 0)
    late.begin()
    for i in range(batch):
        mine, other = token_copies(i)
        mine.wait()
        other.wait_send()
        place = rows_at(tokens.at[i], 1 - x, half)
        spot.send(place, place, token_send.at[i], token_receive.at[i], CROSS).wait_recv()
    for i in range(batch):
        norm_rows(normed.at[i], tokens.at[i], gain1_ref)
    for tree in early:
        tree.finish()

    def save(source, target, index):
        return pltpu.make_async_copy(source, target, save_sem.at[index])

    saves = [save(in_w, in_all, 0), save(out_w, out_all, 1)]
    saves[0].start()

    def project(i, start, stop):
        for at in range(start, stop, CHUNK):
            projected[i, :, at : at + CHUNK] = jnp.dot(
                normed[i], in_w[:, at : at + CHUNK], preferred_element_type=jnp.float32
            )

    scale = features ** (-0.5)

    group = heads // kv_heads

    def prepare_keys(i):
        base = heads * features
        for head in range(kv_heads):
            at = base + head * features
            keys[head] = turned_heads(
                projected[i, :, at : at + features],
                key_gain_ref[...].astype(jnp.float32),
                cosine_ref[...],
                sine_ref[...],
            ).astype(jnp.bfloat16)
            at = base + (kv_heads + head) * features
            values[head] = projected[i, :, at : at + features].astype(jnp.bfloat16)

    def prepare_queries(i, shared):
        def prepare(member):
            columns = head_columns(shared * group + member, features)
            queries[member] = turned_heads(
                projected[i, :, columns], query_gain_ref[...].astype(jnp.float32), cosine_ref[...], sine_ref[...]
            ).astype(jnp.bfloat16)

        for_heads(0, group, 1, prepare)

    def attend(i, shared, start, stop, seen, at_once, low, high):
        count = stop - start

        def block(member):
            query = queries[pl.ds(member, at_once), start:stop, :].reshape(-1, features)
            scores = lax.dot_general(
                keys[shared, :seen, :],
                query,
                TRANSPOSED_RIGHT,
                preferred_element_type=jnp.float32,
            )
            rows = lax.dot_general(
                softmax(scores * scale).astype(jnp.bfloat16),
                values[shared, :seen, :],
                TRANSPOSED_LEFT,
                preferred_element_type=jnp.float32,
            ).astype(jnp.bfloat16)
            for j in range(at_once):
                columns = head_columns(shared * group + member + j, features)
                context[i, start:stop, columns] = rows[j * count : (j + 1) * count]

        for_heads(low, high, at_once, block)

    def mixed_copy(i):
        return spot.send(
            rows_at(mixed.at[i], 1 - x, half),
            mixed_other.at[i],
            mixed_send.at[i],
            mixed_receive.at[i],
            CROSS,
        )

    def mix(i, start, stop):
        for at in range(start, stop, CHUNK):
            mixed[i, :, at : at + CHUNK] = jnp.dot(
                context[i], out_w[:, at : at + CHUNK], preferred_element_type=jnp.float32
            ).astype(jnp.bfloat16)
        if stop == width:
            mixed_copy(i).start()

    def close(i):
        mixed_copy(i).wait()
        add_rows(
            hidden.at[i],
            [rows_at(tokens.at[i], x, half), rows_at(mixed.at[i], x, half), mixed_other.at[i]],
        )
        norm_rows(second.at[i], hidden.at[i], gain2_ref)

    def late_done():
        late.finish()
        saves[1].start()

    def steps_of(trees, low, high):
        return [
            functools.partial(tree.step, step)
            for step in range(low, high)
            for tree in trees
            if step < tree.steps()
        ]

    def mingle(work, trees):
        for index, piece in enumerate(work):
            piece()
            for step in trees[index * len(trees) // len(work) : (index + 1) * len(trees) // len(work)]:
                step()

    in_width = in_w.shape[1]
    parts = lambda size: [(at, min(at + 2 * CHUNK, size)) for at in range(0, size, 2 * CHUNK)]
    opening, middle, closing = [], [], []
    for i in range(batch):
        opening += [functools.partial(project, i, *part) for part in parts(in_width)]
        middle.append(functools.partial(prepare_keys, i))
        for shared in range(kv_heads):
            middle.append(functools.partial(prepare_queries, i, shared))
            for start, stop, seen, at_once in visible_blocks(length, group):
                share = max(at_once, group // 2)
                for low in range(0, group, share):
                    middle.append(
                        functools.partial(
                            attend, i, shared, start, stop, seen, at_once, low, low + share
                        )
                    )
        closing += [functools.partial(mix, i, *part) for part in parts(width)]
    closing += [functools.partial(close, i) for i in range(batch)]
    last = cots[0].steps()
    mingle(opening, steps_of([late] + other_cots, 1, late.steps()))
    mingle(middle, steps_of(first_cots, late.steps(), last))
    late_done()
    mingle(closing, steps_of(other_cots, late.steps(), last))

    saves += [
        save(source, target, 2 + i)
        for i, (source, target) in enumerate(
            [
                (normed, normed_all),
                (projected, projected_all),
                (context, context_all),
                (hidden, hidden_all),
                (second, second_all),
            ]
        )
    ]
    for copy in saves[2:]:
        copy.start()
    for tree in cots:
        tree.finish()
    for copy in saves:
        copy.wait()


def run_forward(tokens, cot, weight_in, weight_out, picks, gains, tables, fsdp_count, kv_heads):
    line = fsdp_count // PLANE
    batch, half, width = tokens.shape
    length = 2 * half
    features = gains[2].shape[1]
    heads = weight_out.shape[0] // features
    in_shape = (weight_in.shape[0] * fsdp_count, weight_in.shape[1])
    out_shape = (weight_out.shape[0], weight_out.shape[1] * fsdp_count)
    narrow = spread_count(line, False)
    anywhere = pl.BlockSpec(memory_space=pl.ANY)
    inside = pl.BlockSpec(memory_space=pltpu.VMEM)
    shape = lambda dims, kind=jnp.bfloat16: jax.ShapeDtypeStruct(dims, kind)
    vmem = lambda *dims: pltpu.VMEM(dims, jnp.bfloat16)
    sem = lambda *dims: pltpu.SemaphoreType.DMA(dims)
    kept = (
        ((batch, length, width), jnp.bfloat16),
        ((batch, length, weight_in.shape[1]), jnp.float32),
        ((batch, length, heads * features), jnp.bfloat16),
        ((batch, half, width), jnp.float32),
        ((batch, half, width), jnp.bfloat16),
    )
    return pl.pallas_call(
        functools.partial(forward_kernel, line, heads, kv_heads),
        out_shape=(
            shape((batch, fsdp_count, length, width)),
            shape(in_shape),
            shape(out_shape),
            shape((fsdp_count, *picks.shape), picks.dtype),
            *(shape(*one) for one in kept),
        ),
        in_specs=[anywhere] * 5 + [inside] * 6,
        out_specs=(anywhere,) * 9,
        scratch_shapes=[
            vmem(*in_shape),
            vmem(*out_shape),
            vmem(batch, length, width),
            *(pltpu.VMEM(*one) for one in kept[:3]),
            vmem(heads // kv_heads, length, features),
            vmem(kv_heads, length, features),
            vmem(kv_heads, length, features),
            vmem(batch, length, width),
            vmem(batch, half, width),
            *(pltpu.VMEM(*one) for one in kept[3:]),
            sem(3, narrow[0]),
            sem(3, narrow[1]),
            *rows_semaphores(batch, line),
            sem(3 + batch),
            sem(batch),
            sem(batch),
            sem(batch),
            sem(batch),
            sem(7),
        ],
        compiler_params=pltpu.CompilerParams(
            collective_id=1, has_side_effects=True, vmem_limit_bytes=60 * MIB
        ),
    )(tokens, cot, weight_in, weight_out, picks, *gains, *tables)


def add_rows(target, sources):
    def body(step, _):
        rows = pl.ds(pl.multiple_of(step * 16, 16), 16)
        total = sources[0][rows, :].astype(jnp.float32)
        for source in sources[1:]:
            total = total + source[rows, :].astype(jnp.float32)
        target[rows, :] = total.astype(target.dtype)
        return 0

    lax.fori_loop(0, target.shape[0] // 16, body, 0)


class Collect:
    def __init__(self, spot, part, total, cores, firsts, rights, lefts, send, receive):
        self.spot = spot
        self.part = part
        self.total = total
        self.places = {CORE: cores, FIRST: firsts, RIGHT: rights, LEFT: lefts}
        line = spot.line
        self.base = {CORE: 0, FIRST: 2 * line, RIGHT: 3 * line, LEFT: 4 * line}
        self.sends = send
        self.receives = receive

    def own(self, first, z):
        return self.part(*self.spot.block(self.spot.core, first, 0, z))

    def copy(self, kind, first, z):
        spot = self.spot
        number = first * spot.line + z if kind == CORE else z
        source = self.part(*spot.block(1 - spot.core, first, 0, z)) if kind == CORE else self.own(first, z)
        at = self.base[kind] + number
        return spot.send(
            source, self.places[kind].at[number], self.sends.at[at], self.receives.at[at], kind
        )

    def arrived(self, kind, number):
        place = self.places[kind].at[number]
        at = self.base[kind] + number
        self.spot.send(place, place, self.sends.at[0], self.receives.at[at], CORE).wait_recv()
        return place

    def begin(self, z):
        for first in (1, 0):
            self.copy(CORE, first, z).start()

    def to_first(self, z):
        add_rows(self.own(1, z), [self.own(1, z), self.arrived(CORE, self.spot.line + z)])
        self.copy(FIRST, 1, z).start()

    def summands(self, z):
        return [self.own(0, z), self.arrived(CORE, z), self.arrived(FIRST, z)]

    def cross(self):
        for step in reversed(range(self.spot.line)):
            for zz, valid in self.spot.order(step):
                when(valid, functools.partial(self.to_first, zz))

    def onward(self, kind, zz):
        spot = self.spot
        sources = self.summands(zz)
        target = self.own(0, zz)
        behind = spot.z > 0 if kind == RIGHT else spot.z + 1 < spot.line
        when(behind, lambda: add_rows(target, sources + [self.arrived(kind, zz)]))
        when(jnp.logical_not(behind), lambda: add_rows(target, sources))
        self.copy(kind, 0, zz).start()

    def last(self):
        z, line = self.spot.z, self.spot.line
        sources = self.summands(z)

        def end(kinds):
            add_rows(self.total, sources + [self.arrived(kind, z) for kind in kinds])

        when(z == 0, lambda: end([LEFT]))
        when(z == line - 1, lambda: end([RIGHT]))
        when(jnp.logical_and(z > 0, z < line - 1), lambda: end([RIGHT, LEFT]))

    def finish(self):
        spot = self.spot
        for zz in range(spot.line):
            for first in (0, 1):
                self.copy(CORE, first, zz).wait_send()
            self.copy(FIRST, 1, zz).wait_send()
            when(zz > spot.z, lambda: self.copy(RIGHT, 0, zz).wait_send())
            when(zz < spot.z, lambda: self.copy(LEFT, 0, zz).wait_send())

    def tasks(self):
        spot = self.spot
        work = []
        for step in reversed(range(1, spot.line)):
            for kind, (zz, valid) in zip((LEFT, RIGHT), spot.order(step)):
                action = functools.partial(self.onward, kind, zz)
                work.append(functools.partial(when, valid, action))
        return work + [self.last, self.finish]


def collect_scratch(line, shape):
    counts = (2 * line, line, line, line)
    return [pltpu.VMEM((count, *shape), jnp.bfloat16) for count in counts] + [
        pltpu.SemaphoreType.DMA((5 * line,)),
        pltpu.SemaphoreType.DMA((5 * line,)),
    ]


BOXES = 6


def plane_in_turn(line, group):
    turn = lax.rem(group, line)
    step = lax.div(turn, 2)
    return jnp.where(lax.rem(turn, 2) == 0, step, line - 1 - step)


class Sums:
    def __init__(self, spot, parts, cores, places, inbox, outbox, semaphores, plane, inside, ready, done, turns):
        self.spot = spot
        self.parts = parts
        self.cores = cores
        self.seconds, self.firsts, self.ends = places
        self.inbox = inbox
        self.outbox = outbox
        (
            self.inbox_sem,
            self.outbox_sem,
            self.second_receive,
            self.first_receive,
            self.end_receive,
        ) = semaphores
        self.plane = plane
        self.inside = inside
        self.ready = ready
        self.done = done
        self.turns = turns

    def second_slot(self, turn, first):
        return turn * 2 + first

    def first_slot(self, turn):
        return 2 * self.turns + turn

    def end_slot(self, turn, kind):
        return 3 * self.turns + turn * 2 + kind

    def free(self, unit, turn, first):
        pass

    def second_send(self, unit, turn, first):
        slot = self.second_slot(turn, first)
        return self.spot.send(
            self.outbox.at[slot],
            self.seconds.at[unit, first],
            self.outbox_sem.at[slot],
            self.second_receive.at[unit, first],
            SECOND,
        )

    def first_send(self, unit, turn):
        slot = self.first_slot(turn)
        return self.spot.send(
            self.outbox.at[slot],
            self.firsts.at[unit],
            self.outbox_sem.at[slot],
            self.first_receive.at[unit],
            FIRST,
        )

    def end_send(self, unit, turn, kind):
        slot = self.end_slot(turn, kind)
        return self.spot.send(
            self.outbox.at[slot],
            self.ends.at[unit, kind],
            self.outbox_sem.at[slot],
            self.end_receive.at[unit, kind],
            kind,
        )

    def received(self, place, semaphore):
        self.spot.send(place, place, self.outbox_sem.at[0], semaphore, CORE).wait_recv()

    def sources(self, unit, first, second):
        y, x = self.spot.side(self.spot.core, first, second)
        half = self.inbox.shape[1]
        return [rows_at(self.parts(unit, y), x, half), rows_at(self.cores(unit, y), x, half)]

    def summands(self, unit):
        return self.sources(unit, 0, 0) + [self.seconds.at[unit, 0], self.firsts.at[unit]]

    def load(self, source, slot):
        return pltpu.make_async_copy(source, self.inbox.at[slot], self.inbox_sem.at[slot])

    def add(self, target, base, numbers):
        add_rows(target, [self.inbox.at[base + i] for i in numbers])

    def end_roles(self, half_step, delay):
        z, line = self.spot.z, self.spot.line
        unit = half_step - 3 - delay
        valid = self.inside(unit)
        plane = self.plane(unit)
        right = jnp.logical_and(valid, jnp.logical_and(z < plane, delay == z))
        left = jnp.logical_and(valid, jnp.logical_and(z > plane, delay == line - 1 - z))
        last = jnp.logical_and(
            valid,
            jnp.logical_and(z == plane, delay == jnp.maximum(plane, line - 1 - plane)),
        )
        return unit, right, left, last

    def end_task(self, half_step, delay, parity):
        z, line = self.spot.z, self.spot.line
        turn = (parity - 3 - delay) % self.turns
        unit, right, left, last = self.end_roles(half_step, delay)
        some = jnp.logical_or(right, jnp.logical_or(left, last))
        from_left = jnp.logical_and(jnp.logical_or(right, last), z > 0)
        from_right = jnp.logical_and(jnp.logical_or(left, last), z + 1 < line)
        present = ((RIGHT, from_left), (LEFT, from_right))

        def fetch(base):
            def action():
                self.received(self.seconds.at[unit, 0], self.second_receive.at[unit, 0])
                self.received(self.firsts.at[unit], self.first_receive.at[unit])
                for i, source in enumerate(self.summands(unit)):
                    self.load(source, base + i).start()
                for kind, there in present:

                    def arrive():
                        self.received(self.ends.at[unit, kind], self.end_receive.at[unit, kind])
                        self.load(self.ends.at[unit, kind], base + 4 + kind).start()

                    when(there, arrive)

            when(some, action)

        def add(base):
            def action():
                for i, source in enumerate(self.summands(unit)):
                    self.load(source, base + i).wait()
                for kind, there in present:
                    when(there, lambda: self.load(self.ends.at[unit, kind], base + 4 + kind).wait())
                numbers = list(range(4))
                for kind, chosen, behind in ((RIGHT, right, z > 0), (LEFT, left, z + 1 < line)):

                    def onward():
                        target = self.outbox.at[self.end_slot(turn, kind)]
                        self.free(unit, turn, 0)
                        when(behind, lambda: self.add(target, base, numbers + [4 + kind]))
                        when(jnp.logical_not(behind), lambda: self.add(target, base, numbers))
                        self.end_send(unit, turn, kind).start()

                    when(chosen, onward)

                def finish():
                    def into(target):
                        both = jnp.logical_and(from_left, from_right)
                        when(both, lambda: self.add(target, base, numbers + [4, 5]))
                        for kind, there in present:
                            when(
                                jnp.logical_and(there, jnp.logical_not(both)),
                                lambda: self.add(target, base, numbers + [4 + kind]),
                            )

                    self.done(unit, turn, into)

                when(last, finish)

            when(some, action)

        return fetch, add

    def retire(self, half_step, parity):
        before = half_step - self.turns
        now, then = (parity - 1) % self.turns, (parity - 2) % self.turns
        when(
            self.inside(before - 1),
            lambda: [self.second_send(before - 1, now, first).wait_send() for first in range(2)],
        )
        when(self.inside(before - 2), lambda: self.first_send(before - 2, then).wait_send())
        for delay in range(self.spot.line):
            if self.inside(before - 3 - delay) is False:
                continue
            unit, right, left, _ = self.end_roles(before, delay)
            turn = (parity - 3 - delay) % self.turns
            when(right, lambda: self.end_send(unit, turn, RIGHT).wait_send())
            when(left, lambda: self.end_send(unit, turn, LEFT).wait_send())

    def simple_task(self, valid, ready, inputs, slot, send, free=lambda: None):
        def fetch(base):
            ready()

            def action():
                for i, source in enumerate(inputs()):
                    self.load(source, base + i).start()

            when(valid, action)

        def add(base):
            def action():
                refs = inputs()
                for i, source in enumerate(refs):
                    self.load(source, base + i).wait()
                free()
                self.add(self.outbox.at[slot], base, range(len(refs)))
                send().start()

            when(valid, action)

        return fetch, add

    def tasks(self, half_step, parity):
        one, two = half_step - 1, half_step - 2
        now, then = (parity - 1) % self.turns, (parity - 2) % self.turns
        tasks = [
            self.second_task(one, now, 1, functools.partial(self.ready, one)),
            self.second_task(one, now, 0, lambda: None),
            self.first_task(two, then),
        ]
        for delay in range(self.spot.line):
            if self.inside(half_step - 3 - delay) is not False:
                tasks.append(self.end_task(half_step, delay, parity))
        return tasks

    def second_task(self, unit, turn, first, ready):
        return self.simple_task(
            self.inside(unit),
            ready,
            lambda: self.sources(unit, first, 1),
            self.second_slot(turn, first),
            lambda: self.second_send(unit, turn, first),
        )

    def first_task(self, unit, turn):
        arrive = lambda: self.received(self.seconds.at[unit, 1], self.second_receive.at[unit, 1])

        def send():
            return self.first_send(unit, turn)

        return self.simple_task(
            self.inside(unit),
            lambda: when(self.inside(unit), arrive),
            lambda: self.sources(unit, 1, 0) + [self.seconds.at[unit, 1]],
            self.first_slot(turn),
            send,
            lambda: self.free(unit, turn, 1),
        )

    def weave(self, tasks, pieces):
        buffers = self.inbox.shape[0] // BOXES
        if buffers > 1:
            tasks[0][0](0)
        for index, (fetch, add) in enumerate(tasks):
            if buffers == 1:
                fetch(0)
            elif index + 1 < len(tasks):
                tasks[index + 1][0]((index + 1) % 2 * BOXES)
            share = -(-len(pieces) // (len(tasks) - index))
            for piece in pieces[:share]:
                piece()
            pieces = pieces[share:]
            add(index % buffers * BOXES)

    def half_steps(self, units):
        return units + self.spot.line + 2


class ReadySums(Sums):
    def first_slot(self, turn):
        return turn * 2 + 1

    def end_slot(self, turn, kind):
        return turn * 2

    def free(self, unit, turn, first):
        self.second_send(unit, turn, first).wait_send()

    def stages(self, units):
        seconds = [
            self.second_task(unit, unit, first, lambda: None)
            for first in (1, 0)
            for unit in range(units)
        ]
        firsts = [self.first_task(unit, unit) for unit in range(units)]
        ends = []
        for delay in range(self.spot.line):
            for unit in range(units):
                half_step = unit + 3 + delay
                ends.append(self.end_task(half_step, delay, half_step))
        return seconds, firsts, ends

    def finish(self, units):
        for unit in range(units):
            self.first_send(unit, unit).wait_send()
            plane, z = self.plane(unit), self.spot.z
            when(plane > z, lambda: self.end_send(unit, unit, RIGHT).wait_send())
            when(plane < z, lambda: self.end_send(unit, unit, LEFT).wait_send())
            when(plane == z, lambda: self.free(unit, unit, 0))


def norm_back(value, grads, gain):
    scale = lax.rsqrt(jnp.mean(value * value, axis=-1, keepdims=True) + EPSILON)
    unit = value * scale
    scaled = grads * gain
    back = scale * (scaled - unit * jnp.mean(scaled * unit, axis=-1, keepdims=True))
    return back, grads * unit


def backward_kernel(
    line,
    heads,
    kv_heads,
    cot_ref,
    totals_ref,
    hidden_ref,
    projected_ref,
    context_ref,
    in_ref,
    out_ref,
    tokens_ref,
    part_ref,
    cores_ref,
    gain1_ref,
    gain2_ref,
    query_gain_ref,
    key_gain_ref,
    cosine_ref,
    sine_ref,
    block_out,
    input_grad,
    grads_all,
    out_total,
    gain_grads,
    seconds,
    middle,
    ends,
    elements,
    cots,
    tokens,
    kept,
    result,
    context,
    hidden_grads,
    context_grads,
    grads,
    normed_other,
    weight_rows,
    queries_f,
    shared_f,
    queries,
    query_grads,
    sums,
    out_grads,
    cores,
    firsts,
    rights,
    lefts,
    tree_send,
    tree_receive,
    load_sem,
    row_sem,
    head_sem,
    save_sem,
    hidden_send,
    hidden_receive,
    normed_send,
    normed_receive,
    inbox,
    outbox,
    summed,
    inbox_sem,
    outbox_sem,
    second_receive,
    first_receive,
    end_receive,
):
    batch, half, width = cot_ref.shape
    length = 2 * half
    features = query_gain_ref.shape[1]
    group = heads // kv_heads
    base = heads * features
    out_width = out_total.shape[1]
    narrow, spot = Spot(line, False), Spot(line, True)
    x = spot.x
    scale = features ** (-0.5)
    normed_grads = context_grads

    def load(source, target, index):
        return pltpu.make_async_copy(source, target, load_sem.at[index])

    def element_loads(i):
        copies = [
            load(hidden_ref.at[i], elements.at[0], 0),
            load(totals_ref.at[i, BACK], elements.at[1], 1),
        ]
        if i:
            copies.append(load(totals_ref.at[i, OUTPUT], elements.at[2], 2))
        return copies

    first_loads = [load(cot_ref, cots, 3), load(tokens_ref, tokens, 4)] + [
        load(context_ref.at[i], rows_at(context, i, length), 5 + i) for i in range(batch)
    ]
    for copy in element_loads(0) + first_loads:
        copy.start()

    def weight_load(ref, step):
        slot = step % 2
        return pltpu.make_async_copy(
            rows_at(ref, step, CHUNK),
            weight_rows.at[slot, :, pl.ds(0, ref.shape[1])],
            row_sem.at[slot],
        )

    out_steps, in_steps = out_ref.shape[0] // CHUNK, in_ref.shape[0] // CHUNK
    for step in range(2):
        weight_load(out_ref, step).start()
    gain_grads[...] = jnp.zeros_like(gain_grads)
    spot.greet()
    for copy in first_loads:
        copy.wait()

    def result_save(i, target):
        return pltpu.make_async_copy(result.at[i], target.at[i], save_sem.at[i])

    def half_copy(ref, i, side):
        return ref.at[pl.ds(pl.multiple_of(i * length + side * half, 16), half), pl.ds(0, width)]

    def hidden_copy(i):
        place = half_copy(hidden_grads, i, x)
        return spot.send(place, place, hidden_send.at[i], hidden_receive.at[i], CROSS)

    def element_rows(i):
        for copy in element_loads(i):
            copy.wait()

        def elementwise(step, _):
            rows = pl.ds(pl.multiple_of(step * 16, 16), 16)
            value = elements[0, rows, :]
            if i:
                result[i, rows, :] = (value + elements[2, rows, :]).astype(jnp.bfloat16)
            back, gain_rows = norm_back(
                value, elements[1, rows, :], gain2_ref[...].astype(jnp.float32)
            )
            gain_grads[1:2, :] += jnp.sum(gain_rows, axis=0, keepdims=True)
            total = cots[i, rows, :].astype(jnp.float32) + back
            kept[i, rows, :] = total
            place = pl.ds(pl.multiple_of(i * length + x * half + step * 16, 16), 16)
            hidden_grads[place, :] = total.astype(jnp.bfloat16)
            return 0

        lax.fori_loop(0, half // 16, elementwise, 0)
        hidden_copy(i).start()
        if i:
            result_save(i, block_out).start()
        if i + 1 < batch:
            for copy in element_loads(i + 1):
                copy.start()

    def hidden_done():
        load(hidden_ref.at[0], elements.at[0], 0).start()
        for i in range(batch):
            hidden_copy(i).wait_send()
            place = half_copy(hidden_grads, i, 1 - x)
            spot.send(place, place, hidden_send.at[i], hidden_receive.at[i], CROSS).wait_recv()

    def context_step(step):
        weight_load(out_ref, step).wait()
        columns = slice(step * CHUNK, (step + 1) * CHUNK)
        context_grads[:, columns] = lax.dot_general(
            hidden_grads[...],
            weight_rows[step % 2, :, :width],
            TRANSPOSED_RIGHT,
            preferred_element_type=jnp.float32,
        ).astype(jnp.bfloat16)
        if step + 2 < out_steps:
            weight_load(out_ref, step + 2).start()

    def out_step(step):
        columns = slice(step * CHUNK, (step + 1) * CHUNK)
        for start in range(0, width, CHUNK):
            out_grads[columns, start : start + CHUNK] = lax.dot_general(
                context[:, columns],
                hidden_grads[:, start : start + CHUNK],
                TRANSPOSED_LEFT,
                preferred_element_type=jnp.float32,
            ).astype(jnp.bfloat16)

    tree = Collect(
        narrow,
        lambda block, side: columns_at(out_grads, block, out_width),
        out_total,
        cores,
        firsts,
        rights,
        lefts,
        tree_send,
        tree_receive,
    )

    def in_start():
        for step in range(2):
            weight_load(in_ref, step).start()

    def tree_start():
        for z in range(line):
            tree.begin(z)
        for copy in head_loads(0):
            copy.start()

    def turns():
        return [(i, shared) for i in range(batch) for shared in range(kv_heads)]

    def head_loads(index):
        i, shared = turns()[index]
        slot = index % 2
        return [
            pltpu.make_async_copy(
                projected_ref.at[i, :, pl.ds(shared * group * features, group * features)],
                queries_f.at[slot],
                head_sem.at[slot, 0],
            )
        ] + [
            pltpu.make_async_copy(
                projected_ref.at[i, :, pl.ds(base + (shared + j * kv_heads) * features, features)],
                shared_f.at[slot, j],
                head_sem.at[slot, 1 + j],
            )
            for j in range(2)
        ]

    def turn_back(grads_in):
        return grads_in * cosine_ref[...] + pltpu.roll(
            grads_in * sine_ref[...], features // 2, 1
        )

    query_gain = lambda: query_gain_ref[...].astype(jnp.float32)
    key_gain = lambda: key_gain_ref[...].astype(jnp.float32)

    def attend_pieces(index):
        i, shared = turns()[index]
        slot = index % 2
        top = i * length

        def columns_of(member):
            return pl.ds(pl.multiple_of(member * features, LANES), features)

        def prepare():
            for copy in head_loads(index):
                copy.wait()
            if index + 1 < len(turns()):
                for copy in head_loads(index + 1):
                    copy.start()
            queries[group] = turned_heads(
                shared_f[slot, 0], key_gain(), cosine_ref[...], sine_ref[...]
            ).astype(jnp.bfloat16)
            queries[group + 1] = shared_f[slot, 1].astype(jnp.bfloat16)
            sums[...] = jnp.zeros_like(sums)

            def one(member):
                queries[member] = turned_heads(
                    queries_f[slot, :, columns_of(member)],
                    query_gain(),
                    cosine_ref[...],
                    sine_ref[...],
                ).astype(jnp.bfloat16)

            for_heads(0, group, 1, one)

        def rows_block(start, stop, seen, at_once, low, high):
            count = stop - start

            def block(member):
                query = queries[pl.ds(member, at_once), start:stop, :].reshape(-1, features)
                keys, values = queries[group, :seen, :], queries[group + 1, :seen, :]
                out_grad = jnp.concatenate(
                    [
                        context_grads[
                            top + start : top + stop,
                            head_columns(shared * group + member + j, features),
                        ]
                        for j in range(at_once)
                    ],
                    axis=0,
                )
                scores = lax.dot_general(
                    keys, query, TRANSPOSED_RIGHT, preferred_element_type=jnp.float32
                )
                shares = softmax(scores * scale)
                share_grads = lax.dot_general(
                    values, out_grad, TRANSPOSED_RIGHT, preferred_element_type=jnp.float32
                )
                sums[1, :seen, :] += jnp.dot(
                    shares.astype(jnp.bfloat16), out_grad, preferred_element_type=jnp.float32
                )
                inner = jnp.sum(shares * share_grads, axis=0, keepdims=True)
                score_grads = (shares * (share_grads - inner)).astype(jnp.bfloat16)
                rows = scale * lax.dot_general(
                    score_grads, keys, TRANSPOSED_LEFT, preferred_element_type=jnp.float32
                )
                query_grads[pl.ds(member, at_once), start:stop, :] = rows.reshape(
                    at_once, count, features
                )
                sums[0, :seen, :] += jnp.dot(
                    score_grads, query, preferred_element_type=jnp.float32
                )

            for_heads(low, high, at_once, block)

        def finish_queries():
            def finish(member):
                back, gain_rows = norm_back(
                    queries_f[slot, :, columns_of(member)],
                    turn_back(query_grads[member]),
                    query_gain(),
                )
                gain_grads[2:3, :features] += jnp.sum(gain_rows, axis=0, keepdims=True)
                grads[top : top + length, head_columns(shared * group + member, features)] = (
                    back.astype(jnp.bfloat16)
                )

            for_heads(0, group, 1, finish)

        def finish_keys():
            back, gain_rows = norm_back(shared_f[slot, 0], turn_back(sums[0] * scale), key_gain())
            gain_grads[3:4, :features] += jnp.sum(gain_rows, axis=0, keepdims=True)
            at = base + shared * features
            grads[top : top + length, at : at + features] = back.astype(jnp.bfloat16)
            at += kv_heads * features
            grads[top : top + length, at : at + features] = sums[1].astype(jnp.bfloat16)

        pieces = [prepare]
        for start, stop, seen, at_once in visible_blocks(length, group):
            share = max(at_once, group // 2)
            for low in range(0, group, share):
                pieces.append(
                    functools.partial(rows_block, start, stop, seen, at_once, low, low + share)
                )
        return pieces + [finish_queries, finish_keys]

    saves = [
        pltpu.make_async_copy(rows_at(grads, i, length), grads_all.at[i], save_sem.at[batch + i])
        for i in range(batch)
    ]

    def normed_step(step):
        weight_load(in_ref, step).wait()
        normed_grads[:, step * CHUNK : (step + 1) * CHUNK] = lax.dot_general(
            grads[...],
            weight_rows[step % 2],
            TRANSPOSED_RIGHT,
            preferred_element_type=jnp.float32,
        ).astype(jnp.bfloat16)
        if step + 2 < in_steps:
            weight_load(in_ref, step + 2).start()

    def normed_copy(i):
        return spot.send(
            half_copy(normed_grads, i, 1 - x),
            normed_other.at[i],
            normed_send.at[i],
            normed_receive.at[i],
            CROSS,
        )

    def input_rows(i):
        normed_copy(i).wait()
        if i:
            result_save(i, block_out).wait()

        def body(step, _):
            rows = pl.ds(pl.multiple_of(step * 16, 16), 16)
            place = pl.ds(pl.multiple_of(i * length + x * half + step * 16, 16), 16)
            total = normed_grads[place, :width].astype(jnp.float32) + normed_other[
                i, rows, :
            ].astype(jnp.float32)
            back, gain_rows = norm_back(
                tokens[i, rows, :].astype(jnp.float32), total, gain1_ref[...].astype(jnp.float32)
            )
            gain_grads[0:1, :] += jnp.sum(gain_rows, axis=0, keepdims=True)
            kept[i, rows, :] = kept[i, rows, :] + back
            return 0

        lax.fori_loop(0, half // 16, body, 0)
        add_rows(result.at[i], [kept.at[i]])
        result_save(i, input_grad).start()

    moved = ReadySums(
        spot,
        lambda unit, y: part_ref.at[2 * unit + OUTPUT, y],
        lambda unit, y: cores_ref.at[2 * unit + OUTPUT, y],
        (seconds, middle, ends),
        inbox,
        outbox,
        (inbox_sem, outbox_sem, second_receive, first_receive, end_receive),
        lambda unit: plane_in_turn(line, unit),
        lambda unit: 0 <= unit < line,
        lambda unit: None,
        lambda unit, turn, into: into(summed),
        line,
    )
    opening = [functools.partial(element_rows, i) for i in range(batch)] + [hidden_done]
    opening += [functools.partial(out_step, step) for step in range(out_steps)]
    opening += [tree_start, functools.partial(context_step, 0), tree.cross]
    opening += [functools.partial(context_step, step) for step in range(1, out_steps)]
    opening.append(in_start)
    attending = [piece for index in range(len(turns())) for piece in attend_pieces(index)]
    closing = attending[len(attending) // 2 :]
    closing += [copy.start for copy in saves]
    closing += [functools.partial(normed_step, step) for step in range(in_steps)]
    closing += [normed_copy(i).start for i in range(batch)]
    closing += [functools.partial(input_rows, i) for i in range(batch)]
    work = tree.tasks()
    woven = []
    for index, piece in enumerate(closing):
        woven += [piece] + work[
            index * len(work) // len(closing) : (index + 1) * len(work) // len(closing)
        ]
    second_tasks, first_tasks, end_tasks = moved.stages(line)
    moved.weave(second_tasks, opening)
    moved.weave(first_tasks, attending[: len(attending) // 2])
    moved.weave(end_tasks, woven)
    moved.finish(line)
    load(hidden_ref.at[0], elements.at[0], 0).wait()
    result_save(0, input_grad).wait()
    add_rows(result.at[0], [elements.at[0], summed])
    result_save(0, block_out).start()
    result_save(0, block_out).wait()
    for i in range(1, batch):
        result_save(i, input_grad).wait()
    for copy in saves:
        copy.wait()


def run_backward(
    cot,
    totals,
    hidden,
    projected,
    context,
    in_full,
    out_full,
    tokens,
    part,
    cores,
    gains,
    tables,
    fsdp_count,
    kv_heads,
):
    line = fsdp_count // PLANE
    batch, half, width = tokens.shape
    length = 2 * half
    features = gains[2].shape[1]
    heads = out_full.shape[0] // features
    group = heads // kv_heads
    in_width, out_depth = in_full.shape[1], out_full.shape[0]
    out_shape = (out_depth, width // fsdp_count)
    anywhere = pl.BlockSpec(memory_space=pl.ANY)
    inside = pl.BlockSpec(memory_space=pltpu.VMEM)
    shape = lambda *dims: jax.ShapeDtypeStruct(dims, jnp.bfloat16)
    vmem = lambda *dims: pltpu.VMEM(dims, jnp.bfloat16)
    wide = lambda *dims: pltpu.VMEM(dims, jnp.float32)
    sem = lambda *dims: pltpu.SemaphoreType.DMA(dims)
    rows = batch * length
    return pl.pallas_call(
        functools.partial(backward_kernel, line, heads, kv_heads),
        out_shape=(
            shape(batch, half, width),
            shape(batch, half, width),
            shape(batch, length, in_width),
            jax.ShapeDtypeStruct(out_shape, jnp.float32),
            jax.ShapeDtypeStruct((8, width), jnp.float32),
            shape(line, 2, half, width),
            shape(line, half, width),
            shape(line, 2, half, width),
        ),
        in_specs=[anywhere] * 10 + [inside] * 6,
        out_specs=(anywhere, anywhere, anywhere, inside, inside, anywhere, anywhere, anywhere),
        scratch_shapes=[
            wide(3, half, width),
            vmem(batch, half, width),
            vmem(batch, half, width),
            wide(batch, half, width),
            vmem(batch, half, width),
            vmem(rows, out_depth),
            vmem(rows, width),
            vmem(rows, max(out_depth, width)),
            vmem(rows, in_width),
            vmem(batch, half, width),
            vmem(2, CHUNK, max(width, in_width)),
            wide(2, length, group * features),
            wide(2, 2, length, features),
            vmem(group + 2, length, features),
            wide(group, length, features),
            wide(2, length, features),
            vmem(out_depth, width),
            *collect_scratch(line, out_shape),
            sem(5 + batch),
            sem(2),
            sem(2, 3),
            sem(2 * batch),
            sem(batch),
            sem(batch),
            sem(batch),
            sem(batch),
            vmem(BOXES, half, width),
            vmem(2 * line, half, width),
            wide(half, width),
            sem(BOXES),
            sem(2 * line),
            sem(line, 2),
            sem(line),
            sem(line, 2),
        ],
        compiler_params=pltpu.CompilerParams(
            collective_id=3, has_side_effects=True, vmem_limit_bytes=62 * MIB
        ),
    )(
        cot,
        totals,
        hidden,
        projected,
        context,
        in_full,
        out_full,
        tokens,
        part,
        cores,
        *gains,
        *tables,
    )[:5]


def gradients_kernel(
    line,
    normed,
    grads,
    gains_ref,
    xe_ref,
    ce_ref,
    act_ref,
    dgate_ref,
    dup_ref,
    in_total,
    gains_all,
    gate_total,
    up_total,
    down_total,
    parts,
    cores,
    firsts,
    rights,
    lefts,
    tree_send,
    tree_receive,
    gain_send,
    gain_receive,
    gain_local,
    wide_rows,
    slim_rows,
    gate_sum,
    up_sum,
    down_sum,
    load_sem,
    save_sem,
):
    narrow, spot = Spot(line, False), Spot(line, True)
    experts, count, _ = xe_ref.shape
    share = wide_rows.shape[1]
    turns = count // share
    pieces = [
        (expert, kind, turn)
        for expert in range(experts)
        for kind in range(2)
        for turn in range(turns)
    ]

    def loads(index):
        expert, kind, turn = pieces[index]
        slot = index % 2
        rows = pl.ds(turn * share, share)
        slim = (dgate_ref, dup_ref) if kind == 0 else (act_ref,)
        return [
            pltpu.make_async_copy(
                (xe_ref, ce_ref)[kind].at[expert, rows], wide_rows.at[slot], load_sem.at[slot, 0]
            )
        ] + [
            pltpu.make_async_copy(
                ref.at[expert, rows], slim_rows.at[slot, i], load_sem.at[slot, 1 + i]
            )
            for i, ref in enumerate(slim)
        ]

    def saves(expert, kind):
        pairs = ((gate_sum, gate_total), (up_sum, up_total))
        if kind:
            return [pltpu.make_async_copy(down_sum, down_total.at[expert], save_sem.at[2])]
        return [
            pltpu.make_async_copy(source, target.at[expert], save_sem.at[i])
            for i, (source, target) in enumerate(pairs)
        ]

    for copy in loads(0):
        copy.start()
    spot.greet()
    gains = Spread(
        spot,
        gains_ref,
        lambda block, half: gains_all.at[block, half],
        gain_send,
        gain_receive,
        gain_local.at[0],
    )
    gains.begin()
    depth, width = in_total.shape
    tree = Collect(
        narrow,
        lambda block, half: rows_at(parts, block, depth),
        in_total,
        cores,
        firsts,
        rights,
        lefts,
        tree_send,
        tree_receive,
    )
    chunk = PLANE * depth

    def plane(step, _):
        z = lax.rem(narrow.z + 1 + step, line)
        columns = pl.ds(pl.multiple_of(z * chunk, LANES), chunk)
        for start in range(0, width, CHUNK):
            parts[pl.ds(pl.multiple_of(z * chunk, 16), chunk), start : start + CHUNK] = (
                lax.dot_general(
                    normed[:, columns],
                    grads[:, start : start + CHUNK],
                    TRANSPOSED_LEFT,
                    preferred_element_type=jnp.float32,
                ).astype(jnp.bfloat16)
            )
        tree.begin(z)
        return 0

    lax.fori_loop(0, line, plane, 0)

    def piece(index):
        expert, kind, turn = pieces[index]
        slot = index % 2
        for copy in loads(index):
            copy.wait()
        if index + 1 < len(pieces):
            for copy in loads(index + 1):
                copy.start()
        if turn == 0 and expert:
            for copy in saves(expert - 1, kind):
                copy.wait()
        size = wide_rows.shape[2] // 4

        def add(target, place, left, right):
            product = lax.dot_general(
                left, right, TRANSPOSED_LEFT, preferred_element_type=jnp.float32
            )
            if turn:
                product = target[place] + product
            target[place] = product

        def part(step, _):
            at = pl.ds(pl.multiple_of(step * size, LANES), size)
            if kind:
                add(down_sum, (slice(None), at), slim_rows[slot, 0], wide_rows[slot, :, at])
            else:
                for i, target in enumerate((gate_sum, up_sum)):
                    add(target, (at, slice(None)), wide_rows[slot, :, at], slim_rows[slot, i])
            return 0

        lax.fori_loop(0, 4, part, 0)
        if turn == turns - 1:
            for copy in saves(expert, kind):
                copy.start()

    tree.cross()
    work = tree.tasks()
    steps = list(range(1, gains.steps()))
    filler = list(range(len(pieces)))
    while work or filler:
        for _ in range(2 if len(filler) > len(work) else 1):
            if filler:
                piece(filler.pop(0))
        if work:
            work.pop(0)()
        if steps:
            gains.step(steps.pop(0))
    gains.finish()
    for copy in saves(experts - 1, 0) + saves(experts - 1, 1):
        copy.wait()


def run_gradients(normed, grads, gains, expert_rows, fsdp_count):
    line = fsdp_count // PLANE
    width = grads.shape[1]
    experts, count, depth = expert_rows[0].shape
    units = expert_rows[2].shape[2]
    share = 2 * CHUNK if count % (2 * CHUNK) == 0 else count // (2 * line)
    shape = (normed.shape[1] // fsdp_count, width)
    sends, receives = spread_count(line, True)
    inside = pl.BlockSpec(memory_space=pltpu.VMEM)
    anywhere = pl.BlockSpec(memory_space=pl.ANY)
    return pl.pallas_call(
        functools.partial(gradients_kernel, line),
        out_shape=(
            jax.ShapeDtypeStruct(shape, jnp.float32),
            jax.ShapeDtypeStruct((fsdp_count, 2, *gains.shape), jnp.float32),
            jax.ShapeDtypeStruct((experts, depth, units), jnp.float32),
            jax.ShapeDtypeStruct((experts, depth, units), jnp.float32),
            jax.ShapeDtypeStruct((experts, units, depth), jnp.float32),
        ),
        in_specs=[inside, inside] + [anywhere] * 6,
        out_specs=(inside,) + (anywhere,) * 4,
        scratch_shapes=[
            pltpu.VMEM((normed.shape[1], width), jnp.bfloat16),
            *collect_scratch(line, shape),
            pltpu.SemaphoreType.DMA((sends,)),
            pltpu.SemaphoreType.DMA((receives,)),
            pltpu.SemaphoreType.DMA((1,)),
            pltpu.VMEM((2, share, depth), jnp.bfloat16),
            pltpu.VMEM((2, 2, share, units), jnp.bfloat16),
            pltpu.VMEM((depth, units), jnp.float32),
            pltpu.VMEM((depth, units), jnp.float32),
            pltpu.VMEM((units, depth), jnp.float32),
            pltpu.SemaphoreType.DMA((2, 3)),
            pltpu.SemaphoreType.DMA((3,)),
        ],
        compiler_params=pltpu.CompilerParams(
            collective_id=4, has_side_effects=True, vmem_limit_bytes=60 * MIB
        ),
    )(normed, grads, gains, *expert_rows)


def experts_kernel(
    line,
    slots,
    own_ref,
    cot_ref,
    info_ref,
    gate_ref,
    up_ref,
    down_ref,
    all_ref,
    total_ref,
    xe_all,
    ce_all,
    act_all,
    dgate_all,
    dup_all,
    part,
    cores,
    seconds,
    firsts,
    ends,
    hidden_w,
    down_w,
    x_rows,
    c_rows,
    xe,
    ce,
    acts,
    dgates,
    dups,
    hidden_grads,
    picks,
    weigh,
    rows,
    stage,
    inbox,
    outbox,
    summed,
    rows_send,
    rows_receive,
    rows_late_send,
    rows_late_receive,
    rows_local,
    load_sem,
    save_sem,
    stage_sem,
    inbox_sem,
    outbox_sem,
    total_sem,
    weight_sem,
    core_receive,
    second_receive,
    first_receive,
    end_receive,
):
    spot = Spot(line, True)
    z, core = spot.z, spot.core
    tree_semaphores = (rows_send, rows_receive, rows_late_send, rows_late_receive, rows_local)
    batch, half, width = own_ref.shape
    length = 2 * half
    units = down_ref.shape[1]
    groups = batch * line
    weights = [
        pltpu.make_async_copy(source, target, weight_sem.at[i])
        for i, (source, target) in enumerate(
            [(down_ref, down_w)]
            + [(gate_ref.at[e], hidden_w.at[e, :, pl.ds(0, units)]) for e in range(2)]
            + [(up_ref.at[e], hidden_w.at[e, :, pl.ds(units, units)]) for e in range(2)]
        )
    ]
    for copy in weights:
        copy.start()
    rows[...] = jnp.zeros_like(rows)
    spot.greet()

    def half_of(ref, index):
        return rows_at(ref, index, half)

    trees = []
    for i in range(batch):
        place = lambda block, start, size, i=i: all_ref.at[
            i, block, pl.ds(pl.multiple_of(start, 16), size)
        ]
        trees.append(rows_spread(spot, own_ref.at[i], place, half, tree_semaphores, i))
    run_trees(trees[0])
    for tree in sum(trees[1:], []):
        tree.begin()
    for copy in weights:
        copy.wait()

    plane_of = functools.partial(plane_in_turn, line)

    def load_group(group, member):
        at = lax.div(group, line)
        sequence = plane_of(group) * PLANE + member
        slot = member % 2
        return [
            pltpu.make_async_copy(all_ref.at[at, sequence], x_rows.at[slot], load_sem.at[0, slot]),
            pltpu.make_async_copy(cot_ref.at[at, sequence], c_rows.at[slot], load_sem.at[1, slot]),
        ]

    def saves(group):
        to = lambda ref, expert: rows_at(ref.at[expert], group, PLANE * slots)
        pairs = ((xe, xe_all), (ce, ce_all), (acts, act_all), (dgates, dgate_all), (dups, dup_all))
        return [
            pltpu.make_async_copy(source.at[expert], to(target, expert), save_sem.at[2 * i + expert])
            for i, (source, target) in enumerate(pairs)
            for expert in range(2)
        ]

    def staged(unit, y, mine):
        slot = y * 2 + mine
        if mine:
            return pltpu.make_async_copy(stage.at[slot], part.at[unit, y], stage_sem.at[slot])
        return spot.send(
            stage.at[slot], cores.at[unit, y], stage_sem.at[slot], core_receive.at[unit, y], CORE
        )

    def combine(unit, y):
        for mine in range(2):
            member = y * 2 + (core if mine else 1 - core)
            for start in range(0, width, CHUNK):
                stage[y * 2 + mine, :, start : start + CHUNK] = lax.dot_general(
                    picks[member],
                    rows[member, :, start : start + CHUNK],
                    TRANSPOSED_LEFT,
                    preferred_element_type=jnp.float32,
                ).astype(jnp.bfloat16)
            staged(unit, y, mine).start()

    def pick(group, member):
        slot = member % 2
        for copy in load_group(group, member):
            copy.wait()
        if member + 1 < PLANE:
            for copy in load_group(group, member + 1):
                copy.start()
        sequence = plane_of(group) * PLANE + member
        info = info_ref[lax.div(group, line) * line * PLANE + sequence]
        places = lax.broadcasted_iota(jnp.int32, (2 * LANES, length), 0)
        lower = places < LANES
        ranks = jnp.where(lower, info[0:1], info[1:2] + float(LANES)).astype(jnp.int32)
        some = jnp.where(lower, info[0:1], info[1:2]) >= 0.0
        hot = jnp.logical_and(ranks == places, some)
        chosen = hot.astype(jnp.float32).astype(jnp.bfloat16)
        picks[member] = chosen
        shares = jnp.where(hot, jnp.where(lower, info[2:3], info[3:4]), 0.0)
        column = jnp.sum(shares, axis=1, keepdims=True)
        here = pl.ds(member * slots, slots)
        for expert in range(2):
            weigh[expert, here, :] = jnp.broadcast_to(
                column[expert * LANES : expert * LANES + slots], (slots, LANES)
            )
        for source, target in ((x_rows, xe), (c_rows, ce)):
            for start in range(0, width, CHUNK):
                selected = jnp.dot(
                    chosen,
                    source[slot, :, start : start + CHUNK],
                    preferred_element_type=jnp.float32,
                ).astype(jnp.bfloat16)
                for expert in range(2):
                    target[expert, here, start : start + CHUNK] = selected[
                        expert * LANES : expert * LANES + slots
                    ]

    def keep(expert, product, start):
        at = pl.ds(expert * LANES, slots)
        for one in range(PLANE):
            rows[one, at, start : start + CHUNK] = product[one * slots : (one + 1) * slots].astype(
                jnp.bfloat16
            )

    def forward(expert):
        hidden = jnp.dot(xe[expert], hidden_w[expert], preferred_element_type=jnp.float32)
        gate, up = hidden[:, :units], hidden[:, units:]
        sigmoid = jax.nn.sigmoid(gate)
        silu = gate * sigmoid
        scale = weigh[expert, :, 0:1]
        acts[expert] = (silu * up * scale).astype(jnp.bfloat16)
        act_grads = scale * lax.dot_general(
            ce[expert], down_w[expert], TRANSPOSED_RIGHT, preferred_element_type=jnp.float32
        )
        gate_grads = (act_grads * up * (sigmoid * (1.0 + gate * (1.0 - sigmoid)))).astype(
            jnp.bfloat16
        )
        up_grads = (act_grads * silu).astype(jnp.bfloat16)
        dgates[expert] = gate_grads
        dups[expert] = up_grads
        hidden_grads[expert, :, :units] = gate_grads
        hidden_grads[expert, :, units:] = up_grads
        for start in range(0, width, CHUNK):
            keep(
                expert,
                jnp.dot(
                    acts[expert],
                    down_w[expert, :, start : start + CHUNK],
                    preferred_element_type=jnp.float32,
                ),
                start,
            )

    def backward(expert):
        for start in range(0, width, CHUNK):
            keep(
                expert,
                lax.dot_general(
                    hidden_grads[expert],
                    hidden_w[expert, start : start + CHUNK, :],
                    TRANSPOSED_RIGHT,
                    preferred_element_type=jnp.float32,
                ),
                start,
            )

    units_all = 2 * groups

    def inside(unit):
        valid = jnp.logical_and(unit >= 0, unit < units_all)
        return jnp.logical_and(valid, jnp.logical_or(unit >= 2 * line, unit % 2 == BACK))

    def ready(unit):
        @pl.when(jnp.logical_and(unit >= 0, unit < units_all))
        def _():
            for y in range(2):
                staged(unit, y, 1).wait()
                staged(unit, y, 0).wait_send()
                place, semaphore = cores.at[unit, y], core_receive.at[unit, y]
                spot.send(place, place, outbox_sem.at[0], semaphore, CORE).wait_recv()

    def done(unit, tensor, into):
        into(summed)
        copy = pltpu.make_async_copy(
            summed, total_ref.at[lax.div(unit, 2 * line), tensor], total_sem.at[0]
        )
        copy.start()
        copy.wait()

    sums = Sums(
        spot,
        lambda unit, y: part.at[unit, y],
        lambda unit, y: cores.at[unit, y],
        (seconds, firsts, ends),
        inbox,
        outbox,
        (inbox_sem, outbox_sem, second_receive, first_receive, end_receive),
        lambda unit: plane_of(lax.div(jnp.maximum(unit, 0), 2)),
        inside,
        ready,
        done,
        2,
    )

    def tree_turn(half_step, last):
        for i in range(1, batch):
            turn = half_step - (i - 1) * 2 * line
            if last:
                when(turn == 2 * line - 1, lambda: [tree.finish() for tree in trees[i]])
            else:
                inner = jnp.logical_and(turn >= 0, turn < 2 * line - 1)
                when(inner, lambda: [tree.step(turn + 1) for tree in trees[i]])

    def begin_pick(group):
        for copy in load_group(group, 0):
            copy.start()

    begin_pick(0)
    for member in range(PLANE):
        pick(0, member)

    def step_body(step, _):
        busy = step < groups
        more = step + 1 < groups
        for parity in range(2):
            half_step = step * 2 + parity
            tree_turn(half_step, False)
            sums.retire(half_step, parity)
            tasks = sums.tasks(half_step, parity)
            pieces = []
            for expert in range(2):
                pieces.append(functools.partial((forward, backward)[parity], expert))
            if parity == 0:
                pieces.append(lambda: [copy.start() for copy in saves(step)])
            for y in range(2):
                pieces.append(functools.partial(combine, half_step, y))
            pieces = [functools.partial(when, busy, piece) for piece in pieces]
            if parity == 1:

                def prepare():
                    for copy in saves(step):
                        copy.wait()
                    begin_pick(step + 1)

                tree_end = functools.partial(tree_turn, half_step, True)
                pieces += [tree_end, functools.partial(when, more, prepare)]
                for member in range(PLANE):
                    pieces.append(
                        functools.partial(when, more, functools.partial(pick, step + 1, member))
                    )
            sums.weave(tasks, pieces)
        return 0

    half_steps = sums.half_steps(units_all)
    lax.fori_loop(0, -(-half_steps // 2), step_body, 0)
    end = -(-half_steps // 2) * 2
    for parity in range(2):
        sums.retire(jnp.int32(end + parity), parity)
    for copy in saves(groups - 1):
        copy.wait()


def run_experts(rows, cot_all, info, w_gate, w_up, w_down, capacity, fsdp_count):
    line = fsdp_count // PLANE
    batch, half, width = rows.shape
    length = 2 * half
    units = w_down.shape[1]
    slots = -(-capacity // 16) * 16
    groups = batch * line
    count = groups * PLANE * slots
    taken = PLANE * slots
    shape = lambda *dims: jax.ShapeDtypeStruct(dims, jnp.bfloat16)
    block = (half, width)
    anywhere = pl.BlockSpec(memory_space=pl.ANY)
    vmem = lambda *dims: pltpu.VMEM(dims, jnp.bfloat16)
    sem = lambda *dims: pltpu.SemaphoreType.DMA(dims)
    return pl.pallas_call(
        functools.partial(experts_kernel, line, slots),
        out_shape=(
            shape(batch, fsdp_count, length, width),
            jax.ShapeDtypeStruct((batch, 2, *block), jnp.float32),
            shape(2, count, width),
            shape(2, count, width),
            shape(2, count, units),
            shape(2, count, units),
            shape(2, count, units),
            shape(2 * groups, 2, length, width),
            shape(2 * groups, 2, length, width),
            shape(2 * groups, 2, *block),
            shape(2 * groups, *block),
            shape(2 * groups, 2, *block),
        ),
        in_specs=[
            anywhere,
            anywhere,
            pl.BlockSpec(memory_space=pltpu.VMEM),
            anywhere,
            anywhere,
            anywhere,
        ],
        out_specs=(anywhere,) * 12,
        scratch_shapes=[
            vmem(2, width, 2 * units),
            vmem(2, units, width),
            vmem(2, length, width),
            vmem(2, length, width),
            vmem(2, taken, width),
            vmem(2, taken, width),
            vmem(2, taken, units),
            vmem(2, taken, units),
            vmem(2, taken, units),
            vmem(2, taken, 2 * units),
            vmem(PLANE, 2 * LANES, length),
            pltpu.VMEM((2, taken, LANES), jnp.float32),
            vmem(PLANE, 2 * LANES, width),
            vmem(PLANE, length, width),
            vmem(12, *block),
            vmem(10, *block),
            pltpu.VMEM(block, jnp.float32),
            *rows_semaphores(batch, line),
            sem(2, 2),
            sem(10),
            sem(PLANE),
            sem(12),
            sem(10),
            sem(1),
            sem(5),
            sem(2 * groups, 2),
            sem(2 * groups, 2),
            sem(2 * groups),
            sem(2 * groups, 2),
        ],
        compiler_params=pltpu.CompilerParams(
            collective_id=2, has_side_effects=True, vmem_limit_bytes=60 * MIB
        ),
    )(rows, cot_all, info, w_gate, w_up, w_down)[1:9]


def packed_picks(routes, gates):
    length = routes.shape[2]
    packed = jnp.concatenate([routes[:, 0].astype(jnp.float32), gates[:, 0]], axis=-1)
    packed = jnp.swapaxes(packed, 1, 2).reshape(-1, length)
    return jnp.pad(packed, ((0, 0), (0, -length % LANES)))


def slot_info(packed, batch, top, length, local_experts):
    fsdp_count = packed.shape[0]
    packed = packed[..., :length].reshape(fsdp_count, batch, 1, 2 * top, length)
    packed = jnp.swapaxes(packed, 0, 1)
    experts = lax.axis_index(FSDP) * local_experts + jnp.arange(local_experts, dtype=jnp.int32)
    same = packed[..., :top, :].astype(jnp.int32) == experts[:, None, None]
    hot = jnp.any(same, axis=3)
    shares = jnp.sum(jnp.where(same, packed[..., top:, :], 0.0), axis=3)
    position = jnp.arange(length)
    upper = (position[:, None] < position[None, :]).astype(jnp.bfloat16)
    rank = jnp.dot(
        hot.astype(jnp.bfloat16).reshape(-1, length), upper, preferred_element_type=jnp.float32
    )
    rank = jnp.where(hot, rank.reshape(hot.shape), -1.0)
    return jnp.concatenate([rank, shares], axis=2).reshape(-1, 2 * local_experts, length)


def gathered_layer(
    tokens,
    cotangent,
    norm1_gain,
    w_query,
    key_projection_weight,
    value_projection_weight,
    query_gain,
    key_gain,
    w_out,
    norm2_gain,
    w_gate,
    w_up,
    w_down,
    routes,
    gates,
):
    batch_count = tokens.shape[0]
    model_width = tokens.shape[3]
    sequence_length = routes.shape[2]
    half_length = tokens.shape[2]
    top_count = routes.shape[3]
    head_features = query_gain.shape[0]
    local_experts = w_gate.shape[0]
    fsdp_count = lax.axis_size(FSDP)
    all_experts = local_experts * fsdp_count
    capacity = 7 * top_count * sequence_length // (6 * all_experts)
    query_width = w_query.shape[1]
    kv_width = key_projection_weight.shape[1]
    kv_heads = kv_width // head_features
    cosine_table, sine_values = rotary_tables(sequence_length, head_features)
    weight_in = jnp.concatenate([w_query, key_projection_weight, value_projection_weight], axis=1)
    half_signs = jnp.where(jnp.arange(head_features) < head_features // 2, -1.0, 1.0)
    tables = (cosine_table[:, 0], sine_values[:, 0] * half_signs)
    gains = [gain[None, :] for gain in (norm1_gain, norm2_gain, query_gain, key_gain)]
    cot_all, in_full, out_full, picks, normed, projected, contexts, hidden, second = run_forward(
        tokens[:, 0],
        cotangent[:, 0],
        weight_in,
        w_out,
        packed_picks(routes, gates),
        gains,
        tables,
        fsdp_count,
        kv_heads,
    )
    info = slot_info(picks, batch_count, top_count, sequence_length, local_experts)
    totals, *expert_rows, part, cores = run_experts(
        second, cot_all, info, w_gate, w_up, w_down, capacity, fsdp_count
    )
    block_out, input_grad, projected_grads, out_sum, gain_grads = run_backward(
        cotangent[:, 0],
        totals,
        hidden,
        projected,
        contexts,
        in_full,
        out_full,
        tokens[:, 0],
        part,
        cores,
        gains,
        tables,
        fsdp_count,
        kv_heads,
    )
    rows = batch_count * sequence_length
    in_sum, gains_all, *expert_grads = run_gradients(
        normed.reshape(rows, -1),
        projected_grads.reshape(rows, -1),
        gain_grads,
        expert_rows,
        fsdp_count,
    )
    gains_sum = jnp.sum(gains_all, axis=(0, 1))
    return (
        block_out[:, None],
        input_grad[:, None],
        gains_sum[0],
        in_sum[:, :query_width],
        in_sum[:, query_width : query_width + kv_width],
        in_sum[:, query_width + kv_width :],
        gains_sum[2, :head_features],
        gains_sum[3, :head_features],
        out_sum,
        gains_sum[1],
        *expert_grads,
    )


def shards(*arrays):
    tokens, routes, w_gate = arrays[0], arrays[13], arrays[10]
    fsdp_count = lax.axis_size(FSDP)
    gathered = fsdp_count * routes.shape[2] * tokens.shape[3] * 2
    fits = gathered <= 24 * MIB and fsdp_count % PLANE == 0 and lax.axis_size(TP) == 2
    if fits and w_gate.shape[0] == 2:
        return gathered_layer(*arrays)
    return exchanged_layer(*arrays)


def solution(mesh):
    in_specs = (
        P(None, "fsdp", "tp", None),
        P(None, "fsdp", "tp", None),
        P(),
        P("fsdp", "tp"),
        P("fsdp", "tp"),
        P("fsdp", "tp"),
        P(),
        P(),
        P("tp", "fsdp"),
        P(),
        P("fsdp", None, "tp"),
        P("fsdp", None, "tp"),
        P("fsdp", "tp", None),
        P(None, "fsdp", None, None),
        P(None, "fsdp", None, None),
    )
    out_specs = (
        P(None, "fsdp", "tp", None),
        P(None, "fsdp", "tp", None),
        P(),
        P("fsdp", "tp"),
        P("fsdp", "tp"),
        P("fsdp", "tp"),
        P(),
        P(),
        P("tp", "fsdp"),
        P(),
        P("fsdp", None, "tp"),
        P("fsdp", None, "tp"),
        P("fsdp", "tp", None),
    )
    return jax.shard_map(shards, mesh=mesh, in_specs=in_specs, out_specs=out_specs, check_vma=False)
```

```python
import functools

import jax
import jax.numpy as jnp
from jax import lax
from jax.experimental import pallas as pl
from jax.experimental.pallas import tpu as pltpu
from jax.sharding import PartitionSpec as P

BLOCK = 256


EPSILON = 1e-06
ROPE_BASE = 1000000.0
MASKED = -1e30
TILE_PICKS = 128


def rms_scale(row_block, gain_row):
    return (
        row_block
        * lax.rsqrt(jnp.mean(row_block * row_block, axis=-1, keepdims=True) + EPSILON)
        * gain_row
    )


def rotary_tables(sequence_length, head_width):
    half_width = head_width // 2
    inverse = ROPE_BASE ** (-2.0 * jnp.arange(half_width, dtype=jnp.float32) / head_width)
    angles = jnp.arange(sequence_length, dtype=jnp.float32)[:, None] * inverse[None, :]
    cosine_table = jnp.concatenate([jnp.cos(angles), jnp.cos(angles)], axis=-1)[:, None, :]
    sine_values = jnp.concatenate([jnp.sin(angles), jnp.sin(angles)], axis=-1)[:, None, :]
    return (cosine_table, sine_values)


def rotate(head_rows, cosine_table, sine_values):
    half_width = head_rows.shape[-1] // 2
    turned = jnp.concatenate([-head_rows[..., half_width:], head_rows[..., :half_width]], axis=-1)
    return head_rows * cosine_table + turned * sine_values


def prepare_heads(projected, gain_row, cosine_table, sine_values):
    return rotate(rms_scale(projected, gain_row), cosine_table, sine_values)


def swiglu(gate_act, up_act):
    return jax.nn.silu(gate_act) * up_act


def slot_tables(route_rows, gate_rows, expert_count, capacity):
    sequence_length = route_rows.shape[0]
    top_count = route_rows.shape[1]
    pick_count = sequence_length * top_count
    tile_count = pick_count // TILE_PICKS
    flat_routes = route_rows.reshape(-1)
    onehot = (flat_routes[:, None] == jnp.arange(expert_count, dtype=jnp.int32)[None, :]).astype(
        jnp.bfloat16
    )
    tiles = onehot.reshape(tile_count, TILE_PICKS, expert_count)
    positions = jnp.arange(TILE_PICKS, dtype=jnp.int32)
    lower = (positions[None, :] < positions[:, None]).astype(jnp.bfloat16)
    within = jnp.einsum("ij,bje->bie", lower, tiles, preferred_element_type=jnp.float32)
    tile_totals = jnp.sum(tiles.astype(jnp.float32), axis=1)
    offsets = jnp.cumsum(tile_totals, axis=0) - tile_totals
    before = within + offsets[:, None, :]
    slot_rank = jnp.sum(before * tiles.astype(jnp.float32), axis=-1).reshape(-1).astype(jnp.int32)
    slot_index = flat_routes * capacity + slot_rank
    pick_ids = jnp.arange(pick_count, dtype=jnp.int32) // top_count
    slot_owner = (
        jnp.full((expert_count * capacity,), sequence_length, jnp.int32)
        .at[slot_index]
        .set(pick_ids)
    )
    slot_weight = (
        jnp.zeros((expert_count * capacity,), jnp.float32).at[slot_index].set(gate_rows.reshape(-1))
    )
    return (slot_index, slot_owner, slot_weight)


def exchanged_layer(
    tokens,
    cotangent,
    norm1_gain,
    w_query,
    key_projection_weight,
    value_projection_weight,
    query_gain,
    key_gain,
    w_out,
    norm2_gain,
    w_gate,
    w_up,
    w_down,
    routes,
    gates,
):
    batch_count = tokens.shape[0]
    model_width = tokens.shape[3]
    sequence_length = routes.shape[2]
    top_count = routes.shape[3]
    head_features = query_gain.shape[0]
    local_experts = w_gate.shape[0]
    fsdp_count = lax.axis_size("fsdp")
    all_experts = local_experts * fsdp_count
    capacity = 7 * top_count * sequence_length // (6 * all_experts)
    query_heads = w_query.shape[1] // head_features
    kv_heads = key_projection_weight.shape[1] // head_features
    group_size = query_heads // kv_heads
    score_scale = head_features ** (-0.5)
    cosine_table, sine_values = rotary_tables(sequence_length, head_features)
    block_ids = jnp.arange(sequence_length, dtype=jnp.int32) // BLOCK
    visible = (block_ids[None, :] <= block_ids[:, None])[None, None]
    first_gain = norm1_gain.astype(jnp.float32)
    second_gain = norm2_gain.astype(jnp.float32)
    query_factor_scale = query_gain.astype(jnp.float32)
    key_scale = key_gain.astype(jnp.float32)
    zero_row = jnp.zeros((1, model_width), jnp.bfloat16)
    buffer_shape = (fsdp_count, local_experts, capacity, model_width)

    def masked_scores(query_fourfold, key_rows):
        raw_scores = (
            jnp.einsum(
                "qcgd,kcd->cgqk", query_fourfold, key_rows, preferred_element_type=jnp.float32
            )
            * score_scale
        )
        return jnp.where(visible, raw_scores, MASKED)

    def prep_heads(projected, gain_row):
        return prepare_heads(projected, gain_row, cosine_table, sine_values)

    gain_sums = (
        jnp.zeros((model_width,), jnp.float32),
        jnp.zeros((model_width,), jnp.float32),
        jnp.zeros((head_features,), jnp.float32),
        jnp.zeros((head_features,), jnp.float32),
    )
    expert_grads = (
        jnp.zeros(w_gate.shape, jnp.float32),
        jnp.zeros(w_up.shape, jnp.float32),
        jnp.zeros(w_down.shape, jnp.float32),
    )
    attn_grads = tuple(
        (
            jnp.zeros(weight_part.shape, jnp.float32)
            for weight_part in (w_query, key_projection_weight, value_projection_weight, w_out)
        )
    )
    outputs = []
    input_grads = []
    for batch_index in range(batch_count):
        query_full, key_full, value_full, out_full = (
            lax.all_gather(w_query, "fsdp", axis=0, tiled=True),
            lax.all_gather(key_projection_weight, "fsdp", axis=0, tiled=True),
            lax.all_gather(value_projection_weight, "fsdp", axis=0, tiled=True),
            lax.all_gather(w_out, "fsdp", axis=1, tiled=True),
        )
        own_rows = tokens[batch_index, 0].astype(jnp.float32)
        own_cot = cotangent[batch_index, 0]
        route_rows = routes[batch_index, 0]
        gate_rows = gates[batch_index, 0]
        first_normed = rms_scale(own_rows, first_gain).astype(jnp.bfloat16)
        normed_all = lax.all_gather(first_normed, "tp", axis=0, tiled=True)
        query_projected = jnp.dot(
            normed_all, query_full, preferred_element_type=jnp.float32
        ).reshape(sequence_length, query_heads, head_features)
        key_projected = jnp.dot(normed_all, key_full, preferred_element_type=jnp.float32).reshape(
            sequence_length, kv_heads, head_features
        )
        value_row_list = (
            jnp.dot(normed_all, value_full, preferred_element_type=jnp.float32)
            .astype(jnp.bfloat16)
            .reshape(sequence_length, kv_heads, head_features)
        )
        query_rot = prep_heads(query_projected, query_factor_scale).astype(jnp.bfloat16)
        key_rot = prep_heads(key_projected, key_scale).astype(jnp.bfloat16)
        query_fourfold = query_rot.reshape(sequence_length, kv_heads, group_size, head_features)
        scores = masked_scores(query_fourfold, key_rot)
        row_max = jnp.max(scores, axis=-1, keepdims=True)
        exp_scores = jnp.exp(scores - row_max)
        totals = jnp.sum(exp_scores, axis=-1, keepdims=True)
        log_total = row_max + jnp.log(totals)
        prob_rows = (exp_scores / totals).astype(jnp.bfloat16)
        context = (
            jnp.einsum(
                "cgqk,kcd->qcgd", prob_rows, value_row_list, preferred_element_type=jnp.float32
            )
            .astype(jnp.bfloat16)
            .reshape(sequence_length, query_heads * head_features)
        )
        attn_own = lax.psum_scatter(
            jnp.dot(context, out_full, preferred_element_type=jnp.float32).astype(jnp.bfloat16),
            "tp",
            scatter_dimension=0,
            tiled=True,
        ).astype(jnp.float32)
        hidden_own = own_rows + attn_own
        second_normed = rms_scale(hidden_own, second_gain).astype(jnp.bfloat16)
        normed_two, cot_all = (
            lax.all_gather(second_normed, "tp", axis=0, tiled=True),
            lax.all_gather(own_cot, "tp", axis=0, tiled=True),
        )
        slot_index, slot_owner, slot_weight = slot_tables(
            route_rows, gate_rows, all_experts, capacity
        )
        padded_rows = jnp.concatenate([normed_two, zero_row], axis=0)
        send_rows = padded_rows[slot_owner].reshape(buffer_shape)
        expert_in = lax.all_to_all(send_rows, "fsdp", split_axis=0, concat_axis=0, tiled=True)
        gate_act = jnp.einsum(
            "sekd,edf->sekf", expert_in, w_gate, preferred_element_type=jnp.float32
        )
        up_act = jnp.einsum("sekd,edf->sekf", expert_in, w_up, preferred_element_type=jnp.float32)
        act_rows = swiglu(gate_act, up_act).astype(jnp.bfloat16)
        expert_out = jnp.einsum(
            "sekf,efd->sekd", act_rows, w_down, preferred_element_type=jnp.float32
        )
        returned = lax.all_to_all(
            expert_out.astype(jnp.bfloat16), "fsdp", split_axis=0, concat_axis=0, tiled=True
        ).astype(expert_out.dtype)
        picked = returned.reshape(all_experts * capacity, model_width)[slot_index].reshape(
            sequence_length, top_count, model_width
        )
        moe_part = jnp.sum(picked * gate_rows[:, :, None], axis=1)
        moe_own = lax.psum_scatter(
            moe_part.astype(jnp.bfloat16), "tp", scatter_dimension=0, tiled=True
        ).astype(jnp.float32)
        outputs.append((hidden_own + moe_own).astype(jnp.bfloat16))
        cot_padded = jnp.concatenate([cot_all, zero_row], axis=0)
        send_grads = (
            (slot_weight[:, None] * cot_padded[slot_owner])
            .astype(jnp.bfloat16)
            .reshape(buffer_shape)
        )
        out_grads = lax.all_to_all(send_grads, "fsdp", split_axis=0, concat_axis=0, tiled=True)
        act_grads = jnp.einsum(
            "sekd,efd->sekf", out_grads, w_down, preferred_element_type=jnp.float32
        )
        _, swiglu_back = jax.vjp(swiglu, gate_act, up_act)
        gate_grads, up_grads = swiglu_back(act_grads)
        gate_grads = gate_grads.astype(jnp.bfloat16)
        up_grads = up_grads.astype(jnp.bfloat16)
        expert_grads = (
            expert_grads[0]
            + jnp.einsum(
                "sekd,sekf->edf", expert_in, gate_grads, preferred_element_type=jnp.float32
            ),
            expert_grads[1]
            + jnp.einsum("sekd,sekf->edf", expert_in, up_grads, preferred_element_type=jnp.float32),
            expert_grads[2]
            + jnp.einsum("sekf,sekd->efd", act_rows, out_grads, preferred_element_type=jnp.float32),
        )
        input_part = jnp.einsum(
            "sekf,edf->sekd", gate_grads, w_gate, preferred_element_type=jnp.float32
        ) + jnp.einsum("sekf,edf->sekd", up_grads, w_up, preferred_element_type=jnp.float32)
        input_back = lax.all_to_all(
            input_part.astype(jnp.bfloat16), "fsdp", split_axis=0, concat_axis=0, tiled=True
        ).astype(input_part.dtype)
        normed_grads = jnp.sum(
            input_back.reshape(all_experts * capacity, model_width)[slot_index].reshape(
                sequence_length, top_count, model_width
            ),
            axis=1,
        )
        normed_own = lax.psum_scatter(
            normed_grads.astype(jnp.bfloat16), "tp", scatter_dimension=0, tiled=True
        ).astype(jnp.float32)
        _, second_back = jax.vjp(rms_scale, hidden_own, second_gain)
        hidden_part, second_gain_grad = second_back(normed_own)
        hidden_grad = own_cot.astype(jnp.float32) + hidden_part
        attn_grad_all = lax.all_gather(hidden_grad.astype(jnp.bfloat16), "tp", axis=0, tiled=True)
        out_weight_grad = jnp.einsum(
            "th,td->hd", context, attn_grad_all, preferred_element_type=jnp.float32
        )
        context_grad = (
            jnp.einsum("td,hd->th", attn_grad_all, out_full, preferred_element_type=jnp.float32)
            .astype(jnp.bfloat16)
            .reshape(sequence_length, kv_heads, group_size, head_features)
        )
        exp_again = jnp.exp(masked_scores(query_fourfold, key_rot) - log_total)
        probs_again = exp_again.astype(jnp.bfloat16)
        prob_grads = jnp.einsum(
            "qcgd,kcd->cgqk", context_grad, value_row_list, preferred_element_type=jnp.float32
        )
        value_grads = (
            jnp.einsum(
                "cgqk,qcgd->kcd", probs_again, context_grad, preferred_element_type=jnp.float32
            )
            .astype(jnp.bfloat16)
            .reshape(sequence_length, kv_heads * head_features)
        )
        score_grads = (
            exp_again * (prob_grads - jnp.sum(exp_again * prob_grads, axis=-1, keepdims=True))
        ).astype(jnp.bfloat16)
        query_rot_grads = (
            jnp.einsum("cgqk,kcd->qcgd", score_grads, key_rot, preferred_element_type=jnp.float32)
            * score_scale
        ).reshape(sequence_length, query_heads, head_features)
        key_rot_grads = (
            jnp.einsum(
                "cgqk,qcgd->kcd", score_grads, query_fourfold, preferred_element_type=jnp.float32
            )
            * score_scale
        )
        _, query_back = jax.vjp(prep_heads, query_projected, query_factor_scale)
        query_proj_grads, query_gain_grad = query_back(query_rot_grads)
        _, key_back = jax.vjp(prep_heads, key_projected, key_scale)
        key_proj_grads, key_gain_grad = key_back(key_rot_grads)
        query_proj_grads = query_proj_grads.astype(jnp.bfloat16).reshape(
            sequence_length, query_heads * head_features
        )
        key_proj_grads = key_proj_grads.astype(jnp.bfloat16).reshape(
            sequence_length, kv_heads * head_features
        )
        first_normed_grads = (
            jnp.einsum(
                "tq,dq->td", query_proj_grads, query_full, preferred_element_type=jnp.float32
            )
            + jnp.einsum("tq,dq->td", key_proj_grads, key_full, preferred_element_type=jnp.float32)
            + jnp.einsum("tq,dq->td", value_grads, value_full, preferred_element_type=jnp.float32)
        )
        weight_parts = (
            jnp.einsum(
                "td,tq->dq", normed_all, query_proj_grads, preferred_element_type=jnp.float32
            ),
            jnp.einsum("td,tq->dq", normed_all, key_proj_grads, preferred_element_type=jnp.float32),
            jnp.einsum("td,tq->dq", normed_all, value_grads, preferred_element_type=jnp.float32),
            out_weight_grad,
        )
        first_own = lax.psum_scatter(
            first_normed_grads.astype(jnp.bfloat16), "tp", scatter_dimension=0, tiled=True
        ).astype(jnp.float32)
        _, first_back = jax.vjp(rms_scale, own_rows, first_gain)
        row_part, first_gain_grad = first_back(first_own)
        input_grads.append((hidden_grad + row_part).astype(jnp.bfloat16))
        gain_sums = (
            gain_sums[0] + first_gain_grad,
            gain_sums[1] + second_gain_grad,
            gain_sums[2] + query_gain_grad,
            gain_sums[3] + key_gain_grad,
        )
        attn_grads = jax.tree.map(
            jnp.add,
            attn_grads,
            (
                lax.psum_scatter(weight_parts[0], "fsdp", scatter_dimension=0, tiled=True),
                lax.psum_scatter(weight_parts[1], "fsdp", scatter_dimension=0, tiled=True),
                lax.psum_scatter(weight_parts[2], "fsdp", scatter_dimension=0, tiled=True),
                lax.psum_scatter(weight_parts[3], "fsdp", scatter_dimension=1, tiled=True),
            ),
        )
    summed = lax.psum((gain_sums[0], gain_sums[1], gain_sums[2], gain_sums[3]), ("fsdp", "tp"))
    block_out = jnp.stack(outputs)[:, None]
    input_grad = jnp.stack(input_grads)[:, None]
    return (
        block_out,
        input_grad,
        summed[0],
        attn_grads[0],
        attn_grads[1],
        attn_grads[2],
        summed[2],
        summed[3],
        attn_grads[3],
        summed[1],
        expert_grads[0],
        expert_grads[1],
        expert_grads[2],
    )


MESH = pl.DeviceIdType.MESH
FSDP, TP = "fsdp", "tp"
PLANE = 4
LANES = 128
MIB = 1 << 20
RIGHT, LEFT, FIRST, SECOND, CORE, CROSS = range(6)
TRANSPOSED_LEFT = (((0,), (0,)), ((), ()))
TRANSPOSED_RIGHT = (((1,), (1,)), ((), ()))
OUTPUT, BACK = range(2)
CHUNK = 512


class Spot:
    def __init__(self, line, wide, turned=True):
        self.line = line
        self.wide = wide
        self.turned = turned
        self.planes = 4 if wide else 2
        index = lax.axis_index(FSDP)
        self.x = lax.axis_index(TP)
        self.z = lax.div(index, PLANE)
        self.y = lax.rem(lax.div(index, 2), 2)
        self.core = lax.rem(index, 2)

    def side(self, core, first, second):
        flip_y, flip_x = first, second
        if self.wide and self.turned:
            flip_y = (1 - core) * first + core * second
            flip_x = core * first + (1 - core) * second
        return self.y + flip_y * (1 - 2 * self.y), self.x + flip_x * (1 - 2 * self.x)

    def block(self, core, first, second, z):
        y, x = self.side(core, first, second)
        return z * PLANE + y * 2 + core, x

    def device(self, kind):
        if kind == RIGHT:
            return self.block(self.core, 0, 0, self.z + 1)
        if kind == LEFT:
            return self.block(self.core, 0, 0, self.z - 1)
        if kind == CORE:
            return self.block(1 - self.core, 0, 0, self.z)
        if kind == CROSS:
            return self.block(self.core, 0, 0, self.z)[0], 1 - self.x
        return self.block(self.core, int(kind == FIRST), int(kind == SECOND), self.z)

    def kinds(self):
        return (FIRST, SECOND, CORE) if self.wide else (FIRST, CORE)

    def number(self, first, second, z):
        return (second * 2 + first) * self.line + z

    def order(self, step):
        if isinstance(step, int) and step == 0:
            return [(self.z, None)]
        return [(self.z - step, self.z - step >= 0), (self.z + step, self.z + step < self.line)]

    def greet(self):
        barrier = pltpu.get_barrier_semaphore()

        def signal(kind):
            pl.semaphore_signal(barrier, inc=1, device_id=self.device(kind), device_id_type=MESH)

        for kind in self.kinds():
            signal(kind)
        when(self.z + 1 < self.line, lambda: signal(RIGHT))
        when(self.z > 0, lambda: signal(LEFT))
        around = (self.z + 1 < self.line).astype(jnp.int32) + (self.z > 0).astype(jnp.int32)
        pl.semaphore_wait(barrier, len(self.kinds()) + around)

    def send(self, source, target, send_sem, receive_sem, kind):
        return pltpu.make_async_remote_copy(
            src_ref=source,
            dst_ref=target,
            send_sem=send_sem,
            recv_sem=receive_sem,
            device_id=self.device(kind),
            device_id_type=MESH,
        )


def when(condition, action):
    def run():
        action()

    if condition is None or condition is True:
        run()
    elif condition is not False:
        pl.when(condition)(run)


class Spread:
    def __init__(self, spot, source, slot, send, receive, local):
        self.spot = spot
        self.slot = slot
        self.source = source
        self.sends = send
        self.receives = receive
        self.mine = pltpu.make_async_copy(source, slot(*spot.block(spot.core, 0, 0, spot.z)), local)

    def copy(self, first, second, z, kind, own=False):
        spot = self.spot
        place = self.slot(*spot.block(spot.core, first, second, z))
        number = spot.number(first, second, z)
        arrival = {
            RIGHT: number,
            LEFT: number,
            FIRST: spot.number(1, 0, z),
            SECOND: spot.number(first, 1, z),
            CORE: spot.planes * spot.line + number,
        }[kind]
        departure = {RIGHT: 0, LEFT: 1, FIRST: 2, SECOND: 3, CORE: 5}[kind] * spot.line + number
        source = self.source if own else place
        return spot.send(source, place, self.sends.at[departure], self.receives.at[arrival], kind)

    def arrived(self, first, second, z, other=False):
        spot = self.spot
        core = 1 - spot.core if other else spot.core
        place = self.slot(*spot.block(core, first, second, z))
        number = spot.number(first, second, z) + (spot.planes * spot.line if other else 0)
        spot.send(place, place, self.sends.at[0], self.receives.at[number], CORE).wait_recv()

    def steps(self):
        return self.spot.line + (3 if self.spot.wide else 1)

    def begin(self):
        spot = self.spot
        z = spot.z
        when(z + 1 < spot.line, lambda: self.copy(0, 0, z, RIGHT, True).start())
        when(z > 0, lambda: self.copy(0, 0, z, LEFT, True).start())
        for kind in spot.kinds():
            self.copy(0, 0, z, kind, True).start()
        self.mine.start()

    def step(self, step):
        spot = self.spot
        line, z = spot.line, spot.z

        def reached(away, action):
            inside = jnp.logical_and(away >= 0, away < line)
            when(jnp.logical_and(inside, z - away >= 0), lambda: action(z - away, True))
            when(
                jnp.logical_and(inside, jnp.logical_and(away > 0, z + away < line)),
                lambda: action(z + away, False),
            )

        def along(zz, from_left):
            self.arrived(0, 0, zz)
            if from_left:
                when(z + 1 < line, lambda: self.copy(0, 0, zz, RIGHT).start())
            else:
                when(z > 0, lambda: self.copy(0, 0, zz, LEFT).start())
            for kind in spot.kinds():
                self.copy(0, 0, zz, kind).start()

        def firsts(zz, _):
            self.arrived(1, 0, zz)
            if spot.wide:
                self.copy(1, 0, zz, SECOND).start()
            self.copy(1, 0, zz, CORE).start()

        def lasts(first):
            def action(zz, _):
                self.arrived(first, 1, zz)
                self.copy(first, 1, zz, CORE).start()

            return action

        step = jnp.asarray(step, jnp.int32)
        reached(step, along)
        reached(step - 1, firsts)
        if spot.wide:
            reached(step - 2, lasts(0))
            reached(step - 3, lasts(1))

    def finish(self):
        spot = self.spot
        z = spot.z

        def body(zz, _):
            when(
                jnp.logical_and(z + 1 < spot.line, zz <= z),
                lambda: self.copy(0, 0, zz, RIGHT).wait_send(),
            )
            when(jnp.logical_and(z > 0, zz >= z), lambda: self.copy(0, 0, zz, LEFT).wait_send())
            self.copy(0, 0, zz, FIRST).wait_send()
            for second in range(2 if spot.wide else 1):
                for first in (0, 1):
                    if spot.wide and not second:
                        self.copy(first, 0, zz, SECOND).wait_send()
                    self.copy(first, second, zz, CORE).wait_send()
                    self.arrived(first, second, zz, other=True)
            return 0

        lax.fori_loop(0, spot.line, body, 0)
        self.mine.wait()


class LateSpread(Spread):
    def steps(self):
        return self.spot.line + 2

    def copy(self, first, second, z, kind, own=False):
        spot = self.spot
        place = self.slot(*spot.block(spot.core, first, second, z))
        number = spot.number(first, second, z)
        arrival = {
            RIGHT: number,
            LEFT: number,
            FIRST: spot.number(1, 0, z),
            SECOND: spot.number(first, 1, z),
            CORE: spot.planes * spot.line + number,
        }[kind]
        departure = {RIGHT: 0, LEFT: 4, CORE: 8, FIRST: 12, SECOND: 13}[kind] * spot.line + number
        source = self.source if own else place
        return spot.send(source, place, self.sends.at[departure], self.receives.at[arrival], kind)

    def along_both(self, first, second, own=False):
        spot = self.spot
        z = spot.z
        when(z + 1 < spot.line, lambda: self.copy(first, second, z, RIGHT, own).start())
        when(z > 0, lambda: self.copy(first, second, z, LEFT, own).start())
        self.copy(first, second, z, CORE, own).start()

    def begin(self):
        self.copy(0, 0, self.spot.z, FIRST, True).start()
        self.copy(0, 0, self.spot.z, SECOND, True).start()
        self.along_both(0, 0, True)
        self.mine.start()

    def step(self, step):
        spot = self.spot
        line, z = spot.line, spot.z
        step = jnp.asarray(step, jnp.int32)

        def passed(first, second, zz, kind, more):
            self.arrived(first, second, zz)
            when(more, lambda: self.copy(first, second, zz, kind).start())
            self.copy(first, second, zz, CORE).start()

        for first, second in ((0, 0), (1, 0), (0, 1), (1, 1)):
            away = step - (first + second)

            def here():
                self.arrived(first, second, z)
                if first and not second:
                    self.copy(1, 0, z, SECOND).start()
                self.along_both(first, second)

            if first or second:
                when(away == 0, here)
            far = jnp.logical_and(away > 0, away < line)
            when(
                jnp.logical_and(far, z - away >= 0),
                lambda: passed(first, second, z - away, RIGHT, z + 1 < line),
            )
            when(
                jnp.logical_and(far, z + away < line),
                lambda: passed(first, second, z + away, LEFT, z > 0),
            )

    def finish(self):
        spot = self.spot
        z = spot.z

        def body(zz, _):
            for second in (0, 1):
                for first in (0, 1):
                    when(
                        jnp.logical_and(z + 1 < spot.line, zz <= z),
                        lambda: self.copy(first, second, zz, RIGHT).wait_send(),
                    )
                    when(
                        jnp.logical_and(z > 0, zz >= z),
                        lambda: self.copy(first, second, zz, LEFT).wait_send(),
                    )
                    self.copy(first, second, zz, CORE).wait_send()
                    self.arrived(first, second, zz, other=True)
            return 0

        lax.fori_loop(0, spot.line, body, 0)
        self.copy(0, 0, z, FIRST).wait_send()
        for first in (0, 1):
            self.copy(first, 0, z, SECOND).wait_send()
        self.mine.wait()


def rows_spread(spot, source, place, rows, semaphores, at):
    late = late_rows(rows)
    early = rows - late
    send, receive, late_send, late_receive, local = semaphores

    def slot(start, size):
        return lambda block, side: place(block, side * rows + start, size)

    return [
        Spread(
            spot,
            source.at[pl.ds(0, early)],
            slot(0, early),
            send.at[at],
            receive.at[at],
            local.at[at, 0],
        ),
        LateSpread(
            spot,
            source.at[pl.ds(early, late)],
            slot(early, late),
            late_send.at[at],
            late_receive.at[at],
            local.at[at, 1],
        ),
    ]


def late_rows(rows):
    return max(16, round(rows * 2 / 9 / 16) * 16)


def rows_semaphores(batch, line):
    counts = (*spread_count(line, True), 15 * line, 8 * line, 2)
    return [pltpu.SemaphoreType.DMA((batch, count)) for count in counts]


def run_trees(trees):
    for tree in trees:
        tree.begin()

    def body(step, _):
        for tree in trees:
            tree.step(step)
        return 0

    lax.fori_loop(1, max(tree.steps() for tree in trees), body, 0)
    for tree in trees:
        tree.finish()


def spread_count(line, wide):
    return (9 if wide else 7) * line, (8 if wide else 4) * line


def mingle(work, others):
    for index, piece in enumerate(work):
        piece()
        for other in others[
            index * len(others) // len(work) : (index + 1) * len(others) // len(work)
        ]:
            other()


def rows_at(ref, index, size):
    return ref.at[pl.ds(pl.multiple_of(index * size, 16), size)]


def columns_at(ref, index, size):
    return ref.at[:, pl.ds(pl.multiple_of(index * size, LANES), size)]


def norm_rows(target, source, gain):
    def body(step, _):
        rows = pl.ds(pl.multiple_of(step * 16, 16), 16)
        value = source[rows, :].astype(jnp.float32)
        target[rows, :] = rms_scale(value, gain[...].astype(jnp.float32)).astype(target.dtype)
        return 0

    lax.fori_loop(0, target.shape[0] // 16, body, 0)


def turned_heads(value, gain, cosine, sine):
    normed = rms_scale(value, gain)
    return normed * cosine + pltpu.roll(normed, normed.shape[-1] // 2, 1) * sine


def visible_blocks(length, group):
    blocks = []
    for start in range(0, length, BLOCK):
        stop = min(start + BLOCK, length)
        heads = max(1, BLOCK // (stop - start))
        while group % heads:
            heads -= 1
        blocks.append((start, stop, stop, heads))
    return blocks


def softmax(scores):
    raised = jnp.exp(scores - jnp.max(scores, axis=0, keepdims=True))
    return raised * (1.0 / jnp.sum(raised, axis=0, keepdims=True))


def for_heads(low, high, heads, body):
    turns = 2 if heads == 1 and (high - low) % 2 == 0 else 1

    def turn(step, _):
        for i in range(turns):
            body(low + (step * turns + i) * heads)
        return 0

    count = (high - low) // (heads * turns)
    if count == 1:
        turn(0, 0)
    else:
        lax.fori_loop(0, count, turn, 0)


def head_columns(head, features):
    return pl.ds(pl.multiple_of(head * features, LANES), features)


def forward_kernel(
    line,
    heads,
    kv_heads,
    tokens_ref,
    cot_ref,
    in_ref,
    out_ref,
    picks_ref,
    gain1_ref,
    gain2_ref,
    query_gain_ref,
    key_gain_ref,
    cosine_ref,
    sine_ref,
    cot_all,
    in_all,
    out_all,
    picks_all,
    normed_all,
    projected_all,
    context_all,
    hidden_all,
    second_all,
    in_w,
    out_w,
    tokens,
    normed,
    projected,
    context,
    queries,
    keys,
    values,
    mixed,
    mixed_other,
    hidden,
    second,
    narrow_send,
    narrow_receive,
    cot_send,
    cot_receive,
    cot_late_send,
    cot_late_receive,
    cot_local,
    local,
    token_send,
    token_receive,
    mixed_send,
    mixed_receive,
    save_sem,
):
    cot_semaphores = (cot_send, cot_receive, cot_late_send, cot_late_receive, cot_local)
    batch, half, width = tokens_ref.shape
    length = 2 * half
    depth, out_width = in_ref.shape[0], out_ref.shape[1]
    features = query_gain_ref.shape[1]
    narrow = Spot(line, False)
    spot = Spot(line, True, turned=False)
    x = spot.x
    spot.greet()
    slots = [
        (picks_ref, lambda block, side: picks_all.at[block]),
        (in_ref, lambda block, side: rows_at(in_w, block, depth)),
        (out_ref, lambda block, side: columns_at(out_w, block, out_width)),
    ]
    weights = [
        Spread(narrow, source, slot, narrow_send.at[i], narrow_receive.at[i], local.at[i])
        for i, (source, slot) in enumerate(slots)
    ]
    place = lambda block, start, size: cot_all.at[block, pl.ds(pl.multiple_of(start, 16), size)]
    cots = rows_spread(spot, cot_ref.at[0], place, half, cot_semaphores, 0)
    early, late = weights[:2], weights[2]
    for tree in early:
        tree.begin()

    def token_copies(i):
        place = rows_at(tokens.at[i], x, half)
        return (
            pltpu.make_async_copy(tokens_ref.at[i], place, local.at[3 + i]),
            spot.send(tokens_ref.at[i], place, token_send.at[i], token_receive.at[i], CROSS),
        )

    for i in range(batch):
        for copy in token_copies(i):
            copy.start()
    def steps(step, _):
        for tree in early:
            tree.step(step)
        return 0

    lax.fori_loop(1, late.steps(), steps, 0)
    late.begin()
    for tree in cots:
        tree.begin()
    for i in range(batch):
        mine, other = token_copies(i)
        mine.wait()
        other.wait_send()
        place = rows_at(tokens.at[i], 1 - x, half)
        spot.send(place, place, token_send.at[i], token_receive.at[i], CROSS).wait_recv()
    for i in range(batch):
        norm_rows(normed.at[i], tokens.at[i], gain1_ref)
    for tree in early:
        tree.finish()

    def save(source, target, index):
        return pltpu.make_async_copy(source, target, save_sem.at[index])

    saves = [save(in_w, in_all, 0), save(out_w, out_all, 1)]
    saves[0].start()

    def project(i, start, stop):
        for at in range(start, stop, CHUNK):
            projected[i, :, at : at + CHUNK] = jnp.dot(
                normed[i], in_w[:, at : at + CHUNK], preferred_element_type=jnp.float32
            )

    scale = features ** (-0.5)

    group = heads // kv_heads

    def prepare_keys(i):
        base = heads * features
        for head in range(kv_heads):
            at = base + head * features
            keys[head] = turned_heads(
                projected[i, :, at : at + features],
                key_gain_ref[...].astype(jnp.float32),
                cosine_ref[...],
                sine_ref[...],
            ).astype(jnp.bfloat16)
            at = base + (kv_heads + head) * features
            values[head] = projected[i, :, at : at + features].astype(jnp.bfloat16)

    def prepare_queries(i, shared):
        def prepare(member):
            columns = head_columns(shared * group + member, features)
            queries[member] = turned_heads(
                projected[i, :, columns], query_gain_ref[...].astype(jnp.float32), cosine_ref[...], sine_ref[...]
            ).astype(jnp.bfloat16)

        for_heads(0, group, 1, prepare)

    def attend(i, shared, start, stop, seen, at_once, low, high):
        count = stop - start

        def block(member):
            query = queries[pl.ds(member, at_once), start:stop, :].reshape(-1, features)
            scores = lax.dot_general(
                keys[shared, :seen, :],
                query,
                TRANSPOSED_RIGHT,
                preferred_element_type=jnp.float32,
            )
            rows = lax.dot_general(
                softmax(scores * scale).astype(jnp.bfloat16),
                values[shared, :seen, :],
                TRANSPOSED_LEFT,
                preferred_element_type=jnp.float32,
            ).astype(jnp.bfloat16)
            for j in range(at_once):
                columns = head_columns(shared * group + member + j, features)
                context[i, start:stop, columns] = rows[j * count : (j + 1) * count]

        for_heads(low, high, at_once, block)

    def mixed_copy(i):
        return spot.send(
            rows_at(mixed.at[i], 1 - x, half),
            mixed_other.at[i],
            mixed_send.at[i],
            mixed_receive.at[i],
            CROSS,
        )

    def mix(i, start, stop):
        for at in range(start, stop, CHUNK):
            mixed[i, :, at : at + CHUNK] = jnp.dot(
                context[i], out_w[:, at : at + CHUNK], preferred_element_type=jnp.float32
            ).astype(jnp.bfloat16)
        if stop == width:
            mixed_copy(i).start()

    def close(i):
        mixed_copy(i).wait()
        add_rows(
            hidden.at[i],
            [rows_at(tokens.at[i], x, half), rows_at(mixed.at[i], x, half), mixed_other.at[i]],
        )
        norm_rows(second.at[i], hidden.at[i], gain2_ref)

    def late_done():
        late.finish()
        saves[1].start()

    def steps_of(trees, low, high):
        return [
            functools.partial(tree.step, step)
            for step in range(low, high)
            for tree in trees
            if step < tree.steps()
        ]

    in_width = in_w.shape[1]
    parts = lambda size: [(at, min(at + 2 * CHUNK, size)) for at in range(0, size, 2 * CHUNK)]
    opening, middle, closing = [], [], []
    for i in range(batch):
        opening += [functools.partial(project, i, *part) for part in parts(in_width)]
        middle.append(functools.partial(prepare_keys, i))
        for shared in range(kv_heads):
            middle.append(functools.partial(prepare_queries, i, shared))
            for start, stop, seen, at_once in visible_blocks(length, group):
                share = max(at_once, group // 2)
                for low in range(0, group, share):
                    middle.append(
                        functools.partial(
                            attend, i, shared, start, stop, seen, at_once, low, low + share
                        )
                    )
        closing += [functools.partial(mix, i, *part) for part in parts(width)]
    closing += [functools.partial(close, i) for i in range(batch)]
    last = cots[0].steps()
    mingle(opening + middle, steps_of([late] + cots, 1, last))
    late_done()
    for piece in closing:
        piece()

    saves += [
        save(source, target, 2 + i)
        for i, (source, target) in enumerate(
            [
                (normed, normed_all),
                (projected, projected_all),
                (context, context_all),
                (hidden, hidden_all),
                (second, second_all),
            ]
        )
    ]
    for copy in saves[2:]:
        copy.start()
    for tree in cots:
        tree.finish()
    for copy in saves:
        copy.wait()


def run_forward(tokens, cot, weight_in, weight_out, picks, gains, tables, fsdp_count, kv_heads):
    line = fsdp_count // PLANE
    batch, half, width = tokens.shape
    length = 2 * half
    features = gains[2].shape[1]
    heads = weight_out.shape[0] // features
    in_shape = (weight_in.shape[0] * fsdp_count, weight_in.shape[1])
    out_shape = (weight_out.shape[0], weight_out.shape[1] * fsdp_count)
    narrow = spread_count(line, False)
    anywhere = pl.BlockSpec(memory_space=pl.ANY)
    inside = pl.BlockSpec(memory_space=pltpu.VMEM)
    shape = lambda dims, kind=jnp.bfloat16: jax.ShapeDtypeStruct(dims, kind)
    vmem = lambda *dims: pltpu.VMEM(dims, jnp.bfloat16)
    sem = lambda *dims: pltpu.SemaphoreType.DMA(dims)
    kept = (
        ((batch, length, width), jnp.bfloat16),
        ((batch, length, weight_in.shape[1]), jnp.float32),
        ((batch, length, heads * features), jnp.bfloat16),
        ((batch, half, width), jnp.float32),
        ((batch, half, width), jnp.bfloat16),
    )
    return pl.pallas_call(
        functools.partial(forward_kernel, line, heads, kv_heads),
        out_shape=(
            shape((fsdp_count, length, width)),
            shape(in_shape),
            shape(out_shape),
            shape((fsdp_count, *picks.shape), picks.dtype),
            *(shape(*one) for one in kept),
        ),
        in_specs=[anywhere] * 5 + [inside] * 6,
        out_specs=(anywhere,) * 9,
        scratch_shapes=[
            vmem(*in_shape),
            vmem(*out_shape),
            vmem(batch, length, width),
            *(pltpu.VMEM(*one) for one in kept[:3]),
            vmem(heads // kv_heads, length, features),
            vmem(kv_heads, length, features),
            vmem(kv_heads, length, features),
            vmem(batch, length, width),
            vmem(batch, half, width),
            *(pltpu.VMEM(*one) for one in kept[3:]),
            sem(3, narrow[0]),
            sem(3, narrow[1]),
            *rows_semaphores(1, line),
            sem(3 + batch),
            sem(batch),
            sem(batch),
            sem(batch),
            sem(batch),
            sem(7),
        ],
        compiler_params=pltpu.CompilerParams(
            collective_id=1, has_side_effects=True, vmem_limit_bytes=60 * MIB
        ),
    )(tokens, cot, weight_in, weight_out, picks, *gains, *tables)


def add_rows(target, sources):
    def body(step, _):
        rows = pl.ds(pl.multiple_of(step * 16, 16), 16)
        total = sources[0][rows, :].astype(jnp.float32)
        for source in sources[1:]:
            total = total + source[rows, :].astype(jnp.float32)
        target[rows, :] = total.astype(target.dtype)
        return 0

    lax.fori_loop(0, target.shape[0] // 16, body, 0)


class Collect:
    def __init__(self, spot, part, total, cores, firsts, rights, lefts, send, receive):
        self.spot = spot
        self.part = part
        self.total = total
        self.places = {CORE: cores, FIRST: firsts, RIGHT: rights, LEFT: lefts}
        line = spot.line
        self.base = {CORE: 0, FIRST: 2 * line, RIGHT: 3 * line, LEFT: 4 * line}
        self.sends = send
        self.receives = receive

    def own(self, first, z):
        return self.part(*self.spot.block(self.spot.core, first, 0, z))

    def copy(self, kind, first, z):
        spot = self.spot
        number = first * spot.line + z if kind == CORE else z
        source = self.part(*spot.block(1 - spot.core, first, 0, z)) if kind == CORE else self.own(first, z)
        at = self.base[kind] + number
        return spot.send(
            source, self.places[kind].at[number], self.sends.at[at], self.receives.at[at], kind
        )

    def arrived(self, kind, number):
        place = self.places[kind].at[number]
        at = self.base[kind] + number
        self.spot.send(place, place, self.sends.at[0], self.receives.at[at], CORE).wait_recv()
        return place

    def begin(self, z):
        for first in (1, 0):
            self.copy(CORE, first, z).start()

    def to_first(self, z):
        add_rows(self.own(1, z), [self.own(1, z), self.arrived(CORE, self.spot.line + z)])
        self.copy(FIRST, 1, z).start()

    def summands(self, z):
        return [self.own(0, z), self.arrived(CORE, z), self.arrived(FIRST, z)]

    def cross(self):
        for step in reversed(range(self.spot.line)):
            for zz, valid in self.spot.order(step):
                when(valid, functools.partial(self.to_first, zz))

    def onward(self, kind, zz):
        spot = self.spot
        sources = self.summands(zz)
        target = self.own(0, zz)
        behind = spot.z > 0 if kind == RIGHT else spot.z + 1 < spot.line
        when(behind, lambda: add_rows(target, sources + [self.arrived(kind, zz)]))
        when(jnp.logical_not(behind), lambda: add_rows(target, sources))
        self.copy(kind, 0, zz).start()

    def last(self):
        z, line = self.spot.z, self.spot.line
        sources = self.summands(z)

        def end(kinds):
            add_rows(self.total, sources + [self.arrived(kind, z) for kind in kinds])

        when(z == 0, lambda: end([LEFT]))
        when(z == line - 1, lambda: end([RIGHT]))
        when(jnp.logical_and(z > 0, z < line - 1), lambda: end([RIGHT, LEFT]))

    def finish(self):
        spot = self.spot
        for zz in range(spot.line):
            for first in (0, 1):
                self.copy(CORE, first, zz).wait_send()
            self.copy(FIRST, 1, zz).wait_send()
            when(zz > spot.z, lambda: self.copy(RIGHT, 0, zz).wait_send())
            when(zz < spot.z, lambda: self.copy(LEFT, 0, zz).wait_send())

    def tasks(self):
        spot = self.spot
        work = []
        for step in reversed(range(1, spot.line)):
            for kind, (zz, valid) in zip((LEFT, RIGHT), spot.order(step)):
                action = functools.partial(self.onward, kind, zz)
                work.append(functools.partial(when, valid, action))
        return work + [self.last, self.finish]


def collect_scratch(line, shape):
    counts = (2 * line, line, line, line)
    return [pltpu.VMEM((count, *shape), jnp.bfloat16) for count in counts] + [
        pltpu.SemaphoreType.DMA((5 * line,)),
        pltpu.SemaphoreType.DMA((5 * line,)),
    ]


BOXES = 6


def plane_in_turn(line, group):
    turn = lax.rem(group, line)
    step = lax.div(turn, 2)
    return jnp.where(lax.rem(turn, 2) == 0, step, line - 1 - step)


class Sums:
    def __init__(self, spot, parts, cores, places, inbox, outbox, semaphores, plane, inside, ready, done, turns):
        self.spot = spot
        self.parts = parts
        self.cores = cores
        self.seconds, self.firsts, self.ends = places
        self.inbox = inbox
        self.outbox = outbox
        (
            self.inbox_sem,
            self.outbox_sem,
            self.second_receive,
            self.first_receive,
            self.end_receive,
        ) = semaphores
        self.plane = plane
        self.inside = inside
        self.ready = ready
        self.done = done
        self.turns = turns

    def second_slot(self, turn, first):
        return turn * 2 + first

    def first_slot(self, turn):
        return 2 * self.turns + turn

    def end_slot(self, turn, kind):
        return 3 * self.turns + turn * 2 + kind

    def free(self, unit, turn, first):
        pass

    def second_send(self, unit, turn, first):
        slot = self.second_slot(turn, first)
        return self.spot.send(
            self.outbox.at[slot],
            self.seconds.at[unit, first],
            self.outbox_sem.at[slot],
            self.second_receive.at[unit, first],
            SECOND,
        )

    def first_send(self, unit, turn):
        slot = self.first_slot(turn)
        return self.spot.send(
            self.outbox.at[slot],
            self.firsts.at[unit],
            self.outbox_sem.at[slot],
            self.first_receive.at[unit],
            FIRST,
        )

    def end_send(self, unit, turn, kind):
        slot = self.end_slot(turn, kind)
        return self.spot.send(
            self.outbox.at[slot],
            self.ends.at[unit, kind],
            self.outbox_sem.at[slot],
            self.end_receive.at[unit, kind],
            kind,
        )

    def received(self, place, semaphore):
        self.spot.send(place, place, self.outbox_sem.at[0], semaphore, CORE).wait_recv()

    def sources(self, unit, first, second):
        y, x = self.spot.side(self.spot.core, first, second)
        half = self.inbox.shape[1]
        return [rows_at(self.parts(unit, y), x, half), rows_at(self.cores(unit, y), x, half)]

    def summands(self, unit):
        return self.sources(unit, 0, 0) + [self.seconds.at[unit, 0], self.firsts.at[unit]]

    def load(self, source, slot):
        return pltpu.make_async_copy(source, self.inbox.at[slot], self.inbox_sem.at[slot])

    def add(self, target, base, numbers):
        add_rows(target, [self.inbox.at[base + i] for i in numbers])

    def end_roles(self, half_step, delay):
        z, line = self.spot.z, self.spot.line
        unit = half_step - 3 - delay
        valid = self.inside(unit)
        plane = self.plane(unit)
        right = jnp.logical_and(valid, jnp.logical_and(z < plane, delay == z))
        left = jnp.logical_and(valid, jnp.logical_and(z > plane, delay == line - 1 - z))
        last = jnp.logical_and(
            valid,
            jnp.logical_and(z == plane, delay == jnp.maximum(plane, line - 1 - plane)),
        )
        return unit, right, left, last

    def end_task(self, half_step, delay, parity):
        z, line = self.spot.z, self.spot.line
        turn = (parity - 3 - delay) % self.turns
        unit, right, left, last = self.end_roles(half_step, delay)
        some = jnp.logical_or(right, jnp.logical_or(left, last))
        from_left = jnp.logical_and(jnp.logical_or(right, last), z > 0)
        from_right = jnp.logical_and(jnp.logical_or(left, last), z + 1 < line)
        present = ((RIGHT, from_left), (LEFT, from_right))

        def fetch(base):
            def action():
                self.received(self.seconds.at[unit, 0], self.second_receive.at[unit, 0])
                self.received(self.firsts.at[unit], self.first_receive.at[unit])
                for i, source in enumerate(self.summands(unit)):
                    self.load(source, base + i).start()
                for kind, there in present:

                    def arrive():
                        self.received(self.ends.at[unit, kind], self.end_receive.at[unit, kind])
                        self.load(self.ends.at[unit, kind], base + 4 + kind).start()

                    when(there, arrive)

            when(some, action)

        def add(base):
            def action():
                for i, source in enumerate(self.summands(unit)):
                    self.load(source, base + i).wait()
                for kind, there in present:
                    when(there, lambda: self.load(self.ends.at[unit, kind], base + 4 + kind).wait())
                numbers = list(range(4))
                for kind, chosen, behind in ((RIGHT, right, z > 0), (LEFT, left, z + 1 < line)):

                    def onward():
                        target = self.outbox.at[self.end_slot(turn, kind)]
                        self.free(unit, turn, 0)
                        when(behind, lambda: self.add(target, base, numbers + [4 + kind]))
                        when(jnp.logical_not(behind), lambda: self.add(target, base, numbers))
                        self.end_send(unit, turn, kind).start()

                    when(chosen, onward)

                def finish():
                    def into(target):
                        both = jnp.logical_and(from_left, from_right)
                        when(both, lambda: self.add(target, base, numbers + [4, 5]))
                        for kind, there in present:
                            when(
                                jnp.logical_and(there, jnp.logical_not(both)),
                                lambda: self.add(target, base, numbers + [4 + kind]),
                            )

                    self.done(unit, turn, into)

                when(last, finish)

            when(some, action)

        return fetch, add

    def retire(self, half_step, parity):
        before = half_step - self.turns
        now, then = (parity - 1) % self.turns, (parity - 2) % self.turns
        when(
            self.inside(before - 1),
            lambda: [self.second_send(before - 1, now, first).wait_send() for first in range(2)],
        )
        when(self.inside(before - 2), lambda: self.first_send(before - 2, then).wait_send())
        for delay in range(self.spot.line):
            if self.inside(before - 3 - delay) is False:
                continue
            unit, right, left, _ = self.end_roles(before, delay)
            turn = (parity - 3 - delay) % self.turns
            when(right, lambda: self.end_send(unit, turn, RIGHT).wait_send())
            when(left, lambda: self.end_send(unit, turn, LEFT).wait_send())

    def simple_task(self, valid, ready, inputs, slot, send, free=lambda: None):
        def fetch(base):
            ready()

            def action():
                for i, source in enumerate(inputs()):
                    self.load(source, base + i).start()

            when(valid, action)

        def add(base):
            def action():
                refs = inputs()
                for i, source in enumerate(refs):
                    self.load(source, base + i).wait()
                free()
                self.add(self.outbox.at[slot], base, range(len(refs)))
                send().start()

            when(valid, action)

        return fetch, add

    def tasks(self, half_step, parity):
        one, two = half_step - 1, half_step - 2
        now, then = (parity - 1) % self.turns, (parity - 2) % self.turns
        tasks = [
            self.second_task(one, now, 1, functools.partial(self.ready, one)),
            self.second_task(one, now, 0, lambda: None),
            self.first_task(two, then),
        ]
        for delay in range(self.spot.line):
            if self.inside(half_step - 3 - delay) is not False:
                tasks.append(self.end_task(half_step, delay, parity))
        return tasks

    def second_task(self, unit, turn, first, ready):
        return self.simple_task(
            self.inside(unit),
            ready,
            lambda: self.sources(unit, first, 1),
            self.second_slot(turn, first),
            lambda: self.second_send(unit, turn, first),
        )

    def first_task(self, unit, turn):
        arrive = lambda: self.received(self.seconds.at[unit, 1], self.second_receive.at[unit, 1])

        def send():
            return self.first_send(unit, turn)

        return self.simple_task(
            self.inside(unit),
            lambda: when(self.inside(unit), arrive),
            lambda: self.sources(unit, 1, 0) + [self.seconds.at[unit, 1]],
            self.first_slot(turn),
            send,
            lambda: self.free(unit, turn, 1),
        )

    def weave(self, tasks, pieces):
        buffers = self.inbox.shape[0] // BOXES
        if buffers > 1:
            tasks[0][0](0)
        for index, (fetch, add) in enumerate(tasks):
            if buffers == 1:
                fetch(0)
            elif index + 1 < len(tasks):
                tasks[index + 1][0]((index + 1) % 2 * BOXES)
            share = -(-len(pieces) // (len(tasks) - index))
            for piece in pieces[:share]:
                piece()
            pieces = pieces[share:]
            add(index % buffers * BOXES)

    def half_steps(self, units):
        return units + self.spot.line + 2


def norm_back(value, grads, gain):
    scale = lax.rsqrt(jnp.mean(value * value, axis=-1, keepdims=True) + EPSILON)
    unit = value * scale
    scaled = grads * gain
    back = scale * (scaled - unit * jnp.mean(scaled * unit, axis=-1, keepdims=True))
    return back, grads * unit


def backward_kernel(
    line,
    heads,
    kv_heads,
    cot_ref,
    totals_ref,
    hidden_ref,
    projected_ref,
    context_ref,
    in_ref,
    out_ref,
    tokens_ref,
    gain1_ref,
    gain2_ref,
    query_gain_ref,
    key_gain_ref,
    cosine_ref,
    sine_ref,
    block_out,
    input_grad,
    grads_all,
    out_total,
    gain_grads,
    elements,
    cots,
    tokens,
    kept,
    result,
    context,
    hidden_grads,
    context_grads,
    grads,
    normed_other,
    weight_rows,
    queries_f,
    shared_f,
    queries,
    query_grads,
    sums,
    out_grads,
    cores,
    firsts,
    rights,
    lefts,
    tree_send,
    tree_receive,
    load_sem,
    row_sem,
    head_sem,
    save_sem,
    hidden_send,
    hidden_receive,
    normed_send,
    normed_receive,
):
    batch, half, width = cot_ref.shape
    length = 2 * half
    features = query_gain_ref.shape[1]
    group = heads // kv_heads
    base = heads * features
    out_width = out_total.shape[1]
    narrow, spot = Spot(line, False), Spot(line, True)
    x = spot.x
    scale = features ** (-0.5)
    normed_grads = context_grads

    def load(source, target, index):
        return pltpu.make_async_copy(source, target, load_sem.at[index])

    def element_loads(i):
        return [
            load(hidden_ref.at[i], elements.at[0], 0),
            load(totals_ref.at[i, BACK], elements.at[1], 1),
            load(totals_ref.at[i, OUTPUT], elements.at[2], 2),
        ]

    first_loads = [load(cot_ref, cots, 3), load(tokens_ref, tokens, 4)] + [
        load(context_ref.at[i], rows_at(context, i, length), 5 + i) for i in range(batch)
    ]
    for copy in element_loads(0) + first_loads:
        copy.start()

    def weight_load(ref, step):
        slot = step % 2
        return pltpu.make_async_copy(
            rows_at(ref, step, CHUNK),
            weight_rows.at[slot, :, pl.ds(0, ref.shape[1])],
            row_sem.at[slot],
        )

    out_steps, in_steps = out_ref.shape[0] // CHUNK, in_ref.shape[0] // CHUNK
    for step in range(2):
        weight_load(out_ref, step).start()
    gain_grads[...] = jnp.zeros_like(gain_grads)
    spot.greet()
    for copy in first_loads:
        copy.wait()

    def result_save(i, target):
        return pltpu.make_async_copy(result.at[i], target.at[i], save_sem.at[i])

    def half_copy(ref, i, side):
        return ref.at[pl.ds(pl.multiple_of(i * length + side * half, 16), half), pl.ds(0, width)]

    def hidden_copy(i):
        place = half_copy(hidden_grads, i, x)
        return spot.send(place, place, hidden_send.at[i], hidden_receive.at[i], CROSS)

    def element_rows(i):
        for copy in element_loads(i):
            copy.wait()

        def elementwise(step, _):
            rows = pl.ds(pl.multiple_of(step * 16, 16), 16)
            value = elements[0, rows, :]
            result[i, rows, :] = (value + elements[2, rows, :]).astype(jnp.bfloat16)
            back, gain_rows = norm_back(
                value, elements[1, rows, :], gain2_ref[...].astype(jnp.float32)
            )
            gain_grads[1:2, :] += jnp.sum(gain_rows, axis=0, keepdims=True)
            total = cots[i, rows, :].astype(jnp.float32) + back
            kept[i, rows, :] = total
            place = pl.ds(pl.multiple_of(i * length + x * half + step * 16, 16), 16)
            hidden_grads[place, :] = total.astype(jnp.bfloat16)
            return 0

        lax.fori_loop(0, half // 16, elementwise, 0)
        hidden_copy(i).start()
        result_save(i, block_out).start()
        if i + 1 < batch:
            for copy in element_loads(i + 1):
                copy.start()

    def hidden_done():
        for i in range(batch):
            hidden_copy(i).wait_send()
            place = half_copy(hidden_grads, i, 1 - x)
            spot.send(place, place, hidden_send.at[i], hidden_receive.at[i], CROSS).wait_recv()

    def context_step(step):
        weight_load(out_ref, step).wait()
        columns = slice(step * CHUNK, (step + 1) * CHUNK)
        context_grads[:, columns] = lax.dot_general(
            hidden_grads[...],
            weight_rows[step % 2, :, :width],
            TRANSPOSED_RIGHT,
            preferred_element_type=jnp.float32,
        ).astype(jnp.bfloat16)
        if step + 2 < out_steps:
            weight_load(out_ref, step + 2).start()

    def out_step(step):
        columns = slice(step * CHUNK, (step + 1) * CHUNK)
        for start in range(0, width, CHUNK):
            out_grads[columns, start : start + CHUNK] = lax.dot_general(
                context[:, columns],
                hidden_grads[:, start : start + CHUNK],
                TRANSPOSED_LEFT,
                preferred_element_type=jnp.float32,
            ).astype(jnp.bfloat16)

    tree = Collect(
        narrow,
        lambda block, side: columns_at(out_grads, block, out_width),
        out_total,
        cores,
        firsts,
        rights,
        lefts,
        tree_send,
        tree_receive,
    )

    def in_start():
        for step in range(2):
            weight_load(in_ref, step).start()

    def tree_start():
        for z in range(line):
            tree.begin(z)
        for copy in head_loads(0):
            copy.start()

    def turns():
        return [(i, shared) for i in range(batch) for shared in range(kv_heads)]

    def head_loads(index):
        i, shared = turns()[index]
        slot = index % 2
        return [
            pltpu.make_async_copy(
                projected_ref.at[i, :, pl.ds(shared * group * features, group * features)],
                queries_f.at[slot],
                head_sem.at[slot, 0],
            )
        ] + [
            pltpu.make_async_copy(
                projected_ref.at[i, :, pl.ds(base + (shared + j * kv_heads) * features, features)],
                shared_f.at[slot, j],
                head_sem.at[slot, 1 + j],
            )
            for j in range(2)
        ]

    def turn_back(grads_in):
        return grads_in * cosine_ref[...] + pltpu.roll(
            grads_in * sine_ref[...], features // 2, 1
        )

    query_gain = lambda: query_gain_ref[...].astype(jnp.float32)
    key_gain = lambda: key_gain_ref[...].astype(jnp.float32)

    def attend_pieces(index):
        i, shared = turns()[index]
        slot = index % 2
        top = i * length

        def columns_of(member):
            return pl.ds(pl.multiple_of(member * features, LANES), features)

        def prepare():
            for copy in head_loads(index):
                copy.wait()
            if index + 1 < len(turns()):
                for copy in head_loads(index + 1):
                    copy.start()
            queries[group] = turned_heads(
                shared_f[slot, 0], key_gain(), cosine_ref[...], sine_ref[...]
            ).astype(jnp.bfloat16)
            queries[group + 1] = shared_f[slot, 1].astype(jnp.bfloat16)
            sums[...] = jnp.zeros_like(sums)

            def one(member):
                queries[member] = turned_heads(
                    queries_f[slot, :, columns_of(member)],
                    query_gain(),
                    cosine_ref[...],
                    sine_ref[...],
                ).astype(jnp.bfloat16)

            for_heads(0, group, 1, one)

        def rows_block(start, stop, seen, at_once, low, high):
            count = stop - start

            def block(member):
                query = queries[pl.ds(member, at_once), start:stop, :].reshape(-1, features)
                keys, values = queries[group, :seen, :], queries[group + 1, :seen, :]
                out_grad = jnp.concatenate(
                    [
                        context_grads[
                            top + start : top + stop,
                            head_columns(shared * group + member + j, features),
                        ]
                        for j in range(at_once)
                    ],
                    axis=0,
                )
                scores = lax.dot_general(
                    keys, query, TRANSPOSED_RIGHT, preferred_element_type=jnp.float32
                )
                shares = softmax(scores * scale)
                share_grads = lax.dot_general(
                    values, out_grad, TRANSPOSED_RIGHT, preferred_element_type=jnp.float32
                )
                sums[1, :seen, :] += jnp.dot(
                    shares.astype(jnp.bfloat16), out_grad, preferred_element_type=jnp.float32
                )
                inner = jnp.sum(shares * share_grads, axis=0, keepdims=True)
                score_grads = (shares * (share_grads - inner)).astype(jnp.bfloat16)
                rows = scale * lax.dot_general(
                    score_grads, keys, TRANSPOSED_LEFT, preferred_element_type=jnp.float32
                )
                query_grads[pl.ds(member, at_once), start:stop, :] = rows.reshape(
                    at_once, count, features
                )
                sums[0, :seen, :] += jnp.dot(
                    score_grads, query, preferred_element_type=jnp.float32
                )

            for_heads(low, high, at_once, block)

        def finish_queries():
            def finish(member):
                back, gain_rows = norm_back(
                    queries_f[slot, :, columns_of(member)],
                    turn_back(query_grads[member]),
                    query_gain(),
                )
                gain_grads[2:3, :features] += jnp.sum(gain_rows, axis=0, keepdims=True)
                grads[top : top + length, head_columns(shared * group + member, features)] = (
                    back.astype(jnp.bfloat16)
                )

            for_heads(0, group, 1, finish)

        def finish_keys():
            back, gain_rows = norm_back(shared_f[slot, 0], turn_back(sums[0] * scale), key_gain())
            gain_grads[3:4, :features] += jnp.sum(gain_rows, axis=0, keepdims=True)
            at = base + shared * features
            grads[top : top + length, at : at + features] = back.astype(jnp.bfloat16)
            at += kv_heads * features
            grads[top : top + length, at : at + features] = sums[1].astype(jnp.bfloat16)

        pieces = [prepare]
        for start, stop, seen, at_once in visible_blocks(length, group):
            share = max(at_once, group // 2)
            for low in range(0, group, share):
                pieces.append(
                    functools.partial(rows_block, start, stop, seen, at_once, low, low + share)
                )
        return pieces + [finish_queries, finish_keys]

    saves = [
        pltpu.make_async_copy(rows_at(grads, i, length), grads_all.at[i], save_sem.at[batch + i])
        for i in range(batch)
    ]

    def normed_step(step):
        weight_load(in_ref, step).wait()
        normed_grads[:, step * CHUNK : (step + 1) * CHUNK] = lax.dot_general(
            grads[...],
            weight_rows[step % 2],
            TRANSPOSED_RIGHT,
            preferred_element_type=jnp.float32,
        ).astype(jnp.bfloat16)
        if step + 2 < in_steps:
            weight_load(in_ref, step + 2).start()

    def normed_copy(i):
        return spot.send(
            half_copy(normed_grads, i, 1 - x),
            normed_other.at[i],
            normed_send.at[i],
            normed_receive.at[i],
            CROSS,
        )

    def input_rows(i):
        normed_copy(i).wait()
        result_save(i, block_out).wait()

        def body(step, _):
            rows = pl.ds(pl.multiple_of(step * 16, 16), 16)
            place = pl.ds(pl.multiple_of(i * length + x * half + step * 16, 16), 16)
            total = normed_grads[place, :width].astype(jnp.float32) + normed_other[
                i, rows, :
            ].astype(jnp.float32)
            back, gain_rows = norm_back(
                tokens[i, rows, :].astype(jnp.float32), total, gain1_ref[...].astype(jnp.float32)
            )
            gain_grads[0:1, :] += jnp.sum(gain_rows, axis=0, keepdims=True)
            kept[i, rows, :] = kept[i, rows, :] + back
            return 0

        lax.fori_loop(0, half // 16, body, 0)
        add_rows(result.at[i], [kept.at[i]])
        result_save(i, input_grad).start()

    opening = [functools.partial(element_rows, i) for i in range(batch)] + [hidden_done]
    opening += [functools.partial(out_step, step) for step in range(out_steps)]
    opening += [tree_start, functools.partial(context_step, 0), tree.cross]
    opening += [functools.partial(context_step, step) for step in range(1, out_steps)]
    opening.append(in_start)
    attending = [piece for index in range(len(turns())) for piece in attend_pieces(index)]
    closing = attending + [copy.start for copy in saves]
    closing += [functools.partial(normed_step, step) for step in range(in_steps)]
    closing += [normed_copy(i).start for i in range(batch)]
    closing += [functools.partial(input_rows, i) for i in range(batch)]
    for piece in opening:
        piece()
    mingle(closing, tree.tasks())
    for i in range(batch):
        result_save(i, input_grad).wait()
    for copy in saves:
        copy.wait()


def run_backward(
    cot,
    totals,
    hidden,
    projected,
    context,
    in_full,
    out_full,
    tokens,
    gains,
    tables,
    fsdp_count,
    kv_heads,
):
    line = fsdp_count // PLANE
    batch, half, width = tokens.shape
    length = 2 * half
    features = gains[2].shape[1]
    heads = out_full.shape[0] // features
    group = heads // kv_heads
    in_width, out_depth = in_full.shape[1], out_full.shape[0]
    out_shape = (out_depth, width // fsdp_count)
    anywhere = pl.BlockSpec(memory_space=pl.ANY)
    inside = pl.BlockSpec(memory_space=pltpu.VMEM)
    shape = lambda *dims: jax.ShapeDtypeStruct(dims, jnp.bfloat16)
    vmem = lambda *dims: pltpu.VMEM(dims, jnp.bfloat16)
    wide = lambda *dims: pltpu.VMEM(dims, jnp.float32)
    sem = lambda *dims: pltpu.SemaphoreType.DMA(dims)
    rows = batch * length
    return pl.pallas_call(
        functools.partial(backward_kernel, line, heads, kv_heads),
        out_shape=(
            shape(batch, half, width),
            shape(batch, half, width),
            shape(batch, length, in_width),
            jax.ShapeDtypeStruct(out_shape, jnp.float32),
            jax.ShapeDtypeStruct((8, width), jnp.float32),
        ),
        in_specs=[anywhere] * 8 + [inside] * 6,
        out_specs=(anywhere, anywhere, anywhere, inside, inside),
        scratch_shapes=[
            wide(3, half, width),
            vmem(batch, half, width),
            vmem(batch, half, width),
            wide(batch, half, width),
            vmem(batch, half, width),
            vmem(rows, out_depth),
            vmem(rows, width),
            vmem(rows, max(out_depth, width)),
            vmem(rows, in_width),
            vmem(batch, half, width),
            vmem(2, CHUNK, max(width, in_width)),
            wide(2, length, group * features),
            wide(2, 2, length, features),
            vmem(group + 2, length, features),
            wide(group, length, features),
            wide(2, length, features),
            vmem(out_depth, width),
            *collect_scratch(line, out_shape),
            sem(5 + batch),
            sem(2),
            sem(2, 3),
            sem(2 * batch),
            sem(batch),
            sem(batch),
            sem(batch),
            sem(batch),
        ],
        compiler_params=pltpu.CompilerParams(
            collective_id=3, has_side_effects=True, vmem_limit_bytes=62 * MIB
        ),
    )(
        cot,
        totals,
        hidden,
        projected,
        context,
        in_full,
        out_full,
        tokens,
        *gains,
        *tables,
    )


def gradients_kernel(
    line,
    normed,
    grads,
    gains_ref,
    xe_ref,
    ce_ref,
    act_ref,
    dgate_ref,
    dup_ref,
    in_total,
    gains_all,
    gate_total,
    up_total,
    down_total,
    parts,
    cores,
    firsts,
    rights,
    lefts,
    tree_send,
    tree_receive,
    gain_send,
    gain_receive,
    gain_local,
    wide_rows,
    slim_rows,
    gate_sum,
    up_sum,
    down_sum,
    load_sem,
    save_sem,
):
    narrow, spot = Spot(line, False), Spot(line, True)
    experts, count, _ = xe_ref.shape
    share = wide_rows.shape[1]
    turns = count // share
    pieces = [
        (expert, kind, turn)
        for expert in range(experts)
        for kind in range(2)
        for turn in range(turns)
    ]

    def loads(index):
        expert, kind, turn = pieces[index]
        slot = index % 2
        rows = pl.ds(turn * share, share)
        slim = (dgate_ref, dup_ref) if kind == 0 else (act_ref,)
        return [
            pltpu.make_async_copy(
                (xe_ref, ce_ref)[kind].at[expert, rows], wide_rows.at[slot], load_sem.at[slot, 0]
            )
        ] + [
            pltpu.make_async_copy(
                ref.at[expert, rows], slim_rows.at[slot, i], load_sem.at[slot, 1 + i]
            )
            for i, ref in enumerate(slim)
        ]

    def saves(expert, kind):
        pairs = ((gate_sum, gate_total), (up_sum, up_total))
        if kind:
            return [pltpu.make_async_copy(down_sum, down_total.at[expert], save_sem.at[2])]
        return [
            pltpu.make_async_copy(source, target.at[expert], save_sem.at[i])
            for i, (source, target) in enumerate(pairs)
        ]

    for copy in loads(0):
        copy.start()
    spot.greet()
    gains = Spread(
        spot,
        gains_ref,
        lambda block, half: gains_all.at[block, half],
        gain_send,
        gain_receive,
        gain_local.at[0],
    )
    gains.begin()
    depth, width = in_total.shape
    tree = Collect(
        narrow,
        lambda block, half: rows_at(parts, block, depth),
        in_total,
        cores,
        firsts,
        rights,
        lefts,
        tree_send,
        tree_receive,
    )
    chunk = PLANE * depth

    def plane(step, _):
        z = lax.rem(narrow.z + 1 + step, line)
        columns = pl.ds(pl.multiple_of(z * chunk, LANES), chunk)
        for start in range(0, width, CHUNK):
            parts[pl.ds(pl.multiple_of(z * chunk, 16), chunk), start : start + CHUNK] = (
                lax.dot_general(
                    normed[:, columns],
                    grads[:, start : start + CHUNK],
                    TRANSPOSED_LEFT,
                    preferred_element_type=jnp.float32,
                ).astype(jnp.bfloat16)
            )
        tree.begin(z)
        return 0

    lax.fori_loop(0, line, plane, 0)

    def piece(index):
        expert, kind, turn = pieces[index]
        slot = index % 2
        for copy in loads(index):
            copy.wait()
        if index + 1 < len(pieces):
            for copy in loads(index + 1):
                copy.start()
        if turn == 0 and expert:
            for copy in saves(expert - 1, kind):
                copy.wait()
        size = wide_rows.shape[2] // 4

        def add(target, place, left, right):
            product = lax.dot_general(
                left, right, TRANSPOSED_LEFT, preferred_element_type=jnp.float32
            )
            if turn:
                product = target[place] + product
            target[place] = product

        def part(step, _):
            at = pl.ds(pl.multiple_of(step * size, LANES), size)
            if kind:
                add(down_sum, (slice(None), at), slim_rows[slot, 0], wide_rows[slot, :, at])
            else:
                for i, target in enumerate((gate_sum, up_sum)):
                    add(target, (at, slice(None)), wide_rows[slot, :, at], slim_rows[slot, i])
            return 0

        lax.fori_loop(0, 4, part, 0)
        if turn == turns - 1:
            for copy in saves(expert, kind):
                copy.start()

    tree.cross()
    work = tree.tasks()
    steps = list(range(1, gains.steps()))
    filler = list(range(len(pieces)))
    while work or filler:
        for _ in range(2 if len(filler) > len(work) else 1):
            if filler:
                piece(filler.pop(0))
        if work:
            work.pop(0)()
        if steps:
            gains.step(steps.pop(0))
    gains.finish()
    for copy in saves(experts - 1, 0) + saves(experts - 1, 1):
        copy.wait()


def run_gradients(normed, grads, gains, expert_rows, fsdp_count):
    line = fsdp_count // PLANE
    width = grads.shape[1]
    experts, count, depth = expert_rows[0].shape
    units = expert_rows[2].shape[2]
    share = 2 * CHUNK if count % (2 * CHUNK) == 0 else count // (2 * line)
    shape = (normed.shape[1] // fsdp_count, width)
    sends, receives = spread_count(line, True)
    inside = pl.BlockSpec(memory_space=pltpu.VMEM)
    anywhere = pl.BlockSpec(memory_space=pl.ANY)
    return pl.pallas_call(
        functools.partial(gradients_kernel, line),
        out_shape=(
            jax.ShapeDtypeStruct(shape, jnp.float32),
            jax.ShapeDtypeStruct((fsdp_count, 2, *gains.shape), jnp.float32),
            jax.ShapeDtypeStruct((experts, depth, units), jnp.float32),
            jax.ShapeDtypeStruct((experts, depth, units), jnp.float32),
            jax.ShapeDtypeStruct((experts, units, depth), jnp.float32),
        ),
        in_specs=[inside, inside] + [anywhere] * 6,
        out_specs=(inside,) + (anywhere,) * 4,
        scratch_shapes=[
            pltpu.VMEM((normed.shape[1], width), jnp.bfloat16),
            *collect_scratch(line, shape),
            pltpu.SemaphoreType.DMA((sends,)),
            pltpu.SemaphoreType.DMA((receives,)),
            pltpu.SemaphoreType.DMA((1,)),
            pltpu.VMEM((2, share, depth), jnp.bfloat16),
            pltpu.VMEM((2, 2, share, units), jnp.bfloat16),
            pltpu.VMEM((depth, units), jnp.float32),
            pltpu.VMEM((depth, units), jnp.float32),
            pltpu.VMEM((units, depth), jnp.float32),
            pltpu.SemaphoreType.DMA((2, 3)),
            pltpu.SemaphoreType.DMA((3,)),
        ],
        compiler_params=pltpu.CompilerParams(
            collective_id=4, has_side_effects=True, vmem_limit_bytes=60 * MIB
        ),
    )(normed, grads, gains, *expert_rows)


def experts_kernel(
    line,
    slots,
    own_ref,
    cot_first,
    cot_ref,
    info_ref,
    gate_ref,
    up_ref,
    down_ref,
    all_ref,
    cot_later,
    total_ref,
    xe_all,
    ce_all,
    act_all,
    dgate_all,
    dup_all,
    part,
    cores,
    seconds,
    firsts,
    ends,
    hidden_w,
    down_w,
    x_rows,
    c_rows,
    xe,
    ce,
    acts,
    dgates,
    dups,
    hidden_grads,
    picks,
    weigh,
    rows,
    stage,
    inbox,
    outbox,
    summed,
    rows_send,
    rows_receive,
    rows_late_send,
    rows_late_receive,
    rows_local,
    cot_send,
    cot_receive,
    cot_late_send,
    cot_late_receive,
    cot_local,
    load_sem,
    save_sem,
    stage_sem,
    inbox_sem,
    outbox_sem,
    total_sem,
    weight_sem,
    core_receive,
    second_receive,
    first_receive,
    end_receive,
):
    spot = Spot(line, True)
    z, core = spot.z, spot.core
    cot_semaphores = (cot_send, cot_receive, cot_late_send, cot_late_receive, cot_local)
    tree_semaphores = (rows_send, rows_receive, rows_late_send, rows_late_receive, rows_local)
    batch, half, width = own_ref.shape
    length = 2 * half
    units = down_ref.shape[1]
    groups = batch * line
    weights = [
        pltpu.make_async_copy(source, target, weight_sem.at[i])
        for i, (source, target) in enumerate(
            [(down_ref, down_w)]
            + [(gate_ref.at[e], hidden_w.at[e, :, pl.ds(0, units)]) for e in range(2)]
            + [(up_ref.at[e], hidden_w.at[e, :, pl.ds(units, units)]) for e in range(2)]
        )
    ]
    for copy in weights:
        copy.start()
    rows[...] = jnp.zeros_like(rows)
    spot.greet()

    def half_of(ref, index):
        return rows_at(ref, index, half)

    trees = []
    for i in range(batch):
        place = lambda block, start, size, i=i: all_ref.at[
            i, block, pl.ds(pl.multiple_of(start, 16), size)
        ]
        trees.append(rows_spread(spot, own_ref.at[i], place, half, tree_semaphores, i))
    for i in range(1, batch):
        place = lambda block, start, size, i=i: cot_later.at[
            i - 1, block, pl.ds(pl.multiple_of(start, 16), size)
        ]
        trees[i] += rows_spread(spot, cot_ref.at[i], place, half, cot_semaphores, i - 1)
    run_trees(trees[0])
    for tree in sum(trees[1:], []):
        tree.begin()
    for copy in weights:
        copy.wait()

    plane_of = functools.partial(plane_in_turn, line)

    def load_group(group, member, start):
        at = lax.div(group, line)
        sequence = plane_of(group) * PLANE + member
        slot = member % 2
        def copy(i, source, target):
            return pltpu.make_async_copy(source, target.at[slot], load_sem.at[i, slot])

        own = copy(0, all_ref.at[at, sequence], x_rows)
        if start:
            own.start()
            later = cot_later.at[jnp.maximum(at - 1, 0), sequence]
            when(at == 0, lambda: copy(1, cot_first.at[sequence], c_rows).start())
            when(at > 0, lambda: copy(1, later, c_rows).start())
        else:
            own.wait()
            copy(1, cot_first.at[sequence], c_rows).wait()

    def saves(group):
        to = lambda ref, expert: rows_at(ref.at[expert], group, PLANE * slots)
        pairs = ((xe, xe_all), (ce, ce_all), (acts, act_all), (dgates, dgate_all), (dups, dup_all))
        return [
            pltpu.make_async_copy(source.at[expert], to(target, expert), save_sem.at[2 * i + expert])
            for i, (source, target) in enumerate(pairs)
            for expert in range(2)
        ]

    def staged(unit, y, mine):
        slot = y * 2 + mine
        if mine:
            return pltpu.make_async_copy(stage.at[slot], part.at[unit, y], stage_sem.at[slot])
        return spot.send(
            stage.at[slot], cores.at[unit, y], stage_sem.at[slot], core_receive.at[unit, y], CORE
        )

    def combine(unit, y):
        for mine in range(2):
            member = y * 2 + (core if mine else 1 - core)
            for start in range(0, width, CHUNK):
                stage[y * 2 + mine, :, start : start + CHUNK] = lax.dot_general(
                    picks[member],
                    rows[member, :, start : start + CHUNK],
                    TRANSPOSED_LEFT,
                    preferred_element_type=jnp.float32,
                ).astype(jnp.bfloat16)
            staged(unit, y, mine).start()

    def pick(group, member):
        slot = member % 2
        load_group(group, member, False)
        if member + 1 < PLANE:
            load_group(group, member + 1, True)
        sequence = plane_of(group) * PLANE + member
        info = info_ref[lax.div(group, line) * line * PLANE + sequence]
        places = lax.broadcasted_iota(jnp.int32, (2 * LANES, length), 0)
        lower = places < LANES
        ranks = jnp.where(lower, info[0:1], info[1:2] + float(LANES)).astype(jnp.int32)
        some = jnp.where(lower, info[0:1], info[1:2]) >= 0.0
        hot = jnp.logical_and(ranks == places, some)
        chosen = hot.astype(jnp.float32).astype(jnp.bfloat16)
        picks[member] = chosen
        shares = jnp.where(hot, jnp.where(lower, info[2:3], info[3:4]), 0.0)
        column = jnp.sum(shares, axis=1, keepdims=True)
        here = pl.ds(member * slots, slots)
        for expert in range(2):
            weigh[expert, here, :] = jnp.broadcast_to(
                column[expert * LANES : expert * LANES + slots], (slots, LANES)
            )
        for source, target in ((x_rows, xe), (c_rows, ce)):
            for start in range(0, width, CHUNK):
                selected = jnp.dot(
                    chosen,
                    source[slot, :, start : start + CHUNK],
                    preferred_element_type=jnp.float32,
                ).astype(jnp.bfloat16)
                for expert in range(2):
                    target[expert, here, start : start + CHUNK] = selected[
                        expert * LANES : expert * LANES + slots
                    ]

    def keep(expert, product, start):
        at = pl.ds(expert * LANES, slots)
        for one in range(PLANE):
            rows[one, at, start : start + CHUNK] = product[one * slots : (one + 1) * slots].astype(
                jnp.bfloat16
            )

    def forward(expert):
        hidden = jnp.dot(xe[expert], hidden_w[expert], preferred_element_type=jnp.float32)
        gate, up = hidden[:, :units], hidden[:, units:]
        sigmoid = jax.nn.sigmoid(gate)
        silu = gate * sigmoid
        scale = weigh[expert, :, 0:1]
        acts[expert] = (silu * up * scale).astype(jnp.bfloat16)
        act_grads = scale * lax.dot_general(
            ce[expert], down_w[expert], TRANSPOSED_RIGHT, preferred_element_type=jnp.float32
        )
        gate_grads = (act_grads * up * (sigmoid * (1.0 + gate * (1.0 - sigmoid)))).astype(
            jnp.bfloat16
        )
        up_grads = (act_grads * silu).astype(jnp.bfloat16)
        dgates[expert] = gate_grads
        dups[expert] = up_grads
        hidden_grads[expert, :, :units] = gate_grads
        hidden_grads[expert, :, units:] = up_grads
        for start in range(0, width, CHUNK):
            keep(
                expert,
                jnp.dot(
                    acts[expert],
                    down_w[expert, :, start : start + CHUNK],
                    preferred_element_type=jnp.float32,
                ),
                start,
            )

    def backward(expert):
        for start in range(0, width, CHUNK):
            keep(
                expert,
                lax.dot_general(
                    hidden_grads[expert],
                    hidden_w[expert, start : start + CHUNK, :],
                    TRANSPOSED_RIGHT,
                    preferred_element_type=jnp.float32,
                ),
                start,
            )

    units_all = 2 * groups

    def inside(unit):
        return jnp.logical_and(unit >= 0, unit < units_all)

    def ready(unit):
        @pl.when(inside(unit))
        def _():
            for y in range(2):
                staged(unit, y, 1).wait()
                staged(unit, y, 0).wait_send()
                place, semaphore = cores.at[unit, y], core_receive.at[unit, y]
                spot.send(place, place, outbox_sem.at[0], semaphore, CORE).wait_recv()

    def done(unit, tensor, into):
        into(summed)
        copy = pltpu.make_async_copy(
            summed, total_ref.at[lax.div(unit, 2 * line), tensor], total_sem.at[0]
        )
        copy.start()
        copy.wait()

    sums = Sums(
        spot,
        lambda unit, y: part.at[unit, y],
        lambda unit, y: cores.at[unit, y],
        (seconds, firsts, ends),
        inbox,
        outbox,
        (inbox_sem, outbox_sem, second_receive, first_receive, end_receive),
        lambda unit: plane_of(lax.div(jnp.maximum(unit, 0), 2)),
        inside,
        ready,
        done,
        2,
    )

    def tree_turn(half_step, last):
        for i in range(1, batch):
            turn = half_step - (i - 1) * 2 * line
            if last:
                when(turn == 2 * line - 1, lambda: [tree.finish() for tree in trees[i]])
            else:
                inner = jnp.logical_and(turn >= 0, turn < 2 * line - 1)
                when(inner, lambda: [tree.step(turn + 1) for tree in trees[i]])

    def begin_pick(group):
        load_group(group, 0, True)

    begin_pick(0)
    for member in range(PLANE):
        pick(0, member)

    def step_body(step, _):
        busy = step < groups
        more = step + 1 < groups
        for parity in range(2):
            half_step = step * 2 + parity
            tree_turn(half_step, False)
            sums.retire(half_step, parity)
            tasks = sums.tasks(half_step, parity)
            pieces = []
            for expert in range(2):
                pieces.append(functools.partial((forward, backward)[parity], expert))
            if parity == 0:
                pieces.append(lambda: [copy.start() for copy in saves(step)])
            for y in range(2):
                pieces.append(functools.partial(combine, half_step, y))
            pieces = [functools.partial(when, busy, piece) for piece in pieces]
            if parity == 1:

                def prepare():
                    for copy in saves(step):
                        copy.wait()
                    begin_pick(step + 1)

                tree_end = functools.partial(tree_turn, half_step, True)
                pieces += [tree_end, functools.partial(when, more, prepare)]
                for member in range(PLANE):
                    pieces.append(
                        functools.partial(when, more, functools.partial(pick, step + 1, member))
                    )
            sums.weave(tasks, pieces)
        return 0

    half_steps = sums.half_steps(units_all)
    lax.fori_loop(0, -(-half_steps // 2), step_body, 0)
    end = -(-half_steps // 2) * 2
    for parity in range(2):
        sums.retire(jnp.int32(end + parity), parity)
    for copy in saves(groups - 1):
        copy.wait()


def run_experts(rows, cot_first, cot, info, w_gate, w_up, w_down, capacity, fsdp_count):
    line = fsdp_count // PLANE
    batch, half, width = rows.shape
    length = 2 * half
    units = w_down.shape[1]
    slots = -(-capacity // 16) * 16
    groups = batch * line
    count = groups * PLANE * slots
    taken = PLANE * slots
    shape = lambda *dims: jax.ShapeDtypeStruct(dims, jnp.bfloat16)
    block = (half, width)
    anywhere = pl.BlockSpec(memory_space=pl.ANY)
    vmem = lambda *dims: pltpu.VMEM(dims, jnp.bfloat16)
    sem = lambda *dims: pltpu.SemaphoreType.DMA(dims)
    return pl.pallas_call(
        functools.partial(experts_kernel, line, slots),
        out_shape=(
            shape(batch, fsdp_count, length, width),
            shape(max(batch - 1, 1), fsdp_count, length, width),
            jax.ShapeDtypeStruct((batch, 2, *block), jnp.float32),
            shape(2, count, width),
            shape(2, count, width),
            shape(2, count, units),
            shape(2, count, units),
            shape(2, count, units),
            shape(2 * groups, 2, length, width),
            shape(2 * groups, 2, length, width),
            shape(2 * groups, 2, *block),
            shape(2 * groups, *block),
            shape(2 * groups, 2, *block),
        ),
        in_specs=[
            anywhere,
            anywhere,
            anywhere,
            pl.BlockSpec(memory_space=pltpu.VMEM),
            anywhere,
            anywhere,
            anywhere,
        ],
        out_specs=(anywhere,) * 13,
        scratch_shapes=[
            vmem(2, width, 2 * units),
            vmem(2, units, width),
            vmem(2, length, width),
            vmem(2, length, width),
            vmem(2, taken, width),
            vmem(2, taken, width),
            vmem(2, taken, units),
            vmem(2, taken, units),
            vmem(2, taken, units),
            vmem(2, taken, 2 * units),
            vmem(PLANE, 2 * LANES, length),
            pltpu.VMEM((2, taken, LANES), jnp.float32),
            vmem(PLANE, 2 * LANES, width),
            vmem(PLANE, length, width),
            vmem(12, *block),
            vmem(10, *block),
            pltpu.VMEM(block, jnp.float32),
            *rows_semaphores(batch, line),
            *rows_semaphores(max(batch - 1, 1), line),
            sem(2, 2),
            sem(10),
            sem(PLANE),
            sem(12),
            sem(10),
            sem(1),
            sem(5),
            sem(2 * groups, 2),
            sem(2 * groups, 2),
            sem(2 * groups),
            sem(2 * groups, 2),
        ],
        compiler_params=pltpu.CompilerParams(
            collective_id=2, has_side_effects=True, vmem_limit_bytes=60 * MIB
        ),
    )(rows, cot_first, cot, info, w_gate, w_up, w_down)[2:8]


def packed_picks(routes, gates):
    length = routes.shape[2]
    packed = jnp.concatenate([routes[:, 0].astype(jnp.float32), gates[:, 0]], axis=-1)
    packed = jnp.swapaxes(packed, 1, 2).reshape(-1, length)
    return jnp.pad(packed, ((0, 0), (0, -length % LANES)))


def slot_info(packed, batch, top, length, local_experts):
    fsdp_count = packed.shape[0]
    packed = packed[..., :length].reshape(fsdp_count, batch, 1, 2 * top, length)
    packed = jnp.swapaxes(packed, 0, 1)
    experts = lax.axis_index(FSDP) * local_experts + jnp.arange(local_experts, dtype=jnp.int32)
    same = packed[..., :top, :].astype(jnp.int32) == experts[:, None, None]
    hot = jnp.any(same, axis=3)
    shares = jnp.sum(jnp.where(same, packed[..., top:, :], 0.0), axis=3)
    position = jnp.arange(length)
    upper = (position[:, None] < position[None, :]).astype(jnp.bfloat16)
    rank = jnp.dot(
        hot.astype(jnp.bfloat16).reshape(-1, length), upper, preferred_element_type=jnp.float32
    )
    rank = jnp.where(hot, rank.reshape(hot.shape), -1.0)
    return jnp.concatenate([rank, shares], axis=2).reshape(-1, 2 * local_experts, length)


def gathered_layer(
    tokens,
    cotangent,
    norm1_gain,
    w_query,
    key_projection_weight,
    value_projection_weight,
    query_gain,
    key_gain,
    w_out,
    norm2_gain,
    w_gate,
    w_up,
    w_down,
    routes,
    gates,
):
    batch_count = tokens.shape[0]
    model_width = tokens.shape[3]
    sequence_length = routes.shape[2]
    half_length = tokens.shape[2]
    top_count = routes.shape[3]
    head_features = query_gain.shape[0]
    local_experts = w_gate.shape[0]
    fsdp_count = lax.axis_size(FSDP)
    all_experts = local_experts * fsdp_count
    capacity = 7 * top_count * sequence_length // (6 * all_experts)
    query_width = w_query.shape[1]
    kv_width = key_projection_weight.shape[1]
    kv_heads = kv_width // head_features
    cosine_table, sine_values = rotary_tables(sequence_length, head_features)
    weight_in = jnp.concatenate([w_query, key_projection_weight, value_projection_weight], axis=1)
    half_signs = jnp.where(jnp.arange(head_features) < head_features // 2, -1.0, 1.0)
    tables = (cosine_table[:, 0], sine_values[:, 0] * half_signs)
    gains = [gain[None, :] for gain in (norm1_gain, norm2_gain, query_gain, key_gain)]
    cot_first, in_full, out_full, picks, normed, projected, contexts, hidden, second = run_forward(
        tokens[:, 0],
        cotangent[:, 0],
        weight_in,
        w_out,
        packed_picks(routes, gates),
        gains,
        tables,
        fsdp_count,
        kv_heads,
    )
    info = slot_info(picks, batch_count, top_count, sequence_length, local_experts)
    totals, *expert_rows = run_experts(
        second, cot_first, cotangent[:, 0], info, w_gate, w_up, w_down, capacity, fsdp_count
    )
    block_out, input_grad, projected_grads, out_sum, gain_grads = run_backward(
        cotangent[:, 0],
        totals,
        hidden,
        projected,
        contexts,
        in_full,
        out_full,
        tokens[:, 0],
        gains,
        tables,
        fsdp_count,
        kv_heads,
    )
    rows = batch_count * sequence_length
    in_sum, gains_all, *expert_grads = run_gradients(
        normed.reshape(rows, -1),
        projected_grads.reshape(rows, -1),
        gain_grads,
        expert_rows,
        fsdp_count,
    )
    gains_sum = jnp.sum(gains_all, axis=(0, 1))
    return (
        block_out[:, None],
        input_grad[:, None],
        gains_sum[0],
        in_sum[:, :query_width],
        in_sum[:, query_width : query_width + kv_width],
        in_sum[:, query_width + kv_width :],
        gains_sum[2, :head_features],
        gains_sum[3, :head_features],
        out_sum,
        gains_sum[1],
        *expert_grads,
    )


def shards(*arrays):
    tokens, routes, w_gate = arrays[0], arrays[13], arrays[10]
    fsdp_count = lax.axis_size(FSDP)
    gathered = fsdp_count * routes.shape[2] * tokens.shape[3] * 2
    fits = gathered <= 24 * MIB and fsdp_count % PLANE == 0 and lax.axis_size(TP) == 2
    if fits and w_gate.shape[0] == 2:
        return gathered_layer(*arrays)
    return exchanged_layer(*arrays)


def solution(mesh):
    in_specs = (
        P(None, "fsdp", "tp", None),
        P(None, "fsdp", "tp", None),
        P(),
        P("fsdp", "tp"),
        P("fsdp", "tp"),
        P("fsdp", "tp"),
        P(),
        P(),
        P("tp", "fsdp"),
        P(),
        P("fsdp", None, "tp"),
        P("fsdp", None, "tp"),
        P("fsdp", "tp", None),
        P(None, "fsdp", None, None),
        P(None, "fsdp", None, None),
    )
    out_specs = (
        P(None, "fsdp", "tp", None),
        P(None, "fsdp", "tp", None),
        P(),
        P("fsdp", "tp"),
        P("fsdp", "tp"),
        P("fsdp", "tp"),
        P(),
        P(),
        P("tp", "fsdp"),
        P(),
        P("fsdp", None, "tp"),
        P("fsdp", None, "tp"),
        P("fsdp", "tp", None),
    )
    return jax.shard_map(shards, mesh=mesh, in_specs=in_specs, out_specs=out_specs, check_vma=False)
```

```python
import functools

import jax
import jax.numpy as jnp
from jax import lax
from jax.experimental import pallas as pl
from jax.experimental.pallas import tpu as pltpu
from jax.sharding import PartitionSpec as P

BLOCK = 256


EPSILON = 1e-06
ROPE_BASE = 1000000.0
MASKED = -1e30
TILE_PICKS = 128


def rms_scale(row_block, gain_row):
    return (
        row_block
        * lax.rsqrt(jnp.mean(row_block * row_block, axis=-1, keepdims=True) + EPSILON)
        * gain_row
    )


def rotary_tables(sequence_length, head_width):
    half_width = head_width // 2
    inverse = ROPE_BASE ** (-2.0 * jnp.arange(half_width, dtype=jnp.float32) / head_width)
    angles = jnp.arange(sequence_length, dtype=jnp.float32)[:, None] * inverse[None, :]
    cosine_table = jnp.concatenate([jnp.cos(angles), jnp.cos(angles)], axis=-1)[:, None, :]
    sine_values = jnp.concatenate([jnp.sin(angles), jnp.sin(angles)], axis=-1)[:, None, :]
    return (cosine_table, sine_values)


def rotate(head_rows, cosine_table, sine_values):
    half_width = head_rows.shape[-1] // 2
    turned = jnp.concatenate([-head_rows[..., half_width:], head_rows[..., :half_width]], axis=-1)
    return head_rows * cosine_table + turned * sine_values


def prepare_heads(projected, gain_row, cosine_table, sine_values):
    return rotate(rms_scale(projected, gain_row), cosine_table, sine_values)


def swiglu(gate_act, up_act):
    return jax.nn.silu(gate_act) * up_act


def slot_tables(route_rows, gate_rows, expert_count, capacity):
    sequence_length = route_rows.shape[0]
    top_count = route_rows.shape[1]
    pick_count = sequence_length * top_count
    tile_count = pick_count // TILE_PICKS
    flat_routes = route_rows.reshape(-1)
    onehot = (flat_routes[:, None] == jnp.arange(expert_count, dtype=jnp.int32)[None, :]).astype(
        jnp.bfloat16
    )
    tiles = onehot.reshape(tile_count, TILE_PICKS, expert_count)
    positions = jnp.arange(TILE_PICKS, dtype=jnp.int32)
    lower = (positions[None, :] < positions[:, None]).astype(jnp.bfloat16)
    within = jnp.einsum("ij,bje->bie", lower, tiles, preferred_element_type=jnp.float32)
    tile_totals = jnp.sum(tiles.astype(jnp.float32), axis=1)
    offsets = jnp.cumsum(tile_totals, axis=0) - tile_totals
    before = within + offsets[:, None, :]
    slot_rank = jnp.sum(before * tiles.astype(jnp.float32), axis=-1).reshape(-1).astype(jnp.int32)
    slot_index = flat_routes * capacity + slot_rank
    pick_ids = jnp.arange(pick_count, dtype=jnp.int32) // top_count
    slot_owner = (
        jnp.full((expert_count * capacity,), sequence_length, jnp.int32)
        .at[slot_index]
        .set(pick_ids)
    )
    slot_weight = (
        jnp.zeros((expert_count * capacity,), jnp.float32).at[slot_index].set(gate_rows.reshape(-1))
    )
    return (slot_index, slot_owner, slot_weight)


def exchanged_layer(
    tokens,
    cotangent,
    norm1_gain,
    w_query,
    key_projection_weight,
    value_projection_weight,
    query_gain,
    key_gain,
    w_out,
    norm2_gain,
    w_gate,
    w_up,
    w_down,
    routes,
    gates,
):
    batch_count = tokens.shape[0]
    model_width = tokens.shape[3]
    sequence_length = routes.shape[2]
    top_count = routes.shape[3]
    head_features = query_gain.shape[0]
    local_experts = w_gate.shape[0]
    fsdp_count = lax.axis_size("fsdp")
    all_experts = local_experts * fsdp_count
    capacity = 7 * top_count * sequence_length // (6 * all_experts)
    query_heads = w_query.shape[1] // head_features
    kv_heads = key_projection_weight.shape[1] // head_features
    group_size = query_heads // kv_heads
    score_scale = head_features ** (-0.5)
    cosine_table, sine_values = rotary_tables(sequence_length, head_features)
    block_ids = jnp.arange(sequence_length, dtype=jnp.int32) // BLOCK
    visible = (block_ids[None, :] <= block_ids[:, None])[None, None]
    first_gain = norm1_gain.astype(jnp.float32)
    second_gain = norm2_gain.astype(jnp.float32)
    query_factor_scale = query_gain.astype(jnp.float32)
    key_scale = key_gain.astype(jnp.float32)
    zero_row = jnp.zeros((1, model_width), jnp.bfloat16)
    buffer_shape = (fsdp_count, local_experts, capacity, model_width)

    def masked_scores(query_fourfold, key_rows):
        raw_scores = (
            jnp.einsum(
                "qcgd,kcd->cgqk", query_fourfold, key_rows, preferred_element_type=jnp.float32
            )
            * score_scale
        )
        return jnp.where(visible, raw_scores, MASKED)

    def prep_heads(projected, gain_row):
        return prepare_heads(projected, gain_row, cosine_table, sine_values)

    gain_sums = (
        jnp.zeros((model_width,), jnp.float32),
        jnp.zeros((model_width,), jnp.float32),
        jnp.zeros((head_features,), jnp.float32),
        jnp.zeros((head_features,), jnp.float32),
    )
    expert_grads = (
        jnp.zeros(w_gate.shape, jnp.float32),
        jnp.zeros(w_up.shape, jnp.float32),
        jnp.zeros(w_down.shape, jnp.float32),
    )
    attn_grads = tuple(
        (
            jnp.zeros(weight_part.shape, jnp.float32)
            for weight_part in (w_query, key_projection_weight, value_projection_weight, w_out)
        )
    )
    outputs = []
    input_grads = []
    for batch_index in range(batch_count):
        query_full, key_full, value_full, out_full = (
            lax.all_gather(w_query, "fsdp", axis=0, tiled=True),
            lax.all_gather(key_projection_weight, "fsdp", axis=0, tiled=True),
            lax.all_gather(value_projection_weight, "fsdp", axis=0, tiled=True),
            lax.all_gather(w_out, "fsdp", axis=1, tiled=True),
        )
        own_rows = tokens[batch_index, 0].astype(jnp.float32)
        own_cot = cotangent[batch_index, 0]
        route_rows = routes[batch_index, 0]
        gate_rows = gates[batch_index, 0]
        first_normed = rms_scale(own_rows, first_gain).astype(jnp.bfloat16)
        normed_all = lax.all_gather(first_normed, "tp", axis=0, tiled=True)
        query_projected = jnp.dot(
            normed_all, query_full, preferred_element_type=jnp.float32
        ).reshape(sequence_length, query_heads, head_features)
        key_projected = jnp.dot(normed_all, key_full, preferred_element_type=jnp.float32).reshape(
            sequence_length, kv_heads, head_features
        )
        value_row_list = (
            jnp.dot(normed_all, value_full, preferred_element_type=jnp.float32)
            .astype(jnp.bfloat16)
            .reshape(sequence_length, kv_heads, head_features)
        )
        query_rot = prep_heads(query_projected, query_factor_scale).astype(jnp.bfloat16)
        key_rot = prep_heads(key_projected, key_scale).astype(jnp.bfloat16)
        query_fourfold = query_rot.reshape(sequence_length, kv_heads, group_size, head_features)
        scores = masked_scores(query_fourfold, key_rot)
        row_max = jnp.max(scores, axis=-1, keepdims=True)
        exp_scores = jnp.exp(scores - row_max)
        totals = jnp.sum(exp_scores, axis=-1, keepdims=True)
        log_total = row_max + jnp.log(totals)
        prob_rows = (exp_scores / totals).astype(jnp.bfloat16)
        context = (
            jnp.einsum(
                "cgqk,kcd->qcgd", prob_rows, value_row_list, preferred_element_type=jnp.float32
            )
            .astype(jnp.bfloat16)
            .reshape(sequence_length, query_heads * head_features)
        )
        attn_own = lax.psum_scatter(
            jnp.dot(context, out_full, preferred_element_type=jnp.float32).astype(jnp.bfloat16),
            "tp",
            scatter_dimension=0,
            tiled=True,
        ).astype(jnp.float32)
        hidden_own = own_rows + attn_own
        second_normed = rms_scale(hidden_own, second_gain).astype(jnp.bfloat16)
        normed_two, cot_all = (
            lax.all_gather(second_normed, "tp", axis=0, tiled=True),
            lax.all_gather(own_cot, "tp", axis=0, tiled=True),
        )
        slot_index, slot_owner, slot_weight = slot_tables(
            route_rows, gate_rows, all_experts, capacity
        )
        padded_rows = jnp.concatenate([normed_two, zero_row], axis=0)
        send_rows = padded_rows[slot_owner].reshape(buffer_shape)
        expert_in = lax.all_to_all(send_rows, "fsdp", split_axis=0, concat_axis=0, tiled=True)
        gate_act = jnp.einsum(
            "sekd,edf->sekf", expert_in, w_gate, preferred_element_type=jnp.float32
        )
        up_act = jnp.einsum("sekd,edf->sekf", expert_in, w_up, preferred_element_type=jnp.float32)
        act_rows = swiglu(gate_act, up_act).astype(jnp.bfloat16)
        expert_out = jnp.einsum(
            "sekf,efd->sekd", act_rows, w_down, preferred_element_type=jnp.float32
        )
        returned = lax.all_to_all(
            expert_out.astype(jnp.bfloat16), "fsdp", split_axis=0, concat_axis=0, tiled=True
        ).astype(expert_out.dtype)
        picked = returned.reshape(all_experts * capacity, model_width)[slot_index].reshape(
            sequence_length, top_count, model_width
        )
        moe_part = jnp.sum(picked * gate_rows[:, :, None], axis=1)
        moe_own = lax.psum_scatter(
            moe_part.astype(jnp.bfloat16), "tp", scatter_dimension=0, tiled=True
        ).astype(jnp.float32)
        outputs.append((hidden_own + moe_own).astype(jnp.bfloat16))
        cot_padded = jnp.concatenate([cot_all, zero_row], axis=0)
        send_grads = (
            (slot_weight[:, None] * cot_padded[slot_owner])
            .astype(jnp.bfloat16)
            .reshape(buffer_shape)
        )
        out_grads = lax.all_to_all(send_grads, "fsdp", split_axis=0, concat_axis=0, tiled=True)
        act_grads = jnp.einsum(
            "sekd,efd->sekf", out_grads, w_down, preferred_element_type=jnp.float32
        )
        _, swiglu_back = jax.vjp(swiglu, gate_act, up_act)
        gate_grads, up_grads = swiglu_back(act_grads)
        gate_grads = gate_grads.astype(jnp.bfloat16)
        up_grads = up_grads.astype(jnp.bfloat16)
        expert_grads = (
            expert_grads[0]
            + jnp.einsum(
                "sekd,sekf->edf", expert_in, gate_grads, preferred_element_type=jnp.float32
            ),
            expert_grads[1]
            + jnp.einsum("sekd,sekf->edf", expert_in, up_grads, preferred_element_type=jnp.float32),
            expert_grads[2]
            + jnp.einsum("sekf,sekd->efd", act_rows, out_grads, preferred_element_type=jnp.float32),
        )
        input_part = jnp.einsum(
            "sekf,edf->sekd", gate_grads, w_gate, preferred_element_type=jnp.float32
        ) + jnp.einsum("sekf,edf->sekd", up_grads, w_up, preferred_element_type=jnp.float32)
        input_back = lax.all_to_all(
            input_part.astype(jnp.bfloat16), "fsdp", split_axis=0, concat_axis=0, tiled=True
        ).astype(input_part.dtype)
        normed_grads = jnp.sum(
            input_back.reshape(all_experts * capacity, model_width)[slot_index].reshape(
                sequence_length, top_count, model_width
            ),
            axis=1,
        )
        normed_own = lax.psum_scatter(
            normed_grads.astype(jnp.bfloat16), "tp", scatter_dimension=0, tiled=True
        ).astype(jnp.float32)
        _, second_back = jax.vjp(rms_scale, hidden_own, second_gain)
        hidden_part, second_gain_grad = second_back(normed_own)
        hidden_grad = own_cot.astype(jnp.float32) + hidden_part
        attn_grad_all = lax.all_gather(hidden_grad.astype(jnp.bfloat16), "tp", axis=0, tiled=True)
        out_weight_grad = jnp.einsum(
            "th,td->hd", context, attn_grad_all, preferred_element_type=jnp.float32
        )
        context_grad = (
            jnp.einsum("td,hd->th", attn_grad_all, out_full, preferred_element_type=jnp.float32)
            .astype(jnp.bfloat16)
            .reshape(sequence_length, kv_heads, group_size, head_features)
        )
        exp_again = jnp.exp(masked_scores(query_fourfold, key_rot) - log_total)
        probs_again = exp_again.astype(jnp.bfloat16)
        prob_grads = jnp.einsum(
            "qcgd,kcd->cgqk", context_grad, value_row_list, preferred_element_type=jnp.float32
        )
        value_grads = (
            jnp.einsum(
                "cgqk,qcgd->kcd", probs_again, context_grad, preferred_element_type=jnp.float32
            )
            .astype(jnp.bfloat16)
            .reshape(sequence_length, kv_heads * head_features)
        )
        score_grads = (
            exp_again * (prob_grads - jnp.sum(exp_again * prob_grads, axis=-1, keepdims=True))
        ).astype(jnp.bfloat16)
        query_rot_grads = (
            jnp.einsum("cgqk,kcd->qcgd", score_grads, key_rot, preferred_element_type=jnp.float32)
            * score_scale
        ).reshape(sequence_length, query_heads, head_features)
        key_rot_grads = (
            jnp.einsum(
                "cgqk,qcgd->kcd", score_grads, query_fourfold, preferred_element_type=jnp.float32
            )
            * score_scale
        )
        _, query_back = jax.vjp(prep_heads, query_projected, query_factor_scale)
        query_proj_grads, query_gain_grad = query_back(query_rot_grads)
        _, key_back = jax.vjp(prep_heads, key_projected, key_scale)
        key_proj_grads, key_gain_grad = key_back(key_rot_grads)
        query_proj_grads = query_proj_grads.astype(jnp.bfloat16).reshape(
            sequence_length, query_heads * head_features
        )
        key_proj_grads = key_proj_grads.astype(jnp.bfloat16).reshape(
            sequence_length, kv_heads * head_features
        )
        first_normed_grads = (
            jnp.einsum(
                "tq,dq->td", query_proj_grads, query_full, preferred_element_type=jnp.float32
            )
            + jnp.einsum("tq,dq->td", key_proj_grads, key_full, preferred_element_type=jnp.float32)
            + jnp.einsum("tq,dq->td", value_grads, value_full, preferred_element_type=jnp.float32)
        )
        weight_parts = (
            jnp.einsum(
                "td,tq->dq", normed_all, query_proj_grads, preferred_element_type=jnp.float32
            ),
            jnp.einsum("td,tq->dq", normed_all, key_proj_grads, preferred_element_type=jnp.float32),
            jnp.einsum("td,tq->dq", normed_all, value_grads, preferred_element_type=jnp.float32),
            out_weight_grad,
        )
        first_own = lax.psum_scatter(
            first_normed_grads.astype(jnp.bfloat16), "tp", scatter_dimension=0, tiled=True
        ).astype(jnp.float32)
        _, first_back = jax.vjp(rms_scale, own_rows, first_gain)
        row_part, first_gain_grad = first_back(first_own)
        input_grads.append((hidden_grad + row_part).astype(jnp.bfloat16))
        gain_sums = (
            gain_sums[0] + first_gain_grad,
            gain_sums[1] + second_gain_grad,
            gain_sums[2] + query_gain_grad,
            gain_sums[3] + key_gain_grad,
        )
        attn_grads = jax.tree.map(
            jnp.add,
            attn_grads,
            (
                lax.psum_scatter(weight_parts[0], "fsdp", scatter_dimension=0, tiled=True),
                lax.psum_scatter(weight_parts[1], "fsdp", scatter_dimension=0, tiled=True),
                lax.psum_scatter(weight_parts[2], "fsdp", scatter_dimension=0, tiled=True),
                lax.psum_scatter(weight_parts[3], "fsdp", scatter_dimension=1, tiled=True),
            ),
        )
    summed = lax.psum((gain_sums[0], gain_sums[1], gain_sums[2], gain_sums[3]), ("fsdp", "tp"))
    block_out = jnp.stack(outputs)[:, None]
    input_grad = jnp.stack(input_grads)[:, None]
    return (
        block_out,
        input_grad,
        summed[0],
        attn_grads[0],
        attn_grads[1],
        attn_grads[2],
        summed[2],
        summed[3],
        attn_grads[3],
        summed[1],
        expert_grads[0],
        expert_grads[1],
        expert_grads[2],
    )


MESH = pl.DeviceIdType.MESH
FSDP, TP = "fsdp", "tp"
PLANE = 4
LANES = 128
MIB = 1 << 20
RIGHT, LEFT, FIRST, SECOND, CORE, CROSS = range(6)
TRANSPOSED_LEFT = (((0,), (0,)), ((), ()))
TRANSPOSED_RIGHT = (((1,), (1,)), ((), ()))
OUTPUT, BACK = range(2)
CHUNK = 512


class Spot:
    def __init__(self, line, wide, turned=True):
        self.line = line
        self.wide = wide
        self.turned = turned
        self.planes = 4 if wide else 2
        index = lax.axis_index(FSDP)
        self.x = lax.axis_index(TP)
        self.z = lax.div(index, PLANE)
        self.y = lax.rem(lax.div(index, 2), 2)
        self.core = lax.rem(index, 2)

    def side(self, core, first, second):
        flip_y, flip_x = first, second
        if self.wide and self.turned:
            flip_y = (1 - core) * first + core * second
            flip_x = core * first + (1 - core) * second
        return self.y + flip_y * (1 - 2 * self.y), self.x + flip_x * (1 - 2 * self.x)

    def block(self, core, first, second, z):
        y, x = self.side(core, first, second)
        return z * PLANE + y * 2 + core, x

    def device(self, kind):
        if kind == RIGHT:
            return self.block(self.core, 0, 0, self.z + 1)
        if kind == LEFT:
            return self.block(self.core, 0, 0, self.z - 1)
        if kind == CORE:
            return self.block(1 - self.core, 0, 0, self.z)
        if kind == CROSS:
            return self.block(self.core, 0, 0, self.z)[0], 1 - self.x
        return self.block(self.core, int(kind == FIRST), int(kind == SECOND), self.z)

    def kinds(self):
        return (FIRST, SECOND, CORE) if self.wide else (FIRST, CORE)

    def number(self, first, second, z):
        return (second * 2 + first) * self.line + z

    def order(self, step):
        if isinstance(step, int) and step == 0:
            return [(self.z, None)]
        return [(self.z - step, self.z - step >= 0), (self.z + step, self.z + step < self.line)]

    def greet(self):
        barrier = pltpu.get_barrier_semaphore()

        def signal(kind):
            pl.semaphore_signal(barrier, inc=1, device_id=self.device(kind), device_id_type=MESH)

        for kind in self.kinds():
            signal(kind)
        when(self.z + 1 < self.line, lambda: signal(RIGHT))
        when(self.z > 0, lambda: signal(LEFT))
        around = (self.z + 1 < self.line).astype(jnp.int32) + (self.z > 0).astype(jnp.int32)
        pl.semaphore_wait(barrier, len(self.kinds()) + around)

    def send(self, source, target, send_sem, receive_sem, kind):
        return pltpu.make_async_remote_copy(
            src_ref=source,
            dst_ref=target,
            send_sem=send_sem,
            recv_sem=receive_sem,
            device_id=self.device(kind),
            device_id_type=MESH,
        )


def when(condition, action):
    def run():
        action()

    if condition is None or condition is True:
        run()
    elif condition is not False:
        pl.when(condition)(run)


class Spread:
    def __init__(self, spot, source, slot, send, receive, local):
        self.spot = spot
        self.slot = slot
        self.source = source
        self.sends = send
        self.receives = receive
        self.mine = pltpu.make_async_copy(source, slot(*spot.block(spot.core, 0, 0, spot.z)), local)

    def copy(self, first, second, z, kind, own=False):
        spot = self.spot
        place = self.slot(*spot.block(spot.core, first, second, z))
        number = spot.number(first, second, z)
        arrival = {
            RIGHT: number,
            LEFT: number,
            FIRST: spot.number(1, 0, z),
            SECOND: spot.number(first, 1, z),
            CORE: spot.planes * spot.line + number,
        }[kind]
        departure = {RIGHT: 0, LEFT: 1, FIRST: 2, SECOND: 3, CORE: 5}[kind] * spot.line + number
        source = self.source if own else place
        return spot.send(source, place, self.sends.at[departure], self.receives.at[arrival], kind)

    def arrived(self, first, second, z, other=False):
        spot = self.spot
        core = 1 - spot.core if other else spot.core
        place = self.slot(*spot.block(core, first, second, z))
        number = spot.number(first, second, z) + (spot.planes * spot.line if other else 0)
        spot.send(place, place, self.sends.at[0], self.receives.at[number], CORE).wait_recv()

    def steps(self):
        return self.spot.line + (3 if self.spot.wide else 1)

    def begin(self):
        spot = self.spot
        z = spot.z
        when(z + 1 < spot.line, lambda: self.copy(0, 0, z, RIGHT, True).start())
        when(z > 0, lambda: self.copy(0, 0, z, LEFT, True).start())
        for kind in spot.kinds():
            self.copy(0, 0, z, kind, True).start()
        self.mine.start()

    def step(self, step):
        spot = self.spot
        line, z = spot.line, spot.z

        def reached(away, action):
            inside = jnp.logical_and(away >= 0, away < line)
            when(jnp.logical_and(inside, z - away >= 0), lambda: action(z - away, True))
            when(
                jnp.logical_and(inside, jnp.logical_and(away > 0, z + away < line)),
                lambda: action(z + away, False),
            )

        def along(zz, from_left):
            self.arrived(0, 0, zz)
            if from_left:
                when(z + 1 < line, lambda: self.copy(0, 0, zz, RIGHT).start())
            else:
                when(z > 0, lambda: self.copy(0, 0, zz, LEFT).start())
            for kind in spot.kinds():
                self.copy(0, 0, zz, kind).start()

        def firsts(zz, _):
            self.arrived(1, 0, zz)
            if spot.wide:
                self.copy(1, 0, zz, SECOND).start()
            self.copy(1, 0, zz, CORE).start()

        def lasts(first):
            def action(zz, _):
                self.arrived(first, 1, zz)
                self.copy(first, 1, zz, CORE).start()

            return action

        step = jnp.asarray(step, jnp.int32)
        reached(step, along)
        reached(step - 1, firsts)
        if spot.wide:
            reached(step - 2, lasts(0))
            reached(step - 3, lasts(1))

    def finish(self):
        spot = self.spot
        z = spot.z

        def body(zz, _):
            when(
                jnp.logical_and(z + 1 < spot.line, zz <= z),
                lambda: self.copy(0, 0, zz, RIGHT).wait_send(),
            )
            when(jnp.logical_and(z > 0, zz >= z), lambda: self.copy(0, 0, zz, LEFT).wait_send())
            self.copy(0, 0, zz, FIRST).wait_send()
            for second in range(2 if spot.wide else 1):
                for first in (0, 1):
                    if spot.wide and not second:
                        self.copy(first, 0, zz, SECOND).wait_send()
                    self.copy(first, second, zz, CORE).wait_send()
                    self.arrived(first, second, zz, other=True)
            return 0

        lax.fori_loop(0, spot.line, body, 0)
        self.mine.wait()


class LateSpread(Spread):
    def steps(self):
        return self.spot.line + 2

    def copy(self, first, second, z, kind, own=False):
        spot = self.spot
        place = self.slot(*spot.block(spot.core, first, second, z))
        number = spot.number(first, second, z)
        arrival = {
            RIGHT: number,
            LEFT: number,
            FIRST: spot.number(1, 0, z),
            SECOND: spot.number(first, 1, z),
            CORE: spot.planes * spot.line + number,
        }[kind]
        departure = {RIGHT: 0, LEFT: 4, CORE: 8, FIRST: 12, SECOND: 13}[kind] * spot.line + number
        source = self.source if own else place
        return spot.send(source, place, self.sends.at[departure], self.receives.at[arrival], kind)

    def along_both(self, first, second, own=False):
        spot = self.spot
        z = spot.z
        when(z + 1 < spot.line, lambda: self.copy(first, second, z, RIGHT, own).start())
        when(z > 0, lambda: self.copy(first, second, z, LEFT, own).start())
        self.copy(first, second, z, CORE, own).start()

    def begin(self):
        self.copy(0, 0, self.spot.z, FIRST, True).start()
        self.copy(0, 0, self.spot.z, SECOND, True).start()
        self.along_both(0, 0, True)
        self.mine.start()

    def step(self, step):
        spot = self.spot
        line, z = spot.line, spot.z
        step = jnp.asarray(step, jnp.int32)

        def passed(first, second, zz, kind, more):
            self.arrived(first, second, zz)
            when(more, lambda: self.copy(first, second, zz, kind).start())
            self.copy(first, second, zz, CORE).start()

        for first, second in ((0, 0), (1, 0), (0, 1), (1, 1)):
            away = step - (first + second)

            def here():
                self.arrived(first, second, z)
                if first and not second:
                    self.copy(1, 0, z, SECOND).start()
                self.along_both(first, second)

            if first or second:
                when(away == 0, here)
            far = jnp.logical_and(away > 0, away < line)
            when(
                jnp.logical_and(far, z - away >= 0),
                lambda: passed(first, second, z - away, RIGHT, z + 1 < line),
            )
            when(
                jnp.logical_and(far, z + away < line),
                lambda: passed(first, second, z + away, LEFT, z > 0),
            )

    def finish(self):
        spot = self.spot
        z = spot.z

        def body(zz, _):
            for second in (0, 1):
                for first in (0, 1):
                    when(
                        jnp.logical_and(z + 1 < spot.line, zz <= z),
                        lambda: self.copy(first, second, zz, RIGHT).wait_send(),
                    )
                    when(
                        jnp.logical_and(z > 0, zz >= z),
                        lambda: self.copy(first, second, zz, LEFT).wait_send(),
                    )
                    self.copy(first, second, zz, CORE).wait_send()
                    self.arrived(first, second, zz, other=True)
            return 0

        lax.fori_loop(0, spot.line, body, 0)
        self.copy(0, 0, z, FIRST).wait_send()
        for first in (0, 1):
            self.copy(first, 0, z, SECOND).wait_send()
        self.mine.wait()


def rows_spread(spot, source, place, rows, semaphores, at):
    late = late_rows(rows)
    early = rows - late
    send, receive, late_send, late_receive, local = semaphores

    def slot(start, size):
        return lambda block, side: place(block, side * rows + start, size)

    return [
        Spread(
            spot,
            source.at[pl.ds(0, early)],
            slot(0, early),
            send.at[at],
            receive.at[at],
            local.at[at, 0],
        ),
        LateSpread(
            spot,
            source.at[pl.ds(early, late)],
            slot(early, late),
            late_send.at[at],
            late_receive.at[at],
            local.at[at, 1],
        ),
    ]


def late_rows(rows):
    return max(16, round(rows * 2 / 9 / 16) * 16)


def rows_semaphores(batch, line):
    counts = (*spread_count(line, True), 15 * line, 8 * line, 2)
    return [pltpu.SemaphoreType.DMA((batch, count)) for count in counts]


def run_trees(trees):
    for tree in trees:
        tree.begin()

    def body(step, _):
        for tree in trees:
            tree.step(step)
        return 0

    lax.fori_loop(1, max(tree.steps() for tree in trees), body, 0)
    for tree in trees:
        tree.finish()


def spread_count(line, wide):
    return (9 if wide else 7) * line, (8 if wide else 4) * line


def mingle(work, others):
    for index, piece in enumerate(work):
        piece()
        for other in others[
            index * len(others) // len(work) : (index + 1) * len(others) // len(work)
        ]:
            other()


def rows_at(ref, index, size):
    return ref.at[pl.ds(pl.multiple_of(index * size, 16), size)]


def columns_at(ref, index, size):
    return ref.at[:, pl.ds(pl.multiple_of(index * size, LANES), size)]


def norm_rows(target, source, gain):
    def body(step, _):
        rows = pl.ds(pl.multiple_of(step * 16, 16), 16)
        value = source[rows, :].astype(jnp.float32)
        target[rows, :] = rms_scale(value, gain[...].astype(jnp.float32)).astype(target.dtype)
        return 0

    lax.fori_loop(0, target.shape[0] // 16, body, 0)


def turned_heads(value, gain, cosine, sine):
    normed = rms_scale(value, gain)
    return normed * cosine + pltpu.roll(normed, normed.shape[-1] // 2, 1) * sine


def visible_blocks(length, group):
    blocks = []
    for start in range(0, length, BLOCK):
        stop = min(start + BLOCK, length)
        heads = max(1, BLOCK // (stop - start))
        while group % heads:
            heads -= 1
        blocks.append((start, stop, stop, heads))
    return blocks


def softmax(scores):
    raised = jnp.exp(scores - jnp.max(scores, axis=0, keepdims=True))
    return raised * (1.0 / jnp.sum(raised, axis=0, keepdims=True))


def for_heads(low, high, heads, body):
    turns = 2 if heads == 1 and (high - low) % 2 == 0 else 1

    def turn(step, _):
        for i in range(turns):
            body(low + (step * turns + i) * heads)
        return 0

    count = (high - low) // (heads * turns)
    if count == 1:
        turn(0, 0)
    else:
        lax.fori_loop(0, count, turn, 0)


def head_columns(head, features):
    return pl.ds(pl.multiple_of(head * features, LANES), features)


def forward_kernel(
    line,
    heads,
    kv_heads,
    tokens_ref,
    cot_ref,
    in_ref,
    out_ref,
    picks_ref,
    gain1_ref,
    gain2_ref,
    query_gain_ref,
    key_gain_ref,
    cosine_ref,
    sine_ref,
    cot_all,
    in_all,
    out_all,
    picks_all,
    normed_all,
    projected_all,
    context_all,
    hidden_all,
    second_all,
    in_w,
    out_w,
    tokens,
    normed,
    projected,
    context,
    queries,
    keys,
    values,
    mixed,
    mixed_other,
    hidden,
    second,
    narrow_send,
    narrow_receive,
    cot_send,
    cot_receive,
    cot_late_send,
    cot_late_receive,
    cot_local,
    local,
    token_send,
    token_receive,
    mixed_send,
    mixed_receive,
    save_sem,
):
    cot_semaphores = (cot_send, cot_receive, cot_late_send, cot_late_receive, cot_local)
    batch, half, width = tokens_ref.shape
    length = 2 * half
    depth, out_width = in_ref.shape[0], out_ref.shape[1]
    features = query_gain_ref.shape[1]
    narrow = Spot(line, False)
    spot = Spot(line, True, turned=False)
    x = spot.x
    spot.greet()
    slots = [
        (picks_ref, lambda block, side: picks_all.at[block]),
        (in_ref, lambda block, side: rows_at(in_w, block, depth)),
        (out_ref, lambda block, side: columns_at(out_w, block, out_width)),
    ]
    weights = [
        Spread(narrow, source, slot, narrow_send.at[i], narrow_receive.at[i], local.at[i])
        for i, (source, slot) in enumerate(slots)
    ]
    place = lambda block, start, size: cot_all.at[block, pl.ds(pl.multiple_of(start, 16), size)]
    cots = rows_spread(spot, cot_ref.at[0], place, half, cot_semaphores, 0)
    early, late = weights[:2], weights[2]
    for tree in early:
        tree.begin()

    def token_copies(i):
        place = rows_at(tokens.at[i], x, half)
        return (
            pltpu.make_async_copy(tokens_ref.at[i], place, local.at[3 + i]),
            spot.send(tokens_ref.at[i], place, token_send.at[i], token_receive.at[i], CROSS),
        )

    for i in range(batch):
        for copy in token_copies(i):
            copy.start()
    def steps(step, _):
        for tree in early:
            tree.step(step)
        return 0

    lax.fori_loop(1, late.steps(), steps, 0)
    late.begin()
    for tree in cots:
        tree.begin()
    for i in range(batch):
        mine, other = token_copies(i)
        mine.wait()
        other.wait_send()
        place = rows_at(tokens.at[i], 1 - x, half)
        spot.send(place, place, token_send.at[i], token_receive.at[i], CROSS).wait_recv()
    for i in range(batch):
        norm_rows(normed.at[i], tokens.at[i], gain1_ref)
    for tree in early:
        tree.finish()

    def save(source, target, index):
        return pltpu.make_async_copy(source, target, save_sem.at[index])

    saves = [save(in_w, in_all, 0), save(out_w, out_all, 1)]
    saves[0].start()

    def project(i, start, stop):
        for at in range(start, stop, CHUNK):
            projected[i, :, at : at + CHUNK] = jnp.dot(
                normed[i], in_w[:, at : at + CHUNK], preferred_element_type=jnp.float32
            )

    scale = features ** (-0.5)

    group = heads // kv_heads

    def prepare_keys(i):
        base = heads * features
        for head in range(kv_heads):
            at = base + head * features
            keys[head] = turned_heads(
                projected[i, :, at : at + features],
                key_gain_ref[...].astype(jnp.float32),
                cosine_ref[...],
                sine_ref[...],
            ).astype(jnp.bfloat16)
            at = base + (kv_heads + head) * features
            values[head] = projected[i, :, at : at + features].astype(jnp.bfloat16)

    def prepare_queries(i, shared):
        def prepare(member):
            columns = head_columns(shared * group + member, features)
            queries[member] = turned_heads(
                projected[i, :, columns], query_gain_ref[...].astype(jnp.float32), cosine_ref[...], sine_ref[...]
            ).astype(jnp.bfloat16)

        for_heads(0, group, 1, prepare)

    def attend(i, shared, start, stop, seen, at_once, low, high):
        count = stop - start

        def block(member):
            query = queries[pl.ds(member, at_once), start:stop, :].reshape(-1, features)
            scores = lax.dot_general(
                keys[shared, :seen, :],
                query,
                TRANSPOSED_RIGHT,
                preferred_element_type=jnp.float32,
            )
            rows = lax.dot_general(
                softmax(scores * scale).astype(jnp.bfloat16),
                values[shared, :seen, :],
                TRANSPOSED_LEFT,
                preferred_element_type=jnp.float32,
            ).astype(jnp.bfloat16)
            for j in range(at_once):
                columns = head_columns(shared * group + member + j, features)
                context[i, start:stop, columns] = rows[j * count : (j + 1) * count]

        for_heads(low, high, at_once, block)

    def mixed_copy(i):
        return spot.send(
            rows_at(mixed.at[i], 1 - x, half),
            mixed_other.at[i],
            mixed_send.at[i],
            mixed_receive.at[i],
            CROSS,
        )

    def mix(i, start, stop):
        for at in range(start, stop, CHUNK):
            mixed[i, :, at : at + CHUNK] = jnp.dot(
                context[i], out_w[:, at : at + CHUNK], preferred_element_type=jnp.float32
            ).astype(jnp.bfloat16)
        if stop == width:
            mixed_copy(i).start()

    def close(i):
        mixed_copy(i).wait()
        add_rows(
            hidden.at[i],
            [rows_at(tokens.at[i], x, half), rows_at(mixed.at[i], x, half), mixed_other.at[i]],
        )
        norm_rows(second.at[i], hidden.at[i], gain2_ref)

    def late_done():
        late.finish()
        saves[1].start()

    def steps_of(trees, low, high):
        return [
            functools.partial(tree.step, step)
            for step in range(low, high)
            for tree in trees
            if step < tree.steps()
        ]

    in_width = in_w.shape[1]
    parts = lambda size: [(at, min(at + 2 * CHUNK, size)) for at in range(0, size, 2 * CHUNK)]
    opening, middle, closing = [], [], []
    for i in range(batch):
        opening += [functools.partial(project, i, *part) for part in parts(in_width)]
        middle.append(functools.partial(prepare_keys, i))
        for shared in range(kv_heads):
            middle.append(functools.partial(prepare_queries, i, shared))
            for start, stop, seen, at_once in visible_blocks(length, group):
                share = max(at_once, group // 2)
                for low in range(0, group, share):
                    middle.append(
                        functools.partial(
                            attend, i, shared, start, stop, seen, at_once, low, low + share
                        )
                    )
        closing += [functools.partial(mix, i, *part) for part in parts(width)]
    closing += [functools.partial(close, i) for i in range(batch)]
    last = cots[0].steps()
    mingle(opening + middle, steps_of([late] + cots, 1, last))
    late_done()
    for piece in closing:
        piece()

    saves += [
        save(source, target, 2 + i)
        for i, (source, target) in enumerate(
            [
                (normed, normed_all),
                (projected, projected_all),
                (context, context_all),
                (hidden, hidden_all),
                (second, second_all),
            ]
        )
    ]
    for copy in saves[2:]:
        copy.start()
    for tree in cots:
        tree.finish()
    for copy in saves:
        copy.wait()


def run_forward(tokens, cot, weight_in, weight_out, picks, gains, tables, fsdp_count, kv_heads):
    line = fsdp_count // PLANE
    batch, half, width = tokens.shape
    length = 2 * half
    features = gains[2].shape[1]
    heads = weight_out.shape[0] // features
    in_shape = (weight_in.shape[0] * fsdp_count, weight_in.shape[1])
    out_shape = (weight_out.shape[0], weight_out.shape[1] * fsdp_count)
    narrow = spread_count(line, False)
    anywhere = pl.BlockSpec(memory_space=pl.ANY)
    inside = pl.BlockSpec(memory_space=pltpu.VMEM)
    shape = lambda dims, kind=jnp.bfloat16: jax.ShapeDtypeStruct(dims, kind)
    vmem = lambda *dims: pltpu.VMEM(dims, jnp.bfloat16)
    sem = lambda *dims: pltpu.SemaphoreType.DMA(dims)
    kept = (
        ((batch, length, width), jnp.bfloat16),
        ((batch, length, weight_in.shape[1]), jnp.float32),
        ((batch, length, heads * features), jnp.bfloat16),
        ((batch, half, width), jnp.float32),
        ((batch, half, width), jnp.bfloat16),
    )
    return pl.pallas_call(
        functools.partial(forward_kernel, line, heads, kv_heads),
        out_shape=(
            shape((fsdp_count, length, width)),
            shape(in_shape),
            shape(out_shape),
            shape((fsdp_count, *picks.shape), picks.dtype),
            *(shape(*one) for one in kept),
        ),
        in_specs=[anywhere] * 5 + [inside] * 6,
        out_specs=(anywhere,) * 9,
        scratch_shapes=[
            vmem(*in_shape),
            vmem(*out_shape),
            vmem(batch, length, width),
            *(pltpu.VMEM(*one) for one in kept[:3]),
            vmem(heads // kv_heads, length, features),
            vmem(kv_heads, length, features),
            vmem(kv_heads, length, features),
            vmem(batch, length, width),
            vmem(batch, half, width),
            *(pltpu.VMEM(*one) for one in kept[3:]),
            sem(3, narrow[0]),
            sem(3, narrow[1]),
            *rows_semaphores(1, line),
            sem(3 + batch),
            sem(batch),
            sem(batch),
            sem(batch),
            sem(batch),
            sem(7),
        ],
        compiler_params=pltpu.CompilerParams(
            collective_id=1, has_side_effects=True, vmem_limit_bytes=60 * MIB
        ),
    )(tokens, cot, weight_in, weight_out, picks, *gains, *tables)


def add_rows(target, sources):
    def body(step, _):
        rows = pl.ds(pl.multiple_of(step * 16, 16), 16)
        total = sources[0][rows, :].astype(jnp.float32)
        for source in sources[1:]:
            total = total + source[rows, :].astype(jnp.float32)
        target[rows, :] = total.astype(target.dtype)
        return 0

    lax.fori_loop(0, target.shape[0] // 16, body, 0)


class Collect:
    def __init__(self, spot, part, total, cores, firsts, rights, lefts, send, receive):
        self.spot = spot
        self.part = part
        self.total = total
        self.places = {CORE: cores, FIRST: firsts, RIGHT: rights, LEFT: lefts}
        line = spot.line
        self.base = {CORE: 0, FIRST: 2 * line, RIGHT: 3 * line, LEFT: 4 * line}
        self.sends = send
        self.receives = receive

    def own(self, first, z):
        return self.part(*self.spot.block(self.spot.core, first, 0, z))

    def copy(self, kind, first, z):
        spot = self.spot
        number = first * spot.line + z if kind == CORE else z
        source = self.part(*spot.block(1 - spot.core, first, 0, z)) if kind == CORE else self.own(first, z)
        at = self.base[kind] + number
        return spot.send(
            source, self.places[kind].at[number], self.sends.at[at], self.receives.at[at], kind
        )

    def arrived(self, kind, number):
        place = self.places[kind].at[number]
        at = self.base[kind] + number
        self.spot.send(place, place, self.sends.at[0], self.receives.at[at], CORE).wait_recv()
        return place

    def begin(self, z):
        for first in (1, 0):
            self.copy(CORE, first, z).start()

    def to_first(self, z):
        add_rows(self.own(1, z), [self.own(1, z), self.arrived(CORE, self.spot.line + z)])
        self.copy(FIRST, 1, z).start()

    def summands(self, z):
        return [self.own(0, z), self.arrived(CORE, z), self.arrived(FIRST, z)]

    def cross(self):
        for step in reversed(range(self.spot.line)):
            for zz, valid in self.spot.order(step):
                when(valid, functools.partial(self.to_first, zz))

    def onward(self, kind, zz):
        spot = self.spot
        sources = self.summands(zz)
        target = self.own(0, zz)
        behind = spot.z > 0 if kind == RIGHT else spot.z + 1 < spot.line
        when(behind, lambda: add_rows(target, sources + [self.arrived(kind, zz)]))
        when(jnp.logical_not(behind), lambda: add_rows(target, sources))
        self.copy(kind, 0, zz).start()

    def last(self):
        z, line = self.spot.z, self.spot.line
        sources = self.summands(z)

        def end(kinds):
            add_rows(self.total, sources + [self.arrived(kind, z) for kind in kinds])

        when(z == 0, lambda: end([LEFT]))
        when(z == line - 1, lambda: end([RIGHT]))
        when(jnp.logical_and(z > 0, z < line - 1), lambda: end([RIGHT, LEFT]))

    def finish(self):
        spot = self.spot
        for zz in range(spot.line):
            for first in (0, 1):
                self.copy(CORE, first, zz).wait_send()
            self.copy(FIRST, 1, zz).wait_send()
            when(zz > spot.z, lambda: self.copy(RIGHT, 0, zz).wait_send())
            when(zz < spot.z, lambda: self.copy(LEFT, 0, zz).wait_send())

    def tasks(self):
        spot = self.spot
        work = []
        for step in reversed(range(1, spot.line)):
            for kind, (zz, valid) in zip((LEFT, RIGHT), spot.order(step)):
                action = functools.partial(self.onward, kind, zz)
                work.append(functools.partial(when, valid, action))
        return work + [self.last, self.finish]


def collect_scratch(line, shape):
    counts = (2 * line, line, line, line)
    return [pltpu.VMEM((count, *shape), jnp.bfloat16) for count in counts] + [
        pltpu.SemaphoreType.DMA((5 * line,)),
        pltpu.SemaphoreType.DMA((5 * line,)),
    ]


BOXES = 6


def plane_in_turn(line, group):
    turn = lax.rem(group, line)
    step = lax.div(turn, 2)
    return jnp.where(lax.rem(turn, 2) == 0, step, line - 1 - step)


class Sums:
    def __init__(
        self, spot, half, parts, cores, places, inbox, outbox, semaphores, late, plane, inside, ready, done, turns
    ):
        self.spot = spot
        self.half = half
        (
            self.late_ends,
            self.late_seconds,
            self.late_firsts,
            self.late_inbox,
            self.late_outbox,
            self.late_sums,
            self.late_inbox_sem,
            self.late_outbox_sem,
            self.late_sums_sem,
            self.late_end_receive,
            self.late_second_receive,
            self.late_first_receive,
        ) = late
        self.parts = parts
        self.cores = cores
        self.seconds, self.firsts, self.ends = places
        self.inbox = inbox
        self.outbox = outbox
        (
            self.inbox_sem,
            self.outbox_sem,
            self.second_receive,
            self.first_receive,
            self.end_receive,
        ) = semaphores
        self.plane = plane
        self.inside = inside
        self.ready = ready
        self.done = done
        self.turns = turns

    def second_slot(self, turn, first):
        return turn * 2 + first

    def first_slot(self, turn):
        return 2 * self.turns + turn

    def end_slot(self, turn, kind):
        return 3 * self.turns + turn * 2 + kind

    def free(self, unit, turn, first):
        pass

    def second_send(self, unit, turn, first):
        slot = self.second_slot(turn, first)
        return self.spot.send(
            self.outbox.at[slot],
            self.seconds.at[unit, first],
            self.outbox_sem.at[slot],
            self.second_receive.at[unit, first],
            SECOND,
        )

    def first_send(self, unit, turn):
        slot = self.first_slot(turn)
        return self.spot.send(
            self.outbox.at[slot],
            self.firsts.at[unit],
            self.outbox_sem.at[slot],
            self.first_receive.at[unit],
            FIRST,
        )

    def end_send(self, unit, turn, kind):
        slot = self.end_slot(turn, kind)
        return self.spot.send(
            self.outbox.at[slot],
            self.ends.at[unit, kind],
            self.outbox_sem.at[slot],
            self.end_receive.at[unit, kind],
            kind,
        )

    def received(self, place, semaphore):
        self.spot.send(place, place, self.outbox_sem.at[0], semaphore, CORE).wait_recv()

    def sources(self, unit, first, second):
        y, x = self.spot.side(self.spot.core, first, second)
        rows = pl.ds(pl.multiple_of(x * self.half, 16), self.inbox.shape[1])
        return [self.parts(unit, y).at[rows], self.cores(unit, y).at[rows]]

    def summands(self, unit):
        return self.sources(unit, 0, 0) + [self.seconds.at[unit, 0], self.firsts.at[unit]]

    def load(self, source, slot):
        return pltpu.make_async_copy(source, self.inbox.at[slot], self.inbox_sem.at[slot])

    def add(self, target, base, numbers):
        add_rows(target, [self.inbox.at[base + i] for i in numbers])

    def end_roles(self, half_step, delay):
        z, line = self.spot.z, self.spot.line
        unit = half_step - 3 - delay
        valid = self.inside(unit)
        plane = self.plane(unit)
        right = jnp.logical_and(valid, jnp.logical_and(z < plane, delay == z))
        left = jnp.logical_and(valid, jnp.logical_and(z > plane, delay == line - 1 - z))
        last = jnp.logical_and(
            valid,
            jnp.logical_and(z == plane, delay == jnp.maximum(plane, line - 1 - plane)),
        )
        return unit, right, left, last

    def end_task(self, half_step, delay, parity):
        z, line = self.spot.z, self.spot.line
        turn = (parity - 3 - delay) % self.turns
        unit, right, left, last = self.end_roles(half_step, delay)
        some = jnp.logical_or(right, jnp.logical_or(left, last))
        from_left = jnp.logical_and(jnp.logical_or(right, last), z > 0)
        from_right = jnp.logical_and(jnp.logical_or(left, last), z + 1 < line)
        present = ((RIGHT, from_left), (LEFT, from_right))

        def fetch(base):
            def action():
                self.received(self.seconds.at[unit, 0], self.second_receive.at[unit, 0])
                self.received(self.firsts.at[unit], self.first_receive.at[unit])
                for i, source in enumerate(self.summands(unit)):
                    self.load(source, base + i).start()
                for kind, there in present:

                    def arrive():
                        self.received(self.ends.at[unit, kind], self.end_receive.at[unit, kind])
                        self.load(self.ends.at[unit, kind], base + 4 + kind).start()

                    when(there, arrive)

            when(some, action)

        def add(base):
            def action():
                for i, source in enumerate(self.summands(unit)):
                    self.load(source, base + i).wait()
                for kind, there in present:
                    when(there, lambda: self.load(self.ends.at[unit, kind], base + 4 + kind).wait())
                numbers = list(range(4))
                for kind, chosen, behind in ((RIGHT, right, z > 0), (LEFT, left, z + 1 < line)):

                    def onward():
                        target = self.outbox.at[self.end_slot(turn, kind)]
                        self.free(unit, turn, 0)
                        when(behind, lambda: self.add(target, base, numbers + [4 + kind]))
                        when(jnp.logical_not(behind), lambda: self.add(target, base, numbers))
                        self.end_send(unit, turn, kind).start()

                    when(chosen, onward)

                def finish():
                    def into(target):
                        both = jnp.logical_and(from_left, from_right)
                        when(both, lambda: self.add(target, base, numbers + [4, 5]))
                        for kind, there in present:
                            when(
                                jnp.logical_and(there, jnp.logical_not(both)),
                                lambda: self.add(target, base, numbers + [4 + kind]),
                            )

                    self.done(unit, turn, 0, into)

                when(last, finish)

            when(some, action)

        return fetch, add

    def retire(self, half_step, parity):
        before = half_step - self.turns
        now, then = (parity - 1) % self.turns, (parity - 2) % self.turns
        when(
            self.inside(before - 1),
            lambda: [self.second_send(before - 1, now, first).wait_send() for first in range(2)],
        )
        when(self.inside(before - 2), lambda: self.first_send(before - 2, then).wait_send())
        for delay in range(self.spot.line):
            unit, right, left, _ = self.end_roles(before, delay)
            turn = (parity - 3 - delay) % self.turns
            when(right, lambda: self.end_send(unit, turn, RIGHT).wait_send())
            when(left, lambda: self.end_send(unit, turn, LEFT).wait_send())
            unit, right, left, _ = self.end_roles(before + 2, delay)
            turn = (parity - 1 - delay) % self.turns
            when(right, lambda: self.late_send(unit, turn, RIGHT).wait_send())
            when(left, lambda: self.late_send(unit, turn, LEFT).wait_send())

    def simple_task(self, valid, ready, inputs, slot, send, free=lambda: None):
        def fetch(base):
            ready()

            def action():
                for i, source in enumerate(inputs()):
                    self.load(source, base + i).start()

            when(valid, action)

        def add(base):
            def action():
                refs = inputs()
                for i, source in enumerate(refs):
                    self.load(source, base + i).wait()
                free()
                self.add(self.outbox.at[slot], base, range(len(refs)))
                send().start()

            when(valid, action)

        return fetch, add

    def tasks(self, half_step, parity):
        one, two = half_step - 1, half_step - 2
        now, then = (parity - 1) % self.turns, (parity - 2) % self.turns
        tasks = [
            self.second_task(one, now, 1, functools.partial(self.ready, one)),
            self.second_task(one, now, 0, lambda: None),
            self.first_task(two, then),
        ]
        line = self.spot.line
        tasks += [self.end_task(half_step, delay, parity) for delay in range(line)]
        others = [self.late_task(half_step, delay, parity) for delay in range(line)]
        others += [self.plane_task(half_step, stage) for stage in range(2)]
        woven = []
        for index, task in enumerate(tasks):
            woven += [task] + others[index : index + 1]
        return woven + others[len(tasks) :]

    def late_rows(self, index):
        return pl.ds(pl.multiple_of(index * self.late_inbox.shape[1] // 4, 16), self.late_inbox.shape[1] // 4)

    def late_send(self, unit, turn, kind):
        slot = turn * 2 + kind
        return self.spot.send(
            self.late_outbox.at[slot],
            self.late_ends.at[unit, kind],
            self.late_outbox_sem.at[slot],
            self.late_end_receive.at[unit, kind],
            kind,
        )

    def late_place(self, turn, first, second):
        y, x = self.spot.side(self.spot.core, first, second)
        return self.late_sums.at[turn, self.late_rows(y * 2 + x)]

    def late_second(self, unit, turn, first):
        return self.spot.send(
            self.late_place(turn, first, 1),
            self.late_seconds.at[unit, first],
            self.late_sums_sem.at[turn * 3 + first],
            self.late_second_receive.at[unit, first],
            SECOND,
        )

    def late_first(self, unit, turn):
        return self.spot.send(
            self.late_place(turn, 1, 0),
            self.late_firsts.at[unit],
            self.late_sums_sem.at[turn * 3 + 2],
            self.late_first_receive.at[unit],
            FIRST,
        )

    def late_load(self, source, target, index):
        return pltpu.make_async_copy(source, target, self.late_inbox_sem.at[index])

    def late_loads(self, unit):
        copies = []
        size = self.late_inbox.shape[1] // 4
        for y in range(2):
            for x in range(2):
                rows = pl.ds(x * self.half + self.half - size, size)
                for i, ref in enumerate((self.parts(unit, y), self.cores(unit, y))):
                    place = self.late_inbox.at[i, pl.ds((y * 2 + x) * size, size)]
                    copies.append(self.late_load(ref.at[rows], place, i * 4 + y * 2 + x))
        return copies

    def late_task(self, half_step, delay, parity):
        z, line = self.spot.z, self.spot.line
        turn = (parity - 1 - delay) % self.turns
        unit, right, left, last = self.end_roles(half_step + 2, delay)
        some = jnp.logical_or(right, jnp.logical_or(left, last))
        from_left = jnp.logical_and(jnp.logical_or(right, last), z > 0)
        from_right = jnp.logical_and(jnp.logical_or(left, last), z + 1 < line)
        present = ((RIGHT, from_left), (LEFT, from_right))
        both = jnp.logical_and(from_left, from_right)

        def behind(kind):
            return self.late_load(self.late_ends.at[unit, kind], self.late_inbox.at[2 + kind], 8 + kind)

        def fetch(base):
            def action():
                for copy in self.late_loads(unit):
                    copy.start()
                for kind, there in present:

                    def arrive():
                        self.received(self.late_ends.at[unit, kind], self.late_end_receive.at[unit, kind])
                        behind(kind).start()

                    when(there, arrive)

            when(some, action)

        def add(base):
            def total(target, kinds):
                add_rows(target, [self.late_inbox.at[i] for i in [0, 1] + [2 + kind for kind in kinds]])

            def action():
                for copy in self.late_loads(unit):
                    copy.wait()
                for kind, there in present:
                    when(there, lambda: behind(kind).wait())
                for kind, chosen, there in ((RIGHT, right, from_left), (LEFT, left, from_right)):

                    def onward():
                        target = self.late_outbox.at[turn * 2 + kind]
                        when(there, lambda: total(target, [kind]))
                        when(jnp.logical_not(there), lambda: total(target, []))
                        self.late_send(unit, turn, kind).start()

                    when(chosen, onward)

                def in_plane():
                    target = self.late_sums.at[turn]
                    when(both, lambda: total(target, [RIGHT, LEFT]))
                    for kind, there in present:
                        when(
                            jnp.logical_and(there, jnp.logical_not(both)),
                            lambda: total(target, [kind]),
                        )
                    for first in (1, 0):
                        self.late_second(unit, turn, first).start()

                when(last, in_plane)

            when(some, action)

        return fetch, add

    def plane_task(self, half_step, stage):
        z, line = self.spot.z, self.spot.line
        unit = half_step - 2 - stage - jnp.maximum(z, line - 1 - z)
        turn = lax.rem(jnp.maximum(unit, 0), self.turns)
        valid = jnp.logical_and(self.inside(unit), self.plane(unit) == z)
        size = self.late_inbox.shape[1] // 4
        place = lambda i: self.late_inbox.at[i, pl.ds(0, size)]
        second = self.late_load(self.late_seconds.at[unit, 1 - stage], place(0), 0)
        first = lambda: self.late_load(self.late_firsts.at[unit], place(1), 4)

        def fetch(base):
            def action():
                self.received(
                    self.late_seconds.at[unit, 1 - stage], self.late_second_receive.at[unit, 1 - stage]
                )
                second.start()
                if stage:
                    self.received(self.late_firsts.at[unit], self.late_first_receive.at[unit])
                    first().start()

            when(valid, action)

        def add(base):
            def action():
                second.wait()
                if stage:
                    first().wait()
                    sources = [self.late_place(turn, 0, 0), place(0), place(1)]
                    self.done(unit, lax.rem(unit, 2), 1, lambda target: add_rows(target, sources))
                    for i in range(2):
                        self.late_second(unit, turn, i).wait_send()
                    self.late_first(unit, turn).wait_send()
                else:
                    target = self.late_place(turn, 1, 0)
                    add_rows(target, [target, place(0)])
                    self.late_first(unit, turn).start()

            when(valid, action)

        return fetch, add

    def second_task(self, unit, turn, first, ready):
        return self.simple_task(
            self.inside(unit),
            ready,
            lambda: self.sources(unit, first, 1),
            self.second_slot(turn, first),
            lambda: self.second_send(unit, turn, first),
        )

    def first_task(self, unit, turn):
        arrive = lambda: self.received(self.seconds.at[unit, 1], self.second_receive.at[unit, 1])

        def send():
            return self.first_send(unit, turn)

        return self.simple_task(
            self.inside(unit),
            lambda: when(self.inside(unit), arrive),
            lambda: self.sources(unit, 1, 0) + [self.seconds.at[unit, 1]],
            self.first_slot(turn),
            send,
            lambda: self.free(unit, turn, 1),
        )

    def weave(self, tasks, pieces):
        buffers = self.inbox.shape[0] // BOXES
        if buffers > 1:
            tasks[0][0](0)
        for index, (fetch, add) in enumerate(tasks):
            if buffers == 1:
                fetch(0)
            elif index + 1 < len(tasks):
                tasks[index + 1][0]((index + 1) % 2 * BOXES)
            share = -(-len(pieces) // (len(tasks) - index))
            for piece in pieces[:share]:
                piece()
            pieces = pieces[share:]
            add(index % buffers * BOXES)

    def half_steps(self, units):
        return units + self.spot.line + 2


def norm_back(value, grads, gain):
    scale = lax.rsqrt(jnp.mean(value * value, axis=-1, keepdims=True) + EPSILON)
    unit = value * scale
    scaled = grads * gain
    back = scale * (scaled - unit * jnp.mean(scaled * unit, axis=-1, keepdims=True))
    return back, grads * unit


def backward_kernel(
    line,
    heads,
    kv_heads,
    cot_ref,
    totals_ref,
    hidden_ref,
    projected_ref,
    context_ref,
    in_ref,
    out_ref,
    tokens_ref,
    gain1_ref,
    gain2_ref,
    query_gain_ref,
    key_gain_ref,
    cosine_ref,
    sine_ref,
    block_out,
    input_grad,
    grads_all,
    out_total,
    gain_grads,
    elements,
    cots,
    tokens,
    kept,
    result,
    context,
    hidden_grads,
    context_grads,
    grads,
    normed_other,
    weight_rows,
    queries_f,
    shared_f,
    queries,
    query_grads,
    sums,
    out_grads,
    cores,
    firsts,
    rights,
    lefts,
    tree_send,
    tree_receive,
    load_sem,
    row_sem,
    head_sem,
    save_sem,
    hidden_send,
    hidden_receive,
    normed_send,
    normed_receive,
):
    batch, half, width = cot_ref.shape
    length = 2 * half
    features = query_gain_ref.shape[1]
    group = heads // kv_heads
    base = heads * features
    out_width = out_total.shape[1]
    narrow, spot = Spot(line, False), Spot(line, True)
    x = spot.x
    scale = features ** (-0.5)
    normed_grads = context_grads

    def load(source, target, index):
        return pltpu.make_async_copy(source, target, load_sem.at[index])

    def element_loads(i):
        return [
            load(hidden_ref.at[i], elements.at[0], 0),
            load(totals_ref.at[i, BACK], elements.at[1], 1),
            load(totals_ref.at[i, OUTPUT], elements.at[2], 2),
        ]

    first_loads = [load(cot_ref, cots, 3), load(tokens_ref, tokens, 4)] + [
        load(context_ref.at[i], rows_at(context, i, length), 5 + i) for i in range(batch)
    ]
    for copy in element_loads(0) + first_loads:
        copy.start()

    def weight_load(ref, step):
        slot = step % 2
        return pltpu.make_async_copy(
            rows_at(ref, step, CHUNK),
            weight_rows.at[slot, :, pl.ds(0, ref.shape[1])],
            row_sem.at[slot],
        )

    out_steps, in_steps = out_ref.shape[0] // CHUNK, in_ref.shape[0] // CHUNK
    for step in range(2):
        weight_load(out_ref, step).start()
    gain_grads[...] = jnp.zeros_like(gain_grads)
    spot.greet()
    for copy in first_loads:
        copy.wait()

    def result_save(i, target):
        return pltpu.make_async_copy(result.at[i], target.at[i], save_sem.at[i])

    def half_copy(ref, i, side):
        return ref.at[pl.ds(pl.multiple_of(i * length + side * half, 16), half), pl.ds(0, width)]

    def hidden_copy(i):
        place = half_copy(hidden_grads, i, x)
        return spot.send(place, place, hidden_send.at[i], hidden_receive.at[i], CROSS)

    def element_rows(i):
        for copy in element_loads(i):
            copy.wait()

        def elementwise(step, _):
            rows = pl.ds(pl.multiple_of(step * 16, 16), 16)
            value = elements[0, rows, :]
            result[i, rows, :] = (value + elements[2, rows, :]).astype(jnp.bfloat16)
            back, gain_rows = norm_back(
                value, elements[1, rows, :], gain2_ref[...].astype(jnp.float32)
            )
            gain_grads[1:2, :] += jnp.sum(gain_rows, axis=0, keepdims=True)
            total = cots[i, rows, :].astype(jnp.float32) + back
            kept[i, rows, :] = total
            place = pl.ds(pl.multiple_of(i * length + x * half + step * 16, 16), 16)
            hidden_grads[place, :] = total.astype(jnp.bfloat16)
            return 0

        lax.fori_loop(0, half // 16, elementwise, 0)
        hidden_copy(i).start()
        result_save(i, block_out).start()
        if i + 1 < batch:
            for copy in element_loads(i + 1):
                copy.start()

    def hidden_done():
        for i in range(batch):
            hidden_copy(i).wait_send()
            place = half_copy(hidden_grads, i, 1 - x)
            spot.send(place, place, hidden_send.at[i], hidden_receive.at[i], CROSS).wait_recv()

    def context_step(step):
        weight_load(out_ref, step).wait()
        columns = slice(step * CHUNK, (step + 1) * CHUNK)
        context_grads[:, columns] = lax.dot_general(
            hidden_grads[...],
            weight_rows[step % 2, :, :width],
            TRANSPOSED_RIGHT,
            preferred_element_type=jnp.float32,
        ).astype(jnp.bfloat16)
        if step + 2 < out_steps:
            weight_load(out_ref, step + 2).start()

    def out_step(step):
        columns = slice(step * CHUNK, (step + 1) * CHUNK)
        for start in range(0, width, CHUNK):
            out_grads[columns, start : start + CHUNK] = lax.dot_general(
                context[:, columns],
                hidden_grads[:, start : start + CHUNK],
                TRANSPOSED_LEFT,
                preferred_element_type=jnp.float32,
            ).astype(jnp.bfloat16)

    tree = Collect(
        narrow,
        lambda block, side: columns_at(out_grads, block, out_width),
        out_total,
        cores,
        firsts,
        rights,
        lefts,
        tree_send,
        tree_receive,
    )

    def in_start():
        for step in range(2):
            weight_load(in_ref, step).start()

    def tree_start():
        for z in range(line):
            tree.begin(z)
        for copy in head_loads(0):
            copy.start()

    def turns():
        return [(i, shared) for i in range(batch) for shared in range(kv_heads)]

    def head_loads(index):
        i, shared = turns()[index]
        slot = index % 2
        return [
            pltpu.make_async_copy(
                projected_ref.at[i, :, pl.ds(shared * group * features, group * features)],
                queries_f.at[slot],
                head_sem.at[slot, 0],
            )
        ] + [
            pltpu.make_async_copy(
                projected_ref.at[i, :, pl.ds(base + (shared + j * kv_heads) * features, features)],
                shared_f.at[slot, j],
                head_sem.at[slot, 1 + j],
            )
            for j in range(2)
        ]

    def turn_back(grads_in):
        return grads_in * cosine_ref[...] + pltpu.roll(
            grads_in * sine_ref[...], features // 2, 1
        )

    query_gain = lambda: query_gain_ref[...].astype(jnp.float32)
    key_gain = lambda: key_gain_ref[...].astype(jnp.float32)

    def attend_pieces(index):
        i, shared = turns()[index]
        slot = index % 2
        top = i * length

        def columns_of(member):
            return pl.ds(pl.multiple_of(member * features, LANES), features)

        def prepare():
            for copy in head_loads(index):
                copy.wait()
            if index + 1 < len(turns()):
                for copy in head_loads(index + 1):
                    copy.start()
            queries[group] = turned_heads(
                shared_f[slot, 0], key_gain(), cosine_ref[...], sine_ref[...]
            ).astype(jnp.bfloat16)
            queries[group + 1] = shared_f[slot, 1].astype(jnp.bfloat16)
            sums[...] = jnp.zeros_like(sums)

            def one(member):
                queries[member] = turned_heads(
                    queries_f[slot, :, columns_of(member)],
                    query_gain(),
                    cosine_ref[...],
                    sine_ref[...],
                ).astype(jnp.bfloat16)

            for_heads(0, group, 1, one)

        def rows_block(start, stop, seen, at_once, low, high):
            count = stop - start

            def block(member):
                query = queries[pl.ds(member, at_once), start:stop, :].reshape(-1, features)
                keys, values = queries[group, :seen, :], queries[group + 1, :seen, :]
                out_grad = jnp.concatenate(
                    [
                        context_grads[
                            top + start : top + stop,
                            head_columns(shared * group + member + j, features),
                        ]
                        for j in range(at_once)
                    ],
                    axis=0,
                )
                scores = lax.dot_general(
                    keys, query, TRANSPOSED_RIGHT, preferred_element_type=jnp.float32
                )
                shares = softmax(scores * scale)
                share_grads = lax.dot_general(
                    values, out_grad, TRANSPOSED_RIGHT, preferred_element_type=jnp.float32
                )
                sums[1, :seen, :] += jnp.dot(
                    shares.astype(jnp.bfloat16), out_grad, preferred_element_type=jnp.float32
                )
                inner = jnp.sum(shares * share_grads, axis=0, keepdims=True)
                score_grads = (shares * (share_grads - inner)).astype(jnp.bfloat16)
                rows = scale * lax.dot_general(
                    score_grads, keys, TRANSPOSED_LEFT, preferred_element_type=jnp.float32
                )
                query_grads[pl.ds(member, at_once), start:stop, :] = rows.reshape(
                    at_once, count, features
                )
                sums[0, :seen, :] += jnp.dot(
                    score_grads, query, preferred_element_type=jnp.float32
                )

            for_heads(low, high, at_once, block)

        def finish_queries():
            def finish(member):
                back, gain_rows = norm_back(
                    queries_f[slot, :, columns_of(member)],
                    turn_back(query_grads[member]),
                    query_gain(),
                )
                gain_grads[2:3, :features] += jnp.sum(gain_rows, axis=0, keepdims=True)
                grads[top : top + length, head_columns(shared * group + member, features)] = (
                    back.astype(jnp.bfloat16)
                )

            for_heads(0, group, 1, finish)

        def finish_keys():
            back, gain_rows = norm_back(shared_f[slot, 0], turn_back(sums[0] * scale), key_gain())
            gain_grads[3:4, :features] += jnp.sum(gain_rows, axis=0, keepdims=True)
            at = base + shared * features
            grads[top : top + length, at : at + features] = back.astype(jnp.bfloat16)
            at += kv_heads * features
            grads[top : top + length, at : at + features] = sums[1].astype(jnp.bfloat16)

        pieces = [prepare]
        for start, stop, seen, at_once in visible_blocks(length, group):
            share = max(at_once, group // 2)
            for low in range(0, group, share):
                pieces.append(
                    functools.partial(rows_block, start, stop, seen, at_once, low, low + share)
                )
        return pieces + [finish_queries, finish_keys]

    saves = [
        pltpu.make_async_copy(rows_at(grads, i, length), grads_all.at[i], save_sem.at[batch + i])
        for i in range(batch)
    ]

    def normed_step(step):
        weight_load(in_ref, step).wait()
        normed_grads[:, step * CHUNK : (step + 1) * CHUNK] = lax.dot_general(
            grads[...],
            weight_rows[step % 2],
            TRANSPOSED_RIGHT,
            preferred_element_type=jnp.float32,
        ).astype(jnp.bfloat16)
        if step + 2 < in_steps:
            weight_load(in_ref, step + 2).start()

    def normed_copy(i):
        return spot.send(
            half_copy(normed_grads, i, 1 - x),
            normed_other.at[i],
            normed_send.at[i],
            normed_receive.at[i],
            CROSS,
        )

    def input_rows(i):
        normed_copy(i).wait()
        result_save(i, block_out).wait()

        def body(step, _):
            rows = pl.ds(pl.multiple_of(step * 16, 16), 16)
            place = pl.ds(pl.multiple_of(i * length + x * half + step * 16, 16), 16)
            total = normed_grads[place, :width].astype(jnp.float32) + normed_other[
                i, rows, :
            ].astype(jnp.float32)
            back, gain_rows = norm_back(
                tokens[i, rows, :].astype(jnp.float32), total, gain1_ref[...].astype(jnp.float32)
            )
            gain_grads[0:1, :] += jnp.sum(gain_rows, axis=0, keepdims=True)
            kept[i, rows, :] = kept[i, rows, :] + back
            return 0

        lax.fori_loop(0, half // 16, body, 0)
        add_rows(result.at[i], [kept.at[i]])
        result_save(i, input_grad).start()

    opening = [functools.partial(element_rows, i) for i in range(batch)] + [hidden_done]
    opening += [functools.partial(out_step, step) for step in range(out_steps)]
    opening += [tree_start, functools.partial(context_step, 0), tree.cross]
    opening += [functools.partial(context_step, step) for step in range(1, out_steps)]
    opening.append(in_start)
    attending = [piece for index in range(len(turns())) for piece in attend_pieces(index)]
    closing = attending + [copy.start for copy in saves]
    closing += [functools.partial(normed_step, step) for step in range(in_steps)]
    closing += [normed_copy(i).start for i in range(batch)]
    closing += [functools.partial(input_rows, i) for i in range(batch)]
    for piece in opening:
        piece()
    mingle(closing, tree.tasks())
    for i in range(batch):
        result_save(i, input_grad).wait()
    for copy in saves:
        copy.wait()


def run_backward(
    cot,
    totals,
    hidden,
    projected,
    context,
    in_full,
    out_full,
    tokens,
    gains,
    tables,
    fsdp_count,
    kv_heads,
):
    line = fsdp_count // PLANE
    batch, half, width = tokens.shape
    length = 2 * half
    features = gains[2].shape[1]
    heads = out_full.shape[0] // features
    group = heads // kv_heads
    in_width, out_depth = in_full.shape[1], out_full.shape[0]
    out_shape = (out_depth, width // fsdp_count)
    anywhere = pl.BlockSpec(memory_space=pl.ANY)
    inside = pl.BlockSpec(memory_space=pltpu.VMEM)
    shape = lambda *dims: jax.ShapeDtypeStruct(dims, jnp.bfloat16)
    vmem = lambda *dims: pltpu.VMEM(dims, jnp.bfloat16)
    wide = lambda *dims: pltpu.VMEM(dims, jnp.float32)
    sem = lambda *dims: pltpu.SemaphoreType.DMA(dims)
    rows = batch * length
    return pl.pallas_call(
        functools.partial(backward_kernel, line, heads, kv_heads),
        out_shape=(
            shape(batch, half, width),
            shape(batch, half, width),
            shape(batch, length, in_width),
            jax.ShapeDtypeStruct(out_shape, jnp.float32),
            jax.ShapeDtypeStruct((8, width), jnp.float32),
        ),
        in_specs=[anywhere] * 8 + [inside] * 6,
        out_specs=(anywhere, anywhere, anywhere, inside, inside),
        scratch_shapes=[
            wide(3, half, width),
            vmem(batch, half, width),
            vmem(batch, half, width),
            wide(batch, half, width),
            vmem(batch, half, width),
            vmem(rows, out_depth),
            vmem(rows, width),
            vmem(rows, max(out_depth, width)),
            vmem(rows, in_width),
            vmem(batch, half, width),
            vmem(2, CHUNK, max(width, in_width)),
            wide(2, length, group * features),
            wide(2, 2, length, features),
            vmem(group + 2, length, features),
            wide(group, length, features),
            wide(2, length, features),
            vmem(out_depth, width),
            *collect_scratch(line, out_shape),
            sem(5 + batch),
            sem(2),
            sem(2, 3),
            sem(2 * batch),
            sem(batch),
            sem(batch),
            sem(batch),
            sem(batch),
        ],
        compiler_params=pltpu.CompilerParams(
            collective_id=3, has_side_effects=True, vmem_limit_bytes=62 * MIB
        ),
    )(
        cot,
        totals,
        hidden,
        projected,
        context,
        in_full,
        out_full,
        tokens,
        *gains,
        *tables,
    )


def gradients_kernel(
    line,
    normed,
    grads,
    gains_ref,
    xe_ref,
    ce_ref,
    act_ref,
    dgate_ref,
    dup_ref,
    in_total,
    gains_all,
    gate_total,
    up_total,
    down_total,
    parts,
    cores,
    firsts,
    rights,
    lefts,
    tree_send,
    tree_receive,
    gain_send,
    gain_receive,
    gain_local,
    wide_rows,
    slim_rows,
    gate_sum,
    up_sum,
    down_sum,
    load_sem,
    save_sem,
):
    narrow, spot = Spot(line, False), Spot(line, True)
    experts, count, _ = xe_ref.shape
    share = wide_rows.shape[1]
    turns = count // share
    pieces = [
        (expert, kind, turn)
        for expert in range(experts)
        for kind in range(2)
        for turn in range(turns)
    ]

    def loads(index):
        expert, kind, turn = pieces[index]
        slot = index % 2
        rows = pl.ds(turn * share, share)
        slim = (dgate_ref, dup_ref) if kind == 0 else (act_ref,)
        return [
            pltpu.make_async_copy(
                (xe_ref, ce_ref)[kind].at[expert, rows], wide_rows.at[slot], load_sem.at[slot, 0]
            )
        ] + [
            pltpu.make_async_copy(
                ref.at[expert, rows], slim_rows.at[slot, i], load_sem.at[slot, 1 + i]
            )
            for i, ref in enumerate(slim)
        ]

    def saves(expert, kind):
        pairs = ((gate_sum, gate_total), (up_sum, up_total))
        if kind:
            return [pltpu.make_async_copy(down_sum, down_total.at[expert], save_sem.at[2])]
        return [
            pltpu.make_async_copy(source, target.at[expert], save_sem.at[i])
            for i, (source, target) in enumerate(pairs)
        ]

    for copy in loads(0):
        copy.start()
    spot.greet()
    gains = Spread(
        spot,
        gains_ref,
        lambda block, half: gains_all.at[block, half],
        gain_send,
        gain_receive,
        gain_local.at[0],
    )
    gains.begin()
    depth, width = in_total.shape
    tree = Collect(
        narrow,
        lambda block, half: rows_at(parts, block, depth),
        in_total,
        cores,
        firsts,
        rights,
        lefts,
        tree_send,
        tree_receive,
    )
    chunk = PLANE * depth

    def plane(step, _):
        z = lax.rem(narrow.z + 1 + step, line)
        columns = pl.ds(pl.multiple_of(z * chunk, LANES), chunk)
        for start in range(0, width, CHUNK):
            parts[pl.ds(pl.multiple_of(z * chunk, 16), chunk), start : start + CHUNK] = (
                lax.dot_general(
                    normed[:, columns],
                    grads[:, start : start + CHUNK],
                    TRANSPOSED_LEFT,
                    preferred_element_type=jnp.float32,
                ).astype(jnp.bfloat16)
            )
        tree.begin(z)
        return 0

    lax.fori_loop(0, line, plane, 0)

    def piece(index):
        expert, kind, turn = pieces[index]
        slot = index % 2
        for copy in loads(index):
            copy.wait()
        if index + 1 < len(pieces):
            for copy in loads(index + 1):
                copy.start()
        if turn == 0 and expert:
            for copy in saves(expert - 1, kind):
                copy.wait()
        size = wide_rows.shape[2] // 4

        def add(target, place, left, right):
            product = lax.dot_general(
                left, right, TRANSPOSED_LEFT, preferred_element_type=jnp.float32
            )
            if turn:
                product = target[place] + product
            target[place] = product

        def part(step, _):
            at = pl.ds(pl.multiple_of(step * size, LANES), size)
            if kind:
                add(down_sum, (slice(None), at), slim_rows[slot, 0], wide_rows[slot, :, at])
            else:
                for i, target in enumerate((gate_sum, up_sum)):
                    add(target, (at, slice(None)), wide_rows[slot, :, at], slim_rows[slot, i])
            return 0

        lax.fori_loop(0, 4, part, 0)
        if turn == turns - 1:
            for copy in saves(expert, kind):
                copy.start()

    tree.cross()
    work = tree.tasks()
    steps = list(range(1, gains.steps()))
    filler = list(range(len(pieces)))
    while work or filler:
        for _ in range(2 if len(filler) > len(work) else 1):
            if filler:
                piece(filler.pop(0))
        if work:
            work.pop(0)()
        if steps:
            gains.step(steps.pop(0))
    gains.finish()
    for copy in saves(experts - 1, 0) + saves(experts - 1, 1):
        copy.wait()


def run_gradients(normed, grads, gains, expert_rows, fsdp_count):
    line = fsdp_count // PLANE
    width = grads.shape[1]
    experts, count, depth = expert_rows[0].shape
    units = expert_rows[2].shape[2]
    share = 2 * CHUNK if count % (2 * CHUNK) == 0 else count // (2 * line)
    shape = (normed.shape[1] // fsdp_count, width)
    sends, receives = spread_count(line, True)
    inside = pl.BlockSpec(memory_space=pltpu.VMEM)
    anywhere = pl.BlockSpec(memory_space=pl.ANY)
    return pl.pallas_call(
        functools.partial(gradients_kernel, line),
        out_shape=(
            jax.ShapeDtypeStruct(shape, jnp.float32),
            jax.ShapeDtypeStruct((fsdp_count, 2, *gains.shape), jnp.float32),
            jax.ShapeDtypeStruct((experts, depth, units), jnp.float32),
            jax.ShapeDtypeStruct((experts, depth, units), jnp.float32),
            jax.ShapeDtypeStruct((experts, units, depth), jnp.float32),
        ),
        in_specs=[inside, inside] + [anywhere] * 6,
        out_specs=(inside,) + (anywhere,) * 4,
        scratch_shapes=[
            pltpu.VMEM((normed.shape[1], width), jnp.bfloat16),
            *collect_scratch(line, shape),
            pltpu.SemaphoreType.DMA((sends,)),
            pltpu.SemaphoreType.DMA((receives,)),
            pltpu.SemaphoreType.DMA((1,)),
            pltpu.VMEM((2, share, depth), jnp.bfloat16),
            pltpu.VMEM((2, 2, share, units), jnp.bfloat16),
            pltpu.VMEM((depth, units), jnp.float32),
            pltpu.VMEM((depth, units), jnp.float32),
            pltpu.VMEM((units, depth), jnp.float32),
            pltpu.SemaphoreType.DMA((2, 3)),
            pltpu.SemaphoreType.DMA((3,)),
        ],
        compiler_params=pltpu.CompilerParams(
            collective_id=4, has_side_effects=True, vmem_limit_bytes=60 * MIB
        ),
    )(normed, grads, gains, *expert_rows)


def experts_kernel(
    line,
    slots,
    own_ref,
    cot_first,
    cot_ref,
    info_ref,
    gate_ref,
    up_ref,
    down_ref,
    all_ref,
    cot_later,
    total_ref,
    xe_all,
    ce_all,
    act_all,
    dgate_all,
    dup_all,
    part,
    cores,
    seconds,
    firsts,
    ends,
    late_ends,
    late_seconds,
    late_firsts,
    hidden_w,
    down_w,
    x_rows,
    c_rows,
    xe,
    ce,
    acts,
    dgates,
    dups,
    hidden_grads,
    picks,
    weigh,
    rows,
    stage,
    inbox,
    outbox,
    summed,
    rows_send,
    rows_receive,
    rows_late_send,
    rows_late_receive,
    rows_local,
    cot_send,
    cot_receive,
    cot_late_send,
    cot_late_receive,
    cot_local,
    load_sem,
    save_sem,
    stage_sem,
    inbox_sem,
    outbox_sem,
    total_sem,
    weight_sem,
    core_receive,
    second_receive,
    first_receive,
    end_receive,
    *late_scratch,
):
    late_refs = (late_ends, late_seconds, late_firsts, *late_scratch)
    spot = Spot(line, True)
    z, core = spot.z, spot.core
    cot_semaphores = (cot_send, cot_receive, cot_late_send, cot_late_receive, cot_local)
    tree_semaphores = (rows_send, rows_receive, rows_late_send, rows_late_receive, rows_local)
    batch, half, width = own_ref.shape
    length = 2 * half
    units = down_ref.shape[1]
    groups = batch * line
    weights = [
        pltpu.make_async_copy(source, target, weight_sem.at[i])
        for i, (source, target) in enumerate(
            [(down_ref, down_w)]
            + [(gate_ref.at[e], hidden_w.at[e, :, pl.ds(0, units)]) for e in range(2)]
            + [(up_ref.at[e], hidden_w.at[e, :, pl.ds(units, units)]) for e in range(2)]
        )
    ]
    for copy in weights:
        copy.start()
    rows[...] = jnp.zeros_like(rows)
    spot.greet()

    def half_of(ref, index):
        return rows_at(ref, index, half)

    trees = []
    for i in range(batch):
        place = lambda block, start, size, i=i: all_ref.at[
            i, block, pl.ds(pl.multiple_of(start, 16), size)
        ]
        trees.append(rows_spread(spot, own_ref.at[i], place, half, tree_semaphores, i))
    for i in range(1, batch):
        place = lambda block, start, size, i=i: cot_later.at[
            i - 1, block, pl.ds(pl.multiple_of(start, 16), size)
        ]
        trees[i] += rows_spread(spot, cot_ref.at[i], place, half, cot_semaphores, i - 1)
    run_trees(trees[0])
    for tree in sum(trees[1:], []):
        tree.begin()
    for copy in weights:
        copy.wait()

    plane_of = functools.partial(plane_in_turn, line)

    def load_group(group, member, start):
        at = lax.div(group, line)
        sequence = plane_of(group) * PLANE + member
        slot = member % 2
        def copy(i, source, target):
            return pltpu.make_async_copy(source, target.at[slot], load_sem.at[i, slot])

        own = copy(0, all_ref.at[at, sequence], x_rows)
        if start:
            own.start()
            later = cot_later.at[jnp.maximum(at - 1, 0), sequence]
            when(at == 0, lambda: copy(1, cot_first.at[sequence], c_rows).start())
            when(at > 0, lambda: copy(1, later, c_rows).start())
        else:
            own.wait()
            copy(1, cot_first.at[sequence], c_rows).wait()

    def saves(group):
        to = lambda ref, expert: rows_at(ref.at[expert], group, PLANE * slots)
        pairs = ((xe, xe_all), (ce, ce_all), (acts, act_all), (dgates, dgate_all), (dups, dup_all))
        return [
            pltpu.make_async_copy(source.at[expert], to(target, expert), save_sem.at[2 * i + expert])
            for i, (source, target) in enumerate(pairs)
            for expert in range(2)
        ]

    def staged(unit, y, mine):
        slot = y * 2 + mine
        if mine:
            return pltpu.make_async_copy(stage.at[slot], part.at[unit, y], stage_sem.at[slot])
        return spot.send(
            stage.at[slot], cores.at[unit, y], stage_sem.at[slot], core_receive.at[unit, y], CORE
        )

    def combine(unit, y):
        for mine in range(2):
            member = y * 2 + (core if mine else 1 - core)
            for start in range(0, width, CHUNK):
                stage[y * 2 + mine, :, start : start + CHUNK] = lax.dot_general(
                    picks[member],
                    rows[member, :, start : start + CHUNK],
                    TRANSPOSED_LEFT,
                    preferred_element_type=jnp.float32,
                ).astype(jnp.bfloat16)
            staged(unit, y, mine).start()

    def pick(group, member):
        slot = member % 2
        load_group(group, member, False)
        if member + 1 < PLANE:
            load_group(group, member + 1, True)
        sequence = plane_of(group) * PLANE + member
        info = info_ref[lax.div(group, line) * line * PLANE + sequence]
        places = lax.broadcasted_iota(jnp.int32, (2 * LANES, length), 0)
        lower = places < LANES
        ranks = jnp.where(lower, info[0:1], info[1:2] + float(LANES)).astype(jnp.int32)
        some = jnp.where(lower, info[0:1], info[1:2]) >= 0.0
        hot = jnp.logical_and(ranks == places, some)
        chosen = hot.astype(jnp.float32).astype(jnp.bfloat16)
        picks[member] = chosen
        shares = jnp.where(hot, jnp.where(lower, info[2:3], info[3:4]), 0.0)
        column = jnp.sum(shares, axis=1, keepdims=True)
        here = pl.ds(member * slots, slots)
        for expert in range(2):
            weigh[expert, here, :] = jnp.broadcast_to(
                column[expert * LANES : expert * LANES + slots], (slots, LANES)
            )
        for source, target in ((x_rows, xe), (c_rows, ce)):
            for start in range(0, width, CHUNK):
                selected = jnp.dot(
                    chosen,
                    source[slot, :, start : start + CHUNK],
                    preferred_element_type=jnp.float32,
                ).astype(jnp.bfloat16)
                for expert in range(2):
                    target[expert, here, start : start + CHUNK] = selected[
                        expert * LANES : expert * LANES + slots
                    ]

    def keep(expert, product, start):
        at = pl.ds(expert * LANES, slots)
        for one in range(PLANE):
            rows[one, at, start : start + CHUNK] = product[one * slots : (one + 1) * slots].astype(
                jnp.bfloat16
            )

    def forward(expert):
        hidden = jnp.dot(xe[expert], hidden_w[expert], preferred_element_type=jnp.float32)
        gate, up = hidden[:, :units], hidden[:, units:]
        sigmoid = jax.nn.sigmoid(gate)
        silu = gate * sigmoid
        scale = weigh[expert, :, 0:1]
        acts[expert] = (silu * up * scale).astype(jnp.bfloat16)
        act_grads = scale * lax.dot_general(
            ce[expert], down_w[expert], TRANSPOSED_RIGHT, preferred_element_type=jnp.float32
        )
        gate_grads = (act_grads * up * (sigmoid * (1.0 + gate * (1.0 - sigmoid)))).astype(
            jnp.bfloat16
        )
        up_grads = (act_grads * silu).astype(jnp.bfloat16)
        dgates[expert] = gate_grads
        dups[expert] = up_grads
        hidden_grads[expert, :, :units] = gate_grads
        hidden_grads[expert, :, units:] = up_grads
        for start in range(0, width, CHUNK):
            keep(
                expert,
                jnp.dot(
                    acts[expert],
                    down_w[expert, :, start : start + CHUNK],
                    preferred_element_type=jnp.float32,
                ),
                start,
            )

    def backward(expert):
        for start in range(0, width, CHUNK):
            keep(
                expert,
                lax.dot_general(
                    hidden_grads[expert],
                    hidden_w[expert, start : start + CHUNK, :],
                    TRANSPOSED_RIGHT,
                    preferred_element_type=jnp.float32,
                ),
                start,
            )

    units_all = 2 * groups

    def inside(unit):
        return jnp.logical_and(unit >= 0, unit < units_all)

    def ready(unit):
        @pl.when(inside(unit))
        def _():
            for y in range(2):
                staged(unit, y, 1).wait()
                staged(unit, y, 0).wait_send()
                place, semaphore = cores.at[unit, y], core_receive.at[unit, y]
                spot.send(place, place, outbox_sem.at[0], semaphore, CORE).wait_recv()

    late = late_rows(half)

    def done(unit, tensor, part_of, into):
        rows = (pl.ds(0, half - late), pl.ds(half - late, late))[part_of]
        place = summed.at[rows]
        into(place)
        copy = pltpu.make_async_copy(
            place, total_ref.at[lax.div(unit, 2 * line), tensor, rows], total_sem.at[0]
        )
        copy.start()
        copy.wait()

    sums = Sums(
        spot,
        half,
        lambda unit, y: part.at[unit, y],
        lambda unit, y: cores.at[unit, y],
        (seconds, firsts, ends),
        inbox,
        outbox,
        (inbox_sem, outbox_sem, second_receive, first_receive, end_receive),
        late_refs,
        lambda unit: plane_of(lax.div(jnp.maximum(unit, 0), 2)),
        inside,
        ready,
        done,
        2,
    )

    def tree_turn(half_step, last):
        for i in range(1, batch):
            turn = half_step - (i - 1) * 2 * line
            if last:
                when(turn == 2 * line - 1, lambda: [tree.finish() for tree in trees[i]])
            else:
                inner = jnp.logical_and(turn >= 0, turn < 2 * line - 1)
                when(inner, lambda: [tree.step(turn + 1) for tree in trees[i]])

    def begin_pick(group):
        load_group(group, 0, True)

    begin_pick(0)
    for member in range(PLANE):
        pick(0, member)

    def step_body(step, _):
        busy = step < groups
        more = step + 1 < groups
        for parity in range(2):
            half_step = step * 2 + parity
            tree_turn(half_step, False)
            sums.retire(half_step, parity)
            tasks = sums.tasks(half_step, parity)
            pieces = []
            for expert in range(2):
                pieces.append(functools.partial((forward, backward)[parity], expert))
            if parity == 0:
                pieces.append(lambda: [copy.start() for copy in saves(step)])
            for y in range(2):
                pieces.append(functools.partial(combine, half_step, y))
            pieces = [functools.partial(when, busy, piece) for piece in pieces]
            if parity == 1:

                def prepare():
                    for copy in saves(step):
                        copy.wait()
                    begin_pick(step + 1)

                tree_end = functools.partial(tree_turn, half_step, True)
                pieces += [tree_end, functools.partial(when, more, prepare)]
                for member in range(PLANE):
                    pieces.append(
                        functools.partial(when, more, functools.partial(pick, step + 1, member))
                    )
            sums.weave(tasks, pieces)
        return 0

    half_steps = sums.half_steps(units_all)
    lax.fori_loop(0, -(-half_steps // 2), step_body, 0)
    end = -(-half_steps // 2) * 2
    for parity in range(2):
        sums.retire(jnp.int32(end + parity), parity)
    for copy in saves(groups - 1):
        copy.wait()


def run_experts(rows, cot_first, cot, info, w_gate, w_up, w_down, capacity, fsdp_count):
    line = fsdp_count // PLANE
    batch, half, width = rows.shape
    length = 2 * half
    units = w_down.shape[1]
    slots = -(-capacity // 16) * 16
    groups = batch * line
    count = groups * PLANE * slots
    taken = PLANE * slots
    shape = lambda *dims: jax.ShapeDtypeStruct(dims, jnp.bfloat16)
    block = (half, width)
    late = late_rows(half)
    early = half - late
    anywhere = pl.BlockSpec(memory_space=pl.ANY)
    vmem = lambda *dims: pltpu.VMEM(dims, jnp.bfloat16)
    sem = lambda *dims: pltpu.SemaphoreType.DMA(dims)
    return pl.pallas_call(
        functools.partial(experts_kernel, line, slots),
        out_shape=(
            shape(batch, fsdp_count, length, width),
            shape(max(batch - 1, 1), fsdp_count, length, width),
            jax.ShapeDtypeStruct((batch, 2, *block), jnp.float32),
            shape(2, count, width),
            shape(2, count, width),
            shape(2, count, units),
            shape(2, count, units),
            shape(2, count, units),
            shape(2 * groups, 2, length, width),
            shape(2 * groups, 2, length, width),
            shape(2 * groups, 2, early, width),
            shape(2 * groups, early, width),
            shape(2 * groups, 2, early, width),
            shape(2 * groups, 2, 4 * late, width),
            shape(2 * groups, 2, late, width),
            shape(2 * groups, late, width),
        ),
        in_specs=[
            anywhere,
            anywhere,
            anywhere,
            pl.BlockSpec(memory_space=pltpu.VMEM),
            anywhere,
            anywhere,
            anywhere,
        ],
        out_specs=(anywhere,) * 16,
        scratch_shapes=[
            vmem(2, width, 2 * units),
            vmem(2, units, width),
            vmem(2, length, width),
            vmem(2, length, width),
            vmem(2, taken, width),
            vmem(2, taken, width),
            vmem(2, taken, units),
            vmem(2, taken, units),
            vmem(2, taken, units),
            vmem(2, taken, 2 * units),
            vmem(PLANE, 2 * LANES, length),
            pltpu.VMEM((2, taken, LANES), jnp.float32),
            vmem(PLANE, 2 * LANES, width),
            vmem(PLANE, length, width),
            vmem(12, early, width),
            vmem(10, early, width),
            pltpu.VMEM(block, jnp.float32),
            *rows_semaphores(batch, line),
            *rows_semaphores(max(batch - 1, 1), line),
            sem(2, 2),
            sem(10),
            sem(PLANE),
            sem(12),
            sem(10),
            sem(1),
            sem(5),
            sem(2 * groups, 2),
            sem(2 * groups, 2),
            sem(2 * groups),
            sem(2 * groups, 2),
            vmem(4, 4 * late, width),
            vmem(4, 4 * late, width),
            vmem(2, 4 * late, width),
            sem(10),
            sem(4),
            sem(6),
            sem(2 * groups, 2),
            sem(2 * groups, 2),
            sem(2 * groups),
        ],
        compiler_params=pltpu.CompilerParams(
            collective_id=2, has_side_effects=True, vmem_limit_bytes=60 * MIB
        ),
    )(rows, cot_first, cot, info, w_gate, w_up, w_down)[2:8]


def packed_picks(routes, gates):
    length = routes.shape[2]
    packed = jnp.concatenate([routes[:, 0].astype(jnp.float32), gates[:, 0]], axis=-1)
    packed = jnp.swapaxes(packed, 1, 2).reshape(-1, length)
    return jnp.pad(packed, ((0, 0), (0, -length % LANES)))


def slot_info(packed, batch, top, length, local_experts):
    fsdp_count = packed.shape[0]
    packed = packed[..., :length].reshape(fsdp_count, batch, 1, 2 * top, length)
    packed = jnp.swapaxes(packed, 0, 1)
    experts = lax.axis_index(FSDP) * local_experts + jnp.arange(local_experts, dtype=jnp.int32)
    same = packed[..., :top, :].astype(jnp.int32) == experts[:, None, None]
    hot = jnp.any(same, axis=3)
    shares = jnp.sum(jnp.where(same, packed[..., top:, :], 0.0), axis=3)
    position = jnp.arange(length)
    upper = (position[:, None] < position[None, :]).astype(jnp.bfloat16)
    rank = jnp.dot(
        hot.astype(jnp.bfloat16).reshape(-1, length), upper, preferred_element_type=jnp.float32
    )
    rank = jnp.where(hot, rank.reshape(hot.shape), -1.0)
    return jnp.concatenate([rank, shares], axis=2).reshape(-1, 2 * local_experts, length)


def gathered_layer(
    tokens,
    cotangent,
    norm1_gain,
    w_query,
    key_projection_weight,
    value_projection_weight,
    query_gain,
    key_gain,
    w_out,
    norm2_gain,
    w_gate,
    w_up,
    w_down,
    routes,
    gates,
):
    batch_count = tokens.shape[0]
    model_width = tokens.shape[3]
    sequence_length = routes.shape[2]
    half_length = tokens.shape[2]
    top_count = routes.shape[3]
    head_features = query_gain.shape[0]
    local_experts = w_gate.shape[0]
    fsdp_count = lax.axis_size(FSDP)
    all_experts = local_experts * fsdp_count
    capacity = 7 * top_count * sequence_length // (6 * all_experts)
    query_width = w_query.shape[1]
    kv_width = key_projection_weight.shape[1]
    kv_heads = kv_width // head_features
    cosine_table, sine_values = rotary_tables(sequence_length, head_features)
    weight_in = jnp.concatenate([w_query, key_projection_weight, value_projection_weight], axis=1)
    half_signs = jnp.where(jnp.arange(head_features) < head_features // 2, -1.0, 1.0)
    tables = (cosine_table[:, 0], sine_values[:, 0] * half_signs)
    gains = [gain[None, :] for gain in (norm1_gain, norm2_gain, query_gain, key_gain)]
    cot_first, in_full, out_full, picks, normed, projected, contexts, hidden, second = run_forward(
        tokens[:, 0],
        cotangent[:, 0],
        weight_in,
        w_out,
        packed_picks(routes, gates),
        gains,
        tables,
        fsdp_count,
        kv_heads,
    )
    info = slot_info(picks, batch_count, top_count, sequence_length, local_experts)
    totals, *expert_rows = run_experts(
        second, cot_first, cotangent[:, 0], info, w_gate, w_up, w_down, capacity, fsdp_count
    )
    block_out, input_grad, projected_grads, out_sum, gain_grads = run_backward(
        cotangent[:, 0],
        totals,
        hidden,
        projected,
        contexts,
        in_full,
        out_full,
        tokens[:, 0],
        gains,
        tables,
        fsdp_count,
        kv_heads,
    )
    rows = batch_count * sequence_length
    in_sum, gains_all, *expert_grads = run_gradients(
        normed.reshape(rows, -1),
        projected_grads.reshape(rows, -1),
        gain_grads,
        expert_rows,
        fsdp_count,
    )
    gains_sum = jnp.sum(gains_all, axis=(0, 1))
    return (
        block_out[:, None],
        input_grad[:, None],
        gains_sum[0],
        in_sum[:, :query_width],
        in_sum[:, query_width : query_width + kv_width],
        in_sum[:, query_width + kv_width :],
        gains_sum[2, :head_features],
        gains_sum[3, :head_features],
        out_sum,
        gains_sum[1],
        *expert_grads,
    )


def shards(*arrays):
    tokens, routes, w_gate = arrays[0], arrays[13], arrays[10]
    fsdp_count = lax.axis_size(FSDP)
    gathered = fsdp_count * routes.shape[2] * tokens.shape[3] * 2
    fits = gathered <= 24 * MIB and fsdp_count % PLANE == 0 and lax.axis_size(TP) == 2
    if fits and w_gate.shape[0] == 2:
        return gathered_layer(*arrays)
    return exchanged_layer(*arrays)


def solution(mesh):
    in_specs = (
        P(None, "fsdp", "tp", None),
        P(None, "fsdp", "tp", None),
        P(),
        P("fsdp", "tp"),
        P("fsdp", "tp"),
        P("fsdp", "tp"),
        P(),
        P(),
        P("tp", "fsdp"),
        P(),
        P("fsdp", None, "tp"),
        P("fsdp", None, "tp"),
        P("fsdp", "tp", None),
        P(None, "fsdp", None, None),
        P(None, "fsdp", None, None),
    )
    out_specs = (
        P(None, "fsdp", "tp", None),
        P(None, "fsdp", "tp", None),
        P(),
        P("fsdp", "tp"),
        P("fsdp", "tp"),
        P("fsdp", "tp"),
        P(),
        P(),
        P("tp", "fsdp"),
        P(),
        P("fsdp", None, "tp"),
        P("fsdp", None, "tp"),
        P("fsdp", "tp", None),
    )
    return jax.shard_map(shards, mesh=mesh, in_specs=in_specs, out_specs=out_specs, check_vma=False)
```

```python
import functools

import jax
import jax.numpy as jnp
from jax import lax
from jax.experimental import pallas as pl
from jax.experimental.pallas import tpu as pltpu
from jax.sharding import PartitionSpec as P

BLOCK = 256


EPSILON = 1e-06
ROPE_BASE = 1000000.0
MASKED = -1e30
TILE_PICKS = 128


def rms_scale(row_block, gain_row):
    return (
        row_block
        * lax.rsqrt(jnp.mean(row_block * row_block, axis=-1, keepdims=True) + EPSILON)
        * gain_row
    )


def rotary_tables(sequence_length, head_width):
    half_width = head_width // 2
    inverse = ROPE_BASE ** (-2.0 * jnp.arange(half_width, dtype=jnp.float32) / head_width)
    angles = jnp.arange(sequence_length, dtype=jnp.float32)[:, None] * inverse[None, :]
    cosine_table = jnp.concatenate([jnp.cos(angles), jnp.cos(angles)], axis=-1)[:, None, :]
    sine_values = jnp.concatenate([jnp.sin(angles), jnp.sin(angles)], axis=-1)[:, None, :]
    return (cosine_table, sine_values)


def rotate(head_rows, cosine_table, sine_values):
    half_width = head_rows.shape[-1] // 2
    turned = jnp.concatenate([-head_rows[..., half_width:], head_rows[..., :half_width]], axis=-1)
    return head_rows * cosine_table + turned * sine_values


def prepare_heads(projected, gain_row, cosine_table, sine_values):
    return rotate(rms_scale(projected, gain_row), cosine_table, sine_values)


def swiglu(gate_act, up_act):
    return jax.nn.silu(gate_act) * up_act


def slot_tables(route_rows, gate_rows, expert_count, capacity):
    sequence_length = route_rows.shape[0]
    top_count = route_rows.shape[1]
    pick_count = sequence_length * top_count
    tile_count = pick_count // TILE_PICKS
    flat_routes = route_rows.reshape(-1)
    onehot = (flat_routes[:, None] == jnp.arange(expert_count, dtype=jnp.int32)[None, :]).astype(
        jnp.bfloat16
    )
    tiles = onehot.reshape(tile_count, TILE_PICKS, expert_count)
    positions = jnp.arange(TILE_PICKS, dtype=jnp.int32)
    lower = (positions[None, :] < positions[:, None]).astype(jnp.bfloat16)
    within = jnp.einsum("ij,bje->bie", lower, tiles, preferred_element_type=jnp.float32)
    tile_totals = jnp.sum(tiles.astype(jnp.float32), axis=1)
    offsets = jnp.cumsum(tile_totals, axis=0) - tile_totals
    before = within + offsets[:, None, :]
    slot_rank = jnp.sum(before * tiles.astype(jnp.float32), axis=-1).reshape(-1).astype(jnp.int32)
    slot_index = flat_routes * capacity + slot_rank
    pick_ids = jnp.arange(pick_count, dtype=jnp.int32) // top_count
    slot_owner = (
        jnp.full((expert_count * capacity,), sequence_length, jnp.int32)
        .at[slot_index]
        .set(pick_ids)
    )
    slot_weight = (
        jnp.zeros((expert_count * capacity,), jnp.float32).at[slot_index].set(gate_rows.reshape(-1))
    )
    return (slot_index, slot_owner, slot_weight)


def exchanged_layer(
    tokens,
    cotangent,
    norm1_gain,
    w_query,
    key_projection_weight,
    value_projection_weight,
    query_gain,
    key_gain,
    w_out,
    norm2_gain,
    w_gate,
    w_up,
    w_down,
    routes,
    gates,
):
    batch_count = tokens.shape[0]
    model_width = tokens.shape[3]
    sequence_length = routes.shape[2]
    top_count = routes.shape[3]
    head_features = query_gain.shape[0]
    local_experts = w_gate.shape[0]
    fsdp_count = lax.axis_size("fsdp")
    all_experts = local_experts * fsdp_count
    capacity = 7 * top_count * sequence_length // (6 * all_experts)
    query_heads = w_query.shape[1] // head_features
    kv_heads = key_projection_weight.shape[1] // head_features
    group_size = query_heads // kv_heads
    score_scale = head_features ** (-0.5)
    cosine_table, sine_values = rotary_tables(sequence_length, head_features)
    block_ids = jnp.arange(sequence_length, dtype=jnp.int32) // BLOCK
    visible = (block_ids[None, :] <= block_ids[:, None])[None, None]
    first_gain = norm1_gain.astype(jnp.float32)
    second_gain = norm2_gain.astype(jnp.float32)
    query_factor_scale = query_gain.astype(jnp.float32)
    key_scale = key_gain.astype(jnp.float32)
    zero_row = jnp.zeros((1, model_width), jnp.bfloat16)
    buffer_shape = (fsdp_count, local_experts, capacity, model_width)

    def masked_scores(query_fourfold, key_rows):
        raw_scores = (
            jnp.einsum(
                "qcgd,kcd->cgqk", query_fourfold, key_rows, preferred_element_type=jnp.float32
            )
            * score_scale
        )
        return jnp.where(visible, raw_scores, MASKED)

    def prep_heads(projected, gain_row):
        return prepare_heads(projected, gain_row, cosine_table, sine_values)

    gain_sums = (
        jnp.zeros((model_width,), jnp.float32),
        jnp.zeros((model_width,), jnp.float32),
        jnp.zeros((head_features,), jnp.float32),
        jnp.zeros((head_features,), jnp.float32),
    )
    expert_grads = (
        jnp.zeros(w_gate.shape, jnp.float32),
        jnp.zeros(w_up.shape, jnp.float32),
        jnp.zeros(w_down.shape, jnp.float32),
    )
    attn_grads = tuple(
        (
            jnp.zeros(weight_part.shape, jnp.float32)
            for weight_part in (w_query, key_projection_weight, value_projection_weight, w_out)
        )
    )
    outputs = []
    input_grads = []
    for batch_index in range(batch_count):
        query_full, key_full, value_full, out_full = (
            lax.all_gather(w_query, "fsdp", axis=0, tiled=True),
            lax.all_gather(key_projection_weight, "fsdp", axis=0, tiled=True),
            lax.all_gather(value_projection_weight, "fsdp", axis=0, tiled=True),
            lax.all_gather(w_out, "fsdp", axis=1, tiled=True),
        )
        own_rows = tokens[batch_index, 0].astype(jnp.float32)
        own_cot = cotangent[batch_index, 0]
        route_rows = routes[batch_index, 0]
        gate_rows = gates[batch_index, 0]
        first_normed = rms_scale(own_rows, first_gain).astype(jnp.bfloat16)
        normed_all = lax.all_gather(first_normed, "tp", axis=0, tiled=True)
        query_projected = jnp.dot(
            normed_all, query_full, preferred_element_type=jnp.float32
        ).reshape(sequence_length, query_heads, head_features)
        key_projected = jnp.dot(normed_all, key_full, preferred_element_type=jnp.float32).reshape(
            sequence_length, kv_heads, head_features
        )
        value_row_list = (
            jnp.dot(normed_all, value_full, preferred_element_type=jnp.float32)
            .astype(jnp.bfloat16)
            .reshape(sequence_length, kv_heads, head_features)
        )
        query_rot = prep_heads(query_projected, query_factor_scale).astype(jnp.bfloat16)
        key_rot = prep_heads(key_projected, key_scale).astype(jnp.bfloat16)
        query_fourfold = query_rot.reshape(sequence_length, kv_heads, group_size, head_features)
        scores = masked_scores(query_fourfold, key_rot)
        row_max = jnp.max(scores, axis=-1, keepdims=True)
        exp_scores = jnp.exp(scores - row_max)
        totals = jnp.sum(exp_scores, axis=-1, keepdims=True)
        log_total = row_max + jnp.log(totals)
        prob_rows = (exp_scores / totals).astype(jnp.bfloat16)
        context = (
            jnp.einsum(
                "cgqk,kcd->qcgd", prob_rows, value_row_list, preferred_element_type=jnp.float32
            )
            .astype(jnp.bfloat16)
            .reshape(sequence_length, query_heads * head_features)
        )
        attn_own = lax.psum_scatter(
            jnp.dot(context, out_full, preferred_element_type=jnp.float32).astype(jnp.bfloat16),
            "tp",
            scatter_dimension=0,
            tiled=True,
        ).astype(jnp.float32)
        hidden_own = own_rows + attn_own
        second_normed = rms_scale(hidden_own, second_gain).astype(jnp.bfloat16)
        normed_two, cot_all = (
            lax.all_gather(second_normed, "tp", axis=0, tiled=True),
            lax.all_gather(own_cot, "tp", axis=0, tiled=True),
        )
        slot_index, slot_owner, slot_weight = slot_tables(
            route_rows, gate_rows, all_experts, capacity
        )
        padded_rows = jnp.concatenate([normed_two, zero_row], axis=0)
        send_rows = padded_rows[slot_owner].reshape(buffer_shape)
        expert_in = lax.all_to_all(send_rows, "fsdp", split_axis=0, concat_axis=0, tiled=True)
        gate_act = jnp.einsum(
            "sekd,edf->sekf", expert_in, w_gate, preferred_element_type=jnp.float32
        )
        up_act = jnp.einsum("sekd,edf->sekf", expert_in, w_up, preferred_element_type=jnp.float32)
        act_rows = swiglu(gate_act, up_act).astype(jnp.bfloat16)
        expert_out = jnp.einsum(
            "sekf,efd->sekd", act_rows, w_down, preferred_element_type=jnp.float32
        )
        returned = lax.all_to_all(
            expert_out.astype(jnp.bfloat16), "fsdp", split_axis=0, concat_axis=0, tiled=True
        ).astype(expert_out.dtype)
        picked = returned.reshape(all_experts * capacity, model_width)[slot_index].reshape(
            sequence_length, top_count, model_width
        )
        moe_part = jnp.sum(picked * gate_rows[:, :, None], axis=1)
        moe_own = lax.psum_scatter(
            moe_part.astype(jnp.bfloat16), "tp", scatter_dimension=0, tiled=True
        ).astype(jnp.float32)
        outputs.append((hidden_own + moe_own).astype(jnp.bfloat16))
        cot_padded = jnp.concatenate([cot_all, zero_row], axis=0)
        send_grads = (
            (slot_weight[:, None] * cot_padded[slot_owner])
            .astype(jnp.bfloat16)
            .reshape(buffer_shape)
        )
        out_grads = lax.all_to_all(send_grads, "fsdp", split_axis=0, concat_axis=0, tiled=True)
        act_grads = jnp.einsum(
            "sekd,efd->sekf", out_grads, w_down, preferred_element_type=jnp.float32
        )
        _, swiglu_back = jax.vjp(swiglu, gate_act, up_act)
        gate_grads, up_grads = swiglu_back(act_grads)
        gate_grads = gate_grads.astype(jnp.bfloat16)
        up_grads = up_grads.astype(jnp.bfloat16)
        expert_grads = (
            expert_grads[0]
            + jnp.einsum(
                "sekd,sekf->edf", expert_in, gate_grads, preferred_element_type=jnp.float32
            ),
            expert_grads[1]
            + jnp.einsum("sekd,sekf->edf", expert_in, up_grads, preferred_element_type=jnp.float32),
            expert_grads[2]
            + jnp.einsum("sekf,sekd->efd", act_rows, out_grads, preferred_element_type=jnp.float32),
        )
        input_part = jnp.einsum(
            "sekf,edf->sekd", gate_grads, w_gate, preferred_element_type=jnp.float32
        ) + jnp.einsum("sekf,edf->sekd", up_grads, w_up, preferred_element_type=jnp.float32)
        input_back = lax.all_to_all(
            input_part.astype(jnp.bfloat16), "fsdp", split_axis=0, concat_axis=0, tiled=True
        ).astype(input_part.dtype)
        normed_grads = jnp.sum(
            input_back.reshape(all_experts * capacity, model_width)[slot_index].reshape(
                sequence_length, top_count, model_width
            ),
            axis=1,
        )
        normed_own = lax.psum_scatter(
            normed_grads.astype(jnp.bfloat16), "tp", scatter_dimension=0, tiled=True
        ).astype(jnp.float32)
        _, second_back = jax.vjp(rms_scale, hidden_own, second_gain)
        hidden_part, second_gain_grad = second_back(normed_own)
        hidden_grad = own_cot.astype(jnp.float32) + hidden_part
        attn_grad_all = lax.all_gather(hidden_grad.astype(jnp.bfloat16), "tp", axis=0, tiled=True)
        out_weight_grad = jnp.einsum(
            "th,td->hd", context, attn_grad_all, preferred_element_type=jnp.float32
        )
        context_grad = (
            jnp.einsum("td,hd->th", attn_grad_all, out_full, preferred_element_type=jnp.float32)
            .astype(jnp.bfloat16)
            .reshape(sequence_length, kv_heads, group_size, head_features)
        )
        exp_again = jnp.exp(masked_scores(query_fourfold, key_rot) - log_total)
        probs_again = exp_again.astype(jnp.bfloat16)
        prob_grads = jnp.einsum(
            "qcgd,kcd->cgqk", context_grad, value_row_list, preferred_element_type=jnp.float32
        )
        value_grads = (
            jnp.einsum(
                "cgqk,qcgd->kcd", probs_again, context_grad, preferred_element_type=jnp.float32
            )
            .astype(jnp.bfloat16)
            .reshape(sequence_length, kv_heads * head_features)
        )
        score_grads = (
            exp_again * (prob_grads - jnp.sum(exp_again * prob_grads, axis=-1, keepdims=True))
        ).astype(jnp.bfloat16)
        query_rot_grads = (
            jnp.einsum("cgqk,kcd->qcgd", score_grads, key_rot, preferred_element_type=jnp.float32)
            * score_scale
        ).reshape(sequence_length, query_heads, head_features)
        key_rot_grads = (
            jnp.einsum(
                "cgqk,qcgd->kcd", score_grads, query_fourfold, preferred_element_type=jnp.float32
            )
            * score_scale
        )
        _, query_back = jax.vjp(prep_heads, query_projected, query_factor_scale)
        query_proj_grads, query_gain_grad = query_back(query_rot_grads)
        _, key_back = jax.vjp(prep_heads, key_projected, key_scale)
        key_proj_grads, key_gain_grad = key_back(key_rot_grads)
        query_proj_grads = query_proj_grads.astype(jnp.bfloat16).reshape(
            sequence_length, query_heads * head_features
        )
        key_proj_grads = key_proj_grads.astype(jnp.bfloat16).reshape(
            sequence_length, kv_heads * head_features
        )
        first_normed_grads = (
            jnp.einsum(
                "tq,dq->td", query_proj_grads, query_full, preferred_element_type=jnp.float32
            )
            + jnp.einsum("tq,dq->td", key_proj_grads, key_full, preferred_element_type=jnp.float32)
            + jnp.einsum("tq,dq->td", value_grads, value_full, preferred_element_type=jnp.float32)
        )
        weight_parts = (
            jnp.einsum(
                "td,tq->dq", normed_all, query_proj_grads, preferred_element_type=jnp.float32
            ),
            jnp.einsum("td,tq->dq", normed_all, key_proj_grads, preferred_element_type=jnp.float32),
            jnp.einsum("td,tq->dq", normed_all, value_grads, preferred_element_type=jnp.float32),
            out_weight_grad,
        )
        first_own = lax.psum_scatter(
            first_normed_grads.astype(jnp.bfloat16), "tp", scatter_dimension=0, tiled=True
        ).astype(jnp.float32)
        _, first_back = jax.vjp(rms_scale, own_rows, first_gain)
        row_part, first_gain_grad = first_back(first_own)
        input_grads.append((hidden_grad + row_part).astype(jnp.bfloat16))
        gain_sums = (
            gain_sums[0] + first_gain_grad,
            gain_sums[1] + second_gain_grad,
            gain_sums[2] + query_gain_grad,
            gain_sums[3] + key_gain_grad,
        )
        attn_grads = jax.tree.map(
            jnp.add,
            attn_grads,
            (
                lax.psum_scatter(weight_parts[0], "fsdp", scatter_dimension=0, tiled=True),
                lax.psum_scatter(weight_parts[1], "fsdp", scatter_dimension=0, tiled=True),
                lax.psum_scatter(weight_parts[2], "fsdp", scatter_dimension=0, tiled=True),
                lax.psum_scatter(weight_parts[3], "fsdp", scatter_dimension=1, tiled=True),
            ),
        )
    summed = lax.psum((gain_sums[0], gain_sums[1], gain_sums[2], gain_sums[3]), ("fsdp", "tp"))
    block_out = jnp.stack(outputs)[:, None]
    input_grad = jnp.stack(input_grads)[:, None]
    return (
        block_out,
        input_grad,
        summed[0],
        attn_grads[0],
        attn_grads[1],
        attn_grads[2],
        summed[2],
        summed[3],
        attn_grads[3],
        summed[1],
        expert_grads[0],
        expert_grads[1],
        expert_grads[2],
    )


MESH = pl.DeviceIdType.MESH
FSDP, TP = "fsdp", "tp"
PLANE = 4
LANES = 128
MIB = 1 << 20
RIGHT, LEFT, FIRST, SECOND, CORE, CROSS = range(6)
TRANSPOSED_LEFT = (((0,), (0,)), ((), ()))
TRANSPOSED_RIGHT = (((1,), (1,)), ((), ()))
OUTPUT, BACK = range(2)
CHUNK = 512


class Spot:
    def __init__(self, line, wide, turned=True):
        self.line = line
        self.wide = wide
        self.turned = turned
        self.planes = 4 if wide else 2
        index = lax.axis_index(FSDP)
        self.x = lax.axis_index(TP)
        self.z = lax.div(index, PLANE)
        self.y = lax.rem(lax.div(index, 2), 2)
        self.core = lax.rem(index, 2)

    def side(self, core, first, second):
        flip_y, flip_x = first, second
        if self.wide and self.turned:
            flip_y = (1 - core) * first + core * second
            flip_x = core * first + (1 - core) * second
        return self.y + flip_y * (1 - 2 * self.y), self.x + flip_x * (1 - 2 * self.x)

    def block(self, core, first, second, z):
        y, x = self.side(core, first, second)
        return z * PLANE + y * 2 + core, x

    def device(self, kind):
        if kind == RIGHT:
            return self.block(self.core, 0, 0, self.z + 1)
        if kind == LEFT:
            return self.block(self.core, 0, 0, self.z - 1)
        if kind == CORE:
            return self.block(1 - self.core, 0, 0, self.z)
        if kind == CROSS:
            return self.block(self.core, 0, 0, self.z)[0], 1 - self.x
        return self.block(self.core, int(kind == FIRST), int(kind == SECOND), self.z)

    def kinds(self):
        return (FIRST, SECOND, CORE) if self.wide else (FIRST, CORE)

    def number(self, first, second, z):
        return (second * 2 + first) * self.line + z

    def order(self, step):
        if isinstance(step, int) and step == 0:
            return [(self.z, None)]
        return [(self.z - step, self.z - step >= 0), (self.z + step, self.z + step < self.line)]

    def greet(self):
        barrier = pltpu.get_barrier_semaphore()

        def signal(kind):
            pl.semaphore_signal(barrier, inc=1, device_id=self.device(kind), device_id_type=MESH)

        for kind in self.kinds():
            signal(kind)
        when(self.z + 1 < self.line, lambda: signal(RIGHT))
        when(self.z > 0, lambda: signal(LEFT))
        around = (self.z + 1 < self.line).astype(jnp.int32) + (self.z > 0).astype(jnp.int32)
        pl.semaphore_wait(barrier, len(self.kinds()) + around)

    def send(self, source, target, send_sem, receive_sem, kind):
        return pltpu.make_async_remote_copy(
            src_ref=source,
            dst_ref=target,
            send_sem=send_sem,
            recv_sem=receive_sem,
            device_id=self.device(kind),
            device_id_type=MESH,
        )


def when(condition, action):
    def run():
        action()

    if condition is None or condition is True:
        run()
    elif condition is not False:
        pl.when(condition)(run)


class Spread:
    def __init__(self, spot, source, slot, send, receive, local):
        self.spot = spot
        self.slot = slot
        self.source = source
        self.sends = send
        self.receives = receive
        self.mine = pltpu.make_async_copy(source, slot(*spot.block(spot.core, 0, 0, spot.z)), local)

    def copy(self, first, second, z, kind, own=False):
        spot = self.spot
        place = self.slot(*spot.block(spot.core, first, second, z))
        number = spot.number(first, second, z)
        arrival = {
            RIGHT: number,
            LEFT: number,
            FIRST: spot.number(1, 0, z),
            SECOND: spot.number(first, 1, z),
            CORE: spot.planes * spot.line + number,
        }[kind]
        departure = {RIGHT: 0, LEFT: 1, FIRST: 2, SECOND: 3, CORE: 5}[kind] * spot.line + number
        source = self.source if own else place
        return spot.send(source, place, self.sends.at[departure], self.receives.at[arrival], kind)

    def arrived(self, first, second, z, other=False):
        spot = self.spot
        core = 1 - spot.core if other else spot.core
        place = self.slot(*spot.block(core, first, second, z))
        number = spot.number(first, second, z) + (spot.planes * spot.line if other else 0)
        spot.send(place, place, self.sends.at[0], self.receives.at[number], CORE).wait_recv()

    def steps(self):
        return self.spot.line + (3 if self.spot.wide else 1)

    def begin(self):
        spot = self.spot
        z = spot.z
        when(z + 1 < spot.line, lambda: self.copy(0, 0, z, RIGHT, True).start())
        when(z > 0, lambda: self.copy(0, 0, z, LEFT, True).start())
        for kind in spot.kinds():
            self.copy(0, 0, z, kind, True).start()
        self.mine.start()

    def step(self, step):
        spot = self.spot
        line, z = spot.line, spot.z

        def reached(away, action):
            inside = jnp.logical_and(away >= 0, away < line)
            when(jnp.logical_and(inside, z - away >= 0), lambda: action(z - away, True))
            when(
                jnp.logical_and(inside, jnp.logical_and(away > 0, z + away < line)),
                lambda: action(z + away, False),
            )

        def along(zz, from_left):
            self.arrived(0, 0, zz)
            if from_left:
                when(z + 1 < line, lambda: self.copy(0, 0, zz, RIGHT).start())
            else:
                when(z > 0, lambda: self.copy(0, 0, zz, LEFT).start())
            for kind in spot.kinds():
                self.copy(0, 0, zz, kind).start()

        def firsts(zz, _):
            self.arrived(1, 0, zz)
            if spot.wide:
                self.copy(1, 0, zz, SECOND).start()
            self.copy(1, 0, zz, CORE).start()

        def lasts(first):
            def action(zz, _):
                self.arrived(first, 1, zz)
                self.copy(first, 1, zz, CORE).start()

            return action

        step = jnp.asarray(step, jnp.int32)
        reached(step, along)
        reached(step - 1, firsts)
        if spot.wide:
            reached(step - 2, lasts(0))
            reached(step - 3, lasts(1))

    def finish(self):
        spot = self.spot
        z = spot.z

        def body(zz, _):
            when(
                jnp.logical_and(z + 1 < spot.line, zz <= z),
                lambda: self.copy(0, 0, zz, RIGHT).wait_send(),
            )
            when(jnp.logical_and(z > 0, zz >= z), lambda: self.copy(0, 0, zz, LEFT).wait_send())
            self.copy(0, 0, zz, FIRST).wait_send()
            for second in range(2 if spot.wide else 1):
                for first in (0, 1):
                    if spot.wide and not second:
                        self.copy(first, 0, zz, SECOND).wait_send()
                    self.copy(first, second, zz, CORE).wait_send()
                    self.arrived(first, second, zz, other=True)
            return 0

        lax.fori_loop(0, spot.line, body, 0)
        self.mine.wait()


class LateSpread(Spread):
    def steps(self):
        return self.spot.line + 2

    def copy(self, first, second, z, kind, own=False):
        spot = self.spot
        place = self.slot(*spot.block(spot.core, first, second, z))
        number = spot.number(first, second, z)
        arrival = {
            RIGHT: number,
            LEFT: number,
            FIRST: spot.number(1, 0, z),
            SECOND: spot.number(first, 1, z),
            CORE: spot.planes * spot.line + number,
        }[kind]
        departure = {RIGHT: 0, LEFT: 4, CORE: 8, FIRST: 12, SECOND: 13}[kind] * spot.line + number
        source = self.source if own else place
        return spot.send(source, place, self.sends.at[departure], self.receives.at[arrival], kind)

    def along_both(self, first, second, own=False):
        spot = self.spot
        z = spot.z
        when(z + 1 < spot.line, lambda: self.copy(first, second, z, RIGHT, own).start())
        when(z > 0, lambda: self.copy(first, second, z, LEFT, own).start())
        self.copy(first, second, z, CORE, own).start()

    def begin(self):
        self.copy(0, 0, self.spot.z, FIRST, True).start()
        self.copy(0, 0, self.spot.z, SECOND, True).start()
        self.along_both(0, 0, True)
        self.mine.start()

    def step(self, step):
        spot = self.spot
        line, z = spot.line, spot.z
        step = jnp.asarray(step, jnp.int32)

        def passed(first, second, zz, kind, more):
            self.arrived(first, second, zz)
            when(more, lambda: self.copy(first, second, zz, kind).start())
            self.copy(first, second, zz, CORE).start()

        for first, second in ((0, 0), (1, 0), (0, 1), (1, 1)):
            away = step - (first + second)

            def here():
                self.arrived(first, second, z)
                if first and not second:
                    self.copy(1, 0, z, SECOND).start()
                self.along_both(first, second)

            if first or second:
                when(away == 0, here)
            far = jnp.logical_and(away > 0, away < line)
            when(
                jnp.logical_and(far, z - away >= 0),
                lambda: passed(first, second, z - away, RIGHT, z + 1 < line),
            )
            when(
                jnp.logical_and(far, z + away < line),
                lambda: passed(first, second, z + away, LEFT, z > 0),
            )

    def finish(self):
        spot = self.spot
        z = spot.z

        def body(zz, _):
            for second in (0, 1):
                for first in (0, 1):
                    when(
                        jnp.logical_and(z + 1 < spot.line, zz <= z),
                        lambda: self.copy(first, second, zz, RIGHT).wait_send(),
                    )
                    when(
                        jnp.logical_and(z > 0, zz >= z),
                        lambda: self.copy(first, second, zz, LEFT).wait_send(),
                    )
                    self.copy(first, second, zz, CORE).wait_send()
                    self.arrived(first, second, zz, other=True)
            return 0

        lax.fori_loop(0, spot.line, body, 0)
        self.copy(0, 0, z, FIRST).wait_send()
        for first in (0, 1):
            self.copy(first, 0, z, SECOND).wait_send()
        self.mine.wait()


def rows_spread(spot, source, place, rows, semaphores, at):
    late = late_rows(rows)
    early = rows - late
    send, receive, late_send, late_receive, local = semaphores

    def slot(start, size):
        return lambda block, side: place(block, side * rows + start, size)

    return [
        Spread(
            spot,
            source.at[pl.ds(0, early)],
            slot(0, early),
            send.at[at],
            receive.at[at],
            local.at[at, 0],
        ),
        LateSpread(
            spot,
            source.at[pl.ds(early, late)],
            slot(early, late),
            late_send.at[at],
            late_receive.at[at],
            local.at[at, 1],
        ),
    ]


def late_rows(rows):
    return max(16, round(rows * 2 / 9 / 16) * 16)


def rows_semaphores(batch, line):
    counts = (*spread_count(line, True), 15 * line, 8 * line, 2)
    return [pltpu.SemaphoreType.DMA((batch, count)) for count in counts]


def run_trees(trees):
    for tree in trees:
        tree.begin()

    def body(step, _):
        for tree in trees:
            tree.step(step)
        return 0

    lax.fori_loop(1, max(tree.steps() for tree in trees), body, 0)
    for tree in trees:
        tree.finish()


def spread_count(line, wide):
    return (9 if wide else 7) * line, (8 if wide else 4) * line


def mingle(work, others):
    for index, piece in enumerate(work):
        piece()
        for other in others[
            index * len(others) // len(work) : (index + 1) * len(others) // len(work)
        ]:
            other()


def rows_at(ref, index, size):
    return ref.at[pl.ds(pl.multiple_of(index * size, 16), size)]


def columns_at(ref, index, size):
    return ref.at[:, pl.ds(pl.multiple_of(index * size, LANES), size)]


def norm_rows(target, source, gain):
    def body(step, _):
        rows = pl.ds(pl.multiple_of(step * 16, 16), 16)
        value = source[rows, :].astype(jnp.float32)
        target[rows, :] = rms_scale(value, gain[...].astype(jnp.float32)).astype(target.dtype)
        return 0

    lax.fori_loop(0, target.shape[0] // 16, body, 0)


def turned_heads(value, gain, cosine, sine):
    normed = rms_scale(value, gain)
    return normed * cosine + pltpu.roll(normed, normed.shape[-1] // 2, 1) * sine


def visible_blocks(length, group):
    blocks = []
    for start in range(0, length, BLOCK):
        stop = min(start + BLOCK, length)
        heads = max(1, BLOCK // (stop - start))
        while group % heads:
            heads -= 1
        blocks.append((start, stop, stop, heads))
    return blocks


def softmax(scores):
    raised = jnp.exp(scores - jnp.max(scores, axis=0, keepdims=True))
    return raised * (1.0 / jnp.sum(raised, axis=0, keepdims=True))


def for_heads(low, high, heads, body):
    turns = 2 if heads == 1 and (high - low) % 2 == 0 else 1

    def turn(step, _):
        for i in range(turns):
            body(low + (step * turns + i) * heads)
        return 0

    count = (high - low) // (heads * turns)
    if count == 1:
        turn(0, 0)
    else:
        lax.fori_loop(0, count, turn, 0)


def head_columns(head, features):
    return pl.ds(pl.multiple_of(head * features, LANES), features)


def forward_kernel(
    line,
    heads,
    kv_heads,
    tokens_ref,
    cot_ref,
    in_ref,
    out_ref,
    picks_ref,
    gain1_ref,
    gain2_ref,
    query_gain_ref,
    key_gain_ref,
    cosine_ref,
    sine_ref,
    cot_all,
    in_all,
    out_all,
    picks_all,
    normed_all,
    projected_all,
    context_all,
    hidden_all,
    second_all,
    in_w,
    out_w,
    tokens,
    normed,
    projected,
    context,
    queries,
    keys,
    values,
    mixed,
    mixed_other,
    hidden,
    second,
    narrow_send,
    narrow_receive,
    cot_send,
    cot_receive,
    cot_late_send,
    cot_late_receive,
    cot_local,
    local,
    token_send,
    token_receive,
    mixed_send,
    mixed_receive,
    save_sem,
):
    cot_semaphores = (cot_send, cot_receive, cot_late_send, cot_late_receive, cot_local)
    batch, half, width = tokens_ref.shape
    length = 2 * half
    depth, out_width = in_ref.shape[0], out_ref.shape[1]
    features = query_gain_ref.shape[1]
    narrow = Spot(line, False)
    spot = Spot(line, True, turned=False)
    x = spot.x
    spot.greet()
    slots = [
        (picks_ref, lambda block, side: picks_all.at[block]),
        (in_ref, lambda block, side: rows_at(in_w, block, depth)),
        (out_ref, lambda block, side: columns_at(out_w, block, out_width)),
    ]
    weights = [
        Spread(narrow, source, slot, narrow_send.at[i], narrow_receive.at[i], local.at[i])
        for i, (source, slot) in enumerate(slots)
    ]
    place = lambda block, start, size: cot_all.at[block, pl.ds(pl.multiple_of(start, 16), size)]
    cots = rows_spread(spot, cot_ref.at[0], place, half, cot_semaphores, 0)
    early, late = weights[:2], weights[2]
    for tree in early:
        tree.begin()

    def token_copies(i):
        place = rows_at(tokens.at[i], x, half)
        return (
            pltpu.make_async_copy(tokens_ref.at[i], place, local.at[3 + i]),
            spot.send(tokens_ref.at[i], place, token_send.at[i], token_receive.at[i], CROSS),
        )

    for i in range(batch):
        for copy in token_copies(i):
            copy.start()
    def steps(step, _):
        for tree in early:
            tree.step(step)
        return 0

    lax.fori_loop(1, late.steps(), steps, 0)
    late.begin()
    for tree in cots:
        tree.begin()
    for i in range(batch):
        mine, other = token_copies(i)
        mine.wait()
        other.wait_send()
        place = rows_at(tokens.at[i], 1 - x, half)
        spot.send(place, place, token_send.at[i], token_receive.at[i], CROSS).wait_recv()
    for i in range(batch):
        norm_rows(normed.at[i], tokens.at[i], gain1_ref)
    for tree in early:
        tree.finish()

    def save(source, target, index):
        return pltpu.make_async_copy(source, target, save_sem.at[index])

    saves = [save(in_w, in_all, 0), save(out_w, out_all, 1)]
    saves[0].start()

    def project(i, start, stop):
        for at in range(start, stop, CHUNK):
            projected[i, :, at : at + CHUNK] = jnp.dot(
                normed[i], in_w[:, at : at + CHUNK], preferred_element_type=jnp.float32
            )

    scale = features ** (-0.5)

    group = heads // kv_heads

    def prepare_keys(i):
        base = heads * features
        for head in range(kv_heads):
            at = base + head * features
            keys[head] = turned_heads(
                projected[i, :, at : at + features],
                key_gain_ref[...].astype(jnp.float32),
                cosine_ref[...],
                sine_ref[...],
            ).astype(jnp.bfloat16)
            at = base + (kv_heads + head) * features
            values[head] = projected[i, :, at : at + features].astype(jnp.bfloat16)

    def prepare_queries(i, shared):
        def prepare(member):
            columns = head_columns(shared * group + member, features)
            queries[member] = turned_heads(
                projected[i, :, columns], query_gain_ref[...].astype(jnp.float32), cosine_ref[...], sine_ref[...]
            ).astype(jnp.bfloat16)

        for_heads(0, group, 1, prepare)

    def attend(i, shared, start, stop, seen, at_once, low, high):
        count = stop - start

        def block(member):
            query = queries[pl.ds(member, at_once), start:stop, :].reshape(-1, features)
            scores = lax.dot_general(
                keys[shared, :seen, :],
                query,
                TRANSPOSED_RIGHT,
                preferred_element_type=jnp.float32,
            )
            rows = lax.dot_general(
                softmax(scores * scale).astype(jnp.bfloat16),
                values[shared, :seen, :],
                TRANSPOSED_LEFT,
                preferred_element_type=jnp.float32,
            ).astype(jnp.bfloat16)
            for j in range(at_once):
                columns = head_columns(shared * group + member + j, features)
                context[i, start:stop, columns] = rows[j * count : (j + 1) * count]

        for_heads(low, high, at_once, block)

    def mixed_copy(i):
        return spot.send(
            rows_at(mixed.at[i], 1 - x, half),
            mixed_other.at[i],
            mixed_send.at[i],
            mixed_receive.at[i],
            CROSS,
        )

    def mix(i, start, stop):
        for at in range(start, stop, CHUNK):
            mixed[i, :, at : at + CHUNK] = jnp.dot(
                context[i], out_w[:, at : at + CHUNK], preferred_element_type=jnp.float32
            ).astype(jnp.bfloat16)
        if stop == width:
            mixed_copy(i).start()

    def close(i):
        mixed_copy(i).wait()
        add_rows(
            hidden.at[i],
            [rows_at(tokens.at[i], x, half), rows_at(mixed.at[i], x, half), mixed_other.at[i]],
        )
        norm_rows(second.at[i], hidden.at[i], gain2_ref)

    def late_done():
        late.finish()
        saves[1].start()

    def steps_of(trees, low, high):
        return [
            functools.partial(tree.step, step)
            for step in range(low, high)
            for tree in trees
            if step < tree.steps()
        ]

    in_width = in_w.shape[1]
    parts = lambda size: [(at, min(at + 2 * CHUNK, size)) for at in range(0, size, 2 * CHUNK)]
    opening, middle, closing = [], [], []
    for i in range(batch):
        opening += [functools.partial(project, i, *part) for part in parts(in_width)]
        middle.append(functools.partial(prepare_keys, i))
        for shared in range(kv_heads):
            middle.append(functools.partial(prepare_queries, i, shared))
            for start, stop, seen, at_once in visible_blocks(length, group):
                share = max(at_once, group // 2)
                for low in range(0, group, share):
                    middle.append(
                        functools.partial(
                            attend, i, shared, start, stop, seen, at_once, low, low + share
                        )
                    )
        closing += [functools.partial(mix, i, *part) for part in parts(width)]
    closing += [functools.partial(close, i) for i in range(batch)]
    last = cots[0].steps()
    mingle(opening + middle, steps_of([late] + cots, 1, late.steps()))
    late_done()
    mingle(closing, steps_of(cots, late.steps(), last))

    saves += [
        save(source, target, 2 + i)
        for i, (source, target) in enumerate(
            [
                (normed, normed_all),
                (projected, projected_all),
                (context, context_all),
                (hidden, hidden_all),
                (second, second_all),
            ]
        )
    ]
    for copy in saves[2:]:
        copy.start()
    for tree in cots:
        tree.finish()
    for copy in saves:
        copy.wait()


def run_forward(tokens, cot, weight_in, weight_out, picks, gains, tables, fsdp_count, kv_heads):
    line = fsdp_count // PLANE
    batch, half, width = tokens.shape
    length = 2 * half
    features = gains[2].shape[1]
    heads = weight_out.shape[0] // features
    in_shape = (weight_in.shape[0] * fsdp_count, weight_in.shape[1])
    out_shape = (weight_out.shape[0], weight_out.shape[1] * fsdp_count)
    narrow = spread_count(line, False)
    anywhere = pl.BlockSpec(memory_space=pl.ANY)
    inside = pl.BlockSpec(memory_space=pltpu.VMEM)
    shape = lambda dims, kind=jnp.bfloat16: jax.ShapeDtypeStruct(dims, kind)
    vmem = lambda *dims: pltpu.VMEM(dims, jnp.bfloat16)
    sem = lambda *dims: pltpu.SemaphoreType.DMA(dims)
    kept = (
        ((batch, length, width), jnp.bfloat16),
        ((batch, length, weight_in.shape[1]), jnp.float32),
        ((batch, length, heads * features), jnp.bfloat16),
        ((batch, half, width), jnp.float32),
        ((batch, half, width), jnp.bfloat16),
    )
    return pl.pallas_call(
        functools.partial(forward_kernel, line, heads, kv_heads),
        out_shape=(
            shape((fsdp_count, length, width)),
            shape(in_shape),
            shape(out_shape),
            shape((fsdp_count, *picks.shape), picks.dtype),
            *(shape(*one) for one in kept),
        ),
        in_specs=[anywhere] * 5 + [inside] * 6,
        out_specs=(anywhere,) * 9,
        scratch_shapes=[
            vmem(*in_shape),
            vmem(*out_shape),
            vmem(batch, length, width),
            *(pltpu.VMEM(*one) for one in kept[:3]),
            vmem(heads // kv_heads, length, features),
            vmem(kv_heads, length, features),
            vmem(kv_heads, length, features),
            vmem(batch, length, width),
            vmem(batch, half, width),
            *(pltpu.VMEM(*one) for one in kept[3:]),
            sem(3, narrow[0]),
            sem(3, narrow[1]),
            *rows_semaphores(1, line),
            sem(3 + batch),
            sem(batch),
            sem(batch),
            sem(batch),
            sem(batch),
            sem(7),
        ],
        compiler_params=pltpu.CompilerParams(
            collective_id=1, has_side_effects=True, vmem_limit_bytes=60 * MIB
        ),
    )(tokens, cot, weight_in, weight_out, picks, *gains, *tables)


def add_rows(target, sources):
    def body(step, _):
        rows = pl.ds(pl.multiple_of(step * 16, 16), 16)
        total = sources[0][rows, :].astype(jnp.float32)
        for source in sources[1:]:
            total = total + source[rows, :].astype(jnp.float32)
        target[rows, :] = total.astype(target.dtype)
        return 0

    lax.fori_loop(0, target.shape[0] // 16, body, 0)


class Collect:
    def __init__(self, spot, part, total, cores, firsts, rights, lefts, send, receive):
        self.spot = spot
        self.part = part
        self.total = total
        self.places = {CORE: cores, FIRST: firsts, RIGHT: rights, LEFT: lefts}
        line = spot.line
        self.base = {CORE: 0, FIRST: 2 * line, RIGHT: 3 * line, LEFT: 4 * line}
        self.sends = send
        self.receives = receive

    def own(self, first, z):
        return self.part(*self.spot.block(self.spot.core, first, 0, z))

    def copy(self, kind, first, z):
        spot = self.spot
        number = first * spot.line + z if kind == CORE else z
        source = self.part(*spot.block(1 - spot.core, first, 0, z)) if kind == CORE else self.own(first, z)
        at = self.base[kind] + number
        return spot.send(
            source, self.places[kind].at[number], self.sends.at[at], self.receives.at[at], kind
        )

    def arrived(self, kind, number):
        place = self.places[kind].at[number]
        at = self.base[kind] + number
        self.spot.send(place, place, self.sends.at[0], self.receives.at[at], CORE).wait_recv()
        return place

    def begin(self, z):
        for first in (1, 0):
            self.copy(CORE, first, z).start()

    def to_first(self, z):
        add_rows(self.own(1, z), [self.own(1, z), self.arrived(CORE, self.spot.line + z)])
        self.copy(FIRST, 1, z).start()

    def summands(self, z):
        return [self.own(0, z), self.arrived(CORE, z), self.arrived(FIRST, z)]

    def cross(self):
        for step in reversed(range(self.spot.line)):
            for zz, valid in self.spot.order(step):
                when(valid, functools.partial(self.to_first, zz))

    def onward(self, kind, zz):
        spot = self.spot
        sources = self.summands(zz)
        target = self.own(0, zz)
        behind = spot.z > 0 if kind == RIGHT else spot.z + 1 < spot.line
        when(behind, lambda: add_rows(target, sources + [self.arrived(kind, zz)]))
        when(jnp.logical_not(behind), lambda: add_rows(target, sources))
        self.copy(kind, 0, zz).start()

    def last(self):
        z, line = self.spot.z, self.spot.line
        sources = self.summands(z)

        def end(kinds):
            add_rows(self.total, sources + [self.arrived(kind, z) for kind in kinds])

        when(z == 0, lambda: end([LEFT]))
        when(z == line - 1, lambda: end([RIGHT]))
        when(jnp.logical_and(z > 0, z < line - 1), lambda: end([RIGHT, LEFT]))

    def finish(self):
        spot = self.spot
        for zz in range(spot.line):
            for first in (0, 1):
                self.copy(CORE, first, zz).wait_send()
            self.copy(FIRST, 1, zz).wait_send()
            when(zz > spot.z, lambda: self.copy(RIGHT, 0, zz).wait_send())
            when(zz < spot.z, lambda: self.copy(LEFT, 0, zz).wait_send())

    def tasks(self):
        spot = self.spot
        work = []
        for step in reversed(range(1, spot.line)):
            for kind, (zz, valid) in zip((LEFT, RIGHT), spot.order(step)):
                action = functools.partial(self.onward, kind, zz)
                work.append(functools.partial(when, valid, action))
        return work + [self.last, self.finish]


def collect_scratch(line, shape):
    counts = (2 * line, line, line, line)
    return [pltpu.VMEM((count, *shape), jnp.bfloat16) for count in counts] + [
        pltpu.SemaphoreType.DMA((5 * line,)),
        pltpu.SemaphoreType.DMA((5 * line,)),
    ]


BOXES = 6


def plane_in_turn(line, group):
    turn = lax.rem(group, line)
    step = lax.div(turn, 2)
    return jnp.where(lax.rem(turn, 2) == 0, step, line - 1 - step)


class Sums:
    def __init__(
        self, spot, half, parts, cores, places, inbox, outbox, semaphores, late, plane, inside, ready, done, turns
    ):
        self.spot = spot
        self.half = half
        (
            self.late_ends,
            self.late_seconds,
            self.late_firsts,
            self.late_inbox,
            self.late_outbox,
            self.late_sums,
            self.late_inbox_sem,
            self.late_outbox_sem,
            self.late_sums_sem,
            self.late_end_receive,
            self.late_second_receive,
            self.late_first_receive,
        ) = late
        self.parts = parts
        self.cores = cores
        self.seconds, self.firsts, self.ends = places
        self.inbox = inbox
        self.outbox = outbox
        (
            self.inbox_sem,
            self.outbox_sem,
            self.second_receive,
            self.first_receive,
            self.end_receive,
        ) = semaphores
        self.plane = plane
        self.inside = inside
        self.ready = ready
        self.done = done
        self.turns = turns

    def second_slot(self, turn, first):
        return turn * 2 + first

    def first_slot(self, turn):
        return 2 * self.turns + turn

    def end_slot(self, turn, kind):
        return 3 * self.turns + turn * 2 + kind

    def free(self, unit, turn, first):
        pass

    def second_send(self, unit, turn, first):
        slot = self.second_slot(turn, first)
        return self.spot.send(
            self.outbox.at[slot],
            self.seconds.at[unit, first],
            self.outbox_sem.at[slot],
            self.second_receive.at[unit, first],
            SECOND,
        )

    def first_send(self, unit, turn):
        slot = self.first_slot(turn)
        return self.spot.send(
            self.outbox.at[slot],
            self.firsts.at[unit],
            self.outbox_sem.at[slot],
            self.first_receive.at[unit],
            FIRST,
        )

    def end_send(self, unit, turn, kind):
        slot = self.end_slot(turn, kind)
        return self.spot.send(
            self.outbox.at[slot],
            self.ends.at[unit, kind],
            self.outbox_sem.at[slot],
            self.end_receive.at[unit, kind],
            kind,
        )

    def received(self, place, semaphore):
        self.spot.send(place, place, self.outbox_sem.at[0], semaphore, CORE).wait_recv()

    def sources(self, unit, first, second):
        y, x = self.spot.side(self.spot.core, first, second)
        rows = pl.ds(pl.multiple_of(x * self.half, 16), self.inbox.shape[1])
        return [self.parts(unit, y).at[rows], self.cores(unit, y).at[rows]]

    def summands(self, unit):
        return self.sources(unit, 0, 0) + [self.seconds.at[unit, 0], self.firsts.at[unit]]

    def load(self, source, slot):
        return pltpu.make_async_copy(source, self.inbox.at[slot], self.inbox_sem.at[slot])

    def add(self, target, base, numbers):
        add_rows(target, [self.inbox.at[base + i] for i in numbers])

    def end_roles(self, half_step, delay):
        z, line = self.spot.z, self.spot.line
        unit = half_step - 3 - delay
        valid = self.inside(unit)
        plane = self.plane(unit)
        right = jnp.logical_and(valid, jnp.logical_and(z < plane, delay == z))
        left = jnp.logical_and(valid, jnp.logical_and(z > plane, delay == line - 1 - z))
        last = jnp.logical_and(
            valid,
            jnp.logical_and(z == plane, delay == jnp.maximum(plane, line - 1 - plane)),
        )
        return unit, right, left, last

    def end_task(self, half_step, delay, parity):
        z, line = self.spot.z, self.spot.line
        turn = (parity - 3 - delay) % self.turns
        unit, right, left, last = self.end_roles(half_step, delay)
        some = jnp.logical_or(right, jnp.logical_or(left, last))
        from_left = jnp.logical_and(jnp.logical_or(right, last), z > 0)
        from_right = jnp.logical_and(jnp.logical_or(left, last), z + 1 < line)
        present = ((RIGHT, from_left), (LEFT, from_right))

        def fetch(base):
            def action():
                self.received(self.seconds.at[unit, 0], self.second_receive.at[unit, 0])
                self.received(self.firsts.at[unit], self.first_receive.at[unit])
                for i, source in enumerate(self.summands(unit)):
                    self.load(source, base + i).start()
                for kind, there in present:

                    def arrive():
                        self.received(self.ends.at[unit, kind], self.end_receive.at[unit, kind])
                        self.load(self.ends.at[unit, kind], base + 4 + kind).start()

                    when(there, arrive)

            when(some, action)

        def add(base):
            def action():
                for i, source in enumerate(self.summands(unit)):
                    self.load(source, base + i).wait()
                for kind, there in present:
                    when(there, lambda: self.load(self.ends.at[unit, kind], base + 4 + kind).wait())
                numbers = list(range(4))
                for kind, chosen, behind in ((RIGHT, right, z > 0), (LEFT, left, z + 1 < line)):

                    def onward():
                        target = self.outbox.at[self.end_slot(turn, kind)]
                        self.free(unit, turn, 0)
                        when(behind, lambda: self.add(target, base, numbers + [4 + kind]))
                        when(jnp.logical_not(behind), lambda: self.add(target, base, numbers))
                        self.end_send(unit, turn, kind).start()

                    when(chosen, onward)

                def finish():
                    def into(target):
                        both = jnp.logical_and(from_left, from_right)
                        when(both, lambda: self.add(target, base, numbers + [4, 5]))
                        for kind, there in present:
                            when(
                                jnp.logical_and(there, jnp.logical_not(both)),
                                lambda: self.add(target, base, numbers + [4 + kind]),
                            )

                    self.done(unit, turn, 0, into)

                when(last, finish)

            when(some, action)

        return fetch, add

    def retire(self, half_step, parity):
        before = half_step - self.turns
        now, then = (parity - 1) % self.turns, (parity - 2) % self.turns
        when(
            self.inside(before - 1),
            lambda: [self.second_send(before - 1, now, first).wait_send() for first in range(2)],
        )
        when(self.inside(before - 2), lambda: self.first_send(before - 2, then).wait_send())
        for delay in range(self.spot.line):
            unit, right, left, _ = self.end_roles(before, delay)
            turn = (parity - 3 - delay) % self.turns
            when(right, lambda: self.end_send(unit, turn, RIGHT).wait_send())
            when(left, lambda: self.end_send(unit, turn, LEFT).wait_send())
            unit, right, left, _ = self.end_roles(before + 2, delay)
            turn = (parity - 1 - delay) % self.turns
            when(right, lambda: self.late_send(unit, turn, RIGHT).wait_send())
            when(left, lambda: self.late_send(unit, turn, LEFT).wait_send())

    def simple_task(self, valid, ready, inputs, slot, send, free=lambda: None):
        def fetch(base):
            ready()

            def action():
                for i, source in enumerate(inputs()):
                    self.load(source, base + i).start()

            when(valid, action)

        def add(base):
            def action():
                refs = inputs()
                for i, source in enumerate(refs):
                    self.load(source, base + i).wait()
                free()
                self.add(self.outbox.at[slot], base, range(len(refs)))
                send().start()

            when(valid, action)

        return fetch, add

    def tasks(self, half_step, parity):
        one, two = half_step - 1, half_step - 2
        now, then = (parity - 1) % self.turns, (parity - 2) % self.turns
        tasks = [
            self.second_task(one, now, 1, functools.partial(self.ready, one)),
            self.second_task(one, now, 0, lambda: None),
            self.first_task(two, then),
        ]
        line = self.spot.line
        tasks += [self.end_task(half_step, delay, parity) for delay in range(line)]
        others = [self.late_task(half_step, delay, parity) for delay in range(line)]
        others += [self.plane_task(half_step, stage) for stage in range(2)]
        woven = []
        for index, task in enumerate(tasks):
            woven += [task] + others[index : index + 1]
        return woven + others[len(tasks) :]

    def late_rows(self, index):
        return pl.ds(pl.multiple_of(index * self.late_inbox.shape[1] // 4, 16), self.late_inbox.shape[1] // 4)

    def late_send(self, unit, turn, kind):
        slot = turn * 2 + kind
        return self.spot.send(
            self.late_outbox.at[slot],
            self.late_ends.at[unit, kind],
            self.late_outbox_sem.at[slot],
            self.late_end_receive.at[unit, kind],
            kind,
        )

    def late_place(self, turn, first, second):
        y, x = self.spot.side(self.spot.core, first, second)
        return self.late_sums.at[turn, self.late_rows(y * 2 + x)]

    def late_second(self, unit, turn, first):
        return self.spot.send(
            self.late_place(turn, first, 1),
            self.late_seconds.at[unit, first],
            self.late_sums_sem.at[turn * 3 + first],
            self.late_second_receive.at[unit, first],
            SECOND,
        )

    def late_first(self, unit, turn):
        return self.spot.send(
            self.late_place(turn, 1, 0),
            self.late_firsts.at[unit],
            self.late_sums_sem.at[turn * 3 + 2],
            self.late_first_receive.at[unit],
            FIRST,
        )

    def late_load(self, source, target, index):
        return pltpu.make_async_copy(source, target, self.late_inbox_sem.at[index])

    def late_loads(self, unit):
        copies = []
        size = self.late_inbox.shape[1] // 4
        for y in range(2):
            for x in range(2):
                rows = pl.ds(x * self.half + self.half - size, size)
                for i, ref in enumerate((self.parts(unit, y), self.cores(unit, y))):
                    place = self.late_inbox.at[i, pl.ds((y * 2 + x) * size, size)]
                    copies.append(self.late_load(ref.at[rows], place, i * 4 + y * 2 + x))
        return copies

    def late_task(self, half_step, delay, parity):
        z, line = self.spot.z, self.spot.line
        turn = (parity - 1 - delay) % self.turns
        unit, right, left, last = self.end_roles(half_step + 2, delay)
        some = jnp.logical_or(right, jnp.logical_or(left, last))
        from_left = jnp.logical_and(jnp.logical_or(right, last), z > 0)
        from_right = jnp.logical_and(jnp.logical_or(left, last), z + 1 < line)
        present = ((RIGHT, from_left), (LEFT, from_right))
        both = jnp.logical_and(from_left, from_right)

        def behind(kind):
            return self.late_load(self.late_ends.at[unit, kind], self.late_inbox.at[2 + kind], 8 + kind)

        def fetch(base):
            def action():
                for copy in self.late_loads(unit):
                    copy.start()
                for kind, there in present:

                    def arrive():
                        self.received(self.late_ends.at[unit, kind], self.late_end_receive.at[unit, kind])
                        behind(kind).start()

                    when(there, arrive)

            when(some, action)

        def add(base):
            def total(target, kinds):
                add_rows(target, [self.late_inbox.at[i] for i in [0, 1] + [2 + kind for kind in kinds]])

            def action():
                for copy in self.late_loads(unit):
                    copy.wait()
                for kind, there in present:
                    when(there, lambda: behind(kind).wait())
                for kind, chosen, there in ((RIGHT, right, from_left), (LEFT, left, from_right)):

                    def onward():
                        target = self.late_outbox.at[turn * 2 + kind]
                        when(there, lambda: total(target, [kind]))
                        when(jnp.logical_not(there), lambda: total(target, []))
                        self.late_send(unit, turn, kind).start()

                    when(chosen, onward)

                def in_plane():
                    target = self.late_sums.at[turn]
                    when(both, lambda: total(target, [RIGHT, LEFT]))
                    for kind, there in present:
                        when(
                            jnp.logical_and(there, jnp.logical_not(both)),
                            lambda: total(target, [kind]),
                        )
                    for first in (1, 0):
                        self.late_second(unit, turn, first).start()

                when(last, in_plane)

            when(some, action)

        return fetch, add

    def plane_task(self, half_step, stage):
        z, line = self.spot.z, self.spot.line
        unit = half_step - 2 - stage - jnp.maximum(z, line - 1 - z)
        turn = lax.rem(jnp.maximum(unit, 0), self.turns)
        valid = jnp.logical_and(self.inside(unit), self.plane(unit) == z)
        size = self.late_inbox.shape[1] // 4
        place = lambda i: self.late_inbox.at[i, pl.ds(0, size)]
        second = self.late_load(self.late_seconds.at[unit, 1 - stage], place(0), 0)
        first = lambda: self.late_load(self.late_firsts.at[unit], place(1), 4)

        def fetch(base):
            def action():
                self.received(
                    self.late_seconds.at[unit, 1 - stage], self.late_second_receive.at[unit, 1 - stage]
                )
                second.start()
                if stage:
                    self.received(self.late_firsts.at[unit], self.late_first_receive.at[unit])
                    first().start()

            when(valid, action)

        def add(base):
            def action():
                second.wait()
                if stage:
                    first().wait()
                    sources = [self.late_place(turn, 0, 0), place(0), place(1)]
                    self.done(unit, lax.rem(unit, 2), 1, lambda target: add_rows(target, sources))
                    for i in range(2):
                        self.late_second(unit, turn, i).wait_send()
                    self.late_first(unit, turn).wait_send()
                else:
                    target = self.late_place(turn, 1, 0)
                    add_rows(target, [target, place(0)])
                    self.late_first(unit, turn).start()

            when(valid, action)

        return fetch, add

    def second_task(self, unit, turn, first, ready):
        return self.simple_task(
            self.inside(unit),
            ready,
            lambda: self.sources(unit, first, 1),
            self.second_slot(turn, first),
            lambda: self.second_send(unit, turn, first),
        )

    def first_task(self, unit, turn):
        arrive = lambda: self.received(self.seconds.at[unit, 1], self.second_receive.at[unit, 1])

        def send():
            return self.first_send(unit, turn)

        return self.simple_task(
            self.inside(unit),
            lambda: when(self.inside(unit), arrive),
            lambda: self.sources(unit, 1, 0) + [self.seconds.at[unit, 1]],
            self.first_slot(turn),
            send,
            lambda: self.free(unit, turn, 1),
        )

    def weave(self, tasks, pieces):
        buffers = self.inbox.shape[0] // BOXES
        if buffers > 1:
            tasks[0][0](0)
        for index, (fetch, add) in enumerate(tasks):
            if buffers == 1:
                fetch(0)
            elif index + 1 < len(tasks):
                tasks[index + 1][0]((index + 1) % 2 * BOXES)
            share = -(-len(pieces) // (len(tasks) - index))
            for piece in pieces[:share]:
                piece()
            pieces = pieces[share:]
            add(index % buffers * BOXES)

    def half_steps(self, units):
        return units + self.spot.line + 2


def norm_back(value, grads, gain):
    scale = lax.rsqrt(jnp.mean(value * value, axis=-1, keepdims=True) + EPSILON)
    unit = value * scale
    scaled = grads * gain
    back = scale * (scaled - unit * jnp.mean(scaled * unit, axis=-1, keepdims=True))
    return back, grads * unit


def backward_kernel(
    line,
    heads,
    kv_heads,
    cot_ref,
    totals_ref,
    hidden_ref,
    projected_ref,
    context_ref,
    in_ref,
    out_ref,
    tokens_ref,
    gain1_ref,
    gain2_ref,
    query_gain_ref,
    key_gain_ref,
    cosine_ref,
    sine_ref,
    block_out,
    input_grad,
    grads_all,
    out_total,
    gain_grads,
    elements,
    cots,
    tokens,
    kept,
    result,
    context,
    hidden_grads,
    context_grads,
    grads,
    normed_other,
    weight_rows,
    queries_f,
    shared_f,
    queries,
    query_grads,
    sums,
    out_grads,
    cores,
    firsts,
    rights,
    lefts,
    tree_send,
    tree_receive,
    load_sem,
    row_sem,
    head_sem,
    save_sem,
    hidden_send,
    hidden_receive,
    normed_send,
    normed_receive,
):
    batch, half, width = cot_ref.shape
    length = 2 * half
    features = query_gain_ref.shape[1]
    group = heads // kv_heads
    base = heads * features
    out_width = out_total.shape[1]
    narrow, spot = Spot(line, False), Spot(line, True)
    x = spot.x
    scale = features ** (-0.5)
    normed_grads = context_grads

    def load(source, target, index):
        return pltpu.make_async_copy(source, target, load_sem.at[index])

    def element_loads(i):
        return [
            load(hidden_ref.at[i], elements.at[0], 0),
            load(totals_ref.at[i, BACK], elements.at[1], 1),
            load(totals_ref.at[i, OUTPUT], elements.at[2], 2),
        ]

    first_loads = [load(cot_ref, cots, 3), load(tokens_ref, tokens, 4)] + [
        load(context_ref.at[i], rows_at(context, i, length), 5 + i) for i in range(batch)
    ]
    for copy in element_loads(0) + first_loads:
        copy.start()

    out_steps, in_steps = out_ref.shape[0] // CHUNK, in_ref.shape[0] // CHUNK
    stream = [(out_ref, step) for _ in range(batch) for step in range(out_steps)]
    stream += [(in_ref, step) for _ in range(batch) for step in range(in_steps)]

    def weight_load(index):
        ref, step = stream[index]
        return pltpu.make_async_copy(
            rows_at(ref, step, CHUNK),
            weight_rows.at[index % 2, :, pl.ds(0, ref.shape[1])],
            row_sem.at[index % 2],
        )

    def next_weights(index):
        if index + 2 < len(stream):
            weight_load(index + 2).start()

    for index in range(2):
        weight_load(index).start()
    gain_grads[...] = jnp.zeros_like(gain_grads)
    spot.greet()
    for copy in first_loads:
        copy.wait()

    def result_save(i, target):
        return pltpu.make_async_copy(result.at[i], target.at[i], save_sem.at[i])

    def half_copy(ref, i, side):
        return ref.at[pl.ds(pl.multiple_of(i * length + side * half, 16), half), pl.ds(0, width)]

    def hidden_copy(i):
        place = half_copy(hidden_grads, i, x)
        return spot.send(place, place, hidden_send.at[i], hidden_receive.at[i], CROSS)

    def element_rows(i):
        for copy in element_loads(i):
            copy.wait()

        def elementwise(step, _):
            rows = pl.ds(pl.multiple_of(step * 16, 16), 16)
            value = elements[0, rows, :]
            result[i, rows, :] = (value + elements[2, rows, :]).astype(jnp.bfloat16)
            back, gain_rows = norm_back(
                value, elements[1, rows, :], gain2_ref[...].astype(jnp.float32)
            )
            gain_grads[1:2, :] += jnp.sum(gain_rows, axis=0, keepdims=True)
            total = cots[i, rows, :].astype(jnp.float32) + back
            kept[i, rows, :] = total
            place = pl.ds(pl.multiple_of(i * length + x * half + step * 16, 16), 16)
            hidden_grads[place, :] = total.astype(jnp.bfloat16)
            return 0

        lax.fori_loop(0, half // 16, elementwise, 0)
        hidden_copy(i).start()
        result_save(i, block_out).start()
        if i + 1 < batch:
            for copy in element_loads(i + 1):
                copy.start()

    def hidden_done(i):
        hidden_copy(i).wait_send()
        place = half_copy(hidden_grads, i, 1 - x)
        spot.send(place, place, hidden_send.at[i], hidden_receive.at[i], CROSS).wait_recv()

    def context_step(i, step):
        index = i * out_steps + step
        weight_load(index).wait()
        rows = slice(i * length, (i + 1) * length)
        context_grads[rows, step * CHUNK : (step + 1) * CHUNK] = lax.dot_general(
            hidden_grads[rows],
            weight_rows[index % 2, :, :width],
            TRANSPOSED_RIGHT,
            preferred_element_type=jnp.float32,
        ).astype(jnp.bfloat16)
        next_weights(index)

    def out_step(step):
        columns = slice(step * CHUNK, (step + 1) * CHUNK)
        for start in range(0, width, CHUNK):
            out_grads[columns, start : start + CHUNK] = lax.dot_general(
                context[:, columns],
                hidden_grads[:, start : start + CHUNK],
                TRANSPOSED_LEFT,
                preferred_element_type=jnp.float32,
            ).astype(jnp.bfloat16)

    tree = Collect(
        narrow,
        lambda block, side: columns_at(out_grads, block, out_width),
        out_total,
        cores,
        firsts,
        rights,
        lefts,
        tree_send,
        tree_receive,
    )

    def tree_start():
        for z in range(line):
            tree.begin(z)

    def turns():
        return [(i, shared) for i in range(batch) for shared in range(kv_heads)]

    def head_loads(index):
        i, shared = turns()[index]
        slot = index % 2
        return [
            pltpu.make_async_copy(
                projected_ref.at[i, :, pl.ds(shared * group * features, group * features)],
                queries_f.at[slot],
                head_sem.at[slot, 0],
            )
        ] + [
            pltpu.make_async_copy(
                projected_ref.at[i, :, pl.ds(base + (shared + j * kv_heads) * features, features)],
                shared_f.at[slot, j],
                head_sem.at[slot, 1 + j],
            )
            for j in range(2)
        ]

    def turn_back(grads_in):
        return grads_in * cosine_ref[...] + pltpu.roll(
            grads_in * sine_ref[...], features // 2, 1
        )

    query_gain = lambda: query_gain_ref[...].astype(jnp.float32)
    key_gain = lambda: key_gain_ref[...].astype(jnp.float32)

    def attend_pieces(index):
        i, shared = turns()[index]
        slot = index % 2
        top = i * length

        def columns_of(member):
            return pl.ds(pl.multiple_of(member * features, LANES), features)

        def prepare():
            for copy in head_loads(index):
                copy.wait()
            if index + 1 < len(turns()):
                for copy in head_loads(index + 1):
                    copy.start()
            queries[group] = turned_heads(
                shared_f[slot, 0], key_gain(), cosine_ref[...], sine_ref[...]
            ).astype(jnp.bfloat16)
            queries[group + 1] = shared_f[slot, 1].astype(jnp.bfloat16)
            sums[...] = jnp.zeros_like(sums)

            def one(member):
                queries[member] = turned_heads(
                    queries_f[slot, :, columns_of(member)],
                    query_gain(),
                    cosine_ref[...],
                    sine_ref[...],
                ).astype(jnp.bfloat16)

            for_heads(0, group, 1, one)

        def rows_block(start, stop, seen, at_once, low, high):
            count = stop - start

            def block(member):
                query = queries[pl.ds(member, at_once), start:stop, :].reshape(-1, features)
                keys, values = queries[group, :seen, :], queries[group + 1, :seen, :]
                out_grad = jnp.concatenate(
                    [
                        context_grads[
                            top + start : top + stop,
                            head_columns(shared * group + member + j, features),
                        ]
                        for j in range(at_once)
                    ],
                    axis=0,
                )
                scores = lax.dot_general(
                    keys, query, TRANSPOSED_RIGHT, preferred_element_type=jnp.float32
                )
                shares = softmax(scores * scale)
                share_grads = lax.dot_general(
                    values, out_grad, TRANSPOSED_RIGHT, preferred_element_type=jnp.float32
                )
                sums[1, :seen, :] += jnp.dot(
                    shares.astype(jnp.bfloat16), out_grad, preferred_element_type=jnp.float32
                )
                inner = jnp.sum(shares * share_grads, axis=0, keepdims=True)
                score_grads = (shares * (share_grads - inner)).astype(jnp.bfloat16)
                rows = scale * lax.dot_general(
                    score_grads, keys, TRANSPOSED_LEFT, preferred_element_type=jnp.float32
                )
                query_grads[pl.ds(member, at_once), start:stop, :] = rows.reshape(
                    at_once, count, features
                )
                sums[0, :seen, :] += jnp.dot(
                    score_grads, query, preferred_element_type=jnp.float32
                )

            for_heads(low, high, at_once, block)

        def finish_queries():
            def finish(member):
                back, gain_rows = norm_back(
                    queries_f[slot, :, columns_of(member)],
                    turn_back(query_grads[member]),
                    query_gain(),
                )
                gain_grads[2:3, :features] += jnp.sum(gain_rows, axis=0, keepdims=True)
                grads[top : top + length, head_columns(shared * group + member, features)] = (
                    back.astype(jnp.bfloat16)
                )

            for_heads(0, group, 1, finish)

        def finish_keys():
            back, gain_rows = norm_back(shared_f[slot, 0], turn_back(sums[0] * scale), key_gain())
            gain_grads[3:4, :features] += jnp.sum(gain_rows, axis=0, keepdims=True)
            at = base + shared * features
            grads[top : top + length, at : at + features] = back.astype(jnp.bfloat16)
            at += kv_heads * features
            grads[top : top + length, at : at + features] = sums[1].astype(jnp.bfloat16)

        pieces = [prepare]
        for start, stop, seen, at_once in visible_blocks(length, group):
            share = max(at_once, group // 2)
            for low in range(0, group, share):
                pieces.append(
                    functools.partial(rows_block, start, stop, seen, at_once, low, low + share)
                )
        return pieces + [finish_queries, finish_keys]

    saves = [
        pltpu.make_async_copy(rows_at(grads, i, length), grads_all.at[i], save_sem.at[batch + i])
        for i in range(batch)
    ]

    def normed_step(i, step):
        index = batch * out_steps + i * in_steps + step
        weight_load(index).wait()
        rows = slice(i * length, (i + 1) * length)
        normed_grads[rows, step * CHUNK : (step + 1) * CHUNK] = lax.dot_general(
            grads[rows],
            weight_rows[index % 2],
            TRANSPOSED_RIGHT,
            preferred_element_type=jnp.float32,
        ).astype(jnp.bfloat16)
        next_weights(index)

    def normed_copy(i):
        return spot.send(
            half_copy(normed_grads, i, 1 - x),
            normed_other.at[i],
            normed_send.at[i],
            normed_receive.at[i],
            CROSS,
        )

    def input_rows(i):
        normed_copy(i).wait()
        result_save(i, block_out).wait()

        def body(step, _):
            rows = pl.ds(pl.multiple_of(step * 16, 16), 16)
            place = pl.ds(pl.multiple_of(i * length + x * half + step * 16, 16), 16)
            total = normed_grads[place, :width].astype(jnp.float32) + normed_other[
                i, rows, :
            ].astype(jnp.float32)
            back, gain_rows = norm_back(
                tokens[i, rows, :].astype(jnp.float32), total, gain1_ref[...].astype(jnp.float32)
            )
            gain_grads[0:1, :] += jnp.sum(gain_rows, axis=0, keepdims=True)
            kept[i, rows, :] = kept[i, rows, :] + back
            return 0

        lax.fori_loop(0, half // 16, body, 0)
        add_rows(result.at[i], [kept.at[i]])
        result_save(i, input_grad).start()

    for copy in head_loads(0):
        copy.start()
    attending = [attend_pieces(index) for index in range(len(turns()))]
    contexts = [
        [functools.partial(context_step, i, step) for step in range(out_steps)]
        for i in range(batch)
    ]
    opening = [functools.partial(element_rows, i) for i in range(batch)]
    opening += attending[0][:1] + [functools.partial(hidden_done, 0)] + contexts[0]
    opening += [functools.partial(hidden_done, i) for i in range(1, batch)]
    opening += [functools.partial(out_step, step) for step in range(out_steps)] + [tree_start]
    for steps in contexts[1:]:
        opening += steps
    opening.append(tree.cross)
    closing = []
    for index in range(len(turns())):
        i = turns()[index][0]
        closing += attending[index][0 if index else 1 :]
        if index + 1 == len(turns()) or turns()[index + 1][0] > i:
            closing += [saves[i].start]
            closing += [functools.partial(normed_step, i, step) for step in range(in_steps)]
            closing += [lambda i=i: normed_copy(i).start()]
    closing += [functools.partial(input_rows, i) for i in range(batch)]
    for piece in opening:
        piece()
    mingle(closing, tree.tasks())
    for i in range(batch):
        result_save(i, input_grad).wait()
    for copy in saves:
        copy.wait()


def run_backward(
    cot,
    totals,
    hidden,
    projected,
    context,
    in_full,
    out_full,
    tokens,
    gains,
    tables,
    fsdp_count,
    kv_heads,
):
    line = fsdp_count // PLANE
    batch, half, width = tokens.shape
    length = 2 * half
    features = gains[2].shape[1]
    heads = out_full.shape[0] // features
    group = heads // kv_heads
    in_width, out_depth = in_full.shape[1], out_full.shape[0]
    out_shape = (out_depth, width // fsdp_count)
    anywhere = pl.BlockSpec(memory_space=pl.ANY)
    inside = pl.BlockSpec(memory_space=pltpu.VMEM)
    shape = lambda *dims: jax.ShapeDtypeStruct(dims, jnp.bfloat16)
    vmem = lambda *dims: pltpu.VMEM(dims, jnp.bfloat16)
    wide = lambda *dims: pltpu.VMEM(dims, jnp.float32)
    sem = lambda *dims: pltpu.SemaphoreType.DMA(dims)
    rows = batch * length
    return pl.pallas_call(
        functools.partial(backward_kernel, line, heads, kv_heads),
        out_shape=(
            shape(batch, half, width),
            shape(batch, half, width),
            shape(batch, length, in_width),
            jax.ShapeDtypeStruct(out_shape, jnp.float32),
            jax.ShapeDtypeStruct((8, width), jnp.float32),
        ),
        in_specs=[anywhere] * 8 + [inside] * 6,
        out_specs=(anywhere, anywhere, anywhere, inside, inside),
        scratch_shapes=[
            wide(3, half, width),
            vmem(batch, half, width),
            vmem(batch, half, width),
            wide(batch, half, width),
            vmem(batch, half, width),
            vmem(rows, out_depth),
            vmem(rows, width),
            vmem(rows, max(out_depth, width)),
            vmem(rows, in_width),
            vmem(batch, half, width),
            vmem(2, CHUNK, max(width, in_width)),
            wide(2, length, group * features),
            wide(2, 2, length, features),
            vmem(group + 2, length, features),
            wide(group, length, features),
            wide(2, length, features),
            vmem(out_depth, width),
            *collect_scratch(line, out_shape),
            sem(5 + batch),
            sem(2),
            sem(2, 3),
            sem(2 * batch),
            sem(batch),
            sem(batch),
            sem(batch),
            sem(batch),
        ],
        compiler_params=pltpu.CompilerParams(
            collective_id=3, has_side_effects=True, vmem_limit_bytes=62 * MIB
        ),
    )(
        cot,
        totals,
        hidden,
        projected,
        context,
        in_full,
        out_full,
        tokens,
        *gains,
        *tables,
    )


def gradients_kernel(
    line,
    normed,
    grads,
    gains_ref,
    xe_ref,
    ce_ref,
    act_ref,
    dgate_ref,
    dup_ref,
    in_total,
    gains_all,
    gate_total,
    up_total,
    down_total,
    parts,
    cores,
    firsts,
    rights,
    lefts,
    tree_send,
    tree_receive,
    gain_send,
    gain_receive,
    gain_local,
    wide_rows,
    slim_rows,
    gate_sum,
    up_sum,
    down_sum,
    load_sem,
    save_sem,
):
    narrow, spot = Spot(line, False), Spot(line, True)
    experts, count, _ = xe_ref.shape
    share = wide_rows.shape[1]
    turns = count // share
    pieces = [
        (expert, kind, turn)
        for expert in range(experts)
        for kind in range(2)
        for turn in range(turns)
    ]

    def loads(index):
        expert, kind, turn = pieces[index]
        slot = index % 2
        rows = pl.ds(turn * share, share)
        slim = (dgate_ref, dup_ref) if kind == 0 else (act_ref,)
        return [
            pltpu.make_async_copy(
                (xe_ref, ce_ref)[kind].at[expert, rows], wide_rows.at[slot], load_sem.at[slot, 0]
            )
        ] + [
            pltpu.make_async_copy(
                ref.at[expert, rows], slim_rows.at[slot, i], load_sem.at[slot, 1 + i]
            )
            for i, ref in enumerate(slim)
        ]

    def saves(expert, kind):
        pairs = ((gate_sum, gate_total), (up_sum, up_total))
        if kind:
            return [pltpu.make_async_copy(down_sum, down_total.at[expert], save_sem.at[2])]
        return [
            pltpu.make_async_copy(source, target.at[expert], save_sem.at[i])
            for i, (source, target) in enumerate(pairs)
        ]

    for copy in loads(0):
        copy.start()
    spot.greet()
    gains = Spread(
        spot,
        gains_ref,
        lambda block, half: gains_all.at[block, half],
        gain_send,
        gain_receive,
        gain_local.at[0],
    )
    gains.begin()
    depth, width = in_total.shape
    tree = Collect(
        narrow,
        lambda block, half: rows_at(parts, block, depth),
        in_total,
        cores,
        firsts,
        rights,
        lefts,
        tree_send,
        tree_receive,
    )
    chunk = PLANE * depth

    def far_first(step):
        z = narrow.z
        down = jnp.where(line - 1 - step > z, line - 1 - step, line - 2 - step)
        up = jnp.where(step < z, step, step + 1)
        return jnp.where(step == line - 1, z, jnp.where(2 * z < line, down, up))

    def plane(step, _):
        z = far_first(step)
        columns = pl.ds(pl.multiple_of(z * chunk, LANES), chunk)
        for start in range(0, width, CHUNK):
            parts[pl.ds(pl.multiple_of(z * chunk, 16), chunk), start : start + CHUNK] = (
                lax.dot_general(
                    normed[:, columns],
                    grads[:, start : start + CHUNK],
                    TRANSPOSED_LEFT,
                    preferred_element_type=jnp.float32,
                ).astype(jnp.bfloat16)
            )
        tree.begin(z)
        when(step > 0, lambda: tree.to_first(far_first(step - 1)))
        return 0

    lax.fori_loop(0, line, plane, 0)
    tree.to_first(narrow.z)

    def piece(index):
        expert, kind, turn = pieces[index]
        slot = index % 2
        for copy in loads(index):
            copy.wait()
        if index + 1 < len(pieces):
            for copy in loads(index + 1):
                copy.start()
        if turn == 0 and expert:
            for copy in saves(expert - 1, kind):
                copy.wait()
        size = wide_rows.shape[2] // 4

        def add(target, place, left, right):
            product = lax.dot_general(
                left, right, TRANSPOSED_LEFT, preferred_element_type=jnp.float32
            )
            if turn:
                product = target[place] + product
            target[place] = product

        def part(step, _):
            at = pl.ds(pl.multiple_of(step * size, LANES), size)
            if kind:
                add(down_sum, (slice(None), at), slim_rows[slot, 0], wide_rows[slot, :, at])
            else:
                for i, target in enumerate((gate_sum, up_sum)):
                    add(target, (at, slice(None)), wide_rows[slot, :, at], slim_rows[slot, i])
            return 0

        lax.fori_loop(0, 4, part, 0)
        if turn == turns - 1:
            for copy in saves(expert, kind):
                copy.start()

    work = tree.tasks()
    steps = list(range(1, gains.steps()))
    filler = list(range(len(pieces)))
    while work or filler:
        for _ in range(2 if len(filler) > len(work) else 1):
            if filler:
                piece(filler.pop(0))
        if work:
            work.pop(0)()
        if steps:
            gains.step(steps.pop(0))
    gains.finish()
    for copy in saves(experts - 1, 0) + saves(experts - 1, 1):
        copy.wait()


def run_gradients(normed, grads, gains, expert_rows, fsdp_count):
    line = fsdp_count // PLANE
    width = grads.shape[1]
    experts, count, depth = expert_rows[0].shape
    units = expert_rows[2].shape[2]
    share = 2 * CHUNK if count % (2 * CHUNK) == 0 else count // (2 * line)
    shape = (normed.shape[1] // fsdp_count, width)
    sends, receives = spread_count(line, True)
    inside = pl.BlockSpec(memory_space=pltpu.VMEM)
    anywhere = pl.BlockSpec(memory_space=pl.ANY)
    return pl.pallas_call(
        functools.partial(gradients_kernel, line),
        out_shape=(
            jax.ShapeDtypeStruct(shape, jnp.float32),
            jax.ShapeDtypeStruct((fsdp_count, 2, *gains.shape), jnp.float32),
            jax.ShapeDtypeStruct((experts, depth, units), jnp.float32),
            jax.ShapeDtypeStruct((experts, depth, units), jnp.float32),
            jax.ShapeDtypeStruct((experts, units, depth), jnp.float32),
        ),
        in_specs=[inside, inside] + [anywhere] * 6,
        out_specs=(inside,) + (anywhere,) * 4,
        scratch_shapes=[
            pltpu.VMEM((normed.shape[1], width), jnp.bfloat16),
            *collect_scratch(line, shape),
            pltpu.SemaphoreType.DMA((sends,)),
            pltpu.SemaphoreType.DMA((receives,)),
            pltpu.SemaphoreType.DMA((1,)),
            pltpu.VMEM((2, share, depth), jnp.bfloat16),
            pltpu.VMEM((2, 2, share, units), jnp.bfloat16),
            pltpu.VMEM((depth, units), jnp.float32),
            pltpu.VMEM((depth, units), jnp.float32),
            pltpu.VMEM((units, depth), jnp.float32),
            pltpu.SemaphoreType.DMA((2, 3)),
            pltpu.SemaphoreType.DMA((3,)),
        ],
        compiler_params=pltpu.CompilerParams(
            collective_id=4, has_side_effects=True, vmem_limit_bytes=60 * MIB
        ),
    )(normed, grads, gains, *expert_rows)


def experts_kernel(
    line,
    slots,
    own_ref,
    cot_first,
    cot_ref,
    info_ref,
    gate_ref,
    up_ref,
    down_ref,
    all_ref,
    cot_later,
    total_ref,
    xe_all,
    ce_all,
    act_all,
    dgate_all,
    dup_all,
    part,
    cores,
    seconds,
    firsts,
    ends,
    late_ends,
    late_seconds,
    late_firsts,
    hidden_w,
    down_w,
    x_rows,
    c_rows,
    xe,
    ce,
    acts,
    dgates,
    dups,
    hidden_grads,
    picks,
    weigh,
    rows,
    stage,
    inbox,
    outbox,
    summed,
    rows_send,
    rows_receive,
    rows_late_send,
    rows_late_receive,
    rows_local,
    cot_send,
    cot_receive,
    cot_late_send,
    cot_late_receive,
    cot_local,
    load_sem,
    save_sem,
    stage_sem,
    inbox_sem,
    outbox_sem,
    total_sem,
    weight_sem,
    core_receive,
    second_receive,
    first_receive,
    end_receive,
    *late_scratch,
):
    late_refs = (late_ends, late_seconds, late_firsts, *late_scratch)
    spot = Spot(line, True)
    z, core = spot.z, spot.core
    cot_semaphores = (cot_send, cot_receive, cot_late_send, cot_late_receive, cot_local)
    tree_semaphores = (rows_send, rows_receive, rows_late_send, rows_late_receive, rows_local)
    batch, half, width = own_ref.shape
    length = 2 * half
    units = down_ref.shape[1]
    groups = batch * line
    weights = [
        pltpu.make_async_copy(source, target, weight_sem.at[i])
        for i, (source, target) in enumerate(
            [(down_ref, down_w)]
            + [(gate_ref.at[e], hidden_w.at[e, :, pl.ds(0, units)]) for e in range(2)]
            + [(up_ref.at[e], hidden_w.at[e, :, pl.ds(units, units)]) for e in range(2)]
        )
    ]
    for copy in weights:
        copy.start()
    rows[...] = jnp.zeros_like(rows)
    spot.greet()

    def half_of(ref, index):
        return rows_at(ref, index, half)

    trees = []
    for i in range(batch):
        place = lambda block, start, size, i=i: all_ref.at[
            i, block, pl.ds(pl.multiple_of(start, 16), size)
        ]
        trees.append(rows_spread(spot, own_ref.at[i], place, half, tree_semaphores, i))
    for i in range(1, batch):
        place = lambda block, start, size, i=i: cot_later.at[
            i - 1, block, pl.ds(pl.multiple_of(start, 16), size)
        ]
        trees[i] += rows_spread(spot, cot_ref.at[i], place, half, cot_semaphores, i - 1)
    run_trees(trees[0])
    for tree in sum(trees[1:], []):
        tree.begin()
    for copy in weights:
        copy.wait()

    plane_of = functools.partial(plane_in_turn, line)

    def load_group(group, member, start):
        at = lax.div(group, line)
        sequence = plane_of(group) * PLANE + member
        slot = member % 2
        def copy(i, source, target):
            return pltpu.make_async_copy(source, target.at[slot], load_sem.at[i, slot])

        own = copy(0, all_ref.at[at, sequence], x_rows)
        if start:
            own.start()
            later = cot_later.at[jnp.maximum(at - 1, 0), sequence]
            when(at == 0, lambda: copy(1, cot_first.at[sequence], c_rows).start())
            when(at > 0, lambda: copy(1, later, c_rows).start())
        else:
            own.wait()
            copy(1, cot_first.at[sequence], c_rows).wait()

    def saves(group):
        to = lambda ref, expert: rows_at(ref.at[expert], group, PLANE * slots)
        pairs = ((xe, xe_all), (ce, ce_all), (acts, act_all), (dgates, dgate_all), (dups, dup_all))
        return [
            pltpu.make_async_copy(source.at[expert], to(target, expert), save_sem.at[2 * i + expert])
            for i, (source, target) in enumerate(pairs)
            for expert in range(2)
        ]

    def staged(unit, y, mine):
        slot = y * 2 + mine
        if mine:
            return pltpu.make_async_copy(stage.at[slot], part.at[unit, y], stage_sem.at[slot])
        return spot.send(
            stage.at[slot], cores.at[unit, y], stage_sem.at[slot], core_receive.at[unit, y], CORE
        )

    def combine(unit, y):
        for mine in range(2):
            member = y * 2 + (core if mine else 1 - core)
            for start in range(0, width, CHUNK):
                stage[y * 2 + mine, :, start : start + CHUNK] = lax.dot_general(
                    picks[member],
                    rows[member, :, start : start + CHUNK],
                    TRANSPOSED_LEFT,
                    preferred_element_type=jnp.float32,
                ).astype(jnp.bfloat16)
            staged(unit, y, mine).start()

    def pick(group, member):
        slot = member % 2
        load_group(group, member, False)
        if member + 1 < PLANE:
            load_group(group, member + 1, True)
        sequence = plane_of(group) * PLANE + member
        info = info_ref[lax.div(group, line) * line * PLANE + sequence]
        places = lax.broadcasted_iota(jnp.int32, (2 * LANES, length), 0)
        lower = places < LANES
        ranks = jnp.where(lower, info[0:1], info[1:2] + float(LANES)).astype(jnp.int32)
        some = jnp.where(lower, info[0:1], info[1:2]) >= 0.0
        hot = jnp.logical_and(ranks == places, some)
        chosen = hot.astype(jnp.float32).astype(jnp.bfloat16)
        picks[member] = chosen
        shares = jnp.where(hot, jnp.where(lower, info[2:3], info[3:4]), 0.0)
        column = jnp.sum(shares, axis=1, keepdims=True)
        here = pl.ds(member * slots, slots)
        for expert in range(2):
            weigh[expert, here, :] = jnp.broadcast_to(
                column[expert * LANES : expert * LANES + slots], (slots, LANES)
            )
        for source, target in ((x_rows, xe), (c_rows, ce)):
            for start in range(0, width, CHUNK):
                selected = jnp.dot(
                    chosen,
                    source[slot, :, start : start + CHUNK],
                    preferred_element_type=jnp.float32,
                ).astype(jnp.bfloat16)
                for expert in range(2):
                    target[expert, here, start : start + CHUNK] = selected[
                        expert * LANES : expert * LANES + slots
                    ]

    def keep(expert, product, start):
        at = pl.ds(expert * LANES, slots)
        for one in range(PLANE):
            rows[one, at, start : start + CHUNK] = product[one * slots : (one + 1) * slots].astype(
                jnp.bfloat16
            )

    def forward(expert):
        hidden = jnp.dot(xe[expert], hidden_w[expert], preferred_element_type=jnp.float32)
        gate, up = hidden[:, :units], hidden[:, units:]
        sigmoid = jax.nn.sigmoid(gate)
        silu = gate * sigmoid
        scale = weigh[expert, :, 0:1]
        acts[expert] = (silu * up * scale).astype(jnp.bfloat16)
        act_grads = scale * lax.dot_general(
            ce[expert], down_w[expert], TRANSPOSED_RIGHT, preferred_element_type=jnp.float32
        )
        gate_grads = (act_grads * up * (sigmoid * (1.0 + gate * (1.0 - sigmoid)))).astype(
            jnp.bfloat16
        )
        up_grads = (act_grads * silu).astype(jnp.bfloat16)
        dgates[expert] = gate_grads
        dups[expert] = up_grads
        hidden_grads[expert, :, :units] = gate_grads
        hidden_grads[expert, :, units:] = up_grads
        for start in range(0, width, CHUNK):
            keep(
                expert,
                jnp.dot(
                    acts[expert],
                    down_w[expert, :, start : start + CHUNK],
                    preferred_element_type=jnp.float32,
                ),
                start,
            )

    def backward(expert):
        for start in range(0, width, CHUNK):
            keep(
                expert,
                lax.dot_general(
                    hidden_grads[expert],
                    hidden_w[expert, start : start + CHUNK, :],
                    TRANSPOSED_RIGHT,
                    preferred_element_type=jnp.float32,
                ),
                start,
            )

    units_all = 2 * groups

    def inside(unit):
        return jnp.logical_and(unit >= 0, unit < units_all)

    def ready(unit):
        @pl.when(inside(unit))
        def _():
            for y in range(2):
                staged(unit, y, 1).wait()
                staged(unit, y, 0).wait_send()
                place, semaphore = cores.at[unit, y], core_receive.at[unit, y]
                spot.send(place, place, outbox_sem.at[0], semaphore, CORE).wait_recv()

    late = late_rows(half)

    def done(unit, tensor, part_of, into):
        rows = (pl.ds(0, half - late), pl.ds(half - late, late))[part_of]
        place = summed.at[rows]
        into(place)
        copy = pltpu.make_async_copy(
            place, total_ref.at[lax.div(unit, 2 * line), tensor, rows], total_sem.at[0]
        )
        copy.start()
        copy.wait()

    sums = Sums(
        spot,
        half,
        lambda unit, y: part.at[unit, y],
        lambda unit, y: cores.at[unit, y],
        (seconds, firsts, ends),
        inbox,
        outbox,
        (inbox_sem, outbox_sem, second_receive, first_receive, end_receive),
        late_refs,
        lambda unit: plane_of(lax.div(jnp.maximum(unit, 0), 2)),
        inside,
        ready,
        done,
        2,
    )

    def tree_turn(half_step, last):
        for i in range(1, batch):
            turn = half_step - (i - 1) * 2 * line
            if last:
                when(turn == 2 * line - 1, lambda: [tree.finish() for tree in trees[i]])
            else:
                inner = jnp.logical_and(turn >= 0, turn < 2 * line - 1)
                when(inner, lambda: [tree.step(turn + 1) for tree in trees[i]])

    def begin_pick(group):
        load_group(group, 0, True)

    begin_pick(0)
    for member in range(PLANE):
        pick(0, member)

    def step_body(step, _):
        busy = step < groups
        more = step + 1 < groups
        for parity in range(2):
            half_step = step * 2 + parity
            tree_turn(half_step, False)
            sums.retire(half_step, parity)
            tasks = sums.tasks(half_step, parity)
            pieces = []
            for expert in range(2):
                pieces.append(functools.partial((forward, backward)[parity], expert))
            if parity == 0:
                pieces.append(lambda: [copy.start() for copy in saves(step)])
            for y in range(2):
                pieces.append(functools.partial(combine, half_step, y))
            pieces = [functools.partial(when, busy, piece) for piece in pieces]
            if parity == 1:

                def prepare():
                    for copy in saves(step):
                        copy.wait()
                    begin_pick(step + 1)

                tree_end = functools.partial(tree_turn, half_step, True)
                pieces += [tree_end, functools.partial(when, more, prepare)]
                for member in range(PLANE):
                    pieces.append(
                        functools.partial(when, more, functools.partial(pick, step + 1, member))
                    )
            sums.weave(tasks, pieces)
        return 0

    half_steps = sums.half_steps(units_all)
    lax.fori_loop(0, -(-half_steps // 2), step_body, 0)
    end = -(-half_steps // 2) * 2
    for parity in range(2):
        sums.retire(jnp.int32(end + parity), parity)
    for copy in saves(groups - 1):
        copy.wait()


def run_experts(rows, cot_first, cot, info, w_gate, w_up, w_down, capacity, fsdp_count):
    line = fsdp_count // PLANE
    batch, half, width = rows.shape
    length = 2 * half
    units = w_down.shape[1]
    slots = -(-capacity // 16) * 16
    groups = batch * line
    count = groups * PLANE * slots
    taken = PLANE * slots
    shape = lambda *dims: jax.ShapeDtypeStruct(dims, jnp.bfloat16)
    block = (half, width)
    late = late_rows(half)
    early = half - late
    anywhere = pl.BlockSpec(memory_space=pl.ANY)
    vmem = lambda *dims: pltpu.VMEM(dims, jnp.bfloat16)
    sem = lambda *dims: pltpu.SemaphoreType.DMA(dims)
    return pl.pallas_call(
        functools.partial(experts_kernel, line, slots),
        out_shape=(
            shape(batch, fsdp_count, length, width),
            shape(max(batch - 1, 1), fsdp_count, length, width),
            jax.ShapeDtypeStruct((batch, 2, *block), jnp.float32),
            shape(2, count, width),
            shape(2, count, width),
            shape(2, count, units),
            shape(2, count, units),
            shape(2, count, units),
            shape(2 * groups, 2, length, width),
            shape(2 * groups, 2, length, width),
            shape(2 * groups, 2, early, width),
            shape(2 * groups, early, width),
            shape(2 * groups, 2, early, width),
            shape(2 * groups, 2, 4 * late, width),
            shape(2 * groups, 2, late, width),
            shape(2 * groups, late, width),
        ),
        in_specs=[
            anywhere,
            anywhere,
            anywhere,
            pl.BlockSpec(memory_space=pltpu.VMEM),
            anywhere,
            anywhere,
            anywhere,
        ],
        out_specs=(anywhere,) * 16,
        scratch_shapes=[
            vmem(2, width, 2 * units),
            vmem(2, units, width),
            vmem(2, length, width),
            vmem(2, length, width),
            vmem(2, taken, width),
            vmem(2, taken, width),
            vmem(2, taken, units),
            vmem(2, taken, units),
            vmem(2, taken, units),
            vmem(2, taken, 2 * units),
            vmem(PLANE, 2 * LANES, length),
            pltpu.VMEM((2, taken, LANES), jnp.float32),
            vmem(PLANE, 2 * LANES, width),
            vmem(PLANE, length, width),
            vmem(12, early, width),
            vmem(10, early, width),
            pltpu.VMEM(block, jnp.float32),
            *rows_semaphores(batch, line),
            *rows_semaphores(max(batch - 1, 1), line),
            sem(2, 2),
            sem(10),
            sem(PLANE),
            sem(12),
            sem(10),
            sem(1),
            sem(5),
            sem(2 * groups, 2),
            sem(2 * groups, 2),
            sem(2 * groups),
            sem(2 * groups, 2),
            vmem(4, 4 * late, width),
            vmem(4, 4 * late, width),
            vmem(2, 4 * late, width),
            sem(10),
            sem(4),
            sem(6),
            sem(2 * groups, 2),
            sem(2 * groups, 2),
            sem(2 * groups),
        ],
        compiler_params=pltpu.CompilerParams(
            collective_id=2, has_side_effects=True, vmem_limit_bytes=60 * MIB
        ),
    )(rows, cot_first, cot, info, w_gate, w_up, w_down)[2:8]


def packed_picks(routes, gates):
    length = routes.shape[2]
    packed = jnp.concatenate([routes[:, 0].astype(jnp.float32), gates[:, 0]], axis=-1)
    packed = jnp.swapaxes(packed, 1, 2).reshape(-1, length)
    return jnp.pad(packed, ((0, 0), (0, -length % LANES)))


def slot_info(packed, batch, top, length, local_experts):
    fsdp_count = packed.shape[0]
    packed = packed[..., :length].reshape(fsdp_count, batch, 1, 2 * top, length)
    packed = jnp.swapaxes(packed, 0, 1)
    experts = lax.axis_index(FSDP) * local_experts + jnp.arange(local_experts, dtype=jnp.int32)
    same = packed[..., :top, :].astype(jnp.int32) == experts[:, None, None]
    hot = jnp.any(same, axis=3)
    shares = jnp.sum(jnp.where(same, packed[..., top:, :], 0.0), axis=3)
    position = jnp.arange(length)
    upper = (position[:, None] < position[None, :]).astype(jnp.bfloat16)
    rank = jnp.dot(
        hot.astype(jnp.bfloat16).reshape(-1, length), upper, preferred_element_type=jnp.float32
    )
    rank = jnp.where(hot, rank.reshape(hot.shape), -1.0)
    return jnp.concatenate([rank, shares], axis=2).reshape(-1, 2 * local_experts, length)


def gathered_layer(
    tokens,
    cotangent,
    norm1_gain,
    w_query,
    key_projection_weight,
    value_projection_weight,
    query_gain,
    key_gain,
    w_out,
    norm2_gain,
    w_gate,
    w_up,
    w_down,
    routes,
    gates,
):
    batch_count = tokens.shape[0]
    model_width = tokens.shape[3]
    sequence_length = routes.shape[2]
    half_length = tokens.shape[2]
    top_count = routes.shape[3]
    head_features = query_gain.shape[0]
    local_experts = w_gate.shape[0]
    fsdp_count = lax.axis_size(FSDP)
    all_experts = local_experts * fsdp_count
    capacity = 7 * top_count * sequence_length // (6 * all_experts)
    query_width = w_query.shape[1]
    kv_width = key_projection_weight.shape[1]
    kv_heads = kv_width // head_features
    cosine_table, sine_values = rotary_tables(sequence_length, head_features)
    weight_in = jnp.concatenate([w_query, key_projection_weight, value_projection_weight], axis=1)
    half_signs = jnp.where(jnp.arange(head_features) < head_features // 2, -1.0, 1.0)
    tables = (cosine_table[:, 0], sine_values[:, 0] * half_signs)
    gains = [gain[None, :] for gain in (norm1_gain, norm2_gain, query_gain, key_gain)]
    cot_first, in_full, out_full, picks, normed, projected, contexts, hidden, second = run_forward(
        tokens[:, 0],
        cotangent[:, 0],
        weight_in,
        w_out,
        packed_picks(routes, gates),
        gains,
        tables,
        fsdp_count,
        kv_heads,
    )
    info = slot_info(picks, batch_count, top_count, sequence_length, local_experts)
    totals, *expert_rows = run_experts(
        second, cot_first, cotangent[:, 0], info, w_gate, w_up, w_down, capacity, fsdp_count
    )
    block_out, input_grad, projected_grads, out_sum, gain_grads = run_backward(
        cotangent[:, 0],
        totals,
        hidden,
        projected,
        contexts,
        in_full,
        out_full,
        tokens[:, 0],
        gains,
        tables,
        fsdp_count,
        kv_heads,
    )
    rows = batch_count * sequence_length
    in_sum, gains_all, *expert_grads = run_gradients(
        normed.reshape(rows, -1),
        projected_grads.reshape(rows, -1),
        gain_grads,
        expert_rows,
        fsdp_count,
    )
    gains_sum = jnp.sum(gains_all, axis=(0, 1))
    return (
        block_out[:, None],
        input_grad[:, None],
        gains_sum[0],
        in_sum[:, :query_width],
        in_sum[:, query_width : query_width + kv_width],
        in_sum[:, query_width + kv_width :],
        gains_sum[2, :head_features],
        gains_sum[3, :head_features],
        out_sum,
        gains_sum[1],
        *expert_grads,
    )


def shards(*arrays):
    tokens, routes, w_gate = arrays[0], arrays[13], arrays[10]
    fsdp_count = lax.axis_size(FSDP)
    gathered = fsdp_count * routes.shape[2] * tokens.shape[3] * 2
    fits = gathered <= 24 * MIB and fsdp_count % PLANE == 0 and lax.axis_size(TP) == 2
    if fits and w_gate.shape[0] == 2:
        return gathered_layer(*arrays)
    return exchanged_layer(*arrays)


def solution(mesh):
    in_specs = (
        P(None, "fsdp", "tp", None),
        P(None, "fsdp", "tp", None),
        P(),
        P("fsdp", "tp"),
        P("fsdp", "tp"),
        P("fsdp", "tp"),
        P(),
        P(),
        P("tp", "fsdp"),
        P(),
        P("fsdp", None, "tp"),
        P("fsdp", None, "tp"),
        P("fsdp", "tp", None),
        P(None, "fsdp", None, None),
        P(None, "fsdp", None, None),
    )
    out_specs = (
        P(None, "fsdp", "tp", None),
        P(None, "fsdp", "tp", None),
        P(),
        P("fsdp", "tp"),
        P("fsdp", "tp"),
        P("fsdp", "tp"),
        P(),
        P(),
        P("tp", "fsdp"),
        P(),
        P("fsdp", None, "tp"),
        P("fsdp", None, "tp"),
        P("fsdp", "tp", None),
    )
    return jax.shard_map(shards, mesh=mesh, in_specs=in_specs, out_specs=out_specs, check_vma=False)
```

```python
import functools

import jax
import jax.numpy as jnp
from jax import lax
from jax.experimental import pallas as pl
from jax.experimental.pallas import tpu as pltpu
from jax.sharding import PartitionSpec as P

BLOCK = 256


EPSILON = 1e-06
ROPE_BASE = 1000000.0
MASKED = -1e30
TILE_PICKS = 128


def rms_scale(row_block, gain_row):
    return (
        row_block
        * lax.rsqrt(jnp.mean(row_block * row_block, axis=-1, keepdims=True) + EPSILON)
        * gain_row
    )


def rotary_tables(sequence_length, head_width):
    half_width = head_width // 2
    inverse = ROPE_BASE ** (-2.0 * jnp.arange(half_width, dtype=jnp.float32) / head_width)
    angles = jnp.arange(sequence_length, dtype=jnp.float32)[:, None] * inverse[None, :]
    cosine_table = jnp.concatenate([jnp.cos(angles), jnp.cos(angles)], axis=-1)[:, None, :]
    sine_values = jnp.concatenate([jnp.sin(angles), jnp.sin(angles)], axis=-1)[:, None, :]
    return (cosine_table, sine_values)


def rotate(head_rows, cosine_table, sine_values):
    half_width = head_rows.shape[-1] // 2
    turned = jnp.concatenate([-head_rows[..., half_width:], head_rows[..., :half_width]], axis=-1)
    return head_rows * cosine_table + turned * sine_values


def prepare_heads(projected, gain_row, cosine_table, sine_values):
    return rotate(rms_scale(projected, gain_row), cosine_table, sine_values)


def swiglu(gate_act, up_act):
    return jax.nn.silu(gate_act) * up_act


def slot_tables(route_rows, gate_rows, expert_count, capacity):
    sequence_length = route_rows.shape[0]
    top_count = route_rows.shape[1]
    pick_count = sequence_length * top_count
    tile_count = pick_count // TILE_PICKS
    flat_routes = route_rows.reshape(-1)
    onehot = (flat_routes[:, None] == jnp.arange(expert_count, dtype=jnp.int32)[None, :]).astype(
        jnp.bfloat16
    )
    tiles = onehot.reshape(tile_count, TILE_PICKS, expert_count)
    positions = jnp.arange(TILE_PICKS, dtype=jnp.int32)
    lower = (positions[None, :] < positions[:, None]).astype(jnp.bfloat16)
    within = jnp.einsum("ij,bje->bie", lower, tiles, preferred_element_type=jnp.float32)
    tile_totals = jnp.sum(tiles.astype(jnp.float32), axis=1)
    offsets = jnp.cumsum(tile_totals, axis=0) - tile_totals
    before = within + offsets[:, None, :]
    slot_rank = jnp.sum(before * tiles.astype(jnp.float32), axis=-1).reshape(-1).astype(jnp.int32)
    slot_index = flat_routes * capacity + slot_rank
    pick_ids = jnp.arange(pick_count, dtype=jnp.int32) // top_count
    slot_owner = (
        jnp.full((expert_count * capacity,), sequence_length, jnp.int32)
        .at[slot_index]
        .set(pick_ids)
    )
    slot_weight = (
        jnp.zeros((expert_count * capacity,), jnp.float32).at[slot_index].set(gate_rows.reshape(-1))
    )
    return (slot_index, slot_owner, slot_weight)


def exchanged_layer(
    tokens,
    cotangent,
    norm1_gain,
    w_query,
    key_projection_weight,
    value_projection_weight,
    query_gain,
    key_gain,
    w_out,
    norm2_gain,
    w_gate,
    w_up,
    w_down,
    routes,
    gates,
):
    batch_count = tokens.shape[0]
    model_width = tokens.shape[3]
    sequence_length = routes.shape[2]
    top_count = routes.shape[3]
    head_features = query_gain.shape[0]
    local_experts = w_gate.shape[0]
    fsdp_count = lax.axis_size("fsdp")
    all_experts = local_experts * fsdp_count
    capacity = 7 * top_count * sequence_length // (6 * all_experts)
    query_heads = w_query.shape[1] // head_features
    kv_heads = key_projection_weight.shape[1] // head_features
    group_size = query_heads // kv_heads
    score_scale = head_features ** (-0.5)
    cosine_table, sine_values = rotary_tables(sequence_length, head_features)
    block_ids = jnp.arange(sequence_length, dtype=jnp.int32) // BLOCK
    visible = (block_ids[None, :] <= block_ids[:, None])[None, None]
    first_gain = norm1_gain.astype(jnp.float32)
    second_gain = norm2_gain.astype(jnp.float32)
    query_factor_scale = query_gain.astype(jnp.float32)
    key_scale = key_gain.astype(jnp.float32)
    zero_row = jnp.zeros((1, model_width), jnp.bfloat16)
    buffer_shape = (fsdp_count, local_experts, capacity, model_width)

    def masked_scores(query_fourfold, key_rows):
        raw_scores = (
            jnp.einsum(
                "qcgd,kcd->cgqk", query_fourfold, key_rows, preferred_element_type=jnp.float32
            )
            * score_scale
        )
        return jnp.where(visible, raw_scores, MASKED)

    def prep_heads(projected, gain_row):
        return prepare_heads(projected, gain_row, cosine_table, sine_values)

    gain_sums = (
        jnp.zeros((model_width,), jnp.float32),
        jnp.zeros((model_width,), jnp.float32),
        jnp.zeros((head_features,), jnp.float32),
        jnp.zeros((head_features,), jnp.float32),
    )
    expert_grads = (
        jnp.zeros(w_gate.shape, jnp.float32),
        jnp.zeros(w_up.shape, jnp.float32),
        jnp.zeros(w_down.shape, jnp.float32),
    )
    attn_grads = tuple(
        (
            jnp.zeros(weight_part.shape, jnp.float32)
            for weight_part in (w_query, key_projection_weight, value_projection_weight, w_out)
        )
    )
    outputs = []
    input_grads = []
    for batch_index in range(batch_count):
        query_full, key_full, value_full, out_full = (
            lax.all_gather(w_query, "fsdp", axis=0, tiled=True),
            lax.all_gather(key_projection_weight, "fsdp", axis=0, tiled=True),
            lax.all_gather(value_projection_weight, "fsdp", axis=0, tiled=True),
            lax.all_gather(w_out, "fsdp", axis=1, tiled=True),
        )
        own_rows = tokens[batch_index, 0].astype(jnp.float32)
        own_cot = cotangent[batch_index, 0]
        route_rows = routes[batch_index, 0]
        gate_rows = gates[batch_index, 0]
        first_normed = rms_scale(own_rows, first_gain).astype(jnp.bfloat16)
        normed_all = lax.all_gather(first_normed, "tp", axis=0, tiled=True)
        query_projected = jnp.dot(
            normed_all, query_full, preferred_element_type=jnp.float32
        ).reshape(sequence_length, query_heads, head_features)
        key_projected = jnp.dot(normed_all, key_full, preferred_element_type=jnp.float32).reshape(
            sequence_length, kv_heads, head_features
        )
        value_row_list = (
            jnp.dot(normed_all, value_full, preferred_element_type=jnp.float32)
            .astype(jnp.bfloat16)
            .reshape(sequence_length, kv_heads, head_features)
        )
        query_rot = prep_heads(query_projected, query_factor_scale).astype(jnp.bfloat16)
        key_rot = prep_heads(key_projected, key_scale).astype(jnp.bfloat16)
        query_fourfold = query_rot.reshape(sequence_length, kv_heads, group_size, head_features)
        scores = masked_scores(query_fourfold, key_rot)
        row_max = jnp.max(scores, axis=-1, keepdims=True)
        exp_scores = jnp.exp(scores - row_max)
        totals = jnp.sum(exp_scores, axis=-1, keepdims=True)
        log_total = row_max + jnp.log(totals)
        prob_rows = (exp_scores / totals).astype(jnp.bfloat16)
        context = (
            jnp.einsum(
                "cgqk,kcd->qcgd", prob_rows, value_row_list, preferred_element_type=jnp.float32
            )
            .astype(jnp.bfloat16)
            .reshape(sequence_length, query_heads * head_features)
        )
        attn_own = lax.psum_scatter(
            jnp.dot(context, out_full, preferred_element_type=jnp.float32).astype(jnp.bfloat16),
            "tp",
            scatter_dimension=0,
            tiled=True,
        ).astype(jnp.float32)
        hidden_own = own_rows + attn_own
        second_normed = rms_scale(hidden_own, second_gain).astype(jnp.bfloat16)
        normed_two, cot_all = (
            lax.all_gather(second_normed, "tp", axis=0, tiled=True),
            lax.all_gather(own_cot, "tp", axis=0, tiled=True),
        )
        slot_index, slot_owner, slot_weight = slot_tables(
            route_rows, gate_rows, all_experts, capacity
        )
        padded_rows = jnp.concatenate([normed_two, zero_row], axis=0)
        send_rows = padded_rows[slot_owner].reshape(buffer_shape)
        expert_in = lax.all_to_all(send_rows, "fsdp", split_axis=0, concat_axis=0, tiled=True)
        gate_act = jnp.einsum(
            "sekd,edf->sekf", expert_in, w_gate, preferred_element_type=jnp.float32
        )
        up_act = jnp.einsum("sekd,edf->sekf", expert_in, w_up, preferred_element_type=jnp.float32)
        act_rows = swiglu(gate_act, up_act).astype(jnp.bfloat16)
        expert_out = jnp.einsum(
            "sekf,efd->sekd", act_rows, w_down, preferred_element_type=jnp.float32
        )
        returned = lax.all_to_all(
            expert_out.astype(jnp.bfloat16), "fsdp", split_axis=0, concat_axis=0, tiled=True
        ).astype(expert_out.dtype)
        picked = returned.reshape(all_experts * capacity, model_width)[slot_index].reshape(
            sequence_length, top_count, model_width
        )
        moe_part = jnp.sum(picked * gate_rows[:, :, None], axis=1)
        moe_own = lax.psum_scatter(
            moe_part.astype(jnp.bfloat16), "tp", scatter_dimension=0, tiled=True
        ).astype(jnp.float32)
        outputs.append((hidden_own + moe_own).astype(jnp.bfloat16))
        cot_padded = jnp.concatenate([cot_all, zero_row], axis=0)
        send_grads = (
            (slot_weight[:, None] * cot_padded[slot_owner])
            .astype(jnp.bfloat16)
            .reshape(buffer_shape)
        )
        out_grads = lax.all_to_all(send_grads, "fsdp", split_axis=0, concat_axis=0, tiled=True)
        act_grads = jnp.einsum(
            "sekd,efd->sekf", out_grads, w_down, preferred_element_type=jnp.float32
        )
        _, swiglu_back = jax.vjp(swiglu, gate_act, up_act)
        gate_grads, up_grads = swiglu_back(act_grads)
        gate_grads = gate_grads.astype(jnp.bfloat16)
        up_grads = up_grads.astype(jnp.bfloat16)
        expert_grads = (
            expert_grads[0]
            + jnp.einsum(
                "sekd,sekf->edf", expert_in, gate_grads, preferred_element_type=jnp.float32
            ),
            expert_grads[1]
            + jnp.einsum("sekd,sekf->edf", expert_in, up_grads, preferred_element_type=jnp.float32),
            expert_grads[2]
            + jnp.einsum("sekf,sekd->efd", act_rows, out_grads, preferred_element_type=jnp.float32),
        )
        input_part = jnp.einsum(
            "sekf,edf->sekd", gate_grads, w_gate, preferred_element_type=jnp.float32
        ) + jnp.einsum("sekf,edf->sekd", up_grads, w_up, preferred_element_type=jnp.float32)
        input_back = lax.all_to_all(
            input_part.astype(jnp.bfloat16), "fsdp", split_axis=0, concat_axis=0, tiled=True
        ).astype(input_part.dtype)
        normed_grads = jnp.sum(
            input_back.reshape(all_experts * capacity, model_width)[slot_index].reshape(
                sequence_length, top_count, model_width
            ),
            axis=1,
        )
        normed_own = lax.psum_scatter(
            normed_grads.astype(jnp.bfloat16), "tp", scatter_dimension=0, tiled=True
        ).astype(jnp.float32)
        _, second_back = jax.vjp(rms_scale, hidden_own, second_gain)
        hidden_part, second_gain_grad = second_back(normed_own)
        hidden_grad = own_cot.astype(jnp.float32) + hidden_part
        attn_grad_all = lax.all_gather(hidden_grad.astype(jnp.bfloat16), "tp", axis=0, tiled=True)
        out_weight_grad = jnp.einsum(
            "th,td->hd", context, attn_grad_all, preferred_element_type=jnp.float32
        )
        context_grad = (
            jnp.einsum("td,hd->th", attn_grad_all, out_full, preferred_element_type=jnp.float32)
            .astype(jnp.bfloat16)
            .reshape(sequence_length, kv_heads, group_size, head_features)
        )
        exp_again = jnp.exp(masked_scores(query_fourfold, key_rot) - log_total)
        probs_again = exp_again.astype(jnp.bfloat16)
        prob_grads = jnp.einsum(
            "qcgd,kcd->cgqk", context_grad, value_row_list, preferred_element_type=jnp.float32
        )
        value_grads = (
            jnp.einsum(
                "cgqk,qcgd->kcd", probs_again, context_grad, preferred_element_type=jnp.float32
            )
            .astype(jnp.bfloat16)
            .reshape(sequence_length, kv_heads * head_features)
        )
        score_grads = (
            exp_again * (prob_grads - jnp.sum(exp_again * prob_grads, axis=-1, keepdims=True))
        ).astype(jnp.bfloat16)
        query_rot_grads = (
            jnp.einsum("cgqk,kcd->qcgd", score_grads, key_rot, preferred_element_type=jnp.float32)
            * score_scale
        ).reshape(sequence_length, query_heads, head_features)
        key_rot_grads = (
            jnp.einsum(
                "cgqk,qcgd->kcd", score_grads, query_fourfold, preferred_element_type=jnp.float32
            )
            * score_scale
        )
        _, query_back = jax.vjp(prep_heads, query_projected, query_factor_scale)
        query_proj_grads, query_gain_grad = query_back(query_rot_grads)
        _, key_back = jax.vjp(prep_heads, key_projected, key_scale)
        key_proj_grads, key_gain_grad = key_back(key_rot_grads)
        query_proj_grads = query_proj_grads.astype(jnp.bfloat16).reshape(
            sequence_length, query_heads * head_features
        )
        key_proj_grads = key_proj_grads.astype(jnp.bfloat16).reshape(
            sequence_length, kv_heads * head_features
        )
        first_normed_grads = (
            jnp.einsum(
                "tq,dq->td", query_proj_grads, query_full, preferred_element_type=jnp.float32
            )
            + jnp.einsum("tq,dq->td", key_proj_grads, key_full, preferred_element_type=jnp.float32)
            + jnp.einsum("tq,dq->td", value_grads, value_full, preferred_element_type=jnp.float32)
        )
        weight_parts = (
            jnp.einsum(
                "td,tq->dq", normed_all, query_proj_grads, preferred_element_type=jnp.float32
            ),
            jnp.einsum("td,tq->dq", normed_all, key_proj_grads, preferred_element_type=jnp.float32),
            jnp.einsum("td,tq->dq", normed_all, value_grads, preferred_element_type=jnp.float32),
            out_weight_grad,
        )
        first_own = lax.psum_scatter(
            first_normed_grads.astype(jnp.bfloat16), "tp", scatter_dimension=0, tiled=True
        ).astype(jnp.float32)
        _, first_back = jax.vjp(rms_scale, own_rows, first_gain)
        row_part, first_gain_grad = first_back(first_own)
        input_grads.append((hidden_grad + row_part).astype(jnp.bfloat16))
        gain_sums = (
            gain_sums[0] + first_gain_grad,
            gain_sums[1] + second_gain_grad,
            gain_sums[2] + query_gain_grad,
            gain_sums[3] + key_gain_grad,
        )
        attn_grads = jax.tree.map(
            jnp.add,
            attn_grads,
            (
                lax.psum_scatter(weight_parts[0], "fsdp", scatter_dimension=0, tiled=True),
                lax.psum_scatter(weight_parts[1], "fsdp", scatter_dimension=0, tiled=True),
                lax.psum_scatter(weight_parts[2], "fsdp", scatter_dimension=0, tiled=True),
                lax.psum_scatter(weight_parts[3], "fsdp", scatter_dimension=1, tiled=True),
            ),
        )
    summed = lax.psum((gain_sums[0], gain_sums[1], gain_sums[2], gain_sums[3]), ("fsdp", "tp"))
    block_out = jnp.stack(outputs)[:, None]
    input_grad = jnp.stack(input_grads)[:, None]
    return (
        block_out,
        input_grad,
        summed[0],
        attn_grads[0],
        attn_grads[1],
        attn_grads[2],
        summed[2],
        summed[3],
        attn_grads[3],
        summed[1],
        expert_grads[0],
        expert_grads[1],
        expert_grads[2],
    )


MESH = pl.DeviceIdType.MESH
FSDP, TP = "fsdp", "tp"
PLANE = 4
LANES = 128
MIB = 1 << 20
RIGHT, LEFT, FIRST, SECOND, CORE, CROSS = range(6)
TRANSPOSED_LEFT = (((0,), (0,)), ((), ()))
TRANSPOSED_RIGHT = (((1,), (1,)), ((), ()))
OUTPUT, BACK = range(2)
CHUNK = 512


class Spot:
    def __init__(self, line, wide, turned=True):
        self.line = line
        self.wide = wide
        self.turned = turned
        self.planes = 4 if wide else 2
        index = lax.axis_index(FSDP)
        self.x = lax.axis_index(TP)
        self.z = lax.div(index, PLANE)
        self.y = lax.rem(lax.div(index, 2), 2)
        self.core = lax.rem(index, 2)

    def side(self, core, first, second):
        flip_y, flip_x = first, second
        if self.wide and self.turned:
            flip_y = (1 - core) * first + core * second
            flip_x = core * first + (1 - core) * second
        return self.y + flip_y * (1 - 2 * self.y), self.x + flip_x * (1 - 2 * self.x)

    def block(self, core, first, second, z):
        y, x = self.side(core, first, second)
        return z * PLANE + y * 2 + core, x

    def device(self, kind):
        if kind == RIGHT:
            return self.block(self.core, 0, 0, self.z + 1)
        if kind == LEFT:
            return self.block(self.core, 0, 0, self.z - 1)
        if kind == CORE:
            return self.block(1 - self.core, 0, 0, self.z)
        if kind == CROSS:
            return self.block(self.core, 0, 0, self.z)[0], 1 - self.x
        return self.block(self.core, int(kind == FIRST), int(kind == SECOND), self.z)

    def kinds(self):
        return (FIRST, SECOND, CORE) if self.wide else (FIRST, CORE)

    def number(self, first, second, z):
        return (second * 2 + first) * self.line + z

    def order(self, step):
        if isinstance(step, int) and step == 0:
            return [(self.z, None)]
        return [(self.z - step, self.z - step >= 0), (self.z + step, self.z + step < self.line)]

    def greet(self):
        barrier = pltpu.get_barrier_semaphore()

        def signal(kind):
            pl.semaphore_signal(barrier, inc=1, device_id=self.device(kind), device_id_type=MESH)

        for kind in self.kinds():
            signal(kind)
        when(self.z + 1 < self.line, lambda: signal(RIGHT))
        when(self.z > 0, lambda: signal(LEFT))
        around = (self.z + 1 < self.line).astype(jnp.int32) + (self.z > 0).astype(jnp.int32)
        pl.semaphore_wait(barrier, len(self.kinds()) + around)

    def send(self, source, target, send_sem, receive_sem, kind):
        return pltpu.make_async_remote_copy(
            src_ref=source,
            dst_ref=target,
            send_sem=send_sem,
            recv_sem=receive_sem,
            device_id=self.device(kind),
            device_id_type=MESH,
        )


def when(condition, action):
    def run():
        action()

    if condition is None or condition is True:
        run()
    elif condition is not False:
        pl.when(condition)(run)


class Spread:
    def __init__(self, spot, source, slot, send, receive, local):
        self.spot = spot
        self.slot = slot
        self.source = source
        self.sends = send
        self.receives = receive
        self.mine = pltpu.make_async_copy(source, slot(*spot.block(spot.core, 0, 0, spot.z)), local)

    def copy(self, first, second, z, kind, own=False):
        spot = self.spot
        place = self.slot(*spot.block(spot.core, first, second, z))
        number = spot.number(first, second, z)
        arrival = {
            RIGHT: number,
            LEFT: number,
            FIRST: spot.number(1, 0, z),
            SECOND: spot.number(first, 1, z),
            CORE: spot.planes * spot.line + number,
        }[kind]
        departure = {RIGHT: 0, LEFT: 1, FIRST: 2, SECOND: 3, CORE: 5}[kind] * spot.line + number
        source = self.source if own else place
        return spot.send(source, place, self.sends.at[departure], self.receives.at[arrival], kind)

    def arrived(self, first, second, z, other=False):
        spot = self.spot
        core = 1 - spot.core if other else spot.core
        place = self.slot(*spot.block(core, first, second, z))
        number = spot.number(first, second, z) + (spot.planes * spot.line if other else 0)
        spot.send(place, place, self.sends.at[0], self.receives.at[number], CORE).wait_recv()

    def steps(self):
        return self.spot.line + (3 if self.spot.wide else 1)

    def begin(self):
        spot = self.spot
        z = spot.z
        when(z + 1 < spot.line, lambda: self.copy(0, 0, z, RIGHT, True).start())
        when(z > 0, lambda: self.copy(0, 0, z, LEFT, True).start())
        for kind in spot.kinds():
            self.copy(0, 0, z, kind, True).start()
        self.mine.start()

    def step(self, step):
        spot = self.spot
        line, z = spot.line, spot.z

        def reached(away, action):
            inside = jnp.logical_and(away >= 0, away < line)
            when(jnp.logical_and(inside, z - away >= 0), lambda: action(z - away, True))
            when(
                jnp.logical_and(inside, jnp.logical_and(away > 0, z + away < line)),
                lambda: action(z + away, False),
            )

        def along(zz, from_left):
            self.arrived(0, 0, zz)
            if from_left:
                when(z + 1 < line, lambda: self.copy(0, 0, zz, RIGHT).start())
            else:
                when(z > 0, lambda: self.copy(0, 0, zz, LEFT).start())
            for kind in spot.kinds():
                self.copy(0, 0, zz, kind).start()

        def firsts(zz, _):
            self.arrived(1, 0, zz)
            if spot.wide:
                self.copy(1, 0, zz, SECOND).start()
            self.copy(1, 0, zz, CORE).start()

        def lasts(first):
            def action(zz, _):
                self.arrived(first, 1, zz)
                self.copy(first, 1, zz, CORE).start()

            return action

        step = jnp.asarray(step, jnp.int32)
        reached(step, along)
        reached(step - 1, firsts)
        if spot.wide:
            reached(step - 2, lasts(0))
            reached(step - 3, lasts(1))

    def finish(self):
        spot = self.spot
        z = spot.z

        def body(zz, _):
            when(
                jnp.logical_and(z + 1 < spot.line, zz <= z),
                lambda: self.copy(0, 0, zz, RIGHT).wait_send(),
            )
            when(jnp.logical_and(z > 0, zz >= z), lambda: self.copy(0, 0, zz, LEFT).wait_send())
            self.copy(0, 0, zz, FIRST).wait_send()
            for second in range(2 if spot.wide else 1):
                for first in (0, 1):
                    if spot.wide and not second:
                        self.copy(first, 0, zz, SECOND).wait_send()
                    self.copy(first, second, zz, CORE).wait_send()
                    self.arrived(first, second, zz, other=True)
            return 0

        lax.fori_loop(0, spot.line, body, 0)
        self.mine.wait()


class LateSpread(Spread):
    def steps(self):
        return self.spot.line + 2

    def copy(self, first, second, z, kind, own=False):
        spot = self.spot
        place = self.slot(*spot.block(spot.core, first, second, z))
        number = spot.number(first, second, z)
        arrival = {
            RIGHT: number,
            LEFT: number,
            FIRST: spot.number(1, 0, z),
            SECOND: spot.number(first, 1, z),
            CORE: spot.planes * spot.line + number,
        }[kind]
        departure = {RIGHT: 0, LEFT: 4, CORE: 8, FIRST: 12, SECOND: 13}[kind] * spot.line + number
        source = self.source if own else place
        return spot.send(source, place, self.sends.at[departure], self.receives.at[arrival], kind)

    def along_both(self, first, second, own=False):
        spot = self.spot
        z = spot.z
        when(z + 1 < spot.line, lambda: self.copy(first, second, z, RIGHT, own).start())
        when(z > 0, lambda: self.copy(first, second, z, LEFT, own).start())
        self.copy(first, second, z, CORE, own).start()

    def begin(self):
        self.copy(0, 0, self.spot.z, FIRST, True).start()
        self.copy(0, 0, self.spot.z, SECOND, True).start()
        self.along_both(0, 0, True)
        self.mine.start()

    def step(self, step):
        spot = self.spot
        line, z = spot.line, spot.z
        step = jnp.asarray(step, jnp.int32)

        def passed(first, second, zz, kind, more):
            self.arrived(first, second, zz)
            when(more, lambda: self.copy(first, second, zz, kind).start())
            self.copy(first, second, zz, CORE).start()

        for first, second in ((0, 0), (1, 0), (0, 1), (1, 1)):
            away = step - (first + second)

            def here():
                self.arrived(first, second, z)
                if first and not second:
                    self.copy(1, 0, z, SECOND).start()
                self.along_both(first, second)

            if first or second:
                when(away == 0, here)
            far = jnp.logical_and(away > 0, away < line)
            when(
                jnp.logical_and(far, z - away >= 0),
                lambda: passed(first, second, z - away, RIGHT, z + 1 < line),
            )
            when(
                jnp.logical_and(far, z + away < line),
                lambda: passed(first, second, z + away, LEFT, z > 0),
            )

    def finish(self):
        spot = self.spot
        z = spot.z

        def body(zz, _):
            for second in (0, 1):
                for first in (0, 1):
                    when(
                        jnp.logical_and(z + 1 < spot.line, zz <= z),
                        lambda: self.copy(first, second, zz, RIGHT).wait_send(),
                    )
                    when(
                        jnp.logical_and(z > 0, zz >= z),
                        lambda: self.copy(first, second, zz, LEFT).wait_send(),
                    )
                    self.copy(first, second, zz, CORE).wait_send()
                    self.arrived(first, second, zz, other=True)
            return 0

        lax.fori_loop(0, spot.line, body, 0)
        self.copy(0, 0, z, FIRST).wait_send()
        for first in (0, 1):
            self.copy(first, 0, z, SECOND).wait_send()
        self.mine.wait()


def rows_spread(spot, source, place, rows, semaphores, at):
    late = late_rows(rows)
    early = rows - late
    send, receive, late_send, late_receive, local = semaphores

    def slot(start, size):
        return lambda block, side: place(block, side * rows + start, size)

    return [
        Spread(
            spot,
            source.at[pl.ds(0, early)],
            slot(0, early),
            send.at[at],
            receive.at[at],
            local.at[at, 0],
        ),
        LateSpread(
            spot,
            source.at[pl.ds(early, late)],
            slot(early, late),
            late_send.at[at],
            late_receive.at[at],
            local.at[at, 1],
        ),
    ]


def late_rows(rows):
    return max(16, round(rows * 2 / 9 / 16) * 16)


def rows_semaphores(batch, line):
    counts = (*spread_count(line, True), 15 * line, 8 * line, 2)
    return [pltpu.SemaphoreType.DMA((batch, count)) for count in counts]


def run_trees(trees):
    for tree in trees:
        tree.begin()

    def body(step, _):
        for tree in trees:
            tree.step(step)
        return 0

    lax.fori_loop(1, max(tree.steps() for tree in trees), body, 0)
    for tree in trees:
        tree.finish()


def spread_count(line, wide):
    return (9 if wide else 7) * line, (8 if wide else 4) * line


def mingle(work, others):
    for index, piece in enumerate(work):
        piece()
        for other in others[
            index * len(others) // len(work) : (index + 1) * len(others) // len(work)
        ]:
            other()


def rows_at(ref, index, size):
    return ref.at[pl.ds(pl.multiple_of(index * size, 16), size)]


def columns_at(ref, index, size):
    return ref.at[:, pl.ds(pl.multiple_of(index * size, LANES), size)]


def norm_rows(target, source, gain):
    def body(step, _):
        rows = pl.ds(pl.multiple_of(step * 16, 16), 16)
        value = source[rows, :].astype(jnp.float32)
        target[rows, :] = rms_scale(value, gain[...].astype(jnp.float32)).astype(target.dtype)
        return 0

    lax.fori_loop(0, target.shape[0] // 16, body, 0)


def turned_heads(value, gain, cosine, sine):
    normed = rms_scale(value, gain)
    return normed * cosine + pltpu.roll(normed, normed.shape[-1] // 2, 1) * sine


def visible_blocks(length, group):
    blocks = []
    for start in range(0, length, BLOCK):
        stop = min(start + BLOCK, length)
        heads = max(1, BLOCK // (stop - start))
        while group % heads:
            heads -= 1
        blocks.append((start, stop, stop, heads))
    return blocks


def softmax(scores):
    raised = jnp.exp(scores - jnp.max(scores, axis=0, keepdims=True))
    return raised * (1.0 / jnp.sum(raised, axis=0, keepdims=True))


def for_heads(low, high, heads, body):
    turns = 2 if heads == 1 and (high - low) % 2 == 0 else 1

    def turn(step, _):
        for i in range(turns):
            body(low + (step * turns + i) * heads)
        return 0

    count = (high - low) // (heads * turns)
    if count == 1:
        turn(0, 0)
    else:
        lax.fori_loop(0, count, turn, 0)


def head_columns(head, features):
    return pl.ds(pl.multiple_of(head * features, LANES), features)


def forward_kernel(
    line,
    heads,
    kv_heads,
    tokens_ref,
    cot_ref,
    in_ref,
    out_ref,
    picks_ref,
    gain1_ref,
    gain2_ref,
    query_gain_ref,
    key_gain_ref,
    cosine_ref,
    sine_ref,
    cot_all,
    in_all,
    out_all,
    picks_all,
    normed_all,
    projected_all,
    context_all,
    hidden_all,
    second_all,
    in_w,
    out_w,
    tokens,
    normed,
    projected,
    context,
    queries,
    keys,
    values,
    mixed,
    mixed_other,
    hidden,
    second,
    narrow_send,
    narrow_receive,
    cot_send,
    cot_receive,
    cot_late_send,
    cot_late_receive,
    cot_local,
    local,
    token_send,
    token_receive,
    mixed_send,
    mixed_receive,
    save_sem,
):
    cot_semaphores = (cot_send, cot_receive, cot_late_send, cot_late_receive, cot_local)
    batch, half, width = tokens_ref.shape
    length = 2 * half
    depth, out_width = in_ref.shape[0], out_ref.shape[1]
    features = query_gain_ref.shape[1]
    narrow = Spot(line, False)
    spot = Spot(line, True, turned=False)
    x = spot.x
    spot.greet()
    slots = [
        (picks_ref, lambda block, side: picks_all.at[block]),
        (in_ref, lambda block, side: rows_at(in_w, block, depth)),
        (out_ref, lambda block, side: columns_at(out_w, block, out_width)),
    ]
    weights = [
        Spread(narrow, source, slot, narrow_send.at[i], narrow_receive.at[i], local.at[i])
        for i, (source, slot) in enumerate(slots)
    ]
    place = lambda block, start, size: cot_all.at[block, pl.ds(pl.multiple_of(start, 16), size)]
    cots = rows_spread(spot, cot_ref.at[0], place, half, cot_semaphores, 0)
    early, late = weights[:2], weights[2]
    for tree in early:
        tree.begin()
    late.begin()

    def token_copies(i):
        place = rows_at(tokens.at[i], x, half)
        return (
            pltpu.make_async_copy(tokens_ref.at[i], place, local.at[3 + i]),
            spot.send(tokens_ref.at[i], place, token_send.at[i], token_receive.at[i], CROSS),
        )

    for i in range(batch):
        for copy in token_copies(i):
            copy.start()
    def steps(step, _):
        for tree in early:
            tree.step(step)
        return 0

    lax.fori_loop(1, late.steps(), steps, 0)
    for tree in cots:
        tree.begin()
    for i in range(batch):
        mine, other = token_copies(i)
        mine.wait()
        other.wait_send()
        place = rows_at(tokens.at[i], 1 - x, half)
        spot.send(place, place, token_send.at[i], token_receive.at[i], CROSS).wait_recv()
    for i in range(batch):
        norm_rows(normed.at[i], tokens.at[i], gain1_ref)
    for tree in early:
        tree.finish()

    def save(source, target, index):
        return pltpu.make_async_copy(source, target, save_sem.at[index])

    saves = [save(in_w, in_all, 0), save(out_w, out_all, 1)]
    saves[0].start()

    def project(i, start, stop):
        for at in range(start, stop, CHUNK):
            projected[i, :, at : at + CHUNK] = jnp.dot(
                normed[i], in_w[:, at : at + CHUNK], preferred_element_type=jnp.float32
            )

    scale = features ** (-0.5)

    group = heads // kv_heads

    def prepare_keys(i):
        base = heads * features
        for head in range(kv_heads):
            at = base + head * features
            keys[head] = turned_heads(
                projected[i, :, at : at + features],
                key_gain_ref[...].astype(jnp.float32),
                cosine_ref[...],
                sine_ref[...],
            ).astype(jnp.bfloat16)
            at = base + (kv_heads + head) * features
            values[head] = projected[i, :, at : at + features].astype(jnp.bfloat16)

    def prepare_queries(i, shared):
        def prepare(member):
            columns = head_columns(shared * group + member, features)
            queries[member] = turned_heads(
                projected[i, :, columns], query_gain_ref[...].astype(jnp.float32), cosine_ref[...], sine_ref[...]
            ).astype(jnp.bfloat16)

        for_heads(0, group, 1, prepare)

    def attend(i, shared, start, stop, seen, at_once, low, high):
        count = stop - start

        def block(member):
            query = queries[pl.ds(member, at_once), start:stop, :].reshape(-1, features)
            scores = lax.dot_general(
                keys[shared, :seen, :],
                query,
                TRANSPOSED_RIGHT,
                preferred_element_type=jnp.float32,
            )
            rows = lax.dot_general(
                softmax(scores * scale).astype(jnp.bfloat16),
                values[shared, :seen, :],
                TRANSPOSED_LEFT,
                preferred_element_type=jnp.float32,
            ).astype(jnp.bfloat16)
            for j in range(at_once):
                columns = head_columns(shared * group + member + j, features)
                context[i, start:stop, columns] = rows[j * count : (j + 1) * count]

        for_heads(low, high, at_once, block)

    def mixed_copy(i):
        return spot.send(
            rows_at(mixed.at[i], 1 - x, half),
            mixed_other.at[i],
            mixed_send.at[i],
            mixed_receive.at[i],
            CROSS,
        )

    def mix(i, start, stop):
        for at in range(start, stop, CHUNK):
            mixed[i, :, at : at + CHUNK] = jnp.dot(
                context[i], out_w[:, at : at + CHUNK], preferred_element_type=jnp.float32
            ).astype(jnp.bfloat16)
        if stop == width:
            mixed_copy(i).start()

    def close(i):
        mixed_copy(i).wait()
        add_rows(
            hidden.at[i],
            [rows_at(tokens.at[i], x, half), rows_at(mixed.at[i], x, half), mixed_other.at[i]],
        )
        norm_rows(second.at[i], hidden.at[i], gain2_ref)

    def late_done():
        late.finish()
        saves[1].start()

    def steps_of(trees, low, high):
        return [
            functools.partial(tree.step, step)
            for step in range(low, high)
            for tree in trees
            if step < tree.steps()
        ]

    in_width = in_w.shape[1]
    parts = lambda size: [(at, min(at + 2 * CHUNK, size)) for at in range(0, size, 2 * CHUNK)]
    opening, middle, closing = [], [], []
    for i in range(batch):
        opening += [functools.partial(project, i, *part) for part in parts(in_width)]
        middle.append(functools.partial(prepare_keys, i))
        for shared in range(kv_heads):
            middle.append(functools.partial(prepare_queries, i, shared))
            for start, stop, seen, at_once in visible_blocks(length, group):
                share = max(at_once, group // 2)
                for low in range(0, group, share):
                    middle.append(
                        functools.partial(
                            attend, i, shared, start, stop, seen, at_once, low, low + share
                        )
                    )
        closing += [functools.partial(mix, i, *part) for part in parts(width)]
    closing += [functools.partial(close, i) for i in range(batch)]
    last = cots[0].steps()
    mingle(opening + middle, steps_of([late] + cots, 1, late.steps()))
    late_done()
    mingle(closing, steps_of(cots, late.steps(), last))

    saves += [
        save(source, target, 2 + i)
        for i, (source, target) in enumerate(
            [
                (normed, normed_all),
                (projected, projected_all),
                (context, context_all),
                (hidden, hidden_all),
                (second, second_all),
            ]
        )
    ]
    for copy in saves[2:]:
        copy.start()
    for tree in cots:
        tree.finish()
    for copy in saves:
        copy.wait()


def run_forward(tokens, cot, weight_in, weight_out, picks, gains, tables, fsdp_count, kv_heads):
    line = fsdp_count // PLANE
    batch, half, width = tokens.shape
    length = 2 * half
    features = gains[2].shape[1]
    heads = weight_out.shape[0] // features
    in_shape = (weight_in.shape[0] * fsdp_count, weight_in.shape[1])
    out_shape = (weight_out.shape[0], weight_out.shape[1] * fsdp_count)
    narrow = spread_count(line, False)
    anywhere = pl.BlockSpec(memory_space=pl.ANY)
    inside = pl.BlockSpec(memory_space=pltpu.VMEM)
    shape = lambda dims, kind=jnp.bfloat16: jax.ShapeDtypeStruct(dims, kind)
    vmem = lambda *dims: pltpu.VMEM(dims, jnp.bfloat16)
    sem = lambda *dims: pltpu.SemaphoreType.DMA(dims)
    kept = (
        ((batch, length, width), jnp.bfloat16),
        ((batch, length, weight_in.shape[1]), jnp.float32),
        ((batch, length, heads * features), jnp.bfloat16),
        ((batch, half, width), jnp.float32),
        ((batch, half, width), jnp.bfloat16),
    )
    return pl.pallas_call(
        functools.partial(forward_kernel, line, heads, kv_heads),
        out_shape=(
            shape((fsdp_count, length, width)),
            shape(in_shape),
            shape(out_shape),
            shape((fsdp_count, *picks.shape), picks.dtype),
            *(shape(*one) for one in kept),
        ),
        in_specs=[anywhere] * 5 + [inside] * 6,
        out_specs=(anywhere,) * 9,
        scratch_shapes=[
            vmem(*in_shape),
            vmem(*out_shape),
            vmem(batch, length, width),
            *(pltpu.VMEM(*one) for one in kept[:3]),
            vmem(heads // kv_heads, length, features),
            vmem(kv_heads, length, features),
            vmem(kv_heads, length, features),
            vmem(batch, length, width),
            vmem(batch, half, width),
            *(pltpu.VMEM(*one) for one in kept[3:]),
            sem(3, narrow[0]),
            sem(3, narrow[1]),
            *rows_semaphores(1, line),
            sem(3 + batch),
            sem(batch),
            sem(batch),
            sem(batch),
            sem(batch),
            sem(7),
        ],
        compiler_params=pltpu.CompilerParams(
            collective_id=1, has_side_effects=True, vmem_limit_bytes=60 * MIB
        ),
    )(tokens, cot, weight_in, weight_out, picks, *gains, *tables)


def add_rows(target, sources):
    def body(step, _):
        rows = pl.ds(pl.multiple_of(step * 16, 16), 16)
        total = sources[0][rows, :].astype(jnp.float32)
        for source in sources[1:]:
            total = total + source[rows, :].astype(jnp.float32)
        target[rows, :] = total.astype(target.dtype)
        return 0

    lax.fori_loop(0, target.shape[0] // 16, body, 0)


class Collect:
    def __init__(self, spot, part, total, cores, firsts, rights, lefts, send, receive):
        self.spot = spot
        self.part = part
        self.total = total
        self.places = {CORE: cores, FIRST: firsts, RIGHT: rights, LEFT: lefts}
        line = spot.line
        self.base = {CORE: 0, FIRST: 2 * line, RIGHT: 3 * line, LEFT: 4 * line}
        self.sends = send
        self.receives = receive

    def own(self, first, z):
        return self.part(*self.spot.block(self.spot.core, first, 0, z))

    def copy(self, kind, first, z):
        spot = self.spot
        number = first * spot.line + z if kind == CORE else z
        source = self.part(*spot.block(1 - spot.core, first, 0, z)) if kind == CORE else self.own(first, z)
        at = self.base[kind] + number
        return spot.send(
            source, self.places[kind].at[number], self.sends.at[at], self.receives.at[at], kind
        )

    def arrived(self, kind, number):
        place = self.places[kind].at[number]
        at = self.base[kind] + number
        self.spot.send(place, place, self.sends.at[0], self.receives.at[at], CORE).wait_recv()
        return place

    def begin(self, z):
        for first in (1, 0):
            self.copy(CORE, first, z).start()

    def to_first(self, z):
        add_rows(self.own(1, z), [self.own(1, z), self.arrived(CORE, self.spot.line + z)])
        self.copy(FIRST, 1, z).start()

    def summands(self, z):
        return [self.own(0, z), self.arrived(CORE, z), self.arrived(FIRST, z)]

    def cross(self):
        for step in reversed(range(self.spot.line)):
            for zz, valid in self.spot.order(step):
                when(valid, functools.partial(self.to_first, zz))

    def onward(self, kind, zz):
        spot = self.spot
        sources = self.summands(zz)
        target = self.own(0, zz)
        behind = spot.z > 0 if kind == RIGHT else spot.z + 1 < spot.line
        when(behind, lambda: add_rows(target, sources + [self.arrived(kind, zz)]))
        when(jnp.logical_not(behind), lambda: add_rows(target, sources))
        self.copy(kind, 0, zz).start()

    def last(self):
        z, line = self.spot.z, self.spot.line
        sources = self.summands(z)

        def end(kinds):
            add_rows(self.total, sources + [self.arrived(kind, z) for kind in kinds])

        when(z == 0, lambda: end([LEFT]))
        when(z == line - 1, lambda: end([RIGHT]))
        when(jnp.logical_and(z > 0, z < line - 1), lambda: end([RIGHT, LEFT]))

    def finish(self):
        spot = self.spot
        for zz in range(spot.line):
            for first in (0, 1):
                self.copy(CORE, first, zz).wait_send()
            self.copy(FIRST, 1, zz).wait_send()
            when(zz > spot.z, lambda: self.copy(RIGHT, 0, zz).wait_send())
            when(zz < spot.z, lambda: self.copy(LEFT, 0, zz).wait_send())

    def tasks(self):
        spot = self.spot
        work = []
        for step in reversed(range(1, spot.line)):
            for kind, (zz, valid) in zip((LEFT, RIGHT), spot.order(step)):
                action = functools.partial(self.onward, kind, zz)
                work.append(functools.partial(when, valid, action))
        return work + [self.last, self.finish]


def collect_scratch(line, shape):
    counts = (2 * line, line, line, line)
    return [pltpu.VMEM((count, *shape), jnp.bfloat16) for count in counts] + [
        pltpu.SemaphoreType.DMA((5 * line,)),
        pltpu.SemaphoreType.DMA((5 * line,)),
    ]


BOXES = 6


def plane_in_turn(line, group):
    turn = lax.rem(group, line)
    step = lax.div(turn, 2)
    return jnp.where(lax.rem(turn, 2) == 0, step, line - 1 - step)


class Sums:
    def __init__(
        self, spot, half, parts, cores, places, inbox, outbox, semaphores, late, plane, inside, ready, done, turns
    ):
        self.spot = spot
        self.half = half
        (
            self.late_ends,
            self.late_seconds,
            self.late_firsts,
            self.late_inbox,
            self.late_outbox,
            self.late_sums,
            self.late_inbox_sem,
            self.late_outbox_sem,
            self.late_sums_sem,
            self.late_end_receive,
            self.late_second_receive,
            self.late_first_receive,
        ) = late
        self.parts = parts
        self.cores = cores
        self.seconds, self.firsts, self.ends = places
        self.inbox = inbox
        self.outbox = outbox
        (
            self.inbox_sem,
            self.outbox_sem,
            self.second_receive,
            self.first_receive,
            self.end_receive,
        ) = semaphores
        self.plane = plane
        self.inside = inside
        self.ready = ready
        self.done = done
        self.turns = turns

    def second_slot(self, turn, first):
        return turn * 2 + first

    def first_slot(self, turn):
        return 2 * self.turns + turn

    def end_slot(self, turn, kind):
        return 3 * self.turns + turn * 2 + kind

    def free(self, unit, turn, first):
        pass

    def second_send(self, unit, turn, first):
        slot = self.second_slot(turn, first)
        return self.spot.send(
            self.outbox.at[slot],
            self.seconds.at[unit, first],
            self.outbox_sem.at[slot],
            self.second_receive.at[unit, first],
            SECOND,
        )

    def first_send(self, unit, turn):
        slot = self.first_slot(turn)
        return self.spot.send(
            self.outbox.at[slot],
            self.firsts.at[unit],
            self.outbox_sem.at[slot],
            self.first_receive.at[unit],
            FIRST,
        )

    def end_send(self, unit, turn, kind):
        slot = self.end_slot(turn, kind)
        return self.spot.send(
            self.outbox.at[slot],
            self.ends.at[unit, kind],
            self.outbox_sem.at[slot],
            self.end_receive.at[unit, kind],
            kind,
        )

    def received(self, place, semaphore):
        self.spot.send(place, place, self.outbox_sem.at[0], semaphore, CORE).wait_recv()

    def sources(self, unit, first, second):
        y, x = self.spot.side(self.spot.core, first, second)
        rows = pl.ds(pl.multiple_of(x * self.half, 16), self.inbox.shape[1])
        return [self.parts(unit, y).at[rows], self.cores(unit, y).at[rows]]

    def summands(self, unit):
        return self.sources(unit, 0, 0) + [self.seconds.at[unit, 0], self.firsts.at[unit]]

    def load(self, source, slot):
        return pltpu.make_async_copy(source, self.inbox.at[slot], self.inbox_sem.at[slot])

    def add(self, target, base, numbers):
        add_rows(target, [self.inbox.at[base + i] for i in numbers])

    def end_roles(self, half_step, delay):
        z, line = self.spot.z, self.spot.line
        unit = half_step - 3 - delay
        valid = self.inside(unit)
        plane = self.plane(unit)
        right = jnp.logical_and(valid, jnp.logical_and(z < plane, delay == z))
        left = jnp.logical_and(valid, jnp.logical_and(z > plane, delay == line - 1 - z))
        last = jnp.logical_and(
            valid,
            jnp.logical_and(z == plane, delay == jnp.maximum(plane, line - 1 - plane)),
        )
        return unit, right, left, last

    def end_task(self, half_step, delay, parity):
        z, line = self.spot.z, self.spot.line
        turn = (parity - 3 - delay) % self.turns
        unit, right, left, last = self.end_roles(half_step, delay)
        some = jnp.logical_or(right, jnp.logical_or(left, last))
        from_left = jnp.logical_and(jnp.logical_or(right, last), z > 0)
        from_right = jnp.logical_and(jnp.logical_or(left, last), z + 1 < line)
        present = ((RIGHT, from_left), (LEFT, from_right))

        def fetch(base):
            def action():
                self.received(self.seconds.at[unit, 0], self.second_receive.at[unit, 0])
                self.received(self.firsts.at[unit], self.first_receive.at[unit])
                for i, source in enumerate(self.summands(unit)):
                    self.load(source, base + i).start()
                for kind, there in present:

                    def arrive():
                        self.received(self.ends.at[unit, kind], self.end_receive.at[unit, kind])
                        self.load(self.ends.at[unit, kind], base + 4 + kind).start()

                    when(there, arrive)

            when(some, action)

        def add(base):
            def action():
                for i, source in enumerate(self.summands(unit)):
                    self.load(source, base + i).wait()
                for kind, there in present:
                    when(there, lambda: self.load(self.ends.at[unit, kind], base + 4 + kind).wait())
                numbers = list(range(4))
                for kind, chosen, behind in ((RIGHT, right, z > 0), (LEFT, left, z + 1 < line)):

                    def onward():
                        target = self.outbox.at[self.end_slot(turn, kind)]
                        self.free(unit, turn, 0)
                        when(behind, lambda: self.add(target, base, numbers + [4 + kind]))
                        when(jnp.logical_not(behind), lambda: self.add(target, base, numbers))
                        self.end_send(unit, turn, kind).start()

                    when(chosen, onward)

                def finish():
                    def into(target):
                        both = jnp.logical_and(from_left, from_right)
                        when(both, lambda: self.add(target, base, numbers + [4, 5]))
                        for kind, there in present:
                            when(
                                jnp.logical_and(there, jnp.logical_not(both)),
                                lambda: self.add(target, base, numbers + [4 + kind]),
                            )

                    self.done(unit, turn, 0, into)

                when(last, finish)

            when(some, action)

        return fetch, add

    def retire(self, half_step, parity):
        before = half_step - self.turns
        now, then = (parity - 1) % self.turns, (parity - 2) % self.turns
        when(
            self.inside(before - 1),
            lambda: [self.second_send(before - 1, now, first).wait_send() for first in range(2)],
        )
        when(self.inside(before - 2), lambda: self.first_send(before - 2, then).wait_send())
        for delay in range(self.spot.line):
            unit, right, left, _ = self.end_roles(before, delay)
            turn = (parity - 3 - delay) % self.turns
            when(right, lambda: self.end_send(unit, turn, RIGHT).wait_send())
            when(left, lambda: self.end_send(unit, turn, LEFT).wait_send())
            unit, right, left, _ = self.end_roles(before + 2, delay)
            turn = (parity - 1 - delay) % self.turns
            when(right, lambda: self.late_send(unit, turn, RIGHT).wait_send())
            when(left, lambda: self.late_send(unit, turn, LEFT).wait_send())

    def simple_task(self, valid, ready, inputs, slot, send, free=lambda: None):
        def fetch(base):
            ready()

            def action():
                for i, source in enumerate(inputs()):
                    self.load(source, base + i).start()

            when(valid, action)

        def add(base):
            def action():
                refs = inputs()
                for i, source in enumerate(refs):
                    self.load(source, base + i).wait()
                free()
                self.add(self.outbox.at[slot], base, range(len(refs)))
                send().start()

            when(valid, action)

        return fetch, add

    def tasks(self, half_step, parity):
        one, two = half_step - 1, half_step - 2
        now, then = (parity - 1) % self.turns, (parity - 2) % self.turns
        tasks = [
            self.second_task(one, now, 1, functools.partial(self.ready, one)),
            self.second_task(one, now, 0, lambda: None),
            self.first_task(two, then),
        ]
        line = self.spot.line
        tasks += [self.end_task(half_step, delay, parity) for delay in range(line)]
        others = [self.late_task(half_step, delay, parity) for delay in range(line)]
        others += [self.plane_task(half_step, stage) for stage in range(2)]
        woven = []
        for index, task in enumerate(tasks):
            woven += [task] + others[index : index + 1]
        return woven + others[len(tasks) :]

    def late_rows(self, index):
        return pl.ds(pl.multiple_of(index * self.late_inbox.shape[1] // 4, 16), self.late_inbox.shape[1] // 4)

    def late_send(self, unit, turn, kind):
        slot = turn * 2 + kind
        return self.spot.send(
            self.late_outbox.at[slot],
            self.late_ends.at[unit, kind],
            self.late_outbox_sem.at[slot],
            self.late_end_receive.at[unit, kind],
            kind,
        )

    def late_place(self, turn, first, second):
        y, x = self.spot.side(self.spot.core, first, second)
        return self.late_sums.at[turn, self.late_rows(y * 2 + x)]

    def late_second(self, unit, turn, first):
        return self.spot.send(
            self.late_place(turn, first, 1),
            self.late_seconds.at[unit, first],
            self.late_sums_sem.at[turn * 3 + first],
            self.late_second_receive.at[unit, first],
            SECOND,
        )

    def late_first(self, unit, turn):
        return self.spot.send(
            self.late_place(turn, 1, 0),
            self.late_firsts.at[unit],
            self.late_sums_sem.at[turn * 3 + 2],
            self.late_first_receive.at[unit],
            FIRST,
        )

    def late_load(self, source, target, index):
        return pltpu.make_async_copy(source, target, self.late_inbox_sem.at[index])

    def late_loads(self, unit):
        copies = []
        size = self.late_inbox.shape[1] // 4
        for y in range(2):
            for x in range(2):
                rows = pl.ds(x * self.half + self.half - size, size)
                for i, ref in enumerate((self.parts(unit, y), self.cores(unit, y))):
                    place = self.late_inbox.at[i, pl.ds((y * 2 + x) * size, size)]
                    copies.append(self.late_load(ref.at[rows], place, i * 4 + y * 2 + x))
        return copies

    def late_task(self, half_step, delay, parity):
        z, line = self.spot.z, self.spot.line
        turn = (parity - 1 - delay) % self.turns
        unit, right, left, last = self.end_roles(half_step + 2, delay)
        some = jnp.logical_or(right, jnp.logical_or(left, last))
        from_left = jnp.logical_and(jnp.logical_or(right, last), z > 0)
        from_right = jnp.logical_and(jnp.logical_or(left, last), z + 1 < line)
        present = ((RIGHT, from_left), (LEFT, from_right))
        both = jnp.logical_and(from_left, from_right)

        def behind(kind):
            return self.late_load(self.late_ends.at[unit, kind], self.late_inbox.at[2 + kind], 8 + kind)

        def fetch(base):
            def action():
                for copy in self.late_loads(unit):
                    copy.start()
                for kind, there in present:

                    def arrive():
                        self.received(self.late_ends.at[unit, kind], self.late_end_receive.at[unit, kind])
                        behind(kind).start()

                    when(there, arrive)

            when(some, action)

        def add(base):
            def total(target, kinds):
                add_rows(target, [self.late_inbox.at[i] for i in [0, 1] + [2 + kind for kind in kinds]])

            def action():
                for copy in self.late_loads(unit):
                    copy.wait()
                for kind, there in present:
                    when(there, lambda: behind(kind).wait())
                for kind, chosen, there in ((RIGHT, right, from_left), (LEFT, left, from_right)):

                    def onward():
                        target = self.late_outbox.at[turn * 2 + kind]
                        when(there, lambda: total(target, [kind]))
                        when(jnp.logical_not(there), lambda: total(target, []))
                        self.late_send(unit, turn, kind).start()

                    when(chosen, onward)

                def in_plane():
                    target = self.late_sums.at[turn]
                    when(both, lambda: total(target, [RIGHT, LEFT]))
                    for kind, there in present:
                        when(
                            jnp.logical_and(there, jnp.logical_not(both)),
                            lambda: total(target, [kind]),
                        )
                    for first in (1, 0):
                        self.late_second(unit, turn, first).start()

                when(last, in_plane)

            when(some, action)

        return fetch, add

    def plane_task(self, half_step, stage):
        z, line = self.spot.z, self.spot.line
        unit = half_step - 2 - stage - jnp.maximum(z, line - 1 - z)
        turn = lax.rem(jnp.maximum(unit, 0), self.turns)
        valid = jnp.logical_and(self.inside(unit), self.plane(unit) == z)
        size = self.late_inbox.shape[1] // 4
        place = lambda i: self.late_inbox.at[i, pl.ds(0, size)]
        second = self.late_load(self.late_seconds.at[unit, 1 - stage], place(0), 0)
        first = lambda: self.late_load(self.late_firsts.at[unit], place(1), 4)

        def fetch(base):
            def action():
                self.received(
                    self.late_seconds.at[unit, 1 - stage], self.late_second_receive.at[unit, 1 - stage]
                )
                second.start()
                if stage:
                    self.received(self.late_firsts.at[unit], self.late_first_receive.at[unit])
                    first().start()

            when(valid, action)

        def add(base):
            def action():
                second.wait()
                if stage:
                    first().wait()
                    sources = [self.late_place(turn, 0, 0), place(0), place(1)]
                    self.done(unit, lax.rem(unit, 2), 1, lambda target: add_rows(target, sources))
                    for i in range(2):
                        self.late_second(unit, turn, i).wait_send()
                    self.late_first(unit, turn).wait_send()
                else:
                    target = self.late_place(turn, 1, 0)
                    add_rows(target, [target, place(0)])
                    self.late_first(unit, turn).start()

            when(valid, action)

        return fetch, add

    def second_task(self, unit, turn, first, ready):
        return self.simple_task(
            self.inside(unit),
            ready,
            lambda: self.sources(unit, first, 1),
            self.second_slot(turn, first),
            lambda: self.second_send(unit, turn, first),
        )

    def first_task(self, unit, turn):
        arrive = lambda: self.received(self.seconds.at[unit, 1], self.second_receive.at[unit, 1])

        def send():
            return self.first_send(unit, turn)

        return self.simple_task(
            self.inside(unit),
            lambda: when(self.inside(unit), arrive),
            lambda: self.sources(unit, 1, 0) + [self.seconds.at[unit, 1]],
            self.first_slot(turn),
            send,
            lambda: self.free(unit, turn, 1),
        )

    def weave(self, tasks, pieces):
        buffers = self.inbox.shape[0] // BOXES
        if buffers > 1:
            tasks[0][0](0)
        for index, (fetch, add) in enumerate(tasks):
            if buffers == 1:
                fetch(0)
            elif index + 1 < len(tasks):
                tasks[index + 1][0]((index + 1) % 2 * BOXES)
            share = -(-len(pieces) // (len(tasks) - index))
            for piece in pieces[:share]:
                piece()
            pieces = pieces[share:]
            add(index % buffers * BOXES)

    def half_steps(self, units):
        return units + self.spot.line + 2


def norm_back(value, grads, gain):
    scale = lax.rsqrt(jnp.mean(value * value, axis=-1, keepdims=True) + EPSILON)
    unit = value * scale
    scaled = grads * gain
    back = scale * (scaled - unit * jnp.mean(scaled * unit, axis=-1, keepdims=True))
    return back, grads * unit


def backward_kernel(
    line,
    heads,
    kv_heads,
    cot_ref,
    totals_ref,
    hidden_ref,
    projected_ref,
    context_ref,
    in_ref,
    out_ref,
    tokens_ref,
    gain1_ref,
    gain2_ref,
    query_gain_ref,
    key_gain_ref,
    cosine_ref,
    sine_ref,
    block_out,
    input_grad,
    grads_all,
    out_total,
    gain_grads,
    elements,
    cots,
    tokens,
    kept,
    result,
    context,
    hidden_grads,
    context_grads,
    grads,
    normed_other,
    weight_rows,
    queries_f,
    shared_f,
    queries,
    query_grads,
    sums,
    out_grads,
    cores,
    firsts,
    rights,
    lefts,
    tree_send,
    tree_receive,
    load_sem,
    row_sem,
    head_sem,
    save_sem,
    hidden_send,
    hidden_receive,
    normed_send,
    normed_receive,
):
    batch, half, width = cot_ref.shape
    length = 2 * half
    features = query_gain_ref.shape[1]
    group = heads // kv_heads
    base = heads * features
    out_width = out_total.shape[1]
    narrow, spot = Spot(line, False), Spot(line, True)
    x = spot.x
    scale = features ** (-0.5)
    normed_grads = context_grads

    def load(source, target, index):
        return pltpu.make_async_copy(source, target, load_sem.at[index])

    def element_loads(i):
        return [
            load(hidden_ref.at[i], elements.at[0], 0),
            load(totals_ref.at[i, BACK], elements.at[1], 1),
            load(totals_ref.at[i, OUTPUT], elements.at[2], 2),
        ]

    first_loads = [load(cot_ref, cots, 3), load(tokens_ref, tokens, 4)] + [
        load(context_ref.at[i], rows_at(context, i, length), 5 + i) for i in range(batch)
    ]
    for copy in element_loads(0) + first_loads:
        copy.start()

    out_steps, in_steps = out_ref.shape[0] // CHUNK, in_ref.shape[0] // CHUNK
    stream = [(out_ref, step) for _ in range(batch) for step in range(out_steps)]
    stream += [(in_ref, step) for _ in range(batch) for step in range(in_steps)]

    def weight_load(index):
        ref, step = stream[index]
        return pltpu.make_async_copy(
            rows_at(ref, step, CHUNK),
            weight_rows.at[index % 2, :, pl.ds(0, ref.shape[1])],
            row_sem.at[index % 2],
        )

    def next_weights(index):
        if index + 2 < len(stream):
            weight_load(index + 2).start()

    for index in range(2):
        weight_load(index).start()
    gain_grads[...] = jnp.zeros_like(gain_grads)
    spot.greet()
    for copy in first_loads:
        copy.wait()

    def result_save(i, target):
        return pltpu.make_async_copy(result.at[i], target.at[i], save_sem.at[i])

    def half_copy(ref, i, side):
        return ref.at[pl.ds(pl.multiple_of(i * length + side * half, 16), half), pl.ds(0, width)]

    def hidden_copy(i):
        place = half_copy(hidden_grads, i, x)
        return spot.send(place, place, hidden_send.at[i], hidden_receive.at[i], CROSS)

    def element_rows(i):
        for copy in element_loads(i):
            copy.wait()

        def elementwise(step, _):
            rows = pl.ds(pl.multiple_of(step * 16, 16), 16)
            value = elements[0, rows, :]
            result[i, rows, :] = (value + elements[2, rows, :]).astype(jnp.bfloat16)
            back, gain_rows = norm_back(
                value, elements[1, rows, :], gain2_ref[...].astype(jnp.float32)
            )
            gain_grads[1:2, :] += jnp.sum(gain_rows, axis=0, keepdims=True)
            total = cots[i, rows, :].astype(jnp.float32) + back
            kept[i, rows, :] = total
            place = pl.ds(pl.multiple_of(i * length + x * half + step * 16, 16), 16)
            hidden_grads[place, :] = total.astype(jnp.bfloat16)
            return 0

        lax.fori_loop(0, half // 16, elementwise, 0)
        hidden_copy(i).start()
        result_save(i, block_out).start()
        if i + 1 < batch:
            for copy in element_loads(i + 1):
                copy.start()

    def hidden_done(i):
        hidden_copy(i).wait_send()
        place = half_copy(hidden_grads, i, 1 - x)
        spot.send(place, place, hidden_send.at[i], hidden_receive.at[i], CROSS).wait_recv()

    def context_step(i, step):
        index = i * out_steps + step
        weight_load(index).wait()
        rows = slice(i * length, (i + 1) * length)
        context_grads[rows, step * CHUNK : (step + 1) * CHUNK] = lax.dot_general(
            hidden_grads[rows],
            weight_rows[index % 2, :, :width],
            TRANSPOSED_RIGHT,
            preferred_element_type=jnp.float32,
        ).astype(jnp.bfloat16)
        next_weights(index)

    def out_step(step):
        columns = slice(step * CHUNK, (step + 1) * CHUNK)
        for start in range(0, width, CHUNK):
            out_grads[columns, start : start + CHUNK] = lax.dot_general(
                context[:, columns],
                hidden_grads[:, start : start + CHUNK],
                TRANSPOSED_LEFT,
                preferred_element_type=jnp.float32,
            ).astype(jnp.bfloat16)

    tree = Collect(
        narrow,
        lambda block, side: columns_at(out_grads, block, out_width),
        out_total,
        cores,
        firsts,
        rights,
        lefts,
        tree_send,
        tree_receive,
    )

    def tree_start():
        for z in range(line):
            tree.begin(z)

    def turns():
        return [(i, shared) for i in range(batch) for shared in range(kv_heads)]

    def head_loads(index):
        i, shared = turns()[index]
        slot = index % 2
        return [
            pltpu.make_async_copy(
                projected_ref.at[i, :, pl.ds(shared * group * features, group * features)],
                queries_f.at[slot],
                head_sem.at[slot, 0],
            )
        ] + [
            pltpu.make_async_copy(
                projected_ref.at[i, :, pl.ds(base + (shared + j * kv_heads) * features, features)],
                shared_f.at[slot, j],
                head_sem.at[slot, 1 + j],
            )
            for j in range(2)
        ]

    def turn_back(grads_in):
        return grads_in * cosine_ref[...] + pltpu.roll(
            grads_in * sine_ref[...], features // 2, 1
        )

    query_gain = lambda: query_gain_ref[...].astype(jnp.float32)
    key_gain = lambda: key_gain_ref[...].astype(jnp.float32)

    def attend_pieces(index):
        i, shared = turns()[index]
        slot = index % 2
        top = i * length

        def columns_of(member):
            return pl.ds(pl.multiple_of(member * features, LANES), features)

        def prepare():
            for copy in head_loads(index):
                copy.wait()
            if index + 1 < len(turns()):
                for copy in head_loads(index + 1):
                    copy.start()
            queries[group] = turned_heads(
                shared_f[slot, 0], key_gain(), cosine_ref[...], sine_ref[...]
            ).astype(jnp.bfloat16)
            queries[group + 1] = shared_f[slot, 1].astype(jnp.bfloat16)
            sums[...] = jnp.zeros_like(sums)

            def one(member):
                queries[member] = turned_heads(
                    queries_f[slot, :, columns_of(member)],
                    query_gain(),
                    cosine_ref[...],
                    sine_ref[...],
                ).astype(jnp.bfloat16)

            for_heads(0, group, 1, one)

        def rows_block(start, stop, seen, at_once, low, high):
            count = stop - start

            def block(member):
                query = queries[pl.ds(member, at_once), start:stop, :].reshape(-1, features)
                keys, values = queries[group, :seen, :], queries[group + 1, :seen, :]
                out_grad = jnp.concatenate(
                    [
                        context_grads[
                            top + start : top + stop,
                            head_columns(shared * group + member + j, features),
                        ]
                        for j in range(at_once)
                    ],
                    axis=0,
                )
                scores = lax.dot_general(
                    keys, query, TRANSPOSED_RIGHT, preferred_element_type=jnp.float32
                )
                shares = softmax(scores * scale)
                share_grads = lax.dot_general(
                    values, out_grad, TRANSPOSED_RIGHT, preferred_element_type=jnp.float32
                )
                sums[1, :seen, :] += jnp.dot(
                    shares.astype(jnp.bfloat16), out_grad, preferred_element_type=jnp.float32
                )
                inner = jnp.sum(shares * share_grads, axis=0, keepdims=True)
                score_grads = (shares * (share_grads - inner)).astype(jnp.bfloat16)
                rows = scale * lax.dot_general(
                    score_grads, keys, TRANSPOSED_LEFT, preferred_element_type=jnp.float32
                )
                query_grads[pl.ds(member, at_once), start:stop, :] = rows.reshape(
                    at_once, count, features
                )
                sums[0, :seen, :] += jnp.dot(
                    score_grads, query, preferred_element_type=jnp.float32
                )

            for_heads(low, high, at_once, block)

        def finish_queries():
            def finish(member):
                back, gain_rows = norm_back(
                    queries_f[slot, :, columns_of(member)],
                    turn_back(query_grads[member]),
                    query_gain(),
                )
                gain_grads[2:3, :features] += jnp.sum(gain_rows, axis=0, keepdims=True)
                grads[top : top + length, head_columns(shared * group + member, features)] = (
                    back.astype(jnp.bfloat16)
                )

            for_heads(0, group, 1, finish)

        def finish_keys():
            back, gain_rows = norm_back(shared_f[slot, 0], turn_back(sums[0] * scale), key_gain())
            gain_grads[3:4, :features] += jnp.sum(gain_rows, axis=0, keepdims=True)
            at = base + shared * features
            grads[top : top + length, at : at + features] = back.astype(jnp.bfloat16)
            at += kv_heads * features
            grads[top : top + length, at : at + features] = sums[1].astype(jnp.bfloat16)

        pieces = [prepare]
        for start, stop, seen, at_once in visible_blocks(length, group):
            share = max(at_once, group // 2)
            for low in range(0, group, share):
                pieces.append(
                    functools.partial(rows_block, start, stop, seen, at_once, low, low + share)
                )
        return pieces + [finish_queries, finish_keys]

    saves = [
        pltpu.make_async_copy(rows_at(grads, i, length), grads_all.at[i], save_sem.at[batch + i])
        for i in range(batch)
    ]

    def normed_step(i, step):
        index = batch * out_steps + i * in_steps + step
        weight_load(index).wait()
        rows = slice(i * length, (i + 1) * length)
        normed_grads[rows, step * CHUNK : (step + 1) * CHUNK] = lax.dot_general(
            grads[rows],
            weight_rows[index % 2],
            TRANSPOSED_RIGHT,
            preferred_element_type=jnp.float32,
        ).astype(jnp.bfloat16)
        next_weights(index)

    def normed_copy(i):
        return spot.send(
            half_copy(normed_grads, i, 1 - x),
            normed_other.at[i],
            normed_send.at[i],
            normed_receive.at[i],
            CROSS,
        )

    def input_rows(i):
        normed_copy(i).wait()
        result_save(i, block_out).wait()

        def body(step, _):
            rows = pl.ds(pl.multiple_of(step * 16, 16), 16)
            place = pl.ds(pl.multiple_of(i * length + x * half + step * 16, 16), 16)
            total = normed_grads[place, :width].astype(jnp.float32) + normed_other[
                i, rows, :
            ].astype(jnp.float32)
            back, gain_rows = norm_back(
                tokens[i, rows, :].astype(jnp.float32), total, gain1_ref[...].astype(jnp.float32)
            )
            gain_grads[0:1, :] += jnp.sum(gain_rows, axis=0, keepdims=True)
            kept[i, rows, :] = kept[i, rows, :] + back
            return 0

        lax.fori_loop(0, half // 16, body, 0)
        add_rows(result.at[i], [kept.at[i]])
        result_save(i, input_grad).start()

    for copy in head_loads(0):
        copy.start()
    attending = [attend_pieces(index) for index in range(len(turns()))]
    contexts = [
        [functools.partial(context_step, i, step) for step in range(out_steps)]
        for i in range(batch)
    ]
    opening = [functools.partial(element_rows, i) for i in range(batch)]
    opening += attending[0][:1] + [functools.partial(hidden_done, 0)] + contexts[0]
    opening += [functools.partial(hidden_done, i) for i in range(1, batch)]
    opening += [functools.partial(out_step, step) for step in range(out_steps)] + [tree_start]
    opening += contexts[1][:1] + [tree.cross] + contexts[1][1:]
    for steps in contexts[2:]:
        opening += steps
    closing = []
    for index in range(len(turns())):
        i = turns()[index][0]
        closing += attending[index][0 if index else 1 :]
        if index + 1 == len(turns()) or turns()[index + 1][0] > i:
            closing += [saves[i].start]
            closing += [functools.partial(normed_step, i, step) for step in range(in_steps)]
            closing += [lambda i=i: normed_copy(i).start()]
    closing += [functools.partial(input_rows, i) for i in range(batch)]
    for piece in opening:
        piece()
    mingle(closing, tree.tasks())
    for i in range(batch):
        result_save(i, input_grad).wait()
    for copy in saves:
        copy.wait()


def run_backward(
    cot,
    totals,
    hidden,
    projected,
    context,
    in_full,
    out_full,
    tokens,
    gains,
    tables,
    fsdp_count,
    kv_heads,
):
    line = fsdp_count // PLANE
    batch, half, width = tokens.shape
    length = 2 * half
    features = gains[2].shape[1]
    heads = out_full.shape[0] // features
    group = heads // kv_heads
    in_width, out_depth = in_full.shape[1], out_full.shape[0]
    out_shape = (out_depth, width // fsdp_count)
    anywhere = pl.BlockSpec(memory_space=pl.ANY)
    inside = pl.BlockSpec(memory_space=pltpu.VMEM)
    shape = lambda *dims: jax.ShapeDtypeStruct(dims, jnp.bfloat16)
    vmem = lambda *dims: pltpu.VMEM(dims, jnp.bfloat16)
    wide = lambda *dims: pltpu.VMEM(dims, jnp.float32)
    sem = lambda *dims: pltpu.SemaphoreType.DMA(dims)
    rows = batch * length
    return pl.pallas_call(
        functools.partial(backward_kernel, line, heads, kv_heads),
        out_shape=(
            shape(batch, half, width),
            shape(batch, half, width),
            shape(batch, length, in_width),
            jax.ShapeDtypeStruct(out_shape, jnp.float32),
            jax.ShapeDtypeStruct((8, width), jnp.float32),
        ),
        in_specs=[anywhere] * 8 + [inside] * 6,
        out_specs=(anywhere, anywhere, anywhere, inside, inside),
        scratch_shapes=[
            wide(3, half, width),
            vmem(batch, half, width),
            vmem(batch, half, width),
            wide(batch, half, width),
            vmem(batch, half, width),
            vmem(rows, out_depth),
            vmem(rows, width),
            vmem(rows, max(out_depth, width)),
            vmem(rows, in_width),
            vmem(batch, half, width),
            vmem(2, CHUNK, max(width, in_width)),
            wide(2, length, group * features),
            wide(2, 2, length, features),
            vmem(group + 2, length, features),
            wide(group, length, features),
            wide(2, length, features),
            vmem(out_depth, width),
            *collect_scratch(line, out_shape),
            sem(5 + batch),
            sem(2),
            sem(2, 3),
            sem(2 * batch),
            sem(batch),
            sem(batch),
            sem(batch),
            sem(batch),
        ],
        compiler_params=pltpu.CompilerParams(
            collective_id=3, has_side_effects=True, vmem_limit_bytes=62 * MIB
        ),
    )(
        cot,
        totals,
        hidden,
        projected,
        context,
        in_full,
        out_full,
        tokens,
        *gains,
        *tables,
    )


def gradients_kernel(
    line,
    normed,
    grads,
    gains_ref,
    xe_ref,
    ce_ref,
    act_ref,
    dgate_ref,
    dup_ref,
    in_total,
    gains_all,
    gate_total,
    up_total,
    down_total,
    parts,
    cores,
    firsts,
    rights,
    lefts,
    tree_send,
    tree_receive,
    gain_send,
    gain_receive,
    gain_local,
    wide_rows,
    slim_rows,
    gate_sum,
    up_sum,
    down_sum,
    load_sem,
    save_sem,
):
    narrow, spot = Spot(line, False), Spot(line, True)
    experts, count, _ = xe_ref.shape
    share = wide_rows.shape[1]
    turns = count // share
    pieces = [
        (expert, kind, turn)
        for expert in range(experts)
        for kind in range(2)
        for turn in range(turns)
    ]

    def loads(index):
        expert, kind, turn = pieces[index]
        slot = index % 2
        rows = pl.ds(turn * share, share)
        slim = (dgate_ref, dup_ref) if kind == 0 else (act_ref,)
        return [
            pltpu.make_async_copy(
                (xe_ref, ce_ref)[kind].at[expert, rows], wide_rows.at[slot], load_sem.at[slot, 0]
            )
        ] + [
            pltpu.make_async_copy(
                ref.at[expert, rows], slim_rows.at[slot, i], load_sem.at[slot, 1 + i]
            )
            for i, ref in enumerate(slim)
        ]

    def saves(expert, kind):
        pairs = ((gate_sum, gate_total), (up_sum, up_total))
        if kind:
            return [pltpu.make_async_copy(down_sum, down_total.at[expert], save_sem.at[2])]
        return [
            pltpu.make_async_copy(source, target.at[expert], save_sem.at[i])
            for i, (source, target) in enumerate(pairs)
        ]

    for copy in loads(0):
        copy.start()
    spot.greet()
    gains = Spread(
        spot,
        gains_ref,
        lambda block, half: gains_all.at[block, half],
        gain_send,
        gain_receive,
        gain_local.at[0],
    )
    gains.begin()
    depth, width = in_total.shape
    tree = Collect(
        narrow,
        lambda block, half: rows_at(parts, block, depth),
        in_total,
        cores,
        firsts,
        rights,
        lefts,
        tree_send,
        tree_receive,
    )
    chunk = PLANE * depth

    def far_first(step):
        z = narrow.z
        down = jnp.where(line - 1 - step > z, line - 1 - step, line - 2 - step)
        up = jnp.where(step < z, step, step + 1)
        return jnp.where(step == line - 1, z, jnp.where(2 * z < line, down, up))

    def plane(step, _):
        z = far_first(step)
        columns = pl.ds(pl.multiple_of(z * chunk, LANES), chunk)
        for start in range(0, width, CHUNK):
            parts[pl.ds(pl.multiple_of(z * chunk, 16), chunk), start : start + CHUNK] = (
                lax.dot_general(
                    normed[:, columns],
                    grads[:, start : start + CHUNK],
                    TRANSPOSED_LEFT,
                    preferred_element_type=jnp.float32,
                ).astype(jnp.bfloat16)
            )
        tree.begin(z)
        when(step > 0, lambda: tree.to_first(far_first(step - 1)))
        return 0

    lax.fori_loop(0, line, plane, 0)
    tree.to_first(narrow.z)

    def piece(index):
        expert, kind, turn = pieces[index]
        slot = index % 2
        for copy in loads(index):
            copy.wait()
        if index + 1 < len(pieces):
            for copy in loads(index + 1):
                copy.start()
        if turn == 0 and expert:
            for copy in saves(expert - 1, kind):
                copy.wait()
        size = wide_rows.shape[2] // 4

        def add(target, place, left, right):
            product = lax.dot_general(
                left, right, TRANSPOSED_LEFT, preferred_element_type=jnp.float32
            )
            if turn:
                product = target[place] + product
            target[place] = product

        def part(step, _):
            at = pl.ds(pl.multiple_of(step * size, LANES), size)
            if kind:
                add(down_sum, (slice(None), at), slim_rows[slot, 0], wide_rows[slot, :, at])
            else:
                for i, target in enumerate((gate_sum, up_sum)):
                    add(target, (at, slice(None)), wide_rows[slot, :, at], slim_rows[slot, i])
            return 0

        lax.fori_loop(0, 4, part, 0)
        if turn == turns - 1:
            for copy in saves(expert, kind):
                copy.start()

    work = tree.tasks()
    steps = list(range(1, gains.steps()))
    filler = list(range(len(pieces)))
    while work or filler:
        for _ in range(2 if len(filler) > len(work) else 1):
            if filler:
                piece(filler.pop(0))
        if work:
            work.pop(0)()
        if steps:
            gains.step(steps.pop(0))
    gains.finish()
    for copy in saves(experts - 1, 0) + saves(experts - 1, 1):
        copy.wait()


def run_gradients(normed, grads, gains, expert_rows, fsdp_count):
    line = fsdp_count // PLANE
    width = grads.shape[1]
    experts, count, depth = expert_rows[0].shape
    units = expert_rows[2].shape[2]
    share = 2 * CHUNK if count % (2 * CHUNK) == 0 else count // (2 * line)
    shape = (normed.shape[1] // fsdp_count, width)
    sends, receives = spread_count(line, True)
    inside = pl.BlockSpec(memory_space=pltpu.VMEM)
    anywhere = pl.BlockSpec(memory_space=pl.ANY)
    return pl.pallas_call(
        functools.partial(gradients_kernel, line),
        out_shape=(
            jax.ShapeDtypeStruct(shape, jnp.float32),
            jax.ShapeDtypeStruct((fsdp_count, 2, *gains.shape), jnp.float32),
            jax.ShapeDtypeStruct((experts, depth, units), jnp.float32),
            jax.ShapeDtypeStruct((experts, depth, units), jnp.float32),
            jax.ShapeDtypeStruct((experts, units, depth), jnp.float32),
        ),
        in_specs=[inside, inside] + [anywhere] * 6,
        out_specs=(inside,) + (anywhere,) * 4,
        scratch_shapes=[
            pltpu.VMEM((normed.shape[1], width), jnp.bfloat16),
            *collect_scratch(line, shape),
            pltpu.SemaphoreType.DMA((sends,)),
            pltpu.SemaphoreType.DMA((receives,)),
            pltpu.SemaphoreType.DMA((1,)),
            pltpu.VMEM((2, share, depth), jnp.bfloat16),
            pltpu.VMEM((2, 2, share, units), jnp.bfloat16),
            pltpu.VMEM((depth, units), jnp.float32),
            pltpu.VMEM((depth, units), jnp.float32),
            pltpu.VMEM((units, depth), jnp.float32),
            pltpu.SemaphoreType.DMA((2, 3)),
            pltpu.SemaphoreType.DMA((3,)),
        ],
        compiler_params=pltpu.CompilerParams(
            collective_id=4, has_side_effects=True, vmem_limit_bytes=60 * MIB
        ),
    )(normed, grads, gains, *expert_rows)


def experts_kernel(
    line,
    slots,
    own_ref,
    cot_first,
    cot_ref,
    info_ref,
    gate_ref,
    up_ref,
    down_ref,
    all_ref,
    cot_later,
    total_ref,
    xe_all,
    ce_all,
    act_all,
    dgate_all,
    dup_all,
    part,
    cores,
    seconds,
    firsts,
    ends,
    late_ends,
    late_seconds,
    late_firsts,
    hidden_w,
    down_w,
    x_rows,
    c_rows,
    xe,
    ce,
    acts,
    dgates,
    dups,
    hidden_grads,
    picks,
    weigh,
    rows,
    stage,
    inbox,
    outbox,
    summed,
    rows_send,
    rows_receive,
    rows_late_send,
    rows_late_receive,
    rows_local,
    cot_send,
    cot_receive,
    cot_late_send,
    cot_late_receive,
    cot_local,
    load_sem,
    save_sem,
    stage_sem,
    inbox_sem,
    outbox_sem,
    total_sem,
    weight_sem,
    core_receive,
    second_receive,
    first_receive,
    end_receive,
    *late_scratch,
):
    late_refs = (late_ends, late_seconds, late_firsts, *late_scratch)
    spot = Spot(line, True)
    z, core = spot.z, spot.core
    cot_semaphores = (cot_send, cot_receive, cot_late_send, cot_late_receive, cot_local)
    tree_semaphores = (rows_send, rows_receive, rows_late_send, rows_late_receive, rows_local)
    batch, half, width = own_ref.shape
    length = 2 * half
    units = down_ref.shape[1]
    groups = batch * line
    weights = [
        pltpu.make_async_copy(source, target, weight_sem.at[i])
        for i, (source, target) in enumerate(
            [(down_ref, down_w)]
            + [(gate_ref.at[e], hidden_w.at[e, :, pl.ds(0, units)]) for e in range(2)]
            + [(up_ref.at[e], hidden_w.at[e, :, pl.ds(units, units)]) for e in range(2)]
        )
    ]
    for copy in weights:
        copy.start()
    rows[...] = jnp.zeros_like(rows)
    spot.greet()

    def half_of(ref, index):
        return rows_at(ref, index, half)

    trees = []
    for i in range(batch):
        place = lambda block, start, size, i=i: all_ref.at[
            i, block, pl.ds(pl.multiple_of(start, 16), size)
        ]
        trees.append(rows_spread(spot, own_ref.at[i], place, half, tree_semaphores, i))
    for i in range(1, batch):
        place = lambda block, start, size, i=i: cot_later.at[
            i - 1, block, pl.ds(pl.multiple_of(start, 16), size)
        ]
        trees[i] += rows_spread(spot, cot_ref.at[i], place, half, cot_semaphores, i - 1)
    run_trees(trees[0])
    for tree in sum(trees[1:], []):
        tree.begin()
    for copy in weights:
        copy.wait()

    plane_of = functools.partial(plane_in_turn, line)

    def load_group(group, member, start):
        at = lax.div(group, line)
        sequence = plane_of(group) * PLANE + member
        slot = member % 2
        def copy(i, source, target):
            return pltpu.make_async_copy(source, target.at[slot], load_sem.at[i, slot])

        own = copy(0, all_ref.at[at, sequence], x_rows)
        if start:
            own.start()
            later = cot_later.at[jnp.maximum(at - 1, 0), sequence]
            when(at == 0, lambda: copy(1, cot_first.at[sequence], c_rows).start())
            when(at > 0, lambda: copy(1, later, c_rows).start())
        else:
            own.wait()
            copy(1, cot_first.at[sequence], c_rows).wait()

    def saves(group):
        to = lambda ref, expert: rows_at(ref.at[expert], group, PLANE * slots)
        pairs = ((xe, xe_all), (ce, ce_all), (acts, act_all), (dgates, dgate_all), (dups, dup_all))
        return [
            pltpu.make_async_copy(source.at[expert], to(target, expert), save_sem.at[2 * i + expert])
            for i, (source, target) in enumerate(pairs)
            for expert in range(2)
        ]

    def staged(unit, y, mine):
        slot = y * 2 + mine
        if mine:
            return pltpu.make_async_copy(stage.at[slot], part.at[unit, y], stage_sem.at[slot])
        return spot.send(
            stage.at[slot], cores.at[unit, y], stage_sem.at[slot], core_receive.at[unit, y], CORE
        )

    def combine(unit, y):
        for mine in range(2):
            member = y * 2 + (core if mine else 1 - core)
            for start in range(0, width, CHUNK):
                stage[y * 2 + mine, :, start : start + CHUNK] = lax.dot_general(
                    picks[member],
                    rows[member, :, start : start + CHUNK],
                    TRANSPOSED_LEFT,
                    preferred_element_type=jnp.float32,
                ).astype(jnp.bfloat16)
            staged(unit, y, mine).start()

    def pick(group, member):
        slot = member % 2
        load_group(group, member, False)
        if member + 1 < PLANE:
            load_group(group, member + 1, True)
        sequence = plane_of(group) * PLANE + member
        info = info_ref[lax.div(group, line) * line * PLANE + sequence]
        places = lax.broadcasted_iota(jnp.int32, (2 * LANES, length), 0)
        lower = places < LANES
        ranks = jnp.where(lower, info[0:1], info[1:2] + float(LANES)).astype(jnp.int32)
        some = jnp.where(lower, info[0:1], info[1:2]) >= 0.0
        hot = jnp.logical_and(ranks == places, some)
        chosen = hot.astype(jnp.float32).astype(jnp.bfloat16)
        picks[member] = chosen
        shares = jnp.where(hot, jnp.where(lower, info[2:3], info[3:4]), 0.0)
        column = jnp.sum(shares, axis=1, keepdims=True)
        here = pl.ds(member * slots, slots)
        for expert in range(2):
            weigh[expert, here, :] = jnp.broadcast_to(
                column[expert * LANES : expert * LANES + slots], (slots, LANES)
            )
        for source, target in ((x_rows, xe), (c_rows, ce)):
            for start in range(0, width, CHUNK):
                selected = jnp.dot(
                    chosen,
                    source[slot, :, start : start + CHUNK],
                    preferred_element_type=jnp.float32,
                ).astype(jnp.bfloat16)
                for expert in range(2):
                    target[expert, here, start : start + CHUNK] = selected[
                        expert * LANES : expert * LANES + slots
                    ]

    def keep(expert, product, start):
        at = pl.ds(expert * LANES, slots)
        for one in range(PLANE):
            rows[one, at, start : start + CHUNK] = product[one * slots : (one + 1) * slots].astype(
                jnp.bfloat16
            )

    def forward(expert):
        hidden = jnp.dot(xe[expert], hidden_w[expert], preferred_element_type=jnp.float32)
        gate, up = hidden[:, :units], hidden[:, units:]
        sigmoid = jax.nn.sigmoid(gate)
        silu = gate * sigmoid
        scale = weigh[expert, :, 0:1]
        acts[expert] = (silu * up * scale).astype(jnp.bfloat16)
        act_grads = scale * lax.dot_general(
            ce[expert], down_w[expert], TRANSPOSED_RIGHT, preferred_element_type=jnp.float32
        )
        gate_grads = (act_grads * up * (sigmoid * (1.0 + gate * (1.0 - sigmoid)))).astype(
            jnp.bfloat16
        )
        up_grads = (act_grads * silu).astype(jnp.bfloat16)
        dgates[expert] = gate_grads
        dups[expert] = up_grads
        hidden_grads[expert, :, :units] = gate_grads
        hidden_grads[expert, :, units:] = up_grads
        for start in range(0, width, CHUNK):
            keep(
                expert,
                jnp.dot(
                    acts[expert],
                    down_w[expert, :, start : start + CHUNK],
                    preferred_element_type=jnp.float32,
                ),
                start,
            )

    def backward(expert):
        for start in range(0, width, CHUNK):
            keep(
                expert,
                lax.dot_general(
                    hidden_grads[expert],
                    hidden_w[expert, start : start + CHUNK, :],
                    TRANSPOSED_RIGHT,
                    preferred_element_type=jnp.float32,
                ),
                start,
            )

    units_all = 2 * groups

    def inside(unit):
        return jnp.logical_and(unit >= 0, unit < units_all)

    def ready(unit):
        @pl.when(inside(unit))
        def _():
            for y in range(2):
                staged(unit, y, 1).wait()
                staged(unit, y, 0).wait_send()
                place, semaphore = cores.at[unit, y], core_receive.at[unit, y]
                spot.send(place, place, outbox_sem.at[0], semaphore, CORE).wait_recv()

    late = late_rows(half)

    def done(unit, tensor, part_of, into):
        rows = (pl.ds(0, half - late), pl.ds(half - late, late))[part_of]
        place = summed.at[rows]
        into(place)
        copy = pltpu.make_async_copy(
            place, total_ref.at[lax.div(unit, 2 * line), tensor, rows], total_sem.at[0]
        )
        copy.start()
        copy.wait()

    sums = Sums(
        spot,
        half,
        lambda unit, y: part.at[unit, y],
        lambda unit, y: cores.at[unit, y],
        (seconds, firsts, ends),
        inbox,
        outbox,
        (inbox_sem, outbox_sem, second_receive, first_receive, end_receive),
        late_refs,
        lambda unit: plane_of(lax.div(jnp.maximum(unit, 0), 2)),
        inside,
        ready,
        done,
        2,
    )

    def tree_turn(half_step, last):
        for i in range(1, batch):
            turn = half_step - (i - 1) * 2 * line
            if last:
                when(turn == 2 * line - 1, lambda: [tree.finish() for tree in trees[i]])
            else:
                inner = jnp.logical_and(turn >= 0, turn < 2 * line - 1)
                when(inner, lambda: [tree.step(turn + 1) for tree in trees[i]])

    def begin_pick(group):
        load_group(group, 0, True)

    begin_pick(0)
    for member in range(PLANE):
        pick(0, member)

    def step_body(step, _):
        busy = step < groups
        more = step + 1 < groups
        for parity in range(2):
            half_step = step * 2 + parity
            tree_turn(half_step, False)
            sums.retire(half_step, parity)
            tasks = sums.tasks(half_step, parity)
            pieces = []
            for expert in range(2):
                pieces.append(functools.partial((forward, backward)[parity], expert))
            if parity == 0:
                pieces.append(lambda: [copy.start() for copy in saves(step)])
            for y in range(2):
                pieces.append(functools.partial(combine, half_step, y))
            pieces = [functools.partial(when, busy, piece) for piece in pieces]
            if parity == 1:

                def prepare():
                    for copy in saves(step):
                        copy.wait()
                    begin_pick(step + 1)

                tree_end = functools.partial(tree_turn, half_step, True)
                pieces += [tree_end, functools.partial(when, more, prepare)]
                for member in range(PLANE):
                    pieces.append(
                        functools.partial(when, more, functools.partial(pick, step + 1, member))
                    )
            sums.weave(tasks, pieces)
        return 0

    half_steps = sums.half_steps(units_all)
    lax.fori_loop(0, -(-half_steps // 2), step_body, 0)
    end = -(-half_steps // 2) * 2
    for parity in range(2):
        sums.retire(jnp.int32(end + parity), parity)
    for copy in saves(groups - 1):
        copy.wait()


def run_experts(rows, cot_first, cot, info, w_gate, w_up, w_down, capacity, fsdp_count):
    line = fsdp_count // PLANE
    batch, half, width = rows.shape
    length = 2 * half
    units = w_down.shape[1]
    slots = -(-capacity // 16) * 16
    groups = batch * line
    count = groups * PLANE * slots
    taken = PLANE * slots
    shape = lambda *dims: jax.ShapeDtypeStruct(dims, jnp.bfloat16)
    block = (half, width)
    late = late_rows(half)
    early = half - late
    anywhere = pl.BlockSpec(memory_space=pl.ANY)
    vmem = lambda *dims: pltpu.VMEM(dims, jnp.bfloat16)
    sem = lambda *dims: pltpu.SemaphoreType.DMA(dims)
    return pl.pallas_call(
        functools.partial(experts_kernel, line, slots),
        out_shape=(
            shape(batch, fsdp_count, length, width),
            shape(max(batch - 1, 1), fsdp_count, length, width),
            jax.ShapeDtypeStruct((batch, 2, *block), jnp.float32),
            shape(2, count, width),
            shape(2, count, width),
            shape(2, count, units),
            shape(2, count, units),
            shape(2, count, units),
            shape(2 * groups, 2, length, width),
            shape(2 * groups, 2, length, width),
            shape(2 * groups, 2, early, width),
            shape(2 * groups, early, width),
            shape(2 * groups, 2, early, width),
            shape(2 * groups, 2, 4 * late, width),
            shape(2 * groups, 2, late, width),
            shape(2 * groups, late, width),
        ),
        in_specs=[
            anywhere,
            anywhere,
            anywhere,
            pl.BlockSpec(memory_space=pltpu.VMEM),
            anywhere,
            anywhere,
            anywhere,
        ],
        out_specs=(anywhere,) * 16,
        scratch_shapes=[
            vmem(2, width, 2 * units),
            vmem(2, units, width),
            vmem(2, length, width),
            vmem(2, length, width),
            vmem(2, taken, width),
            vmem(2, taken, width),
            vmem(2, taken, units),
            vmem(2, taken, units),
            vmem(2, taken, units),
            vmem(2, taken, 2 * units),
            vmem(PLANE, 2 * LANES, length),
            pltpu.VMEM((2, taken, LANES), jnp.float32),
            vmem(PLANE, 2 * LANES, width),
            vmem(PLANE, length, width),
            vmem(12, early, width),
            vmem(10, early, width),
            pltpu.VMEM(block, jnp.float32),
            *rows_semaphores(batch, line),
            *rows_semaphores(max(batch - 1, 1), line),
            sem(2, 2),
            sem(10),
            sem(PLANE),
            sem(12),
            sem(10),
            sem(1),
            sem(5),
            sem(2 * groups, 2),
            sem(2 * groups, 2),
            sem(2 * groups),
            sem(2 * groups, 2),
            vmem(4, 4 * late, width),
            vmem(4, 4 * late, width),
            vmem(2, 4 * late, width),
            sem(10),
            sem(4),
            sem(6),
            sem(2 * groups, 2),
            sem(2 * groups, 2),
            sem(2 * groups),
        ],
        compiler_params=pltpu.CompilerParams(
            collective_id=2, has_side_effects=True, vmem_limit_bytes=60 * MIB
        ),
    )(rows, cot_first, cot, info, w_gate, w_up, w_down)[2:8]


def packed_picks(routes, gates):
    length = routes.shape[2]
    packed = jnp.concatenate([routes[:, 0].astype(jnp.float32), gates[:, 0]], axis=-1)
    packed = jnp.swapaxes(packed, 1, 2).reshape(-1, length)
    return jnp.pad(packed, ((0, 0), (0, -length % LANES)))


def slot_info(packed, batch, top, length, local_experts):
    fsdp_count = packed.shape[0]
    packed = packed[..., :length].reshape(fsdp_count, batch, 1, 2 * top, length)
    packed = jnp.swapaxes(packed, 0, 1)
    experts = lax.axis_index(FSDP) * local_experts + jnp.arange(local_experts, dtype=jnp.int32)
    same = packed[..., :top, :].astype(jnp.int32) == experts[:, None, None]
    hot = jnp.any(same, axis=3)
    shares = jnp.sum(jnp.where(same, packed[..., top:, :], 0.0), axis=3)
    position = jnp.arange(length)
    upper = (position[:, None] < position[None, :]).astype(jnp.bfloat16)
    rank = jnp.dot(
        hot.astype(jnp.bfloat16).reshape(-1, length), upper, preferred_element_type=jnp.float32
    )
    rank = jnp.where(hot, rank.reshape(hot.shape), -1.0)
    return jnp.concatenate([rank, shares], axis=2).reshape(-1, 2 * local_experts, length)


def gathered_layer(
    tokens,
    cotangent,
    norm1_gain,
    w_query,
    key_projection_weight,
    value_projection_weight,
    query_gain,
    key_gain,
    w_out,
    norm2_gain,
    w_gate,
    w_up,
    w_down,
    routes,
    gates,
):
    batch_count = tokens.shape[0]
    model_width = tokens.shape[3]
    sequence_length = routes.shape[2]
    half_length = tokens.shape[2]
    top_count = routes.shape[3]
    head_features = query_gain.shape[0]
    local_experts = w_gate.shape[0]
    fsdp_count = lax.axis_size(FSDP)
    all_experts = local_experts * fsdp_count
    capacity = 7 * top_count * sequence_length // (6 * all_experts)
    query_width = w_query.shape[1]
    kv_width = key_projection_weight.shape[1]
    kv_heads = kv_width // head_features
    cosine_table, sine_values = rotary_tables(sequence_length, head_features)
    weight_in = jnp.concatenate([w_query, key_projection_weight, value_projection_weight], axis=1)
    half_signs = jnp.where(jnp.arange(head_features) < head_features // 2, -1.0, 1.0)
    tables = (cosine_table[:, 0], sine_values[:, 0] * half_signs)
    gains = [gain[None, :] for gain in (norm1_gain, norm2_gain, query_gain, key_gain)]
    cot_first, in_full, out_full, picks, normed, projected, contexts, hidden, second = run_forward(
        tokens[:, 0],
        cotangent[:, 0],
        weight_in,
        w_out,
        packed_picks(routes, gates),
        gains,
        tables,
        fsdp_count,
        kv_heads,
    )
    info = slot_info(picks, batch_count, top_count, sequence_length, local_experts)
    totals, *expert_rows = run_experts(
        second, cot_first, cotangent[:, 0], info, w_gate, w_up, w_down, capacity, fsdp_count
    )
    block_out, input_grad, projected_grads, out_sum, gain_grads = run_backward(
        cotangent[:, 0],
        totals,
        hidden,
        projected,
        contexts,
        in_full,
        out_full,
        tokens[:, 0],
        gains,
        tables,
        fsdp_count,
        kv_heads,
    )
    rows = batch_count * sequence_length
    in_sum, gains_all, *expert_grads = run_gradients(
        normed.reshape(rows, -1),
        projected_grads.reshape(rows, -1),
        gain_grads,
        expert_rows,
        fsdp_count,
    )
    gains_sum = jnp.sum(gains_all, axis=(0, 1))
    return (
        block_out[:, None],
        input_grad[:, None],
        gains_sum[0],
        in_sum[:, :query_width],
        in_sum[:, query_width : query_width + kv_width],
        in_sum[:, query_width + kv_width :],
        gains_sum[2, :head_features],
        gains_sum[3, :head_features],
        out_sum,
        gains_sum[1],
        *expert_grads,
    )


def shards(*arrays):
    tokens, routes, w_gate = arrays[0], arrays[13], arrays[10]
    fsdp_count = lax.axis_size(FSDP)
    gathered = fsdp_count * routes.shape[2] * tokens.shape[3] * 2
    fits = gathered <= 24 * MIB and fsdp_count % PLANE == 0 and lax.axis_size(TP) == 2
    if fits and w_gate.shape[0] == 2:
        return gathered_layer(*arrays)
    return exchanged_layer(*arrays)


def solution(mesh):
    in_specs = (
        P(None, "fsdp", "tp", None),
        P(None, "fsdp", "tp", None),
        P(),
        P("fsdp", "tp"),
        P("fsdp", "tp"),
        P("fsdp", "tp"),
        P(),
        P(),
        P("tp", "fsdp"),
        P(),
        P("fsdp", None, "tp"),
        P("fsdp", None, "tp"),
        P("fsdp", "tp", None),
        P(None, "fsdp", None, None),
        P(None, "fsdp", None, None),
    )
    out_specs = (
        P(None, "fsdp", "tp", None),
        P(None, "fsdp", "tp", None),
        P(),
        P("fsdp", "tp"),
        P("fsdp", "tp"),
        P("fsdp", "tp"),
        P(),
        P(),
        P("tp", "fsdp"),
        P(),
        P("fsdp", None, "tp"),
        P("fsdp", None, "tp"),
        P("fsdp", "tp", None),
    )
    return jax.shard_map(shards, mesh=mesh, in_specs=in_specs, out_specs=out_specs, check_vma=False)
```
